32 devices in a mesh: crop: 4 (over y, x), row: 8 (over z, core).
Axes of the slice: x: 2, y: 2, z: 4, core: 2. Of those that a mesh axis runs over, the one named last changes fastest.
Arguments:
- pair: bfloat16 [4, 256, 256, 128], P('crop', 'row'), may hold values from -6 to 6
- single: bfloat16 [4, 256, 384], P('crop', 'row'), may hold values from -6 to 6
- lengths: int32 [4], P('crop'), may hold values from 192 to 256, as said below
- params: float32 [3070464], P('row'), as said below
- moment_one: float32 [3070464], P('row'), as said below
- moment_two: float32 [3070464], P('row'), as said below
- pair_cotangent: bfloat16 [4, 256, 256, 128], P('crop', 'row'), may hold values from -6 to 6
- single_cotangent: bfloat16 [4, 256, 384], P('crop', 'row'), may hold values from -6 to 6
Outputs:
- pair_out: bfloat16 [4, 256, 256, 128], P('crop', 'row')
- single_out: bfloat16 [4, 256, 384], P('crop', 'row')
- pair_grad: float32 [4, 256, 256, 128], P('crop', 'row')
- single_grad: float32 [4, 256, 384], P('crop', 'row')
- new_params: float32 [3070464], P('row')
- new_first: float32 [3070464], P('row')
- new_second: float32 [3070464], P('row')
- clip_norm: float32 [], replicated
The draws below stay inside these ranges and needn't reach their ends.
Inputs may be any that keep to these rules, and one draw needn't show every extreme that they name: `lengths`: one crop has all 256 tokens live. `params`: matrices about one over the root of their rows (outputs of attention four times that), gains 0.5 to 1.5, biases about 0.3. `moment_one`: both signs. `moment_two`: positive.
All inputs are finite; a program needn't handle non-finite values.
Results may differ from the reference program's by a relative error of at most 0.022.
Values may be sent and summed in bfloat16 or wider, within the bound.
No kernel may reach another device: no remote copies, remote signals or barrier semaphores. Data moves between devices by JAX's collectives and lax.ppermute only.
A program may use at most 768 MiB of HBM per device.

```python
import math
import jax
import jax.numpy as jnp
import numpy as np
from jax import lax

C = 128
H = 128
S = 384
TA_HEADS = 4
SA_HEADS = 16
SA_DIM = 24
LENGTH = 256
STEP = 10
STRIDE = 128
CROPS = 4
PARAMS = 3070464


CLIP = 1.0


def layout_drawn(pair_width, hidden_width, single_width, tri_heads, att_heads):
    entries = []
    for prefix in ('outgoing', 'incoming'):
        entries += [(prefix + '_norm_gain', (pair_width,), 'gain'), (prefix + '_norm_bias', (pair_width,), 'bias'), (prefix + '_proj_gate', (pair_width, 4 * hidden_width), 'matrix'), (prefix + '_out_gain', (hidden_width,), 'gain'), (prefix + '_out_bias', (hidden_width,), 'bias'), (prefix + '_proj_out', (hidden_width, pair_width), 'matrix'), (prefix + '_gate_out', (pair_width, pair_width), 'matrix')]
    for prefix in ('starting', 'ending'):
        entries += [(prefix + '_norm_gain', (pair_width,), 'gain'), (prefix + '_norm_bias', (pair_width,), 'bias'), (prefix + '_qkvg', (pair_width, 4 * pair_width), 'matrix'), (prefix + '_bias_proj', (pair_width, tri_heads), 'matrix'), (prefix + '_output', (pair_width, pair_width), 'output')]
    entries += [('pair_norm_gain', (pair_width,), 'gain'), ('pair_norm_bias', (pair_width,), 'bias'), ('pair_up', (pair_width, 8 * pair_width), 'matrix'), ('pair_down', (4 * pair_width, pair_width), 'matrix'), ('attend_norm_gain', (single_width,), 'gain'), ('attend_norm_bias', (single_width,), 'bias'), ('attend_qkvg', (single_width, 4 * single_width), 'matrix'), ('attend_pair_gain', (pair_width,), 'gain'), ('attend_pair_bias', (pair_width,), 'bias'), ('attend_pair_proj', (pair_width, att_heads), 'matrix'), ('attend_output', (single_width, single_width), 'output'), ('single_norm_gain', (single_width,), 'gain'), ('single_norm_bias', (single_width,), 'bias'), ('single_up', (single_width, 8 * single_width), 'matrix'), ('single_down', (4 * single_width, single_width), 'matrix')]
    return entries


def stored_order_drawn(vector):
    return vector.reshape(STRIDE, -1).T.reshape(-1)


def gradient_scale(kind):
    factor = 3.0 if kind in ('gain', 'bias') else 1.0
    return CLIP / math.sqrt(PARAMS) * factor


def draw_params(key, part):
    key = jax.random.fold_in(key, 11)
    pieces = []
    for number, (name, shape, kind) in enumerate(layout_drawn(C, H, S, TA_HEADS, SA_HEADS)):
        sub = jax.random.fold_in(key, number)
        count = math.prod(shape)
        if kind == 'gain':
            values = jax.random.uniform(sub, (count,), jnp.float32, 0.5, 1.5)
        elif kind == 'bias':
            values = 0.3 * jax.random.normal(sub, (count,), jnp.float32)
        elif kind == 'output':
            values = 4.0 / math.sqrt(shape[0]) * jax.random.normal(sub, (count,), jnp.float32)
        else:
            values = 1.0 / math.sqrt(shape[0]) * jax.random.normal(sub, (count,), jnp.float32)
        pieces.append(values)
    return stored_order_drawn(jnp.concatenate(pieces))


def draw_moment_one(key, part):
    key = jax.random.fold_in(key, 12)
    pieces = []
    for number, (name, shape, kind) in enumerate(layout_drawn(C, H, S, TA_HEADS, SA_HEADS)):
        sub = jax.random.fold_in(key, number)
        count = math.prod(shape)
        level = 0.1 / 0.9 * gradient_scale(kind)
        pieces.append(level * jax.random.normal(sub, (count,), jnp.float32))
    return stored_order_drawn(jnp.concatenate(pieces))


def draw_moment_two(key, part):
    key = jax.random.fold_in(key, 13)
    pieces = []
    for number, (name, shape, kind) in enumerate(layout_drawn(C, H, S, TA_HEADS, SA_HEADS)):
        sub = jax.random.fold_in(key, number)
        count = math.prod(shape)
        level = 0.05 / 0.95 * gradient_scale(kind) ** 2
        pieces.append(level * jax.random.uniform(sub, (count,), jnp.float32, 1.0, 4.0))
    return stored_order_drawn(jnp.concatenate(pieces))


def draw_lengths(key, part):
    key = jax.random.fold_in(key, 3)
    first, second = jax.random.split(key)
    drawn = jax.random.randint(first, (CROPS,), 3 * LENGTH // 4, LENGTH + 1)
    chosen = jax.random.randint(second, (), 0, CROPS)
    return jnp.where(jnp.arange(CROPS) == chosen, LENGTH, drawn).astype(jnp.int32)


def block_levels(key, extent, cuts, least, high):
    def one(position, shards_of):
        steps = jax.random.uniform(jax.random.fold_in(jax.random.fold_in(key, 6), position), (shards_of,), jnp.float32, least / len(cuts), high / len(cuts))
        return jnp.repeat(jnp.exp(steps), extent[position] // shards_of).reshape((-1,) + (1,) * (len(extent) - position - 1))

    level = one(*cuts[0])
    for cut in cuts[1:]:
        level = level * one(*cut)
    return level


def normal_values(own_key, extent, deviation, bound, cuts=(), kind=jnp.bfloat16):
    result = jax.random.normal(own_key, extent, jnp.float32) * deviation
    if len(cuts) > 0:
        result = block_levels(own_key, extent, cuts, -0.22, 0.18) * result
    return jnp.clip(result, min=-bound, max=bound).astype(kind)


def setup_inputs(seed: int = 0) -> dict:
    key_list = jax.random.split(jax.random.key(seed), 9)
    pair = normal_values(key_list[0], (CROPS, LENGTH, LENGTH, C), 1.0, 6.0, ((0, 4), (1, 8)))
    single = normal_values(key_list[1], (CROPS, LENGTH, S), 1.0, 6.0, ((0, 4), (1, 8)))
    lengths = draw_lengths(jax.random.fold_in(key_list[8], 71), 0)
    params = draw_params(jax.random.fold_in(key_list[8], 71), 0)
    moment_one = draw_moment_one(jax.random.fold_in(key_list[8], 71), 0)
    moment_two = draw_moment_two(jax.random.fold_in(key_list[8], 71), 0)
    pair_cotangent = normal_values(key_list[6], (CROPS, LENGTH, LENGTH, C), 1.0, 6.0, ((0, 4), (1, 8)))
    single_cotangent = normal_values(key_list[7], (CROPS, LENGTH, S), 1.0, 6.0, ((0, 4), (1, 8)))
    return dict(pair=pair, single=single, lengths=lengths, params=params, moment_one=moment_one, moment_two=moment_two, pair_cotangent=pair_cotangent, single_cotangent=single_cotangent)


EPSILON = 1e-05
MASKED = 1000000000.0
BETA_ONE = 0.9
BETA_TWO = 0.95
ADAM_EPS = 1e-08
CLIP = 1.0
row_block = 16

@jax.custom_vjp
def low(v):
    return lax.optimization_barrier(v.astype(jnp.bfloat16)).astype(jnp.float32)

@jax.custom_vjp
def low_back(v):
    return v

def low_keep(v):
    return (low(v), None)

def low_pass(kept, grad):
    return (grad,)

def back_keep(v):
    return (v, None)

def back_low(kept, grad):
    return (low(grad),)
low.defvjp(low_keep, low_pass)
low_back.defvjp(back_keep, back_low)

def layout(pair_width, hidden_width, single_width, tri_heads, att_heads):
    entries = []
    for prefix in ('outgoing', 'incoming'):
        entries += [(prefix + '_norm_gain', (pair_width,), 'gain'), (prefix + '_norm_bias', (pair_width,), 'bias'), (prefix + '_proj_gate', (pair_width, 4 * hidden_width), 'matrix'), (prefix + '_out_gain', (hidden_width,), 'gain'), (prefix + '_out_bias', (hidden_width,), 'bias'), (prefix + '_proj_out', (hidden_width, pair_width), 'matrix'), (prefix + '_gate_out', (pair_width, pair_width), 'matrix')]
    for prefix in ('starting', 'ending'):
        entries += [(prefix + '_norm_gain', (pair_width,), 'gain'), (prefix + '_norm_bias', (pair_width,), 'bias'), (prefix + '_qkvg', (pair_width, 4 * pair_width), 'matrix'), (prefix + '_bias_proj', (pair_width, tri_heads), 'matrix'), (prefix + '_output', (pair_width, pair_width), 'output')]
    entries += [('pair_norm_gain', (pair_width,), 'gain'), ('pair_norm_bias', (pair_width,), 'bias'), ('pair_up', (pair_width, 8 * pair_width), 'matrix'), ('pair_down', (4 * pair_width, pair_width), 'matrix'), ('attend_norm_gain', (single_width,), 'gain'), ('attend_norm_bias', (single_width,), 'bias'), ('attend_qkvg', (single_width, 4 * single_width), 'matrix'), ('attend_pair_gain', (pair_width,), 'gain'), ('attend_pair_bias', (pair_width,), 'bias'), ('attend_pair_proj', (pair_width, att_heads), 'matrix'), ('attend_output', (single_width, single_width), 'output'), ('single_norm_gain', (single_width,), 'gain'), ('single_norm_bias', (single_width,), 'bias'), ('single_up', (single_width, 8 * single_width), 'matrix'), ('single_down', (4 * single_width, single_width), 'matrix')]
    return entries

def logical_order(flat):
    return flat.reshape(-1, STRIDE).T.reshape(-1)

def stored_order(vector):
    return vector.reshape(STRIDE, -1).T.reshape(-1)

def rate_tables(entries):
    rates = []
    decays = []
    for name, shape, kind in entries:
        count = math.prod(shape)
        if kind in ('gain', 'bias'):
            rates.append(np.full(count, 0.5, np.float32))
            decays.append(np.zeros(count, np.float32))
        else:
            rates.append(np.full(count, 2.0 / math.sqrt(shape[0]), np.float32))
            decays.append(np.full(count, 0.01, np.float32))
    rates = np.concatenate(rates)
    decays = np.concatenate(decays)
    return (rates.reshape(STRIDE, -1).T.reshape(-1), decays.reshape(STRIDE, -1).T.reshape(-1))

def unpack(flat, entries):
    pieces = {}
    offset = 0
    for name, shape, kind in entries:
        count = math.prod(shape)
        pieces[name] = flat[offset:offset + count].reshape(shape)
        offset += count
    return pieces

def layer_norm(values, gain, shift):
    centred = values - lax.optimization_barrier(jnp.mean(values, axis=-1, keepdims=True))
    spread = lax.optimization_barrier(jnp.mean(centred * centred, axis=-1, keepdims=True))
    return centred * lax.rsqrt(spread + EPSILON) * gain + shift

def matmul(left, right):
    return jnp.dot(left, right, precision=lax.Precision.HIGHEST)

def gated_pair(project, pair_mask):
    half = project.shape[-1] // 2
    return project[..., :half] * jax.nn.sigmoid(project[..., half:]) * pair_mask[..., None]

def swiglu(hidden):
    half = hidden.shape[-1] // 2
    return jax.nn.silu(hidden[..., :half]) * hidden[..., half:]

def triangle_mult(pair, weights, prefix, mask, incoming):
    lowered = low(layer_norm(pair, weights[prefix + '_norm_gain'], weights[prefix + '_norm_bias']))
    source = low_back(lowered) if incoming else lowered
    project = low_back(matmul(source, weights[prefix + '_proj_gate']))
    product = low(gated_pair(project, mask[:, None] * mask[None, :]))
    half = product.shape[-1] // 2
    first = product[..., :half]
    second = product[..., half:]
    if incoming:
        tri = jnp.einsum('kih,kjh->ijh', first, second, precision=lax.Precision.HIGHEST)
        tri = low(low_back(tri))
    else:
        tri = jnp.einsum('ikh,jkh->ijh', first, second, precision=lax.Precision.HIGHEST)
        tri = low_back(tri)
    out_low = low(layer_norm(tri, weights[prefix + '_out_gain'], weights[prefix + '_out_bias']))
    output = low_back(matmul(out_low, weights[prefix + '_proj_out']))
    gate_out = low_back(matmul(lowered, weights[prefix + '_gate_out']))
    return output * jax.nn.sigmoid(gate_out)

def row_attention(query, key, value, bias, mask, scale):
    scores = jnp.einsum('bjhd,bkhd->bhjk', query, key, precision=lax.Precision.HIGHEST) * scale
    scores = low_back(scores + bias[None] + ((mask - 1.0) * MASKED)[None, None, None, :])
    probs = low(jax.nn.softmax(scores, axis=-1))
    return jnp.einsum('bhjk,bkhd->bjhd', probs, value, precision=lax.Precision.HIGHEST)

def triangle_attention(pair, weights, prefix, mask, ending):
    lowered = low(layer_norm(pair, weights[prefix + '_norm_gain'], weights[prefix + '_norm_bias']))
    if ending:
        lowered = jnp.swapaxes(low_back(lowered), 0, 1)
    width = pair.shape[-1]
    size = width // TA_HEADS
    project = low_back(matmul(lowered, weights[prefix + '_qkvg']))
    shaped = lambda part: low(part).reshape(LENGTH // row_block, row_block, LENGTH, TA_HEADS, size)
    query = shaped(project[..., :width])
    key = shaped(project[..., width:2 * width])
    value = shaped(project[..., 2 * width:3 * width])
    gate = project[..., 3 * width:]
    bias = low(low_back(matmul(lowered, weights[prefix + '_bias_proj']))).transpose(2, 0, 1)
    scale = size ** (-0.5)

    def block(items):
        return row_attention(items[0], items[1], items[2], bias, mask, scale)
    mixed = lax.map(jax.checkpoint(block), (query, key, value))
    mixed = low_back(mixed.reshape(LENGTH, LENGTH, width))
    gated = mixed * jax.nn.sigmoid(gate)
    if ending:
        gated = jnp.swapaxes(low(low_back(gated)), 0, 1)
    else:
        gated = low(gated)
    return low_back(matmul(gated, weights[prefix + '_output']))

def transition(values, weights, prefix):
    lowered = low(layer_norm(values, weights[prefix + '_norm_gain'], weights[prefix + '_norm_bias']))
    hidden = low_back(matmul(lowered, weights[prefix + '_up']))
    mixed = low(swiglu(hidden))
    return low_back(matmul(mixed, weights[prefix + '_down']))

def single_attention(single, pair, weights, mask):
    lowered = low(layer_norm(single, weights['attend_norm_gain'], weights['attend_norm_bias']))
    project = low_back(matmul(lowered, weights['attend_qkvg']))
    query = low(project[:, :S]).reshape(LENGTH, SA_HEADS, SA_DIM)
    key = low(project[:, S:2 * S]).reshape(LENGTH, SA_HEADS, SA_DIM)
    value = low(project[:, 2 * S:3 * S]).reshape(LENGTH, SA_HEADS, SA_DIM)
    gate = project[:, 3 * S:]
    pair_low = low(layer_norm(pair, weights['attend_pair_gain'], weights['attend_pair_bias']))
    bias = matmul(pair_low, weights['attend_pair_proj']).transpose(2, 0, 1)
    scores = jnp.einsum('ihd,jhd->hij', query, key, precision=lax.Precision.HIGHEST) * SA_DIM ** (-0.5)
    scores = low_back(scores + bias + ((mask - 1.0) * MASKED)[None, None, :])
    probs = low(jax.nn.softmax(scores, axis=-1))
    mixed = jnp.einsum('hij,jhd->ihd', probs, value, precision=lax.Precision.HIGHEST)
    mixed = low_back(mixed.reshape(LENGTH, S))
    gated = low(mixed * jax.nn.sigmoid(gate))
    return low_back(matmul(gated, weights['attend_output']))

def block_forward(flat, pair, single, mask):
    weights = unpack(logical_order(low(flat)), layout(C, H, S, TA_HEADS, SA_HEADS))
    pair = pair + jax.checkpoint(lambda p, w: triangle_mult(p, w, 'outgoing', mask, False))(pair, weights)
    pair = pair + jax.checkpoint(lambda p, w: triangle_mult(p, w, 'incoming', mask, True))(pair, weights)
    pair = pair + jax.checkpoint(lambda p, w: triangle_attention(p, w, 'starting', mask, False))(pair, weights)
    pair = pair + jax.checkpoint(lambda p, w: triangle_attention(p, w, 'ending', mask, True))(pair, weights)
    pair = pair + jax.checkpoint(lambda p, w: transition(p, w, 'pair'))(pair, weights)
    single = single + jax.checkpoint(lambda s, p, w: single_attention(s, p, w, mask))(single, pair, weights)
    single = single + transition(single, weights, 'single')
    return (pair, single)

def reference(pair, single, lengths, params, moment_one, moment_two, pair_cotangent, single_cotangent):
    positions = jnp.arange(LENGTH, dtype=jnp.int32)

    def crop_step(total, items):
        pair_crop, single_crop, length, pair_back, single_back = items
        mask = (positions < length).astype(jnp.float32)

        def forward(flat, pair_in, single_in):
            return block_forward(flat, pair_in, single_in, mask)
        outputs, pullback = jax.vjp(forward, params, pair_crop.astype(jnp.float32), single_crop.astype(jnp.float32))
        grad_flat, grad_pair, grad_single = pullback((pair_back.astype(jnp.float32), single_back.astype(jnp.float32)))
        return (total + grad_flat, (outputs[0].astype(jnp.bfloat16), outputs[1].astype(jnp.bfloat16), grad_pair, grad_single))
    total, results = lax.scan(crop_step, jnp.zeros((PARAMS,), jnp.float32), (pair, single, lengths, pair_cotangent, single_cotangent))
    pair_out, single_out, pair_grad, single_grad = results
    clip_norm = jnp.sqrt(jnp.sum(total * total))
    clipped = total * (CLIP / jnp.maximum(clip_norm, CLIP))
    new_first = BETA_ONE * moment_one + (1.0 - BETA_ONE) * clipped
    new_second = BETA_TWO * moment_two + (1.0 - BETA_TWO) * clipped * clipped
    rates, decays = rate_tables(layout(C, H, S, TA_HEADS, SA_HEADS))
    first_hat = new_first / (1.0 - BETA_ONE ** STEP)
    second_hat = new_second / (1.0 - BETA_TWO ** STEP)
    new_params = params - jnp.asarray(rates) * (first_hat / (jnp.sqrt(second_hat) + ADAM_EPS) + jnp.asarray(decays) * params)
    return (pair_out, single_out, pair_grad, single_grad, new_params, new_first, new_second, clip_norm)
```

```python
import functools
import math

import jax
import jax.numpy as jnp
import numpy as np
from jax import lax
from jax.experimental import pallas as pl
from jax.experimental.pallas import tpu as pltpu
from jax.sharding import PartitionSpec as P

C = 128
H = 128
S = 384
TA_HEADS = 4
SA_HEADS = 16
STEP = 10
STRIDE = 128
LENGTH = 256

OUTGOING, INCOMING, STARTING, ENDING, PAIR, ATTEND, SINGLE = range(7)
(
    NORM_GAIN,
    NORM_BIAS,
    PROJ_GATE,
    OUT_GAIN,
    OUT_BIAS,
    PROJ_OUT,
    GATE_OUT,
    QKVG,
    BIAS_PROJ,
    OUTPUT,
    UP,
    DOWN,
    PAIR_GAIN,
    PAIR_BIAS,
    PAIR_PROJ,
    COLS,
    BIAS_W,
    BIAS_T,
    VECTORS,
    T,
) = range(7, 27)


EPSILON = 1e-05
MASKED = 1000000000.0
BETA_ONE = 0.9
BETA_TWO = 0.95
ADAM_EPS = 1e-08
CLIP = 1.0


def layout(pair_width, hidden_width, single_width, tri_heads, att_heads):
    entries = []
    for prefix in (OUTGOING, INCOMING):
        entries += [
            ((prefix, NORM_GAIN), (pair_width,)),
            ((prefix, NORM_BIAS), (pair_width,)),
            ((prefix, PROJ_GATE), (pair_width, 4 * hidden_width)),
            ((prefix, OUT_GAIN), (hidden_width,)),
            ((prefix, OUT_BIAS), (hidden_width,)),
            ((prefix, PROJ_OUT), (hidden_width, pair_width)),
            ((prefix, GATE_OUT), (pair_width, pair_width)),
        ]
    for prefix in (STARTING, ENDING):
        entries += [
            ((prefix, NORM_GAIN), (pair_width,)),
            ((prefix, NORM_BIAS), (pair_width,)),
            ((prefix, QKVG), (pair_width, 4 * pair_width)),
            ((prefix, BIAS_PROJ), (pair_width, tri_heads)),
            ((prefix, OUTPUT), (pair_width, pair_width)),
        ]
    entries += [
        ((PAIR, NORM_GAIN), (pair_width,)),
        ((PAIR, NORM_BIAS), (pair_width,)),
        ((PAIR, UP), (pair_width, 8 * pair_width)),
        ((PAIR, DOWN), (4 * pair_width, pair_width)),
        ((ATTEND, NORM_GAIN), (single_width,)),
        ((ATTEND, NORM_BIAS), (single_width,)),
        ((ATTEND, QKVG), (single_width, 4 * single_width)),
        ((ATTEND, PAIR_GAIN), (pair_width,)),
        ((ATTEND, PAIR_BIAS), (pair_width,)),
        ((ATTEND, PAIR_PROJ), (pair_width, att_heads)),
        ((ATTEND, OUTPUT), (single_width, single_width)),
        ((SINGLE, NORM_GAIN), (single_width,)),
        ((SINGLE, NORM_BIAS), (single_width,)),
        ((SINGLE, UP), (single_width, 8 * single_width)),
        ((SINGLE, DOWN), (4 * single_width, single_width)),
    ]
    return entries


def logical_order(flat):
    return flat.reshape(-1, STRIDE).T.reshape(-1)


def stored_order(vector):
    return vector.reshape(STRIDE, -1).T.reshape(-1)


def rate_tables(entries):
    rates = []
    decays = []
    for name, shape in entries:
        count = math.prod(shape)
        if len(shape) == 1:
            rates.append(np.full(count, 0.5, np.float32))
            decays.append(np.zeros(count, np.float32))
        else:
            rates.append(np.full(count, 2.0 / math.sqrt(shape[0]), np.float32))
            decays.append(np.full(count, 0.01, np.float32))
    rates = np.concatenate(rates)
    decays = np.concatenate(decays)
    return (rates.reshape(STRIDE, -1).T.reshape(-1), decays.reshape(STRIDE, -1).T.reshape(-1))


def unpack(flat, entries):
    pieces = {}
    offset = 0
    for name, shape in entries:
        count = math.prod(shape)
        pieces[name] = flat[offset : offset + count].reshape(shape)
        offset += count
    return pieces


def layer_norm(values, gain, shift):
    centred = values - jnp.mean(values, axis=-1, keepdims=True)
    spread = jnp.mean(centred * centred, axis=-1, keepdims=True)
    return centred * lax.rsqrt(spread + EPSILON) * gain + shift


def norm_backward(values, gain, shift, grad):
    _, pullback = jax.vjp(layer_norm, values, gain, shift)
    return pullback(grad)


def norm_pair(weights, prefix):
    return (
        weights[(prefix, NORM_GAIN)].astype(jnp.float32),
        weights[(prefix, NORM_BIAS)].astype(jnp.float32),
    )


def gated_pair(project, pair_mask):
    half = project.shape[-1] // 2
    return project[..., :half] * jax.nn.sigmoid(project[..., half:]) * pair_mask[..., None]


def gated_output(values, gate):
    return values * jax.nn.sigmoid(gate)


def swiglu(hidden):
    half = hidden.shape[-1] // 2
    return jax.nn.silu(hidden[..., :half]) * hidden[..., half:]


def matmul(left, right):
    return jnp.dot(left, right, preferred_element_type=jnp.float32)


def outer_sum(left, right):
    return jnp.einsum(
        "nc,nd->cd",
        left.reshape(-1, left.shape[-1]),
        right.reshape(-1, right.shape[-1]),
        preferred_element_type=jnp.float32,
    )


def flip(values):
    moved = lax.all_to_all(values, "row", split_axis=1, concat_axis=0, tiled=True)
    return jnp.swapaxes(moved, 0, 1)


def channel_forward(first, second, incoming):
    whole_first, whole_second = (
        lax.all_to_all(first, "row", split_axis=2, concat_axis=0, tiled=True),
        lax.all_to_all(second, "row", split_axis=2, concat_axis=0, tiled=True),
    )
    if incoming:
        local_tri = jnp.einsum(
            "kih,kjh->ijh", whole_first, whole_second, preferred_element_type=jnp.float32
        )
        local_tri = local_tri.astype(jnp.bfloat16).astype(jnp.float32)
    else:
        local_tri = jnp.einsum(
            "ikh,jkh->ijh", whole_first, whole_second, preferred_element_type=jnp.float32
        )
    tri = lax.all_to_all(
        local_tri.astype(jnp.bfloat16), "row", split_axis=0, concat_axis=2, tiled=True
    ).astype(local_tri.dtype)
    return (tri, whole_first, whole_second)


def channel_backward(grad_tri, whole_first, whole_second, incoming):
    whole_grad = lax.all_to_all(grad_tri, "row", split_axis=2, concat_axis=0, tiled=True)
    if incoming:
        grad_a = jnp.einsum(
            "ijh,kjh->kih", whole_grad, whole_second, preferred_element_type=jnp.float32
        )
        grad_b = jnp.einsum(
            "ijh,kih->kjh", whole_grad, whole_first, preferred_element_type=jnp.float32
        )
    else:
        grad_a = jnp.einsum(
            "ijh,jkh->ikh", whole_grad, whole_second, preferred_element_type=jnp.float32
        )
        grad_b = jnp.einsum(
            "ijh,ikh->jkh", whole_grad, whole_first, preferred_element_type=jnp.float32
        )
    return (
        lax.all_to_all(
            grad_a.astype(jnp.bfloat16), "row", split_axis=0, concat_axis=2, tiled=True
        ).astype(grad_a.dtype),
        lax.all_to_all(
            grad_b.astype(jnp.bfloat16), "row", split_axis=0, concat_axis=2, tiled=True
        ).astype(grad_b.dtype),
    )


def triangle_forward(state, pair_mask, weights, prefix, incoming):
    gain, shift = norm_pair(weights, prefix)
    lowered = layer_norm(state, gain, shift).astype(jnp.bfloat16)
    project = matmul(lowered, weights[(prefix, PROJ_GATE)])
    product = gated_pair(project, pair_mask).astype(jnp.bfloat16)
    half = product.shape[-1] // 2
    tri, own, other = channel_forward(product[..., :half], product[..., half:], incoming)
    out_gain = weights[(prefix, OUT_GAIN)].astype(jnp.float32)
    out_shift = weights[(prefix, OUT_BIAS)].astype(jnp.float32)
    out_low = layer_norm(tri, out_gain, out_shift).astype(jnp.bfloat16)
    output = matmul(out_low, weights[(prefix, PROJ_OUT)])
    gate_out = matmul(lowered, weights[(prefix, GATE_OUT)])
    update = gated_output(output, gate_out)
    return (update, (state, lowered, lowered, project, own, other, tri, out_low, output, gate_out))


def triangle_backward(saved, grad_update, pair_mask, weights, prefix, incoming, grads):
    state, lowered, framed, project, own, other, tri, out_low, output, gate_out = saved
    _, pullback = jax.vjp(gated_output, output, gate_out)
    grad_output, grad_gate = pullback(grad_update)
    grad_output = grad_output.astype(jnp.bfloat16)
    grad_gate = grad_gate.astype(jnp.bfloat16)
    grads[(prefix, PROJ_OUT)] = outer_sum(out_low, grad_output)
    grads[(prefix, GATE_OUT)] = outer_sum(lowered, grad_gate)
    grad_normed = matmul(grad_output, weights[(prefix, PROJ_OUT)].T)
    out_gain = weights[(prefix, OUT_GAIN)].astype(jnp.float32)
    out_shift = weights[(prefix, OUT_BIAS)].astype(jnp.float32)
    grad_tri, grads[(prefix, OUT_GAIN)], grads[(prefix, OUT_BIAS)] = norm_backward(
        tri, out_gain, out_shift, grad_normed
    )
    grad_tri = grad_tri.astype(jnp.bfloat16)
    grad_first, grad_second = channel_backward(grad_tri, own, other, incoming)
    _, pullback = jax.vjp(lambda values: gated_pair(values, pair_mask), project)
    (grad_project,) = pullback(jnp.concatenate([grad_first, grad_second], axis=-1))
    grad_project = grad_project.astype(jnp.bfloat16)
    grads[(prefix, PROJ_GATE)] = outer_sum(framed, grad_project)
    grad_framed = matmul(grad_project, weights[(prefix, PROJ_GATE)].T)
    if incoming:
        grad_framed = grad_framed.astype(jnp.bfloat16).astype(jnp.float32)
    grad_lowered = grad_framed + matmul(grad_gate, weights[(prefix, GATE_OUT)].T)
    gain, shift = norm_pair(weights, prefix)
    grad_state, grads[(prefix, NORM_GAIN)], grads[(prefix, NORM_BIAS)] = norm_backward(
        state, gain, shift, grad_lowered
    )
    return grad_state


def row_scores(query, key, bias, penalty, scale):
    scores = jnp.einsum("jhd,khd->hjk", query, key, preferred_element_type=jnp.float32) * scale
    return scores + bias.astype(jnp.float32) + penalty[None, None, :]


def attention_forward(state, penalty, weights, prefix, ending):
    gain, shift = norm_pair(weights, prefix)
    lowered = layer_norm(state, gain, shift).astype(jnp.bfloat16)
    framed = flip(lowered) if ending else lowered
    rows, length, width = framed.shape
    size = width // TA_HEADS
    scale = size ** (-0.5)
    qkvg = matmul(framed, weights[(prefix, QKVG)])
    queries = qkvg[..., :width].astype(jnp.bfloat16).reshape(rows, length, TA_HEADS, size)
    keys = qkvg[..., width : 2 * width].astype(jnp.bfloat16).reshape(rows, length, TA_HEADS, size)
    values = (
        qkvg[..., 2 * width : 3 * width].astype(jnp.bfloat16).reshape(rows, length, TA_HEADS, size)
    )
    gate = qkvg[..., 3 * width :]
    local_bias = (
        matmul(framed, weights[(prefix, BIAS_PROJ)]).astype(jnp.bfloat16).transpose(2, 0, 1)
    )
    bias = lax.all_gather(local_bias, "row", axis=1, tiled=True)

    def forward_row(items):
        query, key, value = items
        scores = row_scores(query, key, bias, penalty, scale)
        top = jnp.max(scores, axis=-1, keepdims=True)
        shifted = jnp.exp(scores - top)
        total = jnp.sum(shifted, axis=-1, keepdims=True)
        probs = (shifted / total).astype(jnp.bfloat16)
        mixed = jnp.einsum("hjk,khd->jhd", probs, value, preferred_element_type=jnp.float32)
        return (mixed, top[..., 0] + jnp.log(total[..., 0]))

    mixed, log_totals = lax.map(forward_row, (queries, keys, values))
    mixed = mixed.reshape(rows, length, width)
    gated_low = gated_output(mixed, gate).astype(jnp.bfloat16)
    returned = flip(gated_low) if ending else gated_low
    update = matmul(returned, weights[(prefix, OUTPUT)])
    return (update, (state, framed, queries, keys, values, gate, bias, mixed, log_totals, returned))


def attention_backward(saved, grad_update, penalty, weights, prefix, ending, grads):
    state, framed, queries, keys, values, gate, bias, mixed, log_totals, returned = saved
    rows, length, width = framed.shape
    size = width // TA_HEADS
    scale = size ** (-0.5)
    grad_low = grad_update.astype(jnp.bfloat16)
    grads[(prefix, OUTPUT)] = outer_sum(returned, grad_low)
    grad_gated = matmul(grad_low, weights[(prefix, OUTPUT)].T)
    if ending:
        grad_gated = flip(grad_gated.astype(jnp.bfloat16)).astype(jnp.float32)
    _, pullback = jax.vjp(gated_output, mixed, gate)
    grad_mixed, grad_gate = pullback(grad_gated)
    grad_mixed = grad_mixed.astype(jnp.bfloat16).reshape(rows, length, TA_HEADS, size)

    def back_row(carry, items):
        query, key, value, log_total, grad_row = items
        scores = row_scores(query, key, bias, penalty, scale)
        probs = jnp.exp(scores - log_total[..., None])
        grad_probs = jnp.einsum("jhd,khd->hjk", grad_row, value, preferred_element_type=jnp.float32)
        delta = jnp.sum(probs * grad_probs, axis=-1, keepdims=True)
        grad_scores = (probs * (grad_probs - delta)).astype(jnp.bfloat16)
        grad_query = (
            jnp.einsum("hjk,khd->jhd", grad_scores, key, preferred_element_type=jnp.float32) * scale
        )
        grad_key = (
            jnp.einsum("hjk,jhd->khd", grad_scores, query, preferred_element_type=jnp.float32)
            * scale
        )
        grad_value = jnp.einsum(
            "hjk,jhd->khd", probs.astype(jnp.bfloat16), grad_row, preferred_element_type=jnp.float32
        )
        return (carry + grad_scores.astype(jnp.float32), (grad_query, grad_key, grad_value))

    empty = jnp.zeros(bias.shape, jnp.float32)
    grad_bias, (grad_query, grad_key, grad_value) = lax.scan(
        back_row, empty, (queries, keys, values, log_totals, grad_mixed)
    )
    grad_bias = lax.psum_scatter(grad_bias, "row", scatter_dimension=1, tiled=True)
    grad_bias = grad_bias.transpose(1, 2, 0).astype(jnp.bfloat16)
    grad_qkvg = jnp.concatenate(
        [
            grad_query.reshape(rows, length, width),
            grad_key.reshape(rows, length, width),
            grad_value.reshape(rows, length, width),
            grad_gate,
        ],
        axis=-1,
    ).astype(jnp.bfloat16)
    grads[(prefix, QKVG)] = outer_sum(framed, grad_qkvg)
    grads[(prefix, BIAS_PROJ)] = outer_sum(framed, grad_bias)
    grad_framed = matmul(grad_qkvg, weights[(prefix, QKVG)].T) + matmul(
        grad_bias, weights[(prefix, BIAS_PROJ)].T
    )
    if ending:
        grad_framed = flip(grad_framed.astype(jnp.bfloat16)).astype(jnp.float32)
    gain, shift = norm_pair(weights, prefix)
    grad_state, grads[(prefix, NORM_GAIN)], grads[(prefix, NORM_BIAS)] = norm_backward(
        state, gain, shift, grad_framed
    )
    return grad_state


def transition_forward(state, weights, prefix):
    gain, shift = norm_pair(weights, prefix)
    lowered = layer_norm(state, gain, shift).astype(jnp.bfloat16)
    hidden = matmul(lowered, weights[(prefix, UP)])
    mixed_low = swiglu(hidden).astype(jnp.bfloat16)
    update = matmul(mixed_low, weights[(prefix, DOWN)])
    return (update, (state, lowered, hidden, mixed_low))


def transition_backward(saved, grad_update, weights, prefix, grads):
    state, lowered, hidden, mixed_low = saved
    grad_low = grad_update.astype(jnp.bfloat16)
    grads[(prefix, DOWN)] = outer_sum(mixed_low, grad_low)
    grad_mixed = matmul(grad_low, weights[(prefix, DOWN)].T)
    _, pullback = jax.vjp(swiglu, hidden)
    (grad_hidden,) = pullback(grad_mixed)
    grad_hidden = grad_hidden.astype(jnp.bfloat16)
    grads[(prefix, UP)] = outer_sum(lowered, grad_hidden)
    grad_lowered = matmul(grad_hidden, weights[(prefix, UP)].T)
    gain, shift = norm_pair(weights, prefix)
    grad_state, grads[(prefix, NORM_GAIN)], grads[(prefix, NORM_BIAS)] = norm_backward(
        state, gain, shift, grad_lowered
    )
    return grad_state


def single_forward(single_state, pair_state, penalty, weights):
    gain, shift = norm_pair(weights, ATTEND)
    lowered = layer_norm(single_state, gain, shift).astype(jnp.bfloat16)
    rows, width = lowered.shape
    size = width // SA_HEADS
    qkvg = matmul(lowered, weights[(ATTEND, QKVG)])
    query = qkvg[:, :width].astype(jnp.bfloat16).reshape(rows, SA_HEADS, size)
    key = qkvg[:, width : 2 * width].astype(jnp.bfloat16)
    value = qkvg[:, 2 * width : 3 * width].astype(jnp.bfloat16)
    gate = qkvg[:, 3 * width :]
    keys_all, values_all = (
        lax.all_gather(key, "row", axis=0, tiled=True),
        lax.all_gather(value, "row", axis=0, tiled=True),
    )
    keys_all = keys_all.reshape(-1, SA_HEADS, size)
    values_all = values_all.reshape(-1, SA_HEADS, size)
    pair_gain = weights[(ATTEND, PAIR_GAIN)].astype(jnp.float32)
    pair_shift = weights[(ATTEND, PAIR_BIAS)].astype(jnp.float32)
    pair_low = layer_norm(pair_state, pair_gain, pair_shift).astype(jnp.bfloat16)
    bias = matmul(pair_low, weights[(ATTEND, PAIR_PROJ)]).transpose(2, 0, 1)
    scores = jnp.einsum(
        "ihd,jhd->hij", query, keys_all, preferred_element_type=jnp.float32
    ) * size ** (-0.5)
    scores = scores + bias + penalty[None, None, :]
    probs = jax.nn.softmax(scores, axis=-1)
    probs_low = probs.astype(jnp.bfloat16)
    mixed = jnp.einsum(
        "hij,jhd->ihd", probs_low, values_all, preferred_element_type=jnp.float32
    ).reshape(rows, width)
    gated_low = gated_output(mixed, gate).astype(jnp.bfloat16)
    update = matmul(gated_low, weights[(ATTEND, OUTPUT)])
    return (
        update,
        (
            single_state,
            pair_state,
            lowered,
            query,
            keys_all,
            values_all,
            gate,
            pair_low,
            probs,
            probs_low,
            mixed,
            gated_low,
        ),
    )


def single_backward(saved, grad_update, weights, grads):
    (
        single_state,
        pair_state,
        lowered,
        query,
        keys_all,
        values_all,
        gate,
        pair_low,
        probs,
        probs_low,
        mixed,
        gated_low,
    ) = saved
    rows, width = lowered.shape
    size = width // SA_HEADS
    scale = size ** (-0.5)
    grad_low = grad_update.astype(jnp.bfloat16)
    grads[(ATTEND, OUTPUT)] = outer_sum(gated_low, grad_low)
    grad_gated = matmul(grad_low, weights[(ATTEND, OUTPUT)].T)
    _, pullback = jax.vjp(gated_output, mixed, gate)
    grad_mixed, grad_gate = pullback(grad_gated)
    grad_mixed = grad_mixed.astype(jnp.bfloat16).reshape(rows, SA_HEADS, size)
    grad_probs = jnp.einsum(
        "ihd,jhd->hij", grad_mixed, values_all, preferred_element_type=jnp.float32
    )
    delta = jnp.sum(probs * grad_probs, axis=-1, keepdims=True)
    grad_scores = (probs * (grad_probs - delta)).astype(jnp.bfloat16)
    grad_query = (
        jnp.einsum("hij,jhd->ihd", grad_scores, keys_all, preferred_element_type=jnp.float32)
        * scale
    )
    key_part = (
        jnp.einsum("hij,ihd->jhd", grad_scores, query, preferred_element_type=jnp.float32) * scale
    )
    value_part = jnp.einsum(
        "hij,ihd->jhd", probs_low, grad_mixed, preferred_element_type=jnp.float32
    )
    grad_key, grad_value = (
        lax.psum_scatter(key_part.reshape(-1, width), "row", scatter_dimension=0, tiled=True),
        lax.psum_scatter(value_part.reshape(-1, width), "row", scatter_dimension=0, tiled=True),
    )
    grad_qkvg = jnp.concatenate(
        [grad_query.reshape(rows, width), grad_key, grad_value, grad_gate], axis=-1
    ).astype(jnp.bfloat16)
    grads[(ATTEND, QKVG)] = outer_sum(lowered, grad_qkvg)
    grad_lowered = matmul(grad_qkvg, weights[(ATTEND, QKVG)].T)
    gain, shift = norm_pair(weights, ATTEND)
    grad_single, grads[(ATTEND, NORM_GAIN)], grads[(ATTEND, NORM_BIAS)] = norm_backward(
        single_state, gain, shift, grad_lowered
    )
    grad_bias = grad_scores.transpose(1, 2, 0)
    grads[(ATTEND, PAIR_PROJ)] = outer_sum(pair_low, grad_bias)
    grad_pair_low = matmul(grad_bias, weights[(ATTEND, PAIR_PROJ)].T)
    pair_gain = weights[(ATTEND, PAIR_GAIN)].astype(jnp.float32)
    pair_shift = weights[(ATTEND, PAIR_BIAS)].astype(jnp.float32)
    grad_pair, grads[(ATTEND, PAIR_GAIN)], grads[(ATTEND, PAIR_BIAS)] = norm_backward(
        pair_state, pair_gain, pair_shift, grad_pair_low
    )
    return (grad_single, grad_pair)


def shards(pair, single, lengths, params, moment_one, moment_two, pair_cotangent, single_cotangent):
    entries = layout(C, H, S, TA_HEADS, SA_HEADS)
    full = lax.all_gather(params.astype(jnp.bfloat16), "row", axis=0, tiled=True)
    weights = unpack(logical_order(full), entries)
    rows = pair.shape[1]
    length = pair.shape[2]
    first_row = lax.axis_index("row") * rows
    mask = (jnp.arange(length, dtype=jnp.int32) < lengths[0]).astype(jnp.float32)
    mask_rows = lax.dynamic_slice_in_dim(mask, first_row, rows)
    pair_mask = mask_rows[:, None] * mask[None, :]
    penalty = (mask - 1.0) * MASKED
    state = pair[0].astype(jnp.float32)
    saved = {}
    for prefix, incoming in ((OUTGOING, False), (INCOMING, True)):
        update, saved[prefix] = triangle_forward(state, pair_mask, weights, prefix, incoming)
        state = state + update
    for prefix, ending in ((STARTING, False), (ENDING, True)):
        update, saved[prefix] = attention_forward(state, penalty, weights, prefix, ending)
        state = state + update
    update, saved[PAIR] = transition_forward(state, weights, PAIR)
    pair_final = state + update
    single_state = single[0].astype(jnp.float32)
    update, saved[ATTEND] = single_forward(single_state, pair_final, penalty, weights)
    single_mid = single_state + update
    update, saved[SINGLE] = transition_forward(single_mid, weights, SINGLE)
    single_final = single_mid + update
    grads = {}
    grad_single = single_cotangent[0].astype(jnp.float32)
    grad_single = grad_single + transition_backward(
        saved[SINGLE], grad_single, weights, SINGLE, grads
    )
    from_single, from_pair = single_backward(saved[ATTEND], grad_single, weights, grads)
    grad_single = grad_single + from_single
    grad_pair = pair_cotangent[0].astype(jnp.float32) + from_pair
    grad_pair = grad_pair + transition_backward(saved[PAIR], grad_pair, weights, PAIR, grads)
    for prefix, ending in ((ENDING, True), (STARTING, False)):
        grad_pair = grad_pair + attention_backward(
            saved[prefix], grad_pair, penalty, weights, prefix, ending, grads
        )
    for prefix, incoming in ((INCOMING, True), (OUTGOING, False)):
        grad_pair = grad_pair + triangle_backward(
            saved[prefix], grad_pair, pair_mask, weights, prefix, incoming, grads
        )
    flat = stored_order(jnp.concatenate([grads[name].reshape(-1) for name, shape in entries]))
    shard_size = params.shape[0]
    row_index = lax.axis_index("row")
    total = lax.psum(flat, ("crop", "row"))
    shard = lax.dynamic_slice_in_dim(total, row_index * shard_size, shard_size)
    norm_squared = jnp.sum(total * total)
    clip_norm = jnp.sqrt(norm_squared)
    clipped = shard * (CLIP / jnp.maximum(clip_norm, CLIP))
    new_first = BETA_ONE * moment_one + (1.0 - BETA_ONE) * clipped
    new_second = BETA_TWO * moment_two + (1.0 - BETA_TWO) * clipped * clipped
    rates, decays = rate_tables(entries)
    rate_shard = lax.dynamic_slice_in_dim(jnp.asarray(rates), row_index * shard_size, shard_size)
    decay_shard = lax.dynamic_slice_in_dim(jnp.asarray(decays), row_index * shard_size, shard_size)
    first_hat = new_first / (1.0 - BETA_ONE**STEP)
    second_hat = new_second / (1.0 - BETA_TWO**STEP)
    new_params = params - rate_shard * (
        first_hat / (jnp.sqrt(second_hat) + ADAM_EPS) + decay_shard * params
    )
    return (
        pair_final.astype(jnp.bfloat16)[None],
        single_final.astype(jnp.bfloat16)[None],
        grad_pair[None],
        grad_single[None],
        new_params,
        new_first,
        new_second,
        clip_norm,
    )


F32 = jnp.float32
BF16 = jnp.bfloat16
LOG2E = 1.4426950408889634
VMEM_LIMIT = 56 * 1024 * 1024


def mm(left, right):
    return lax.dot_general(left, right, (((1,), (0,)), ((), ())), preferred_element_type=F32)


def mm_nt(left, right):
    return lax.dot_general(left, right, (((1,), (1,)), ((), ())), preferred_element_type=F32)


def mm_tn(left, right):
    return lax.dot_general(left, right, (((0,), (0,)), ((), ())), preferred_element_type=F32)


def standardize(values):
    centred = values - jnp.mean(values, axis=0, keepdims=True)
    spread = jnp.mean(centred * centred, axis=0, keepdims=True)
    inverse = lax.rsqrt(spread + EPSILON)
    return centred * inverse, inverse


def standardize_back(unit, inverse, grad_unit):
    first = jnp.mean(grad_unit, axis=0, keepdims=True)
    second = jnp.mean(grad_unit * unit, axis=0, keepdims=True)
    return inverse * (grad_unit - first - unit * second)


def sigmoid(values):
    return 0.5 * jnp.tanh(0.5 * values) + 0.5


def column(ref, index):
    return ref[:, index : index + 1]


def live_pair(info, alive, row):
    return jnp.where(info[row] > 0, alive[0:1], 0.0)


def each_row(count, body):
    def step(index, carry):
        body(index)
        return carry

    lax.fori_loop(0, count, step, 0)


def spec_full(shape):
    return pl.BlockSpec(shape, lambda step: (0,) * len(shape))


def spec_rows(shape, block, axis):
    sizes = tuple(block if place == axis else size for place, size in enumerate(shape))
    return pl.BlockSpec(
        sizes, lambda step: tuple(step if place == axis else 0 for place in range(len(shape)))
    )


def run_rows(kernel, name, steps, ins, outs, scratch):
    in_specs = []
    for array, axis in ins:
        if axis == "smem":
            in_specs.append(pl.BlockSpec(memory_space=pltpu.SMEM))
        elif axis is None:
            in_specs.append(spec_full(array.shape))
        else:
            in_specs.append(spec_rows(array.shape, array.shape[axis] // steps, axis))
    out_specs = []
    for shape, dtype, axis in outs:
        if axis is None:
            out_specs.append(spec_full(shape))
        else:
            out_specs.append(spec_rows(shape, shape[axis] // steps, axis))
    return pl.pallas_call(
        kernel,
        grid=(steps,),
        in_specs=in_specs,
        out_specs=out_specs,
        out_shape=[jax.ShapeDtypeStruct(shape, dtype) for shape, dtype, axis in outs],
        scratch_shapes=[pltpu.VMEM(shape, dtype) for shape, dtype in scratch],
        compiler_params=pltpu.CompilerParams(vmem_limit_bytes=VMEM_LIMIT),
        name=name,
    )(*[array for array, axis in ins])


def zero_first(*refs):
    @pl.when(pl.program_id(0) == 0)
    def _():
        for ref in refs:
            ref[...] = jnp.zeros(ref.shape, ref.dtype)


def lane_sums(ref):
    return jnp.sum(ref[...].T, axis=0, keepdims=True)


def on_last(steps, body):
    @pl.when(pl.program_id(0) == steps - 1)
    def _():
        body()


def read_plain(ref, row):
    return ref[row].astype(F32)


def reorder(values, order):
    size = values.shape[0] // len(order)
    return jnp.concatenate([values[place * size : (place + 1) * size] for place in order], axis=0)


def read_tokens(order, ref, row):
    return reorder(ref[row].astype(F32), order).T


def read_flipped(ref, row):
    parts = ref[:, row]
    return parts.reshape(-1, parts.shape[-1]).astype(F32).T


def read_turned(order, ref, row):
    parts = ref[:, row]
    return reorder(parts.reshape(-1, parts.shape[-1]).astype(F32), order).T


def tri_pre_row(info, alive, row, state, cols, first, proj_t):
    unit, inverse = standardize(state)
    lowered = (unit * column(cols, first) + column(cols, first + 1)).astype(BF16)
    project = mm(proj_t[...], lowered)
    half = project.shape[0] // 2
    return project[:half] * sigmoid(project[half:]) * live_pair(info, alive, row)


def store_product(out, scratch, devices):
    hidden = scratch.shape[0] // 2
    part = hidden // devices

    def one(device, carry):
        out[device, 0] = scratch[pl.ds(device * part, part)].astype(BF16)
        out[device, 1] = scratch[pl.ds(hidden + device * part, part)].astype(BF16)
        return carry

    lax.fori_loop(0, devices, one, 0)


def copy_blocks(target, source, count):
    def one(index, carry):
        target[index] = source[index].astype(target.dtype)
        return carry

    lax.fori_loop(0, count, one, 0)


def store_flipped(out, scratch):
    devices, part = out.shape[0], out.shape[1]

    def one(device, carry):
        out[device] = scratch[pl.ds(device * part, part)].astype(out.dtype)
        return carry

    lax.fori_loop(0, devices, one, 0)


def tri_post_row(state, tri, cols, proj_t, gate_t):
    unit, inverse = standardize(state)
    lowered = (unit * column(cols, 0) + column(cols, 1)).astype(BF16)
    tri_unit, tri_inverse = standardize(tri)
    out_low = (tri_unit * column(cols, 2) + column(cols, 3)).astype(BF16)
    output = mm(proj_t[...], out_low)
    gate = sigmoid(mm(gate_t[...], lowered))
    return unit, inverse, lowered, tri_unit, tri_inverse, out_low, output, gate


def row_base(rows):
    return pl.program_id(0) * rows


def tri_pre_first_kernel(devices, read, info, alive, pair, cols, proj_t, out, scratch):
    rows = pair.shape[0]

    def body(row):
        scratch[:, row, :] = tri_pre_row(
            info, alive, row_base(rows) + row, read(pair, row), cols, 0, proj_t
        )

    each_row(rows, body)
    store_product(out, scratch, devices)


def tri_product_kernel(incoming, operands, out):
    def body(channel):
        length = operands.shape[-1]
        first = operands[:, 0, channel].reshape(length, length)
        second = operands[:, 1, channel].reshape(length, length)
        tri = mm_tn(first, second) if incoming else mm_nt(first, second)
        out[:, channel] = tri.astype(BF16).reshape(out.shape[0], out.shape[2], length)

    each_row(operands.shape[2], body)


def tri_join_kernel(
    devices, read, info, alive, source, tri_in, cols, proj_t, gate_t, next_cols, next_proj_t,
    state_out, out, tri_scratch, scratch,
):
    rows = state_out.shape[0]
    copy_blocks(tri_scratch, tri_in, tri_in.shape[0])

    def body(row):
        state = read(source, row)
        pieces = tri_post_row(state, tri_scratch[:, row, :], cols, proj_t, gate_t)
        state = state + pieces[6] * pieces[7]
        state_out[row] = state
        scratch[:, row, :] = tri_pre_row(
            info, alive, row_base(rows) + row, state, next_cols, 0, next_proj_t
        )

    each_row(rows, body)
    store_product(out, scratch, devices)


def tri_last_kernel(
    source, tri_in, cols, proj_t, gate_t, next_cols, bias_t, state_out, bias_out, tri_scratch, scratch
):
    rows = state_out.shape[0]
    copy_blocks(tri_scratch, tri_in, tri_in.shape[0])

    def body(row):
        state = source[row]
        pieces = tri_post_row(state, tri_scratch[:, row, :], cols, proj_t, gate_t)
        state = state + pieces[6] * pieces[7]
        state_out[row] = state
        unit, inverse = standardize(state)
        lowered = (unit * column(next_cols, 0) + column(next_cols, 1)).astype(BF16)
        scratch[:, row, :] = mm(bias_t[...], lowered)

    each_row(rows, body)
    bias_out[...] = scratch[: bias_out.shape[0]].astype(BF16)


def flipped_bias_kernel(source, cols, bias_t, bias_out, scratch):
    rows = source.shape[1]

    def body(row):
        unit, inverse = standardize(read_flipped(source, row))
        lowered = (unit * column(cols, 0) + column(cols, 1)).astype(BF16)
        scratch[:, row, :] = mm(bias_t[...], lowered)

    each_row(rows, body)
    bias_out[...] = scratch[: bias_out.shape[0]].astype(BF16)


def fill_bias(alive, bias_in, table):
    @pl.when(pl.program_id(0) == 0)
    def _():
        length = table.shape[1]
        penalty = (alive[0:1] - 1.0) * (MASKED * LOG2E)
        for head in range(table.shape[0]):
            values = bias_in[:, head].reshape(length, length).astype(F32)
            table[head] = (values * LOG2E + penalty).T


def attention_row(state, cols, proj_t):
    unit, inverse = standardize(state)
    lowered = (unit * column(cols, 0) + column(cols, 1)).astype(BF16)
    project = mm(proj_t[...], lowered)
    width = project.shape[0] // 4
    size = width // TA_HEADS
    query = (project[:width] * (size**-0.5 * LOG2E)).astype(BF16)
    key = project[width : 2 * width].astype(BF16)
    value = project[2 * width : 3 * width].astype(BF16)
    gate = sigmoid(project[3 * width :])
    return unit, inverse, lowered, query, key, value, gate


def attend_rows(state, cols, proj_t, output_t, table, save_total, save_mixed):
    unit, inverse, lowered, query, key, value, gate = attention_row(state, cols, proj_t)
    size = query.shape[0] // TA_HEADS
    mixed = []
    totals = []
    for head in range(TA_HEADS):
        part = slice(head * size, (head + 1) * size)
        scores = mm_tn(key[part], query[part]) + table[head]
        top = jnp.max(scores, axis=0, keepdims=True)
        shifted = jnp.exp2(scores - top)
        total = jnp.sum(shifted, axis=0, keepdims=True)
        mixed.append(mm(value[part], shifted.astype(BF16)) / total)
        totals.append(top + jnp.log2(total))
    mixed = jnp.concatenate(mixed, axis=0)
    save_total(jnp.concatenate(totals, axis=0))
    save_mixed(mixed.astype(BF16))
    return state + mm(output_t[...], (mixed * gate).astype(BF16))


def starting_kernel(
    alive, source, bias_in, cols, proj_t, output_t, out, totals, mixed, table, scratch
):
    fill_bias(alive, bias_in, table)
    rows = source.shape[0]

    def body(row):
        def save_total(values):
            totals[row] = values

        def save_mixed(values):
            mixed[row] = values

        state = attend_rows(source[row], cols, proj_t, output_t, table, save_total, save_mixed)
        scratch[:, row, :] = state.T

    each_row(rows, body)
    store_flipped(out, scratch)


def ending_kernel(alive, source, bias_in, cols, proj_t, output_t, out, totals, mixed, table):
    fill_bias(alive, bias_in, table)
    rows = source.shape[1]

    def body(row):
        def save_total(values):
            totals[row] = values

        def save_mixed(values):
            mixed[row] = values

        out[row] = attend_rows(
            read_flipped(source, row), cols, proj_t, output_t, table, save_total, save_mixed
        )

    each_row(rows, body)


def transition_kernel(
    order, source, cols, up_t, down_t, next_cols, bias_t, state_out, pair_out, bias_out, scratch, bias_scratch
):
    rows = source.shape[0]

    def body(row):
        state = source[row]
        unit, inverse = standardize(state)
        lowered = (unit * column(cols, 0) + column(cols, 1)).astype(BF16)
        hidden = mm(up_t[...], lowered)
        half = hidden.shape[0] // 2
        first = hidden[:half]
        mixed = (first * sigmoid(first) * hidden[half:]).astype(BF16)
        state = state + mm(down_t[...], mixed)
        state_out[row] = state
        scratch[:, row, :] = state.T
        unit, inverse = standardize(state)
        lowered = (unit * column(next_cols, 0) + column(next_cols, 1)).astype(BF16)
        bias_scratch[:, row, :] = mm(bias_t[...], lowered)

    each_row(rows, body)
    size = pair_out.shape[0] // len(order)
    for place, held in enumerate(order):
        pair_out[place * size : (place + 1) * size] = scratch[held * size : (held + 1) * size].astype(BF16)
    bias_out[...] = bias_scratch[...].astype(BF16)


def transition_back_kernel(
    steps, read, mid, final, cotangent, bias_grad, cols, up_t, up, down, next_cols, bias_w,
    grad_out, up_grad, down_grad, bias_w_grad, vecs, norm_gain, norm_bias, pair_gain, pair_bias, bias_scratch,
):
    zero_first(up_grad, down_grad, bias_w_grad, norm_gain, norm_bias, pair_gain, pair_bias)
    rows = mid.shape[0]
    bias_scratch[...] = bias_grad[...].astype(F32)

    def body(row):
        grad = read(cotangent, row)
        unit, inverse = standardize(final[row])
        gain = column(next_cols, 0)
        lowered = (unit * gain + column(next_cols, 1)).astype(BF16)
        grad_bias = bias_scratch[:, row, :].astype(BF16)
        bias_w_grad[...] += mm_nt(lowered, grad_bias)
        grad_lowered = mm(bias_w[...], grad_bias)
        pair_gain[...] += grad_lowered * unit
        pair_bias[...] += grad_lowered
        grad = grad + standardize_back(unit, inverse, grad_lowered * gain)
        unit, inverse = standardize(mid[row])
        gain = column(cols, 0)
        lowered = (unit * gain + column(cols, 1)).astype(BF16)
        hidden = mm(up_t[...], lowered)
        half = hidden.shape[0] // 2
        first, second = hidden[:half], hidden[half:]
        slope = sigmoid(first)
        silu = first * slope
        grad_low = grad.astype(BF16)
        grad_mixed = mm(down[...], grad_low)
        down_grad[...] += mm_nt((silu * second).astype(BF16), grad_low)
        grad_hidden = jnp.concatenate(
            [
                (grad_mixed * second * (slope + silu * (1.0 - slope))).astype(BF16),
                (grad_mixed * silu).astype(BF16),
            ],
            axis=0,
        )
        up_grad[...] += mm_nt(lowered, grad_hidden)
        grad_lowered = mm(up[...], grad_hidden)
        norm_gain[...] += grad_lowered * unit
        norm_bias[...] += grad_lowered
        grad_out[row] = grad + standardize_back(unit, inverse, grad_lowered * gain)

    each_row(rows, body)

    def finish():
        vecs[0:1] = lane_sums(norm_gain)
        vecs[1:2] = lane_sums(norm_bias)
        vecs[2:3] = lane_sums(pair_gain)
        vecs[3:4] = lane_sums(pair_bias)

    on_last(steps, finish)


def attention_back_kernel(
    steps, read, read_grad, alive, source, grad_in, bias_in, totals, mixed_in, cols, proj_t, proj, output,
    grad_out, bias_out, proj_grad, output_grad, table, grad_table,
):
    fill_bias(alive, bias_in, table)
    zero_first(proj_grad, output_grad, grad_table)
    rows = grad_out.shape[0]

    def body(row):
        unit, inverse, lowered, query, key, value, gate = attention_row(
            read(source, row), cols, proj_t
        )
        mixed = mixed_in[row].astype(F32)
        total = totals[row]
        grad_low = read_grad(grad_in, row).astype(BF16)
        gated = mixed * gate
        output_grad[...] += mm_nt(gated.astype(BF16), grad_low)
        grad_gated = mm(output[...], grad_low)
        grad_gate = grad_gated * gated * (1.0 - gate)
        grad_mixed = grad_gated * gate
        grad_mixed_low = grad_mixed.astype(BF16)
        product = grad_mixed_low.astype(F32) * mixed
        size = query.shape[0] // TA_HEADS
        grad_query, grad_key, grad_value = [], [], []
        for head in range(TA_HEADS):
            part = slice(head * size, (head + 1) * size)
            scores = mm_tn(key[part], query[part]) + table[head]
            probs = jnp.exp2(scores - total[head : head + 1])
            grad_probs = mm_tn(value[part], grad_mixed_low[part])
            delta = jnp.sum(product[part], axis=0, keepdims=True)
            grad_scores = probs * (grad_probs - delta)
            grad_table[head] += grad_scores
            grad_scores = grad_scores.astype(BF16)
            grad_query.append(mm(key[part], grad_scores) * size**-0.5)
            grad_key.append(mm_nt(query[part], grad_scores) * (1.0 / LOG2E))
            grad_value.append(mm_nt(grad_mixed_low[part], probs.astype(BF16)))
        grad_project = jnp.concatenate(
            grad_query + grad_key + grad_value + [grad_gate], axis=0
        ).astype(BF16)
        proj_grad[...] += mm_nt(lowered, grad_project)
        grad_out[row] = mm(proj[...], grad_project).astype(grad_out.dtype)

    each_row(rows, body)

    def finish():
        for head in range(TA_HEADS):
            bias_out[:, head] = (
                grad_table[head].T.astype(BF16).reshape(bias_out.shape[0], bias_out.shape[2], -1)
            )

    on_last(steps, finish)


def attention_end_row(
    state, grad, grad_lowered, grad_bias, cols, bias_w, bias_w_grad, norm_gain, norm_bias
):
    unit, inverse = standardize(state)
    gain = column(cols, 0)
    lowered = (unit * gain + column(cols, 1)).astype(BF16)
    bias_w_grad[...] += mm_nt(lowered, grad_bias)
    grad_lowered = grad_lowered + mm(bias_w[...], grad_bias)
    norm_gain[...] += grad_lowered * unit
    norm_bias[...] += grad_lowered
    return grad + standardize_back(unit, inverse, grad_lowered * gain)


def fill_bias_grad(scratch, bias_grad):
    heads = bias_grad.shape[1]
    total = bias_grad[0].astype(F32)
    for device in range(1, bias_grad.shape[0]):
        total = total + bias_grad[device].astype(F32)
    scratch[:heads] = total
    scratch[heads:] = jnp.zeros((scratch.shape[0] - heads,) + scratch.shape[1:], F32)


def ending_end_kernel(
    steps, source, grad_in, grad_lowered, bias_grad, cols, bias_w,
    grad_out, bias_w_grad, vecs, norm_gain, norm_bias, bias_scratch, scratch,
):
    zero_first(bias_w_grad, norm_gain, norm_bias)
    fill_bias_grad(bias_scratch, bias_grad)
    rows = grad_in.shape[0]

    def body(row):
        grad = attention_end_row(
            read_flipped(source, row), grad_in[row], grad_lowered[row].astype(F32),
            bias_scratch[:, row, :].astype(BF16), cols, bias_w, bias_w_grad, norm_gain, norm_bias,
        )
        scratch[:, row, :] = grad.T

    each_row(rows, body)
    store_flipped(grad_out, scratch)

    def finish():
        vecs[0:1] = lane_sums(norm_gain)
        vecs[1:2] = lane_sums(norm_bias)

    on_last(steps, finish)


def tri_post_back_row(
    state, tri, grad, cols, proj_t, gate_t, proj, gate_w, proj_grad, gate_grad, out_gain, out_bias
):
    unit, inverse, lowered, tri_unit, tri_inverse, out_low, output, gate = tri_post_row(
        state, tri, cols, proj_t, gate_t
    )
    grad_output = grad * gate
    grad_gate = (grad_output * output * (1.0 - gate)).astype(BF16)
    grad_output = grad_output.astype(BF16)
    proj_grad[...] += mm_nt(out_low, grad_output)
    gate_grad[...] += mm_nt(lowered, grad_gate)
    grad_normed = mm(proj[...], grad_output)
    out_gain[...] += grad_normed * tri_unit
    out_bias[...] += grad_normed
    grad_tri = standardize_back(tri_unit, tri_inverse, grad_normed * column(cols, 2))
    return grad_tri, mm(gate_w[...], grad_gate)


def starting_end_kernel(
    steps, source, grad_in, grad_lowered, bias_grad, cols, bias_w,
    below, tri_in, tri_cols, proj_t, gate_t, proj, gate_w,
    grad_out, tri_out, gate_back, bias_w_grad, proj_grad, gate_grad, vecs,
    norm_gain, norm_bias, out_gain, out_bias, bias_scratch, tri_scratch,
):
    zero_first(bias_w_grad, proj_grad, gate_grad, norm_gain, norm_bias, out_gain, out_bias)
    fill_bias_grad(bias_scratch, bias_grad)
    copy_blocks(tri_scratch, tri_in, tri_in.shape[0])
    rows = source.shape[0]

    def body(row):
        grad = attention_end_row(
            source[row], read_flipped(grad_in, row), grad_lowered[row].astype(F32),
            bias_scratch[:, row, :].astype(BF16), cols, bias_w, bias_w_grad, norm_gain, norm_bias,
        )
        grad_out[row] = grad
        grad_tri, back = tri_post_back_row(
            below[row], tri_scratch[:, row, :], grad, tri_cols, proj_t, gate_t, proj, gate_w,
            proj_grad, gate_grad, out_gain, out_bias,
        )
        gate_back[row] = back.astype(gate_back.dtype)
        tri_scratch[:, row, :] = grad_tri

    each_row(rows, body)
    copy_blocks(tri_out, tri_scratch, tri_out.shape[0])

    def finish():
        vecs[0:1] = lane_sums(norm_gain)
        vecs[1:2] = lane_sums(norm_bias)
        vecs[2:3] = lane_sums(out_gain)
        vecs[3:4] = lane_sums(out_bias)

    on_last(steps, finish)


def tri_product_back_kernel(incoming, grad, operands, out):
    def body(channel):
        length = operands.shape[-1]
        first = operands[:, 0, channel].reshape(length, length)
        second = operands[:, 1, channel].reshape(length, length)
        tri = grad[:, channel].reshape(length, length)
        if incoming:
            grad_first = mm_nt(second, tri)
            grad_second = mm(first, tri)
        else:
            grad_first = mm(tri, second)
            grad_second = mm_tn(tri, first)
        shape = (out.shape[0], out.shape[3], length)
        out[:, 0, channel] = grad_first.astype(BF16).reshape(shape)
        out[:, 1, channel] = grad_second.astype(BF16).reshape(shape)

    each_row(operands.shape[2], body)


def tri_pre_back_row(
    info, alive, row, state, product_grad, gate_back, grad, cols, proj_t, proj, proj_grad, norm_gain, norm_bias
):
    unit, inverse = standardize(state)
    gain = column(cols, 0)
    lowered = (unit * gain + column(cols, 1)).astype(BF16)
    project = mm(proj_t[...], lowered)
    half = project.shape[0] // 2
    gate = sigmoid(project[half:])
    grad_first = product_grad * gate * live_pair(info, alive, row)
    grad_second = grad_first * project[:half] * (1.0 - gate)
    grad_project = jnp.concatenate([grad_first.astype(BF16), grad_second.astype(BF16)], axis=0)
    proj_grad[...] += mm_nt(lowered, grad_project)
    grad_lowered = mm(proj[...], grad_project) + gate_back
    norm_gain[...] += grad_lowered * unit
    norm_bias[...] += grad_lowered
    return grad + standardize_back(unit, inverse, grad_lowered * gain)


def fill_product_grad(scratch, product_grad):
    devices, part = product_grad.shape[0], product_grad.shape[2]

    def one(device, carry):
        scratch[pl.ds(device * part, part)] = product_grad[device, 0].astype(F32)
        scratch[pl.ds((devices + device) * part, part)] = product_grad[device, 1].astype(F32)
        return carry

    lax.fori_loop(0, devices, one, 0)


def tri_join_back_kernel(
    steps, read, info, alive, source, product_grad, gate_in, grad_in, cols, proj_t, proj,
    below, tri_in, tri_cols, out_t, gate_t, out_w, gate_w,
    grad_out, tri_out, gate_back, proj_grad, out_grad, gate_grad, vecs,
    norm_gain, norm_bias, out_gain, out_bias, scratch, tri_scratch,
):
    zero_first(proj_grad, out_grad, gate_grad, norm_gain, norm_bias, out_gain, out_bias)
    fill_product_grad(scratch, product_grad)
    copy_blocks(tri_scratch, tri_in, tri_in.shape[0])
    rows = source.shape[0]

    def body(row):
        grad = tri_pre_back_row(
            info, alive, row_base(rows) + row, source[row], scratch[:, row, :], gate_in[row].astype(F32),
            grad_in[row], cols, proj_t, proj, proj_grad, norm_gain, norm_bias,
        )
        grad_out[row] = grad
        grad_tri, back = tri_post_back_row(
            read(below, row), tri_scratch[:, row, :], grad, tri_cols, out_t, gate_t, out_w, gate_w,
            out_grad, gate_grad, out_gain, out_bias,
        )
        gate_back[row] = back.astype(gate_back.dtype)
        tri_scratch[:, row, :] = grad_tri

    each_row(rows, body)
    copy_blocks(tri_out, tri_scratch, tri_out.shape[0])

    def finish():
        vecs[0:1] = lane_sums(norm_gain)
        vecs[1:2] = lane_sums(norm_bias)
        vecs[2:3] = lane_sums(out_gain)
        vecs[3:4] = lane_sums(out_bias)

    on_last(steps, finish)


def tri_first_back_kernel(
    steps, read, order, info, alive, source, product_grad, gate_in, grad_in, cols, proj_t, proj,
    grad_out, proj_grad, vecs, norm_gain, norm_bias, scratch,
):
    zero_first(proj_grad, norm_gain, norm_bias)
    fill_product_grad(scratch, product_grad)
    rows = source.shape[0]

    def body(row):
        grad = tri_pre_back_row(
            info, alive, row_base(rows) + row, read(source, row), scratch[:, row, :],
            gate_in[row].astype(F32), grad_in[row], cols, proj_t, proj, proj_grad, norm_gain, norm_bias,
        )
        grad_out[row] = reorder(grad.T, order).astype(grad_out.dtype)

    each_row(rows, body)

    def finish():
        vecs[0:1] = lane_sums(norm_gain)
        vecs[1:2] = lane_sums(norm_bias)

    on_last(steps, finish)


RUN = 24


def table_of(entries):
    table = {}
    offset = 0
    for name, shape in entries:
        table[name] = (offset // STRIDE, shape)
        offset += math.prod(shape)
    return table, offset


def runs_kernel(info, shard, out, scratch):
    def one(block, carry):
        scratch[:, block, :] = shard[pl.ds(block * STRIDE, STRIDE), :].T
        return carry

    lax.fori_loop(0, RUN, one, 0)
    half = STRIDE // 2
    turn = info[0] * half

    def move(lane, carry):
        out[lane] = scratch[lax.rem(lane + turn, STRIDE)].astype(BF16)
        return carry

    lax.fori_loop(0, STRIDE, move, 0)


def run_place(shards, total, lane, shard):
    count = total // STRIDE
    whole = total // shards
    step, odd = whole // STRIDE, (whole % STRIDE) // (STRIDE // 2)
    extra = lax.div(shard * odd + jnp.where(lane < STRIDE // 2, 1, 0), 2)
    start = lane * count + shard * step + extra
    return lax.div(start, STRIDE), lax.rem(start, STRIDE)


def rows_from_runs(runs, rows, first_lane, total):
    shards, lanes = runs.shape[0], runs.shape[1]
    base = first_lane * (total // STRIDE) // STRIDE

    def one(index, carry):
        lane, shard = lax.div(index, shards), lax.rem(index, shards)
        row, shift = run_place(shards, total, first_lane + lane, shard)
        row = row - base
        turned = pltpu.roll(runs[shard, lane].astype(F32), shift, 1)
        place = lax.broadcasted_iota(jnp.int32, (RUN + 1, STRIDE), 1)
        last, before = carry
        joint = jnp.where(row - before == RUN, last[2:3], last[1:2])
        below = jnp.concatenate([joint, turned], axis=0)
        above = jnp.concatenate([turned, turned[RUN - 1 :]], axis=0)
        values = jnp.where(place < shift, below, above)
        rows[pl.ds(row, RUN + 1), :] = values
        return values[RUN - 2 :], row

    lax.fori_loop(0, shards * lanes, one, (jnp.zeros((3, STRIDE), F32), -RUN), unroll=4)


def runs_from_rows(rows, out, first_lane, base, total):
    shards, lanes = out.shape[0], out.shape[1]

    def one(index, carry):
        lane, shard = lax.div(index, shards), lax.rem(index, shards)
        row, shift = run_place(shards, total, first_lane + lane, shard)
        turned = pltpu.roll(rows[pl.ds(row - base, RUN + 1), :], (STRIDE - shift) % STRIDE, 1)
        place = lax.broadcasted_iota(jnp.int32, (RUN, STRIDE), 1)
        out[shard, lane] = jnp.where(
            place < STRIDE - shift, turned[:RUN], turned[1:]
        ).astype(BF16)
        return carry

    lax.fori_loop(0, shards * lanes, one, 0, unroll=4)


def row_height(base, first_lane, last_lane, total):
    end = (last_lane * (total // STRIDE)) // STRIDE + RUN + 2
    return -(-(end - base) // 8) * 8


def take_matrix(rows, first, shape):
    blocks = shape[1] // STRIDE
    return [
        rows[pl.ds(first + block, shape[0], stride=blocks), :]
        if blocks > 1
        else rows[first : first + shape[0], :]
        for block in range(blocks)
    ]


def put_matrix(rows, first, matrix):
    height, width = matrix.shape
    blocks = width // STRIDE
    for block in range(blocks):
        part = matrix[:, block * STRIDE : (block + 1) * STRIDE]
        if blocks > 1:
            rows[pl.ds(first + block, height, stride=blocks), :] = part
        else:
            rows[first : first + height, :] = part


def spread(index, heads, rows):
    lane = lax.broadcasted_iota(jnp.int32, (STRIDE, STRIDE), 0)
    channel = lax.broadcasted_iota(jnp.int32, (STRIDE, STRIDE), 1)
    return (channel == index * (STRIDE // heads) + lane // heads).astype(BF16)


def take_narrow(rows, first, heads, high):
    total = jnp.zeros((high, STRIDE), F32)
    head = lax.broadcasted_iota(jnp.int32, (high, STRIDE), 0)
    lane = lax.broadcasted_iota(jnp.int32, (high, STRIDE), 1)
    for index in range(heads):
        line = rows[first + index : first + index + 1, :]
        picked = jnp.where(lane % heads == head, line, 0.0).astype(BF16)
        total = total + mm(picked, spread(index, heads, rows))
    return total


def put_narrow(rows, first, heads, matrix):
    turned = matrix.T.astype(BF16)
    high = turned.shape[0]
    head = lax.broadcasted_iota(jnp.int32, (high, STRIDE), 0)
    lane = lax.broadcasted_iota(jnp.int32, (high, STRIDE), 1)
    for index in range(heads):
        wide = mm_nt(turned, spread(index, heads, rows))
        rows[first + index : first + index + 1, :] = jnp.sum(
            jnp.where(lane % heads == head, wide, 0.0), axis=0, keepdims=True
        )


PAIR_MATRICES = (
    (OUTGOING, PROJ_GATE), (OUTGOING, PROJ_OUT), (OUTGOING, GATE_OUT),
    (INCOMING, PROJ_GATE), (INCOMING, PROJ_OUT), (INCOMING, GATE_OUT),
    (STARTING, QKVG), (STARTING, OUTPUT), (ENDING, QKVG), (ENDING, OUTPUT), (PAIR, UP), (PAIR, DOWN),
)
PAIR_COLUMNS = (
    (OUTGOING, ((OUTGOING, NORM_GAIN), (OUTGOING, NORM_BIAS), (OUTGOING, OUT_GAIN), (OUTGOING, OUT_BIAS))),
    (INCOMING, ((INCOMING, NORM_GAIN), (INCOMING, NORM_BIAS), (INCOMING, OUT_GAIN), (INCOMING, OUT_BIAS))),
    (STARTING, ((STARTING, NORM_GAIN), (STARTING, NORM_BIAS))),
    (ENDING, ((ENDING, NORM_GAIN), (ENDING, NORM_BIAS))),
    (PAIR, ((PAIR, NORM_GAIN), (PAIR, NORM_BIAS))),
)
SINGLE_MATRICES = ((ATTEND, QKVG), (ATTEND, OUTPUT), (SINGLE, UP), (SINGLE, DOWN))
SINGLE_VECTORS = ((ATTEND, NORM_GAIN), (ATTEND, NORM_BIAS), (SINGLE, NORM_GAIN), (SINGLE, NORM_BIAS))


def put_columns(rows, out, table, base, names):
    out[...] = jnp.zeros(out.shape, F32)
    lines = [rows[table[name][0] - base : table[name][0] - base + 1, :] for name in names]
    lines.append(jnp.zeros((8 - len(lines), STRIDE), F32))
    out[...] = jnp.concatenate(lines, axis=0).T


def unpack_pair_kernel(table, total, runs, *refs):
    rows = refs[-1]
    outs = list(refs[:-1])
    rows_from_runs(runs, rows, 0, total)
    for name in PAIR_MATRICES:
        first, shape = table[name]
        plain, turned = outs.pop(0), outs.pop(0)
        for block, part in enumerate(take_matrix(rows, first, shape)):
            place = slice(block * STRIDE, (block + 1) * STRIDE)
            plain[:, place] = part.astype(BF16)
            turned[place, :] = part.T.astype(BF16)
    for prefix in (STARTING, ENDING):
        plain, turned = outs.pop(0), outs.pop(0)
        first, shape = table[(prefix, BIAS_PROJ)]
        matrix = take_narrow(rows, first, shape[1], 8)
        turned[...] = matrix.astype(BF16)
        plain[...] = matrix.T.astype(BF16)
    for prefix, names in PAIR_COLUMNS:
        put_columns(rows, outs.pop(0), table, 0, names)


def unpack_single_kernel(table, total, first_lane, runs, *refs):
    rows = refs[-1]
    outs = list(refs[:-1])
    rows_from_runs(runs, rows, first_lane, total)
    base = first_lane * (total // STRIDE) // STRIDE
    for name in SINGLE_MATRICES:
        first, shape = table[name]
        out = outs.pop(0)
        for block, part in enumerate(take_matrix(rows, first - base, shape)):
            out[:, block * STRIDE : (block + 1) * STRIDE] = part.astype(BF16)
    first, shape = table[(ATTEND, PAIR_PROJ)]
    matrix = take_narrow(rows, first - base, shape[1], shape[1])
    plain, turned = outs.pop(0), outs.pop(0)
    turned[...] = matrix.astype(BF16)
    plain[...] = matrix.T.astype(BF16)
    put_columns(rows, outs.pop(0), table, base, ((ATTEND, PAIR_GAIN), (ATTEND, PAIR_BIAS)))
    lines = outs.pop(0)
    lines[...] = jnp.zeros(lines.shape, F32)
    for index, name in enumerate(SINGLE_VECTORS):
        first, shape = table[name]
        for block in range(shape[0] // STRIDE):
            lines[index : index + 1, block * STRIDE : (block + 1) * STRIDE] = rows[
                first - base + block : first - base + block + 1, :
            ]


def pack_kernel(table, total, first_lane, base, names, *refs):
    ins, out, rows = refs[: len(names)], refs[-2], refs[-1]
    for name, ref in zip(names, ins):
        if isinstance(name, tuple):
            first, shape = table[name]
            if shape[1] % STRIDE:
                put_narrow(rows, first - base, shape[1], ref[...])
            else:
                put_matrix(rows, first - base, ref)
        else:
            for index, vector in name:
                first, shape = table[vector]
                for block in range(shape[0] // STRIDE):
                    rows[first + block - base : first + block - base + 1, :] = ref[
                        index : index + 1, block * STRIDE : (block + 1) * STRIDE
                    ]
    runs_from_rows(rows, out, first_lane, base, total)


def shard_kernel(whole, info, runs, out, squares):
    half = STRIDE // 2
    squares[...] = jnp.zeros(squares.shape, F32)

    def one(block, carry):
        first = runs[pl.ds(info[0] * half, half), block, :]
        second = runs[pl.ds(half - info[0] * half, half), block, :]
        values = jnp.concatenate([first, second], axis=0).T
        row = block * STRIDE + lax.broadcasted_iota(jnp.int32, values.shape, 0)
        lane = lax.broadcasted_iota(jnp.int32, values.shape, 1)
        values = jnp.where(row * STRIDE + lane < whole, values, 0.0)
        out[pl.ds(block * STRIDE, STRIDE), :] = values
        squares[...] += jnp.sum((values * values).reshape(-1, 8, STRIDE), axis=0)
        return carry

    lax.fori_loop(0, RUN, one, 0)


def whole_call(kernel, name, ins, outs, scratch):
    def spec(axis):
        return pl.BlockSpec(memory_space=pltpu.SMEM if axis == "smem" else pltpu.VMEM)

    return pl.pallas_call(
        kernel,
        in_specs=[spec(axis) for array, axis in ins],
        out_specs=[pl.BlockSpec(memory_space=pltpu.VMEM) for shape, dtype in outs],
        out_shape=[jax.ShapeDtypeStruct(shape, dtype) for shape, dtype in outs],
        scratch_shapes=[pltpu.VMEM(shape, dtype) for shape, dtype in scratch],
        compiler_params=pltpu.CompilerParams(vmem_limit_bytes=VMEM_LIMIT),
        name=name,
    )(*[array for array, axis in ins])


def unpack_pair(table, total, runs):
    outs = []
    names = []
    for name in PAIR_MATRICES:
        shape = table[name][1]
        outs += [(shape, BF16), (shape[::-1], BF16)]
        names += [name, (name, T)]
    for prefix in (STARTING, ENDING):
        outs += [((STRIDE, 8), BF16), ((8, STRIDE), BF16)]
        names += [(prefix, BIAS_W), (prefix, BIAS_T)]
    for prefix, parts in PAIR_COLUMNS:
        outs.append(((STRIDE, 8), F32))
        names.append((prefix, COLS))
    height = row_height(0, 0, runs.shape[1], total)
    values = whole_call(
        functools.partial(unpack_pair_kernel, table, total), "pair_weights", [(runs, None)], outs,
        [((height, STRIDE), F32)],
    )
    return dict(zip(names, values))


def unpack_single(table, total, first_lane, runs):
    outs = [(table[name][1], BF16) for name in SINGLE_MATRICES]
    names = list(SINGLE_MATRICES)
    shape = table[(ATTEND, PAIR_PROJ)][1]
    outs += [(shape, BF16), (shape[::-1], BF16), ((STRIDE, 8), F32), ((8, S), F32)]
    names += [(ATTEND, PAIR_PROJ), ((ATTEND, PAIR_PROJ), T), (ATTEND, COLS), (SINGLE, VECTORS)]
    base = first_lane * (total // STRIDE) // STRIDE
    height = row_height(base, first_lane, first_lane + runs.shape[1], total)
    values = whole_call(
        functools.partial(unpack_single_kernel, table, total, first_lane), "single_weights",
        [(runs, None)], outs, [((height, STRIDE), F32)],
    )
    return dict(zip(names, values))


def pack(name, table, total, shards, lanes, base, parts):
    height = row_height(base, *lanes, total)
    for held, array in parts:
        if isinstance(held, tuple):
            end = table[held][0] - base + array.shape[0] * max(1, array.shape[1] // STRIDE)
            height = max(height, -(-end // 8) * 8)
    return whole_call(
        functools.partial(pack_kernel, table, total, lanes[0], base, [held for held, array in parts]),
        name, [(array, None) for held, array in parts],
        [((shards, lanes[1] - lanes[0], RUN, STRIDE), BF16)], [((height, STRIDE), F32)],
    )[0]


def swap(values, group):
    return lax.all_to_all(values, group, split_axis=0, concat_axis=0, tiled=True)


def single_attend(single_state, bias, penalty, weights, group):
    gain, shift = norm_pair(weights, ATTEND)
    lowered = layer_norm(single_state, gain, shift).astype(BF16)
    rows, width = lowered.shape
    size = width // SA_HEADS
    qkvg = matmul(lowered, weights[(ATTEND, QKVG)])
    query = qkvg[:, :width].astype(BF16).reshape(rows, SA_HEADS, size)
    gate = qkvg[:, 3 * width :]
    both = lax.all_gather(qkvg[:, width : 3 * width].astype(BF16), group, axis=0, tiled=True)
    keys_all = both[:, :width].reshape(-1, SA_HEADS, size)
    values_all = both[:, width:].reshape(-1, SA_HEADS, size)
    scores = jnp.einsum(
        "ihd,jhd->hij", query, keys_all, preferred_element_type=F32
    ) * size ** (-0.5)
    scores = scores + bias + penalty[None, None, :]
    probs = jax.nn.softmax(scores, axis=-1)
    probs_low = probs.astype(BF16)
    mixed = jnp.einsum("hij,jhd->ihd", probs_low, values_all, preferred_element_type=F32)
    mixed = mixed.reshape(rows, width)
    gated_low = gated_output(mixed, gate).astype(BF16)
    update = matmul(gated_low, weights[(ATTEND, OUTPUT)])
    return (
        update,
        (single_state, lowered, query, keys_all, values_all, gate, probs, probs_low, mixed, gated_low),
    )


def single_attend_back(saved, grad_update, weights, grads, group):
    single_state, lowered, query, keys_all, values_all, gate, probs, probs_low, mixed, gated_low = saved
    rows, width = lowered.shape
    size = width // SA_HEADS
    scale = size ** (-0.5)
    grad_low = grad_update.astype(BF16)
    grads[(ATTEND, OUTPUT)] = outer_sum(gated_low, grad_low)
    grad_gated = matmul(grad_low, weights[(ATTEND, OUTPUT)].T)
    _, pullback = jax.vjp(gated_output, mixed, gate)
    grad_mixed, grad_gate = pullback(grad_gated)
    grad_mixed = grad_mixed.astype(BF16).reshape(rows, SA_HEADS, size)
    grad_probs = jnp.einsum("ihd,jhd->hij", grad_mixed, values_all, preferred_element_type=F32)
    delta = jnp.sum(probs * grad_probs, axis=-1, keepdims=True)
    grad_scores = (probs * (grad_probs - delta)).astype(BF16)
    grad_query = (
        jnp.einsum("hij,jhd->ihd", grad_scores, keys_all, preferred_element_type=F32) * scale
    )
    key_part = jnp.einsum("hij,ihd->jhd", grad_scores, query, preferred_element_type=F32) * scale
    value_part = jnp.einsum("hij,ihd->jhd", probs_low, grad_mixed, preferred_element_type=F32)
    parts = jnp.concatenate(
        [key_part.reshape(-1, rows, width), value_part.reshape(-1, rows, width)], axis=-1
    )
    grad_both = jnp.sum(swap(parts.astype(BF16), group).astype(F32), axis=0)
    grad_qkvg = jnp.concatenate(
        [grad_query.reshape(rows, width), grad_both, grad_gate], axis=-1
    ).astype(BF16)
    grads[(ATTEND, QKVG)] = outer_sum(lowered, grad_qkvg)
    grad_lowered = matmul(grad_qkvg, weights[(ATTEND, QKVG)].T)
    gain, shift = norm_pair(weights, ATTEND)
    grad_single, grads[(ATTEND, NORM_GAIN)], grads[(ATTEND, NORM_BIAS)] = norm_backward(
        single_state, gain, shift, grad_lowered
    )
    return grad_single, grad_scores


def to_plane(values, parts):
    shape = values.shape
    values = swap(values.reshape((parts, -1) + shape[1:]), "crop")
    return swap(values, "z").reshape(shape)


def from_plane(values, parts):
    shape = values.shape
    values = swap(values.reshape((parts, -1) + shape[1:]), "z")
    return swap(values, "crop").reshape(shape)


def after(values, *others):
    held = lax.optimization_barrier((values,) + others)
    return held


def pair_path(pair, info, alive, orders, weights, cotangent, middle, group, parts):
    rows, length, width = pair.shape
    hidden = weights[(OUTGOING, PROJ_OUT)].shape[0]
    devices = length // rows
    cores = devices // parts
    order, order_back = orders
    read_first = functools.partial(read_tokens, order)
    read_last = functools.partial(read_turned, order)
    part = hidden // devices
    steps = rows // 16
    state_shape = (rows, width, length)
    flip_shape = (devices, rows, rows, width)
    product_shape = (devices, 2, part, rows, length)
    tri_shape = (devices, part, rows, length)
    block = rows // steps
    channel_block = math.gcd(part, 4)

    def products(name, kernel, arrays, out_shape):
        axes = {4: 1, 5: 2}
        return run_rows(
            kernel, name, part // channel_block,
            [(array, axes[array.ndim]) for array in arrays],
            [(out_shape, BF16, axes[len(out_shape)])], [],
        )[0]

    def cols(prefix):
        return weights[(prefix, COLS)]

    tri_cols = cols

    def turned(name):
        return weights[(name, T)]

    tri_scratch = ((hidden, block, length), F32)
    product_scratch = ((2 * hidden, block, length), F32)
    head_scratch = ((8, block, length), F32)
    wide = ((width, length), F32)
    flip_scratch = ((length, block, width), F32)
    table = ((TA_HEADS, length, length), F32)
    attend_saves = [((rows, TA_HEADS, length), F32, 0), (state_shape, BF16, 0)]

    (product,) = run_rows(
        functools.partial(tri_pre_first_kernel, devices, read_first), "outgoing_in", steps,
        [
            (info, "smem"), (alive, None), (pair, 0), (tri_cols(OUTGOING), None),
            (turned((OUTGOING, PROJ_GATE)), None),
        ],
        [(product_shape, BF16, 3)], [product_scratch],
    )
    product_one = swap(product, group)
    tri_one = products(
        "outgoing_product", functools.partial(tri_product_kernel, False), [product_one], tri_shape
    )
    tri_one = swap(tri_one, group).reshape(hidden, rows, length)
    state_one, product = run_rows(
        functools.partial(tri_join_kernel, devices, read_first), "outgoing_out_incoming_in", steps,
        [
            (info, "smem"), (alive, None), (pair, 0), (tri_one, 1), (tri_cols(OUTGOING), None),
            (turned((OUTGOING, PROJ_OUT)), None), (turned((OUTGOING, GATE_OUT)), None),
            (tri_cols(INCOMING), None), (turned((INCOMING, PROJ_GATE)), None),
        ],
        [(state_shape, F32, 0), (product_shape, BF16, 3)], [tri_scratch, product_scratch],
    )
    product_two = swap(product, group)
    tri_two = products(
        "incoming_product", functools.partial(tri_product_kernel, True), [product_two], tri_shape
    )
    tri_two = swap(tri_two, group).reshape(hidden, rows, length)
    state_two, bias = run_rows(
        tri_last_kernel, "incoming_out_starting_bias", steps,
        [
            (state_one, 0), (tri_two, 1), (tri_cols(INCOMING), None),
            (turned((INCOMING, PROJ_OUT)), None), (turned((INCOMING, GATE_OUT)), None),
            (cols(STARTING), None), (weights[(STARTING, BIAS_T)], None),
        ],
        [(state_shape, F32, 0), ((TA_HEADS, rows, length), BF16, 1)], [tri_scratch, head_scratch],
    )
    bias_one = lax.all_gather(bias, group, axis=0, tiled=False)
    cotangent = cotangent.reshape(rows, parts, cores, parts, -1, width).transpose(3, 2, 1, 4, 0, 5)
    cotangent = swap(cotangent.reshape(flip_shape), group)
    cotangent = swap(cotangent.reshape((parts, cores) + flip_shape[1:]), "z").reshape(flip_shape)
    flipped, totals_one, mixed_one = run_rows(
        starting_kernel, "starting_attention", steps,
        [
            (alive, None), (state_two, 0), (bias_one, None), (cols(STARTING), None),
            (turned((STARTING, QKVG)), None), (turned((STARTING, OUTPUT)), None),
        ],
        [(flip_shape, BF16, 2)] + attend_saves, [table, flip_scratch],
    )
    state_three = swap(flipped, group)
    (bias,) = run_rows(
        flipped_bias_kernel, "ending_bias", steps,
        [(state_three, 1), (cols(ENDING), None), (weights[(ENDING, BIAS_T)], None)],
        [((TA_HEADS, rows, length), BF16, 1)], [head_scratch],
    )
    bias_two = lax.all_gather(bias, group, axis=0, tiled=False)
    state_four, totals_two, mixed_two = run_rows(
        ending_kernel, "ending_attention", steps,
        [
            (alive, None), (state_three, 1), (bias_two, None), (cols(ENDING), None),
            (turned((ENDING, QKVG)), None), (turned((ENDING, OUTPUT)), None),
        ],
        [(state_shape, F32, 0)] + attend_saves, [table],
    )
    pair_cols, attend_cols = cols(PAIR), cols(ATTEND)
    state_four, cotangent = after(state_four, cotangent)
    state_five, pair_out, single_bias = run_rows(
        functools.partial(transition_kernel, order_back), "pair_transition", steps,
        [
            (state_four, 0), (pair_cols, None), (turned((PAIR, UP)), None), (turned((PAIR, DOWN)), None),
            (attend_cols, None), (turned((ATTEND, PAIR_PROJ)), None),
        ],
        [(state_shape, F32, 0), ((length, rows, width), BF16, 1), ((SA_HEADS, rows, length), BF16, 1)],
        [flip_scratch, ((SA_HEADS, block, length), F32)],
    )
    pair_out = swap(pair_out.reshape((parts, -1) + pair_out.shape[1:]), "z")

    def turn(values):
        heads = values.shape[0]
        sent = values.reshape(heads, rows, devices, rows).transpose(2, 0, 3, 1)
        return swap(sent, group).transpose(1, 2, 0, 3).reshape(heads, rows, length)

    single_grad_scores = middle(turn(single_bias).astype(F32))
    grads = {}
    grad_four, grads[(PAIR, UP)], grads[(PAIR, DOWN)], grads[(ATTEND, PAIR_PROJ)], vecs = run_rows(
        functools.partial(transition_back_kernel, steps, read_last), "pair_transition_back", steps,
        [
            (state_four, 0), (state_five, 0), (cotangent, 1), (turn(single_grad_scores), 1),
            (pair_cols, None), (turned((PAIR, UP)), None), (weights[(PAIR, UP)], None),
            (weights[(PAIR, DOWN)], None), (attend_cols, None), (weights[(ATTEND, PAIR_PROJ)], None),
        ],
        [
            (state_shape, F32, 0), (weights[(PAIR, UP)].shape, F32, None),
            (weights[(PAIR, DOWN)].shape, F32, None), (weights[(ATTEND, PAIR_PROJ)].shape, F32, None),
            ((8, width), F32, None),
        ],
        [wide, wide, wide, wide, ((SA_HEADS, block, length), F32)],
    )
    grads[(PAIR, VECTORS)] = vecs

    grad_four, pair_out = after(grad_four, pair_out)
    pair_out = swap(pair_out.reshape(flip_shape), group)

    def attention_back(prefix, read, read_grad, source, source_axis, grad, grad_axis, bias, totals, mixed):
        lowered_grad, bias_grad, grads[(prefix, QKVG)], grads[(prefix, OUTPUT)] = run_rows(
            functools.partial(attention_back_kernel, steps, read, read_grad),
            "attention_back", steps,
            [
                (alive, None), (source, source_axis), (grad, grad_axis), (bias, None), (totals, 0),
                (mixed, 0), (cols(prefix), None), (turned((prefix, QKVG)), None),
                (weights[(prefix, QKVG)], None), (weights[(prefix, OUTPUT)], None),
            ],
            [
                (state_shape, BF16, 0), ((devices, TA_HEADS, rows, length), BF16, None),
                (weights[(prefix, QKVG)].shape, F32, None), (weights[(prefix, OUTPUT)].shape, F32, None),
            ],
            [table, table],
        )
        return lowered_grad, swap(bias_grad, group)

    lowered_grad, bias_grad = attention_back(
        ENDING, read_flipped, read_plain, state_three, 1, grad_four, 0, bias_two, totals_two, mixed_two
    )
    bias_grad, pair_out = after(bias_grad, pair_out)
    pair_out = pair_out.reshape(parts, cores, rows, parts, -1, width).transpose(2, 3, 1, 0, 4, 5)
    pair_out = pair_out.reshape(rows, length, width)
    flipped, bias_w_grad, vecs = run_rows(
        functools.partial(ending_end_kernel, steps), "ending_attention_end", steps,
        [
            (state_three, 1), (grad_four, 0), (lowered_grad, 0), (bias_grad, 2), (cols(ENDING), None),
            (weights[(ENDING, BIAS_W)], None),
        ],
        [(flip_shape, BF16, 2), ((width, 8), F32, None), ((8, width), F32, None)],
        [wide, wide, head_scratch, flip_scratch],
    )
    grads[(ENDING, BIAS_PROJ)], grads[(ENDING, VECTORS)] = bias_w_grad, vecs
    grad_three = swap(flipped, group)
    lowered_grad, bias_grad = attention_back(
        STARTING, read_plain, read_flipped, state_two, 0, grad_three, 1, bias_one, totals_one, mixed_one
    )
    square = weights[(INCOMING, GATE_OUT)].shape
    (
        grad_two, grad_tri, gate_back, bias_w_grad, grads[(INCOMING, PROJ_OUT)], grads[(INCOMING, GATE_OUT)], vecs,
    ) = run_rows(
        functools.partial(starting_end_kernel, steps), "starting_end_incoming_out_back", steps,
        [
            (state_two, 0), (grad_three, 1), (lowered_grad, 0), (bias_grad, 2), (cols(STARTING), None),
            (weights[(STARTING, BIAS_W)], None), (state_one, 0), (tri_two, 1), (tri_cols(INCOMING), None),
            (turned((INCOMING, PROJ_OUT)), None), (turned((INCOMING, GATE_OUT)), None),
            (weights[(INCOMING, PROJ_OUT)], None), (weights[(INCOMING, GATE_OUT)], None),
        ],
        [
            (state_shape, F32, 0), ((hidden, rows, length), BF16, 1), (state_shape, BF16, 0),
            ((width, 8), F32, None), (square, F32, None), (square, F32, None), ((8, width), F32, None),
        ],
        [wide, wide, wide, wide, head_scratch, tri_scratch],
    )
    grads[(STARTING, BIAS_PROJ)], grads[(STARTING, VECTORS)] = bias_w_grad, vecs
    grad_tri = swap(grad_tri.reshape(tri_shape), group)
    product_grad = swap(
        products(
            "incoming_product_back", functools.partial(tri_product_back_kernel, True),
            [grad_tri, product_two], product_shape,
        ),
        group,
    )
    (
        grad_one, grad_tri, gate_back, grads[(INCOMING, PROJ_GATE)], grads[(OUTGOING, PROJ_OUT)],
        grads[(OUTGOING, GATE_OUT)], vecs,
    ) = run_rows(
        functools.partial(tri_join_back_kernel, steps, read_first), "incoming_in_outgoing_out_back", steps,
        [
            (info, "smem"), (alive, None), (state_one, 0), (product_grad, 3), (gate_back, 0), (grad_two, 0),
            (tri_cols(INCOMING), None), (turned((INCOMING, PROJ_GATE)), None),
            (weights[(INCOMING, PROJ_GATE)], None), (pair, 0), (tri_one, 1), (tri_cols(OUTGOING), None),
            (turned((OUTGOING, PROJ_OUT)), None), (turned((OUTGOING, GATE_OUT)), None),
            (weights[(OUTGOING, PROJ_OUT)], None), (weights[(OUTGOING, GATE_OUT)], None),
        ],
        [
            (state_shape, F32, 0), ((hidden, rows, length), BF16, 1), (state_shape, BF16, 0),
            (weights[(INCOMING, PROJ_GATE)].shape, F32, None), (square, F32, None), (square, F32, None),
            ((8, width), F32, None),
        ],
        [wide, wide, wide, wide, product_scratch, tri_scratch],
    )
    grads[(INCOMING, VECTORS)] = vecs
    grad_tri = swap(grad_tri.reshape(tri_shape), group)
    product_grad = swap(
        products(
            "outgoing_product_back", functools.partial(tri_product_back_kernel, False),
            [grad_tri, product_one], product_shape,
        ),
        group,
    )
    pair_grad, grads[(OUTGOING, PROJ_GATE)], vecs = run_rows(
        functools.partial(tri_first_back_kernel, steps, read_first, order_back), "outgoing_in_back", steps,
        [
            (info, "smem"), (alive, None), (pair, 0), (product_grad, 3), (gate_back, 0), (grad_one, 0),
            (tri_cols(OUTGOING), None), (turned((OUTGOING, PROJ_GATE)), None),
            (weights[(OUTGOING, PROJ_GATE)], None),
        ],
        [
            ((rows, length, width), BF16, 0), (weights[(OUTGOING, PROJ_GATE)].shape, F32, None),
            ((8, width), F32, None),
        ],
        [wide, wide, product_scratch],
    )
    grads[(OUTGOING, VECTORS)] = vecs
    return pair_out, pair_grad, grads


HELD = {
    (PAIR, VECTORS): ((PAIR, NORM_GAIN), (PAIR, NORM_BIAS), (ATTEND, PAIR_GAIN), (ATTEND, PAIR_BIAS)),
    (ENDING, VECTORS): ((ENDING, NORM_GAIN), (ENDING, NORM_BIAS)),
    (STARTING, VECTORS): (
        (STARTING, NORM_GAIN), (STARTING, NORM_BIAS), (INCOMING, OUT_GAIN), (INCOMING, OUT_BIAS)
    ),
    (INCOMING, VECTORS): (
        (INCOMING, NORM_GAIN), (INCOMING, NORM_BIAS), (OUTGOING, OUT_GAIN), (OUTGOING, OUT_BIAS)
    ),
    (OUTGOING, VECTORS): ((OUTGOING, NORM_GAIN), (OUTGOING, NORM_BIAS)),
}


def vector_part(grads, name, prefix):
    pairs = [(row, held) for row, held in enumerate(HELD[name]) if prefix in (None, held[0])]
    return (pairs, grads[name])


def fast_shards(parts, cores, pair, single, lengths, params, moment_one, moment_two, pair_cotangent, single_cotangent):
    entries = layout(C, H, S, TA_HEADS, SA_HEADS)
    table, total = table_of(entries)
    count = total // STRIDE
    shard_size = params.shape[0]
    attend = table[(ATTEND, NORM_GAIN)][0]
    pair_lanes = -(-attend * STRIDE // count)
    single_lane = attend * STRIDE // count
    devices = parts * cores
    line, group = ("z", "core"), ("crop", "core")
    row_index = lax.axis_index(line)
    odd = ((row_index * shard_size) % STRIDE) // (STRIDE // 2)
    place = jnp.stack([odd, odd]).astype(jnp.int32)
    shard_rows = jnp.pad(params, (0, RUN * STRIDE * STRIDE - shard_size)).reshape(-1, STRIDE)
    (runs,) = whole_call(
        runs_kernel, "parameter_runs", [(place, "smem"), (shard_rows, None)],
        [((STRIDE, RUN, STRIDE), BF16)], [((STRIDE, RUN, STRIDE), F32)],
    )
    weights = unpack_pair(table, total, lax.all_gather(runs[:pair_lanes], line))
    weights.update(
        unpack_single(table, total, single_lane, lax.all_gather(runs[single_lane:], line))
    )
    for index, name in enumerate(SINGLE_VECTORS):
        weights[name] = weights[(SINGLE, VECTORS)][index]
    rows, length = pair.shape[1:3]
    size = rows // parts
    blocks = np.arange(length // size).reshape(parts, cores, parts)
    order = blocks.transpose(2, 1, 0).reshape(-1)
    orders = (order.tolist(), np.argsort(order).tolist())
    tokens = (order[:, None] * size + np.arange(size)).reshape(-1)
    width = single.shape[2]
    length_lanes = jnp.broadcast_to(lengths.astype(BF16), (rows, STRIDE))
    both = jnp.concatenate([single[0], single_cotangent[0], length_lanes], axis=1)
    both = to_plane(both, parts).astype(F32)
    single_state, single_back, live = both[:, :width], both[:, width : 2 * width], both[0, 2 * width]
    mask = (tokens.astype(np.float32) < live).astype(F32)
    info = lax.dynamic_slice_in_dim(mask, lax.axis_index(group) * rows, rows).astype(jnp.int32)
    alive = jnp.broadcast_to(mask, (8, length))
    penalty = (mask - 1.0) * MASKED
    results = {}
    single_grads = {}

    def middle(bias):
        update, saved = single_attend(single_state, bias, penalty, weights, group)
        single_mid = single_state + update
        update, saved_last = transition_forward(single_mid, weights, SINGLE)
        results[SINGLE] = single_mid + update
        grad = single_back
        grad = grad + transition_backward(saved_last, grad, weights, SINGLE, single_grads)
        more, grad_scores = single_attend_back(saved, grad, weights, single_grads, group)
        results["single_grad"] = grad + more
        return grad_scores

    pair_out, pair_grad, grads = pair_path(
        to_plane(pair[0], parts), info, alive, orders, weights, pair_cotangent[0], middle, group, parts
    )
    pair_grad = from_plane(pair_grad, parts).astype(F32)
    both = from_plane(jnp.concatenate([results[SINGLE], results["single_grad"]], axis=1), parts)
    single_out, single_grad = both[:, :width].astype(BF16), both[:, width:]
    grads.update(single_grads)
    lines = jnp.concatenate([grads[name].reshape(1, S) for name in SINGLE_VECTORS], axis=0)
    lines = (list(enumerate(SINGLE_VECTORS)), jnp.pad(lines, ((0, 8 - len(SINGLE_VECTORS)), (0, 0))))
    single_runs = pack(
        "single_gradient", table, total, devices, (pair_lanes, STRIDE), attend,
        [(name, grads[name]) for name in SINGLE_MATRICES + ((ATTEND, PAIR_PROJ),)]
        + [vector_part(grads, (PAIR, VECTORS), ATTEND), lines],
    )
    single_runs = lax.psum(
        lax.psum_scatter(single_runs, line, scatter_dimension=0, tiled=False), "crop"
    ).astype(F32)
    early = -(-(pair_lanes * count - (attend + 2 * S // STRIDE) * STRIDE) // table[(ATTEND, QKVG)][1][1])
    pair_runs = pack(
        "pair_gradient", table, total, devices, (0, pair_lanes), 0,
        [(name, grads[name]) for name in PAIR_MATRICES + ((STARTING, BIAS_PROJ), (ENDING, BIAS_PROJ))]
        + [vector_part(grads, name, None) for name in HELD if name != (PAIR, VECTORS)]
        + [vector_part(grads, (PAIR, VECTORS), PAIR)]
        + [((lines[0][:2]), lines[1]), ((ATTEND, QKVG), grads[(ATTEND, QKVG)][: -(-early // 8) * 8])],
    )
    pair_runs = jnp.sum(swap(pair_runs, line).astype(F32), axis=0)
    pair_runs = jnp.sum(lax.all_gather(pair_runs, "crop"), axis=0)
    shard, squares = whole_call(
        functools.partial(shard_kernel, shard_size), "gradient_share",
        [(place, "smem"), (jnp.concatenate([pair_runs, single_runs], axis=0), None)],
        [((RUN * STRIDE, STRIDE), F32), ((8, STRIDE), F32)], [],
    )
    shard = shard.reshape(-1)[:shard_size]
    clip_norm = jnp.sqrt(jnp.sum(lax.all_gather(squares, line)))
    clipped = shard * (CLIP / jnp.maximum(clip_norm, CLIP))
    new_first = BETA_ONE * moment_one + (1.0 - BETA_ONE) * clipped
    new_second = BETA_TWO * moment_two + (1.0 - BETA_TWO) * clipped * clipped
    rates, decays = rate_tables(entries)
    rate_shard = lax.dynamic_slice_in_dim(jnp.asarray(rates), row_index * shard_size, shard_size)
    decay_shard = lax.dynamic_slice_in_dim(jnp.asarray(decays), row_index * shard_size, shard_size)
    first_hat = new_first / (1.0 - BETA_ONE**STEP)
    second_hat = new_second / (1.0 - BETA_TWO**STEP)
    new_params = params - rate_shard * (
        first_hat / (jnp.sqrt(second_hat) + ADAM_EPS) + decay_shard * params
    )
    return (
        pair_out[None],
        single_out[None],
        pair_grad[None],
        single_grad[None],
        new_params,
        new_first,
        new_second,
        clip_norm,
    )


def solution(mesh):
    crops, devices = mesh.devices.shape
    count = table_of(layout(C, H, S, TA_HEADS, SA_HEADS))[1] // STRIDE
    fast = devices == 2 * crops and LENGTH % (devices * 16) == 0 and count // devices + 2 <= RUN * STRIDE
    row = "row"
    if fast:
        mesh = jax.sharding.Mesh(mesh.devices.reshape(crops, crops, 2), ("crop", "z", "core"))
        row = ("z", "core")
    split = [P("crop", row, None, None), P("crop", row, None), P("crop"), P(row)]
    pair, single, lengths, share = split
    return jax.shard_map(
        functools.partial(fast_shards, crops, 2) if fast else shards,
        mesh=mesh,
        in_specs=(pair, single, lengths, share, share, share, pair, single),
        out_specs=(pair, single, pair, single, share, share, share, P()),
        check_vma=False,
    )
```

```python
import functools
import math

import jax
import jax.numpy as jnp
import numpy as np
from jax import lax
from jax.experimental import pallas as pl
from jax.experimental.pallas import tpu as pltpu
from jax.sharding import PartitionSpec as P

C = 128
H = 128
S = 384
TA_HEADS = 4
SA_HEADS = 16
STEP = 10
STRIDE = 128
LENGTH = 256

OUTGOING, INCOMING, STARTING, ENDING, PAIR, ATTEND, SINGLE = range(7)
(
    NORM_GAIN,
    NORM_BIAS,
    PROJ_GATE,
    OUT_GAIN,
    OUT_BIAS,
    PROJ_OUT,
    GATE_OUT,
    QKVG,
    BIAS_PROJ,
    OUTPUT,
    UP,
    DOWN,
    PAIR_GAIN,
    PAIR_BIAS,
    PAIR_PROJ,
    COLS,
    BIAS_W,
    BIAS_T,
    VECTORS,
    T,
) = range(7, 27)


EPSILON = 1e-05
MASKED = 1000000000.0
BETA_ONE = 0.9
BETA_TWO = 0.95
ADAM_EPS = 1e-08
CLIP = 1.0


def layout(pair_width, hidden_width, single_width, tri_heads, att_heads):
    entries = []
    for prefix in (OUTGOING, INCOMING):
        entries += [
            ((prefix, NORM_GAIN), (pair_width,)),
            ((prefix, NORM_BIAS), (pair_width,)),
            ((prefix, PROJ_GATE), (pair_width, 4 * hidden_width)),
            ((prefix, OUT_GAIN), (hidden_width,)),
            ((prefix, OUT_BIAS), (hidden_width,)),
            ((prefix, PROJ_OUT), (hidden_width, pair_width)),
            ((prefix, GATE_OUT), (pair_width, pair_width)),
        ]
    for prefix in (STARTING, ENDING):
        entries += [
            ((prefix, NORM_GAIN), (pair_width,)),
            ((prefix, NORM_BIAS), (pair_width,)),
            ((prefix, QKVG), (pair_width, 4 * pair_width)),
            ((prefix, BIAS_PROJ), (pair_width, tri_heads)),
            ((prefix, OUTPUT), (pair_width, pair_width)),
        ]
    entries += [
        ((PAIR, NORM_GAIN), (pair_width,)),
        ((PAIR, NORM_BIAS), (pair_width,)),
        ((PAIR, UP), (pair_width, 8 * pair_width)),
        ((PAIR, DOWN), (4 * pair_width, pair_width)),
        ((ATTEND, NORM_GAIN), (single_width,)),
        ((ATTEND, NORM_BIAS), (single_width,)),
        ((ATTEND, QKVG), (single_width, 4 * single_width)),
        ((ATTEND, PAIR_GAIN), (pair_width,)),
        ((ATTEND, PAIR_BIAS), (pair_width,)),
        ((ATTEND, PAIR_PROJ), (pair_width, att_heads)),
        ((ATTEND, OUTPUT), (single_width, single_width)),
        ((SINGLE, NORM_GAIN), (single_width,)),
        ((SINGLE, NORM_BIAS), (single_width,)),
        ((SINGLE, UP), (single_width, 8 * single_width)),
        ((SINGLE, DOWN), (4 * single_width, single_width)),
    ]
    return entries


def logical_order(flat):
    return flat.reshape(-1, STRIDE).T.reshape(-1)


def stored_order(vector):
    return vector.reshape(STRIDE, -1).T.reshape(-1)


def rate_tables(entries):
    rates = []
    decays = []
    for name, shape in entries:
        count = math.prod(shape)
        if len(shape) == 1:
            rates.append(np.full(count, 0.5, np.float32))
            decays.append(np.zeros(count, np.float32))
        else:
            rates.append(np.full(count, 2.0 / math.sqrt(shape[0]), np.float32))
            decays.append(np.full(count, 0.01, np.float32))
    rates = np.concatenate(rates)
    decays = np.concatenate(decays)
    return (rates.reshape(STRIDE, -1).T.reshape(-1), decays.reshape(STRIDE, -1).T.reshape(-1))


def unpack(flat, entries):
    pieces = {}
    offset = 0
    for name, shape in entries:
        count = math.prod(shape)
        pieces[name] = flat[offset : offset + count].reshape(shape)
        offset += count
    return pieces


def layer_norm(values, gain, shift):
    centred = values - jnp.mean(values, axis=-1, keepdims=True)
    spread = jnp.mean(centred * centred, axis=-1, keepdims=True)
    return centred * lax.rsqrt(spread + EPSILON) * gain + shift


def norm_backward(values, gain, shift, grad):
    _, pullback = jax.vjp(layer_norm, values, gain, shift)
    return pullback(grad)


def norm_pair(weights, prefix):
    return (
        weights[(prefix, NORM_GAIN)].astype(jnp.float32),
        weights[(prefix, NORM_BIAS)].astype(jnp.float32),
    )


def gated_pair(project, pair_mask):
    half = project.shape[-1] // 2
    return project[..., :half] * jax.nn.sigmoid(project[..., half:]) * pair_mask[..., None]


def gated_output(values, gate):
    return values * jax.nn.sigmoid(gate)


def swiglu(hidden):
    half = hidden.shape[-1] // 2
    return jax.nn.silu(hidden[..., :half]) * hidden[..., half:]


def matmul(left, right):
    return jnp.dot(left, right, preferred_element_type=jnp.float32)


def outer_sum(left, right):
    return jnp.einsum(
        "nc,nd->cd",
        left.reshape(-1, left.shape[-1]),
        right.reshape(-1, right.shape[-1]),
        preferred_element_type=jnp.float32,
    )


def flip(values):
    moved = lax.all_to_all(values, "row", split_axis=1, concat_axis=0, tiled=True)
    return jnp.swapaxes(moved, 0, 1)


def channel_forward(first, second, incoming):
    whole_first, whole_second = (
        lax.all_to_all(first, "row", split_axis=2, concat_axis=0, tiled=True),
        lax.all_to_all(second, "row", split_axis=2, concat_axis=0, tiled=True),
    )
    if incoming:
        local_tri = jnp.einsum(
            "kih,kjh->ijh", whole_first, whole_second, preferred_element_type=jnp.float32
        )
        local_tri = local_tri.astype(jnp.bfloat16).astype(jnp.float32)
    else:
        local_tri = jnp.einsum(
            "ikh,jkh->ijh", whole_first, whole_second, preferred_element_type=jnp.float32
        )
    tri = lax.all_to_all(
        local_tri.astype(jnp.bfloat16), "row", split_axis=0, concat_axis=2, tiled=True
    ).astype(local_tri.dtype)
    return (tri, whole_first, whole_second)


def channel_backward(grad_tri, whole_first, whole_second, incoming):
    whole_grad = lax.all_to_all(grad_tri, "row", split_axis=2, concat_axis=0, tiled=True)
    if incoming:
        grad_a = jnp.einsum(
            "ijh,kjh->kih", whole_grad, whole_second, preferred_element_type=jnp.float32
        )
        grad_b = jnp.einsum(
            "ijh,kih->kjh", whole_grad, whole_first, preferred_element_type=jnp.float32
        )
    else:
        grad_a = jnp.einsum(
            "ijh,jkh->ikh", whole_grad, whole_second, preferred_element_type=jnp.float32
        )
        grad_b = jnp.einsum(
            "ijh,ikh->jkh", whole_grad, whole_first, preferred_element_type=jnp.float32
        )
    return (
        lax.all_to_all(
            grad_a.astype(jnp.bfloat16), "row", split_axis=0, concat_axis=2, tiled=True
        ).astype(grad_a.dtype),
        lax.all_to_all(
            grad_b.astype(jnp.bfloat16), "row", split_axis=0, concat_axis=2, tiled=True
        ).astype(grad_b.dtype),
    )


def triangle_forward(state, pair_mask, weights, prefix, incoming):
    gain, shift = norm_pair(weights, prefix)
    lowered = layer_norm(state, gain, shift).astype(jnp.bfloat16)
    project = matmul(lowered, weights[(prefix, PROJ_GATE)])
    product = gated_pair(project, pair_mask).astype(jnp.bfloat16)
    half = product.shape[-1] // 2
    tri, own, other = channel_forward(product[..., :half], product[..., half:], incoming)
    out_gain = weights[(prefix, OUT_GAIN)].astype(jnp.float32)
    out_shift = weights[(prefix, OUT_BIAS)].astype(jnp.float32)
    out_low = layer_norm(tri, out_gain, out_shift).astype(jnp.bfloat16)
    output = matmul(out_low, weights[(prefix, PROJ_OUT)])
    gate_out = matmul(lowered, weights[(prefix, GATE_OUT)])
    update = gated_output(output, gate_out)
    return (update, (state, lowered, lowered, project, own, other, tri, out_low, output, gate_out))


def triangle_backward(saved, grad_update, pair_mask, weights, prefix, incoming, grads):
    state, lowered, framed, project, own, other, tri, out_low, output, gate_out = saved
    _, pullback = jax.vjp(gated_output, output, gate_out)
    grad_output, grad_gate = pullback(grad_update)
    grad_output = grad_output.astype(jnp.bfloat16)
    grad_gate = grad_gate.astype(jnp.bfloat16)
    grads[(prefix, PROJ_OUT)] = outer_sum(out_low, grad_output)
    grads[(prefix, GATE_OUT)] = outer_sum(lowered, grad_gate)
    grad_normed = matmul(grad_output, weights[(prefix, PROJ_OUT)].T)
    out_gain = weights[(prefix, OUT_GAIN)].astype(jnp.float32)
    out_shift = weights[(prefix, OUT_BIAS)].astype(jnp.float32)
    grad_tri, grads[(prefix, OUT_GAIN)], grads[(prefix, OUT_BIAS)] = norm_backward(
        tri, out_gain, out_shift, grad_normed
    )
    grad_tri = grad_tri.astype(jnp.bfloat16)
    grad_first, grad_second = channel_backward(grad_tri, own, other, incoming)
    _, pullback = jax.vjp(lambda values: gated_pair(values, pair_mask), project)
    (grad_project,) = pullback(jnp.concatenate([grad_first, grad_second], axis=-1))
    grad_project = grad_project.astype(jnp.bfloat16)
    grads[(prefix, PROJ_GATE)] = outer_sum(framed, grad_project)
    grad_framed = matmul(grad_project, weights[(prefix, PROJ_GATE)].T)
    if incoming:
        grad_framed = grad_framed.astype(jnp.bfloat16).astype(jnp.float32)
    grad_lowered = grad_framed + matmul(grad_gate, weights[(prefix, GATE_OUT)].T)
    gain, shift = norm_pair(weights, prefix)
    grad_state, grads[(prefix, NORM_GAIN)], grads[(prefix, NORM_BIAS)] = norm_backward(
        state, gain, shift, grad_lowered
    )
    return grad_state


def row_scores(query, key, bias, penalty, scale):
    scores = jnp.einsum("jhd,khd->hjk", query, key, preferred_element_type=jnp.float32) * scale
    return scores + bias.astype(jnp.float32) + penalty[None, None, :]


def attention_forward(state, penalty, weights, prefix, ending):
    gain, shift = norm_pair(weights, prefix)
    lowered = layer_norm(state, gain, shift).astype(jnp.bfloat16)
    framed = flip(lowered) if ending else lowered
    rows, length, width = framed.shape
    size = width // TA_HEADS
    scale = size ** (-0.5)
    qkvg = matmul(framed, weights[(prefix, QKVG)])
    queries = qkvg[..., :width].astype(jnp.bfloat16).reshape(rows, length, TA_HEADS, size)
    keys = qkvg[..., width : 2 * width].astype(jnp.bfloat16).reshape(rows, length, TA_HEADS, size)
    values = (
        qkvg[..., 2 * width : 3 * width].astype(jnp.bfloat16).reshape(rows, length, TA_HEADS, size)
    )
    gate = qkvg[..., 3 * width :]
    local_bias = (
        matmul(framed, weights[(prefix, BIAS_PROJ)]).astype(jnp.bfloat16).transpose(2, 0, 1)
    )
    bias = lax.all_gather(local_bias, "row", axis=1, tiled=True)

    def forward_row(items):
        query, key, value = items
        scores = row_scores(query, key, bias, penalty, scale)
        top = jnp.max(scores, axis=-1, keepdims=True)
        shifted = jnp.exp(scores - top)
        total = jnp.sum(shifted, axis=-1, keepdims=True)
        probs = (shifted / total).astype(jnp.bfloat16)
        mixed = jnp.einsum("hjk,khd->jhd", probs, value, preferred_element_type=jnp.float32)
        return (mixed, top[..., 0] + jnp.log(total[..., 0]))

    mixed, log_totals = lax.map(forward_row, (queries, keys, values))
    mixed = mixed.reshape(rows, length, width)
    gated_low = gated_output(mixed, gate).astype(jnp.bfloat16)
    returned = flip(gated_low) if ending else gated_low
    update = matmul(returned, weights[(prefix, OUTPUT)])
    return (update, (state, framed, queries, keys, values, gate, bias, mixed, log_totals, returned))


def attention_backward(saved, grad_update, penalty, weights, prefix, ending, grads):
    state, framed, queries, keys, values, gate, bias, mixed, log_totals, returned = saved
    rows, length, width = framed.shape
    size = width // TA_HEADS
    scale = size ** (-0.5)
    grad_low = grad_update.astype(jnp.bfloat16)
    grads[(prefix, OUTPUT)] = outer_sum(returned, grad_low)
    grad_gated = matmul(grad_low, weights[(prefix, OUTPUT)].T)
    if ending:
        grad_gated = flip(grad_gated.astype(jnp.bfloat16)).astype(jnp.float32)
    _, pullback = jax.vjp(gated_output, mixed, gate)
    grad_mixed, grad_gate = pullback(grad_gated)
    grad_mixed = grad_mixed.astype(jnp.bfloat16).reshape(rows, length, TA_HEADS, size)

    def back_row(carry, items):
        query, key, value, log_total, grad_row = items
        scores = row_scores(query, key, bias, penalty, scale)
        probs = jnp.exp(scores - log_total[..., None])
        grad_probs = jnp.einsum("jhd,khd->hjk", grad_row, value, preferred_element_type=jnp.float32)
        delta = jnp.sum(probs * grad_probs, axis=-1, keepdims=True)
        grad_scores = (probs * (grad_probs - delta)).astype(jnp.bfloat16)
        grad_query = (
            jnp.einsum("hjk,khd->jhd", grad_scores, key, preferred_element_type=jnp.float32) * scale
        )
        grad_key = (
            jnp.einsum("hjk,jhd->khd", grad_scores, query, preferred_element_type=jnp.float32)
            * scale
        )
        grad_value = jnp.einsum(
            "hjk,jhd->khd", probs.astype(jnp.bfloat16), grad_row, preferred_element_type=jnp.float32
        )
        return (carry + grad_scores.astype(jnp.float32), (grad_query, grad_key, grad_value))

    empty = jnp.zeros(bias.shape, jnp.float32)
    grad_bias, (grad_query, grad_key, grad_value) = lax.scan(
        back_row, empty, (queries, keys, values, log_totals, grad_mixed)
    )
    grad_bias = lax.psum_scatter(grad_bias, "row", scatter_dimension=1, tiled=True)
    grad_bias = grad_bias.transpose(1, 2, 0).astype(jnp.bfloat16)
    grad_qkvg = jnp.concatenate(
        [
            grad_query.reshape(rows, length, width),
            grad_key.reshape(rows, length, width),
            grad_value.reshape(rows, length, width),
            grad_gate,
        ],
        axis=-1,
    ).astype(jnp.bfloat16)
    grads[(prefix, QKVG)] = outer_sum(framed, grad_qkvg)
    grads[(prefix, BIAS_PROJ)] = outer_sum(framed, grad_bias)
    grad_framed = matmul(grad_qkvg, weights[(prefix, QKVG)].T) + matmul(
        grad_bias, weights[(prefix, BIAS_PROJ)].T
    )
    if ending:
        grad_framed = flip(grad_framed.astype(jnp.bfloat16)).astype(jnp.float32)
    gain, shift = norm_pair(weights, prefix)
    grad_state, grads[(prefix, NORM_GAIN)], grads[(prefix, NORM_BIAS)] = norm_backward(
        state, gain, shift, grad_framed
    )
    return grad_state


def transition_forward(state, weights, prefix):
    gain, shift = norm_pair(weights, prefix)
    lowered = layer_norm(state, gain, shift).astype(jnp.bfloat16)
    hidden = matmul(lowered, weights[(prefix, UP)])
    mixed_low = swiglu(hidden).astype(jnp.bfloat16)
    update = matmul(mixed_low, weights[(prefix, DOWN)])
    return (update, (state, lowered, hidden, mixed_low))


def transition_backward(saved, grad_update, weights, prefix, grads):
    state, lowered, hidden, mixed_low = saved
    grad_low = grad_update.astype(jnp.bfloat16)
    grads[(prefix, DOWN)] = outer_sum(mixed_low, grad_low)
    grad_mixed = matmul(grad_low, weights[(prefix, DOWN)].T)
    _, pullback = jax.vjp(swiglu, hidden)
    (grad_hidden,) = pullback(grad_mixed)
    grad_hidden = grad_hidden.astype(jnp.bfloat16)
    grads[(prefix, UP)] = outer_sum(lowered, grad_hidden)
    grad_lowered = matmul(grad_hidden, weights[(prefix, UP)].T)
    gain, shift = norm_pair(weights, prefix)
    grad_state, grads[(prefix, NORM_GAIN)], grads[(prefix, NORM_BIAS)] = norm_backward(
        state, gain, shift, grad_lowered
    )
    return grad_state


def single_forward(single_state, pair_state, penalty, weights):
    gain, shift = norm_pair(weights, ATTEND)
    lowered = layer_norm(single_state, gain, shift).astype(jnp.bfloat16)
    rows, width = lowered.shape
    size = width // SA_HEADS
    qkvg = matmul(lowered, weights[(ATTEND, QKVG)])
    query = qkvg[:, :width].astype(jnp.bfloat16).reshape(rows, SA_HEADS, size)
    key = qkvg[:, width : 2 * width].astype(jnp.bfloat16)
    value = qkvg[:, 2 * width : 3 * width].astype(jnp.bfloat16)
    gate = qkvg[:, 3 * width :]
    keys_all, values_all = (
        lax.all_gather(key, "row", axis=0, tiled=True),
        lax.all_gather(value, "row", axis=0, tiled=True),
    )
    keys_all = keys_all.reshape(-1, SA_HEADS, size)
    values_all = values_all.reshape(-1, SA_HEADS, size)
    pair_gain = weights[(ATTEND, PAIR_GAIN)].astype(jnp.float32)
    pair_shift = weights[(ATTEND, PAIR_BIAS)].astype(jnp.float32)
    pair_low = layer_norm(pair_state, pair_gain, pair_shift).astype(jnp.bfloat16)
    bias = matmul(pair_low, weights[(ATTEND, PAIR_PROJ)]).transpose(2, 0, 1)
    scores = jnp.einsum(
        "ihd,jhd->hij", query, keys_all, preferred_element_type=jnp.float32
    ) * size ** (-0.5)
    scores = scores + bias + penalty[None, None, :]
    probs = jax.nn.softmax(scores, axis=-1)
    probs_low = probs.astype(jnp.bfloat16)
    mixed = jnp.einsum(
        "hij,jhd->ihd", probs_low, values_all, preferred_element_type=jnp.float32
    ).reshape(rows, width)
    gated_low = gated_output(mixed, gate).astype(jnp.bfloat16)
    update = matmul(gated_low, weights[(ATTEND, OUTPUT)])
    return (
        update,
        (
            single_state,
            pair_state,
            lowered,
            query,
            keys_all,
            values_all,
            gate,
            pair_low,
            probs,
            probs_low,
            mixed,
            gated_low,
        ),
    )


def single_backward(saved, grad_update, weights, grads):
    (
        single_state,
        pair_state,
        lowered,
        query,
        keys_all,
        values_all,
        gate,
        pair_low,
        probs,
        probs_low,
        mixed,
        gated_low,
    ) = saved
    rows, width = lowered.shape
    size = width // SA_HEADS
    scale = size ** (-0.5)
    grad_low = grad_update.astype(jnp.bfloat16)
    grads[(ATTEND, OUTPUT)] = outer_sum(gated_low, grad_low)
    grad_gated = matmul(grad_low, weights[(ATTEND, OUTPUT)].T)
    _, pullback = jax.vjp(gated_output, mixed, gate)
    grad_mixed, grad_gate = pullback(grad_gated)
    grad_mixed = grad_mixed.astype(jnp.bfloat16).reshape(rows, SA_HEADS, size)
    grad_probs = jnp.einsum(
        "ihd,jhd->hij", grad_mixed, values_all, preferred_element_type=jnp.float32
    )
    delta = jnp.sum(probs * grad_probs, axis=-1, keepdims=True)
    grad_scores = (probs * (grad_probs - delta)).astype(jnp.bfloat16)
    grad_query = (
        jnp.einsum("hij,jhd->ihd", grad_scores, keys_all, preferred_element_type=jnp.float32)
        * scale
    )
    key_part = (
        jnp.einsum("hij,ihd->jhd", grad_scores, query, preferred_element_type=jnp.float32) * scale
    )
    value_part = jnp.einsum(
        "hij,ihd->jhd", probs_low, grad_mixed, preferred_element_type=jnp.float32
    )
    grad_key, grad_value = (
        lax.psum_scatter(key_part.reshape(-1, width), "row", scatter_dimension=0, tiled=True),
        lax.psum_scatter(value_part.reshape(-1, width), "row", scatter_dimension=0, tiled=True),
    )
    grad_qkvg = jnp.concatenate(
        [grad_query.reshape(rows, width), grad_key, grad_value, grad_gate], axis=-1
    ).astype(jnp.bfloat16)
    grads[(ATTEND, QKVG)] = outer_sum(lowered, grad_qkvg)
    grad_lowered = matmul(grad_qkvg, weights[(ATTEND, QKVG)].T)
    gain, shift = norm_pair(weights, ATTEND)
    grad_single, grads[(ATTEND, NORM_GAIN)], grads[(ATTEND, NORM_BIAS)] = norm_backward(
        single_state, gain, shift, grad_lowered
    )
    grad_bias = grad_scores.transpose(1, 2, 0)
    grads[(ATTEND, PAIR_PROJ)] = outer_sum(pair_low, grad_bias)
    grad_pair_low = matmul(grad_bias, weights[(ATTEND, PAIR_PROJ)].T)
    pair_gain = weights[(ATTEND, PAIR_GAIN)].astype(jnp.float32)
    pair_shift = weights[(ATTEND, PAIR_BIAS)].astype(jnp.float32)
    grad_pair, grads[(ATTEND, PAIR_GAIN)], grads[(ATTEND, PAIR_BIAS)] = norm_backward(
        pair_state, pair_gain, pair_shift, grad_pair_low
    )
    return (grad_single, grad_pair)


def shards(pair, single, lengths, params, moment_one, moment_two, pair_cotangent, single_cotangent):
    entries = layout(C, H, S, TA_HEADS, SA_HEADS)
    full = lax.all_gather(params.astype(jnp.bfloat16), "row", axis=0, tiled=True)
    weights = unpack(logical_order(full), entries)
    rows = pair.shape[1]
    length = pair.shape[2]
    first_row = lax.axis_index("row") * rows
    mask = (jnp.arange(length, dtype=jnp.int32) < lengths[0]).astype(jnp.float32)
    mask_rows = lax.dynamic_slice_in_dim(mask, first_row, rows)
    pair_mask = mask_rows[:, None] * mask[None, :]
    penalty = (mask - 1.0) * MASKED
    state = pair[0].astype(jnp.float32)
    saved = {}
    for prefix, incoming in ((OUTGOING, False), (INCOMING, True)):
        update, saved[prefix] = triangle_forward(state, pair_mask, weights, prefix, incoming)
        state = state + update
    for prefix, ending in ((STARTING, False), (ENDING, True)):
        update, saved[prefix] = attention_forward(state, penalty, weights, prefix, ending)
        state = state + update
    update, saved[PAIR] = transition_forward(state, weights, PAIR)
    pair_final = state + update
    single_state = single[0].astype(jnp.float32)
    update, saved[ATTEND] = single_forward(single_state, pair_final, penalty, weights)
    single_mid = single_state + update
    update, saved[SINGLE] = transition_forward(single_mid, weights, SINGLE)
    single_final = single_mid + update
    grads = {}
    grad_single = single_cotangent[0].astype(jnp.float32)
    grad_single = grad_single + transition_backward(
        saved[SINGLE], grad_single, weights, SINGLE, grads
    )
    from_single, from_pair = single_backward(saved[ATTEND], grad_single, weights, grads)
    grad_single = grad_single + from_single
    grad_pair = pair_cotangent[0].astype(jnp.float32) + from_pair
    grad_pair = grad_pair + transition_backward(saved[PAIR], grad_pair, weights, PAIR, grads)
    for prefix, ending in ((ENDING, True), (STARTING, False)):
        grad_pair = grad_pair + attention_backward(
            saved[prefix], grad_pair, penalty, weights, prefix, ending, grads
        )
    for prefix, incoming in ((INCOMING, True), (OUTGOING, False)):
        grad_pair = grad_pair + triangle_backward(
            saved[prefix], grad_pair, pair_mask, weights, prefix, incoming, grads
        )
    flat = stored_order(jnp.concatenate([grads[name].reshape(-1) for name, shape in entries]))
    shard_size = params.shape[0]
    row_index = lax.axis_index("row")
    total = lax.psum(flat, ("crop", "row"))
    shard = lax.dynamic_slice_in_dim(total, row_index * shard_size, shard_size)
    norm_squared = jnp.sum(total * total)
    clip_norm = jnp.sqrt(norm_squared)
    clipped = shard * (CLIP / jnp.maximum(clip_norm, CLIP))
    new_first = BETA_ONE * moment_one + (1.0 - BETA_ONE) * clipped
    new_second = BETA_TWO * moment_two + (1.0 - BETA_TWO) * clipped * clipped
    rates, decays = rate_tables(entries)
    rate_shard = lax.dynamic_slice_in_dim(jnp.asarray(rates), row_index * shard_size, shard_size)
    decay_shard = lax.dynamic_slice_in_dim(jnp.asarray(decays), row_index * shard_size, shard_size)
    first_hat = new_first / (1.0 - BETA_ONE**STEP)
    second_hat = new_second / (1.0 - BETA_TWO**STEP)
    new_params = params - rate_shard * (
        first_hat / (jnp.sqrt(second_hat) + ADAM_EPS) + decay_shard * params
    )
    return (
        pair_final.astype(jnp.bfloat16)[None],
        single_final.astype(jnp.bfloat16)[None],
        grad_pair[None],
        grad_single[None],
        new_params,
        new_first,
        new_second,
        clip_norm,
    )


F32 = jnp.float32
BF16 = jnp.bfloat16
LOG2E = 1.4426950408889634
VMEM_LIMIT = 56 * 1024 * 1024


def mm(left, right):
    return lax.dot_general(left, right, (((1,), (0,)), ((), ())), preferred_element_type=F32)


def mm_nt(left, right):
    return lax.dot_general(left, right, (((1,), (1,)), ((), ())), preferred_element_type=F32)


def mm_tn(left, right):
    return lax.dot_general(left, right, (((0,), (0,)), ((), ())), preferred_element_type=F32)


def standardize(values):
    centred = values - jnp.mean(values, axis=0, keepdims=True)
    spread = jnp.mean(centred * centred, axis=0, keepdims=True)
    inverse = lax.rsqrt(spread + EPSILON)
    return centred * inverse, inverse


def standardize_back(unit, inverse, grad_unit):
    first = jnp.mean(grad_unit, axis=0, keepdims=True)
    second = jnp.mean(grad_unit * unit, axis=0, keepdims=True)
    return inverse * (grad_unit - first - unit * second)


def sigmoid(values):
    return 0.5 * jnp.tanh(0.5 * values) + 0.5


def column(ref, index):
    return ref[:, index : index + 1]


def live_pair(info, alive, row):
    return jnp.concatenate(
        [jnp.where(info[row + place] > 0, alive[0:1], 0.0) for place in range(GROUP)], axis=1
    )


GROUP = 4
LAG = 4


def each_group(count, body):
    def step(index, carry):
        body(index * GROUP)
        return carry

    lax.fori_loop(0, count // GROUP, step, 0)


def each_channel(count, body):
    def step(index, carry):
        body(index)
        return carry

    lax.fori_loop(0, count, step, 0)


def join(read, ref, row):
    return jnp.concatenate([read(ref, row + place) for place in range(GROUP)], axis=1)


def pieces_of(values):
    length = values.shape[1] // GROUP
    return [values[:, place * length : (place + 1) * length] for place in range(GROUP)]


def put_rows(ref, row, values):
    for place, part in enumerate(pieces_of(values)):
        ref[row + place] = part.astype(ref.dtype)


def put_inner(scratch, row, values):
    for place, part in enumerate(pieces_of(values)):
        scratch[:, row + place, :] = part


def read_inner(scratch, row):
    return scratch[:, row, :]


def put_turned(scratch, row, values):
    for place, part in enumerate(pieces_of(values)):
        scratch[:, row + place, :] = part.T


def add_lanes(ref, values):
    ref[...] += sum(pieces_of(values))


def spec_full(shape):
    return pl.BlockSpec(shape, lambda step: (0,) * len(shape))


def spec_rows(shape, block, axis):
    sizes = tuple(block if place == axis else size for place, size in enumerate(shape))
    return pl.BlockSpec(
        sizes, lambda step: tuple(step if place == axis else 0 for place in range(len(shape)))
    )


def cost(microseconds):
    return pl.CostEstimate(
        flops=int(microseconds * 1e9), bytes_accessed=int(microseconds * 3e6), transcendentals=0
    )


def run_rows(kernel, name, steps, ins, outs, scratch, time=15):
    in_specs = []
    for array, axis in ins:
        if axis == "smem":
            in_specs.append(pl.BlockSpec(memory_space=pltpu.SMEM))
        elif axis is None:
            in_specs.append(spec_full(array.shape))
        else:
            in_specs.append(spec_rows(array.shape, array.shape[axis] // steps, axis))
    out_specs = []
    for shape, dtype, axis in outs:
        if axis is None:
            out_specs.append(spec_full(shape))
        else:
            out_specs.append(spec_rows(shape, shape[axis] // steps, axis))
    return pl.pallas_call(
        kernel,
        grid=(steps,),
        in_specs=in_specs,
        out_specs=out_specs,
        out_shape=[jax.ShapeDtypeStruct(shape, dtype) for shape, dtype, axis in outs],
        scratch_shapes=[pltpu.VMEM(shape, dtype) for shape, dtype in scratch],
        compiler_params=pltpu.CompilerParams(vmem_limit_bytes=VMEM_LIMIT),
        cost_estimate=cost(time),
        name=name,
    )(*[array for array, axis in ins])


def zero_first(*refs):
    @pl.when(pl.program_id(0) == 0)
    def _():
        for ref in refs:
            ref[...] = jnp.zeros(ref.shape, ref.dtype)


def lane_sums(ref):
    return jnp.sum(ref[...].T, axis=0, keepdims=True)


def on_last(steps, body):
    @pl.when(pl.program_id(0) == steps - 1)
    def _():
        body()


def read_plain(ref, row):
    return ref[row].astype(F32)


def reorder(values, order):
    size = values.shape[0] // len(order)
    return jnp.concatenate([values[place * size : (place + 1) * size] for place in order], axis=0)


def read_tokens(order, ref, row):
    return reorder(ref[row].astype(F32), order).T


def read_flipped(ref, row):
    parts = ref[:, row]
    return parts.reshape(-1, parts.shape[-1]).astype(F32).T


def read_turned(order, ref, row):
    parts = ref[:, row]
    return reorder(parts.reshape(-1, parts.shape[-1]).astype(F32), order).T


def tri_pre_row(info, alive, row, state, cols, first, proj_t):
    unit, inverse = standardize(state)
    lowered = (unit * column(cols, first) + column(cols, first + 1)).astype(BF16)
    project = mm(proj_t[...], lowered)
    half = project.shape[0] // 2
    return project[:half] * sigmoid(project[half:]) * live_pair(info, alive, row)


def store_product(out, scratch, devices):
    hidden = scratch.shape[0] // 2
    part = hidden // devices

    def one(device, carry):
        out[device, 0] = scratch[pl.ds(device * part, part)].astype(BF16)
        out[device, 1] = scratch[pl.ds(hidden + device * part, part)].astype(BF16)
        return carry

    lax.fori_loop(0, devices, one, 0)


def copy_blocks(target, source, count):
    def one(index, carry):
        target[index] = source[index].astype(target.dtype)
        return carry

    lax.fori_loop(0, count, one, 0)


def store_flipped(out, scratch):
    devices, part = out.shape[0], out.shape[1]

    def one(device, carry):
        out[device] = scratch[pl.ds(device * part, part)].astype(out.dtype)
        return carry

    lax.fori_loop(0, devices, one, 0)


def tri_post_row(state, tri, cols, proj_t, gate_t):
    unit, inverse = standardize(state)
    lowered = (unit * column(cols, 0) + column(cols, 1)).astype(BF16)
    tri_unit, tri_inverse = standardize(tri)
    out_low = (tri_unit * column(cols, 2) + column(cols, 3)).astype(BF16)
    output = mm(proj_t[...], out_low)
    gate = sigmoid(mm(gate_t[...], lowered))
    return unit, inverse, lowered, tri_unit, tri_inverse, out_low, output, gate


def row_base(rows):
    return pl.program_id(0) * rows


def tri_pre_first_kernel(devices, read, info, alive, pair, cols, proj_t, out, scratch):
    rows = pair.shape[0]

    def body(row):
        product = tri_pre_row(
            info, alive, row_base(rows) + row, join(read, pair, row), cols, 0, proj_t
        )
        put_inner(scratch, row, product)

    each_group(rows, body)
    store_product(out, scratch, devices)


def tri_product_kernel(incoming, operands, out):
    def body(channel):
        length = operands.shape[-1]
        first = operands[:, 0, channel].reshape(length, length)
        second = operands[:, 1, channel].reshape(length, length)
        tri = mm_tn(first, second) if incoming else mm_nt(first, second)
        out[:, channel] = tri.astype(BF16).reshape(out.shape[0], out.shape[2], length)

    each_channel(operands.shape[2], body)


def tri_join_kernel(
    devices, read, info, alive, source, tri_in, cols, proj_t, gate_t, next_cols, next_proj_t,
    state_out, out, tri_scratch, scratch,
):
    rows = state_out.shape[0]
    copy_blocks(tri_scratch, tri_in, tri_in.shape[0])

    def body(row):
        state = join(read, source, row)
        pieces = tri_post_row(state, join(read_inner, tri_scratch, row), cols, proj_t, gate_t)
        state = state + pieces[6] * pieces[7]
        put_rows(state_out, row, state)
        product = tri_pre_row(
            info, alive, row_base(rows) + row, state, next_cols, 0, next_proj_t
        )
        put_inner(scratch, row, product)

    each_group(rows, body)
    store_product(out, scratch, devices)


def tri_last_kernel(
    source, tri_in, cols, proj_t, gate_t, next_cols, bias_t, state_out, bias_out, tri_scratch, scratch
):
    rows = state_out.shape[0]
    copy_blocks(tri_scratch, tri_in, tri_in.shape[0])

    def body(row):
        state = join(read_plain, source, row)
        pieces = tri_post_row(state, join(read_inner, tri_scratch, row), cols, proj_t, gate_t)
        state = state + pieces[6] * pieces[7]
        put_rows(state_out, row, state)
        unit, inverse = standardize(state)
        lowered = (unit * column(next_cols, 0) + column(next_cols, 1)).astype(BF16)
        put_inner(scratch, row, mm(bias_t[...], lowered))

    each_group(rows, body)
    bias_out[...] = scratch[: bias_out.shape[0]].astype(BF16)


def flipped_bias_kernel(source, cols, bias_t, bias_out, scratch):
    rows = source.shape[1]

    def body(row):
        unit, inverse = standardize(join(read_flipped, source, row))
        lowered = (unit * column(cols, 0) + column(cols, 1)).astype(BF16)
        put_inner(scratch, row, mm(bias_t[...], lowered))

    each_group(rows, body)
    bias_out[...] = scratch[: bias_out.shape[0]].astype(BF16)


def fill_bias(alive, bias_in, table):
    @pl.when(pl.program_id(0) == 0)
    def _():
        length = table.shape[1]
        penalty = (alive[0:1] - 1.0) * (MASKED * LOG2E)
        for head in range(table.shape[0]):
            values = bias_in[:, head].reshape(length, length).astype(F32)
            table[head] = (values * LOG2E + penalty).T


def attention_row(state, cols, proj_t):
    unit, inverse = standardize(state)
    lowered = (unit * column(cols, 0) + column(cols, 1)).astype(BF16)
    project = mm(proj_t[...], lowered)
    width = project.shape[0] // 4
    size = width // TA_HEADS
    query = (project[:width] * (size**-0.5 * LOG2E)).astype(BF16)
    key = project[width : 2 * width].astype(BF16)
    value = project[2 * width : 3 * width].astype(BF16)
    gate = sigmoid(project[3 * width :])
    return unit, inverse, lowered, query, key, value, gate


def in_stages(blocks, first, second, third):
    early, late, done = {}, {}, {}
    count = len(blocks)
    for step in range(count + 2 * LAG):
        if step < count:
            early[step] = first(*blocks[step])
        if 0 <= step - LAG < count:
            late[step - LAG] = second(*blocks[step - LAG], early.pop(step - LAG))
        if 0 <= step - 2 * LAG < count:
            place = step - 2 * LAG
            done[blocks[place]] = third(*blocks[place], late.pop(place))
    return done


def head_rows(values, place, head):
    size, length = values.shape[0] // TA_HEADS, values.shape[1] // GROUP
    return values[head * size : (head + 1) * size, place * length : (place + 1) * length]


def gather_heads(done):
    return jnp.concatenate(
        [
            jnp.concatenate([done[place, head] for head in range(TA_HEADS)], axis=0)
            for place in range(GROUP)
        ],
        axis=1,
    )


ROW_BLOCKS = [(place, head) for place in range(GROUP) for head in range(TA_HEADS)]
HEAD_BLOCKS = [(place, head) for head in range(TA_HEADS) for place in range(GROUP)]


def attend_rows(state, row, cols, proj_t, output_t, table, totals, mixed_out):
    unit, inverse, lowered, query, key, value, gate = attention_row(state, cols, proj_t)

    def score(place, head):
        return mm_tn(head_rows(key, place, head), head_rows(query, place, head)) + table[head]

    def shift(place, head, scores):
        top = jnp.max(scores, axis=0, keepdims=True)
        return top, jnp.exp2(scores - top).astype(BF16)

    def mix(place, head, items):
        top, shifted = items
        values = head_rows(value, place, head)
        size = values.shape[0]
        values = jnp.concatenate([values, jnp.ones((16, values.shape[1]), BF16)], axis=0)
        result = mm(values, shifted)
        total = result[size : size + 1]
        return result[:size] / total, top + jnp.log2(total)

    done = in_stages(ROW_BLOCKS, score, shift, mix)
    mixed = gather_heads({block: items[0] for block, items in done.items()})
    put_rows(totals, row, gather_heads({block: items[1] for block, items in done.items()}))
    put_rows(mixed_out, row, mixed)
    return state + mm(output_t[...], (mixed * gate).astype(BF16))


def starting_kernel(
    alive, source, bias_in, cols, proj_t, output_t, out, totals, mixed, table, scratch
):
    fill_bias(alive, bias_in, table)
    rows = source.shape[0]

    def body(row):
        state = attend_rows(
            join(read_plain, source, row), row, cols, proj_t, output_t, table, totals, mixed
        )
        put_turned(scratch, row, state)

    each_group(rows, body)
    store_flipped(out, scratch)


def ending_kernel(alive, source, bias_in, cols, proj_t, output_t, out, totals, mixed, table):
    fill_bias(alive, bias_in, table)
    rows = source.shape[1]

    def body(row):
        state = attend_rows(
            join(read_flipped, source, row), row, cols, proj_t, output_t, table, totals, mixed
        )
        put_rows(out, row, state)

    each_group(rows, body)


def transition_kernel(
    order, source, cols, up_t, down_t, next_cols, bias_t, state_out, pair_out, bias_out, scratch, bias_scratch
):
    rows = source.shape[0]

    def body(row):
        state = join(read_plain, source, row)
        unit, inverse = standardize(state)
        lowered = (unit * column(cols, 0) + column(cols, 1)).astype(BF16)
        hidden = mm(up_t[...], lowered)
        half = hidden.shape[0] // 2
        first = hidden[:half]
        mixed = (first * sigmoid(first) * hidden[half:]).astype(BF16)
        state = state + mm(down_t[...], mixed)
        put_rows(state_out, row, state)
        put_turned(scratch, row, state)
        unit, inverse = standardize(state)
        lowered = (unit * column(next_cols, 0) + column(next_cols, 1)).astype(BF16)
        put_inner(bias_scratch, row, mm(bias_t[...], lowered))

    each_group(rows, body)
    size = pair_out.shape[0] // len(order)
    for place, held in enumerate(order):
        pair_out[place * size : (place + 1) * size] = scratch[held * size : (held + 1) * size].astype(BF16)
    bias_out[...] = bias_scratch[...].astype(BF16)


def transition_back_kernel(
    steps, read, mid, final, cotangent, bias_grad, cols, up_t, up, down, next_cols, bias_w,
    grad_out, up_grad, down_grad, bias_w_grad, vecs, norm_gain, norm_bias, pair_gain, pair_bias, bias_scratch,
):
    zero_first(up_grad, down_grad, bias_w_grad, norm_gain, norm_bias, pair_gain, pair_bias)
    rows = mid.shape[0]
    bias_scratch[...] = bias_grad[...].astype(F32)

    def body(row):
        grad = join(read, cotangent, row)
        unit, inverse = standardize(join(read_plain, final, row))
        gain = column(next_cols, 0)
        lowered = (unit * gain + column(next_cols, 1)).astype(BF16)
        grad_bias = join(read_inner, bias_scratch, row).astype(BF16)
        bias_w_grad[...] += mm_nt(lowered, grad_bias)
        grad_lowered = mm(bias_w[...], grad_bias)
        add_lanes(pair_gain, grad_lowered * unit)
        add_lanes(pair_bias, grad_lowered)
        grad = grad + standardize_back(unit, inverse, grad_lowered * gain)
        unit, inverse = standardize(join(read_plain, mid, row))
        gain = column(cols, 0)
        lowered = (unit * gain + column(cols, 1)).astype(BF16)
        hidden = mm(up_t[...], lowered)
        half = hidden.shape[0] // 2
        first, second = hidden[:half], hidden[half:]
        slope = sigmoid(first)
        silu = first * slope
        grad_low = grad.astype(BF16)
        grad_mixed = mm(down[...], grad_low)
        down_grad[...] += mm_nt((silu * second).astype(BF16), grad_low)
        grad_hidden = jnp.concatenate(
            [
                (grad_mixed * second * (slope + silu * (1.0 - slope))).astype(BF16),
                (grad_mixed * silu).astype(BF16),
            ],
            axis=0,
        )
        up_grad[...] += mm_nt(lowered, grad_hidden)
        grad_lowered = mm(up[...], grad_hidden)
        add_lanes(norm_gain, grad_lowered * unit)
        add_lanes(norm_bias, grad_lowered)
        put_rows(grad_out, row, grad + standardize_back(unit, inverse, grad_lowered * gain))

    each_group(rows, body)

    def finish():
        vecs[0:1] = lane_sums(norm_gain)
        vecs[1:2] = lane_sums(norm_bias)
        vecs[2:3] = lane_sums(pair_gain)
        vecs[3:4] = lane_sums(pair_bias)

    on_last(steps, finish)


def attention_back_kernel(
    steps, read, read_grad, alive, source, grad_in, bias_in, totals, mixed_in, cols, proj_t, proj, output,
    grad_out, bias_out, proj_grad, output_grad, table, grad_table,
):
    fill_bias(alive, bias_in, table)
    zero_first(proj_grad, output_grad, grad_table)
    rows = grad_out.shape[0]

    def body(row):
        unit, inverse, lowered, query, key, value, gate = attention_row(
            join(read, source, row), cols, proj_t
        )
        mixed = join(read_plain, mixed_in, row)
        total = join(read_plain, totals, row)
        grad_low = join(read_grad, grad_in, row).astype(BF16)
        gated = mixed * gate
        output_grad[...] += mm_nt(gated.astype(BF16), grad_low)
        grad_gated = mm(output[...], grad_low)
        grad_gate = grad_gated * gated * (1.0 - gate)
        grad_mixed = (grad_gated * gate).astype(BF16)
        product = grad_mixed.astype(F32) * mixed
        size = query.shape[0] // TA_HEADS

        def score(place, head):
            scores = mm_tn(head_rows(key, place, head), head_rows(query, place, head))
            grads = mm_tn(head_rows(value, place, head), head_rows(grad_mixed, place, head))
            return scores + table[head], grads

        def slope(place, head, items):
            scores, grads = items
            probs = jnp.exp2(scores - head_rows(total, place, head))
            delta = jnp.sum(head_rows(product, place, head), axis=0, keepdims=True)
            grad_scores = probs * (grads - delta)
            grad_table[head] += grad_scores
            return probs.astype(BF16), grad_scores.astype(BF16)

        def back(place, head, items):
            probs, grad_scores = items
            return (
                mm(head_rows(key, place, head), grad_scores) * size**-0.5,
                mm_nt(head_rows(query, place, head), grad_scores) * (1.0 / LOG2E),
                mm_nt(head_rows(grad_mixed, place, head), probs),
            )

        done = in_stages(HEAD_BLOCKS, score, slope, back)
        grad_project = jnp.concatenate(
            [
                gather_heads({block: items[part] for block, items in done.items()})
                for part in range(3)
            ]
            + [grad_gate],
            axis=0,
        ).astype(BF16)
        proj_grad[...] += mm_nt(lowered, grad_project)
        put_rows(grad_out, row, mm(proj[...], grad_project))

    each_group(rows, body)

    def finish():
        for head in range(TA_HEADS):
            bias_out[:, head] = (
                grad_table[head].T.astype(BF16).reshape(bias_out.shape[0], bias_out.shape[2], -1)
            )

    on_last(steps, finish)


def attention_end_row(
    state, grad, grad_lowered, grad_bias, cols, bias_w, bias_w_grad, norm_gain, norm_bias
):
    unit, inverse = standardize(state)
    gain = column(cols, 0)
    lowered = (unit * gain + column(cols, 1)).astype(BF16)
    bias_w_grad[...] += mm_nt(lowered, grad_bias)
    grad_lowered = grad_lowered + mm(bias_w[...], grad_bias)
    add_lanes(norm_gain, grad_lowered * unit)
    add_lanes(norm_bias, grad_lowered)
    return grad + standardize_back(unit, inverse, grad_lowered * gain)


def fill_bias_grad(scratch, bias_grad):
    heads = bias_grad.shape[1]
    total = bias_grad[0].astype(F32)
    for device in range(1, bias_grad.shape[0]):
        total = total + bias_grad[device].astype(F32)
    scratch[:heads] = total
    scratch[heads:] = jnp.zeros((scratch.shape[0] - heads,) + scratch.shape[1:], F32)


def ending_end_kernel(
    steps, source, grad_in, grad_lowered, bias_grad, cols, bias_w,
    grad_out, bias_w_grad, vecs, norm_gain, norm_bias, bias_scratch, scratch,
):
    zero_first(bias_w_grad, norm_gain, norm_bias)
    fill_bias_grad(bias_scratch, bias_grad)
    rows = grad_in.shape[0]

    def body(row):
        grad = attention_end_row(
            join(read_flipped, source, row), join(read_plain, grad_in, row),
            join(read_plain, grad_lowered, row), join(read_inner, bias_scratch, row).astype(BF16), cols, bias_w, bias_w_grad, norm_gain, norm_bias,
        )
        put_turned(scratch, row, grad)

    each_group(rows, body)
    store_flipped(grad_out, scratch)

    def finish():
        vecs[0:1] = lane_sums(norm_gain)
        vecs[1:2] = lane_sums(norm_bias)

    on_last(steps, finish)


def tri_post_back_row(
    state, tri, grad, cols, proj_t, gate_t, proj, gate_w, proj_grad, gate_grad, out_gain, out_bias
):
    unit, inverse, lowered, tri_unit, tri_inverse, out_low, output, gate = tri_post_row(
        state, tri, cols, proj_t, gate_t
    )
    grad_output = grad * gate
    grad_gate = (grad_output * output * (1.0 - gate)).astype(BF16)
    grad_output = grad_output.astype(BF16)
    proj_grad[...] += mm_nt(out_low, grad_output)
    gate_grad[...] += mm_nt(lowered, grad_gate)
    grad_normed = mm(proj[...], grad_output)
    add_lanes(out_gain, grad_normed * tri_unit)
    add_lanes(out_bias, grad_normed)
    grad_tri = standardize_back(tri_unit, tri_inverse, grad_normed * column(cols, 2))
    return grad_tri, mm(gate_w[...], grad_gate)


def starting_end_kernel(
    steps, source, grad_in, grad_lowered, bias_grad, cols, bias_w,
    below, tri_in, tri_cols, proj_t, gate_t, proj, gate_w,
    grad_out, tri_out, gate_back, bias_w_grad, proj_grad, gate_grad, vecs,
    norm_gain, norm_bias, out_gain, out_bias, bias_scratch, tri_scratch,
):
    zero_first(bias_w_grad, proj_grad, gate_grad, norm_gain, norm_bias, out_gain, out_bias)
    fill_bias_grad(bias_scratch, bias_grad)
    copy_blocks(tri_scratch, tri_in, tri_in.shape[0])
    rows = source.shape[0]

    def body(row):
        grad = attention_end_row(
            join(read_plain, source, row), join(read_flipped, grad_in, row),
            join(read_plain, grad_lowered, row), join(read_inner, bias_scratch, row).astype(BF16), cols, bias_w, bias_w_grad, norm_gain, norm_bias,
        )
        put_rows(grad_out, row, grad)
        grad_tri, back = tri_post_back_row(
            join(read_plain, below, row), join(read_inner, tri_scratch, row), grad, tri_cols, proj_t, gate_t, proj, gate_w,
            proj_grad, gate_grad, out_gain, out_bias,
        )
        put_rows(gate_back, row, back)
        put_inner(tri_scratch, row, grad_tri)

    each_group(rows, body)
    copy_blocks(tri_out, tri_scratch, tri_out.shape[0])

    def finish():
        vecs[0:1] = lane_sums(norm_gain)
        vecs[1:2] = lane_sums(norm_bias)
        vecs[2:3] = lane_sums(out_gain)
        vecs[3:4] = lane_sums(out_bias)

    on_last(steps, finish)


def tri_product_back_kernel(incoming, grad, operands, out):
    def body(channel):
        length = operands.shape[-1]
        first = operands[:, 0, channel].reshape(length, length)
        second = operands[:, 1, channel].reshape(length, length)
        tri = grad[:, channel].reshape(length, length)
        if incoming:
            grad_first = mm_nt(second, tri)
            grad_second = mm(first, tri)
        else:
            grad_first = mm(tri, second)
            grad_second = mm_tn(tri, first)
        shape = (out.shape[0], out.shape[3], length)
        out[:, 0, channel] = grad_first.astype(BF16).reshape(shape)
        out[:, 1, channel] = grad_second.astype(BF16).reshape(shape)

    each_channel(operands.shape[2], body)


def tri_pre_back_row(
    info, alive, row, state, product_grad, gate_back, grad, cols, proj_t, proj, proj_grad, norm_gain, norm_bias
):
    unit, inverse = standardize(state)
    gain = column(cols, 0)
    lowered = (unit * gain + column(cols, 1)).astype(BF16)
    project = mm(proj_t[...], lowered)
    half = project.shape[0] // 2
    gate = sigmoid(project[half:])
    grad_first = product_grad * gate * live_pair(info, alive, row)
    grad_second = grad_first * project[:half] * (1.0 - gate)
    grad_project = jnp.concatenate([grad_first.astype(BF16), grad_second.astype(BF16)], axis=0)
    proj_grad[...] += mm_nt(lowered, grad_project)
    grad_lowered = mm(proj[...], grad_project) + gate_back
    add_lanes(norm_gain, grad_lowered * unit)
    add_lanes(norm_bias, grad_lowered)
    return grad + standardize_back(unit, inverse, grad_lowered * gain)


def fill_product_grad(scratch, product_grad):
    devices, part = product_grad.shape[0], product_grad.shape[2]

    def one(device, carry):
        scratch[pl.ds(device * part, part)] = product_grad[device, 0].astype(F32)
        scratch[pl.ds((devices + device) * part, part)] = product_grad[device, 1].astype(F32)
        return carry

    lax.fori_loop(0, devices, one, 0)


def tri_join_back_kernel(
    steps, read, info, alive, source, product_grad, gate_in, grad_in, cols, proj_t, proj,
    below, tri_in, tri_cols, out_t, gate_t, out_w, gate_w,
    grad_out, tri_out, gate_back, proj_grad, out_grad, gate_grad, vecs,
    norm_gain, norm_bias, out_gain, out_bias, scratch, tri_scratch,
):
    zero_first(proj_grad, out_grad, gate_grad, norm_gain, norm_bias, out_gain, out_bias)
    fill_product_grad(scratch, product_grad)
    copy_blocks(tri_scratch, tri_in, tri_in.shape[0])
    rows = source.shape[0]

    def body(row):
        grad = tri_pre_back_row(
            info, alive, row_base(rows) + row, join(read_plain, source, row),
            join(read_inner, scratch, row), join(read_plain, gate_in, row),
            join(read_plain, grad_in, row), cols, proj_t, proj, proj_grad, norm_gain, norm_bias,
        )
        put_rows(grad_out, row, grad)
        grad_tri, back = tri_post_back_row(
            join(read, below, row), join(read_inner, tri_scratch, row), grad, tri_cols, out_t, gate_t, out_w, gate_w,
            out_grad, gate_grad, out_gain, out_bias,
        )
        put_rows(gate_back, row, back)
        put_inner(tri_scratch, row, grad_tri)

    each_group(rows, body)
    copy_blocks(tri_out, tri_scratch, tri_out.shape[0])

    def finish():
        vecs[0:1] = lane_sums(norm_gain)
        vecs[1:2] = lane_sums(norm_bias)
        vecs[2:3] = lane_sums(out_gain)
        vecs[3:4] = lane_sums(out_bias)

    on_last(steps, finish)


def tri_first_back_kernel(
    steps, read, order, info, alive, source, product_grad, gate_in, grad_in, cols, proj_t, proj,
    grad_out, proj_grad, vecs, norm_gain, norm_bias, scratch,
):
    zero_first(proj_grad, norm_gain, norm_bias)
    fill_product_grad(scratch, product_grad)
    rows = source.shape[0]

    def body(row):
        grad = tri_pre_back_row(
            info, alive, row_base(rows) + row, join(read, source, row),
            join(read_inner, scratch, row), join(read_plain, gate_in, row),
            join(read_plain, grad_in, row), cols, proj_t, proj, proj_grad, norm_gain, norm_bias,
        )
        for place, part in enumerate(pieces_of(grad)):
            grad_out[row + place] = reorder(part.T, order).astype(grad_out.dtype)

    each_group(rows, body)

    def finish():
        vecs[0:1] = lane_sums(norm_gain)
        vecs[1:2] = lane_sums(norm_bias)

    on_last(steps, finish)


RUN = 24


def table_of(entries):
    table = {}
    offset = 0
    for name, shape in entries:
        table[name] = (offset // STRIDE, shape)
        offset += math.prod(shape)
    return table, offset


def runs_kernel(info, shard, out, scratch):
    def one(block, carry):
        scratch[:, block, :] = shard[pl.ds(block * STRIDE, STRIDE), :].T
        return carry

    lax.fori_loop(0, RUN, one, 0)
    half = STRIDE // 2
    turn = info[0] * half

    def move(lane, carry):
        out[lane] = scratch[lax.rem(lane + turn, STRIDE)].astype(BF16)
        return carry

    lax.fori_loop(0, STRIDE, move, 0)


def run_place(shards, total, lane, shard):
    count = total // STRIDE
    whole = total // shards
    step, odd = whole // STRIDE, (whole % STRIDE) // (STRIDE // 2)
    extra = lax.div(shard * odd + jnp.where(lane < STRIDE // 2, 1, 0), 2)
    start = lane * count + shard * step + extra
    return lax.div(start, STRIDE), lax.rem(start, STRIDE)


def rows_from_runs(runs, rows, first_lane, total):
    shards, lanes = runs.shape[0], runs.shape[1]
    base = first_lane * (total // STRIDE) // STRIDE

    def one(index, carry):
        lane, shard = lax.div(index, shards), lax.rem(index, shards)
        row, shift = run_place(shards, total, first_lane + lane, shard)
        row = row - base
        turned = pltpu.roll(runs[shard, lane].astype(F32), shift, 1)
        place = lax.broadcasted_iota(jnp.int32, (RUN + 1, STRIDE), 1)
        last, before = carry
        joint = jnp.where(row - before == RUN, last[2:3], last[1:2])
        below = jnp.concatenate([joint, turned], axis=0)
        above = jnp.concatenate([turned, turned[RUN - 1 :]], axis=0)
        values = jnp.where(place < shift, below, above)
        rows[pl.ds(row, RUN + 1), :] = values
        return values[RUN - 2 :], row

    lax.fori_loop(0, shards * lanes, one, (jnp.zeros((3, STRIDE), F32), -RUN), unroll=4)


def runs_from_rows(rows, out, first_lane, base, total):
    shards, lanes = out.shape[0], out.shape[1]

    def one(index, carry):
        lane, shard = lax.div(index, shards), lax.rem(index, shards)
        row, shift = run_place(shards, total, first_lane + lane, shard)
        turned = pltpu.roll(rows[pl.ds(row - base, RUN + 1), :], (STRIDE - shift) % STRIDE, 1)
        place = lax.broadcasted_iota(jnp.int32, (RUN, STRIDE), 1)
        out[shard, lane] = jnp.where(
            place < STRIDE - shift, turned[:RUN], turned[1:]
        ).astype(BF16)
        return carry

    lax.fori_loop(0, shards * lanes, one, 0, unroll=4)


def row_height(base, first_lane, last_lane, total):
    end = (last_lane * (total // STRIDE)) // STRIDE + RUN + 2
    return -(-(end - base) // 8) * 8


def take_matrix(rows, first, shape):
    blocks = shape[1] // STRIDE
    return [
        rows[pl.ds(first + block, shape[0], stride=blocks), :]
        if blocks > 1
        else rows[first : first + shape[0], :]
        for block in range(blocks)
    ]


def put_matrix(rows, first, matrix):
    height, width = matrix.shape
    blocks = width // STRIDE
    for block in range(blocks):
        part = matrix[:, block * STRIDE : (block + 1) * STRIDE]
        if blocks > 1:
            rows[pl.ds(first + block, height, stride=blocks), :] = part
        else:
            rows[first : first + height, :] = part


def spread(index, heads, rows):
    lane = lax.broadcasted_iota(jnp.int32, (STRIDE, STRIDE), 0)
    channel = lax.broadcasted_iota(jnp.int32, (STRIDE, STRIDE), 1)
    return (channel == index * (STRIDE // heads) + lane // heads).astype(BF16)


def take_narrow(rows, first, heads, high):
    total = jnp.zeros((high, STRIDE), F32)
    head = lax.broadcasted_iota(jnp.int32, (high, STRIDE), 0)
    lane = lax.broadcasted_iota(jnp.int32, (high, STRIDE), 1)
    for index in range(heads):
        line = rows[first + index : first + index + 1, :]
        picked = jnp.where(lane % heads == head, line, 0.0).astype(BF16)
        total = total + mm(picked, spread(index, heads, rows))
    return total


def put_narrow(rows, first, heads, matrix):
    turned = matrix.T.astype(BF16)
    high = turned.shape[0]
    head = lax.broadcasted_iota(jnp.int32, (high, STRIDE), 0)
    lane = lax.broadcasted_iota(jnp.int32, (high, STRIDE), 1)
    for index in range(heads):
        wide = mm_nt(turned, spread(index, heads, rows))
        rows[first + index : first + index + 1, :] = jnp.sum(
            jnp.where(lane % heads == head, wide, 0.0), axis=0, keepdims=True
        )


PAIR_MATRICES = (
    (OUTGOING, PROJ_GATE), (OUTGOING, PROJ_OUT), (OUTGOING, GATE_OUT),
    (INCOMING, PROJ_GATE), (INCOMING, PROJ_OUT), (INCOMING, GATE_OUT),
    (STARTING, QKVG), (STARTING, OUTPUT), (ENDING, QKVG), (ENDING, OUTPUT), (PAIR, UP), (PAIR, DOWN),
)
PAIR_COLUMNS = (
    (OUTGOING, ((OUTGOING, NORM_GAIN), (OUTGOING, NORM_BIAS), (OUTGOING, OUT_GAIN), (OUTGOING, OUT_BIAS))),
    (INCOMING, ((INCOMING, NORM_GAIN), (INCOMING, NORM_BIAS), (INCOMING, OUT_GAIN), (INCOMING, OUT_BIAS))),
    (STARTING, ((STARTING, NORM_GAIN), (STARTING, NORM_BIAS))),
    (ENDING, ((ENDING, NORM_GAIN), (ENDING, NORM_BIAS))),
    (PAIR, ((PAIR, NORM_GAIN), (PAIR, NORM_BIAS))),
)
SINGLE_MATRICES = ((ATTEND, QKVG), (ATTEND, OUTPUT), (SINGLE, UP), (SINGLE, DOWN))
SINGLE_VECTORS = ((ATTEND, NORM_GAIN), (ATTEND, NORM_BIAS), (SINGLE, NORM_GAIN), (SINGLE, NORM_BIAS))


def put_columns(rows, out, table, base, names):
    out[...] = jnp.zeros(out.shape, F32)
    lines = [rows[table[name][0] - base : table[name][0] - base + 1, :] for name in names]
    lines.append(jnp.zeros((8 - len(lines), STRIDE), F32))
    out[...] = jnp.concatenate(lines, axis=0).T


def unpack_pair_kernel(table, total, runs, *refs):
    rows = refs[-1]
    outs = list(refs[:-1])
    rows_from_runs(runs, rows, 0, total)
    for name in PAIR_MATRICES:
        first, shape = table[name]
        plain, turned = outs.pop(0), outs.pop(0)
        for block, part in enumerate(take_matrix(rows, first, shape)):
            place = slice(block * STRIDE, (block + 1) * STRIDE)
            plain[:, place] = part.astype(BF16)
            turned[place, :] = part.T.astype(BF16)
    for prefix in (STARTING, ENDING):
        plain, turned = outs.pop(0), outs.pop(0)
        first, shape = table[(prefix, BIAS_PROJ)]
        matrix = take_narrow(rows, first, shape[1], 8)
        turned[...] = matrix.astype(BF16)
        plain[...] = matrix.T.astype(BF16)
    for prefix, names in PAIR_COLUMNS:
        put_columns(rows, outs.pop(0), table, 0, names)


def unpack_single_kernel(table, total, first_lane, runs, *refs):
    rows = refs[-1]
    outs = list(refs[:-1])
    rows_from_runs(runs, rows, first_lane, total)
    base = first_lane * (total // STRIDE) // STRIDE
    for name in SINGLE_MATRICES:
        first, shape = table[name]
        out = outs.pop(0)
        for block, part in enumerate(take_matrix(rows, first - base, shape)):
            out[:, block * STRIDE : (block + 1) * STRIDE] = part.astype(BF16)
    first, shape = table[(ATTEND, PAIR_PROJ)]
    matrix = take_narrow(rows, first - base, shape[1], shape[1])
    plain, turned = outs.pop(0), outs.pop(0)
    turned[...] = matrix.astype(BF16)
    plain[...] = matrix.T.astype(BF16)
    put_columns(rows, outs.pop(0), table, base, ((ATTEND, PAIR_GAIN), (ATTEND, PAIR_BIAS)))
    lines = outs.pop(0)
    lines[...] = jnp.zeros(lines.shape, F32)
    for index, name in enumerate(SINGLE_VECTORS):
        first, shape = table[name]
        for block in range(shape[0] // STRIDE):
            lines[index : index + 1, block * STRIDE : (block + 1) * STRIDE] = rows[
                first - base + block : first - base + block + 1, :
            ]


def pack_kernel(table, total, first_lane, base, names, *refs):
    ins, out, rows = refs[: len(names)], refs[-2], refs[-1]
    for name, ref in zip(names, ins):
        if isinstance(name, tuple):
            first, shape = table[name]
            if shape[1] % STRIDE:
                put_narrow(rows, first - base, shape[1], ref[...])
            else:
                put_matrix(rows, first - base, ref)
        else:
            for index, vector in name:
                first, shape = table[vector]
                for block in range(shape[0] // STRIDE):
                    rows[first + block - base : first + block - base + 1, :] = ref[
                        index : index + 1, block * STRIDE : (block + 1) * STRIDE
                    ]
    runs_from_rows(rows, out, first_lane, base, total)


def shard_kernel(whole, info, runs, out, squares):
    half = STRIDE // 2
    squares[...] = jnp.zeros(squares.shape, F32)

    def one(block, carry):
        first = runs[pl.ds(info[0] * half, half), block, :]
        second = runs[pl.ds(half - info[0] * half, half), block, :]
        values = jnp.concatenate([first, second], axis=0).T
        row = block * STRIDE + lax.broadcasted_iota(jnp.int32, values.shape, 0)
        lane = lax.broadcasted_iota(jnp.int32, values.shape, 1)
        values = jnp.where(row * STRIDE + lane < whole, values, 0.0)
        out[pl.ds(block * STRIDE, STRIDE), :] = values
        squares[...] += jnp.sum((values * values).reshape(-1, 8, STRIDE), axis=0)
        return carry

    lax.fori_loop(0, RUN, one, 0)


def whole_call(kernel, name, ins, outs, scratch, time=8):
    def spec(axis):
        return pl.BlockSpec(memory_space=pltpu.SMEM if axis == "smem" else pltpu.VMEM)

    return pl.pallas_call(
        kernel,
        in_specs=[spec(axis) for array, axis in ins],
        out_specs=[pl.BlockSpec(memory_space=pltpu.VMEM) for shape, dtype in outs],
        out_shape=[jax.ShapeDtypeStruct(shape, dtype) for shape, dtype in outs],
        scratch_shapes=[pltpu.VMEM(shape, dtype) for shape, dtype in scratch],
        compiler_params=pltpu.CompilerParams(vmem_limit_bytes=VMEM_LIMIT),
        cost_estimate=cost(time),
        name=name,
    )(*[array for array, axis in ins])


def unpack_pair(table, total, runs):
    outs = []
    names = []
    for name in PAIR_MATRICES:
        shape = table[name][1]
        outs += [(shape, BF16), (shape[::-1], BF16)]
        names += [name, (name, T)]
    for prefix in (STARTING, ENDING):
        outs += [((STRIDE, 8), BF16), ((8, STRIDE), BF16)]
        names += [(prefix, BIAS_W), (prefix, BIAS_T)]
    for prefix, parts in PAIR_COLUMNS:
        outs.append(((STRIDE, 8), F32))
        names.append((prefix, COLS))
    height = row_height(0, 0, runs.shape[1], total)
    values = whole_call(
        functools.partial(unpack_pair_kernel, table, total), "pair_weights", [(runs, None)], outs,
        [((height, STRIDE), F32)],
    )
    return dict(zip(names, values))


def unpack_single(table, total, first_lane, runs):
    outs = [(table[name][1], BF16) for name in SINGLE_MATRICES]
    names = list(SINGLE_MATRICES)
    shape = table[(ATTEND, PAIR_PROJ)][1]
    outs += [(shape, BF16), (shape[::-1], BF16), ((STRIDE, 8), F32), ((8, S), F32)]
    names += [(ATTEND, PAIR_PROJ), ((ATTEND, PAIR_PROJ), T), (ATTEND, COLS), (SINGLE, VECTORS)]
    base = first_lane * (total // STRIDE) // STRIDE
    height = row_height(base, first_lane, first_lane + runs.shape[1], total)
    values = whole_call(
        functools.partial(unpack_single_kernel, table, total, first_lane), "single_weights",
        [(runs, None)], outs, [((height, STRIDE), F32)],
    )
    return dict(zip(names, values))


def pack(name, table, total, shards, lanes, base, parts):
    height = row_height(base, *lanes, total)
    for held, array in parts:
        if isinstance(held, tuple):
            end = table[held][0] - base + array.shape[0] * max(1, array.shape[1] // STRIDE)
            height = max(height, -(-end // 8) * 8)
    return whole_call(
        functools.partial(pack_kernel, table, total, lanes[0], base, [held for held, array in parts]),
        name, [(array, None) for held, array in parts],
        [((shards, lanes[1] - lanes[0], RUN, STRIDE), BF16)], [((height, STRIDE), F32)],
    )[0]


def swap(values, group):
    return lax.all_to_all(values, group, split_axis=0, concat_axis=0, tiled=True)


def single_attend(single_state, bias, penalty, weights, group):
    gain, shift = norm_pair(weights, ATTEND)
    lowered = layer_norm(single_state, gain, shift).astype(BF16)
    rows, width = lowered.shape
    size = width // SA_HEADS
    qkvg = matmul(lowered, weights[(ATTEND, QKVG)])
    query = qkvg[:, :width].astype(BF16).reshape(rows, SA_HEADS, size)
    gate = qkvg[:, 3 * width :]
    both = lax.all_gather(qkvg[:, width : 3 * width].astype(BF16), group, axis=0, tiled=True)
    keys_all = both[:, :width].reshape(-1, SA_HEADS, size)
    values_all = both[:, width:].reshape(-1, SA_HEADS, size)
    scores = jnp.einsum(
        "ihd,jhd->hij", query, keys_all, preferred_element_type=F32
    ) * size ** (-0.5)
    scores = scores + bias + penalty[None, None, :]
    probs = jax.nn.softmax(scores, axis=-1)
    probs_low = probs.astype(BF16)
    mixed = jnp.einsum("hij,jhd->ihd", probs_low, values_all, preferred_element_type=F32)
    mixed = mixed.reshape(rows, width)
    gated_low = gated_output(mixed, gate).astype(BF16)
    update = matmul(gated_low, weights[(ATTEND, OUTPUT)])
    return (
        update,
        (single_state, lowered, query, keys_all, values_all, gate, probs, probs_low, mixed, gated_low),
    )


def single_attend_back(saved, grad_update, weights, grads, group):
    single_state, lowered, query, keys_all, values_all, gate, probs, probs_low, mixed, gated_low = saved
    rows, width = lowered.shape
    size = width // SA_HEADS
    scale = size ** (-0.5)
    grad_low = grad_update.astype(BF16)
    grads[(ATTEND, OUTPUT)] = outer_sum(gated_low, grad_low)
    grad_gated = matmul(grad_low, weights[(ATTEND, OUTPUT)].T)
    _, pullback = jax.vjp(gated_output, mixed, gate)
    grad_mixed, grad_gate = pullback(grad_gated)
    grad_mixed = grad_mixed.astype(BF16).reshape(rows, SA_HEADS, size)
    grad_probs = jnp.einsum("ihd,jhd->hij", grad_mixed, values_all, preferred_element_type=F32)
    delta = jnp.sum(probs * grad_probs, axis=-1, keepdims=True)
    grad_scores = (probs * (grad_probs - delta)).astype(BF16)
    grad_query = (
        jnp.einsum("hij,jhd->ihd", grad_scores, keys_all, preferred_element_type=F32) * scale
    )
    key_part = jnp.einsum("hij,ihd->jhd", grad_scores, query, preferred_element_type=F32) * scale
    value_part = jnp.einsum("hij,ihd->jhd", probs_low, grad_mixed, preferred_element_type=F32)
    parts = jnp.concatenate(
        [key_part.reshape(-1, rows, width), value_part.reshape(-1, rows, width)], axis=-1
    )
    grad_both = jnp.sum(swap(parts.astype(BF16), group).astype(F32), axis=0)
    grad_qkvg = jnp.concatenate(
        [grad_query.reshape(rows, width), grad_both, grad_gate], axis=-1
    ).astype(BF16)
    grads[(ATTEND, QKVG)] = outer_sum(lowered, grad_qkvg)
    grad_lowered = matmul(grad_qkvg, weights[(ATTEND, QKVG)].T)
    gain, shift = norm_pair(weights, ATTEND)
    grad_single, grads[(ATTEND, NORM_GAIN)], grads[(ATTEND, NORM_BIAS)] = norm_backward(
        single_state, gain, shift, grad_lowered
    )
    return grad_single, grad_scores


def to_plane(values, parts):
    shape = values.shape
    values = swap(values.reshape((parts, -1) + shape[1:]), "crop")
    return swap(values, "z").reshape(shape)


def from_plane(values, parts):
    shape = values.shape
    values = swap(values.reshape((parts, -1) + shape[1:]), "z")
    return swap(values, "crop").reshape(shape)


def after(values, *others):
    held = lax.optimization_barrier((values,) + others)
    return held


def pair_path(pair, info, alive, orders, weights, cotangent, middle, between, group, parts):
    rows, length, width = pair.shape
    hidden = weights[(OUTGOING, PROJ_OUT)].shape[0]
    devices = length // rows
    cores = devices // parts
    order, order_back = orders
    read_first = functools.partial(read_tokens, order)
    read_last = functools.partial(read_turned, order)
    part = hidden // devices
    steps = rows // 16
    state_shape = (rows, width, length)
    flip_shape = (devices, rows, rows, width)
    product_shape = (devices, 2, part, rows, length)
    tri_shape = (devices, part, rows, length)
    block = rows // steps
    channel_block = math.gcd(part, 4)

    def products(name, kernel, arrays, out_shape):
        axes = {4: 1, 5: 2}
        return run_rows(
            kernel, name, part // channel_block,
            [(array, axes[array.ndim]) for array in arrays],
            [(out_shape, BF16, axes[len(out_shape)])], [],
        )[0]

    def cols(prefix):
        return weights[(prefix, COLS)]

    tri_cols = cols

    def turned(name):
        return weights[(name, T)]

    tri_scratch = ((hidden, block, length), F32)
    product_scratch = ((2 * hidden, block, length), F32)
    head_scratch = ((8, block, length), F32)
    wide = ((width, length), F32)
    flip_scratch = ((length, block, width), F32)
    table = ((TA_HEADS, length, length), F32)
    attend_saves = [((rows, TA_HEADS, length), F32, 0), (state_shape, BF16, 0)]

    (product,) = run_rows(
        functools.partial(tri_pre_first_kernel, devices, read_first), "outgoing_in", steps,
        [
            (info, "smem"), (alive, None), (pair, 0), (tri_cols(OUTGOING), None),
            (turned((OUTGOING, PROJ_GATE)), None),
        ],
        [(product_shape, BF16, 3)], [product_scratch],
    )
    product_one = swap(product, group)
    tri_one = products(
        "outgoing_product", functools.partial(tri_product_kernel, False), [product_one], tri_shape
    )
    tri_one = swap(tri_one, group).reshape(hidden, rows, length)
    state_one, product = run_rows(
        functools.partial(tri_join_kernel, devices, read_first), "outgoing_out_incoming_in", steps,
        [
            (info, "smem"), (alive, None), (pair, 0), (tri_one, 1), (tri_cols(OUTGOING), None),
            (turned((OUTGOING, PROJ_OUT)), None), (turned((OUTGOING, GATE_OUT)), None),
            (tri_cols(INCOMING), None), (turned((INCOMING, PROJ_GATE)), None),
        ],
        [(state_shape, F32, 0), (product_shape, BF16, 3)], [tri_scratch, product_scratch],
    )
    product_two = swap(product, group)
    tri_two = products(
        "incoming_product", functools.partial(tri_product_kernel, True), [product_two], tri_shape
    )
    tri_two = swap(tri_two, group).reshape(hidden, rows, length)
    state_two, bias = run_rows(
        tri_last_kernel, "incoming_out_starting_bias", steps,
        [
            (state_one, 0), (tri_two, 1), (tri_cols(INCOMING), None),
            (turned((INCOMING, PROJ_OUT)), None), (turned((INCOMING, GATE_OUT)), None),
            (cols(STARTING), None), (weights[(STARTING, BIAS_T)], None),
        ],
        [(state_shape, F32, 0), ((TA_HEADS, rows, length), BF16, 1)], [tri_scratch, head_scratch],
    )
    bias_one = lax.all_gather(bias, group, axis=0, tiled=False)
    cotangent = cotangent.reshape(rows, parts, cores, parts, -1, width).transpose(3, 2, 1, 4, 0, 5)
    cotangent = swap(cotangent.reshape(flip_shape), group)
    cotangent = swap(cotangent.reshape((parts, cores) + flip_shape[1:]), "z").reshape(flip_shape)
    flipped, totals_one, mixed_one = run_rows(
        starting_kernel, "starting_attention", steps,
        [
            (alive, None), (state_two, 0), (bias_one, None), (cols(STARTING), None),
            (turned((STARTING, QKVG)), None), (turned((STARTING, OUTPUT)), None),
        ],
        [(flip_shape, BF16, 2)] + attend_saves, [table, flip_scratch],
    )
    state_three = swap(flipped, group)
    (bias,) = run_rows(
        flipped_bias_kernel, "ending_bias", steps,
        [(state_three, 1), (cols(ENDING), None), (weights[(ENDING, BIAS_T)], None)],
        [((TA_HEADS, rows, length), BF16, 1)], [head_scratch],
    )
    bias_two = lax.all_gather(bias, group, axis=0, tiled=False)
    state_four, totals_two, mixed_two = run_rows(
        ending_kernel, "ending_attention", steps,
        [
            (alive, None), (state_three, 1), (bias_two, None), (cols(ENDING), None),
            (turned((ENDING, QKVG)), None), (turned((ENDING, OUTPUT)), None),
        ],
        [(state_shape, F32, 0)] + attend_saves, [table],
    )
    pair_cols, attend_cols = cols(PAIR), cols(ATTEND)
    state_four, cotangent = after(state_four, cotangent)
    state_five, pair_out, single_bias = run_rows(
        functools.partial(transition_kernel, order_back), "pair_transition", steps,
        [
            (state_four, 0), (pair_cols, None), (turned((PAIR, UP)), None), (turned((PAIR, DOWN)), None),
            (attend_cols, None), (turned((ATTEND, PAIR_PROJ)), None),
        ],
        [(state_shape, F32, 0), ((length, rows, width), BF16, 1), ((SA_HEADS, rows, length), BF16, 1)],
        [flip_scratch, ((SA_HEADS, block, length), F32)],
    )
    pair_out = swap(pair_out.reshape((parts, -1) + pair_out.shape[1:]), "z")

    def turn(values):
        heads = values.shape[0]
        sent = values.reshape(heads, rows, devices, rows).transpose(2, 0, 3, 1)
        return swap(sent, group).transpose(1, 2, 0, 3).reshape(heads, rows, length)

    single_grad_scores = middle(turn(single_bias).astype(F32))
    grads = {}
    grad_four, grads[(PAIR, UP)], grads[(PAIR, DOWN)], grads[(ATTEND, PAIR_PROJ)], vecs = run_rows(
        functools.partial(transition_back_kernel, steps, read_last), "pair_transition_back", steps,
        [
            (state_four, 0), (state_five, 0), (cotangent, 1), (turn(single_grad_scores), 1),
            (pair_cols, None), (turned((PAIR, UP)), None), (weights[(PAIR, UP)], None),
            (weights[(PAIR, DOWN)], None), (attend_cols, None), (weights[(ATTEND, PAIR_PROJ)], None),
        ],
        [
            (state_shape, F32, 0), (weights[(PAIR, UP)].shape, F32, None),
            (weights[(PAIR, DOWN)].shape, F32, None), (weights[(ATTEND, PAIR_PROJ)].shape, F32, None),
            ((8, width), F32, None),
        ],
        [wide, wide, wide, wide, ((SA_HEADS, block, length), F32)],
    )
    grads[(PAIR, VECTORS)] = vecs

    grad_four, pair_out = after(grad_four, pair_out)
    pair_out = swap(pair_out.reshape(flip_shape), group)

    def attention_back(prefix, read, read_grad, source, source_axis, grad, grad_axis, bias, totals, mixed):
        lowered_grad, bias_grad, grads[(prefix, QKVG)], grads[(prefix, OUTPUT)] = run_rows(
            functools.partial(attention_back_kernel, steps, read, read_grad),
            "attention_back", steps,
            [
                (alive, None), (source, source_axis), (grad, grad_axis), (bias, None), (totals, 0),
                (mixed, 0), (cols(prefix), None), (turned((prefix, QKVG)), None),
                (weights[(prefix, QKVG)], None), (weights[(prefix, OUTPUT)], None),
            ],
            [
                (state_shape, BF16, 0), ((devices, TA_HEADS, rows, length), BF16, None),
                (weights[(prefix, QKVG)].shape, F32, None), (weights[(prefix, OUTPUT)].shape, F32, None),
            ],
            [table, table],
        )
        return lowered_grad, swap(bias_grad, group)

    lowered_grad, bias_grad = attention_back(
        ENDING, read_flipped, read_plain, state_three, 1, grad_four, 0, bias_two, totals_two, mixed_two
    )
    bias_grad, pair_out = after(bias_grad, pair_out)
    pair_out = pair_out.reshape(parts, cores, rows, parts, -1, width).transpose(2, 3, 1, 0, 4, 5)
    pair_out = pair_out.reshape(rows, length, width)
    flipped, bias_w_grad, vecs = run_rows(
        functools.partial(ending_end_kernel, steps), "ending_attention_end", steps,
        [
            (state_three, 1), (grad_four, 0), (lowered_grad, 0), (bias_grad, 2), (cols(ENDING), None),
            (weights[(ENDING, BIAS_W)], None),
        ],
        [(flip_shape, BF16, 2), ((width, 8), F32, None), ((8, width), F32, None)],
        [wide, wide, head_scratch, flip_scratch],
    )
    grads[(ENDING, BIAS_PROJ)], grads[(ENDING, VECTORS)] = bias_w_grad, vecs
    grad_three = swap(flipped, group)
    grad_three, *_ = after(grad_three, between(0, grads))
    lowered_grad, bias_grad = attention_back(
        STARTING, read_plain, read_flipped, state_two, 0, grad_three, 1, bias_one, totals_one, mixed_one
    )
    square = weights[(INCOMING, GATE_OUT)].shape
    (
        grad_two, grad_tri, gate_back, bias_w_grad, grads[(INCOMING, PROJ_OUT)], grads[(INCOMING, GATE_OUT)], vecs,
    ) = run_rows(
        functools.partial(starting_end_kernel, steps), "starting_end_incoming_out_back", steps,
        [
            (state_two, 0), (grad_three, 1), (lowered_grad, 0), (bias_grad, 2), (cols(STARTING), None),
            (weights[(STARTING, BIAS_W)], None), (state_one, 0), (tri_two, 1), (tri_cols(INCOMING), None),
            (turned((INCOMING, PROJ_OUT)), None), (turned((INCOMING, GATE_OUT)), None),
            (weights[(INCOMING, PROJ_OUT)], None), (weights[(INCOMING, GATE_OUT)], None),
        ],
        [
            (state_shape, F32, 0), ((hidden, rows, length), BF16, 1), (state_shape, BF16, 0),
            ((width, 8), F32, None), (square, F32, None), (square, F32, None), ((8, width), F32, None),
        ],
        [wide, wide, wide, wide, head_scratch, tri_scratch],
    )
    grads[(STARTING, BIAS_PROJ)], grads[(STARTING, VECTORS)] = bias_w_grad, vecs
    grad_tri = swap(grad_tri.reshape(tri_shape), group)
    product_grad = swap(
        products(
            "incoming_product_back", functools.partial(tri_product_back_kernel, True),
            [grad_tri, product_two], product_shape,
        ),
        group,
    )
    (
        grad_one, grad_tri, gate_back, grads[(INCOMING, PROJ_GATE)], grads[(OUTGOING, PROJ_OUT)],
        grads[(OUTGOING, GATE_OUT)], vecs,
    ) = run_rows(
        functools.partial(tri_join_back_kernel, steps, read_first), "incoming_in_outgoing_out_back", steps,
        [
            (info, "smem"), (alive, None), (state_one, 0), (product_grad, 3), (gate_back, 0), (grad_two, 0),
            (tri_cols(INCOMING), None), (turned((INCOMING, PROJ_GATE)), None),
            (weights[(INCOMING, PROJ_GATE)], None), (pair, 0), (tri_one, 1), (tri_cols(OUTGOING), None),
            (turned((OUTGOING, PROJ_OUT)), None), (turned((OUTGOING, GATE_OUT)), None),
            (weights[(OUTGOING, PROJ_OUT)], None), (weights[(OUTGOING, GATE_OUT)], None),
        ],
        [
            (state_shape, F32, 0), ((hidden, rows, length), BF16, 1), (state_shape, BF16, 0),
            (weights[(INCOMING, PROJ_GATE)].shape, F32, None), (square, F32, None), (square, F32, None),
            ((8, width), F32, None),
        ],
        [wide, wide, wide, wide, product_scratch, tri_scratch],
    )
    grads[(INCOMING, VECTORS)] = vecs
    between(1, grads)
    grad_tri = swap(grad_tri.reshape(tri_shape), group)
    product_grad = swap(
        products(
            "outgoing_product_back", functools.partial(tri_product_back_kernel, False),
            [grad_tri, product_one], product_shape,
        ),
        group,
    )
    pair_grad, grads[(OUTGOING, PROJ_GATE)], vecs = run_rows(
        functools.partial(tri_first_back_kernel, steps, read_first, order_back), "outgoing_in_back", steps,
        [
            (info, "smem"), (alive, None), (pair, 0), (product_grad, 3), (gate_back, 0), (grad_one, 0),
            (tri_cols(OUTGOING), None), (turned((OUTGOING, PROJ_GATE)), None),
            (weights[(OUTGOING, PROJ_GATE)], None),
        ],
        [
            ((rows, length, width), BF16, 0), (weights[(OUTGOING, PROJ_GATE)].shape, F32, None),
            ((8, width), F32, None),
        ],
        [wide, wide, product_scratch],
    )
    grads[(OUTGOING, VECTORS)] = vecs
    return pair_out, pair_grad, grads


HELD = {
    (PAIR, VECTORS): ((PAIR, NORM_GAIN), (PAIR, NORM_BIAS), (ATTEND, PAIR_GAIN), (ATTEND, PAIR_BIAS)),
    (ENDING, VECTORS): ((ENDING, NORM_GAIN), (ENDING, NORM_BIAS)),
    (STARTING, VECTORS): (
        (STARTING, NORM_GAIN), (STARTING, NORM_BIAS), (INCOMING, OUT_GAIN), (INCOMING, OUT_BIAS)
    ),
    (INCOMING, VECTORS): (
        (INCOMING, NORM_GAIN), (INCOMING, NORM_BIAS), (OUTGOING, OUT_GAIN), (OUTGOING, OUT_BIAS)
    ),
    (OUTGOING, VECTORS): ((OUTGOING, NORM_GAIN), (OUTGOING, NORM_BIAS)),
}


def vector_part(grads, name, prefix):
    pairs = [(row, held) for row, held in enumerate(HELD[name]) if prefix in (None, held[0])]
    return (pairs, grads[name])


def fast_shards(parts, cores, pair, single, lengths, params, moment_one, moment_two, pair_cotangent, single_cotangent):
    entries = layout(C, H, S, TA_HEADS, SA_HEADS)
    table, total = table_of(entries)
    count = total // STRIDE
    shard_size = params.shape[0]
    attend = table[(ATTEND, NORM_GAIN)][0]
    pair_lanes = -(-attend * STRIDE // count)
    single_lane = attend * STRIDE // count
    devices = parts * cores
    line, group = ("z", "core"), ("crop", "core")
    row_index = lax.axis_index(line)
    odd = ((row_index * shard_size) % STRIDE) // (STRIDE // 2)
    place = jnp.stack([odd, odd]).astype(jnp.int32)
    shard_rows = jnp.pad(params, (0, RUN * STRIDE * STRIDE - shard_size)).reshape(-1, STRIDE)
    (runs,) = whole_call(
        runs_kernel, "parameter_runs", [(place, "smem"), (shard_rows, None)],
        [((STRIDE, RUN, STRIDE), BF16)], [((STRIDE, RUN, STRIDE), F32)],
    )
    rows, length, width = pair.shape[1:]
    pair_in = swap(pair[0].reshape(parts, -1, length, width), "crop")
    pair_in, first_runs, live = after(
        pair_in, runs[:pair_lanes], swap(jnp.broadcast_to(lengths.astype(F32), (parts, STRIDE)), "crop")
    )
    pair_in = swap(pair_in, "z").reshape(rows, length, width)
    weights = unpack_pair(table, total, lax.all_gather(first_runs, line))
    pair_in, last_runs = after(pair_in, runs[single_lane:])
    weights.update(unpack_single(table, total, single_lane, lax.all_gather(last_runs, line)))
    for index, name in enumerate(SINGLE_VECTORS):
        weights[name] = weights[(SINGLE, VECTORS)][index]
    size = rows // parts
    blocks = np.arange(length // size).reshape(parts, cores, parts)
    order = blocks.transpose(2, 1, 0).reshape(-1)
    orders = (order.tolist(), np.argsort(order).tolist())
    tokens = (order[:, None] * size + np.arange(size)).reshape(-1)
    live = live[lax.axis_index("z"), 0]
    width = single.shape[2]
    both = to_plane(jnp.concatenate([single[0], single_cotangent[0]], axis=1), parts).astype(F32)
    single_state, single_back = both[:, :width], both[:, width:]
    mask = (tokens.astype(np.float32) < live).astype(F32)
    info = lax.dynamic_slice_in_dim(mask, lax.axis_index(group) * rows, rows).astype(jnp.int32)
    alive = jnp.broadcast_to(mask, (8, length))
    penalty = (mask - 1.0) * MASKED
    results = {}
    single_grads = {}

    def middle(bias):
        update, saved = single_attend(single_state, bias, penalty, weights, group)
        single_mid = single_state + update
        update, saved_last = transition_forward(single_mid, weights, SINGLE)
        results[SINGLE] = single_mid + update
        grad = single_back
        grad = grad + transition_backward(saved_last, grad, weights, SINGLE, single_grads)
        more, grad_scores = single_attend_back(saved, grad, weights, single_grads, group)
        results["single_grad"] = grad + more
        return grad_scores

    def reduce_runs(sent):
        part = jnp.sum(swap(sent, line).astype(F32), axis=0).astype(BF16)
        return jnp.sum(lax.all_gather(part, "crop").astype(F32), axis=0)

    reduced = {}
    lines_held = list(enumerate(SINGLE_VECTORS))
    late_lanes = -(-table[(INCOMING, NORM_GAIN)][0] * STRIDE // count)

    def lines():
        values = jnp.concatenate([single_grads[name].reshape(1, S) for name in SINGLE_VECTORS], axis=0)
        return jnp.pad(values, ((0, 8 - len(SINGLE_VECTORS)), (0, 0)))

    def between(number, grads):
        if number == 0:
            sent = pack(
                "single_gradient", table, total, devices, (pair_lanes, STRIDE), attend,
                [(name, single_grads[name]) for name in SINGLE_MATRICES]
                + [((ATTEND, PAIR_PROJ), grads[(ATTEND, PAIR_PROJ)])]
                + [vector_part(grads, (PAIR, VECTORS), ATTEND), (lines_held, lines())],
            )
            reduced[2] = lax.psum(
                lax.psum_scatter(sent, line, scatter_dimension=0, tiled=False), "crop"
            ).astype(F32)
            return sent
        taken = -(-(pair_lanes * count - (attend + 2 * S // STRIDE) * STRIDE) // (4 * S))
        first = table[(INCOMING, NORM_GAIN)][0]
        sent = pack(
            "pair_gradient", table, total, devices, (late_lanes, pair_lanes), first,
            [(name, grads[name]) for name in PAIR_MATRICES if table[name][0] >= first]
            + [(name, grads[name]) for name in ((STARTING, BIAS_PROJ), (ENDING, BIAS_PROJ))]
            + [vector_part(grads, name, None) for name in ((ENDING, VECTORS), (STARTING, VECTORS))]
            + [vector_part(grads, (INCOMING, VECTORS), INCOMING)]
            + [vector_part(grads, (PAIR, VECTORS), PAIR)]
            + [(lines_held[:2], lines()), ((ATTEND, QKVG), single_grads[(ATTEND, QKVG)][: -(-taken // 8) * 8])],
        )
        reduced[1] = reduce_runs(sent)
        return sent

    pair_out, pair_grad, grads = pair_path(
        pair_in, info, alive, orders, weights, pair_cotangent[0], middle, between, group, parts
    )
    pair_grad = from_plane(pair_grad, parts).astype(F32)
    both = from_plane(jnp.concatenate([results[SINGLE], results["single_grad"]], axis=1), parts)
    single_out, single_grad = both[:, :width].astype(BF16), both[:, width:]
    first = table[(INCOMING, NORM_GAIN)][0]
    taken = -(-(late_lanes * count - (first + 2) * STRIDE) // (4 * H))
    sent = pack(
        "outgoing_gradient", table, total, devices, (0, late_lanes), 0,
        [(name, grads[name]) for name in PAIR_MATRICES if table[name][0] < first]
        + [vector_part(grads, (OUTGOING, VECTORS), None)]
        + [vector_part(grads, (INCOMING, VECTORS), None)]
        + [((INCOMING, PROJ_GATE), grads[(INCOMING, PROJ_GATE)][: -(-taken // 8) * 8])],
    )
    reduced[0] = reduce_runs(sent)
    shard, squares = whole_call(
        functools.partial(shard_kernel, shard_size), "gradient_share",
        [(place, "smem"), (jnp.concatenate([reduced[part] for part in range(3)], axis=0), None)],
        [((RUN * STRIDE, STRIDE), F32), ((8, STRIDE), F32)], [],
    )
    shard = shard.reshape(-1)[:shard_size]
    clip_norm = jnp.sqrt(jnp.sum(lax.all_gather(squares, line)))
    clipped = shard * (CLIP / jnp.maximum(clip_norm, CLIP))
    new_first = BETA_ONE * moment_one + (1.0 - BETA_ONE) * clipped
    new_second = BETA_TWO * moment_two + (1.0 - BETA_TWO) * clipped * clipped
    rates, decays = rate_tables(entries)
    rate_shard = lax.dynamic_slice_in_dim(jnp.asarray(rates), row_index * shard_size, shard_size)
    decay_shard = lax.dynamic_slice_in_dim(jnp.asarray(decays), row_index * shard_size, shard_size)
    first_hat = new_first / (1.0 - BETA_ONE**STEP)
    second_hat = new_second / (1.0 - BETA_TWO**STEP)
    new_params = params - rate_shard * (
        first_hat / (jnp.sqrt(second_hat) + ADAM_EPS) + decay_shard * params
    )
    return (
        pair_out[None],
        single_out[None],
        pair_grad[None],
        single_grad[None],
        new_params,
        new_first,
        new_second,
        clip_norm,
    )


def solution(mesh):
    crops, devices = mesh.devices.shape
    count = table_of(layout(C, H, S, TA_HEADS, SA_HEADS))[1] // STRIDE
    fast = devices == 2 * crops and LENGTH % (devices * 16) == 0 and count // devices + 2 <= RUN * STRIDE
    row = "row"
    if fast:
        mesh = jax.sharding.Mesh(mesh.devices.reshape(crops, crops, 2), ("crop", "z", "core"))
        row = ("z", "core")
    split = [P("crop", row, None, None), P("crop", row, None), P("crop"), P(row)]
    pair, single, lengths, share = split
    return jax.shard_map(
        functools.partial(fast_shards, crops, 2) if fast else shards,
        mesh=mesh,
        in_specs=(pair, single, lengths, share, share, share, pair, single),
        out_specs=(pair, single, pair, single, share, share, share, P()),
        check_vma=False,
    )
```

```python
import functools
import math

import jax
import jax.numpy as jnp
import numpy as np
from jax import lax
from jax.experimental import pallas as pl
from jax.experimental.pallas import tpu as pltpu
from jax.sharding import PartitionSpec as P

C = 128
H = 128
S = 384
TA_HEADS = 4
SA_HEADS = 16
STEP = 10
STRIDE = 128
LENGTH = 256

OUTGOING, INCOMING, STARTING, ENDING, PAIR, ATTEND, SINGLE = range(7)
(
    NORM_GAIN,
    NORM_BIAS,
    PROJ_GATE,
    OUT_GAIN,
    OUT_BIAS,
    PROJ_OUT,
    GATE_OUT,
    QKVG,
    BIAS_PROJ,
    OUTPUT,
    UP,
    DOWN,
    PAIR_GAIN,
    PAIR_BIAS,
    PAIR_PROJ,
    COLS,
    BIAS_W,
    BIAS_T,
    VECTORS,
    T,
) = range(7, 27)


EPSILON = 1e-05
MASKED = 1000000000.0
BETA_ONE = 0.9
BETA_TWO = 0.95
ADAM_EPS = 1e-08
CLIP = 1.0


def layout(pair_width, hidden_width, single_width, tri_heads, att_heads):
    entries = []
    for prefix in (OUTGOING, INCOMING):
        entries += [
            ((prefix, NORM_GAIN), (pair_width,)),
            ((prefix, NORM_BIAS), (pair_width,)),
            ((prefix, PROJ_GATE), (pair_width, 4 * hidden_width)),
            ((prefix, OUT_GAIN), (hidden_width,)),
            ((prefix, OUT_BIAS), (hidden_width,)),
            ((prefix, PROJ_OUT), (hidden_width, pair_width)),
            ((prefix, GATE_OUT), (pair_width, pair_width)),
        ]
    for prefix in (STARTING, ENDING):
        entries += [
            ((prefix, NORM_GAIN), (pair_width,)),
            ((prefix, NORM_BIAS), (pair_width,)),
            ((prefix, QKVG), (pair_width, 4 * pair_width)),
            ((prefix, BIAS_PROJ), (pair_width, tri_heads)),
            ((prefix, OUTPUT), (pair_width, pair_width)),
        ]
    entries += [
        ((PAIR, NORM_GAIN), (pair_width,)),
        ((PAIR, NORM_BIAS), (pair_width,)),
        ((PAIR, UP), (pair_width, 8 * pair_width)),
        ((PAIR, DOWN), (4 * pair_width, pair_width)),
        ((ATTEND, NORM_GAIN), (single_width,)),
        ((ATTEND, NORM_BIAS), (single_width,)),
        ((ATTEND, QKVG), (single_width, 4 * single_width)),
        ((ATTEND, PAIR_GAIN), (pair_width,)),
        ((ATTEND, PAIR_BIAS), (pair_width,)),
        ((ATTEND, PAIR_PROJ), (pair_width, att_heads)),
        ((ATTEND, OUTPUT), (single_width, single_width)),
        ((SINGLE, NORM_GAIN), (single_width,)),
        ((SINGLE, NORM_BIAS), (single_width,)),
        ((SINGLE, UP), (single_width, 8 * single_width)),
        ((SINGLE, DOWN), (4 * single_width, single_width)),
    ]
    return entries


def logical_order(flat):
    return flat.reshape(-1, STRIDE).T.reshape(-1)


def stored_order(vector):
    return vector.reshape(STRIDE, -1).T.reshape(-1)


def rate_tables(entries):
    rates = []
    decays = []
    for name, shape in entries:
        count = math.prod(shape)
        if len(shape) == 1:
            rates.append(np.full(count, 0.5, np.float32))
            decays.append(np.zeros(count, np.float32))
        else:
            rates.append(np.full(count, 2.0 / math.sqrt(shape[0]), np.float32))
            decays.append(np.full(count, 0.01, np.float32))
    rates = np.concatenate(rates)
    decays = np.concatenate(decays)
    return (rates.reshape(STRIDE, -1).T.reshape(-1), decays.reshape(STRIDE, -1).T.reshape(-1))


def unpack(flat, entries):
    pieces = {}
    offset = 0
    for name, shape in entries:
        count = math.prod(shape)
        pieces[name] = flat[offset : offset + count].reshape(shape)
        offset += count
    return pieces


def layer_norm(values, gain, shift):
    centred = values - jnp.mean(values, axis=-1, keepdims=True)
    spread = jnp.mean(centred * centred, axis=-1, keepdims=True)
    return centred * lax.rsqrt(spread + EPSILON) * gain + shift


def norm_backward(values, gain, shift, grad):
    _, pullback = jax.vjp(layer_norm, values, gain, shift)
    return pullback(grad)


def norm_pair(weights, prefix):
    return (
        weights[(prefix, NORM_GAIN)].astype(jnp.float32),
        weights[(prefix, NORM_BIAS)].astype(jnp.float32),
    )


def gated_pair(project, pair_mask):
    half = project.shape[-1] // 2
    return project[..., :half] * jax.nn.sigmoid(project[..., half:]) * pair_mask[..., None]


def gated_output(values, gate):
    return values * jax.nn.sigmoid(gate)


def swiglu(hidden):
    half = hidden.shape[-1] // 2
    return jax.nn.silu(hidden[..., :half]) * hidden[..., half:]


def matmul(left, right):
    return jnp.dot(left, right, preferred_element_type=jnp.float32)


def outer_sum(left, right):
    return jnp.einsum(
        "nc,nd->cd",
        left.reshape(-1, left.shape[-1]),
        right.reshape(-1, right.shape[-1]),
        preferred_element_type=jnp.float32,
    )


def flip(values):
    moved = lax.all_to_all(values, "row", split_axis=1, concat_axis=0, tiled=True)
    return jnp.swapaxes(moved, 0, 1)


def channel_forward(first, second, incoming):
    whole_first, whole_second = (
        lax.all_to_all(first, "row", split_axis=2, concat_axis=0, tiled=True),
        lax.all_to_all(second, "row", split_axis=2, concat_axis=0, tiled=True),
    )
    if incoming:
        local_tri = jnp.einsum(
            "kih,kjh->ijh", whole_first, whole_second, preferred_element_type=jnp.float32
        )
        local_tri = local_tri.astype(jnp.bfloat16).astype(jnp.float32)
    else:
        local_tri = jnp.einsum(
            "ikh,jkh->ijh", whole_first, whole_second, preferred_element_type=jnp.float32
        )
    tri = lax.all_to_all(
        local_tri.astype(jnp.bfloat16), "row", split_axis=0, concat_axis=2, tiled=True
    ).astype(local_tri.dtype)
    return (tri, whole_first, whole_second)


def channel_backward(grad_tri, whole_first, whole_second, incoming):
    whole_grad = lax.all_to_all(grad_tri, "row", split_axis=2, concat_axis=0, tiled=True)
    if incoming:
        grad_a = jnp.einsum(
            "ijh,kjh->kih", whole_grad, whole_second, preferred_element_type=jnp.float32
        )
        grad_b = jnp.einsum(
            "ijh,kih->kjh", whole_grad, whole_first, preferred_element_type=jnp.float32
        )
    else:
        grad_a = jnp.einsum(
            "ijh,jkh->ikh", whole_grad, whole_second, preferred_element_type=jnp.float32
        )
        grad_b = jnp.einsum(
            "ijh,ikh->jkh", whole_grad, whole_first, preferred_element_type=jnp.float32
        )
    return (
        lax.all_to_all(
            grad_a.astype(jnp.bfloat16), "row", split_axis=0, concat_axis=2, tiled=True
        ).astype(grad_a.dtype),
        lax.all_to_all(
            grad_b.astype(jnp.bfloat16), "row", split_axis=0, concat_axis=2, tiled=True
        ).astype(grad_b.dtype),
    )


def triangle_forward(state, pair_mask, weights, prefix, incoming):
    gain, shift = norm_pair(weights, prefix)
    lowered = layer_norm(state, gain, shift).astype(jnp.bfloat16)
    project = matmul(lowered, weights[(prefix, PROJ_GATE)])
    product = gated_pair(project, pair_mask).astype(jnp.bfloat16)
    half = product.shape[-1] // 2
    tri, own, other = channel_forward(product[..., :half], product[..., half:], incoming)
    out_gain = weights[(prefix, OUT_GAIN)].astype(jnp.float32)
    out_shift = weights[(prefix, OUT_BIAS)].astype(jnp.float32)
    out_low = layer_norm(tri, out_gain, out_shift).astype(jnp.bfloat16)
    output = matmul(out_low, weights[(prefix, PROJ_OUT)])
    gate_out = matmul(lowered, weights[(prefix, GATE_OUT)])
    update = gated_output(output, gate_out)
    return (update, (state, lowered, lowered, project, own, other, tri, out_low, output, gate_out))


def triangle_backward(saved, grad_update, pair_mask, weights, prefix, incoming, grads):
    state, lowered, framed, project, own, other, tri, out_low, output, gate_out = saved
    _, pullback = jax.vjp(gated_output, output, gate_out)
    grad_output, grad_gate = pullback(grad_update)
    grad_output = grad_output.astype(jnp.bfloat16)
    grad_gate = grad_gate.astype(jnp.bfloat16)
    grads[(prefix, PROJ_OUT)] = outer_sum(out_low, grad_output)
    grads[(prefix, GATE_OUT)] = outer_sum(lowered, grad_gate)
    grad_normed = matmul(grad_output, weights[(prefix, PROJ_OUT)].T)
    out_gain = weights[(prefix, OUT_GAIN)].astype(jnp.float32)
    out_shift = weights[(prefix, OUT_BIAS)].astype(jnp.float32)
    grad_tri, grads[(prefix, OUT_GAIN)], grads[(prefix, OUT_BIAS)] = norm_backward(
        tri, out_gain, out_shift, grad_normed
    )
    grad_tri = grad_tri.astype(jnp.bfloat16)
    grad_first, grad_second = channel_backward(grad_tri, own, other, incoming)
    _, pullback = jax.vjp(lambda values: gated_pair(values, pair_mask), project)
    (grad_project,) = pullback(jnp.concatenate([grad_first, grad_second], axis=-1))
    grad_project = grad_project.astype(jnp.bfloat16)
    grads[(prefix, PROJ_GATE)] = outer_sum(framed, grad_project)
    grad_framed = matmul(grad_project, weights[(prefix, PROJ_GATE)].T)
    if incoming:
        grad_framed = grad_framed.astype(jnp.bfloat16).astype(jnp.float32)
    grad_lowered = grad_framed + matmul(grad_gate, weights[(prefix, GATE_OUT)].T)
    gain, shift = norm_pair(weights, prefix)
    grad_state, grads[(prefix, NORM_GAIN)], grads[(prefix, NORM_BIAS)] = norm_backward(
        state, gain, shift, grad_lowered
    )
    return grad_state


def row_scores(query, key, bias, penalty, scale):
    scores = jnp.einsum("jhd,khd->hjk", query, key, preferred_element_type=jnp.float32) * scale
    return scores + bias.astype(jnp.float32) + penalty[None, None, :]


def attention_forward(state, penalty, weights, prefix, ending):
    gain, shift = norm_pair(weights, prefix)
    lowered = layer_norm(state, gain, shift).astype(jnp.bfloat16)
    framed = flip(lowered) if ending else lowered
    rows, length, width = framed.shape
    size = width // TA_HEADS
    scale = size ** (-0.5)
    qkvg = matmul(framed, weights[(prefix, QKVG)])
    queries = qkvg[..., :width].astype(jnp.bfloat16).reshape(rows, length, TA_HEADS, size)
    keys = qkvg[..., width : 2 * width].astype(jnp.bfloat16).reshape(rows, length, TA_HEADS, size)
    values = (
        qkvg[..., 2 * width : 3 * width].astype(jnp.bfloat16).reshape(rows, length, TA_HEADS, size)
    )
    gate = qkvg[..., 3 * width :]
    local_bias = (
        matmul(framed, weights[(prefix, BIAS_PROJ)]).astype(jnp.bfloat16).transpose(2, 0, 1)
    )
    bias = lax.all_gather(local_bias, "row", axis=1, tiled=True)

    def forward_row(items):
        query, key, value = items
        scores = row_scores(query, key, bias, penalty, scale)
        top = jnp.max(scores, axis=-1, keepdims=True)
        shifted = jnp.exp(scores - top)
        total = jnp.sum(shifted, axis=-1, keepdims=True)
        probs = (shifted / total).astype(jnp.bfloat16)
        mixed = jnp.einsum("hjk,khd->jhd", probs, value, preferred_element_type=jnp.float32)
        return (mixed, top[..., 0] + jnp.log(total[..., 0]))

    mixed, log_totals = lax.map(forward_row, (queries, keys, values))
    mixed = mixed.reshape(rows, length, width)
    gated_low = gated_output(mixed, gate).astype(jnp.bfloat16)
    returned = flip(gated_low) if ending else gated_low
    update = matmul(returned, weights[(prefix, OUTPUT)])
    return (update, (state, framed, queries, keys, values, gate, bias, mixed, log_totals, returned))


def attention_backward(saved, grad_update, penalty, weights, prefix, ending, grads):
    state, framed, queries, keys, values, gate, bias, mixed, log_totals, returned = saved
    rows, length, width = framed.shape
    size = width // TA_HEADS
    scale = size ** (-0.5)
    grad_low = grad_update.astype(jnp.bfloat16)
    grads[(prefix, OUTPUT)] = outer_sum(returned, grad_low)
    grad_gated = matmul(grad_low, weights[(prefix, OUTPUT)].T)
    if ending:
        grad_gated = flip(grad_gated.astype(jnp.bfloat16)).astype(jnp.float32)
    _, pullback = jax.vjp(gated_output, mixed, gate)
    grad_mixed, grad_gate = pullback(grad_gated)
    grad_mixed = grad_mixed.astype(jnp.bfloat16).reshape(rows, length, TA_HEADS, size)

    def back_row(carry, items):
        query, key, value, log_total, grad_row = items
        scores = row_scores(query, key, bias, penalty, scale)
        probs = jnp.exp(scores - log_total[..., None])
        grad_probs = jnp.einsum("jhd,khd->hjk", grad_row, value, preferred_element_type=jnp.float32)
        delta = jnp.sum(probs * grad_probs, axis=-1, keepdims=True)
        grad_scores = (probs * (grad_probs - delta)).astype(jnp.bfloat16)
        grad_query = (
            jnp.einsum("hjk,khd->jhd", grad_scores, key, preferred_element_type=jnp.float32) * scale
        )
        grad_key = (
            jnp.einsum("hjk,jhd->khd", grad_scores, query, preferred_element_type=jnp.float32)
            * scale
        )
        grad_value = jnp.einsum(
            "hjk,jhd->khd", probs.astype(jnp.bfloat16), grad_row, preferred_element_type=jnp.float32
        )
        return (carry + grad_scores.astype(jnp.float32), (grad_query, grad_key, grad_value))

    empty = jnp.zeros(bias.shape, jnp.float32)
    grad_bias, (grad_query, grad_key, grad_value) = lax.scan(
        back_row, empty, (queries, keys, values, log_totals, grad_mixed)
    )
    grad_bias = lax.psum_scatter(grad_bias, "row", scatter_dimension=1, tiled=True)
    grad_bias = grad_bias.transpose(1, 2, 0).astype(jnp.bfloat16)
    grad_qkvg = jnp.concatenate(
        [
            grad_query.reshape(rows, length, width),
            grad_key.reshape(rows, length, width),
            grad_value.reshape(rows, length, width),
            grad_gate,
        ],
        axis=-1,
    ).astype(jnp.bfloat16)
    grads[(prefix, QKVG)] = outer_sum(framed, grad_qkvg)
    grads[(prefix, BIAS_PROJ)] = outer_sum(framed, grad_bias)
    grad_framed = matmul(grad_qkvg, weights[(prefix, QKVG)].T) + matmul(
        grad_bias, weights[(prefix, BIAS_PROJ)].T
    )
    if ending:
        grad_framed = flip(grad_framed.astype(jnp.bfloat16)).astype(jnp.float32)
    gain, shift = norm_pair(weights, prefix)
    grad_state, grads[(prefix, NORM_GAIN)], grads[(prefix, NORM_BIAS)] = norm_backward(
        state, gain, shift, grad_framed
    )
    return grad_state


def transition_forward(state, weights, prefix):
    gain, shift = norm_pair(weights, prefix)
    lowered = layer_norm(state, gain, shift).astype(jnp.bfloat16)
    hidden = matmul(lowered, weights[(prefix, UP)])
    mixed_low = swiglu(hidden).astype(jnp.bfloat16)
    update = matmul(mixed_low, weights[(prefix, DOWN)])
    return (update, (state, lowered, hidden, mixed_low))


def transition_backward(saved, grad_update, weights, prefix, grads):
    state, lowered, hidden, mixed_low = saved
    grad_low = grad_update.astype(jnp.bfloat16)
    grads[(prefix, DOWN)] = outer_sum(mixed_low, grad_low)
    grad_mixed = matmul(grad_low, weights[(prefix, DOWN)].T)
    _, pullback = jax.vjp(swiglu, hidden)
    (grad_hidden,) = pullback(grad_mixed)
    grad_hidden = grad_hidden.astype(jnp.bfloat16)
    grads[(prefix, UP)] = outer_sum(lowered, grad_hidden)
    grad_lowered = matmul(grad_hidden, weights[(prefix, UP)].T)
    gain, shift = norm_pair(weights, prefix)
    grad_state, grads[(prefix, NORM_GAIN)], grads[(prefix, NORM_BIAS)] = norm_backward(
        state, gain, shift, grad_lowered
    )
    return grad_state


def single_forward(single_state, pair_state, penalty, weights):
    gain, shift = norm_pair(weights, ATTEND)
    lowered = layer_norm(single_state, gain, shift).astype(jnp.bfloat16)
    rows, width = lowered.shape
    size = width // SA_HEADS
    qkvg = matmul(lowered, weights[(ATTEND, QKVG)])
    query = qkvg[:, :width].astype(jnp.bfloat16).reshape(rows, SA_HEADS, size)
    key = qkvg[:, width : 2 * width].astype(jnp.bfloat16)
    value = qkvg[:, 2 * width : 3 * width].astype(jnp.bfloat16)
    gate = qkvg[:, 3 * width :]
    keys_all, values_all = (
        lax.all_gather(key, "row", axis=0, tiled=True),
        lax.all_gather(value, "row", axis=0, tiled=True),
    )
    keys_all = keys_all.reshape(-1, SA_HEADS, size)
    values_all = values_all.reshape(-1, SA_HEADS, size)
    pair_gain = weights[(ATTEND, PAIR_GAIN)].astype(jnp.float32)
    pair_shift = weights[(ATTEND, PAIR_BIAS)].astype(jnp.float32)
    pair_low = layer_norm(pair_state, pair_gain, pair_shift).astype(jnp.bfloat16)
    bias = matmul(pair_low, weights[(ATTEND, PAIR_PROJ)]).transpose(2, 0, 1)
    scores = jnp.einsum(
        "ihd,jhd->hij", query, keys_all, preferred_element_type=jnp.float32
    ) * size ** (-0.5)
    scores = scores + bias + penalty[None, None, :]
    probs = jax.nn.softmax(scores, axis=-1)
    probs_low = probs.astype(jnp.bfloat16)
    mixed = jnp.einsum(
        "hij,jhd->ihd", probs_low, values_all, preferred_element_type=jnp.float32
    ).reshape(rows, width)
    gated_low = gated_output(mixed, gate).astype(jnp.bfloat16)
    update = matmul(gated_low, weights[(ATTEND, OUTPUT)])
    return (
        update,
        (
            single_state,
            pair_state,
            lowered,
            query,
            keys_all,
            values_all,
            gate,
            pair_low,
            probs,
            probs_low,
            mixed,
            gated_low,
        ),
    )


def single_backward(saved, grad_update, weights, grads):
    (
        single_state,
        pair_state,
        lowered,
        query,
        keys_all,
        values_all,
        gate,
        pair_low,
        probs,
        probs_low,
        mixed,
        gated_low,
    ) = saved
    rows, width = lowered.shape
    size = width // SA_HEADS
    scale = size ** (-0.5)
    grad_low = grad_update.astype(jnp.bfloat16)
    grads[(ATTEND, OUTPUT)] = outer_sum(gated_low, grad_low)
    grad_gated = matmul(grad_low, weights[(ATTEND, OUTPUT)].T)
    _, pullback = jax.vjp(gated_output, mixed, gate)
    grad_mixed, grad_gate = pullback(grad_gated)
    grad_mixed = grad_mixed.astype(jnp.bfloat16).reshape(rows, SA_HEADS, size)
    grad_probs = jnp.einsum(
        "ihd,jhd->hij", grad_mixed, values_all, preferred_element_type=jnp.float32
    )
    delta = jnp.sum(probs * grad_probs, axis=-1, keepdims=True)
    grad_scores = (probs * (grad_probs - delta)).astype(jnp.bfloat16)
    grad_query = (
        jnp.einsum("hij,jhd->ihd", grad_scores, keys_all, preferred_element_type=jnp.float32)
        * scale
    )
    key_part = (
        jnp.einsum("hij,ihd->jhd", grad_scores, query, preferred_element_type=jnp.float32) * scale
    )
    value_part = jnp.einsum(
        "hij,ihd->jhd", probs_low, grad_mixed, preferred_element_type=jnp.float32
    )
    grad_key, grad_value = (
        lax.psum_scatter(key_part.reshape(-1, width), "row", scatter_dimension=0, tiled=True),
        lax.psum_scatter(value_part.reshape(-1, width), "row", scatter_dimension=0, tiled=True),
    )
    grad_qkvg = jnp.concatenate(
        [grad_query.reshape(rows, width), grad_key, grad_value, grad_gate], axis=-1
    ).astype(jnp.bfloat16)
    grads[(ATTEND, QKVG)] = outer_sum(lowered, grad_qkvg)
    grad_lowered = matmul(grad_qkvg, weights[(ATTEND, QKVG)].T)
    gain, shift = norm_pair(weights, ATTEND)
    grad_single, grads[(ATTEND, NORM_GAIN)], grads[(ATTEND, NORM_BIAS)] = norm_backward(
        single_state, gain, shift, grad_lowered
    )
    grad_bias = grad_scores.transpose(1, 2, 0)
    grads[(ATTEND, PAIR_PROJ)] = outer_sum(pair_low, grad_bias)
    grad_pair_low = matmul(grad_bias, weights[(ATTEND, PAIR_PROJ)].T)
    pair_gain = weights[(ATTEND, PAIR_GAIN)].astype(jnp.float32)
    pair_shift = weights[(ATTEND, PAIR_BIAS)].astype(jnp.float32)
    grad_pair, grads[(ATTEND, PAIR_GAIN)], grads[(ATTEND, PAIR_BIAS)] = norm_backward(
        pair_state, pair_gain, pair_shift, grad_pair_low
    )
    return (grad_single, grad_pair)


def shards(pair, single, lengths, params, moment_one, moment_two, pair_cotangent, single_cotangent):
    entries = layout(C, H, S, TA_HEADS, SA_HEADS)
    full = lax.all_gather(params.astype(jnp.bfloat16), "row", axis=0, tiled=True)
    weights = unpack(logical_order(full), entries)
    rows = pair.shape[1]
    length = pair.shape[2]
    first_row = lax.axis_index("row") * rows
    mask = (jnp.arange(length, dtype=jnp.int32) < lengths[0]).astype(jnp.float32)
    mask_rows = lax.dynamic_slice_in_dim(mask, first_row, rows)
    pair_mask = mask_rows[:, None] * mask[None, :]
    penalty = (mask - 1.0) * MASKED
    state = pair[0].astype(jnp.float32)
    saved = {}
    for prefix, incoming in ((OUTGOING, False), (INCOMING, True)):
        update, saved[prefix] = triangle_forward(state, pair_mask, weights, prefix, incoming)
        state = state + update
    for prefix, ending in ((STARTING, False), (ENDING, True)):
        update, saved[prefix] = attention_forward(state, penalty, weights, prefix, ending)
        state = state + update
    update, saved[PAIR] = transition_forward(state, weights, PAIR)
    pair_final = state + update
    single_state = single[0].astype(jnp.float32)
    update, saved[ATTEND] = single_forward(single_state, pair_final, penalty, weights)
    single_mid = single_state + update
    update, saved[SINGLE] = transition_forward(single_mid, weights, SINGLE)
    single_final = single_mid + update
    grads = {}
    grad_single = single_cotangent[0].astype(jnp.float32)
    grad_single = grad_single + transition_backward(
        saved[SINGLE], grad_single, weights, SINGLE, grads
    )
    from_single, from_pair = single_backward(saved[ATTEND], grad_single, weights, grads)
    grad_single = grad_single + from_single
    grad_pair = pair_cotangent[0].astype(jnp.float32) + from_pair
    grad_pair = grad_pair + transition_backward(saved[PAIR], grad_pair, weights, PAIR, grads)
    for prefix, ending in ((ENDING, True), (STARTING, False)):
        grad_pair = grad_pair + attention_backward(
            saved[prefix], grad_pair, penalty, weights, prefix, ending, grads
        )
    for prefix, incoming in ((INCOMING, True), (OUTGOING, False)):
        grad_pair = grad_pair + triangle_backward(
            saved[prefix], grad_pair, pair_mask, weights, prefix, incoming, grads
        )
    flat = stored_order(jnp.concatenate([grads[name].reshape(-1) for name, shape in entries]))
    shard_size = params.shape[0]
    row_index = lax.axis_index("row")
    total = lax.psum(flat, ("crop", "row"))
    shard = lax.dynamic_slice_in_dim(total, row_index * shard_size, shard_size)
    norm_squared = jnp.sum(total * total)
    clip_norm = jnp.sqrt(norm_squared)
    clipped = shard * (CLIP / jnp.maximum(clip_norm, CLIP))
    new_first = BETA_ONE * moment_one + (1.0 - BETA_ONE) * clipped
    new_second = BETA_TWO * moment_two + (1.0 - BETA_TWO) * clipped * clipped
    rates, decays = rate_tables(entries)
    rate_shard = lax.dynamic_slice_in_dim(jnp.asarray(rates), row_index * shard_size, shard_size)
    decay_shard = lax.dynamic_slice_in_dim(jnp.asarray(decays), row_index * shard_size, shard_size)
    first_hat = new_first / (1.0 - BETA_ONE**STEP)
    second_hat = new_second / (1.0 - BETA_TWO**STEP)
    new_params = params - rate_shard * (
        first_hat / (jnp.sqrt(second_hat) + ADAM_EPS) + decay_shard * params
    )
    return (
        pair_final.astype(jnp.bfloat16)[None],
        single_final.astype(jnp.bfloat16)[None],
        grad_pair[None],
        grad_single[None],
        new_params,
        new_first,
        new_second,
        clip_norm,
    )


F32 = jnp.float32
BF16 = jnp.bfloat16
LOG2E = 1.4426950408889634
VMEM_LIMIT = 56 * 1024 * 1024


def mm(left, right):
    return lax.dot_general(left, right, (((1,), (0,)), ((), ())), preferred_element_type=F32)


def mm_nt(left, right):
    return lax.dot_general(left, right, (((1,), (1,)), ((), ())), preferred_element_type=F32)


def mm_tn(left, right):
    return lax.dot_general(left, right, (((0,), (0,)), ((), ())), preferred_element_type=F32)


def standardize(values):
    centred = values - jnp.mean(values, axis=0, keepdims=True)
    spread = jnp.mean(centred * centred, axis=0, keepdims=True)
    inverse = lax.rsqrt(spread + EPSILON)
    return centred * inverse, inverse


def standardize_back(unit, inverse, grad_unit):
    first = jnp.mean(grad_unit, axis=0, keepdims=True)
    second = jnp.mean(grad_unit * unit, axis=0, keepdims=True)
    return inverse * (grad_unit - first - unit * second)


def sigmoid(values):
    return 0.5 * jnp.tanh(0.5 * values) + 0.5


def column(ref, index):
    return ref[:, index : index + 1]


def live_pair(info, alive, row):
    return jnp.concatenate(
        [jnp.where(info[row + place] > 0, alive[0:1], 0.0) for place in range(GROUP)], axis=1
    )


GROUP = 4
LAG = 4


def each_group(count, body):
    def step(index, carry):
        body(index * GROUP)
        return carry

    lax.fori_loop(0, count // GROUP, step, 0)


def each_channel(count, body):
    def step(index, carry):
        body(index)
        return carry

    lax.fori_loop(0, count, step, 0)


def join(read, ref, row):
    return jnp.concatenate([read(ref, row + place) for place in range(GROUP)], axis=1)


def pieces_of(values):
    length = values.shape[1] // GROUP
    return [values[:, place * length : (place + 1) * length] for place in range(GROUP)]


def put_rows(ref, row, values):
    for place, part in enumerate(pieces_of(values)):
        ref[row + place] = part.astype(ref.dtype)


def put_inner(scratch, row, values):
    for place, part in enumerate(pieces_of(values)):
        scratch[:, row + place, :] = part


def read_inner(scratch, row):
    return scratch[:, row, :]


def put_turned(scratch, row, values):
    for place, part in enumerate(pieces_of(values)):
        scratch[:, row + place, :] = part.T


def add_lanes(ref, values):
    ref[...] += sum(pieces_of(values))


def spec_full(shape):
    return pl.BlockSpec(shape, lambda step: (0,) * len(shape))


def cost(microseconds):
    return pl.CostEstimate(
        flops=int(microseconds * 1e9), bytes_accessed=int(microseconds * 3e6), transcendentals=0
    )


class Both(list):
    pass


def all_rows(ins, outs):
    extents = [shape[axis] for shape, dtype, axis in outs if axis is not None]
    for array, axis in ins:
        if isinstance(axis, int):
            extents += [member.shape[axis] for member in (array if isinstance(array, list) else [array])]
    return max(extents)


def run_rows(kernel, name, steps, ins, outs, scratch, time=15, half=None, before=None):
    grid = steps if half is None else steps // 2
    offset = grid * (half or 0)
    flat = []
    groups = []
    for array, axis in ins:
        members = array if isinstance(array, Both) else [array]
        flat += [(member, axis) for member in members]
        groups.append((len(members), isinstance(array, Both)))
    full = all_rows(flat, outs)

    def spec(shape, axis):
        if axis is None:
            return spec_full(shape)
        size = full // steps
        first = offset if shape[axis] == full else 0
        sizes = tuple(size if place == axis else extent for place, extent in enumerate(shape))
        return pl.BlockSpec(
            sizes,
            lambda step: tuple(step + first if place == axis else 0 for place in range(len(shape))),
        )

    in_specs = [
        pl.BlockSpec(memory_space=pltpu.SMEM) if axis == "smem" else spec(array.shape, axis)
        for array, axis in flat
    ]
    out_specs = [spec(shape, axis) for shape, dtype, axis in outs]
    arrays = [array for array, axis in flat]
    aliases = {}
    kept = []
    for place, (shape, dtype, axis) in enumerate(outs):
        if before is not None and (axis is None or shape[axis] == full):
            aliases[len(arrays)] = place
            kept.append(place)
            arrays.append(before[place])
            in_specs.append(spec_full(shape) if axis is None else pl.BlockSpec(memory_space=pl.ANY))

    def run(*refs):
        taken = iter(refs)
        given = []
        for number, together in groups:
            members = [next(taken) for _ in range(number)]
            given.append(members if together else members[0])
        held = {place: next(taken) for place in kept}
        results = [next(taken) for _ in outs]

        @pl.when(pl.program_id(0) == 0)
        def _():
            for place, (shape, dtype, axis) in enumerate(outs):
                if axis is None:
                    results[place][...] = (
                        held[place][...] if place in held else jnp.zeros(shape, dtype)
                    )

        kernel(*given, *results, *taken)

    return pl.pallas_call(
        run,
        grid=(grid,),
        in_specs=in_specs,
        out_specs=out_specs,
        out_shape=[jax.ShapeDtypeStruct(shape, dtype) for shape, dtype, axis in outs],
        scratch_shapes=[pltpu.VMEM(shape, dtype) for shape, dtype in scratch],
        input_output_aliases=aliases,
        compiler_params=pltpu.CompilerParams(vmem_limit_bytes=VMEM_LIMIT),
        cost_estimate=cost(time if half is None else time / 2),
        name=name,
    )(*arrays)


def run_halves(kernel, name, steps, ins, outs, scratch, time=15):
    results = []
    for half in range(2):
        chosen = [
            (array[half] if type(array) is list else array, axis) for array, axis in ins
        ]
        before = results[0] if half else None
        results.append(run_rows(kernel, name, steps, chosen, outs, scratch, time, half, before))
    full = all_rows(ins, outs)
    return [
        [results[0][place], results[1][place]]
        if axis is not None and shape[axis] != full
        else results[1][place]
        for place, (shape, dtype, axis) in enumerate(outs)
    ]


def zero_first(*refs):
    @pl.when(pl.program_id(0) == 0)
    def _():
        for ref in refs:
            ref[...] = jnp.zeros(ref.shape, ref.dtype)


def lane_sums(ref):
    return jnp.sum(ref[...].T, axis=0, keepdims=True)


def on_last(body):
    @pl.when(pl.program_id(0) == pl.num_programs(0) - 1)
    def _():
        body()


def read_plain(ref, row):
    return ref[row].astype(F32)


def reorder(values, order):
    size = values.shape[0] // len(order)
    return jnp.concatenate([values[place * size : (place + 1) * size] for place in order], axis=0)


def read_tokens(order, ref, row):
    return reorder(ref[row].astype(F32), order).T


def read_flipped(refs, row):
    parts = jnp.concatenate([ref[:, row] for ref in refs], axis=1)
    return parts.reshape(-1, parts.shape[-1]).astype(F32).T


def read_turned(order, ref, row):
    parts = ref[:, row]
    return reorder(parts.reshape(-1, parts.shape[-1]).astype(F32), order).T


def tri_pre_row(info, alive, row, state, cols, first, proj_t):
    unit, inverse = standardize(state)
    lowered = (unit * column(cols, first) + column(cols, first + 1)).astype(BF16)
    project = mm(proj_t[...], lowered)
    half = project.shape[0] // 2
    return project[:half] * sigmoid(project[half:]) * live_pair(info, alive, row)


def store_product(out, scratch, devices):
    hidden = scratch.shape[0] // 2
    part = hidden // devices

    def one(device, carry):
        out[device, 0] = scratch[pl.ds(device * part, part)].astype(BF16)
        out[device, 1] = scratch[pl.ds(hidden + device * part, part)].astype(BF16)
        return carry

    lax.fori_loop(0, devices, one, 0)


def copy_blocks(target, source, count):
    def one(index, carry):
        target[index] = source[index].astype(target.dtype)
        return carry

    lax.fori_loop(0, count, one, 0)


def store_flipped(out, scratch):
    devices, part = out.shape[0], out.shape[1]

    def one(device, carry):
        out[device] = scratch[pl.ds(device * part, part)].astype(out.dtype)
        return carry

    lax.fori_loop(0, devices, one, 0)


def tri_post_row(state, tri, cols, proj_t, gate_t):
    unit, inverse = standardize(state)
    lowered = (unit * column(cols, 0) + column(cols, 1)).astype(BF16)
    tri_unit, tri_inverse = standardize(tri)
    out_low = (tri_unit * column(cols, 2) + column(cols, 3)).astype(BF16)
    output = mm(proj_t[...], out_low)
    gate = sigmoid(mm(gate_t[...], lowered))
    return unit, inverse, lowered, tri_unit, tri_inverse, out_low, output, gate


def row_base(rows):
    return pl.program_id(0) * rows


def tri_pre_first_kernel(devices, read, info, alive, pair, cols, proj_t, out, scratch):
    rows = pair.shape[0]

    def body(row):
        product = tri_pre_row(
            info, alive, row_base(rows) + row, join(read, pair, row), cols, 0, proj_t
        )
        put_inner(scratch, row, product)

    each_group(rows, body)
    store_product(out, scratch, devices)


def whole_rows(refs, *place):
    parts = jnp.concatenate([ref[(slice(None),) + place] for ref in refs], axis=1)
    return parts.reshape(-1, parts.shape[-1])


def split_rows(values, outs, *place):
    part = outs[0].shape[-2]
    parts = values.astype(BF16).reshape(outs[0].shape[0], -1, values.shape[-1])
    for half, out in enumerate(outs):
        out[(slice(None),) + place] = parts[:, half * part : (half + 1) * part]


def tri_product_kernel(incoming, operands, first_out, second_out):
    def body(channel):
        first = whole_rows(operands, 0, channel)
        second = whole_rows(operands, 1, channel)
        tri = mm_tn(first, second) if incoming else mm_nt(first, second)
        split_rows(tri, (first_out, second_out), channel)

    each_channel(operands[0].shape[2], body)


def tri_join_kernel(
    devices, read, info, alive, source, tri_in, cols, proj_t, gate_t, next_cols, next_proj_t,
    state_out, out, tri_scratch, scratch,
):
    rows = state_out.shape[0]
    copy_blocks(tri_scratch, tri_in, tri_in.shape[0])

    def body(row):
        state = join(read, source, row)
        pieces = tri_post_row(state, join(read_inner, tri_scratch, row), cols, proj_t, gate_t)
        state = state + pieces[6] * pieces[7]
        put_rows(state_out, row, state)
        product = tri_pre_row(
            info, alive, row_base(rows) + row, state, next_cols, 0, next_proj_t
        )
        put_inner(scratch, row, product)

    each_group(rows, body)
    store_product(out, scratch, devices)


def tri_last_kernel(
    source, tri_in, cols, proj_t, gate_t, next_cols, bias_t, state_out, bias_out, tri_scratch, scratch
):
    rows = state_out.shape[0]
    copy_blocks(tri_scratch, tri_in, tri_in.shape[0])

    def body(row):
        state = join(read_plain, source, row)
        pieces = tri_post_row(state, join(read_inner, tri_scratch, row), cols, proj_t, gate_t)
        state = state + pieces[6] * pieces[7]
        put_rows(state_out, row, state)
        unit, inverse = standardize(state)
        lowered = (unit * column(next_cols, 0) + column(next_cols, 1)).astype(BF16)
        put_inner(scratch, row, mm(bias_t[...], lowered))

    each_group(rows, body)
    bias_out[...] = scratch[: bias_out.shape[0]].astype(BF16)


def flipped_bias_kernel(source, cols, bias_t, bias_out, scratch):
    rows = source[0].shape[1]

    def body(row):
        unit, inverse = standardize(join(read_flipped, source, row))
        lowered = (unit * column(cols, 0) + column(cols, 1)).astype(BF16)
        put_inner(scratch, row, mm(bias_t[...], lowered))

    each_group(rows, body)
    bias_out[...] = scratch[: bias_out.shape[0]].astype(BF16)


def fill_bias(alive, bias_in, table):
    @pl.when(pl.program_id(0) == 0)
    def _():
        length = table.shape[1]
        penalty = (alive[0:1] - 1.0) * (MASKED * LOG2E)
        for head in range(table.shape[0]):
            values = bias_in[:, head].reshape(length, length).astype(F32)
            table[head] = (values * LOG2E + penalty).T


def attention_row(state, cols, proj_t):
    unit, inverse = standardize(state)
    lowered = (unit * column(cols, 0) + column(cols, 1)).astype(BF16)
    project = mm(proj_t[...], lowered)
    width = project.shape[0] // 4
    size = width // TA_HEADS
    query = (project[:width] * (size**-0.5 * LOG2E)).astype(BF16)
    key = project[width : 2 * width].astype(BF16)
    value = project[2 * width : 3 * width].astype(BF16)
    gate = sigmoid(project[3 * width :])
    return unit, inverse, lowered, query, key, value, gate


def in_stages(blocks, first, second, third):
    early, late, done = {}, {}, {}
    count = len(blocks)
    for step in range(count + 2 * LAG):
        if step < count:
            early[step] = first(*blocks[step])
        if 0 <= step - LAG < count:
            late[step - LAG] = second(*blocks[step - LAG], early.pop(step - LAG))
        if 0 <= step - 2 * LAG < count:
            place = step - 2 * LAG
            done[blocks[place]] = third(*blocks[place], late.pop(place))
    return done


def head_rows(values, place, head):
    size, length = values.shape[0] // TA_HEADS, values.shape[1] // GROUP
    return values[head * size : (head + 1) * size, place * length : (place + 1) * length]


def gather_heads(done):
    return jnp.concatenate(
        [
            jnp.concatenate([done[place, head] for head in range(TA_HEADS)], axis=0)
            for place in range(GROUP)
        ],
        axis=1,
    )


ROW_BLOCKS = [(place, head) for place in range(GROUP) for head in range(TA_HEADS)]
HEAD_BLOCKS = [(place, head) for head in range(TA_HEADS) for place in range(GROUP)]


def attend_rows(state, row, cols, proj_t, output_t, table, totals, mixed_out):
    unit, inverse, lowered, query, key, value, gate = attention_row(state, cols, proj_t)

    def score(place, head):
        return mm_tn(head_rows(key, place, head), head_rows(query, place, head)) + table[head]

    def shift(place, head, scores):
        top = jnp.max(scores, axis=0, keepdims=True)
        return top, jnp.exp2(scores - top).astype(BF16)

    def mix(place, head, items):
        top, shifted = items
        values = head_rows(value, place, head)
        size = values.shape[0]
        values = jnp.concatenate([values, jnp.ones((16, values.shape[1]), BF16)], axis=0)
        result = mm(values, shifted)
        total = result[size : size + 1]
        return result[:size] / total, top + jnp.log2(total)

    done = in_stages(ROW_BLOCKS, score, shift, mix)
    mixed = gather_heads({block: items[0] for block, items in done.items()})
    put_rows(totals, row, gather_heads({block: items[1] for block, items in done.items()}))
    put_rows(mixed_out, row, mixed)
    return state + mm(output_t[...], (mixed * gate).astype(BF16))


def starting_kernel(
    alive, source, bias_in, cols, proj_t, output_t, out, totals, mixed, table, scratch
):
    fill_bias(alive, bias_in, table)
    rows = source.shape[0]

    def body(row):
        state = attend_rows(
            join(read_plain, source, row), row, cols, proj_t, output_t, table, totals, mixed
        )
        put_turned(scratch, row, state)

    each_group(rows, body)
    store_flipped(out, scratch)


def ending_kernel(alive, source, bias_in, cols, proj_t, output_t, out, totals, mixed, table):
    fill_bias(alive, bias_in, table)
    rows = source[0].shape[1]

    def body(row):
        state = attend_rows(
            join(read_flipped, source, row), row, cols, proj_t, output_t, table, totals, mixed
        )
        put_rows(out, row, state)

    each_group(rows, body)


def transition_kernel(
    order, source, cols, up_t, down_t, next_cols, bias_t, state_out, pair_out, bias_out, scratch, bias_scratch
):
    rows = source.shape[0]

    def body(row):
        state = join(read_plain, source, row)
        unit, inverse = standardize(state)
        lowered = (unit * column(cols, 0) + column(cols, 1)).astype(BF16)
        hidden = mm(up_t[...], lowered)
        half = hidden.shape[0] // 2
        first = hidden[:half]
        mixed = (first * sigmoid(first) * hidden[half:]).astype(BF16)
        state = state + mm(down_t[...], mixed)
        put_rows(state_out, row, state)
        put_turned(scratch, row, state)
        unit, inverse = standardize(state)
        lowered = (unit * column(next_cols, 0) + column(next_cols, 1)).astype(BF16)
        put_inner(bias_scratch, row, mm(bias_t[...], lowered))

    each_group(rows, body)
    size = pair_out.shape[0] // len(order)
    for place, held in enumerate(order):
        pair_out[place * size : (place + 1) * size] = scratch[held * size : (held + 1) * size].astype(BF16)
    bias_out[...] = bias_scratch[...].astype(BF16)


def transition_back_kernel(
    read, mid, final, cotangent, bias_grad, cols, up_t, up, down, next_cols, bias_w,
    grad_out, up_grad, down_grad, bias_w_grad, vecs, norm_gain, norm_bias, pair_gain, pair_bias, bias_scratch,
):
    zero_first(norm_gain, norm_bias, pair_gain, pair_bias)
    rows = mid.shape[0]
    bias_scratch[...] = bias_grad[...].astype(F32)

    def body(row):
        grad = join(read, cotangent, row)
        unit, inverse = standardize(join(read_plain, final, row))
        gain = column(next_cols, 0)
        lowered = (unit * gain + column(next_cols, 1)).astype(BF16)
        grad_bias = join(read_inner, bias_scratch, row).astype(BF16)
        bias_w_grad[...] += mm_nt(lowered, grad_bias)
        grad_lowered = mm(bias_w[...], grad_bias)
        add_lanes(pair_gain, grad_lowered * unit)
        add_lanes(pair_bias, grad_lowered)
        grad = grad + standardize_back(unit, inverse, grad_lowered * gain)
        unit, inverse = standardize(join(read_plain, mid, row))
        gain = column(cols, 0)
        lowered = (unit * gain + column(cols, 1)).astype(BF16)
        hidden = mm(up_t[...], lowered)
        half = hidden.shape[0] // 2
        first, second = hidden[:half], hidden[half:]
        slope = sigmoid(first)
        silu = first * slope
        grad_low = grad.astype(BF16)
        grad_mixed = mm(down[...], grad_low)
        down_grad[...] += mm_nt((silu * second).astype(BF16), grad_low)
        grad_hidden = jnp.concatenate(
            [
                (grad_mixed * second * (slope + silu * (1.0 - slope))).astype(BF16),
                (grad_mixed * silu).astype(BF16),
            ],
            axis=0,
        )
        up_grad[...] += mm_nt(lowered, grad_hidden)
        grad_lowered = mm(up[...], grad_hidden)
        add_lanes(norm_gain, grad_lowered * unit)
        add_lanes(norm_bias, grad_lowered)
        put_rows(grad_out, row, grad + standardize_back(unit, inverse, grad_lowered * gain))

    each_group(rows, body)

    def finish():
        vecs[0:1] += lane_sums(norm_gain)
        vecs[1:2] += lane_sums(norm_bias)
        vecs[2:3] += lane_sums(pair_gain)
        vecs[3:4] += lane_sums(pair_bias)

    on_last(finish)


def attention_back_kernel(
    read, read_grad, alive, source, grad_in, bias_in, totals, mixed_in, cols, proj_t, proj, output,
    grad_out, bias_out, proj_grad, output_grad, table, grad_table,
):
    fill_bias(alive, bias_in, table)
    zero_first(grad_table)
    rows = grad_out.shape[0]

    def body(row):
        unit, inverse, lowered, query, key, value, gate = attention_row(
            join(read, source, row), cols, proj_t
        )
        mixed = join(read_plain, mixed_in, row)
        total = join(read_plain, totals, row)
        grad_low = join(read_grad, grad_in, row).astype(BF16)
        gated = mixed * gate
        output_grad[...] += mm_nt(gated.astype(BF16), grad_low)
        grad_gated = mm(output[...], grad_low)
        grad_gate = grad_gated * gated * (1.0 - gate)
        grad_mixed = (grad_gated * gate).astype(BF16)
        product = grad_mixed.astype(F32) * mixed
        size = query.shape[0] // TA_HEADS

        def score(place, head):
            scores = mm_tn(head_rows(key, place, head), head_rows(query, place, head))
            grads = mm_tn(head_rows(value, place, head), head_rows(grad_mixed, place, head))
            return scores + table[head], grads

        def slope(place, head, items):
            scores, grads = items
            probs = jnp.exp2(scores - head_rows(total, place, head))
            delta = jnp.sum(head_rows(product, place, head), axis=0, keepdims=True)
            grad_scores = probs * (grads - delta)
            grad_table[head] += grad_scores
            return probs.astype(BF16), grad_scores.astype(BF16)

        def back(place, head, items):
            probs, grad_scores = items
            return (
                mm(head_rows(key, place, head), grad_scores) * size**-0.5,
                mm_nt(head_rows(query, place, head), grad_scores) * (1.0 / LOG2E),
                mm_nt(head_rows(grad_mixed, place, head), probs),
            )

        done = in_stages(HEAD_BLOCKS, score, slope, back)
        grad_project = jnp.concatenate(
            [
                gather_heads({block: items[part] for block, items in done.items()})
                for part in range(3)
            ]
            + [grad_gate],
            axis=0,
        ).astype(BF16)
        proj_grad[...] += mm_nt(lowered, grad_project)
        put_rows(grad_out, row, mm(proj[...], grad_project))

    each_group(rows, body)

    def finish():
        for head in range(TA_HEADS):
            bias_out[:, head] = (
                grad_table[head].T.astype(BF16).reshape(bias_out.shape[0], bias_out.shape[2], -1)
            )

    on_last(finish)


def attention_end_row(
    state, grad, grad_lowered, grad_bias, cols, bias_w, bias_w_grad, norm_gain, norm_bias
):
    unit, inverse = standardize(state)
    gain = column(cols, 0)
    lowered = (unit * gain + column(cols, 1)).astype(BF16)
    bias_w_grad[...] += mm_nt(lowered, grad_bias)
    grad_lowered = grad_lowered + mm(bias_w[...], grad_bias)
    add_lanes(norm_gain, grad_lowered * unit)
    add_lanes(norm_bias, grad_lowered)
    return grad + standardize_back(unit, inverse, grad_lowered * gain)


def fill_bias_grad(scratch, bias_grad):
    heads = bias_grad.shape[1]
    total = bias_grad[0].astype(F32)
    for device in range(1, bias_grad.shape[0]):
        total = total + bias_grad[device].astype(F32)
    scratch[:heads] = total
    scratch[heads:] = jnp.zeros((scratch.shape[0] - heads,) + scratch.shape[1:], F32)


def ending_end_kernel(
    source, grad_in, grad_lowered, bias_grad, cols, bias_w,
    grad_out, bias_w_grad, vecs, norm_gain, norm_bias, bias_scratch, scratch,
):
    zero_first(norm_gain, norm_bias)
    fill_bias_grad(bias_scratch, bias_grad)
    rows = grad_in.shape[0]

    def body(row):
        grad = attention_end_row(
            join(read_flipped, source, row), join(read_plain, grad_in, row),
            join(read_plain, grad_lowered, row), join(read_inner, bias_scratch, row).astype(BF16), cols, bias_w, bias_w_grad, norm_gain, norm_bias,
        )
        put_turned(scratch, row, grad)

    each_group(rows, body)
    store_flipped(grad_out, scratch)

    def finish():
        vecs[0:1] += lane_sums(norm_gain)
        vecs[1:2] += lane_sums(norm_bias)

    on_last(finish)


def tri_post_back_row(
    state, tri, grad, cols, proj_t, gate_t, proj, gate_w, proj_grad, gate_grad, out_gain, out_bias
):
    unit, inverse, lowered, tri_unit, tri_inverse, out_low, output, gate = tri_post_row(
        state, tri, cols, proj_t, gate_t
    )
    grad_output = grad * gate
    grad_gate = (grad_output * output * (1.0 - gate)).astype(BF16)
    grad_output = grad_output.astype(BF16)
    proj_grad[...] += mm_nt(out_low, grad_output)
    gate_grad[...] += mm_nt(lowered, grad_gate)
    grad_normed = mm(proj[...], grad_output)
    add_lanes(out_gain, grad_normed * tri_unit)
    add_lanes(out_bias, grad_normed)
    grad_tri = standardize_back(tri_unit, tri_inverse, grad_normed * column(cols, 2))
    return grad_tri, mm(gate_w[...], grad_gate)


def starting_end_kernel(
    source, grad_in, grad_lowered, bias_grad, cols, bias_w,
    below, tri_in, tri_cols, proj_t, gate_t, proj, gate_w,
    grad_out, tri_out, gate_back, bias_w_grad, proj_grad, gate_grad, vecs,
    norm_gain, norm_bias, out_gain, out_bias, bias_scratch, tri_scratch,
):
    zero_first(norm_gain, norm_bias, out_gain, out_bias)
    fill_bias_grad(bias_scratch, bias_grad)
    copy_blocks(tri_scratch, tri_in, tri_in.shape[0])
    rows = source.shape[0]

    def body(row):
        grad = attention_end_row(
            join(read_plain, source, row), join(read_flipped, grad_in, row),
            join(read_plain, grad_lowered, row), join(read_inner, bias_scratch, row).astype(BF16), cols, bias_w, bias_w_grad, norm_gain, norm_bias,
        )
        put_rows(grad_out, row, grad)
        grad_tri, back = tri_post_back_row(
            join(read_plain, below, row), join(read_inner, tri_scratch, row), grad, tri_cols, proj_t, gate_t, proj, gate_w,
            proj_grad, gate_grad, out_gain, out_bias,
        )
        put_rows(gate_back, row, back)
        put_inner(tri_scratch, row, grad_tri)

    each_group(rows, body)
    copy_blocks(tri_out, tri_scratch, tri_out.shape[0])

    def finish():
        vecs[0:1] += lane_sums(norm_gain)
        vecs[1:2] += lane_sums(norm_bias)
        vecs[2:3] += lane_sums(out_gain)
        vecs[3:4] += lane_sums(out_bias)

    on_last(finish)


def tri_product_back_kernel(incoming, grad, operands, first_out, second_out):
    def body(channel):
        first = whole_rows(operands, 0, channel)
        second = whole_rows(operands, 1, channel)
        tri = whole_rows(grad, channel)
        if incoming:
            grad_first = mm_nt(second, tri)
            grad_second = mm(first, tri)
        else:
            grad_first = mm(tri, second)
            grad_second = mm_tn(tri, first)
        split_rows(grad_first, (first_out, second_out), 0, channel)
        split_rows(grad_second, (first_out, second_out), 1, channel)

    each_channel(operands[0].shape[2], body)


def tri_pre_back_row(
    info, alive, row, state, product_grad, gate_back, grad, cols, proj_t, proj, proj_grad, norm_gain, norm_bias
):
    unit, inverse = standardize(state)
    gain = column(cols, 0)
    lowered = (unit * gain + column(cols, 1)).astype(BF16)
    project = mm(proj_t[...], lowered)
    half = project.shape[0] // 2
    gate = sigmoid(project[half:])
    grad_first = product_grad * gate * live_pair(info, alive, row)
    grad_second = grad_first * project[:half] * (1.0 - gate)
    grad_project = jnp.concatenate([grad_first.astype(BF16), grad_second.astype(BF16)], axis=0)
    proj_grad[...] += mm_nt(lowered, grad_project)
    grad_lowered = mm(proj[...], grad_project) + gate_back
    add_lanes(norm_gain, grad_lowered * unit)
    add_lanes(norm_bias, grad_lowered)
    return grad + standardize_back(unit, inverse, grad_lowered * gain)


def fill_product_grad(scratch, product_grad):
    devices, part = product_grad.shape[0], product_grad.shape[2]

    def one(device, carry):
        scratch[pl.ds(device * part, part)] = product_grad[device, 0].astype(F32)
        scratch[pl.ds((devices + device) * part, part)] = product_grad[device, 1].astype(F32)
        return carry

    lax.fori_loop(0, devices, one, 0)


def tri_join_back_kernel(
    read, info, alive, source, product_grad, gate_in, grad_in, cols, proj_t, proj,
    below, tri_in, tri_cols, out_t, gate_t, out_w, gate_w,
    grad_out, tri_out, gate_back, proj_grad, out_grad, gate_grad, vecs,
    norm_gain, norm_bias, out_gain, out_bias, scratch, tri_scratch,
):
    zero_first(norm_gain, norm_bias, out_gain, out_bias)
    fill_product_grad(scratch, product_grad)
    copy_blocks(tri_scratch, tri_in, tri_in.shape[0])
    rows = source.shape[0]

    def body(row):
        grad = tri_pre_back_row(
            info, alive, row_base(rows) + row, join(read_plain, source, row),
            join(read_inner, scratch, row), join(read_plain, gate_in, row),
            join(read_plain, grad_in, row), cols, proj_t, proj, proj_grad, norm_gain, norm_bias,
        )
        put_rows(grad_out, row, grad)
        grad_tri, back = tri_post_back_row(
            join(read, below, row), join(read_inner, tri_scratch, row), grad, tri_cols, out_t, gate_t, out_w, gate_w,
            out_grad, gate_grad, out_gain, out_bias,
        )
        put_rows(gate_back, row, back)
        put_inner(tri_scratch, row, grad_tri)

    each_group(rows, body)
    copy_blocks(tri_out, tri_scratch, tri_out.shape[0])

    def finish():
        vecs[0:1] += lane_sums(norm_gain)
        vecs[1:2] += lane_sums(norm_bias)
        vecs[2:3] += lane_sums(out_gain)
        vecs[3:4] += lane_sums(out_bias)

    on_last(finish)


def tri_first_back_kernel(
    read, order, info, alive, source, product_grad, gate_in, grad_in, cols, proj_t, proj,
    grad_out, proj_grad, vecs, norm_gain, norm_bias, scratch,
):
    zero_first(norm_gain, norm_bias)
    fill_product_grad(scratch, product_grad)
    rows = source.shape[0]

    def body(row):
        grad = tri_pre_back_row(
            info, alive, row_base(rows) + row, join(read, source, row),
            join(read_inner, scratch, row), join(read_plain, gate_in, row),
            join(read_plain, grad_in, row), cols, proj_t, proj, proj_grad, norm_gain, norm_bias,
        )
        for place, part in enumerate(pieces_of(grad)):
            grad_out[row + place] = reorder(part.T, order).astype(grad_out.dtype)

    each_group(rows, body)

    def finish():
        vecs[0:1] += lane_sums(norm_gain)
        vecs[1:2] += lane_sums(norm_bias)

    on_last(finish)


RUN = 24


def table_of(entries):
    table = {}
    offset = 0
    for name, shape in entries:
        table[name] = (offset // STRIDE, shape)
        offset += math.prod(shape)
    return table, offset


def runs_kernel(info, shard, out, scratch):
    def one(block, carry):
        scratch[:, block, :] = shard[pl.ds(block * STRIDE, STRIDE), :].T
        return carry

    lax.fori_loop(0, RUN, one, 0)
    half = STRIDE // 2
    turn = info[0] * half

    def move(lane, carry):
        out[lane] = scratch[lax.rem(lane + turn, STRIDE)].astype(BF16)
        return carry

    lax.fori_loop(0, STRIDE, move, 0)


def run_place(shards, total, lane, shard):
    count = total // STRIDE
    whole = total // shards
    step, odd = whole // STRIDE, (whole % STRIDE) // (STRIDE // 2)
    extra = lax.div(shard * odd + jnp.where(lane < STRIDE // 2, 1, 0), 2)
    start = lane * count + shard * step + extra
    return lax.div(start, STRIDE), lax.rem(start, STRIDE)


def rows_from_runs(runs, rows, first_lane, total):
    shards, lanes = runs.shape[0], runs.shape[1]
    base = first_lane * (total // STRIDE) // STRIDE

    def one(index, carry):
        lane, shard = lax.div(index, shards), lax.rem(index, shards)
        row, shift = run_place(shards, total, first_lane + lane, shard)
        row = row - base
        turned = pltpu.roll(runs[shard, lane].astype(F32), shift, 1)
        place = lax.broadcasted_iota(jnp.int32, (RUN + 1, STRIDE), 1)
        last, before = carry
        joint = jnp.where(row - before == RUN, last[2:3], last[1:2])
        below = jnp.concatenate([joint, turned], axis=0)
        above = jnp.concatenate([turned, turned[RUN - 1 :]], axis=0)
        values = jnp.where(place < shift, below, above)
        rows[pl.ds(row, RUN + 1), :] = values
        return values[RUN - 2 :], row

    lax.fori_loop(0, shards * lanes, one, (jnp.zeros((3, STRIDE), F32), -RUN), unroll=4)


def runs_from_rows(rows, out, first_lane, base, total):
    shards, lanes = out.shape[0], out.shape[1]

    def one(index, carry):
        lane, shard = lax.div(index, shards), lax.rem(index, shards)
        row, shift = run_place(shards, total, first_lane + lane, shard)
        turned = pltpu.roll(rows[pl.ds(row - base, RUN + 1), :], (STRIDE - shift) % STRIDE, 1)
        place = lax.broadcasted_iota(jnp.int32, (RUN, STRIDE), 1)
        out[shard, lane] = jnp.where(
            place < STRIDE - shift, turned[:RUN], turned[1:]
        ).astype(BF16)
        return carry

    lax.fori_loop(0, shards * lanes, one, 0, unroll=4)


def row_height(base, first_lane, last_lane, total):
    end = (last_lane * (total // STRIDE)) // STRIDE + RUN + 2
    return -(-(end - base) // 8) * 8


def take_matrix(rows, first, shape):
    blocks = shape[1] // STRIDE
    return [
        rows[pl.ds(first + block, shape[0], stride=blocks), :]
        if blocks > 1
        else rows[first : first + shape[0], :]
        for block in range(blocks)
    ]


def put_matrix(rows, first, matrix):
    height, width = matrix.shape
    blocks = width // STRIDE
    for block in range(blocks):
        part = matrix[:, block * STRIDE : (block + 1) * STRIDE]
        if blocks > 1:
            rows[pl.ds(first + block, height, stride=blocks), :] = part
        else:
            rows[first : first + height, :] = part


def spread(index, heads, rows):
    lane = lax.broadcasted_iota(jnp.int32, (STRIDE, STRIDE), 0)
    channel = lax.broadcasted_iota(jnp.int32, (STRIDE, STRIDE), 1)
    return (channel == index * (STRIDE // heads) + lane // heads).astype(BF16)


def take_narrow(rows, first, heads, high):
    total = jnp.zeros((high, STRIDE), F32)
    head = lax.broadcasted_iota(jnp.int32, (high, STRIDE), 0)
    lane = lax.broadcasted_iota(jnp.int32, (high, STRIDE), 1)
    for index in range(heads):
        line = rows[first + index : first + index + 1, :]
        picked = jnp.where(lane % heads == head, line, 0.0).astype(BF16)
        total = total + mm(picked, spread(index, heads, rows))
    return total


def put_narrow(rows, first, heads, matrix):
    turned = matrix.T.astype(BF16)
    high = turned.shape[0]
    head = lax.broadcasted_iota(jnp.int32, (high, STRIDE), 0)
    lane = lax.broadcasted_iota(jnp.int32, (high, STRIDE), 1)
    for index in range(heads):
        wide = mm_nt(turned, spread(index, heads, rows))
        rows[first + index : first + index + 1, :] = jnp.sum(
            jnp.where(lane % heads == head, wide, 0.0), axis=0, keepdims=True
        )


PAIR_MATRICES = (
    (OUTGOING, PROJ_GATE), (OUTGOING, PROJ_OUT), (OUTGOING, GATE_OUT),
    (INCOMING, PROJ_GATE), (INCOMING, PROJ_OUT), (INCOMING, GATE_OUT),
    (STARTING, QKVG), (STARTING, OUTPUT), (ENDING, QKVG), (ENDING, OUTPUT), (PAIR, UP), (PAIR, DOWN),
)
PAIR_COLUMNS = (
    (OUTGOING, ((OUTGOING, NORM_GAIN), (OUTGOING, NORM_BIAS), (OUTGOING, OUT_GAIN), (OUTGOING, OUT_BIAS))),
    (INCOMING, ((INCOMING, NORM_GAIN), (INCOMING, NORM_BIAS), (INCOMING, OUT_GAIN), (INCOMING, OUT_BIAS))),
    (STARTING, ((STARTING, NORM_GAIN), (STARTING, NORM_BIAS))),
    (ENDING, ((ENDING, NORM_GAIN), (ENDING, NORM_BIAS))),
    (PAIR, ((PAIR, NORM_GAIN), (PAIR, NORM_BIAS))),
)
SINGLE_MATRICES = ((ATTEND, QKVG), (ATTEND, OUTPUT), (SINGLE, UP), (SINGLE, DOWN))
SINGLE_VECTORS = ((ATTEND, NORM_GAIN), (ATTEND, NORM_BIAS), (SINGLE, NORM_GAIN), (SINGLE, NORM_BIAS))


def put_columns(rows, out, table, base, names):
    out[...] = jnp.zeros(out.shape, F32)
    lines = [rows[table[name][0] - base : table[name][0] - base + 1, :] for name in names]
    lines.append(jnp.zeros((8 - len(lines), STRIDE), F32))
    out[...] = jnp.concatenate(lines, axis=0).T


def unpack_pair_kernel(table, total, runs, *refs):
    rows = refs[-1]
    outs = list(refs[:-1])
    rows_from_runs(runs, rows, 0, total)
    for name in PAIR_MATRICES:
        first, shape = table[name]
        plain, turned = outs.pop(0), outs.pop(0)
        for block, part in enumerate(take_matrix(rows, first, shape)):
            place = slice(block * STRIDE, (block + 1) * STRIDE)
            plain[:, place] = part.astype(BF16)
            turned[place, :] = part.T.astype(BF16)
    for prefix in (STARTING, ENDING):
        plain, turned = outs.pop(0), outs.pop(0)
        first, shape = table[(prefix, BIAS_PROJ)]
        matrix = take_narrow(rows, first, shape[1], 8)
        turned[...] = matrix.astype(BF16)
        plain[...] = matrix.T.astype(BF16)
    for prefix, names in PAIR_COLUMNS:
        put_columns(rows, outs.pop(0), table, 0, names)


def unpack_single_kernel(table, total, first_lane, runs, *refs):
    rows = refs[-1]
    outs = list(refs[:-1])
    rows_from_runs(runs, rows, first_lane, total)
    base = first_lane * (total // STRIDE) // STRIDE
    for name in SINGLE_MATRICES:
        first, shape = table[name]
        out = outs.pop(0)
        for block, part in enumerate(take_matrix(rows, first - base, shape)):
            out[:, block * STRIDE : (block + 1) * STRIDE] = part.astype(BF16)
    first, shape = table[(ATTEND, PAIR_PROJ)]
    matrix = take_narrow(rows, first - base, shape[1], shape[1])
    plain, turned = outs.pop(0), outs.pop(0)
    turned[...] = matrix.astype(BF16)
    plain[...] = matrix.T.astype(BF16)
    put_columns(rows, outs.pop(0), table, base, ((ATTEND, PAIR_GAIN), (ATTEND, PAIR_BIAS)))
    lines = outs.pop(0)
    lines[...] = jnp.zeros(lines.shape, F32)
    for index, name in enumerate(SINGLE_VECTORS):
        first, shape = table[name]
        for block in range(shape[0] // STRIDE):
            lines[index : index + 1, block * STRIDE : (block + 1) * STRIDE] = rows[
                first - base + block : first - base + block + 1, :
            ]


def pack_kernel(table, total, first_lane, base, names, *refs):
    ins, out, rows = refs[: len(names)], refs[-2], refs[-1]
    for name, ref in zip(names, ins):
        if isinstance(name, tuple):
            first, shape = table[name]
            if shape[1] % STRIDE:
                put_narrow(rows, first - base, shape[1], ref[...])
            else:
                put_matrix(rows, first - base, ref)
        else:
            for index, vector in name:
                first, shape = table[vector]
                for block in range(shape[0] // STRIDE):
                    rows[first + block - base : first + block - base + 1, :] = ref[
                        index : index + 1, block * STRIDE : (block + 1) * STRIDE
                    ]
    runs_from_rows(rows, out, first_lane, base, total)


def shard_kernel(whole, info, runs, out, squares):
    half = STRIDE // 2
    squares[...] = jnp.zeros(squares.shape, F32)

    def one(block, carry):
        first = runs[pl.ds(info[0] * half, half), block, :]
        second = runs[pl.ds(half - info[0] * half, half), block, :]
        values = jnp.concatenate([first, second], axis=0).T
        row = block * STRIDE + lax.broadcasted_iota(jnp.int32, values.shape, 0)
        lane = lax.broadcasted_iota(jnp.int32, values.shape, 1)
        values = jnp.where(row * STRIDE + lane < whole, values, 0.0)
        out[pl.ds(block * STRIDE, STRIDE), :] = values
        squares[...] += jnp.sum((values * values).reshape(-1, 8, STRIDE), axis=0)
        return carry

    lax.fori_loop(0, RUN, one, 0)


def whole_call(kernel, name, ins, outs, scratch, time=8):
    def spec(axis):
        return pl.BlockSpec(memory_space=pltpu.SMEM if axis == "smem" else pltpu.VMEM)

    return pl.pallas_call(
        kernel,
        in_specs=[spec(axis) for array, axis in ins],
        out_specs=[pl.BlockSpec(memory_space=pltpu.VMEM) for shape, dtype in outs],
        out_shape=[jax.ShapeDtypeStruct(shape, dtype) for shape, dtype in outs],
        scratch_shapes=[pltpu.VMEM(shape, dtype) for shape, dtype in scratch],
        compiler_params=pltpu.CompilerParams(vmem_limit_bytes=VMEM_LIMIT),
        cost_estimate=cost(time),
        name=name,
    )(*[array for array, axis in ins])


def unpack_pair(table, total, runs):
    outs = []
    names = []
    for name in PAIR_MATRICES:
        shape = table[name][1]
        outs += [(shape, BF16), (shape[::-1], BF16)]
        names += [name, (name, T)]
    for prefix in (STARTING, ENDING):
        outs += [((STRIDE, 8), BF16), ((8, STRIDE), BF16)]
        names += [(prefix, BIAS_W), (prefix, BIAS_T)]
    for prefix, parts in PAIR_COLUMNS:
        outs.append(((STRIDE, 8), F32))
        names.append((prefix, COLS))
    height = row_height(0, 0, runs.shape[1], total)
    values = whole_call(
        functools.partial(unpack_pair_kernel, table, total), "pair_weights", [(runs, None)], outs,
        [((height, STRIDE), F32)],
    )
    return dict(zip(names, values))


def unpack_single(table, total, first_lane, runs):
    outs = [(table[name][1], BF16) for name in SINGLE_MATRICES]
    names = list(SINGLE_MATRICES)
    shape = table[(ATTEND, PAIR_PROJ)][1]
    outs += [(shape, BF16), (shape[::-1], BF16), ((STRIDE, 8), F32), ((8, S), F32)]
    names += [(ATTEND, PAIR_PROJ), ((ATTEND, PAIR_PROJ), T), (ATTEND, COLS), (SINGLE, VECTORS)]
    base = first_lane * (total // STRIDE) // STRIDE
    height = row_height(base, first_lane, first_lane + runs.shape[1], total)
    values = whole_call(
        functools.partial(unpack_single_kernel, table, total, first_lane), "single_weights",
        [(runs, None)], outs, [((height, STRIDE), F32)],
    )
    return dict(zip(names, values))


def pack(name, table, total, shards, lanes, base, parts):
    height = row_height(base, *lanes, total)
    for held, array in parts:
        if isinstance(held, tuple):
            end = table[held][0] - base + array.shape[0] * max(1, array.shape[1] // STRIDE)
            height = max(height, -(-end // 8) * 8)
    return whole_call(
        functools.partial(pack_kernel, table, total, lanes[0], base, [held for held, array in parts]),
        name, [(array, None) for held, array in parts],
        [((shards, lanes[1] - lanes[0], RUN, STRIDE), BF16)], [((height, STRIDE), F32)],
    )[0]


def swap(values, group):
    return lax.all_to_all(values, group, split_axis=0, concat_axis=0, tiled=True)


def single_attend(single_state, bias, penalty, weights, group):
    gain, shift = norm_pair(weights, ATTEND)
    lowered = layer_norm(single_state, gain, shift).astype(BF16)
    rows, width = lowered.shape
    size = width // SA_HEADS
    qkvg = matmul(lowered, weights[(ATTEND, QKVG)])
    query = qkvg[:, :width].astype(BF16).reshape(rows, SA_HEADS, size)
    gate = qkvg[:, 3 * width :]
    both = lax.all_gather(qkvg[:, width : 3 * width].astype(BF16), group, axis=0, tiled=True)
    keys_all = both[:, :width].reshape(-1, SA_HEADS, size)
    values_all = both[:, width:].reshape(-1, SA_HEADS, size)
    scores = jnp.einsum(
        "ihd,jhd->hij", query, keys_all, preferred_element_type=F32
    ) * size ** (-0.5)
    scores = scores + bias + penalty[None, None, :]
    probs = jax.nn.softmax(scores, axis=-1)
    probs_low = probs.astype(BF16)
    mixed = jnp.einsum("hij,jhd->ihd", probs_low, values_all, preferred_element_type=F32)
    mixed = mixed.reshape(rows, width)
    gated_low = gated_output(mixed, gate).astype(BF16)
    update = matmul(gated_low, weights[(ATTEND, OUTPUT)])
    return (
        update,
        (single_state, lowered, query, keys_all, values_all, gate, probs, probs_low, mixed, gated_low),
    )


def single_attend_back(saved, grad_update, weights, grads, group):
    single_state, lowered, query, keys_all, values_all, gate, probs, probs_low, mixed, gated_low = saved
    rows, width = lowered.shape
    size = width // SA_HEADS
    scale = size ** (-0.5)
    grad_low = grad_update.astype(BF16)
    grads[(ATTEND, OUTPUT)] = outer_sum(gated_low, grad_low)
    grad_gated = matmul(grad_low, weights[(ATTEND, OUTPUT)].T)
    _, pullback = jax.vjp(gated_output, mixed, gate)
    grad_mixed, grad_gate = pullback(grad_gated)
    grad_mixed = grad_mixed.astype(BF16).reshape(rows, SA_HEADS, size)
    grad_probs = jnp.einsum("ihd,jhd->hij", grad_mixed, values_all, preferred_element_type=F32)
    delta = jnp.sum(probs * grad_probs, axis=-1, keepdims=True)
    grad_scores = (probs * (grad_probs - delta)).astype(BF16)
    grad_query = (
        jnp.einsum("hij,jhd->ihd", grad_scores, keys_all, preferred_element_type=F32) * scale
    )
    key_part = jnp.einsum("hij,ihd->jhd", grad_scores, query, preferred_element_type=F32) * scale
    value_part = jnp.einsum("hij,ihd->jhd", probs_low, grad_mixed, preferred_element_type=F32)
    parts = jnp.concatenate(
        [key_part.reshape(-1, rows, width), value_part.reshape(-1, rows, width)], axis=-1
    )
    grad_both = jnp.sum(swap(parts.astype(BF16), group).astype(F32), axis=0)
    grad_qkvg = jnp.concatenate(
        [grad_query.reshape(rows, width), grad_both, grad_gate], axis=-1
    ).astype(BF16)
    grads[(ATTEND, QKVG)] = outer_sum(lowered, grad_qkvg)
    grad_lowered = matmul(grad_qkvg, weights[(ATTEND, QKVG)].T)
    gain, shift = norm_pair(weights, ATTEND)
    grad_single, grads[(ATTEND, NORM_GAIN)], grads[(ATTEND, NORM_BIAS)] = norm_backward(
        single_state, gain, shift, grad_lowered
    )
    return grad_single, grad_scores


def to_plane(values, parts):
    shape = values.shape
    values = swap(values.reshape((parts, -1) + shape[1:]), "crop")
    return swap(values, "z").reshape(shape)


def from_plane(values, parts):
    shape = values.shape
    values = swap(values.reshape((parts, -1) + shape[1:]), "z")
    return swap(values, "crop").reshape(shape)


def after(values, *others):
    held = lax.optimization_barrier((values,) + others)
    return held


def pair_path(pair, info, alive, orders, weights, cotangent, middle, between, group, parts):
    rows, length, width = pair.shape
    hidden = weights[(OUTGOING, PROJ_OUT)].shape[0]
    devices = length // rows
    cores = devices // parts
    order, order_back = orders
    read_first = functools.partial(read_tokens, order)
    read_last = functools.partial(read_turned, order)
    part = hidden // devices
    steps = rows // 16
    state_shape = (rows, width, length)
    block = rows // steps
    half = rows // 2
    flip_shape = (devices, rows, rows, width)
    flip_half = (devices, rows, half, width)
    product_half = (devices, 2, part, half, length)
    tri_half = (devices, part, half, length)
    tri_rows = (hidden, half, length)
    channel_block = math.gcd(part, 4)

    def products(name, kernel, arrays, out_shape):
        axes = {4: 1, 5: 2}
        out = (out_shape, BF16, axes[len(out_shape)])
        return run_rows(
            kernel, name, part // channel_block,
            [(Both(halves), axes[halves[0].ndim]) for halves in arrays], [out, out], [], 7,
        )

    def swap_halves(halves, shape=None):
        moved = [swap(values, group) for values in halves]
        return moved if shape is None else [values.reshape(shape) for values in moved]

    def cols(prefix):
        return weights[(prefix, COLS)]

    tri_cols = cols

    def turned(name):
        return weights[(name, T)]

    tri_scratch = ((hidden, block, length), F32)
    product_scratch = ((2 * hidden, block, length), F32)
    head_scratch = ((8, block, length), F32)
    wide = ((width, length), F32)
    flip_scratch = ((length, block, width), F32)
    table = ((TA_HEADS, length, length), F32)
    attend_saves = [((rows, TA_HEADS, length), F32, 0), (state_shape, BF16, 0)]

    (product,) = run_halves(
        functools.partial(tri_pre_first_kernel, devices, read_first), "outgoing_in", steps,
        [
            ([info[:half], info[half:]], "smem"), (alive, None), (pair, 0), (tri_cols(OUTGOING), None),
            (turned((OUTGOING, PROJ_GATE)), None),
        ],
        [(product_half, BF16, 3)], [product_scratch], 13,
    )
    product_one = swap_halves(product)
    tri_one = products(
        "outgoing_product", functools.partial(tri_product_kernel, False), [product_one], tri_half
    )
    tri_one = swap_halves(tri_one, tri_rows)
    state_one, product = run_halves(
        functools.partial(tri_join_kernel, devices, read_first), "outgoing_out_incoming_in", steps,
        [
            ([info[:half], info[half:]], "smem"), (alive, None), (pair, 0), (tri_one, 1), (tri_cols(OUTGOING), None),
            (turned((OUTGOING, PROJ_OUT)), None), (turned((OUTGOING, GATE_OUT)), None),
            (tri_cols(INCOMING), None), (turned((INCOMING, PROJ_GATE)), None),
        ],
        [(state_shape, F32, 0), (product_half, BF16, 3)], [tri_scratch, product_scratch], 22,
    )
    product_two = swap_halves(product)
    tri_two = products(
        "incoming_product", functools.partial(tri_product_kernel, True), [product_two], tri_half
    )
    tri_two = swap_halves(tri_two, tri_rows)
    state_two, bias = run_halves(
        tri_last_kernel, "incoming_out_starting_bias", steps,
        [
            (state_one, 0), (tri_two, 1), (tri_cols(INCOMING), None),
            (turned((INCOMING, PROJ_OUT)), None), (turned((INCOMING, GATE_OUT)), None),
            (cols(STARTING), None), (weights[(STARTING, BIAS_T)], None),
        ],
        [(state_shape, F32, 0), ((TA_HEADS, rows, length), BF16, 1)], [tri_scratch, head_scratch],
    )
    bias_one = lax.all_gather(bias, group, axis=0, tiled=False)
    cotangent = cotangent.reshape(rows, parts, cores, parts, -1, width).transpose(3, 2, 1, 4, 0, 5)
    cotangent = swap(cotangent.reshape(flip_shape), group)
    cotangent = swap(cotangent.reshape((parts, cores) + flip_shape[1:]), "z").reshape(flip_shape)
    flipped, totals_one, mixed_one = run_halves(
        starting_kernel, "starting_attention", steps,
        [
            (alive, None), (state_two, 0), (bias_one, None), (cols(STARTING), None),
            (turned((STARTING, QKVG)), None), (turned((STARTING, OUTPUT)), None),
        ],
        [(flip_half, BF16, 2)] + attend_saves, [table, flip_scratch], 21,
    )
    state_three = Both(swap_halves(flipped))
    (bias,) = run_rows(
        flipped_bias_kernel, "ending_bias", steps,
        [(state_three, 1), (cols(ENDING), None), (weights[(ENDING, BIAS_T)], None)],
        [((TA_HEADS, rows, length), BF16, 1)], [head_scratch],
    )
    bias_two = lax.all_gather(bias, group, axis=0, tiled=False)
    state_four, totals_two, mixed_two = run_rows(
        ending_kernel, "ending_attention", steps,
        [
            (alive, None), (state_three, 1), (bias_two, None), (cols(ENDING), None),
            (turned((ENDING, QKVG)), None), (turned((ENDING, OUTPUT)), None),
        ],
        [(state_shape, F32, 0)] + attend_saves, [table],
    )
    pair_cols, attend_cols = cols(PAIR), cols(ATTEND)
    state_four, cotangent = after(state_four, cotangent)
    state_five, pair_out, single_bias = run_rows(
        functools.partial(transition_kernel, order_back), "pair_transition", steps,
        [
            (state_four, 0), (pair_cols, None), (turned((PAIR, UP)), None), (turned((PAIR, DOWN)), None),
            (attend_cols, None), (turned((ATTEND, PAIR_PROJ)), None),
        ],
        [(state_shape, F32, 0), ((length, rows, width), BF16, 1), ((SA_HEADS, rows, length), BF16, 1)],
        [flip_scratch, ((SA_HEADS, block, length), F32)],
    )
    pair_out = swap(pair_out.reshape((parts, -1) + pair_out.shape[1:]), "z")

    def turn(values):
        heads = values.shape[0]
        sent = values.reshape(heads, rows, devices, rows).transpose(2, 0, 3, 1)
        return swap(sent, group).transpose(1, 2, 0, 3).reshape(heads, rows, length)

    single_grad_scores = middle(turn(single_bias).astype(F32))
    grads = {}
    grad_four, grads[(PAIR, UP)], grads[(PAIR, DOWN)], grads[(ATTEND, PAIR_PROJ)], vecs = run_rows(
        functools.partial(transition_back_kernel, read_last), "pair_transition_back", steps,
        [
            (state_four, 0), (state_five, 0), (cotangent, 1), (turn(single_grad_scores), 1),
            (pair_cols, None), (turned((PAIR, UP)), None), (weights[(PAIR, UP)], None),
            (weights[(PAIR, DOWN)], None), (attend_cols, None), (weights[(ATTEND, PAIR_PROJ)], None),
        ],
        [
            (state_shape, F32, 0), (weights[(PAIR, UP)].shape, F32, None),
            (weights[(PAIR, DOWN)].shape, F32, None), (weights[(ATTEND, PAIR_PROJ)].shape, F32, None),
            ((8, width), F32, None),
        ],
        [wide, wide, wide, wide, ((SA_HEADS, block, length), F32)], 30,
    )
    grads[(PAIR, VECTORS)] = vecs

    grad_four, pair_out = after(grad_four, pair_out)
    pair_out = swap(pair_out.reshape(flip_shape), group)

    def attention_back(prefix, read, read_grad, source, source_axis, grad, grad_axis, bias, totals, mixed):
        lowered_grad, bias_grad, grads[(prefix, QKVG)], grads[(prefix, OUTPUT)] = run_rows(
            functools.partial(attention_back_kernel, read, read_grad),
            "attention_back", steps,
            [
                (alive, None), (source, source_axis), (grad, grad_axis), (bias, None), (totals, 0),
                (mixed, 0), (cols(prefix), None), (turned((prefix, QKVG)), None),
                (weights[(prefix, QKVG)], None), (weights[(prefix, OUTPUT)], None),
            ],
            [
                (state_shape, BF16, 0), ((devices, TA_HEADS, rows, length), BF16, None),
                (weights[(prefix, QKVG)].shape, F32, None), (weights[(prefix, OUTPUT)].shape, F32, None),
            ],
            [table, table], 34,
        )
        return lowered_grad, swap(bias_grad, group)

    lowered_grad, bias_grad = attention_back(
        ENDING, read_flipped, read_plain, state_three, 1, grad_four, 0, bias_two, totals_two, mixed_two
    )
    bias_grad, pair_out = after(bias_grad, pair_out)
    pair_out = pair_out.reshape(parts, cores, rows, parts, -1, width).transpose(2, 3, 1, 0, 4, 5)
    pair_out = pair_out.reshape(rows, length, width)
    flipped, bias_w_grad, vecs = run_halves(
        ending_end_kernel, "ending_attention_end", steps,
        [
            (state_three, 1), (grad_four, 0), (lowered_grad, 0), (bias_grad, 2), (cols(ENDING), None),
            (weights[(ENDING, BIAS_W)], None),
        ],
        [(flip_half, BF16, 2), ((width, 8), F32, None), ((8, width), F32, None)],
        [wide, wide, head_scratch, flip_scratch],
    )
    grads[(ENDING, BIAS_PROJ)], grads[(ENDING, VECTORS)] = bias_w_grad, vecs
    grad_three = Both(after(*swap_halves(flipped), between(0, grads))[:2])
    lowered_grad, bias_grad = attention_back(
        STARTING, read_plain, read_flipped, state_two, 0, grad_three, 1, bias_one, totals_one, mixed_one
    )
    square = weights[(INCOMING, GATE_OUT)].shape
    (
        grad_two, grad_tri, gate_back, bias_w_grad, grads[(INCOMING, PROJ_OUT)], grads[(INCOMING, GATE_OUT)], vecs,
    ) = run_halves(
        starting_end_kernel, "starting_end_incoming_out_back", steps,
        [
            (state_two, 0), (grad_three, 1), (lowered_grad, 0), (bias_grad, 2), (cols(STARTING), None),
            (weights[(STARTING, BIAS_W)], None), (state_one, 0), (tri_two, 1), (tri_cols(INCOMING), None),
            (turned((INCOMING, PROJ_OUT)), None), (turned((INCOMING, GATE_OUT)), None),
            (weights[(INCOMING, PROJ_OUT)], None), (weights[(INCOMING, GATE_OUT)], None),
        ],
        [
            (state_shape, F32, 0), (tri_rows, BF16, 1), (state_shape, BF16, 0),
            ((width, 8), F32, None), (square, F32, None), (square, F32, None), ((8, width), F32, None),
        ],
        [wide, wide, wide, wide, head_scratch, tri_scratch], 26,
    )
    grads[(STARTING, BIAS_PROJ)], grads[(STARTING, VECTORS)] = bias_w_grad, vecs
    grad_tri = swap_halves([values.reshape(tri_half) for values in grad_tri])
    grad_tri = after(*grad_tri, between(1, grads))[:2]
    product_grad = products(
        "incoming_product_back", functools.partial(tri_product_back_kernel, True),
        [grad_tri, product_two], product_half,
    )
    product_grad = swap_halves(product_grad)
    (
        grad_one, grad_tri, gate_back, grads[(INCOMING, PROJ_GATE)], grads[(OUTGOING, PROJ_OUT)],
        grads[(OUTGOING, GATE_OUT)], vecs,
    ) = run_halves(
        functools.partial(tri_join_back_kernel, read_first), "incoming_in_outgoing_out_back", steps,
        [
            ([info[:half], info[half:]], "smem"), (alive, None), (state_one, 0), (product_grad, 3), (gate_back, 0), (grad_two, 0),
            (tri_cols(INCOMING), None), (turned((INCOMING, PROJ_GATE)), None),
            (weights[(INCOMING, PROJ_GATE)], None), (pair, 0), (tri_one, 1), (tri_cols(OUTGOING), None),
            (turned((OUTGOING, PROJ_OUT)), None), (turned((OUTGOING, GATE_OUT)), None),
            (weights[(OUTGOING, PROJ_OUT)], None), (weights[(OUTGOING, GATE_OUT)], None),
        ],
        [
            (state_shape, F32, 0), (tri_rows, BF16, 1), (state_shape, BF16, 0),
            (weights[(INCOMING, PROJ_GATE)].shape, F32, None), (square, F32, None), (square, F32, None),
            ((8, width), F32, None),
        ],
        [wide, wide, wide, wide, product_scratch, tri_scratch], 37,
    )
    grads[(INCOMING, VECTORS)] = vecs
    between(2, grads)
    grad_tri = swap_halves([values.reshape(tri_half) for values in grad_tri])
    grad_tri = after(*grad_tri, between(3, grads))[:2]
    product_grad = products(
        "outgoing_product_back", functools.partial(tri_product_back_kernel, False),
        [grad_tri, product_one], product_half,
    )
    product_grad = swap_halves(product_grad)
    pair_grad, grads[(OUTGOING, PROJ_GATE)], vecs = run_halves(
        functools.partial(tri_first_back_kernel, read_first, order_back), "outgoing_in_back", steps,
        [
            ([info[:half], info[half:]], "smem"), (alive, None), (pair, 0), (product_grad, 3), (gate_back, 0), (grad_one, 0),
            (tri_cols(OUTGOING), None), (turned((OUTGOING, PROJ_GATE)), None),
            (weights[(OUTGOING, PROJ_GATE)], None),
        ],
        [
            ((rows, length, width), BF16, 0), (weights[(OUTGOING, PROJ_GATE)].shape, F32, None),
            ((8, width), F32, None),
        ],
        [wide, wide, product_scratch], 20,
    )
    grads[(OUTGOING, VECTORS)] = vecs
    return pair_out, pair_grad, grads


HELD = {
    (PAIR, VECTORS): ((PAIR, NORM_GAIN), (PAIR, NORM_BIAS), (ATTEND, PAIR_GAIN), (ATTEND, PAIR_BIAS)),
    (ENDING, VECTORS): ((ENDING, NORM_GAIN), (ENDING, NORM_BIAS)),
    (STARTING, VECTORS): (
        (STARTING, NORM_GAIN), (STARTING, NORM_BIAS), (INCOMING, OUT_GAIN), (INCOMING, OUT_BIAS)
    ),
    (INCOMING, VECTORS): (
        (INCOMING, NORM_GAIN), (INCOMING, NORM_BIAS), (OUTGOING, OUT_GAIN), (OUTGOING, OUT_BIAS)
    ),
    (OUTGOING, VECTORS): ((OUTGOING, NORM_GAIN), (OUTGOING, NORM_BIAS)),
}


def vector_part(grads, name, prefix):
    pairs = [(row, held) for row, held in enumerate(HELD[name]) if prefix in (None, held[0])]
    return (pairs, grads[name])


def fast_shards(parts, cores, pair, single, lengths, params, moment_one, moment_two, pair_cotangent, single_cotangent):
    entries = layout(C, H, S, TA_HEADS, SA_HEADS)
    table, total = table_of(entries)
    count = total // STRIDE
    shard_size = params.shape[0]
    attend = table[(ATTEND, NORM_GAIN)][0]
    pair_lanes = -(-attend * STRIDE // count)
    single_lane = attend * STRIDE // count
    devices = parts * cores
    line, group = ("z", "core"), ("crop", "core")
    row_index = lax.axis_index(line)
    odd = ((row_index * shard_size) % STRIDE) // (STRIDE // 2)
    place = jnp.stack([odd, odd]).astype(jnp.int32)
    shard_rows = jnp.pad(params, (0, RUN * STRIDE * STRIDE - shard_size)).reshape(-1, STRIDE)
    (runs,) = whole_call(
        runs_kernel, "parameter_runs", [(place, "smem"), (shard_rows, None)],
        [((STRIDE, RUN, STRIDE), BF16)], [((STRIDE, RUN, STRIDE), F32)],
    )
    rows, length, width = pair.shape[1:]
    pair_in = swap(pair[0].reshape(parts, -1, length, width), "crop")
    pair_in, first_runs, lengths = after(pair_in, runs[:pair_lanes], lengths)
    pair_in = swap(pair_in, "z").reshape(rows, length, width)
    live = swap(jnp.broadcast_to(lengths.astype(F32), (parts, STRIDE)), "crop")
    weights = unpack_pair(table, total, lax.all_gather(first_runs, line))
    pair_in, last_runs = after(pair_in, runs[single_lane:])
    weights.update(unpack_single(table, total, single_lane, lax.all_gather(last_runs, line)))
    for index, name in enumerate(SINGLE_VECTORS):
        weights[name] = weights[(SINGLE, VECTORS)][index]
    size = rows // parts
    blocks = np.arange(length // size).reshape(parts, cores, parts)
    order = blocks.transpose(2, 1, 0).reshape(-1)
    orders = (order.tolist(), np.argsort(order).tolist())
    tokens = (order[:, None] * size + np.arange(size)).reshape(-1)
    live = live[lax.axis_index("z"), 0]
    width = single.shape[2]
    both = to_plane(jnp.concatenate([single[0], single_cotangent[0]], axis=1), parts).astype(F32)
    single_state, single_back = both[:, :width], both[:, width:]
    mask = (tokens.astype(np.float32) < live).astype(F32)
    info = lax.dynamic_slice_in_dim(mask, lax.axis_index(group) * rows, rows).astype(jnp.int32)
    alive = jnp.broadcast_to(mask, (8, length))
    penalty = (mask - 1.0) * MASKED
    results = {}
    single_grads = {}

    def middle(bias):
        update, saved = single_attend(single_state, bias, penalty, weights, group)
        single_mid = single_state + update
        update, saved_last = transition_forward(single_mid, weights, SINGLE)
        results[SINGLE] = single_mid + update
        grad = single_back
        grad = grad + transition_backward(saved_last, grad, weights, SINGLE, single_grads)
        more, grad_scores = single_attend_back(saved, grad, weights, single_grads, group)
        results["single_grad"] = grad + more
        return grad_scores

    def reduce_runs(sent):
        part = jnp.sum(swap(sent, line).astype(F32), axis=0).astype(BF16)
        return jnp.sum(lax.all_gather(part, "crop").astype(F32), axis=0)

    reduced = {}
    lines_held = list(enumerate(SINGLE_VECTORS))
    late_lanes = -(-table[(INCOMING, NORM_GAIN)][0] * STRIDE // count)

    def lines():
        values = jnp.concatenate([single_grads[name].reshape(1, S) for name in SINGLE_VECTORS], axis=0)
        return jnp.pad(values, ((0, 8 - len(SINGLE_VECTORS)), (0, 0)))

    def between(number, grads):
        if number == 0:
            sent = pack(
                "single_gradient", table, total, devices, (pair_lanes, STRIDE), attend,
                [(name, single_grads[name]) for name in SINGLE_MATRICES]
                + [((ATTEND, PAIR_PROJ), grads[(ATTEND, PAIR_PROJ)])]
                + [vector_part(grads, (PAIR, VECTORS), ATTEND), (lines_held, lines())],
            )
            reduced[2] = lax.psum_scatter(sent, line, scatter_dimension=0, tiled=False)
            return sent
        if number == 1:
            scattered = reduced[2]
            reduced[2] = lax.psum(scattered, "crop")
            return scattered
        if number == 3:
            return reduced[2]
        taken = -(-(pair_lanes * count - (attend + 2 * S // STRIDE) * STRIDE) // (4 * S))
        first = table[(INCOMING, NORM_GAIN)][0]
        sent = pack(
            "pair_gradient", table, total, devices, (late_lanes, pair_lanes), first,
            [(name, grads[name]) for name in PAIR_MATRICES if table[name][0] >= first]
            + [(name, grads[name]) for name in ((STARTING, BIAS_PROJ), (ENDING, BIAS_PROJ))]
            + [vector_part(grads, name, None) for name in ((ENDING, VECTORS), (STARTING, VECTORS))]
            + [vector_part(grads, (INCOMING, VECTORS), INCOMING)]
            + [vector_part(grads, (PAIR, VECTORS), PAIR)]
            + [(lines_held[:2], lines()), ((ATTEND, QKVG), single_grads[(ATTEND, QKVG)][: -(-taken // 8) * 8])],
        )
        reduced[1] = reduce_runs(sent)
        return None

    pair_out, pair_grad, grads = pair_path(
        pair_in, info, alive, orders, weights, pair_cotangent[0], middle, between, group, parts
    )
    pair_grad = from_plane(pair_grad, parts).astype(F32)
    both = from_plane(jnp.concatenate([results[SINGLE], results["single_grad"]], axis=1), parts)
    single_out, single_grad = both[:, :width].astype(BF16), both[:, width:]
    first = table[(INCOMING, NORM_GAIN)][0]
    taken = -(-(late_lanes * count - (first + 2) * STRIDE) // (4 * H))
    sent = pack(
        "outgoing_gradient", table, total, devices, (0, late_lanes), 0,
        [(name, grads[name]) for name in PAIR_MATRICES if table[name][0] < first]
        + [vector_part(grads, (OUTGOING, VECTORS), None)]
        + [vector_part(grads, (INCOMING, VECTORS), None)]
        + [((INCOMING, PROJ_GATE), grads[(INCOMING, PROJ_GATE)][: -(-taken // 8) * 8])],
    )
    reduced[0] = reduce_runs(sent)
    shard, squares = whole_call(
        functools.partial(shard_kernel, shard_size), "gradient_share",
        [(place, "smem"), (jnp.concatenate([reduced[part].astype(F32) for part in range(3)], axis=0), None)],
        [((RUN * STRIDE, STRIDE), F32), ((8, STRIDE), F32)], [],
    )
    shard = shard.reshape(-1)[:shard_size]
    clip_norm = jnp.sqrt(jnp.sum(lax.all_gather(squares, line)))
    clipped = shard * (CLIP / jnp.maximum(clip_norm, CLIP))
    new_first = BETA_ONE * moment_one + (1.0 - BETA_ONE) * clipped
    new_second = BETA_TWO * moment_two + (1.0 - BETA_TWO) * clipped * clipped
    rates, decays = rate_tables(entries)
    rate_shard = lax.dynamic_slice_in_dim(jnp.asarray(rates), row_index * shard_size, shard_size)
    decay_shard = lax.dynamic_slice_in_dim(jnp.asarray(decays), row_index * shard_size, shard_size)
    first_hat = new_first / (1.0 - BETA_ONE**STEP)
    second_hat = new_second / (1.0 - BETA_TWO**STEP)
    new_params = params - rate_shard * (
        first_hat / (jnp.sqrt(second_hat) + ADAM_EPS) + decay_shard * params
    )
    return (
        pair_out[None],
        single_out[None],
        pair_grad[None],
        single_grad[None],
        new_params,
        new_first,
        new_second,
        clip_norm,
    )


def solution(mesh):
    crops, devices = mesh.devices.shape
    count = table_of(layout(C, H, S, TA_HEADS, SA_HEADS))[1] // STRIDE
    fast = devices == 2 * crops and LENGTH % (devices * 16) == 0 and count // devices + 2 <= RUN * STRIDE
    row = "row"
    if fast:
        mesh = jax.sharding.Mesh(mesh.devices.reshape(crops, crops, 2), ("crop", "z", "core"))
        row = ("z", "core")
    split = [P("crop", row, None, None), P("crop", row, None), P("crop"), P(row)]
    pair, single, lengths, share = split
    return jax.shard_map(
        functools.partial(fast_shards, crops, 2) if fast else shards,
        mesh=mesh,
        in_specs=(pair, single, lengths, share, share, share, pair, single),
        out_specs=(pair, single, pair, single, share, share, share, P()),
        check_vma=False,
    )
```

```python
import functools
import math

import jax
import jax.numpy as jnp
import numpy as np
from jax import lax
from jax.experimental import pallas as pl
from jax.experimental.pallas import tpu as pltpu
from jax.sharding import PartitionSpec as P

C = 128
H = 128
S = 384
TA_HEADS = 4
SA_HEADS = 16
STEP = 10
STRIDE = 128
LENGTH = 256

OUTGOING, INCOMING, STARTING, ENDING, PAIR, ATTEND, SINGLE = range(7)
(
    NORM_GAIN,
    NORM_BIAS,
    PROJ_GATE,
    OUT_GAIN,
    OUT_BIAS,
    PROJ_OUT,
    GATE_OUT,
    QKVG,
    BIAS_PROJ,
    OUTPUT,
    UP,
    DOWN,
    PAIR_GAIN,
    PAIR_BIAS,
    PAIR_PROJ,
    COLS,
    BIAS_W,
    BIAS_T,
    VECTORS,
    T,
) = range(7, 27)


EPSILON = 1e-05
MASKED = 1000000000.0
BETA_ONE = 0.9
BETA_TWO = 0.95
ADAM_EPS = 1e-08
CLIP = 1.0


def layout(pair_width, hidden_width, single_width, tri_heads, att_heads):
    entries = []
    for prefix in (OUTGOING, INCOMING):
        entries += [
            ((prefix, NORM_GAIN), (pair_width,)),
            ((prefix, NORM_BIAS), (pair_width,)),
            ((prefix, PROJ_GATE), (pair_width, 4 * hidden_width)),
            ((prefix, OUT_GAIN), (hidden_width,)),
            ((prefix, OUT_BIAS), (hidden_width,)),
            ((prefix, PROJ_OUT), (hidden_width, pair_width)),
            ((prefix, GATE_OUT), (pair_width, pair_width)),
        ]
    for prefix in (STARTING, ENDING):
        entries += [
            ((prefix, NORM_GAIN), (pair_width,)),
            ((prefix, NORM_BIAS), (pair_width,)),
            ((prefix, QKVG), (pair_width, 4 * pair_width)),
            ((prefix, BIAS_PROJ), (pair_width, tri_heads)),
            ((prefix, OUTPUT), (pair_width, pair_width)),
        ]
    entries += [
        ((PAIR, NORM_GAIN), (pair_width,)),
        ((PAIR, NORM_BIAS), (pair_width,)),
        ((PAIR, UP), (pair_width, 8 * pair_width)),
        ((PAIR, DOWN), (4 * pair_width, pair_width)),
        ((ATTEND, NORM_GAIN), (single_width,)),
        ((ATTEND, NORM_BIAS), (single_width,)),
        ((ATTEND, QKVG), (single_width, 4 * single_width)),
        ((ATTEND, PAIR_GAIN), (pair_width,)),
        ((ATTEND, PAIR_BIAS), (pair_width,)),
        ((ATTEND, PAIR_PROJ), (pair_width, att_heads)),
        ((ATTEND, OUTPUT), (single_width, single_width)),
        ((SINGLE, NORM_GAIN), (single_width,)),
        ((SINGLE, NORM_BIAS), (single_width,)),
        ((SINGLE, UP), (single_width, 8 * single_width)),
        ((SINGLE, DOWN), (4 * single_width, single_width)),
    ]
    return entries


def logical_order(flat):
    return flat.reshape(-1, STRIDE).T.reshape(-1)


def stored_order(vector):
    return vector.reshape(STRIDE, -1).T.reshape(-1)


def rate_tables(entries):
    rates = []
    decays = []
    for name, shape in entries:
        count = math.prod(shape)
        if len(shape) == 1:
            rates.append(np.full(count, 0.5, np.float32))
            decays.append(np.zeros(count, np.float32))
        else:
            rates.append(np.full(count, 2.0 / math.sqrt(shape[0]), np.float32))
            decays.append(np.full(count, 0.01, np.float32))
    rates = np.concatenate(rates)
    decays = np.concatenate(decays)
    return (rates.reshape(STRIDE, -1).T.reshape(-1), decays.reshape(STRIDE, -1).T.reshape(-1))


def unpack(flat, entries):
    pieces = {}
    offset = 0
    for name, shape in entries:
        count = math.prod(shape)
        pieces[name] = flat[offset : offset + count].reshape(shape)
        offset += count
    return pieces


def layer_norm(values, gain, shift):
    centred = values - jnp.mean(values, axis=-1, keepdims=True)
    spread = jnp.mean(centred * centred, axis=-1, keepdims=True)
    return centred * lax.rsqrt(spread + EPSILON) * gain + shift


def norm_backward(values, gain, shift, grad):
    _, pullback = jax.vjp(layer_norm, values, gain, shift)
    return pullback(grad)


def norm_pair(weights, prefix):
    return (
        weights[(prefix, NORM_GAIN)].astype(jnp.float32),
        weights[(prefix, NORM_BIAS)].astype(jnp.float32),
    )


def gated_pair(project, pair_mask):
    half = project.shape[-1] // 2
    return project[..., :half] * jax.nn.sigmoid(project[..., half:]) * pair_mask[..., None]


def gated_output(values, gate):
    return values * jax.nn.sigmoid(gate)


def swiglu(hidden):
    half = hidden.shape[-1] // 2
    return jax.nn.silu(hidden[..., :half]) * hidden[..., half:]


def matmul(left, right):
    return jnp.dot(left, right, preferred_element_type=jnp.float32)


def outer_sum(left, right):
    return jnp.einsum(
        "nc,nd->cd",
        left.reshape(-1, left.shape[-1]),
        right.reshape(-1, right.shape[-1]),
        preferred_element_type=jnp.float32,
    )


def flip(values):
    moved = lax.all_to_all(values, "row", split_axis=1, concat_axis=0, tiled=True)
    return jnp.swapaxes(moved, 0, 1)


def channel_forward(first, second, incoming):
    whole_first, whole_second = (
        lax.all_to_all(first, "row", split_axis=2, concat_axis=0, tiled=True),
        lax.all_to_all(second, "row", split_axis=2, concat_axis=0, tiled=True),
    )
    if incoming:
        local_tri = jnp.einsum(
            "kih,kjh->ijh", whole_first, whole_second, preferred_element_type=jnp.float32
        )
        local_tri = local_tri.astype(jnp.bfloat16).astype(jnp.float32)
    else:
        local_tri = jnp.einsum(
            "ikh,jkh->ijh", whole_first, whole_second, preferred_element_type=jnp.float32
        )
    tri = lax.all_to_all(
        local_tri.astype(jnp.bfloat16), "row", split_axis=0, concat_axis=2, tiled=True
    ).astype(local_tri.dtype)
    return (tri, whole_first, whole_second)


def channel_backward(grad_tri, whole_first, whole_second, incoming):
    whole_grad = lax.all_to_all(grad_tri, "row", split_axis=2, concat_axis=0, tiled=True)
    if incoming:
        grad_a = jnp.einsum(
            "ijh,kjh->kih", whole_grad, whole_second, preferred_element_type=jnp.float32
        )
        grad_b = jnp.einsum(
            "ijh,kih->kjh", whole_grad, whole_first, preferred_element_type=jnp.float32
        )
    else:
        grad_a = jnp.einsum(
            "ijh,jkh->ikh", whole_grad, whole_second, preferred_element_type=jnp.float32
        )
        grad_b = jnp.einsum(
            "ijh,ikh->jkh", whole_grad, whole_first, preferred_element_type=jnp.float32
        )
    return (
        lax.all_to_all(
            grad_a.astype(jnp.bfloat16), "row", split_axis=0, concat_axis=2, tiled=True
        ).astype(grad_a.dtype),
        lax.all_to_all(
            grad_b.astype(jnp.bfloat16), "row", split_axis=0, concat_axis=2, tiled=True
        ).astype(grad_b.dtype),
    )


def triangle_forward(state, pair_mask, weights, prefix, incoming):
    gain, shift = norm_pair(weights, prefix)
    lowered = layer_norm(state, gain, shift).astype(jnp.bfloat16)
    project = matmul(lowered, weights[(prefix, PROJ_GATE)])
    product = gated_pair(project, pair_mask).astype(jnp.bfloat16)
    half = product.shape[-1] // 2
    tri, own, other = channel_forward(product[..., :half], product[..., half:], incoming)
    out_gain = weights[(prefix, OUT_GAIN)].astype(jnp.float32)
    out_shift = weights[(prefix, OUT_BIAS)].astype(jnp.float32)
    out_low = layer_norm(tri, out_gain, out_shift).astype(jnp.bfloat16)
    output = matmul(out_low, weights[(prefix, PROJ_OUT)])
    gate_out = matmul(lowered, weights[(prefix, GATE_OUT)])
    update = gated_output(output, gate_out)
    return (update, (state, lowered, lowered, project, own, other, tri, out_low, output, gate_out))


def triangle_backward(saved, grad_update, pair_mask, weights, prefix, incoming, grads):
    state, lowered, framed, project, own, other, tri, out_low, output, gate_out = saved
    _, pullback = jax.vjp(gated_output, output, gate_out)
    grad_output, grad_gate = pullback(grad_update)
    grad_output = grad_output.astype(jnp.bfloat16)
    grad_gate = grad_gate.astype(jnp.bfloat16)
    grads[(prefix, PROJ_OUT)] = outer_sum(out_low, grad_output)
    grads[(prefix, GATE_OUT)] = outer_sum(lowered, grad_gate)
    grad_normed = matmul(grad_output, weights[(prefix, PROJ_OUT)].T)
    out_gain = weights[(prefix, OUT_GAIN)].astype(jnp.float32)
    out_shift = weights[(prefix, OUT_BIAS)].astype(jnp.float32)
    grad_tri, grads[(prefix, OUT_GAIN)], grads[(prefix, OUT_BIAS)] = norm_backward(
        tri, out_gain, out_shift, grad_normed
    )
    grad_tri = grad_tri.astype(jnp.bfloat16)
    grad_first, grad_second = channel_backward(grad_tri, own, other, incoming)
    _, pullback = jax.vjp(lambda values: gated_pair(values, pair_mask), project)
    (grad_project,) = pullback(jnp.concatenate([grad_first, grad_second], axis=-1))
    grad_project = grad_project.astype(jnp.bfloat16)
    grads[(prefix, PROJ_GATE)] = outer_sum(framed, grad_project)
    grad_framed = matmul(grad_project, weights[(prefix, PROJ_GATE)].T)
    if incoming:
        grad_framed = grad_framed.astype(jnp.bfloat16).astype(jnp.float32)
    grad_lowered = grad_framed + matmul(grad_gate, weights[(prefix, GATE_OUT)].T)
    gain, shift = norm_pair(weights, prefix)
    grad_state, grads[(prefix, NORM_GAIN)], grads[(prefix, NORM_BIAS)] = norm_backward(
        state, gain, shift, grad_lowered
    )
    return grad_state


def row_scores(query, key, bias, penalty, scale):
    scores = jnp.einsum("jhd,khd->hjk", query, key, preferred_element_type=jnp.float32) * scale
    return scores + bias.astype(jnp.float32) + penalty[None, None, :]


def attention_forward(state, penalty, weights, prefix, ending):
    gain, shift = norm_pair(weights, prefix)
    lowered = layer_norm(state, gain, shift).astype(jnp.bfloat16)
    framed = flip(lowered) if ending else lowered
    rows, length, width = framed.shape
    size = width // TA_HEADS
    scale = size ** (-0.5)
    qkvg = matmul(framed, weights[(prefix, QKVG)])
    queries = qkvg[..., :width].astype(jnp.bfloat16).reshape(rows, length, TA_HEADS, size)
    keys = qkvg[..., width : 2 * width].astype(jnp.bfloat16).reshape(rows, length, TA_HEADS, size)
    values = (
        qkvg[..., 2 * width : 3 * width].astype(jnp.bfloat16).reshape(rows, length, TA_HEADS, size)
    )
    gate = qkvg[..., 3 * width :]
    local_bias = (
        matmul(framed, weights[(prefix, BIAS_PROJ)]).astype(jnp.bfloat16).transpose(2, 0, 1)
    )
    bias = lax.all_gather(local_bias, "row", axis=1, tiled=True)

    def forward_row(items):
        query, key, value = items
        scores = row_scores(query, key, bias, penalty, scale)
        top = jnp.max(scores, axis=-1, keepdims=True)
        shifted = jnp.exp(scores - top)
        total = jnp.sum(shifted, axis=-1, keepdims=True)
        probs = (shifted / total).astype(jnp.bfloat16)
        mixed = jnp.einsum("hjk,khd->jhd", probs, value, preferred_element_type=jnp.float32)
        return (mixed, top[..., 0] + jnp.log(total[..., 0]))

    mixed, log_totals = lax.map(forward_row, (queries, keys, values))
    mixed = mixed.reshape(rows, length, width)
    gated_low = gated_output(mixed, gate).astype(jnp.bfloat16)
    returned = flip(gated_low) if ending else gated_low
    update = matmul(returned, weights[(prefix, OUTPUT)])
    return (update, (state, framed, queries, keys, values, gate, bias, mixed, log_totals, returned))


def attention_backward(saved, grad_update, penalty, weights, prefix, ending, grads):
    state, framed, queries, keys, values, gate, bias, mixed, log_totals, returned = saved
    rows, length, width = framed.shape
    size = width // TA_HEADS
    scale = size ** (-0.5)
    grad_low = grad_update.astype(jnp.bfloat16)
    grads[(prefix, OUTPUT)] = outer_sum(returned, grad_low)
    grad_gated = matmul(grad_low, weights[(prefix, OUTPUT)].T)
    if ending:
        grad_gated = flip(grad_gated.astype(jnp.bfloat16)).astype(jnp.float32)
    _, pullback = jax.vjp(gated_output, mixed, gate)
    grad_mixed, grad_gate = pullback(grad_gated)
    grad_mixed = grad_mixed.astype(jnp.bfloat16).reshape(rows, length, TA_HEADS, size)

    def back_row(carry, items):
        query, key, value, log_total, grad_row = items
        scores = row_scores(query, key, bias, penalty, scale)
        probs = jnp.exp(scores - log_total[..., None])
        grad_probs = jnp.einsum("jhd,khd->hjk", grad_row, value, preferred_element_type=jnp.float32)
        delta = jnp.sum(probs * grad_probs, axis=-1, keepdims=True)
        grad_scores = (probs * (grad_probs - delta)).astype(jnp.bfloat16)
        grad_query = (
            jnp.einsum("hjk,khd->jhd", grad_scores, key, preferred_element_type=jnp.float32) * scale
        )
        grad_key = (
            jnp.einsum("hjk,jhd->khd", grad_scores, query, preferred_element_type=jnp.float32)
            * scale
        )
        grad_value = jnp.einsum(
            "hjk,jhd->khd", probs.astype(jnp.bfloat16), grad_row, preferred_element_type=jnp.float32
        )
        return (carry + grad_scores.astype(jnp.float32), (grad_query, grad_key, grad_value))

    empty = jnp.zeros(bias.shape, jnp.float32)
    grad_bias, (grad_query, grad_key, grad_value) = lax.scan(
        back_row, empty, (queries, keys, values, log_totals, grad_mixed)
    )
    grad_bias = lax.psum_scatter(grad_bias, "row", scatter_dimension=1, tiled=True)
    grad_bias = grad_bias.transpose(1, 2, 0).astype(jnp.bfloat16)
    grad_qkvg = jnp.concatenate(
        [
            grad_query.reshape(rows, length, width),
            grad_key.reshape(rows, length, width),
            grad_value.reshape(rows, length, width),
            grad_gate,
        ],
        axis=-1,
    ).astype(jnp.bfloat16)
    grads[(prefix, QKVG)] = outer_sum(framed, grad_qkvg)
    grads[(prefix, BIAS_PROJ)] = outer_sum(framed, grad_bias)
    grad_framed = matmul(grad_qkvg, weights[(prefix, QKVG)].T) + matmul(
        grad_bias, weights[(prefix, BIAS_PROJ)].T
    )
    if ending:
        grad_framed = flip(grad_framed.astype(jnp.bfloat16)).astype(jnp.float32)
    gain, shift = norm_pair(weights, prefix)
    grad_state, grads[(prefix, NORM_GAIN)], grads[(prefix, NORM_BIAS)] = norm_backward(
        state, gain, shift, grad_framed
    )
    return grad_state


def transition_forward(state, weights, prefix):
    gain, shift = norm_pair(weights, prefix)
    lowered = layer_norm(state, gain, shift).astype(jnp.bfloat16)
    hidden = matmul(lowered, weights[(prefix, UP)])
    mixed_low = swiglu(hidden).astype(jnp.bfloat16)
    update = matmul(mixed_low, weights[(prefix, DOWN)])
    return (update, (state, lowered, hidden, mixed_low))


def transition_backward(saved, grad_update, weights, prefix, grads):
    state, lowered, hidden, mixed_low = saved
    grad_low = grad_update.astype(jnp.bfloat16)
    grads[(prefix, DOWN)] = outer_sum(mixed_low, grad_low)
    grad_mixed = matmul(grad_low, weights[(prefix, DOWN)].T)
    _, pullback = jax.vjp(swiglu, hidden)
    (grad_hidden,) = pullback(grad_mixed)
    grad_hidden = grad_hidden.astype(jnp.bfloat16)
    grads[(prefix, UP)] = outer_sum(lowered, grad_hidden)
    grad_lowered = matmul(grad_hidden, weights[(prefix, UP)].T)
    gain, shift = norm_pair(weights, prefix)
    grad_state, grads[(prefix, NORM_GAIN)], grads[(prefix, NORM_BIAS)] = norm_backward(
        state, gain, shift, grad_lowered
    )
    return grad_state


def single_forward(single_state, pair_state, penalty, weights):
    gain, shift = norm_pair(weights, ATTEND)
    lowered = layer_norm(single_state, gain, shift).astype(jnp.bfloat16)
    rows, width = lowered.shape
    size = width // SA_HEADS
    qkvg = matmul(lowered, weights[(ATTEND, QKVG)])
    query = qkvg[:, :width].astype(jnp.bfloat16).reshape(rows, SA_HEADS, size)
    key = qkvg[:, width : 2 * width].astype(jnp.bfloat16)
    value = qkvg[:, 2 * width : 3 * width].astype(jnp.bfloat16)
    gate = qkvg[:, 3 * width :]
    keys_all, values_all = (
        lax.all_gather(key, "row", axis=0, tiled=True),
        lax.all_gather(value, "row", axis=0, tiled=True),
    )
    keys_all = keys_all.reshape(-1, SA_HEADS, size)
    values_all = values_all.reshape(-1, SA_HEADS, size)
    pair_gain = weights[(ATTEND, PAIR_GAIN)].astype(jnp.float32)
    pair_shift = weights[(ATTEND, PAIR_BIAS)].astype(jnp.float32)
    pair_low = layer_norm(pair_state, pair_gain, pair_shift).astype(jnp.bfloat16)
    bias = matmul(pair_low, weights[(ATTEND, PAIR_PROJ)]).transpose(2, 0, 1)
    scores = jnp.einsum(
        "ihd,jhd->hij", query, keys_all, preferred_element_type=jnp.float32
    ) * size ** (-0.5)
    scores = scores + bias + penalty[None, None, :]
    probs = jax.nn.softmax(scores, axis=-1)
    probs_low = probs.astype(jnp.bfloat16)
    mixed = jnp.einsum(
        "hij,jhd->ihd", probs_low, values_all, preferred_element_type=jnp.float32
    ).reshape(rows, width)
    gated_low = gated_output(mixed, gate).astype(jnp.bfloat16)
    update = matmul(gated_low, weights[(ATTEND, OUTPUT)])
    return (
        update,
        (
            single_state,
            pair_state,
            lowered,
            query,
            keys_all,
            values_all,
            gate,
            pair_low,
            probs,
            probs_low,
            mixed,
            gated_low,
        ),
    )


def single_backward(saved, grad_update, weights, grads):
    (
        single_state,
        pair_state,
        lowered,
        query,
        keys_all,
        values_all,
        gate,
        pair_low,
        probs,
        probs_low,
        mixed,
        gated_low,
    ) = saved
    rows, width = lowered.shape
    size = width // SA_HEADS
    scale = size ** (-0.5)
    grad_low = grad_update.astype(jnp.bfloat16)
    grads[(ATTEND, OUTPUT)] = outer_sum(gated_low, grad_low)
    grad_gated = matmul(grad_low, weights[(ATTEND, OUTPUT)].T)
    _, pullback = jax.vjp(gated_output, mixed, gate)
    grad_mixed, grad_gate = pullback(grad_gated)
    grad_mixed = grad_mixed.astype(jnp.bfloat16).reshape(rows, SA_HEADS, size)
    grad_probs = jnp.einsum(
        "ihd,jhd->hij", grad_mixed, values_all, preferred_element_type=jnp.float32
    )
    delta = jnp.sum(probs * grad_probs, axis=-1, keepdims=True)
    grad_scores = (probs * (grad_probs - delta)).astype(jnp.bfloat16)
    grad_query = (
        jnp.einsum("hij,jhd->ihd", grad_scores, keys_all, preferred_element_type=jnp.float32)
        * scale
    )
    key_part = (
        jnp.einsum("hij,ihd->jhd", grad_scores, query, preferred_element_type=jnp.float32) * scale
    )
    value_part = jnp.einsum(
        "hij,ihd->jhd", probs_low, grad_mixed, preferred_element_type=jnp.float32
    )
    grad_key, grad_value = (
        lax.psum_scatter(key_part.reshape(-1, width), "row", scatter_dimension=0, tiled=True),
        lax.psum_scatter(value_part.reshape(-1, width), "row", scatter_dimension=0, tiled=True),
    )
    grad_qkvg = jnp.concatenate(
        [grad_query.reshape(rows, width), grad_key, grad_value, grad_gate], axis=-1
    ).astype(jnp.bfloat16)
    grads[(ATTEND, QKVG)] = outer_sum(lowered, grad_qkvg)
    grad_lowered = matmul(grad_qkvg, weights[(ATTEND, QKVG)].T)
    gain, shift = norm_pair(weights, ATTEND)
    grad_single, grads[(ATTEND, NORM_GAIN)], grads[(ATTEND, NORM_BIAS)] = norm_backward(
        single_state, gain, shift, grad_lowered
    )
    grad_bias = grad_scores.transpose(1, 2, 0)
    grads[(ATTEND, PAIR_PROJ)] = outer_sum(pair_low, grad_bias)
    grad_pair_low = matmul(grad_bias, weights[(ATTEND, PAIR_PROJ)].T)
    pair_gain = weights[(ATTEND, PAIR_GAIN)].astype(jnp.float32)
    pair_shift = weights[(ATTEND, PAIR_BIAS)].astype(jnp.float32)
    grad_pair, grads[(ATTEND, PAIR_GAIN)], grads[(ATTEND, PAIR_BIAS)] = norm_backward(
        pair_state, pair_gain, pair_shift, grad_pair_low
    )
    return (grad_single, grad_pair)


def shards(pair, single, lengths, params, moment_one, moment_two, pair_cotangent, single_cotangent):
    entries = layout(C, H, S, TA_HEADS, SA_HEADS)
    full = lax.all_gather(params.astype(jnp.bfloat16), "row", axis=0, tiled=True)
    weights = unpack(logical_order(full), entries)
    rows = pair.shape[1]
    length = pair.shape[2]
    first_row = lax.axis_index("row") * rows
    mask = (jnp.arange(length, dtype=jnp.int32) < lengths[0]).astype(jnp.float32)
    mask_rows = lax.dynamic_slice_in_dim(mask, first_row, rows)
    pair_mask = mask_rows[:, None] * mask[None, :]
    penalty = (mask - 1.0) * MASKED
    state = pair[0].astype(jnp.float32)
    saved = {}
    for prefix, incoming in ((OUTGOING, False), (INCOMING, True)):
        update, saved[prefix] = triangle_forward(state, pair_mask, weights, prefix, incoming)
        state = state + update
    for prefix, ending in ((STARTING, False), (ENDING, True)):
        update, saved[prefix] = attention_forward(state, penalty, weights, prefix, ending)
        state = state + update
    update, saved[PAIR] = transition_forward(state, weights, PAIR)
    pair_final = state + update
    single_state = single[0].astype(jnp.float32)
    update, saved[ATTEND] = single_forward(single_state, pair_final, penalty, weights)
    single_mid = single_state + update
    update, saved[SINGLE] = transition_forward(single_mid, weights, SINGLE)
    single_final = single_mid + update
    grads = {}
    grad_single = single_cotangent[0].astype(jnp.float32)
    grad_single = grad_single + transition_backward(
        saved[SINGLE], grad_single, weights, SINGLE, grads
    )
    from_single, from_pair = single_backward(saved[ATTEND], grad_single, weights, grads)
    grad_single = grad_single + from_single
    grad_pair = pair_cotangent[0].astype(jnp.float32) + from_pair
    grad_pair = grad_pair + transition_backward(saved[PAIR], grad_pair, weights, PAIR, grads)
    for prefix, ending in ((ENDING, True), (STARTING, False)):
        grad_pair = grad_pair + attention_backward(
            saved[prefix], grad_pair, penalty, weights, prefix, ending, grads
        )
    for prefix, incoming in ((INCOMING, True), (OUTGOING, False)):
        grad_pair = grad_pair + triangle_backward(
            saved[prefix], grad_pair, pair_mask, weights, prefix, incoming, grads
        )
    flat = stored_order(jnp.concatenate([grads[name].reshape(-1) for name, shape in entries]))
    shard_size = params.shape[0]
    row_index = lax.axis_index("row")
    total = lax.psum(flat, ("crop", "row"))
    shard = lax.dynamic_slice_in_dim(total, row_index * shard_size, shard_size)
    norm_squared = jnp.sum(total * total)
    clip_norm = jnp.sqrt(norm_squared)
    clipped = shard * (CLIP / jnp.maximum(clip_norm, CLIP))
    new_first = BETA_ONE * moment_one + (1.0 - BETA_ONE) * clipped
    new_second = BETA_TWO * moment_two + (1.0 - BETA_TWO) * clipped * clipped
    rates, decays = rate_tables(entries)
    rate_shard = lax.dynamic_slice_in_dim(jnp.asarray(rates), row_index * shard_size, shard_size)
    decay_shard = lax.dynamic_slice_in_dim(jnp.asarray(decays), row_index * shard_size, shard_size)
    first_hat = new_first / (1.0 - BETA_ONE**STEP)
    second_hat = new_second / (1.0 - BETA_TWO**STEP)
    new_params = params - rate_shard * (
        first_hat / (jnp.sqrt(second_hat) + ADAM_EPS) + decay_shard * params
    )
    return (
        pair_final.astype(jnp.bfloat16)[None],
        single_final.astype(jnp.bfloat16)[None],
        grad_pair[None],
        grad_single[None],
        new_params,
        new_first,
        new_second,
        clip_norm,
    )


F32 = jnp.float32
BF16 = jnp.bfloat16
LOG2E = 1.4426950408889634
VMEM_LIMIT = 56 * 1024 * 1024


def mm(left, right):
    return lax.dot_general(left, right, (((1,), (0,)), ((), ())), preferred_element_type=F32)


def mm_nt(left, right):
    return lax.dot_general(left, right, (((1,), (1,)), ((), ())), preferred_element_type=F32)


def mm_tn(left, right):
    return lax.dot_general(left, right, (((0,), (0,)), ((), ())), preferred_element_type=F32)


def standardize(values):
    centred = values - jnp.mean(values, axis=0, keepdims=True)
    spread = jnp.mean(centred * centred, axis=0, keepdims=True)
    inverse = lax.rsqrt(spread + EPSILON)
    return centred * inverse, inverse


def standardize_back(unit, inverse, grad_unit):
    first = jnp.mean(grad_unit, axis=0, keepdims=True)
    second = jnp.mean(grad_unit * unit, axis=0, keepdims=True)
    return inverse * (grad_unit - first - unit * second)


def sigmoid(values):
    return 0.5 * jnp.tanh(0.5 * values) + 0.5


def column(ref, index):
    return ref[:, index : index + 1]


def live_pair(info, alive, row):
    return jnp.concatenate(
        [jnp.where(info[row + place] > 0, alive[0:1], 0.0) for place in range(GROUP)], axis=1
    )


GROUP = 4
LAG = 4


def each_group(count, body):
    def step(index, carry):
        body(index * GROUP)
        return carry

    lax.fori_loop(0, count // GROUP, step, 0)


def each_channel(count, body):
    def step(index, carry):
        body(index)
        return carry

    lax.fori_loop(0, count, step, 0)


def join(read, ref, row):
    return jnp.concatenate([read(ref, row + place) for place in range(GROUP)], axis=1)


def pieces_of(values):
    length = values.shape[1] // GROUP
    return [values[:, place * length : (place + 1) * length] for place in range(GROUP)]


def put_rows(ref, row, values):
    for place, part in enumerate(pieces_of(values)):
        ref[row + place] = part.astype(ref.dtype)


def put_inner(scratch, row, values):
    for place, part in enumerate(pieces_of(values)):
        scratch[:, row + place, :] = part


def read_inner(scratch, row):
    return scratch[:, row, :]


def put_turned(scratch, row, values):
    for place, part in enumerate(pieces_of(values)):
        scratch[:, row + place, :] = part.T


def add_lanes(ref, values):
    ref[...] += sum(pieces_of(values))


def spec_full(shape):
    return pl.BlockSpec(shape, lambda step: (0,) * len(shape))


def cost(microseconds):
    return pl.CostEstimate(
        flops=int(microseconds * 1e9), bytes_accessed=int(microseconds * 3e6), transcendentals=0
    )


class Both(list):
    pass


def all_rows(ins, outs):
    extents = [shape[axis] for shape, dtype, axis in outs if axis is not None]
    for array, axis in ins:
        if isinstance(axis, int):
            extents += [member.shape[axis] for member in (array if isinstance(array, list) else [array])]
    return max(extents)


def run_rows(kernel, name, steps, ins, outs, scratch, time=15, half=None, before=None):
    grid = steps if half is None else steps // 2
    offset = grid * (half or 0)
    flat = []
    groups = []
    for array, axis in ins:
        members = array if isinstance(array, Both) else [array]
        flat += [(member, axis) for member in members]
        groups.append((len(members), isinstance(array, Both)))
    full = all_rows(flat, outs)

    def spec(shape, axis):
        if axis is None:
            return spec_full(shape)
        size = full // steps
        first = offset if shape[axis] == full else 0
        sizes = tuple(size if place == axis else extent for place, extent in enumerate(shape))
        return pl.BlockSpec(
            sizes,
            lambda step: tuple(step + first if place == axis else 0 for place in range(len(shape))),
        )

    in_specs = [
        pl.BlockSpec(memory_space=pltpu.SMEM) if axis == "smem" else spec(array.shape, axis)
        for array, axis in flat
    ]
    out_specs = [spec(shape, axis) for shape, dtype, axis in outs]
    arrays = [array for array, axis in flat]
    aliases = {}
    kept = []
    for place, (shape, dtype, axis) in enumerate(outs):
        if before is not None and (axis is None or shape[axis] == full):
            aliases[len(arrays)] = place
            kept.append(place)
            arrays.append(before[place])
            in_specs.append(spec_full(shape) if axis is None else pl.BlockSpec(memory_space=pl.ANY))

    def run(*refs):
        taken = iter(refs)
        given = []
        for number, together in groups:
            members = [next(taken) for _ in range(number)]
            given.append(members if together else members[0])
        held = {place: next(taken) for place in kept}
        results = [next(taken) for _ in outs]

        @pl.when(pl.program_id(0) == 0)
        def _():
            for place, (shape, dtype, axis) in enumerate(outs):
                if axis is None:
                    results[place][...] = (
                        held[place][...] if place in held else jnp.zeros(shape, dtype)
                    )

        kernel(*given, *results, *taken)

    return pl.pallas_call(
        run,
        grid=(grid,),
        in_specs=in_specs,
        out_specs=out_specs,
        out_shape=[jax.ShapeDtypeStruct(shape, dtype) for shape, dtype, axis in outs],
        scratch_shapes=[pltpu.VMEM(shape, dtype) for shape, dtype in scratch],
        input_output_aliases=aliases,
        compiler_params=pltpu.CompilerParams(vmem_limit_bytes=VMEM_LIMIT),
        cost_estimate=cost(time if half is None else time / 2),
        name=name,
    )(*arrays)


def run_halves(kernel, name, steps, ins, outs, scratch, time=15):
    results = []
    for half in range(2):
        chosen = [
            (array[half] if type(array) is list else array, axis) for array, axis in ins
        ]
        before = results[0] if half else None
        results.append(run_rows(kernel, name, steps, chosen, outs, scratch, time, half, before))
    full = all_rows(ins, outs)
    return [
        [results[0][place], results[1][place]]
        if axis is not None and shape[axis] != full
        else results[1][place]
        for place, (shape, dtype, axis) in enumerate(outs)
    ]


def zero_first(*refs):
    @pl.when(pl.program_id(0) == 0)
    def _():
        for ref in refs:
            ref[...] = jnp.zeros(ref.shape, ref.dtype)


def lane_sums(ref):
    return jnp.sum(ref[...].T, axis=0, keepdims=True)


def on_last(body):
    @pl.when(pl.program_id(0) == pl.num_programs(0) - 1)
    def _():
        body()


def read_plain(ref, row):
    return ref[row].astype(F32)


def reorder(values, order):
    size = values.shape[0] // len(order)
    return jnp.concatenate([values[place * size : (place + 1) * size] for place in order], axis=0)


def read_tokens(order, ref, row):
    return reorder(ref[row].astype(F32), order).T


def read_flipped(refs, row):
    parts = jnp.concatenate([ref[:, row] for ref in refs], axis=1)
    return parts.reshape(-1, parts.shape[-1]).astype(F32).T


def read_turned(order, ref, row):
    parts = ref[:, row]
    return reorder(parts.reshape(-1, parts.shape[-1]).astype(F32), order).T


def tri_pre_row(info, alive, row, state, cols, first, proj_t):
    unit, inverse = standardize(state)
    lowered = (unit * column(cols, first) + column(cols, first + 1)).astype(BF16)
    project = mm(proj_t[...], lowered)
    half = project.shape[0] // 2
    return project[:half] * sigmoid(project[half:]) * live_pair(info, alive, row)


def store_product(out, scratch, devices):
    hidden = scratch.shape[0] // 2
    part = hidden // devices

    def one(device, carry):
        out[device, 0] = scratch[pl.ds(device * part, part)].astype(BF16)
        out[device, 1] = scratch[pl.ds(hidden + device * part, part)].astype(BF16)
        return carry

    lax.fori_loop(0, devices, one, 0)


def copy_blocks(target, source, count):
    def one(index, carry):
        target[index] = source[index].astype(target.dtype)
        return carry

    lax.fori_loop(0, count, one, 0)


def store_flipped(out, scratch):
    devices, part = out.shape[0], out.shape[1]

    def one(device, carry):
        out[device] = scratch[pl.ds(device * part, part)].astype(out.dtype)
        return carry

    lax.fori_loop(0, devices, one, 0)


def tri_post_row(state, tri, cols, proj_t, gate_t):
    unit, inverse = standardize(state)
    lowered = (unit * column(cols, 0) + column(cols, 1)).astype(BF16)
    tri_unit, tri_inverse = standardize(tri)
    out_low = (tri_unit * column(cols, 2) + column(cols, 3)).astype(BF16)
    output = mm(proj_t[...], out_low)
    gate = sigmoid(mm(gate_t[...], lowered))
    return unit, inverse, lowered, tri_unit, tri_inverse, out_low, output, gate


def row_base(rows):
    return pl.program_id(0) * rows


def tri_pre_first_kernel(devices, read, info, alive, pair, cols, proj_t, out, scratch):
    rows = pair.shape[0]

    def body(row):
        product = tri_pre_row(
            info, alive, row_base(rows) + row, join(read, pair, row), cols, 0, proj_t
        )
        put_inner(scratch, row, product)

    each_group(rows, body)
    store_product(out, scratch, devices)


def whole_rows(refs, *place):
    parts = jnp.concatenate([ref[(slice(None),) + place] for ref in refs], axis=1)
    return parts.reshape(-1, parts.shape[-1])


def split_rows(values, outs, *place):
    part = outs[0].shape[-2]
    parts = values.astype(BF16).reshape(outs[0].shape[0], -1, values.shape[-1])
    for half, out in enumerate(outs):
        out[(slice(None),) + place] = parts[:, half * part : (half + 1) * part]


def tri_product_kernel(incoming, operands, *outs):
    def body(channel):
        first = whole_rows(operands, 0, channel)
        second = whole_rows(operands, 1, channel)
        tri = mm_tn(first, second) if incoming else mm_nt(first, second)
        split_rows(tri, outs, channel)

    each_channel(operands[0].shape[2], body)


def tri_join_kernel(
    devices, read, info, alive, source, tri_in, cols, proj_t, gate_t, next_cols, next_proj_t,
    state_out, out, tri_scratch, scratch,
):
    rows = state_out.shape[0]
    copy_blocks(tri_scratch, tri_in, tri_in.shape[0])

    def body(row):
        state = join(read, source, row)
        pieces = tri_post_row(state, join(read_inner, tri_scratch, row), cols, proj_t, gate_t)
        state = state + pieces[6] * pieces[7]
        put_rows(state_out, row, state)
        product = tri_pre_row(
            info, alive, row_base(rows) + row, state, next_cols, 0, next_proj_t
        )
        put_inner(scratch, row, product)

    each_group(rows, body)
    store_product(out, scratch, devices)


def tri_last_kernel(
    source, tri_in, cols, proj_t, gate_t, next_cols, bias_t, state_out, bias_out, tri_scratch, scratch
):
    rows = state_out.shape[0]
    copy_blocks(tri_scratch, tri_in, tri_in.shape[0])

    def body(row):
        state = join(read_plain, source, row)
        pieces = tri_post_row(state, join(read_inner, tri_scratch, row), cols, proj_t, gate_t)
        state = state + pieces[6] * pieces[7]
        put_rows(state_out, row, state)
        unit, inverse = standardize(state)
        lowered = (unit * column(next_cols, 0) + column(next_cols, 1)).astype(BF16)
        put_inner(scratch, row, mm(bias_t[...], lowered))

    each_group(rows, body)
    bias_out[...] = scratch[: bias_out.shape[0]].astype(BF16)


def flipped_bias_kernel(source, cols, bias_t, bias_out, scratch):
    rows = source[0].shape[1]

    def body(row):
        unit, inverse = standardize(join(read_flipped, source, row))
        lowered = (unit * column(cols, 0) + column(cols, 1)).astype(BF16)
        put_inner(scratch, row, mm(bias_t[...], lowered))

    each_group(rows, body)
    bias_out[...] = scratch[: bias_out.shape[0]].astype(BF16)


def fill_bias(alive, bias_in, table):
    @pl.when(pl.program_id(0) == 0)
    def _():
        length = table.shape[1]
        penalty = (alive[0:1] - 1.0) * (MASKED * LOG2E)
        for head in range(table.shape[0]):
            values = bias_in[:, head].reshape(length, length).astype(F32)
            table[head] = (values * LOG2E + penalty).T


def attention_row(state, cols, proj_t):
    unit, inverse = standardize(state)
    lowered = (unit * column(cols, 0) + column(cols, 1)).astype(BF16)
    project = mm(proj_t[...], lowered)
    width = project.shape[0] // 4
    size = width // TA_HEADS
    query = (project[:width] * (size**-0.5 * LOG2E)).astype(BF16)
    key = project[width : 2 * width].astype(BF16)
    value = project[2 * width : 3 * width].astype(BF16)
    gate = sigmoid(project[3 * width :])
    return unit, inverse, lowered, query, key, value, gate


def in_stages(blocks, first, second, third):
    early, late, done = {}, {}, {}
    count = len(blocks)
    for step in range(count + 2 * LAG):
        if step < count:
            early[step] = first(*blocks[step])
        if 0 <= step - LAG < count:
            late[step - LAG] = second(*blocks[step - LAG], early.pop(step - LAG))
        if 0 <= step - 2 * LAG < count:
            place = step - 2 * LAG
            done[blocks[place]] = third(*blocks[place], late.pop(place))
    return done


def head_rows(values, place, head):
    size, length = values.shape[0] // TA_HEADS, values.shape[1] // GROUP
    return values[head * size : (head + 1) * size, place * length : (place + 1) * length]


def gather_heads(done):
    return jnp.concatenate(
        [
            jnp.concatenate([done[place, head] for head in range(TA_HEADS)], axis=0)
            for place in range(GROUP)
        ],
        axis=1,
    )


ROW_BLOCKS = [(place, head) for place in range(GROUP) for head in range(TA_HEADS)]
HEAD_BLOCKS = [(place, head) for head in range(TA_HEADS) for place in range(GROUP)]


def attend_rows(state, row, cols, proj_t, output_t, table, totals, mixed_out):
    unit, inverse, lowered, query, key, value, gate = attention_row(state, cols, proj_t)

    def score(place, head):
        return mm_tn(head_rows(key, place, head), head_rows(query, place, head)) + table[head]

    def shift(place, head, scores):
        top = jnp.max(scores, axis=0, keepdims=True)
        return top, jnp.exp2(scores - top).astype(BF16)

    def mix(place, head, items):
        top, shifted = items
        values = head_rows(value, place, head)
        size = values.shape[0]
        values = jnp.concatenate([values, jnp.ones((16, values.shape[1]), BF16)], axis=0)
        result = mm(values, shifted)
        total = result[size : size + 1]
        return result[:size] / total, top + jnp.log2(total)

    done = in_stages(ROW_BLOCKS, score, shift, mix)
    mixed = gather_heads({block: items[0] for block, items in done.items()})
    put_rows(totals, row, gather_heads({block: items[1] for block, items in done.items()}))
    put_rows(mixed_out, row, mixed)
    return state + mm(output_t[...], (mixed * gate).astype(BF16))


def starting_kernel(
    alive, source, bias_in, cols, proj_t, output_t, out, totals, mixed, table, scratch
):
    fill_bias(alive, bias_in, table)
    rows = source.shape[0]

    def body(row):
        state = attend_rows(
            join(read_plain, source, row), row, cols, proj_t, output_t, table, totals, mixed
        )
        put_turned(scratch, row, state)

    each_group(rows, body)
    store_flipped(out, scratch)


def ending_kernel(alive, source, bias_in, cols, proj_t, output_t, out, totals, mixed, table):
    fill_bias(alive, bias_in, table)
    rows = source[0].shape[1]

    def body(row):
        state = attend_rows(
            join(read_flipped, source, row), row, cols, proj_t, output_t, table, totals, mixed
        )
        put_rows(out, row, state)

    each_group(rows, body)


def transition_kernel(
    order, source, cols, up_t, down_t, next_cols, bias_t, state_out, pair_out, bias_out, scratch, bias_scratch
):
    rows = source.shape[0]

    def body(row):
        state = join(read_plain, source, row)
        unit, inverse = standardize(state)
        lowered = (unit * column(cols, 0) + column(cols, 1)).astype(BF16)
        hidden = mm(up_t[...], lowered)
        half = hidden.shape[0] // 2
        first = hidden[:half]
        mixed = (first * sigmoid(first) * hidden[half:]).astype(BF16)
        state = state + mm(down_t[...], mixed)
        put_rows(state_out, row, state)
        put_turned(scratch, row, state)
        unit, inverse = standardize(state)
        lowered = (unit * column(next_cols, 0) + column(next_cols, 1)).astype(BF16)
        put_inner(bias_scratch, row, mm(bias_t[...], lowered))

    each_group(rows, body)
    size = pair_out.shape[0] // len(order)
    for place, held in enumerate(order):
        pair_out[place * size : (place + 1) * size] = scratch[held * size : (held + 1) * size].astype(BF16)
    bias_out[...] = bias_scratch[...].astype(BF16)


def transition_back_kernel(
    read, mid, final, cotangent, bias_grad, cols, up_t, up, down, next_cols, bias_w,
    grad_out, up_grad, down_grad, bias_w_grad, vecs, norm_gain, norm_bias, pair_gain, pair_bias, bias_scratch,
):
    zero_first(norm_gain, norm_bias, pair_gain, pair_bias)
    rows = mid.shape[0]
    bias_scratch[...] = bias_grad[...].astype(F32)

    def body(row):
        grad = join(read, cotangent, row)
        unit, inverse = standardize(join(read_plain, final, row))
        gain = column(next_cols, 0)
        lowered = (unit * gain + column(next_cols, 1)).astype(BF16)
        grad_bias = join(read_inner, bias_scratch, row).astype(BF16)
        bias_w_grad[...] += mm_nt(lowered, grad_bias)
        grad_lowered = mm(bias_w[...], grad_bias)
        add_lanes(pair_gain, grad_lowered * unit)
        add_lanes(pair_bias, grad_lowered)
        grad = grad + standardize_back(unit, inverse, grad_lowered * gain)
        unit, inverse = standardize(join(read_plain, mid, row))
        gain = column(cols, 0)
        lowered = (unit * gain + column(cols, 1)).astype(BF16)
        hidden = mm(up_t[...], lowered)
        half = hidden.shape[0] // 2
        first, second = hidden[:half], hidden[half:]
        slope = sigmoid(first)
        silu = first * slope
        grad_low = grad.astype(BF16)
        grad_mixed = mm(down[...], grad_low)
        down_grad[...] += mm_nt((silu * second).astype(BF16), grad_low)
        grad_hidden = jnp.concatenate(
            [
                (grad_mixed * second * (slope + silu * (1.0 - slope))).astype(BF16),
                (grad_mixed * silu).astype(BF16),
            ],
            axis=0,
        )
        up_grad[...] += mm_nt(lowered, grad_hidden)
        grad_lowered = mm(up[...], grad_hidden)
        add_lanes(norm_gain, grad_lowered * unit)
        add_lanes(norm_bias, grad_lowered)
        put_rows(grad_out, row, grad + standardize_back(unit, inverse, grad_lowered * gain))

    each_group(rows, body)

    def finish():
        vecs[0:1] += lane_sums(norm_gain)
        vecs[1:2] += lane_sums(norm_bias)
        vecs[2:3] += lane_sums(pair_gain)
        vecs[3:4] += lane_sums(pair_bias)

    on_last(finish)


def attention_back_kernel(
    read, read_grad, alive, source, grad_in, bias_in, totals, mixed_in, cols, proj_t, proj, output,
    grad_out, bias_out, proj_grad, output_grad, table, grad_table,
):
    fill_bias(alive, bias_in, table)
    zero_first(grad_table)
    rows = grad_out.shape[0]

    def body(row):
        unit, inverse, lowered, query, key, value, gate = attention_row(
            join(read, source, row), cols, proj_t
        )
        mixed = join(read_plain, mixed_in, row)
        total = join(read_plain, totals, row)
        grad_low = join(read_grad, grad_in, row).astype(BF16)
        gated = mixed * gate
        output_grad[...] += mm_nt(gated.astype(BF16), grad_low)
        grad_gated = mm(output[...], grad_low)
        grad_gate = grad_gated * gated * (1.0 - gate)
        grad_mixed = (grad_gated * gate).astype(BF16)
        product = grad_mixed.astype(F32) * mixed
        size = query.shape[0] // TA_HEADS

        def score(place, head):
            scores = mm_tn(head_rows(key, place, head), head_rows(query, place, head))
            grads = mm_tn(head_rows(value, place, head), head_rows(grad_mixed, place, head))
            return scores + table[head], grads

        def slope(place, head, items):
            scores, grads = items
            probs = jnp.exp2(scores - head_rows(total, place, head))
            delta = jnp.sum(head_rows(product, place, head), axis=0, keepdims=True)
            grad_scores = probs * (grads - delta)
            grad_table[head] += grad_scores
            return probs.astype(BF16), grad_scores.astype(BF16)

        def back(place, head, items):
            probs, grad_scores = items
            return (
                mm(head_rows(key, place, head), grad_scores) * size**-0.5,
                mm_nt(head_rows(query, place, head), grad_scores) * (1.0 / LOG2E),
                mm_nt(head_rows(grad_mixed, place, head), probs),
            )

        done = in_stages(HEAD_BLOCKS, score, slope, back)
        grad_project = jnp.concatenate(
            [
                gather_heads({block: items[part] for block, items in done.items()})
                for part in range(3)
            ]
            + [grad_gate],
            axis=0,
        ).astype(BF16)
        proj_grad[...] += mm_nt(lowered, grad_project)
        put_rows(grad_out, row, mm(proj[...], grad_project))

    each_group(rows, body)

    def finish():
        for head in range(TA_HEADS):
            bias_out[:, head] = (
                grad_table[head].T.astype(BF16).reshape(bias_out.shape[0], bias_out.shape[2], -1)
            )

    on_last(finish)


def attention_end_row(
    state, grad, grad_lowered, grad_bias, cols, bias_w, bias_w_grad, norm_gain, norm_bias
):
    unit, inverse = standardize(state)
    gain = column(cols, 0)
    lowered = (unit * gain + column(cols, 1)).astype(BF16)
    bias_w_grad[...] += mm_nt(lowered, grad_bias)
    grad_lowered = grad_lowered + mm(bias_w[...], grad_bias)
    add_lanes(norm_gain, grad_lowered * unit)
    add_lanes(norm_bias, grad_lowered)
    return grad + standardize_back(unit, inverse, grad_lowered * gain)


def fill_bias_grad(scratch, bias_grad):
    heads = bias_grad.shape[1]
    total = bias_grad[0].astype(F32)
    for device in range(1, bias_grad.shape[0]):
        total = total + bias_grad[device].astype(F32)
    scratch[:heads] = total
    scratch[heads:] = jnp.zeros((scratch.shape[0] - heads,) + scratch.shape[1:], F32)


def ending_end_kernel(
    source, grad_in, grad_lowered, bias_grad, cols, bias_w,
    grad_out, bias_w_grad, vecs, norm_gain, norm_bias, bias_scratch, scratch,
):
    zero_first(norm_gain, norm_bias)
    fill_bias_grad(bias_scratch, bias_grad)
    rows = grad_in.shape[0]

    def body(row):
        grad = attention_end_row(
            join(read_flipped, source, row), join(read_plain, grad_in, row),
            join(read_plain, grad_lowered, row), join(read_inner, bias_scratch, row).astype(BF16), cols, bias_w, bias_w_grad, norm_gain, norm_bias,
        )
        put_turned(scratch, row, grad)

    each_group(rows, body)
    store_flipped(grad_out, scratch)

    def finish():
        vecs[0:1] += lane_sums(norm_gain)
        vecs[1:2] += lane_sums(norm_bias)

    on_last(finish)


def tri_post_back_row(
    state, tri, grad, cols, proj_t, gate_t, proj, gate_w, proj_grad, gate_grad, out_gain, out_bias
):
    unit, inverse, lowered, tri_unit, tri_inverse, out_low, output, gate = tri_post_row(
        state, tri, cols, proj_t, gate_t
    )
    grad_output = grad * gate
    grad_gate = (grad_output * output * (1.0 - gate)).astype(BF16)
    grad_output = grad_output.astype(BF16)
    proj_grad[...] += mm_nt(out_low, grad_output)
    gate_grad[...] += mm_nt(lowered, grad_gate)
    grad_normed = mm(proj[...], grad_output)
    add_lanes(out_gain, grad_normed * tri_unit)
    add_lanes(out_bias, grad_normed)
    grad_tri = standardize_back(tri_unit, tri_inverse, grad_normed * column(cols, 2))
    return grad_tri, mm(gate_w[...], grad_gate)


def starting_end_kernel(
    source, grad_in, grad_lowered, bias_grad, cols, bias_w,
    below, tri_in, tri_cols, proj_t, gate_t, proj, gate_w,
    grad_out, tri_out, gate_back, bias_w_grad, proj_grad, gate_grad, vecs,
    norm_gain, norm_bias, out_gain, out_bias, bias_scratch, tri_scratch,
):
    zero_first(norm_gain, norm_bias, out_gain, out_bias)
    fill_bias_grad(bias_scratch, bias_grad)
    copy_blocks(tri_scratch, tri_in, tri_in.shape[0])
    rows = source.shape[0]

    def body(row):
        grad = attention_end_row(
            join(read_plain, source, row), join(read_flipped, grad_in, row),
            join(read_plain, grad_lowered, row), join(read_inner, bias_scratch, row).astype(BF16), cols, bias_w, bias_w_grad, norm_gain, norm_bias,
        )
        put_rows(grad_out, row, grad)
        grad_tri, back = tri_post_back_row(
            join(read_plain, below, row), join(read_inner, tri_scratch, row), grad, tri_cols, proj_t, gate_t, proj, gate_w,
            proj_grad, gate_grad, out_gain, out_bias,
        )
        put_rows(gate_back, row, back)
        put_inner(tri_scratch, row, grad_tri)

    each_group(rows, body)
    copy_blocks(tri_out, tri_scratch, tri_out.shape[0])

    def finish():
        vecs[0:1] += lane_sums(norm_gain)
        vecs[1:2] += lane_sums(norm_bias)
        vecs[2:3] += lane_sums(out_gain)
        vecs[3:4] += lane_sums(out_bias)

    on_last(finish)


def tri_product_back_kernel(incoming, grad, operands, *outs):
    def body(channel):
        first = whole_rows(operands, 0, channel)
        second = whole_rows(operands, 1, channel)
        tri = whole_rows(grad, channel)
        if incoming:
            grad_first = mm_nt(second, tri)
            grad_second = mm(first, tri)
        else:
            grad_first = mm(tri, second)
            grad_second = mm_tn(tri, first)
        split_rows(grad_first, outs, 0, channel)
        split_rows(grad_second, outs, 1, channel)

    each_channel(operands[0].shape[2], body)


def tri_pre_back_row(
    info, alive, row, state, product_grad, gate_back, grad, cols, proj_t, proj, proj_grad, norm_gain, norm_bias
):
    unit, inverse = standardize(state)
    gain = column(cols, 0)
    lowered = (unit * gain + column(cols, 1)).astype(BF16)
    project = mm(proj_t[...], lowered)
    half = project.shape[0] // 2
    gate = sigmoid(project[half:])
    grad_first = product_grad * gate * live_pair(info, alive, row)
    grad_second = grad_first * project[:half] * (1.0 - gate)
    grad_project = jnp.concatenate([grad_first.astype(BF16), grad_second.astype(BF16)], axis=0)
    proj_grad[...] += mm_nt(lowered, grad_project)
    grad_lowered = mm(proj[...], grad_project) + gate_back
    add_lanes(norm_gain, grad_lowered * unit)
    add_lanes(norm_bias, grad_lowered)
    return grad + standardize_back(unit, inverse, grad_lowered * gain)


def fill_product_grad(scratch, product_grad):
    devices, part = product_grad.shape[0], product_grad.shape[2]

    def one(device, carry):
        scratch[pl.ds(device * part, part)] = product_grad[device, 0].astype(F32)
        scratch[pl.ds((devices + device) * part, part)] = product_grad[device, 1].astype(F32)
        return carry

    lax.fori_loop(0, devices, one, 0)


def tri_join_back_kernel(
    read, info, alive, source, product_grad, gate_in, grad_in, cols, proj_t, proj,
    below, tri_in, tri_cols, out_t, gate_t, out_w, gate_w,
    grad_out, tri_out, gate_back, proj_grad, out_grad, gate_grad, vecs,
    norm_gain, norm_bias, out_gain, out_bias, scratch, tri_scratch,
):
    zero_first(norm_gain, norm_bias, out_gain, out_bias)
    fill_product_grad(scratch, product_grad)
    copy_blocks(tri_scratch, tri_in, tri_in.shape[0])
    rows = source.shape[0]

    def body(row):
        grad = tri_pre_back_row(
            info, alive, row_base(rows) + row, join(read_plain, source, row),
            join(read_inner, scratch, row), join(read_plain, gate_in, row),
            join(read_plain, grad_in, row), cols, proj_t, proj, proj_grad, norm_gain, norm_bias,
        )
        put_rows(grad_out, row, grad)
        grad_tri, back = tri_post_back_row(
            join(read, below, row), join(read_inner, tri_scratch, row), grad, tri_cols, out_t, gate_t, out_w, gate_w,
            out_grad, gate_grad, out_gain, out_bias,
        )
        put_rows(gate_back, row, back)
        put_inner(tri_scratch, row, grad_tri)

    each_group(rows, body)
    copy_blocks(tri_out, tri_scratch, tri_out.shape[0])

    def finish():
        vecs[0:1] += lane_sums(norm_gain)
        vecs[1:2] += lane_sums(norm_bias)
        vecs[2:3] += lane_sums(out_gain)
        vecs[3:4] += lane_sums(out_bias)

    on_last(finish)


def tri_first_back_kernel(
    read, order, info, alive, source, product_grad, gate_in, grad_in, cols, proj_t, proj,
    grad_out, proj_grad, vecs, norm_gain, norm_bias, scratch,
):
    zero_first(norm_gain, norm_bias)
    fill_product_grad(scratch, product_grad)
    rows = source.shape[0]

    def body(row):
        grad = tri_pre_back_row(
            info, alive, row_base(rows) + row, join(read, source, row),
            join(read_inner, scratch, row), join(read_plain, gate_in, row),
            join(read_plain, grad_in, row), cols, proj_t, proj, proj_grad, norm_gain, norm_bias,
        )
        for place, part in enumerate(pieces_of(grad)):
            grad_out[row + place] = reorder(part.T, order).astype(grad_out.dtype)

    each_group(rows, body)

    def finish():
        vecs[0:1] += lane_sums(norm_gain)
        vecs[1:2] += lane_sums(norm_bias)

    on_last(finish)


RUN = 24


def table_of(entries):
    table = {}
    offset = 0
    for name, shape in entries:
        table[name] = (offset // STRIDE, shape)
        offset += math.prod(shape)
    return table, offset


def runs_kernel(info, shard, out, scratch):
    def one(block, carry):
        scratch[:, block, :] = shard[pl.ds(block * STRIDE, STRIDE), :].T
        return carry

    lax.fori_loop(0, RUN, one, 0)
    half = STRIDE // 2
    turn = info[0] * half

    def move(lane, carry):
        out[lane] = scratch[lax.rem(lane + turn, STRIDE)].astype(BF16)
        return carry

    lax.fori_loop(0, STRIDE, move, 0)


def run_place(shards, total, lane, shard):
    count = total // STRIDE
    whole = total // shards
    step, odd = whole // STRIDE, (whole % STRIDE) // (STRIDE // 2)
    extra = lax.div(shard * odd + jnp.where(lane < STRIDE // 2, 1, 0), 2)
    start = lane * count + shard * step + extra
    return lax.div(start, STRIDE), lax.rem(start, STRIDE)


def rows_from_runs(runs, rows, first_lane, total):
    shards, lanes = runs.shape[0], runs.shape[1]
    base = first_lane * (total // STRIDE) // STRIDE

    def one(index, carry):
        lane, shard = lax.div(index, shards), lax.rem(index, shards)
        row, shift = run_place(shards, total, first_lane + lane, shard)
        row = row - base
        turned = pltpu.roll(runs[shard, lane].astype(F32), shift, 1)
        place = lax.broadcasted_iota(jnp.int32, (RUN + 1, STRIDE), 1)
        last, before = carry
        joint = jnp.where(row - before == RUN, last[2:3], last[1:2])
        below = jnp.concatenate([joint, turned], axis=0)
        above = jnp.concatenate([turned, turned[RUN - 1 :]], axis=0)
        values = jnp.where(place < shift, below, above)
        rows[pl.ds(row, RUN + 1), :] = values
        return values[RUN - 2 :], row

    lax.fori_loop(0, shards * lanes, one, (jnp.zeros((3, STRIDE), F32), -RUN), unroll=4)


def runs_from_rows(rows, out, first_lane, base, total):
    shards, lanes = out.shape[0], out.shape[1]

    def one(index, carry):
        lane, shard = lax.div(index, shards), lax.rem(index, shards)
        row, shift = run_place(shards, total, first_lane + lane, shard)
        turned = pltpu.roll(rows[pl.ds(row - base, RUN + 1), :], (STRIDE - shift) % STRIDE, 1)
        place = lax.broadcasted_iota(jnp.int32, (RUN, STRIDE), 1)
        out[shard, lane] = jnp.where(
            place < STRIDE - shift, turned[:RUN], turned[1:]
        ).astype(BF16)
        return carry

    lax.fori_loop(0, shards * lanes, one, 0, unroll=4)


def row_height(base, first_lane, last_lane, total):
    end = (last_lane * (total // STRIDE)) // STRIDE + RUN + 2
    return -(-(end - base) // 8) * 8


def take_matrix(rows, first, shape):
    blocks = shape[1] // STRIDE
    return [
        rows[pl.ds(first + block, shape[0], stride=blocks), :]
        if blocks > 1
        else rows[first : first + shape[0], :]
        for block in range(blocks)
    ]


def put_matrix(rows, first, matrix):
    height, width = matrix.shape
    blocks = width // STRIDE
    for block in range(blocks):
        part = matrix[:, block * STRIDE : (block + 1) * STRIDE]
        if blocks > 1:
            rows[pl.ds(first + block, height, stride=blocks), :] = part
        else:
            rows[first : first + height, :] = part


def spread(index, heads, rows):
    lane = lax.broadcasted_iota(jnp.int32, (STRIDE, STRIDE), 0)
    channel = lax.broadcasted_iota(jnp.int32, (STRIDE, STRIDE), 1)
    return (channel == index * (STRIDE // heads) + lane // heads).astype(BF16)


def take_narrow(rows, first, heads, high):
    total = jnp.zeros((high, STRIDE), F32)
    head = lax.broadcasted_iota(jnp.int32, (high, STRIDE), 0)
    lane = lax.broadcasted_iota(jnp.int32, (high, STRIDE), 1)
    for index in range(heads):
        line = rows[first + index : first + index + 1, :]
        picked = jnp.where(lane % heads == head, line, 0.0).astype(BF16)
        total = total + mm(picked, spread(index, heads, rows))
    return total


def put_narrow(rows, first, heads, matrix):
    turned = matrix.T.astype(BF16)
    high = turned.shape[0]
    head = lax.broadcasted_iota(jnp.int32, (high, STRIDE), 0)
    lane = lax.broadcasted_iota(jnp.int32, (high, STRIDE), 1)
    for index in range(heads):
        wide = mm_nt(turned, spread(index, heads, rows))
        rows[first + index : first + index + 1, :] = jnp.sum(
            jnp.where(lane % heads == head, wide, 0.0), axis=0, keepdims=True
        )


PAIR_MATRICES = (
    (OUTGOING, PROJ_GATE), (OUTGOING, PROJ_OUT), (OUTGOING, GATE_OUT),
    (INCOMING, PROJ_GATE), (INCOMING, PROJ_OUT), (INCOMING, GATE_OUT),
    (STARTING, QKVG), (STARTING, OUTPUT), (ENDING, QKVG), (ENDING, OUTPUT), (PAIR, UP), (PAIR, DOWN),
)
PAIR_COLUMNS = (
    (OUTGOING, ((OUTGOING, NORM_GAIN), (OUTGOING, NORM_BIAS), (OUTGOING, OUT_GAIN), (OUTGOING, OUT_BIAS))),
    (INCOMING, ((INCOMING, NORM_GAIN), (INCOMING, NORM_BIAS), (INCOMING, OUT_GAIN), (INCOMING, OUT_BIAS))),
    (STARTING, ((STARTING, NORM_GAIN), (STARTING, NORM_BIAS))),
    (ENDING, ((ENDING, NORM_GAIN), (ENDING, NORM_BIAS))),
    (PAIR, ((PAIR, NORM_GAIN), (PAIR, NORM_BIAS))),
)
SINGLE_MATRICES = ((ATTEND, QKVG), (ATTEND, OUTPUT), (SINGLE, UP), (SINGLE, DOWN))
SINGLE_VECTORS = ((ATTEND, NORM_GAIN), (ATTEND, NORM_BIAS), (SINGLE, NORM_GAIN), (SINGLE, NORM_BIAS))


def put_columns(rows, out, table, base, names):
    out[...] = jnp.zeros(out.shape, F32)
    lines = [rows[table[name][0] - base : table[name][0] - base + 1, :] for name in names]
    lines.append(jnp.zeros((8 - len(lines), STRIDE), F32))
    out[...] = jnp.concatenate(lines, axis=0).T


def unpack_pair_kernel(table, total, runs, *refs):
    rows = refs[-1]
    outs = list(refs[:-1])
    rows_from_runs(runs, rows, 0, total)
    for name in PAIR_MATRICES:
        first, shape = table[name]
        plain, turned = outs.pop(0), outs.pop(0)
        for block, part in enumerate(take_matrix(rows, first, shape)):
            place = slice(block * STRIDE, (block + 1) * STRIDE)
            plain[:, place] = part.astype(BF16)
            turned[place, :] = part.T.astype(BF16)
    for prefix in (STARTING, ENDING):
        plain, turned = outs.pop(0), outs.pop(0)
        first, shape = table[(prefix, BIAS_PROJ)]
        matrix = take_narrow(rows, first, shape[1], 8)
        turned[...] = matrix.astype(BF16)
        plain[...] = matrix.T.astype(BF16)
    for prefix, names in PAIR_COLUMNS:
        put_columns(rows, outs.pop(0), table, 0, names)


def unpack_single_kernel(table, total, first_lane, runs, *refs):
    rows = refs[-1]
    outs = list(refs[:-1])
    rows_from_runs(runs, rows, first_lane, total)
    base = first_lane * (total // STRIDE) // STRIDE
    for name in SINGLE_MATRICES:
        first, shape = table[name]
        out = outs.pop(0)
        for block, part in enumerate(take_matrix(rows, first - base, shape)):
            out[:, block * STRIDE : (block + 1) * STRIDE] = part.astype(BF16)
    first, shape = table[(ATTEND, PAIR_PROJ)]
    matrix = take_narrow(rows, first - base, shape[1], shape[1])
    plain, turned = outs.pop(0), outs.pop(0)
    turned[...] = matrix.astype(BF16)
    plain[...] = matrix.T.astype(BF16)
    put_columns(rows, outs.pop(0), table, base, ((ATTEND, PAIR_GAIN), (ATTEND, PAIR_BIAS)))
    lines = outs.pop(0)
    lines[...] = jnp.zeros(lines.shape, F32)
    for index, name in enumerate(SINGLE_VECTORS):
        first, shape = table[name]
        for block in range(shape[0] // STRIDE):
            lines[index : index + 1, block * STRIDE : (block + 1) * STRIDE] = rows[
                first - base + block : first - base + block + 1, :
            ]


def pack_kernel(table, total, first_lane, base, names, *refs):
    ins, out, rows = refs[: len(names)], refs[-2], refs[-1]
    for name, ref in zip(names, ins):
        if isinstance(name, tuple):
            first, shape = table[name]
            if shape[1] % STRIDE:
                put_narrow(rows, first - base, shape[1], ref[...])
            else:
                put_matrix(rows, first - base, ref)
        else:
            for index, vector in name:
                first, shape = table[vector]
                for block in range(shape[0] // STRIDE):
                    rows[first + block - base : first + block - base + 1, :] = ref[
                        index : index + 1, block * STRIDE : (block + 1) * STRIDE
                    ]
    runs_from_rows(rows, out, first_lane, base, total)


def shard_kernel(whole, info, runs, out, squares):
    half = STRIDE // 2
    squares[...] = jnp.zeros(squares.shape, F32)

    def one(block, carry):
        first = runs[pl.ds(info[0] * half, half), block, :]
        second = runs[pl.ds(half - info[0] * half, half), block, :]
        values = jnp.concatenate([first, second], axis=0).T
        row = block * STRIDE + lax.broadcasted_iota(jnp.int32, values.shape, 0)
        lane = lax.broadcasted_iota(jnp.int32, values.shape, 1)
        values = jnp.where(row * STRIDE + lane < whole, values, 0.0)
        out[pl.ds(block * STRIDE, STRIDE), :] = values
        squares[...] += jnp.sum((values * values).reshape(-1, 8, STRIDE), axis=0)
        return carry

    lax.fori_loop(0, RUN, one, 0)


def whole_call(kernel, name, ins, outs, scratch, time=8):
    def spec(axis):
        return pl.BlockSpec(memory_space=pltpu.SMEM if axis == "smem" else pltpu.VMEM)

    return pl.pallas_call(
        kernel,
        in_specs=[spec(axis) for array, axis in ins],
        out_specs=[pl.BlockSpec(memory_space=pltpu.VMEM) for shape, dtype in outs],
        out_shape=[jax.ShapeDtypeStruct(shape, dtype) for shape, dtype in outs],
        scratch_shapes=[pltpu.VMEM(shape, dtype) for shape, dtype in scratch],
        compiler_params=pltpu.CompilerParams(vmem_limit_bytes=VMEM_LIMIT),
        cost_estimate=cost(time),
        name=name,
    )(*[array for array, axis in ins])


def unpack_pair(table, total, runs):
    outs = []
    names = []
    for name in PAIR_MATRICES:
        shape = table[name][1]
        outs += [(shape, BF16), (shape[::-1], BF16)]
        names += [name, (name, T)]
    for prefix in (STARTING, ENDING):
        outs += [((STRIDE, 8), BF16), ((8, STRIDE), BF16)]
        names += [(prefix, BIAS_W), (prefix, BIAS_T)]
    for prefix, parts in PAIR_COLUMNS:
        outs.append(((STRIDE, 8), F32))
        names.append((prefix, COLS))
    height = row_height(0, 0, runs.shape[1], total)
    values = whole_call(
        functools.partial(unpack_pair_kernel, table, total), "pair_weights", [(runs, None)], outs,
        [((height, STRIDE), F32)],
    )
    return dict(zip(names, values))


def unpack_single(table, total, first_lane, runs):
    outs = [(table[name][1], BF16) for name in SINGLE_MATRICES]
    names = list(SINGLE_MATRICES)
    shape = table[(ATTEND, PAIR_PROJ)][1]
    outs += [(shape, BF16), (shape[::-1], BF16), ((STRIDE, 8), F32), ((8, S), F32)]
    names += [(ATTEND, PAIR_PROJ), ((ATTEND, PAIR_PROJ), T), (ATTEND, COLS), (SINGLE, VECTORS)]
    base = first_lane * (total // STRIDE) // STRIDE
    height = row_height(base, first_lane, first_lane + runs.shape[1], total)
    values = whole_call(
        functools.partial(unpack_single_kernel, table, total, first_lane), "single_weights",
        [(runs, None)], outs, [((height, STRIDE), F32)],
    )
    return dict(zip(names, values))


def pack(name, table, total, shards, lanes, base, parts):
    height = row_height(base, *lanes, total)
    for held, array in parts:
        if isinstance(held, tuple):
            end = table[held][0] - base + array.shape[0] * max(1, array.shape[1] // STRIDE)
            height = max(height, -(-end // 8) * 8)
    return whole_call(
        functools.partial(pack_kernel, table, total, lanes[0], base, [held for held, array in parts]),
        name, [(array, None) for held, array in parts],
        [((shards, lanes[1] - lanes[0], RUN, STRIDE), BF16)], [((height, STRIDE), F32)],
    )[0]


def swap(values, group):
    return lax.all_to_all(values, group, split_axis=0, concat_axis=0, tiled=True)


def single_project(single_state, weights, devices):
    gain, shift = norm_pair(weights, ATTEND)
    lowered = layer_norm(single_state, gain, shift).astype(BF16)
    width = lowered.shape[1]
    qkvg = matmul(lowered, weights[(ATTEND, QKVG)])
    both = qkvg[:, width : 3 * width].astype(BF16)
    both = jnp.broadcast_to(both[None], (devices,) + both.shape)
    return lowered, qkvg, both


def single_attend(single_state, projected, bias, penalty, weights):
    lowered, qkvg, both = projected
    rows, width = lowered.shape
    size = width // SA_HEADS
    query = qkvg[:, :width].astype(BF16).reshape(rows, SA_HEADS, size)
    gate = qkvg[:, 3 * width :]
    both = both.reshape(-1, 2 * width)
    keys_all = both[:, :width].reshape(-1, SA_HEADS, size)
    values_all = both[:, width:].reshape(-1, SA_HEADS, size)
    scores = jnp.einsum(
        "ihd,jhd->hij", query, keys_all, preferred_element_type=F32
    ) * size ** (-0.5)
    scores = scores + bias + penalty[None, None, :]
    probs = jax.nn.softmax(scores, axis=-1)
    probs_low = probs.astype(BF16)
    mixed = jnp.einsum("hij,jhd->ihd", probs_low, values_all, preferred_element_type=F32)
    mixed = mixed.reshape(rows, width)
    gated_low = gated_output(mixed, gate).astype(BF16)
    update = matmul(gated_low, weights[(ATTEND, OUTPUT)])
    return (
        update,
        (single_state, lowered, query, keys_all, values_all, gate, probs, probs_low, mixed, gated_low),
    )


def single_attend_back(saved, grad_update, weights, grads):
    single_state, lowered, query, keys_all, values_all, gate, probs, probs_low, mixed, gated_low = saved
    rows, width = lowered.shape
    size = width // SA_HEADS
    scale = size ** (-0.5)
    grad_low = grad_update.astype(BF16)
    grads[(ATTEND, OUTPUT)] = outer_sum(gated_low, grad_low)
    grad_gated = matmul(grad_low, weights[(ATTEND, OUTPUT)].T)
    _, pullback = jax.vjp(gated_output, mixed, gate)
    grad_mixed, grad_gate = pullback(grad_gated)
    grad_mixed = grad_mixed.astype(BF16).reshape(rows, SA_HEADS, size)
    grad_probs = jnp.einsum("ihd,jhd->hij", grad_mixed, values_all, preferred_element_type=F32)
    delta = jnp.sum(probs * grad_probs, axis=-1, keepdims=True)
    grad_scores = (probs * (grad_probs - delta)).astype(BF16)
    grad_query = (
        jnp.einsum("hij,jhd->ihd", grad_scores, keys_all, preferred_element_type=F32) * scale
    )
    key_part = jnp.einsum("hij,ihd->jhd", grad_scores, query, preferred_element_type=F32) * scale
    value_part = jnp.einsum("hij,ihd->jhd", probs_low, grad_mixed, preferred_element_type=F32)
    parts = jnp.concatenate(
        [key_part.reshape(-1, rows, width), value_part.reshape(-1, rows, width)], axis=-1
    )
    return grad_scores, (parts.astype(BF16), single_state, lowered, grad_query, grad_gate)


def single_attend_end(pending, parts, weights, grads):
    _, single_state, lowered, grad_query, grad_gate = pending
    rows, width = lowered.shape
    grad_both = jnp.sum(parts.astype(F32), axis=0)
    grad_qkvg = jnp.concatenate(
        [grad_query.reshape(rows, width), grad_both, grad_gate], axis=-1
    ).astype(BF16)
    grads[(ATTEND, QKVG)] = outer_sum(lowered, grad_qkvg)
    grad_lowered = matmul(grad_qkvg, weights[(ATTEND, QKVG)].T)
    gain, shift = norm_pair(weights, ATTEND)
    grad_single, grads[(ATTEND, NORM_GAIN)], grads[(ATTEND, NORM_BIAS)] = norm_backward(
        single_state, gain, shift, grad_lowered
    )
    return grad_single


def after(values, *others):
    held = lax.optimization_barrier((values,) + others)
    return held


def in_turn():
    last = []

    def send(values, axes):
        if last:
            values = after(values, last.pop())[0]
        moved = swap(values, axes)
        last.append(moved)
        return moved

    return send


def to_plane(values, parts, send):
    shape = values.shape
    values = send(values.reshape((parts, -1) + shape[1:]), "crop")
    return send(values, "z").reshape(shape)


def pair_path(pair, info, alive, orders, weights, cotangent, middle, between, meet, send, group, parts):
    rows, length, width = pair.shape
    hidden = weights[(OUTGOING, PROJ_OUT)].shape[0]
    devices = length // rows
    cores = devices // parts
    order, order_back = orders
    read_first = functools.partial(read_tokens, order)
    read_last = functools.partial(read_turned, order)
    part = hidden // devices
    steps = rows // 16
    state_shape = (rows, width, length)
    block = rows // steps
    half = rows // 2
    flip_shape = (devices, rows, rows, width)
    product_shape = (devices, 2, part, rows, length)
    product_half = (devices, 2, part, half, length)
    tri_shape = (devices, part, rows, length)
    tri_half = (devices, part, half, length)
    channel_block = math.gcd(part, 4)

    def products(name, kernel, arrays, out_shape):
        axes = {4: 1, 5: 2}
        out = (out_shape, BF16, axes[len(out_shape)])
        return run_rows(
            kernel, name, part // channel_block,
            [(Both(pieces), axes[pieces[0].ndim]) for pieces in arrays],
            [out] * (rows // out_shape[-2]), [], 7,
        )

    def swap_all(pieces):
        return [send(values, group) for values in pieces]

    def by_hidden(pieces):
        return [values.reshape((hidden,) + values.shape[2:]) for values in pieces]

    def by_device(pieces):
        return [values.reshape((devices, part) + values.shape[1:]) for values in pieces]

    def cols(prefix):
        return weights[(prefix, COLS)]

    tri_cols = cols

    def turned(name):
        return weights[(name, T)]

    tri_scratch = ((hidden, block, length), F32)
    product_scratch = ((2 * hidden, block, length), F32)
    head_scratch = ((8, block, length), F32)
    wide = ((width, length), F32)
    flip_scratch = ((length, block, width), F32)
    table = ((TA_HEADS, length, length), F32)
    attend_saves = [((rows, TA_HEADS, length), F32, 0), (state_shape, BF16, 0)]

    product = run_rows(
        functools.partial(tri_pre_first_kernel, devices, read_first), "outgoing_in", steps,
        [
            (info, "smem"), (alive, None), (pair, 0), (tri_cols(OUTGOING), None),
            (turned((OUTGOING, PROJ_GATE)), None),
        ],
        [(product_shape, BF16, 3)], [product_scratch], 13,
    )
    between(0, None)
    product_one = swap_all(product)
    tri_one = products(
        "outgoing_product", functools.partial(tri_product_kernel, False), [product_one], tri_half
    )
    tri_one = by_hidden(swap_all(tri_one))
    tri_one = [tri_one[0], *meet(0, tri_one[1])]
    state_one, product = run_halves(
        functools.partial(tri_join_kernel, devices, read_first), "outgoing_out_incoming_in", steps,
        [
            ([info[:half], info[half:]], "smem"), (alive, None), (pair, 0), (tri_one, 1), (tri_cols(OUTGOING), None),
            (turned((OUTGOING, PROJ_OUT)), None), (turned((OUTGOING, GATE_OUT)), None),
            (tri_cols(INCOMING), None), (turned((INCOMING, PROJ_GATE)), None),
        ],
        [(state_shape, F32, 0), (product_half, BF16, 3)], [tri_scratch, product_scratch], 22,
    )
    product_two = list(meet(1, *swap_all(product)))
    tri_two = products(
        "incoming_product", functools.partial(tri_product_kernel, True), [product_two], tri_shape
    )
    tri_two = by_hidden(swap_all(tri_two))
    between(1, None)
    (tri_two,) = meet(2, *tri_two)
    cotangent = cotangent.reshape(rows, parts, cores, parts, -1, width).transpose(3, 2, 1, 4, 0, 5)
    cotangent = send(cotangent.reshape(flip_shape), group)
    state_two, bias = run_rows(
        tri_last_kernel, "incoming_out_starting_bias", steps,
        [
            (state_one, 0), (tri_two, 1), (tri_cols(INCOMING), None),
            (turned((INCOMING, PROJ_OUT)), None), (turned((INCOMING, GATE_OUT)), None),
            (cols(STARTING), None), (weights[(STARTING, BIAS_T)], None),
        ],
        [(state_shape, F32, 0), ((TA_HEADS, rows, length), BF16, 1)], [tri_scratch, head_scratch],
    )
    bias_one = lax.all_gather(bias, group, axis=0, tiled=False)
    flipped, totals_one, mixed_one = run_rows(
        starting_kernel, "starting_attention", steps,
        [
            (alive, None), (state_two, 0), (bias_one, None), (cols(STARTING), None),
            (turned((STARTING, QKVG)), None), (turned((STARTING, OUTPUT)), None),
        ],
        [(flip_shape, BF16, 2)] + attend_saves, [table, flip_scratch], 21,
    )
    state_three = Both([send(flipped, group)])
    cotangent = send(cotangent.reshape((parts, cores) + flip_shape[1:]), "z").reshape(flip_shape)
    (bias,) = run_rows(
        flipped_bias_kernel, "ending_bias", steps,
        [(state_three, 1), (cols(ENDING), None), (weights[(ENDING, BIAS_T)], None)],
        [((TA_HEADS, rows, length), BF16, 1)], [head_scratch],
    )
    bias_two = lax.all_gather(bias, group, axis=0, tiled=False)
    state_four, totals_two, mixed_two = run_rows(
        ending_kernel, "ending_attention", steps,
        [
            (alive, None), (state_three, 1), (bias_two, None), (cols(ENDING), None),
            (turned((ENDING, QKVG)), None), (turned((ENDING, OUTPUT)), None),
        ],
        [(state_shape, F32, 0)] + attend_saves, [table],
    )
    pair_cols, attend_cols = cols(PAIR), cols(ATTEND)
    state_four, cotangent = after(state_four, cotangent)
    state_five, pair_out, single_bias = run_rows(
        functools.partial(transition_kernel, order_back), "pair_transition", steps,
        [
            (state_four, 0), (pair_cols, None), (turned((PAIR, UP)), None), (turned((PAIR, DOWN)), None),
            (attend_cols, None), (turned((ATTEND, PAIR_PROJ)), None),
        ],
        [(state_shape, F32, 0), ((length, rows, width), BF16, 1), ((SA_HEADS, rows, length), BF16, 1)],
        [flip_scratch, ((SA_HEADS, block, length), F32)],
    )
    def turn(values):
        heads = values.shape[0]
        sent = values.reshape(heads, rows, devices, rows).transpose(2, 0, 3, 1)
        return send(sent, group).transpose(1, 2, 0, 3).reshape(heads, rows, length)

    single_grad_scores = turn(middle(turn(single_bias).astype(F32)))
    pair_out = send(pair_out.reshape((parts, -1) + pair_out.shape[1:]), "z")
    between(2, None)
    grads = {}
    grad_four, grads[(PAIR, UP)], grads[(PAIR, DOWN)], grads[(ATTEND, PAIR_PROJ)], vecs = run_rows(
        functools.partial(transition_back_kernel, read_last), "pair_transition_back", steps,
        [
            (state_four, 0), (state_five, 0), (cotangent, 1), (single_grad_scores, 1),
            (pair_cols, None), (turned((PAIR, UP)), None), (weights[(PAIR, UP)], None),
            (weights[(PAIR, DOWN)], None), (attend_cols, None), (weights[(ATTEND, PAIR_PROJ)], None),
        ],
        [
            (state_shape, F32, 0), (weights[(PAIR, UP)].shape, F32, None),
            (weights[(PAIR, DOWN)].shape, F32, None), (weights[(ATTEND, PAIR_PROJ)].shape, F32, None),
            ((8, width), F32, None),
        ],
        [wide, wide, wide, wide, ((SA_HEADS, block, length), F32)], 30,
    )
    grads[(PAIR, VECTORS)] = vecs

    def attention_back(prefix, read, read_grad, source, source_axis, grad, grad_axis, bias, totals, mixed):
        lowered_grad, bias_grad, grads[(prefix, QKVG)], grads[(prefix, OUTPUT)] = run_rows(
            functools.partial(attention_back_kernel, read, read_grad),
            "attention_back", steps,
            [
                (alive, None), (source, source_axis), (grad, grad_axis), (bias, None), (totals, 0),
                (mixed, 0), (cols(prefix), None), (turned((prefix, QKVG)), None),
                (weights[(prefix, QKVG)], None), (weights[(prefix, OUTPUT)], None),
            ],
            [
                (state_shape, BF16, 0), ((devices, TA_HEADS, rows, length), BF16, None),
                (weights[(prefix, QKVG)].shape, F32, None), (weights[(prefix, OUTPUT)].shape, F32, None),
            ],
            [table, table], 34,
        )
        return lowered_grad, send(bias_grad, group)

    lowered_grad, bias_grad = attention_back(
        ENDING, read_flipped, read_plain, state_three, 1, grad_four, 0, bias_two, totals_two, mixed_two
    )
    between(3, grads)
    flipped, bias_w_grad, vecs = run_rows(
        ending_end_kernel, "ending_attention_end", steps,
        [
            (state_three, 1), (grad_four, 0), (lowered_grad, 0), (bias_grad, 2), (cols(ENDING), None),
            (weights[(ENDING, BIAS_W)], None),
        ],
        [(flip_shape, BF16, 2), ((width, 8), F32, None), ((8, width), F32, None)],
        [wide, wide, head_scratch, flip_scratch],
    )
    grads[(ENDING, BIAS_PROJ)], grads[(ENDING, VECTORS)] = bias_w_grad, vecs
    flipped, held = after(flipped, grads[(ATTEND, PAIR_PROJ)])
    grads[(ATTEND, PAIR_PROJ)] = held
    grad_three = send(flipped, group)
    between(4, grads)
    grad_three = Both(meet(3, grad_three))
    pair_out = send(pair_out.reshape(flip_shape), group)
    pair_out = pair_out.reshape(parts, cores, rows, parts, -1, width).transpose(2, 3, 1, 0, 4, 5)
    pair_out = pair_out.reshape(rows, length, width)
    lowered_grad, bias_grad = attention_back(
        STARTING, read_plain, read_flipped, state_two, 0, grad_three, 1, bias_one, totals_one, mixed_one
    )
    between(7, grads)
    square = weights[(INCOMING, GATE_OUT)].shape
    (
        grad_two, grad_tri, gate_back, bias_w_grad, grads[(INCOMING, PROJ_OUT)], grads[(INCOMING, GATE_OUT)], vecs,
    ) = run_halves(
        starting_end_kernel, "starting_end_incoming_out_back", steps,
        [
            (state_two, 0), (grad_three, 1), (lowered_grad, 0), (bias_grad, 2), (cols(STARTING), None),
            (weights[(STARTING, BIAS_W)], None), (state_one, 0), (tri_two, 1), (tri_cols(INCOMING), None),
            (turned((INCOMING, PROJ_OUT)), None), (turned((INCOMING, GATE_OUT)), None),
            (weights[(INCOMING, PROJ_OUT)], None), (weights[(INCOMING, GATE_OUT)], None),
        ],
        [
            (state_shape, F32, 0), ((hidden, half, length), BF16, 1), (state_shape, BF16, 0),
            ((width, 8), F32, None), (square, F32, None), (square, F32, None), ((8, width), F32, None),
        ],
        [wide, wide, wide, wide, head_scratch, tri_scratch], 26,
    )
    grads[(STARTING, BIAS_PROJ)], grads[(STARTING, VECTORS)] = bias_w_grad, vecs
    grad_tri = swap_all(by_device(grad_tri))
    product_grad = products(
        "incoming_product_back", functools.partial(tri_product_back_kernel, True),
        [grad_tri, product_two], product_half,
    )
    product_grad = swap_all(product_grad)
    product_grad = [*meet(4, product_grad[0]), product_grad[1]]
    (
        grad_one, grad_tri, gate_back, grads[(INCOMING, PROJ_GATE)], grads[(OUTGOING, PROJ_OUT)],
        grads[(OUTGOING, GATE_OUT)], vecs,
    ) = run_halves(
        functools.partial(tri_join_back_kernel, read_first), "incoming_in_outgoing_out_back", steps,
        [
            ([info[:half], info[half:]], "smem"), (alive, None), (state_one, 0), (product_grad, 3), (gate_back, 0), (grad_two, 0),
            (tri_cols(INCOMING), None), (turned((INCOMING, PROJ_GATE)), None),
            (weights[(INCOMING, PROJ_GATE)], None), (pair, 0), (tri_one, 1), (tri_cols(OUTGOING), None),
            (turned((OUTGOING, PROJ_OUT)), None), (turned((OUTGOING, GATE_OUT)), None),
            (weights[(OUTGOING, PROJ_OUT)], None), (weights[(OUTGOING, GATE_OUT)], None),
        ],
        [
            (state_shape, F32, 0), ((hidden, half, length), BF16, 1), (state_shape, BF16, 0),
            (weights[(INCOMING, PROJ_GATE)].shape, F32, None), (square, F32, None), (square, F32, None),
            ((8, width), F32, None),
        ],
        [wide, wide, wide, wide, product_scratch, tri_scratch], 37,
    )
    grads[(INCOMING, VECTORS)] = vecs
    between(5, grads)
    grad_tri = swap_all(by_device(grad_tri))
    grad_tri = [grad_tri[0], *meet(6, grad_tri[1])]
    product_grad = products(
        "outgoing_product_back", functools.partial(tri_product_back_kernel, False),
        [grad_tri, product_one], product_shape,
    )
    (product_grad,) = meet(5, *swap_all(product_grad))
    between(6, grads)
    pair_grad, grads[(OUTGOING, PROJ_GATE)], vecs = run_rows(
        functools.partial(tri_first_back_kernel, read_first, order_back), "outgoing_in_back", steps,
        [
            (info, "smem"), (alive, None), (pair, 0), (product_grad, 3), (gate_back, 0), (grad_one, 0),
            (tri_cols(OUTGOING), None), (turned((OUTGOING, PROJ_GATE)), None),
            (weights[(OUTGOING, PROJ_GATE)], None),
        ],
        [
            ((rows, length, width), BF16, 0), (weights[(OUTGOING, PROJ_GATE)].shape, F32, None),
            ((8, width), F32, None),
        ],
        [wide, wide, product_scratch], 20,
    )
    grads[(OUTGOING, VECTORS)] = vecs
    return pair_out, pair_grad, grads


HELD = {
    (PAIR, VECTORS): ((PAIR, NORM_GAIN), (PAIR, NORM_BIAS), (ATTEND, PAIR_GAIN), (ATTEND, PAIR_BIAS)),
    (ENDING, VECTORS): ((ENDING, NORM_GAIN), (ENDING, NORM_BIAS)),
    (STARTING, VECTORS): (
        (STARTING, NORM_GAIN), (STARTING, NORM_BIAS), (INCOMING, OUT_GAIN), (INCOMING, OUT_BIAS)
    ),
    (INCOMING, VECTORS): (
        (INCOMING, NORM_GAIN), (INCOMING, NORM_BIAS), (OUTGOING, OUT_GAIN), (OUTGOING, OUT_BIAS)
    ),
    (OUTGOING, VECTORS): ((OUTGOING, NORM_GAIN), (OUTGOING, NORM_BIAS)),
}


def vector_part(grads, name, prefix):
    pairs = [(row, held) for row, held in enumerate(HELD[name]) if prefix in (None, held[0])]
    return (pairs, grads[name])


def fast_shards(parts, cores, pair, single, lengths, params, moment_one, moment_two, pair_cotangent, single_cotangent):
    entries = layout(C, H, S, TA_HEADS, SA_HEADS)
    table, total = table_of(entries)
    count = total // STRIDE
    shard_size = params.shape[0]
    attend = table[(ATTEND, NORM_GAIN)][0]
    pair_lanes = -(-attend * STRIDE // count)
    single_lane = attend * STRIDE // count
    devices = parts * cores
    line, group = ("z", "core"), ("crop", "core")
    row_index = lax.axis_index(line)
    odd = ((row_index * shard_size) % STRIDE) // (STRIDE // 2)
    place = jnp.stack([odd, odd]).astype(jnp.int32)
    shard_rows = jnp.pad(params, (0, RUN * STRIDE * STRIDE - shard_size)).reshape(-1, STRIDE)
    (runs,) = whole_call(
        runs_kernel, "parameter_runs", [(place, "smem"), (shard_rows, None)],
        [((STRIDE, RUN, STRIDE), BF16)], [((STRIDE, RUN, STRIDE), F32)],
    )
    rows, length, width = pair.shape[1:]
    send = in_turn()
    pair_in = send(pair[0].reshape(parts, -1, length, width), "crop")
    first_runs = lax.all_gather(runs[:pair_lanes], line)
    pair_in, _, lengths = after(pair_in, runs, lengths)
    live = lax.all_gather(jnp.broadcast_to(lengths.astype(F32), (8, STRIDE)), "crop")
    pair_in = send(pair_in, "z").reshape(rows, length, width)
    weights = unpack_pair(table, total, first_runs)
    pair_in, last_runs = after(pair_in, runs[single_lane:])
    last_runs = lax.all_gather(last_runs, line)
    weights.update(unpack_single(table, total, single_lane, last_runs))
    for index, name in enumerate(SINGLE_VECTORS):
        weights[name] = weights[(SINGLE, VECTORS)][index]
    size = rows // parts
    blocks = np.arange(length // size).reshape(parts, cores, parts)
    order = blocks.transpose(2, 1, 0).reshape(-1)
    orders = (order.tolist(), np.argsort(order).tolist())
    tokens = (order[:, None] * size + np.arange(size)).reshape(-1)
    live = live[lax.axis_index("z"), 0, 0]
    width = single.shape[2]
    mask = (tokens.astype(np.float32) < live).astype(F32)
    info = lax.dynamic_slice_in_dim(mask, lax.axis_index(group) * rows, rows).astype(jnp.int32)
    alive = jnp.broadcast_to(mask, (8, length))
    penalty = (mask - 1.0) * MASKED
    held = {}
    single_grads = {}

    def middle(bias):
        update, saved = single_attend(held["state"], held["projected"], bias, penalty, weights)
        single_mid = held["state"] + update
        update, saved_last = transition_forward(single_mid, weights, SINGLE)
        held["out"] = single_mid + update
        grad = held["back"] + transition_backward(saved_last, held["back"], weights, SINGLE, single_grads)
        held["grad"] = grad
        grad_scores, held["pending"] = single_attend_back(saved, grad, weights, single_grads)
        return grad_scores

    def meet(number, *values):
        if number == 0:
            others = [last_runs]
        elif number == 1:
            others = [weights[(SINGLE, UP)]]
        elif number == 2:
            others = [held["projected"][1]]
        elif number == 3:
            others = [reduced[3]]
        elif number == 4:
            others = [reduced[2]]
            reduced[2] = lax.psum(reduced[2], "crop")
        elif number == 5:
            others = [reduced[2]]
        else:
            others = [reduced[1]]
        return after(*values, *others)[: len(values)]

    def reduce_runs(sent):
        part = jnp.sum(send(sent, line).astype(F32), axis=0).astype(BF16)
        return jnp.sum(lax.all_gather(part, "crop").astype(F32), axis=0)

    reduced = {}
    lines_held = list(enumerate(SINGLE_VECTORS))
    late_lanes = -(-table[(INCOMING, NORM_GAIN)][0] * STRIDE // count)

    def lines():
        values = jnp.concatenate([single_grads[name].reshape(1, S) for name in SINGLE_VECTORS], axis=0)
        return jnp.pad(values, ((0, 8 - len(SINGLE_VECTORS)), (0, 0)))

    def between(number, grads):
        if number == 0:
            both = jnp.concatenate([single[0], single_cotangent[0]], axis=1)
            both = to_plane(both, parts, send).astype(F32)
            held["state"], held["back"] = both[:, :width], both[:, width:]
            return
        if number == 1:
            lowered, qkvg, both = single_project(held["state"], weights, devices)
            held["projected"] = lowered, qkvg, send(both, group)
            return
        if number == 2:
            pending = held["pending"]
            moved = send(pending[0], group)
            grad = held["grad"] + single_attend_end(pending, moved, weights, single_grads)
            held["both"] = jnp.concatenate([held["out"], grad], axis=1).reshape(parts, -1, 2 * width)
            return
        if number == 3:
            held["both"] = send(held["both"], "z")
            return
        if number == 7:
            both = send(held["both"], "crop").reshape(rows, 2 * width)
            held[SINGLE] = both[:, :width].astype(BF16), both[:, width:]
            return
        if number == 6:
            reduced[1] = reduce_runs(reduced[1])
            return
        if number == 4:
            sent = pack(
                "single_gradient", table, total, devices, (pair_lanes, STRIDE), attend,
                [(name, single_grads[name]) for name in SINGLE_MATRICES]
                + [((ATTEND, PAIR_PROJ), grads[(ATTEND, PAIR_PROJ)])]
                + [vector_part(grads, (PAIR, VECTORS), ATTEND), (lines_held, lines())],
            )
            reduced[3] = sent
            reduced[2] = lax.psum_scatter(sent, line, scatter_dimension=0, tiled=False)
            return
        taken = -(-(pair_lanes * count - (attend + 2 * S // STRIDE) * STRIDE) // (4 * S))
        first = table[(INCOMING, NORM_GAIN)][0]
        sent = pack(
            "pair_gradient", table, total, devices, (late_lanes, pair_lanes), first,
            [(name, grads[name]) for name in PAIR_MATRICES if table[name][0] >= first]
            + [(name, grads[name]) for name in ((STARTING, BIAS_PROJ), (ENDING, BIAS_PROJ))]
            + [vector_part(grads, name, None) for name in ((ENDING, VECTORS), (STARTING, VECTORS))]
            + [vector_part(grads, (INCOMING, VECTORS), INCOMING)]
            + [vector_part(grads, (PAIR, VECTORS), PAIR)]
            + [(lines_held[:2], lines()), ((ATTEND, QKVG), single_grads[(ATTEND, QKVG)][: -(-taken // 8) * 8])],
        )
        reduced[1] = sent

    pair_out, pair_grad, grads = pair_path(
        pair_in, info, alive, orders, weights, pair_cotangent[0], middle, between, meet, send, group, parts
    )
    first = table[(INCOMING, NORM_GAIN)][0]
    taken = -(-(late_lanes * count - (first + 2) * STRIDE) // (4 * H))
    sent = pack(
        "outgoing_gradient", table, total, devices, (0, late_lanes), 0,
        [(name, grads[name]) for name in PAIR_MATRICES if table[name][0] < first]
        + [vector_part(grads, (OUTGOING, VECTORS), None)]
        + [vector_part(grads, (INCOMING, VECTORS), None)]
        + [((INCOMING, PROJ_GATE), grads[(INCOMING, PROJ_GATE)][: -(-taken // 8) * 8])],
    )
    reduced[0] = reduce_runs(sent)
    pair_grad = send(pair_grad.reshape(parts, -1, length, pair_grad.shape[2]), "z")
    pair_grad = send(pair_grad, "crop").reshape(rows, length, -1).astype(F32)
    single_out, single_grad = held[SINGLE]
    shard, squares = whole_call(
        functools.partial(shard_kernel, shard_size), "gradient_share",
        [(place, "smem"), (jnp.concatenate([reduced[part].astype(F32) for part in range(3)], axis=0), None)],
        [((RUN * STRIDE, STRIDE), F32), ((8, STRIDE), F32)], [],
    )
    shard = shard.reshape(-1)[:shard_size]
    clip_norm = jnp.sqrt(jnp.sum(lax.all_gather(squares, line)))
    clipped = shard * (CLIP / jnp.maximum(clip_norm, CLIP))
    new_first = BETA_ONE * moment_one + (1.0 - BETA_ONE) * clipped
    new_second = BETA_TWO * moment_two + (1.0 - BETA_TWO) * clipped * clipped
    rates, decays = rate_tables(entries)
    rate_shard = lax.dynamic_slice_in_dim(jnp.asarray(rates), row_index * shard_size, shard_size)
    decay_shard = lax.dynamic_slice_in_dim(jnp.asarray(decays), row_index * shard_size, shard_size)
    first_hat = new_first / (1.0 - BETA_ONE**STEP)
    second_hat = new_second / (1.0 - BETA_TWO**STEP)
    new_params = params - rate_shard * (
        first_hat / (jnp.sqrt(second_hat) + ADAM_EPS) + decay_shard * params
    )
    return (
        pair_out[None],
        single_out[None],
        pair_grad[None],
        single_grad[None],
        new_params,
        new_first,
        new_second,
        clip_norm,
    )


def solution(mesh):
    crops, devices = mesh.devices.shape
    count = table_of(layout(C, H, S, TA_HEADS, SA_HEADS))[1] // STRIDE
    fast = devices == 2 * crops and LENGTH % (devices * 16) == 0 and count // devices + 2 <= RUN * STRIDE
    row = "row"
    if fast:
        mesh = jax.sharding.Mesh(mesh.devices.reshape(crops, crops, 2), ("crop", "z", "core"))
        row = ("z", "core")
    split = [P("crop", row, None, None), P("crop", row, None), P("crop"), P(row)]
    pair, single, lengths, share = split
    return jax.shard_map(
        functools.partial(fast_shards, crops, 2) if fast else shards,
        mesh=mesh,
        in_specs=(pair, single, lengths, share, share, share, pair, single),
        out_specs=(pair, single, pair, single, share, share, share, P()),
        check_vma=False,
    )
```

```python
import functools
import math

import jax
import jax.numpy as jnp
import numpy as np
from jax import lax
from jax.experimental import pallas as pl
from jax.experimental.pallas import tpu as pltpu
from jax.sharding import PartitionSpec as P

C = 128
H = 128
S = 384
TA_HEADS = 4
SA_HEADS = 16
STEP = 10
STRIDE = 128
LENGTH = 256

OUTGOING, INCOMING, STARTING, ENDING, PAIR, ATTEND, SINGLE = range(7)
(
    NORM_GAIN,
    NORM_BIAS,
    PROJ_GATE,
    OUT_GAIN,
    OUT_BIAS,
    PROJ_OUT,
    GATE_OUT,
    QKVG,
    BIAS_PROJ,
    OUTPUT,
    UP,
    DOWN,
    PAIR_GAIN,
    PAIR_BIAS,
    PAIR_PROJ,
    COLS,
    BIAS_W,
    BIAS_T,
    VECTORS,
    T,
) = range(7, 27)


EPSILON = 1e-05
MASKED = 1000000000.0
BETA_ONE = 0.9
BETA_TWO = 0.95
ADAM_EPS = 1e-08
CLIP = 1.0


def layout(pair_width, hidden_width, single_width, tri_heads, att_heads):
    entries = []
    for prefix in (OUTGOING, INCOMING):
        entries += [
            ((prefix, NORM_GAIN), (pair_width,)),
            ((prefix, NORM_BIAS), (pair_width,)),
            ((prefix, PROJ_GATE), (pair_width, 4 * hidden_width)),
            ((prefix, OUT_GAIN), (hidden_width,)),
            ((prefix, OUT_BIAS), (hidden_width,)),
            ((prefix, PROJ_OUT), (hidden_width, pair_width)),
            ((prefix, GATE_OUT), (pair_width, pair_width)),
        ]
    for prefix in (STARTING, ENDING):
        entries += [
            ((prefix, NORM_GAIN), (pair_width,)),
            ((prefix, NORM_BIAS), (pair_width,)),
            ((prefix, QKVG), (pair_width, 4 * pair_width)),
            ((prefix, BIAS_PROJ), (pair_width, tri_heads)),
            ((prefix, OUTPUT), (pair_width, pair_width)),
        ]
    entries += [
        ((PAIR, NORM_GAIN), (pair_width,)),
        ((PAIR, NORM_BIAS), (pair_width,)),
        ((PAIR, UP), (pair_width, 8 * pair_width)),
        ((PAIR, DOWN), (4 * pair_width, pair_width)),
        ((ATTEND, NORM_GAIN), (single_width,)),
        ((ATTEND, NORM_BIAS), (single_width,)),
        ((ATTEND, QKVG), (single_width, 4 * single_width)),
        ((ATTEND, PAIR_GAIN), (pair_width,)),
        ((ATTEND, PAIR_BIAS), (pair_width,)),
        ((ATTEND, PAIR_PROJ), (pair_width, att_heads)),
        ((ATTEND, OUTPUT), (single_width, single_width)),
        ((SINGLE, NORM_GAIN), (single_width,)),
        ((SINGLE, NORM_BIAS), (single_width,)),
        ((SINGLE, UP), (single_width, 8 * single_width)),
        ((SINGLE, DOWN), (4 * single_width, single_width)),
    ]
    return entries


def logical_order(flat):
    return flat.reshape(-1, STRIDE).T.reshape(-1)


def stored_order(vector):
    return vector.reshape(STRIDE, -1).T.reshape(-1)


def rate_tables(entries):
    rates = []
    decays = []
    for name, shape in entries:
        count = math.prod(shape)
        if len(shape) == 1:
            rates.append(np.full(count, 0.5, np.float32))
            decays.append(np.zeros(count, np.float32))
        else:
            rates.append(np.full(count, 2.0 / math.sqrt(shape[0]), np.float32))
            decays.append(np.full(count, 0.01, np.float32))
    rates = np.concatenate(rates)
    decays = np.concatenate(decays)
    return (rates.reshape(STRIDE, -1).T.reshape(-1), decays.reshape(STRIDE, -1).T.reshape(-1))


def unpack(flat, entries):
    pieces = {}
    offset = 0
    for name, shape in entries:
        count = math.prod(shape)
        pieces[name] = flat[offset : offset + count].reshape(shape)
        offset += count
    return pieces


def layer_norm(values, gain, shift):
    centred = values - jnp.mean(values, axis=-1, keepdims=True)
    spread = jnp.mean(centred * centred, axis=-1, keepdims=True)
    return centred * lax.rsqrt(spread + EPSILON) * gain + shift


def norm_backward(values, gain, shift, grad):
    _, pullback = jax.vjp(layer_norm, values, gain, shift)
    return pullback(grad)


def norm_pair(weights, prefix):
    return (
        weights[(prefix, NORM_GAIN)].astype(jnp.float32),
        weights[(prefix, NORM_BIAS)].astype(jnp.float32),
    )


def gated_pair(project, pair_mask):
    half = project.shape[-1] // 2
    return project[..., :half] * jax.nn.sigmoid(project[..., half:]) * pair_mask[..., None]


def gated_output(values, gate):
    return values * jax.nn.sigmoid(gate)


def swiglu(hidden):
    half = hidden.shape[-1] // 2
    return jax.nn.silu(hidden[..., :half]) * hidden[..., half:]


def matmul(left, right):
    return jnp.dot(left, right, preferred_element_type=jnp.float32)


def outer_sum(left, right):
    return jnp.einsum(
        "nc,nd->cd",
        left.reshape(-1, left.shape[-1]),
        right.reshape(-1, right.shape[-1]),
        preferred_element_type=jnp.float32,
    )


def flip(values):
    moved = lax.all_to_all(values, "row", split_axis=1, concat_axis=0, tiled=True)
    return jnp.swapaxes(moved, 0, 1)


def channel_forward(first, second, incoming):
    whole_first, whole_second = (
        lax.all_to_all(first, "row", split_axis=2, concat_axis=0, tiled=True),
        lax.all_to_all(second, "row", split_axis=2, concat_axis=0, tiled=True),
    )
    if incoming:
        local_tri = jnp.einsum(
            "kih,kjh->ijh", whole_first, whole_second, preferred_element_type=jnp.float32
        )
        local_tri = local_tri.astype(jnp.bfloat16).astype(jnp.float32)
    else:
        local_tri = jnp.einsum(
            "ikh,jkh->ijh", whole_first, whole_second, preferred_element_type=jnp.float32
        )
    tri = lax.all_to_all(
        local_tri.astype(jnp.bfloat16), "row", split_axis=0, concat_axis=2, tiled=True
    ).astype(local_tri.dtype)
    return (tri, whole_first, whole_second)


def channel_backward(grad_tri, whole_first, whole_second, incoming):
    whole_grad = lax.all_to_all(grad_tri, "row", split_axis=2, concat_axis=0, tiled=True)
    if incoming:
        grad_a = jnp.einsum(
            "ijh,kjh->kih", whole_grad, whole_second, preferred_element_type=jnp.float32
        )
        grad_b = jnp.einsum(
            "ijh,kih->kjh", whole_grad, whole_first, preferred_element_type=jnp.float32
        )
    else:
        grad_a = jnp.einsum(
            "ijh,jkh->ikh", whole_grad, whole_second, preferred_element_type=jnp.float32
        )
        grad_b = jnp.einsum(
            "ijh,ikh->jkh", whole_grad, whole_first, preferred_element_type=jnp.float32
        )
    return (
        lax.all_to_all(
            grad_a.astype(jnp.bfloat16), "row", split_axis=0, concat_axis=2, tiled=True
        ).astype(grad_a.dtype),
        lax.all_to_all(
            grad_b.astype(jnp.bfloat16), "row", split_axis=0, concat_axis=2, tiled=True
        ).astype(grad_b.dtype),
    )


def triangle_forward(state, pair_mask, weights, prefix, incoming):
    gain, shift = norm_pair(weights, prefix)
    lowered = layer_norm(state, gain, shift).astype(jnp.bfloat16)
    project = matmul(lowered, weights[(prefix, PROJ_GATE)])
    product = gated_pair(project, pair_mask).astype(jnp.bfloat16)
    half = product.shape[-1] // 2
    tri, own, other = channel_forward(product[..., :half], product[..., half:], incoming)
    out_gain = weights[(prefix, OUT_GAIN)].astype(jnp.float32)
    out_shift = weights[(prefix, OUT_BIAS)].astype(jnp.float32)
    out_low = layer_norm(tri, out_gain, out_shift).astype(jnp.bfloat16)
    output = matmul(out_low, weights[(prefix, PROJ_OUT)])
    gate_out = matmul(lowered, weights[(prefix, GATE_OUT)])
    update = gated_output(output, gate_out)
    return (update, (state, lowered, lowered, project, own, other, tri, out_low, output, gate_out))


def triangle_backward(saved, grad_update, pair_mask, weights, prefix, incoming, grads):
    state, lowered, framed, project, own, other, tri, out_low, output, gate_out = saved
    _, pullback = jax.vjp(gated_output, output, gate_out)
    grad_output, grad_gate = pullback(grad_update)
    grad_output = grad_output.astype(jnp.bfloat16)
    grad_gate = grad_gate.astype(jnp.bfloat16)
    grads[(prefix, PROJ_OUT)] = outer_sum(out_low, grad_output)
    grads[(prefix, GATE_OUT)] = outer_sum(lowered, grad_gate)
    grad_normed = matmul(grad_output, weights[(prefix, PROJ_OUT)].T)
    out_gain = weights[(prefix, OUT_GAIN)].astype(jnp.float32)
    out_shift = weights[(prefix, OUT_BIAS)].astype(jnp.float32)
    grad_tri, grads[(prefix, OUT_GAIN)], grads[(prefix, OUT_BIAS)] = norm_backward(
        tri, out_gain, out_shift, grad_normed
    )
    grad_tri = grad_tri.astype(jnp.bfloat16)
    grad_first, grad_second = channel_backward(grad_tri, own, other, incoming)
    _, pullback = jax.vjp(lambda values: gated_pair(values, pair_mask), project)
    (grad_project,) = pullback(jnp.concatenate([grad_first, grad_second], axis=-1))
    grad_project = grad_project.astype(jnp.bfloat16)
    grads[(prefix, PROJ_GATE)] = outer_sum(framed, grad_project)
    grad_framed = matmul(grad_project, weights[(prefix, PROJ_GATE)].T)
    if incoming:
        grad_framed = grad_framed.astype(jnp.bfloat16).astype(jnp.float32)
    grad_lowered = grad_framed + matmul(grad_gate, weights[(prefix, GATE_OUT)].T)
    gain, shift = norm_pair(weights, prefix)
    grad_state, grads[(prefix, NORM_GAIN)], grads[(prefix, NORM_BIAS)] = norm_backward(
        state, gain, shift, grad_lowered
    )
    return grad_state


def row_scores(query, key, bias, penalty, scale):
    scores = jnp.einsum("jhd,khd->hjk", query, key, preferred_element_type=jnp.float32) * scale
    return scores + bias.astype(jnp.float32) + penalty[None, None, :]


def attention_forward(state, penalty, weights, prefix, ending):
    gain, shift = norm_pair(weights, prefix)
    lowered = layer_norm(state, gain, shift).astype(jnp.bfloat16)
    framed = flip(lowered) if ending else lowered
    rows, length, width = framed.shape
    size = width // TA_HEADS
    scale = size ** (-0.5)
    qkvg = matmul(framed, weights[(prefix, QKVG)])
    queries = qkvg[..., :width].astype(jnp.bfloat16).reshape(rows, length, TA_HEADS, size)
    keys = qkvg[..., width : 2 * width].astype(jnp.bfloat16).reshape(rows, length, TA_HEADS, size)
    values = (
        qkvg[..., 2 * width : 3 * width].astype(jnp.bfloat16).reshape(rows, length, TA_HEADS, size)
    )
    gate = qkvg[..., 3 * width :]
    local_bias = (
        matmul(framed, weights[(prefix, BIAS_PROJ)]).astype(jnp.bfloat16).transpose(2, 0, 1)
    )
    bias = lax.all_gather(local_bias, "row", axis=1, tiled=True)

    def forward_row(items):
        query, key, value = items
        scores = row_scores(query, key, bias, penalty, scale)
        top = jnp.max(scores, axis=-1, keepdims=True)
        shifted = jnp.exp(scores - top)
        total = jnp.sum(shifted, axis=-1, keepdims=True)
        probs = (shifted / total).astype(jnp.bfloat16)
        mixed = jnp.einsum("hjk,khd->jhd", probs, value, preferred_element_type=jnp.float32)
        return (mixed, top[..., 0] + jnp.log(total[..., 0]))

    mixed, log_totals = lax.map(forward_row, (queries, keys, values))
    mixed = mixed.reshape(rows, length, width)
    gated_low = gated_output(mixed, gate).astype(jnp.bfloat16)
    returned = flip(gated_low) if ending else gated_low
    update = matmul(returned, weights[(prefix, OUTPUT)])
    return (update, (state, framed, queries, keys, values, gate, bias, mixed, log_totals, returned))


def attention_backward(saved, grad_update, penalty, weights, prefix, ending, grads):
    state, framed, queries, keys, values, gate, bias, mixed, log_totals, returned = saved
    rows, length, width = framed.shape
    size = width // TA_HEADS
    scale = size ** (-0.5)
    grad_low = grad_update.astype(jnp.bfloat16)
    grads[(prefix, OUTPUT)] = outer_sum(returned, grad_low)
    grad_gated = matmul(grad_low, weights[(prefix, OUTPUT)].T)
    if ending:
        grad_gated = flip(grad_gated.astype(jnp.bfloat16)).astype(jnp.float32)
    _, pullback = jax.vjp(gated_output, mixed, gate)
    grad_mixed, grad_gate = pullback(grad_gated)
    grad_mixed = grad_mixed.astype(jnp.bfloat16).reshape(rows, length, TA_HEADS, size)

    def back_row(carry, items):
        query, key, value, log_total, grad_row = items
        scores = row_scores(query, key, bias, penalty, scale)
        probs = jnp.exp(scores - log_total[..., None])
        grad_probs = jnp.einsum("jhd,khd->hjk", grad_row, value, preferred_element_type=jnp.float32)
        delta = jnp.sum(probs * grad_probs, axis=-1, keepdims=True)
        grad_scores = (probs * (grad_probs - delta)).astype(jnp.bfloat16)
        grad_query = (
            jnp.einsum("hjk,khd->jhd", grad_scores, key, preferred_element_type=jnp.float32) * scale
        )
        grad_key = (
            jnp.einsum("hjk,jhd->khd", grad_scores, query, preferred_element_type=jnp.float32)
            * scale
        )
        grad_value = jnp.einsum(
            "hjk,jhd->khd", probs.astype(jnp.bfloat16), grad_row, preferred_element_type=jnp.float32
        )
        return (carry + grad_scores.astype(jnp.float32), (grad_query, grad_key, grad_value))

    empty = jnp.zeros(bias.shape, jnp.float32)
    grad_bias, (grad_query, grad_key, grad_value) = lax.scan(
        back_row, empty, (queries, keys, values, log_totals, grad_mixed)
    )
    grad_bias = lax.psum_scatter(grad_bias, "row", scatter_dimension=1, tiled=True)
    grad_bias = grad_bias.transpose(1, 2, 0).astype(jnp.bfloat16)
    grad_qkvg = jnp.concatenate(
        [
            grad_query.reshape(rows, length, width),
            grad_key.reshape(rows, length, width),
            grad_value.reshape(rows, length, width),
            grad_gate,
        ],
        axis=-1,
    ).astype(jnp.bfloat16)
    grads[(prefix, QKVG)] = outer_sum(framed, grad_qkvg)
    grads[(prefix, BIAS_PROJ)] = outer_sum(framed, grad_bias)
    grad_framed = matmul(grad_qkvg, weights[(prefix, QKVG)].T) + matmul(
        grad_bias, weights[(prefix, BIAS_PROJ)].T
    )
    if ending:
        grad_framed = flip(grad_framed.astype(jnp.bfloat16)).astype(jnp.float32)
    gain, shift = norm_pair(weights, prefix)
    grad_state, grads[(prefix, NORM_GAIN)], grads[(prefix, NORM_BIAS)] = norm_backward(
        state, gain, shift, grad_framed
    )
    return grad_state


def transition_forward(state, weights, prefix):
    gain, shift = norm_pair(weights, prefix)
    lowered = layer_norm(state, gain, shift).astype(jnp.bfloat16)
    hidden = matmul(lowered, weights[(prefix, UP)])
    mixed_low = swiglu(hidden).astype(jnp.bfloat16)
    update = matmul(mixed_low, weights[(prefix, DOWN)])
    return (update, (state, lowered, hidden, mixed_low))


def transition_backward(saved, grad_update, weights, prefix, grads):
    state, lowered, hidden, mixed_low = saved
    grad_low = grad_update.astype(jnp.bfloat16)
    grads[(prefix, DOWN)] = outer_sum(mixed_low, grad_low)
    grad_mixed = matmul(grad_low, weights[(prefix, DOWN)].T)
    _, pullback = jax.vjp(swiglu, hidden)
    (grad_hidden,) = pullback(grad_mixed)
    grad_hidden = grad_hidden.astype(jnp.bfloat16)
    grads[(prefix, UP)] = outer_sum(lowered, grad_hidden)
    grad_lowered = matmul(grad_hidden, weights[(prefix, UP)].T)
    gain, shift = norm_pair(weights, prefix)
    grad_state, grads[(prefix, NORM_GAIN)], grads[(prefix, NORM_BIAS)] = norm_backward(
        state, gain, shift, grad_lowered
    )
    return grad_state


def single_forward(single_state, pair_state, penalty, weights):
    gain, shift = norm_pair(weights, ATTEND)
    lowered = layer_norm(single_state, gain, shift).astype(jnp.bfloat16)
    rows, width = lowered.shape
    size = width // SA_HEADS
    qkvg = matmul(lowered, weights[(ATTEND, QKVG)])
    query = qkvg[:, :width].astype(jnp.bfloat16).reshape(rows, SA_HEADS, size)
    key = qkvg[:, width : 2 * width].astype(jnp.bfloat16)
    value = qkvg[:, 2 * width : 3 * width].astype(jnp.bfloat16)
    gate = qkvg[:, 3 * width :]
    keys_all, values_all = (
        lax.all_gather(key, "row", axis=0, tiled=True),
        lax.all_gather(value, "row", axis=0, tiled=True),
    )
    keys_all = keys_all.reshape(-1, SA_HEADS, size)
    values_all = values_all.reshape(-1, SA_HEADS, size)
    pair_gain = weights[(ATTEND, PAIR_GAIN)].astype(jnp.float32)
    pair_shift = weights[(ATTEND, PAIR_BIAS)].astype(jnp.float32)
    pair_low = layer_norm(pair_state, pair_gain, pair_shift).astype(jnp.bfloat16)
    bias = matmul(pair_low, weights[(ATTEND, PAIR_PROJ)]).transpose(2, 0, 1)
    scores = jnp.einsum(
        "ihd,jhd->hij", query, keys_all, preferred_element_type=jnp.float32
    ) * size ** (-0.5)
    scores = scores + bias + penalty[None, None, :]
    probs = jax.nn.softmax(scores, axis=-1)
    probs_low = probs.astype(jnp.bfloat16)
    mixed = jnp.einsum(
        "hij,jhd->ihd", probs_low, values_all, preferred_element_type=jnp.float32
    ).reshape(rows, width)
    gated_low = gated_output(mixed, gate).astype(jnp.bfloat16)
    update = matmul(gated_low, weights[(ATTEND, OUTPUT)])
    return (
        update,
        (
            single_state,
            pair_state,
            lowered,
            query,
            keys_all,
            values_all,
            gate,
            pair_low,
            probs,
            probs_low,
            mixed,
            gated_low,
        ),
    )


def single_backward(saved, grad_update, weights, grads):
    (
        single_state,
        pair_state,
        lowered,
        query,
        keys_all,
        values_all,
        gate,
        pair_low,
        probs,
        probs_low,
        mixed,
        gated_low,
    ) = saved
    rows, width = lowered.shape
    size = width // SA_HEADS
    scale = size ** (-0.5)
    grad_low = grad_update.astype(jnp.bfloat16)
    grads[(ATTEND, OUTPUT)] = outer_sum(gated_low, grad_low)
    grad_gated = matmul(grad_low, weights[(ATTEND, OUTPUT)].T)
    _, pullback = jax.vjp(gated_output, mixed, gate)
    grad_mixed, grad_gate = pullback(grad_gated)
    grad_mixed = grad_mixed.astype(jnp.bfloat16).reshape(rows, SA_HEADS, size)
    grad_probs = jnp.einsum(
        "ihd,jhd->hij", grad_mixed, values_all, preferred_element_type=jnp.float32
    )
    delta = jnp.sum(probs * grad_probs, axis=-1, keepdims=True)
    grad_scores = (probs * (grad_probs - delta)).astype(jnp.bfloat16)
    grad_query = (
        jnp.einsum("hij,jhd->ihd", grad_scores, keys_all, preferred_element_type=jnp.float32)
        * scale
    )
    key_part = (
        jnp.einsum("hij,ihd->jhd", grad_scores, query, preferred_element_type=jnp.float32) * scale
    )
    value_part = jnp.einsum(
        "hij,ihd->jhd", probs_low, grad_mixed, preferred_element_type=jnp.float32
    )
    grad_key, grad_value = (
        lax.psum_scatter(key_part.reshape(-1, width), "row", scatter_dimension=0, tiled=True),
        lax.psum_scatter(value_part.reshape(-1, width), "row", scatter_dimension=0, tiled=True),
    )
    grad_qkvg = jnp.concatenate(
        [grad_query.reshape(rows, width), grad_key, grad_value, grad_gate], axis=-1
    ).astype(jnp.bfloat16)
    grads[(ATTEND, QKVG)] = outer_sum(lowered, grad_qkvg)
    grad_lowered = matmul(grad_qkvg, weights[(ATTEND, QKVG)].T)
    gain, shift = norm_pair(weights, ATTEND)
    grad_single, grads[(ATTEND, NORM_GAIN)], grads[(ATTEND, NORM_BIAS)] = norm_backward(
        single_state, gain, shift, grad_lowered
    )
    grad_bias = grad_scores.transpose(1, 2, 0)
    grads[(ATTEND, PAIR_PROJ)] = outer_sum(pair_low, grad_bias)
    grad_pair_low = matmul(grad_bias, weights[(ATTEND, PAIR_PROJ)].T)
    pair_gain = weights[(ATTEND, PAIR_GAIN)].astype(jnp.float32)
    pair_shift = weights[(ATTEND, PAIR_BIAS)].astype(jnp.float32)
    grad_pair, grads[(ATTEND, PAIR_GAIN)], grads[(ATTEND, PAIR_BIAS)] = norm_backward(
        pair_state, pair_gain, pair_shift, grad_pair_low
    )
    return (grad_single, grad_pair)


def shards(pair, single, lengths, params, moment_one, moment_two, pair_cotangent, single_cotangent):
    entries = layout(C, H, S, TA_HEADS, SA_HEADS)
    full = lax.all_gather(params.astype(jnp.bfloat16), "row", axis=0, tiled=True)
    weights = unpack(logical_order(full), entries)
    rows = pair.shape[1]
    length = pair.shape[2]
    first_row = lax.axis_index("row") * rows
    mask = (jnp.arange(length, dtype=jnp.int32) < lengths[0]).astype(jnp.float32)
    mask_rows = lax.dynamic_slice_in_dim(mask, first_row, rows)
    pair_mask = mask_rows[:, None] * mask[None, :]
    penalty = (mask - 1.0) * MASKED
    state = pair[0].astype(jnp.float32)
    saved = {}
    for prefix, incoming in ((OUTGOING, False), (INCOMING, True)):
        update, saved[prefix] = triangle_forward(state, pair_mask, weights, prefix, incoming)
        state = state + update
    for prefix, ending in ((STARTING, False), (ENDING, True)):
        update, saved[prefix] = attention_forward(state, penalty, weights, prefix, ending)
        state = state + update
    update, saved[PAIR] = transition_forward(state, weights, PAIR)
    pair_final = state + update
    single_state = single[0].astype(jnp.float32)
    update, saved[ATTEND] = single_forward(single_state, pair_final, penalty, weights)
    single_mid = single_state + update
    update, saved[SINGLE] = transition_forward(single_mid, weights, SINGLE)
    single_final = single_mid + update
    grads = {}
    grad_single = single_cotangent[0].astype(jnp.float32)
    grad_single = grad_single + transition_backward(
        saved[SINGLE], grad_single, weights, SINGLE, grads
    )
    from_single, from_pair = single_backward(saved[ATTEND], grad_single, weights, grads)
    grad_single = grad_single + from_single
    grad_pair = pair_cotangent[0].astype(jnp.float32) + from_pair
    grad_pair = grad_pair + transition_backward(saved[PAIR], grad_pair, weights, PAIR, grads)
    for prefix, ending in ((ENDING, True), (STARTING, False)):
        grad_pair = grad_pair + attention_backward(
            saved[prefix], grad_pair, penalty, weights, prefix, ending, grads
        )
    for prefix, incoming in ((INCOMING, True), (OUTGOING, False)):
        grad_pair = grad_pair + triangle_backward(
            saved[prefix], grad_pair, pair_mask, weights, prefix, incoming, grads
        )
    flat = stored_order(jnp.concatenate([grads[name].reshape(-1) for name, shape in entries]))
    shard_size = params.shape[0]
    row_index = lax.axis_index("row")
    total = lax.psum(flat, ("crop", "row"))
    shard = lax.dynamic_slice_in_dim(total, row_index * shard_size, shard_size)
    norm_squared = jnp.sum(total * total)
    clip_norm = jnp.sqrt(norm_squared)
    clipped = shard * (CLIP / jnp.maximum(clip_norm, CLIP))
    new_first = BETA_ONE * moment_one + (1.0 - BETA_ONE) * clipped
    new_second = BETA_TWO * moment_two + (1.0 - BETA_TWO) * clipped * clipped
    rates, decays = rate_tables(entries)
    rate_shard = lax.dynamic_slice_in_dim(jnp.asarray(rates), row_index * shard_size, shard_size)
    decay_shard = lax.dynamic_slice_in_dim(jnp.asarray(decays), row_index * shard_size, shard_size)
    first_hat = new_first / (1.0 - BETA_ONE**STEP)
    second_hat = new_second / (1.0 - BETA_TWO**STEP)
    new_params = params - rate_shard * (
        first_hat / (jnp.sqrt(second_hat) + ADAM_EPS) + decay_shard * params
    )
    return (
        pair_final.astype(jnp.bfloat16)[None],
        single_final.astype(jnp.bfloat16)[None],
        grad_pair[None],
        grad_single[None],
        new_params,
        new_first,
        new_second,
        clip_norm,
    )


F32 = jnp.float32
BF16 = jnp.bfloat16
LOG2E = 1.4426950408889634
VMEM_LIMIT = 56 * 1024 * 1024


def mm(left, right):
    return lax.dot_general(left, right, (((1,), (0,)), ((), ())), preferred_element_type=F32)


def mm_nt(left, right):
    return lax.dot_general(left, right, (((1,), (1,)), ((), ())), preferred_element_type=F32)


def mm_tn(left, right):
    return lax.dot_general(left, right, (((0,), (0,)), ((), ())), preferred_element_type=F32)


def standardize(values):
    centred = values - jnp.mean(values, axis=0, keepdims=True)
    spread = jnp.mean(centred * centred, axis=0, keepdims=True)
    inverse = lax.rsqrt(spread + EPSILON)
    return centred * inverse, inverse


def standardize_back(unit, inverse, grad_unit):
    first = jnp.mean(grad_unit, axis=0, keepdims=True)
    second = jnp.mean(grad_unit * unit, axis=0, keepdims=True)
    return inverse * (grad_unit - first - unit * second)


def sigmoid(values):
    return 0.5 * jnp.tanh(0.5 * values) + 0.5


def column(ref, index):
    return ref[:, index : index + 1]


def live_pair(info, alive, row):
    return jnp.concatenate(
        [jnp.where(info[row + place] > 0, alive[0:1], 0.0) for place in range(GROUP)], axis=1
    )


GROUP = 4
LAG = 4


def each_group(count, body):
    def step(index, carry):
        body(index * GROUP)
        return carry

    lax.fori_loop(0, count // GROUP, step, 0)


def each_channel(count, body):
    def step(index, carry):
        body(index)
        return carry

    lax.fori_loop(0, count, step, 0)


def join(read, ref, row):
    return jnp.concatenate([read(ref, row + place) for place in range(GROUP)], axis=1)


def pieces_of(values):
    length = values.shape[1] // GROUP
    return [values[:, place * length : (place + 1) * length] for place in range(GROUP)]


def put_rows(ref, row, values):
    for place, part in enumerate(pieces_of(values)):
        ref[row + place] = part.astype(ref.dtype)


def put_inner(scratch, row, values):
    for place, part in enumerate(pieces_of(values)):
        scratch[:, row + place, :] = part


def read_inner(scratch, row):
    return scratch[:, row, :]


def put_turned(scratch, row, values):
    for place, part in enumerate(pieces_of(values)):
        scratch[:, row + place, :] = part.T


def add_lanes(ref, values):
    ref[...] += sum(pieces_of(values))


def spec_full(shape):
    return pl.BlockSpec(shape, lambda step: (0,) * len(shape))


def cost(microseconds):
    return pl.CostEstimate(
        flops=int(microseconds * 1e9), bytes_accessed=int(microseconds * 3e6), transcendentals=0
    )


class Both(list):
    pass


def all_rows(ins, outs):
    extents = [shape[axis] for shape, dtype, axis in outs if axis is not None]
    for array, axis in ins:
        if isinstance(axis, int):
            extents += [member.shape[axis] for member in (array if isinstance(array, list) else [array])]
    return max(extents)


def run_rows(kernel, name, steps, ins, outs, scratch, time=15, half=None, before=None):
    grid = steps if half is None else steps // 2
    offset = grid * (half or 0)
    flat = []
    groups = []
    for array, axis in ins:
        members = array if isinstance(array, Both) else [array]
        flat += [(member, axis) for member in members]
        groups.append((len(members), isinstance(array, Both)))
    full = all_rows(flat, outs)

    def spec(shape, axis):
        if axis is None:
            return spec_full(shape)
        size = full // steps
        first = offset if shape[axis] == full else 0
        sizes = tuple(size if place == axis else extent for place, extent in enumerate(shape))
        return pl.BlockSpec(
            sizes,
            lambda step: tuple(step + first if place == axis else 0 for place in range(len(shape))),
        )

    in_specs = [
        pl.BlockSpec(memory_space=pltpu.SMEM) if axis == "smem" else spec(array.shape, axis)
        for array, axis in flat
    ]
    out_specs = [spec(shape, axis) for shape, dtype, axis in outs]
    arrays = [array for array, axis in flat]
    aliases = {}
    kept = []
    for place, (shape, dtype, axis) in enumerate(outs):
        if before is not None and (axis is None or shape[axis] == full):
            aliases[len(arrays)] = place
            kept.append(place)
            arrays.append(before[place])
            in_specs.append(spec_full(shape) if axis is None else pl.BlockSpec(memory_space=pl.ANY))

    def run(*refs):
        taken = iter(refs)
        given = []
        for number, together in groups:
            members = [next(taken) for _ in range(number)]
            given.append(members if together else members[0])
        held = {place: next(taken) for place in kept}
        results = [next(taken) for _ in outs]

        @pl.when(pl.program_id(0) == 0)
        def _():
            for place, (shape, dtype, axis) in enumerate(outs):
                if axis is None:
                    results[place][...] = (
                        held[place][...] if place in held else jnp.zeros(shape, dtype)
                    )

        kernel(*given, *results, *taken)

    return pl.pallas_call(
        run,
        grid=(grid,),
        in_specs=in_specs,
        out_specs=out_specs,
        out_shape=[jax.ShapeDtypeStruct(shape, dtype) for shape, dtype, axis in outs],
        scratch_shapes=[pltpu.VMEM(shape, dtype) for shape, dtype in scratch],
        input_output_aliases=aliases,
        compiler_params=pltpu.CompilerParams(vmem_limit_bytes=VMEM_LIMIT),
        cost_estimate=cost(time if half is None else time / 2),
        name=name,
    )(*arrays)


def run_halves(kernel, name, steps, ins, outs, scratch, time=15):
    results = []
    for half in range(2):
        chosen = [
            (array[half] if type(array) is list else array, axis) for array, axis in ins
        ]
        before = results[0] if half else None
        results.append(run_rows(kernel, name, steps, chosen, outs, scratch, time, half, before))
    full = all_rows(ins, outs)
    return [
        [results[0][place], results[1][place]]
        if axis is not None and shape[axis] != full
        else results[1][place]
        for place, (shape, dtype, axis) in enumerate(outs)
    ]


def zero_first(*refs):
    @pl.when(pl.program_id(0) == 0)
    def _():
        for ref in refs:
            ref[...] = jnp.zeros(ref.shape, ref.dtype)


def lane_sums(ref):
    return jnp.sum(ref[...].T, axis=0, keepdims=True)


def on_last(body):
    @pl.when(pl.program_id(0) == pl.num_programs(0) - 1)
    def _():
        body()


def read_plain(ref, row):
    return ref[row].astype(F32)


def reorder(values, order):
    size = values.shape[0] // len(order)
    return jnp.concatenate([values[place * size : (place + 1) * size] for place in order], axis=0)


def read_tokens(order, ref, row):
    return reorder(ref[row].astype(F32), order).T


def read_flipped(refs, row):
    parts = jnp.concatenate([ref[:, row] for ref in refs], axis=1)
    return parts.reshape(-1, parts.shape[-1]).astype(F32).T


def read_turned(order, ref, row):
    parts = ref[:, row]
    return reorder(parts.reshape(-1, parts.shape[-1]).astype(F32), order).T


def tri_pre_row(info, alive, row, state, cols, first, proj_t):
    unit, inverse = standardize(state)
    lowered = (unit * column(cols, first) + column(cols, first + 1)).astype(BF16)
    project = mm(proj_t[...], lowered)
    half = project.shape[0] // 2
    return project[:half] * sigmoid(project[half:]) * live_pair(info, alive, row)


def store_product(out, scratch, devices):
    hidden = scratch.shape[0] // 2
    part = hidden // devices

    def one(device, carry):
        out[device, 0] = scratch[pl.ds(device * part, part)].astype(BF16)
        out[device, 1] = scratch[pl.ds(hidden + device * part, part)].astype(BF16)
        return carry

    lax.fori_loop(0, devices, one, 0)


def copy_blocks(target, source, count):
    def one(index, carry):
        target[index] = source[index].astype(target.dtype)
        return carry

    lax.fori_loop(0, count, one, 0)


def store_flipped(out, scratch):
    devices, part = out.shape[0], out.shape[1]

    def one(device, carry):
        out[device] = scratch[pl.ds(device * part, part)].astype(out.dtype)
        return carry

    lax.fori_loop(0, devices, one, 0)


def tri_post_row(state, tri, cols, proj_t, gate_t):
    unit, inverse = standardize(state)
    lowered = (unit * column(cols, 0) + column(cols, 1)).astype(BF16)
    tri_unit, tri_inverse = standardize(tri)
    out_low = (tri_unit * column(cols, 2) + column(cols, 3)).astype(BF16)
    output = mm(proj_t[...], out_low)
    gate = sigmoid(mm(gate_t[...], lowered))
    return unit, inverse, lowered, tri_unit, tri_inverse, out_low, output, gate


def row_base(rows):
    return pl.program_id(0) * rows


def tri_pre_first_kernel(devices, read, info, alive, pair, cols, proj_t, out, scratch):
    rows = pair.shape[0]

    def body(row):
        product = tri_pre_row(
            info, alive, row_base(rows) + row, join(read, pair, row), cols, 0, proj_t
        )
        put_inner(scratch, row, product)

    each_group(rows, body)
    store_product(out, scratch, devices)


def whole_rows(refs, *place):
    parts = jnp.concatenate([ref[(slice(None),) + place] for ref in refs], axis=1)
    return parts.reshape(-1, parts.shape[-1])


def split_rows(values, outs, *place):
    part = outs[0].shape[-2]
    parts = values.astype(BF16).reshape(outs[0].shape[0], -1, values.shape[-1])
    for half, out in enumerate(outs):
        out[(slice(None),) + place] = parts[:, half * part : (half + 1) * part]


def tri_product_kernel(incoming, operands, *outs):
    def body(channel):
        first = whole_rows(operands, 0, channel)
        second = whole_rows(operands, 1, channel)
        tri = mm_tn(first, second) if incoming else mm_nt(first, second)
        split_rows(tri, outs, channel)

    each_channel(operands[0].shape[2], body)


def tri_join_kernel(
    devices, read, info, alive, source, tri_in, cols, proj_t, gate_t, next_cols, next_proj_t,
    state_out, out, tri_scratch, scratch,
):
    rows = state_out.shape[0]
    copy_blocks(tri_scratch, tri_in, tri_in.shape[0])

    def body(row):
        state = join(read, source, row)
        pieces = tri_post_row(state, join(read_inner, tri_scratch, row), cols, proj_t, gate_t)
        state = state + pieces[6] * pieces[7]
        put_rows(state_out, row, state)
        product = tri_pre_row(
            info, alive, row_base(rows) + row, state, next_cols, 0, next_proj_t
        )
        put_inner(scratch, row, product)

    each_group(rows, body)
    store_product(out, scratch, devices)


def tri_last_kernel(
    source, tri_in, cols, proj_t, gate_t, next_cols, bias_t, state_out, bias_out, tri_scratch, scratch
):
    rows = state_out.shape[0]
    copy_blocks(tri_scratch, tri_in, tri_in.shape[0])

    def body(row):
        state = join(read_plain, source, row)
        pieces = tri_post_row(state, join(read_inner, tri_scratch, row), cols, proj_t, gate_t)
        state = state + pieces[6] * pieces[7]
        put_rows(state_out, row, state)
        unit, inverse = standardize(state)
        lowered = (unit * column(next_cols, 0) + column(next_cols, 1)).astype(BF16)
        put_inner(scratch, row, mm(bias_t[...], lowered))

    each_group(rows, body)
    bias_out[...] = scratch[: bias_out.shape[0]].astype(BF16)


def flipped_bias_kernel(source, cols, bias_t, bias_out, scratch):
    rows = source[0].shape[1]

    def body(row):
        unit, inverse = standardize(join(read_flipped, source, row))
        lowered = (unit * column(cols, 0) + column(cols, 1)).astype(BF16)
        put_inner(scratch, row, mm(bias_t[...], lowered))

    each_group(rows, body)
    bias_out[...] = scratch[: bias_out.shape[0]].astype(BF16)


def fill_bias(alive, bias_in, table):
    @pl.when(pl.program_id(0) == 0)
    def _():
        length = table.shape[1]
        penalty = (alive[0:1] - 1.0) * (MASKED * LOG2E)
        for head in range(table.shape[0]):
            values = bias_in[:, head].reshape(length, length).astype(F32)
            table[head] = (values * LOG2E + penalty).T


def attention_row(state, cols, proj_t):
    unit, inverse = standardize(state)
    lowered = (unit * column(cols, 0) + column(cols, 1)).astype(BF16)
    project = mm(proj_t[...], lowered)
    width = project.shape[0] // 4
    size = width // TA_HEADS
    query = (project[:width] * (size**-0.5 * LOG2E)).astype(BF16)
    key = project[width : 2 * width].astype(BF16)
    value = project[2 * width : 3 * width].astype(BF16)
    gate = sigmoid(project[3 * width :])
    return unit, inverse, lowered, query, key, value, gate


def in_stages(blocks, first, second, third):
    early, late, done = {}, {}, {}
    count = len(blocks)
    for step in range(count + 2 * LAG):
        if step < count:
            early[step] = first(*blocks[step])
        if 0 <= step - LAG < count:
            late[step - LAG] = second(*blocks[step - LAG], early.pop(step - LAG))
        if 0 <= step - 2 * LAG < count:
            place = step - 2 * LAG
            done[blocks[place]] = third(*blocks[place], late.pop(place))
    return done


def head_rows(values, place, head):
    size, length = values.shape[0] // TA_HEADS, values.shape[1] // GROUP
    return values[head * size : (head + 1) * size, place * length : (place + 1) * length]


def gather_heads(done):
    return jnp.concatenate(
        [
            jnp.concatenate([done[place, head] for head in range(TA_HEADS)], axis=0)
            for place in range(GROUP)
        ],
        axis=1,
    )


ROW_BLOCKS = [(place, head) for place in range(GROUP) for head in range(TA_HEADS)]
HEAD_BLOCKS = [(place, head) for head in range(TA_HEADS) for place in range(GROUP)]


def attend_rows(state, row, cols, proj_t, output_t, table, totals, mixed_out):
    unit, inverse, lowered, query, key, value, gate = attention_row(state, cols, proj_t)

    def score(place, head):
        return mm_tn(head_rows(key, place, head), head_rows(query, place, head)) + table[head]

    def shift(place, head, scores):
        top = jnp.max(scores, axis=0, keepdims=True)
        return top, jnp.exp2(scores - top).astype(BF16)

    def mix(place, head, items):
        top, shifted = items
        values = head_rows(value, place, head)
        size = values.shape[0]
        values = jnp.concatenate([values, jnp.ones((16, values.shape[1]), BF16)], axis=0)
        result = mm(values, shifted)
        total = result[size : size + 1]
        return result[:size] / total, top + jnp.log2(total)

    done = in_stages(ROW_BLOCKS, score, shift, mix)
    mixed = gather_heads({block: items[0] for block, items in done.items()})
    put_rows(totals, row, gather_heads({block: items[1] for block, items in done.items()}))
    put_rows(mixed_out, row, mixed)
    return state + mm(output_t[...], (mixed * gate).astype(BF16))


def starting_kernel(
    alive, source, bias_in, cols, proj_t, output_t, out, totals, mixed, table, scratch
):
    fill_bias(alive, bias_in, table)
    rows = source.shape[0]

    def body(row):
        state = attend_rows(
            join(read_plain, source, row), row, cols, proj_t, output_t, table, totals, mixed
        )
        put_turned(scratch, row, state)

    each_group(rows, body)
    store_flipped(out, scratch)


def ending_kernel(alive, source, bias_in, cols, proj_t, output_t, out, totals, mixed, table):
    fill_bias(alive, bias_in, table)
    rows = source[0].shape[1]

    def body(row):
        state = attend_rows(
            join(read_flipped, source, row), row, cols, proj_t, output_t, table, totals, mixed
        )
        put_rows(out, row, state)

    each_group(rows, body)


def transition_kernel(
    order, source, cols, up_t, down_t, next_cols, bias_t, state_out, pair_out, bias_out, scratch, bias_scratch
):
    rows = source.shape[0]

    def body(row):
        state = join(read_plain, source, row)
        unit, inverse = standardize(state)
        lowered = (unit * column(cols, 0) + column(cols, 1)).astype(BF16)
        hidden = mm(up_t[...], lowered)
        half = hidden.shape[0] // 2
        first = hidden[:half]
        mixed = (first * sigmoid(first) * hidden[half:]).astype(BF16)
        state = state + mm(down_t[...], mixed)
        put_rows(state_out, row, state)
        put_turned(scratch, row, state)
        unit, inverse = standardize(state)
        lowered = (unit * column(next_cols, 0) + column(next_cols, 1)).astype(BF16)
        put_inner(bias_scratch, row, mm(bias_t[...], lowered))

    each_group(rows, body)
    size = pair_out.shape[0] // len(order)
    for place, held in enumerate(order):
        pair_out[place * size : (place + 1) * size] = scratch[held * size : (held + 1) * size].astype(BF16)
    bias_out[...] = bias_scratch[...].astype(BF16)


def transition_back_kernel(
    read, mid, final, cotangent, bias_grad, cols, up_t, up, down, next_cols, bias_w,
    grad_out, up_grad, down_grad, bias_w_grad, vecs, norm_gain, norm_bias, pair_gain, pair_bias, bias_scratch,
):
    zero_first(norm_gain, norm_bias, pair_gain, pair_bias)
    rows = mid.shape[0]
    bias_scratch[...] = bias_grad[...].astype(F32)

    def body(row):
        grad = join(read, cotangent, row)
        unit, inverse = standardize(join(read_plain, final, row))
        gain = column(next_cols, 0)
        lowered = (unit * gain + column(next_cols, 1)).astype(BF16)
        grad_bias = join(read_inner, bias_scratch, row).astype(BF16)
        bias_w_grad[...] += mm_nt(lowered, grad_bias)
        grad_lowered = mm(bias_w[...], grad_bias)
        add_lanes(pair_gain, grad_lowered * unit)
        add_lanes(pair_bias, grad_lowered)
        grad = grad + standardize_back(unit, inverse, grad_lowered * gain)
        unit, inverse = standardize(join(read_plain, mid, row))
        gain = column(cols, 0)
        lowered = (unit * gain + column(cols, 1)).astype(BF16)
        hidden = mm(up_t[...], lowered)
        half = hidden.shape[0] // 2
        first, second = hidden[:half], hidden[half:]
        slope = sigmoid(first)
        silu = first * slope
        grad_low = grad.astype(BF16)
        grad_mixed = mm(down[...], grad_low)
        down_grad[...] += mm_nt((silu * second).astype(BF16), grad_low)
        grad_hidden = jnp.concatenate(
            [
                (grad_mixed * second * (slope + silu * (1.0 - slope))).astype(BF16),
                (grad_mixed * silu).astype(BF16),
            ],
            axis=0,
        )
        up_grad[...] += mm_nt(lowered, grad_hidden)
        grad_lowered = mm(up[...], grad_hidden)
        add_lanes(norm_gain, grad_lowered * unit)
        add_lanes(norm_bias, grad_lowered)
        put_rows(grad_out, row, grad + standardize_back(unit, inverse, grad_lowered * gain))

    each_group(rows, body)

    def finish():
        vecs[0:1] += lane_sums(norm_gain)
        vecs[1:2] += lane_sums(norm_bias)
        vecs[2:3] += lane_sums(pair_gain)
        vecs[3:4] += lane_sums(pair_bias)

    on_last(finish)


def attention_back_kernel(
    read, read_grad, alive, source, grad_in, bias_in, totals, mixed_in, cols, proj_t, proj, output,
    grad_out, bias_out, proj_grad, output_grad, table, grad_table,
):
    fill_bias(alive, bias_in, table)
    zero_first(grad_table)
    rows = grad_out.shape[0]

    def body(row):
        unit, inverse, lowered, query, key, value, gate = attention_row(
            join(read, source, row), cols, proj_t
        )
        mixed = join(read_plain, mixed_in, row)
        total = join(read_plain, totals, row)
        grad_low = join(read_grad, grad_in, row).astype(BF16)
        gated = mixed * gate
        output_grad[...] += mm_nt(gated.astype(BF16), grad_low)
        grad_gated = mm(output[...], grad_low)
        grad_gate = grad_gated * gated * (1.0 - gate)
        grad_mixed = (grad_gated * gate).astype(BF16)
        product = grad_mixed.astype(F32) * mixed
        size = query.shape[0] // TA_HEADS

        def score(place, head):
            scores = mm_tn(head_rows(key, place, head), head_rows(query, place, head))
            grads = mm_tn(head_rows(value, place, head), head_rows(grad_mixed, place, head))
            return scores + table[head], grads

        def slope(place, head, items):
            scores, grads = items
            probs = jnp.exp2(scores - head_rows(total, place, head))
            delta = jnp.sum(head_rows(product, place, head), axis=0, keepdims=True)
            grad_scores = probs * (grads - delta)
            grad_table[head] += grad_scores
            return probs.astype(BF16), grad_scores.astype(BF16)

        def back(place, head, items):
            probs, grad_scores = items
            return (
                mm(head_rows(key, place, head), grad_scores) * size**-0.5,
                mm_nt(head_rows(query, place, head), grad_scores) * (1.0 / LOG2E),
                mm_nt(head_rows(grad_mixed, place, head), probs),
            )

        done = in_stages(HEAD_BLOCKS, score, slope, back)
        grad_project = jnp.concatenate(
            [
                gather_heads({block: items[part] for block, items in done.items()})
                for part in range(3)
            ]
            + [grad_gate],
            axis=0,
        ).astype(BF16)
        proj_grad[...] += mm_nt(lowered, grad_project)
        put_rows(grad_out, row, mm(proj[...], grad_project))

    each_group(rows, body)

    def finish():
        for head in range(TA_HEADS):
            bias_out[:, head] = (
                grad_table[head].T.astype(BF16).reshape(bias_out.shape[0], bias_out.shape[2], -1)
            )

    on_last(finish)


def attention_end_row(
    state, grad, grad_lowered, grad_bias, cols, bias_w, bias_w_grad, norm_gain, norm_bias
):
    unit, inverse = standardize(state)
    gain = column(cols, 0)
    lowered = (unit * gain + column(cols, 1)).astype(BF16)
    bias_w_grad[...] += mm_nt(lowered, grad_bias)
    grad_lowered = grad_lowered + mm(bias_w[...], grad_bias)
    add_lanes(norm_gain, grad_lowered * unit)
    add_lanes(norm_bias, grad_lowered)
    return grad + standardize_back(unit, inverse, grad_lowered * gain)


def fill_bias_grad(scratch, bias_grad):
    heads = bias_grad.shape[1]
    total = bias_grad[0].astype(F32)
    for device in range(1, bias_grad.shape[0]):
        total = total + bias_grad[device].astype(F32)
    scratch[:heads] = total
    scratch[heads:] = jnp.zeros((scratch.shape[0] - heads,) + scratch.shape[1:], F32)


def ending_end_kernel(
    source, grad_in, grad_lowered, bias_grad, cols, bias_w,
    grad_out, bias_w_grad, vecs, norm_gain, norm_bias, bias_scratch, scratch,
):
    zero_first(norm_gain, norm_bias)
    fill_bias_grad(bias_scratch, bias_grad)
    rows = grad_in.shape[0]

    def body(row):
        grad = attention_end_row(
            join(read_flipped, source, row), join(read_plain, grad_in, row),
            join(read_plain, grad_lowered, row), join(read_inner, bias_scratch, row).astype(BF16), cols, bias_w, bias_w_grad, norm_gain, norm_bias,
        )
        put_turned(scratch, row, grad)

    each_group(rows, body)
    store_flipped(grad_out, scratch)

    def finish():
        vecs[0:1] += lane_sums(norm_gain)
        vecs[1:2] += lane_sums(norm_bias)

    on_last(finish)


def tri_post_back_row(
    state, tri, grad, cols, proj_t, gate_t, proj, gate_w, proj_grad, gate_grad, out_gain, out_bias
):
    unit, inverse, lowered, tri_unit, tri_inverse, out_low, output, gate = tri_post_row(
        state, tri, cols, proj_t, gate_t
    )
    grad_output = grad * gate
    grad_gate = (grad_output * output * (1.0 - gate)).astype(BF16)
    grad_output = grad_output.astype(BF16)
    proj_grad[...] += mm_nt(out_low, grad_output)
    gate_grad[...] += mm_nt(lowered, grad_gate)
    grad_normed = mm(proj[...], grad_output)
    add_lanes(out_gain, grad_normed * tri_unit)
    add_lanes(out_bias, grad_normed)
    grad_tri = standardize_back(tri_unit, tri_inverse, grad_normed * column(cols, 2))
    return grad_tri, mm(gate_w[...], grad_gate)


def starting_end_kernel(
    source, grad_in, grad_lowered, bias_grad, cols, bias_w,
    below, tri_in, tri_cols, proj_t, gate_t, proj, gate_w,
    grad_out, tri_out, gate_back, bias_w_grad, proj_grad, gate_grad, vecs,
    norm_gain, norm_bias, out_gain, out_bias, bias_scratch, tri_scratch,
):
    zero_first(norm_gain, norm_bias, out_gain, out_bias)
    fill_bias_grad(bias_scratch, bias_grad)
    copy_blocks(tri_scratch, tri_in, tri_in.shape[0])
    rows = source.shape[0]

    def body(row):
        grad = attention_end_row(
            join(read_plain, source, row), join(read_flipped, grad_in, row),
            join(read_plain, grad_lowered, row), join(read_inner, bias_scratch, row).astype(BF16), cols, bias_w, bias_w_grad, norm_gain, norm_bias,
        )
        put_rows(grad_out, row, grad)
        grad_tri, back = tri_post_back_row(
            join(read_plain, below, row), join(read_inner, tri_scratch, row), grad, tri_cols, proj_t, gate_t, proj, gate_w,
            proj_grad, gate_grad, out_gain, out_bias,
        )
        put_rows(gate_back, row, back)
        put_inner(tri_scratch, row, grad_tri)

    each_group(rows, body)
    copy_blocks(tri_out, tri_scratch, tri_out.shape[0])

    def finish():
        vecs[0:1] += lane_sums(norm_gain)
        vecs[1:2] += lane_sums(norm_bias)
        vecs[2:3] += lane_sums(out_gain)
        vecs[3:4] += lane_sums(out_bias)

    on_last(finish)


def tri_product_back_kernel(incoming, grad, operands, *outs):
    def body(channel):
        first = whole_rows(operands, 0, channel)
        second = whole_rows(operands, 1, channel)
        tri = whole_rows(grad, channel)
        if incoming:
            grad_first = mm_nt(second, tri)
            grad_second = mm(first, tri)
        else:
            grad_first = mm(tri, second)
            grad_second = mm_tn(tri, first)
        split_rows(grad_first, outs, 0, channel)
        split_rows(grad_second, outs, 1, channel)

    each_channel(operands[0].shape[2], body)


def tri_pre_back_row(
    info, alive, row, state, product_grad, gate_back, grad, cols, proj_t, proj, proj_grad, norm_gain, norm_bias
):
    unit, inverse = standardize(state)
    gain = column(cols, 0)
    lowered = (unit * gain + column(cols, 1)).astype(BF16)
    project = mm(proj_t[...], lowered)
    half = project.shape[0] // 2
    gate = sigmoid(project[half:])
    grad_first = product_grad * gate * live_pair(info, alive, row)
    grad_second = grad_first * project[:half] * (1.0 - gate)
    grad_project = jnp.concatenate([grad_first.astype(BF16), grad_second.astype(BF16)], axis=0)
    proj_grad[...] += mm_nt(lowered, grad_project)
    grad_lowered = mm(proj[...], grad_project) + gate_back
    add_lanes(norm_gain, grad_lowered * unit)
    add_lanes(norm_bias, grad_lowered)
    return grad + standardize_back(unit, inverse, grad_lowered * gain)


def fill_product_grad(scratch, product_grad):
    devices, part = product_grad.shape[0], product_grad.shape[2]

    def one(device, carry):
        scratch[pl.ds(device * part, part)] = product_grad[device, 0].astype(F32)
        scratch[pl.ds((devices + device) * part, part)] = product_grad[device, 1].astype(F32)
        return carry

    lax.fori_loop(0, devices, one, 0)


def tri_join_back_kernel(
    read, info, alive, source, product_grad, gate_in, grad_in, cols, proj_t, proj,
    below, tri_in, tri_cols, out_t, gate_t, out_w, gate_w,
    grad_out, tri_out, gate_back, proj_grad, out_grad, gate_grad, vecs,
    norm_gain, norm_bias, out_gain, out_bias, scratch, tri_scratch,
):
    zero_first(norm_gain, norm_bias, out_gain, out_bias)
    fill_product_grad(scratch, product_grad)
    copy_blocks(tri_scratch, tri_in, tri_in.shape[0])
    rows = source.shape[0]

    def body(row):
        grad = tri_pre_back_row(
            info, alive, row_base(rows) + row, join(read_plain, source, row),
            join(read_inner, scratch, row), join(read_plain, gate_in, row),
            join(read_plain, grad_in, row), cols, proj_t, proj, proj_grad, norm_gain, norm_bias,
        )
        put_rows(grad_out, row, grad)
        grad_tri, back = tri_post_back_row(
            join(read, below, row), join(read_inner, tri_scratch, row), grad, tri_cols, out_t, gate_t, out_w, gate_w,
            out_grad, gate_grad, out_gain, out_bias,
        )
        put_rows(gate_back, row, back)
        put_inner(tri_scratch, row, grad_tri)

    each_group(rows, body)
    copy_blocks(tri_out, tri_scratch, tri_out.shape[0])

    def finish():
        vecs[0:1] += lane_sums(norm_gain)
        vecs[1:2] += lane_sums(norm_bias)
        vecs[2:3] += lane_sums(out_gain)
        vecs[3:4] += lane_sums(out_bias)

    on_last(finish)


def tri_first_back_kernel(
    read, order, info, alive, source, product_grad, gate_in, grad_in, cols, proj_t, proj,
    grad_out, proj_grad, vecs, norm_gain, norm_bias, scratch,
):
    zero_first(norm_gain, norm_bias)
    fill_product_grad(scratch, product_grad)
    rows = source.shape[0]

    def body(row):
        grad = tri_pre_back_row(
            info, alive, row_base(rows) + row, join(read, source, row),
            join(read_inner, scratch, row), join(read_plain, gate_in, row),
            join(read_plain, grad_in, row), cols, proj_t, proj, proj_grad, norm_gain, norm_bias,
        )
        for place, part in enumerate(pieces_of(grad)):
            grad_out[row + place] = reorder(part.T, order).astype(grad_out.dtype)

    each_group(rows, body)

    def finish():
        vecs[0:1] += lane_sums(norm_gain)
        vecs[1:2] += lane_sums(norm_bias)

    on_last(finish)


RUN = 24


def table_of(entries):
    table = {}
    offset = 0
    for name, shape in entries:
        table[name] = (offset // STRIDE, shape)
        offset += math.prod(shape)
    return table, offset


def runs_kernel(info, shard, out, scratch):
    def one(block, carry):
        scratch[:, block, :] = shard[pl.ds(block * STRIDE, STRIDE), :].T
        return carry

    lax.fori_loop(0, RUN, one, 0)
    half = STRIDE // 2
    turn = info[0] * half

    def move(lane, carry):
        out[lane] = scratch[lax.rem(lane + turn, STRIDE)].astype(BF16)
        return carry

    lax.fori_loop(0, STRIDE, move, 0)


def run_place(shards, total, lane, shard):
    count = total // STRIDE
    whole = total // shards
    step, odd = whole // STRIDE, (whole % STRIDE) // (STRIDE // 2)
    extra = lax.div(shard * odd + jnp.where(lane < STRIDE // 2, 1, 0), 2)
    start = lane * count + shard * step + extra
    return lax.div(start, STRIDE), lax.rem(start, STRIDE)


def rows_from_runs(runs, rows, first_lane, total):
    shards, lanes = runs.shape[0], runs.shape[1]
    base = first_lane * (total // STRIDE) // STRIDE

    def one(index, carry):
        lane, shard = lax.div(index, shards), lax.rem(index, shards)
        row, shift = run_place(shards, total, first_lane + lane, shard)
        row = row - base
        turned = pltpu.roll(runs[shard, lane].astype(F32), shift, 1)
        place = lax.broadcasted_iota(jnp.int32, (RUN + 1, STRIDE), 1)
        last, before = carry
        joint = jnp.where(row - before == RUN, last[2:3], last[1:2])
        below = jnp.concatenate([joint, turned], axis=0)
        above = jnp.concatenate([turned, turned[RUN - 1 :]], axis=0)
        values = jnp.where(place < shift, below, above)
        rows[pl.ds(row, RUN + 1), :] = values
        return values[RUN - 2 :], row

    lax.fori_loop(0, shards * lanes, one, (jnp.zeros((3, STRIDE), F32), -RUN), unroll=4)


def runs_from_rows(rows, out, first_lane, base, total):
    shards, lanes = out.shape[0], out.shape[1]

    def one(index, carry):
        lane, shard = lax.div(index, shards), lax.rem(index, shards)
        row, shift = run_place(shards, total, first_lane + lane, shard)
        turned = pltpu.roll(rows[pl.ds(row - base, RUN + 1), :], (STRIDE - shift) % STRIDE, 1)
        place = lax.broadcasted_iota(jnp.int32, (RUN, STRIDE), 1)
        out[shard, lane] = jnp.where(
            place < STRIDE - shift, turned[:RUN], turned[1:]
        ).astype(BF16)
        return carry

    lax.fori_loop(0, shards * lanes, one, 0, unroll=4)


def row_height(base, first_lane, last_lane, total):
    end = (last_lane * (total // STRIDE)) // STRIDE + RUN + 2
    return -(-(end - base) // 8) * 8


def take_matrix(rows, first, shape):
    blocks = shape[1] // STRIDE
    return [
        rows[pl.ds(first + block, shape[0], stride=blocks), :]
        if blocks > 1
        else rows[first : first + shape[0], :]
        for block in range(blocks)
    ]


def put_matrix(rows, first, matrix):
    height, width = matrix.shape
    blocks = width // STRIDE
    for block in range(blocks):
        part = matrix[:, block * STRIDE : (block + 1) * STRIDE]
        if blocks > 1:
            rows[pl.ds(first + block, height, stride=blocks), :] = part
        else:
            rows[first : first + height, :] = part


def spread(index, heads, rows):
    lane = lax.broadcasted_iota(jnp.int32, (STRIDE, STRIDE), 0)
    channel = lax.broadcasted_iota(jnp.int32, (STRIDE, STRIDE), 1)
    return (channel == index * (STRIDE // heads) + lane // heads).astype(BF16)


def take_narrow(rows, first, heads, high):
    total = jnp.zeros((high, STRIDE), F32)
    head = lax.broadcasted_iota(jnp.int32, (high, STRIDE), 0)
    lane = lax.broadcasted_iota(jnp.int32, (high, STRIDE), 1)
    for index in range(heads):
        line = rows[first + index : first + index + 1, :]
        picked = jnp.where(lane % heads == head, line, 0.0).astype(BF16)
        total = total + mm(picked, spread(index, heads, rows))
    return total


def put_narrow(rows, first, heads, matrix):
    turned = matrix.T.astype(BF16)
    high = turned.shape[0]
    head = lax.broadcasted_iota(jnp.int32, (high, STRIDE), 0)
    lane = lax.broadcasted_iota(jnp.int32, (high, STRIDE), 1)
    for index in range(heads):
        wide = mm_nt(turned, spread(index, heads, rows))
        rows[first + index : first + index + 1, :] = jnp.sum(
            jnp.where(lane % heads == head, wide, 0.0), axis=0, keepdims=True
        )


PAIR_MATRICES = (
    (OUTGOING, PROJ_GATE), (OUTGOING, PROJ_OUT), (OUTGOING, GATE_OUT),
    (INCOMING, PROJ_GATE), (INCOMING, PROJ_OUT), (INCOMING, GATE_OUT),
    (STARTING, QKVG), (STARTING, OUTPUT), (ENDING, QKVG), (ENDING, OUTPUT), (PAIR, UP), (PAIR, DOWN),
)
PAIR_COLUMNS = (
    (OUTGOING, ((OUTGOING, NORM_GAIN), (OUTGOING, NORM_BIAS), (OUTGOING, OUT_GAIN), (OUTGOING, OUT_BIAS))),
    (INCOMING, ((INCOMING, NORM_GAIN), (INCOMING, NORM_BIAS), (INCOMING, OUT_GAIN), (INCOMING, OUT_BIAS))),
    (STARTING, ((STARTING, NORM_GAIN), (STARTING, NORM_BIAS))),
    (ENDING, ((ENDING, NORM_GAIN), (ENDING, NORM_BIAS))),
    (PAIR, ((PAIR, NORM_GAIN), (PAIR, NORM_BIAS))),
)
SINGLE_MATRICES = ((ATTEND, QKVG), (ATTEND, OUTPUT), (SINGLE, UP), (SINGLE, DOWN))
SINGLE_VECTORS = ((ATTEND, NORM_GAIN), (ATTEND, NORM_BIAS), (SINGLE, NORM_GAIN), (SINGLE, NORM_BIAS))


def put_columns(rows, out, table, base, names):
    out[...] = jnp.zeros(out.shape, F32)
    lines = [rows[table[name][0] - base : table[name][0] - base + 1, :] for name in names]
    lines.append(jnp.zeros((8 - len(lines), STRIDE), F32))
    out[...] = jnp.concatenate(lines, axis=0).T


def unpack_pair_kernel(table, total, runs, *refs):
    rows = refs[-1]
    outs = list(refs[:-1])
    rows_from_runs(runs, rows, 0, total)
    for name in PAIR_MATRICES:
        first, shape = table[name]
        plain, turned = outs.pop(0), outs.pop(0)
        for block, part in enumerate(take_matrix(rows, first, shape)):
            place = slice(block * STRIDE, (block + 1) * STRIDE)
            plain[:, place] = part.astype(BF16)
            turned[place, :] = part.T.astype(BF16)
    for prefix in (STARTING, ENDING):
        plain, turned = outs.pop(0), outs.pop(0)
        first, shape = table[(prefix, BIAS_PROJ)]
        matrix = take_narrow(rows, first, shape[1], 8)
        turned[...] = matrix.astype(BF16)
        plain[...] = matrix.T.astype(BF16)
    for prefix, names in PAIR_COLUMNS:
        put_columns(rows, outs.pop(0), table, 0, names)


def unpack_single_kernel(table, total, first_lane, runs, *refs):
    rows = refs[-1]
    outs = list(refs[:-1])
    rows_from_runs(runs, rows, first_lane, total)
    base = first_lane * (total // STRIDE) // STRIDE
    for name in SINGLE_MATRICES:
        first, shape = table[name]
        out = outs.pop(0)
        for block, part in enumerate(take_matrix(rows, first - base, shape)):
            out[:, block * STRIDE : (block + 1) * STRIDE] = part.astype(BF16)
    first, shape = table[(ATTEND, PAIR_PROJ)]
    matrix = take_narrow(rows, first - base, shape[1], shape[1])
    plain, turned = outs.pop(0), outs.pop(0)
    turned[...] = matrix.astype(BF16)
    plain[...] = matrix.T.astype(BF16)
    put_columns(rows, outs.pop(0), table, base, ((ATTEND, PAIR_GAIN), (ATTEND, PAIR_BIAS)))
    lines = outs.pop(0)
    lines[...] = jnp.zeros(lines.shape, F32)
    for index, name in enumerate(SINGLE_VECTORS):
        first, shape = table[name]
        for block in range(shape[0] // STRIDE):
            lines[index : index + 1, block * STRIDE : (block + 1) * STRIDE] = rows[
                first - base + block : first - base + block + 1, :
            ]


def pack_kernel(table, total, first_lane, base, names, *refs):
    ins, out, rows = refs[: len(names)], refs[-2], refs[-1]
    for name, ref in zip(names, ins):
        if isinstance(name, tuple):
            first, shape = table[name]
            if shape[1] % STRIDE:
                put_narrow(rows, first - base, shape[1], ref[...])
            else:
                put_matrix(rows, first - base, ref)
        else:
            for index, vector in name:
                first, shape = table[vector]
                for block in range(shape[0] // STRIDE):
                    rows[first + block - base : first + block - base + 1, :] = ref[
                        index : index + 1, block * STRIDE : (block + 1) * STRIDE
                    ]
    runs_from_rows(rows, out, first_lane, base, total)


def shard_kernel(whole, info, summed, others, out, squares, runs):
    half = STRIDE // 2
    crops, first, part = summed.shape[0], summed.shape[1], others.shape[1]

    def add(lane, carry):
        runs[lane] = sum(summed[crop, lane].astype(F32) for crop in range(crops))
        return carry

    lax.fori_loop(0, first, add, 0)
    for crop in range(crops):

        def move(lane, carry, crop=crop):
            runs[first + crop * part + lane] = others[crop, lane].astype(F32)
            return carry

        lax.fori_loop(0, part, move, 0)
    squares[...] = jnp.zeros(squares.shape, F32)

    def one(block, carry):
        first = runs[pl.ds(info[0] * half, half), block, :]
        second = runs[pl.ds(half - info[0] * half, half), block, :]
        values = jnp.concatenate([first, second], axis=0).T
        row = block * STRIDE + lax.broadcasted_iota(jnp.int32, values.shape, 0)
        lane = lax.broadcasted_iota(jnp.int32, values.shape, 1)
        values = jnp.where(row * STRIDE + lane < whole, values, 0.0)
        out[pl.ds(block * STRIDE, STRIDE), :] = values
        squares[...] += jnp.sum((values * values).reshape(-1, 8, STRIDE), axis=0)
        return carry

    lax.fori_loop(0, RUN, one, 0)


def whole_call(kernel, name, ins, outs, scratch, time=8):
    def spec(axis):
        return pl.BlockSpec(memory_space=pltpu.SMEM if axis == "smem" else pltpu.VMEM)

    return pl.pallas_call(
        kernel,
        in_specs=[spec(axis) for array, axis in ins],
        out_specs=[pl.BlockSpec(memory_space=pltpu.VMEM) for shape, dtype in outs],
        out_shape=[jax.ShapeDtypeStruct(shape, dtype) for shape, dtype in outs],
        scratch_shapes=[pltpu.VMEM(shape, dtype) for shape, dtype in scratch],
        compiler_params=pltpu.CompilerParams(vmem_limit_bytes=VMEM_LIMIT),
        cost_estimate=cost(time),
        name=name,
    )(*[array for array, axis in ins])


def unpack_pair(table, total, runs):
    outs = []
    names = []
    for name in PAIR_MATRICES:
        shape = table[name][1]
        outs += [(shape, BF16), (shape[::-1], BF16)]
        names += [name, (name, T)]
    for prefix in (STARTING, ENDING):
        outs += [((STRIDE, 8), BF16), ((8, STRIDE), BF16)]
        names += [(prefix, BIAS_W), (prefix, BIAS_T)]
    for prefix, parts in PAIR_COLUMNS:
        outs.append(((STRIDE, 8), F32))
        names.append((prefix, COLS))
    height = row_height(0, 0, runs.shape[1], total)
    values = whole_call(
        functools.partial(unpack_pair_kernel, table, total), "pair_weights", [(runs, None)], outs,
        [((height, STRIDE), F32)],
    )
    return dict(zip(names, values))


def unpack_single(table, total, first_lane, runs):
    outs = [(table[name][1], BF16) for name in SINGLE_MATRICES]
    names = list(SINGLE_MATRICES)
    shape = table[(ATTEND, PAIR_PROJ)][1]
    outs += [(shape, BF16), (shape[::-1], BF16), ((STRIDE, 8), F32), ((8, S), F32)]
    names += [(ATTEND, PAIR_PROJ), ((ATTEND, PAIR_PROJ), T), (ATTEND, COLS), (SINGLE, VECTORS)]
    base = first_lane * (total // STRIDE) // STRIDE
    height = row_height(base, first_lane, first_lane + runs.shape[1], total)
    values = whole_call(
        functools.partial(unpack_single_kernel, table, total, first_lane), "single_weights",
        [(runs, None)], outs, [((height, STRIDE), F32)],
    )
    return dict(zip(names, values))


def pack(name, table, total, shards, lanes, base, parts):
    height = row_height(base, *lanes, total)
    for held, array in parts:
        if isinstance(held, tuple):
            end = table[held][0] - base + array.shape[0] * max(1, array.shape[1] // STRIDE)
            height = max(height, -(-end // 8) * 8)
    return whole_call(
        functools.partial(pack_kernel, table, total, lanes[0], base, [held for held, array in parts]),
        name, [(array, None) for held, array in parts],
        [((shards, lanes[1] - lanes[0], RUN, STRIDE), BF16)], [((height, STRIDE), F32)],
    )[0]


def swap(values, group):
    return lax.all_to_all(values, group, split_axis=0, concat_axis=0, tiled=True)


def single_project(single_state, weights, devices):
    gain, shift = norm_pair(weights, ATTEND)
    lowered = layer_norm(single_state, gain, shift).astype(BF16)
    width = lowered.shape[1]
    qkvg = matmul(lowered, weights[(ATTEND, QKVG)])
    both = qkvg[:, width : 3 * width].astype(BF16)
    both = jnp.broadcast_to(both[None], (devices,) + both.shape)
    return lowered, qkvg, both


def single_attend(single_state, projected, bias, penalty, weights):
    lowered, qkvg, both = projected
    rows, width = lowered.shape
    size = width // SA_HEADS
    query = qkvg[:, :width].astype(BF16).reshape(rows, SA_HEADS, size)
    gate = qkvg[:, 3 * width :]
    both = both.reshape(-1, 2 * width)
    keys_all = both[:, :width].reshape(-1, SA_HEADS, size)
    values_all = both[:, width:].reshape(-1, SA_HEADS, size)
    scores = jnp.einsum(
        "ihd,jhd->hij", query, keys_all, preferred_element_type=F32
    ) * size ** (-0.5)
    scores = scores + bias + penalty[None, None, :]
    probs = jax.nn.softmax(scores, axis=-1)
    probs_low = probs.astype(BF16)
    mixed = jnp.einsum("hij,jhd->ihd", probs_low, values_all, preferred_element_type=F32)
    mixed = mixed.reshape(rows, width)
    gated_low = gated_output(mixed, gate).astype(BF16)
    update = matmul(gated_low, weights[(ATTEND, OUTPUT)])
    return (
        update,
        (single_state, lowered, query, keys_all, values_all, gate, probs, probs_low, mixed, gated_low),
    )


def single_attend_back(saved, grad_update, weights, grads):
    single_state, lowered, query, keys_all, values_all, gate, probs, probs_low, mixed, gated_low = saved
    rows, width = lowered.shape
    size = width // SA_HEADS
    scale = size ** (-0.5)
    grad_low = grad_update.astype(BF16)
    grads[(ATTEND, OUTPUT)] = outer_sum(gated_low, grad_low)
    grad_gated = matmul(grad_low, weights[(ATTEND, OUTPUT)].T)
    _, pullback = jax.vjp(gated_output, mixed, gate)
    grad_mixed, grad_gate = pullback(grad_gated)
    grad_mixed = grad_mixed.astype(BF16).reshape(rows, SA_HEADS, size)
    grad_probs = jnp.einsum("ihd,jhd->hij", grad_mixed, values_all, preferred_element_type=F32)
    delta = jnp.sum(probs * grad_probs, axis=-1, keepdims=True)
    grad_scores = (probs * (grad_probs - delta)).astype(BF16)
    grad_query = (
        jnp.einsum("hij,jhd->ihd", grad_scores, keys_all, preferred_element_type=F32) * scale
    )
    key_part = jnp.einsum("hij,ihd->jhd", grad_scores, query, preferred_element_type=F32) * scale
    value_part = jnp.einsum("hij,ihd->jhd", probs_low, grad_mixed, preferred_element_type=F32)
    parts = jnp.concatenate(
        [key_part.reshape(-1, rows, width), value_part.reshape(-1, rows, width)], axis=-1
    )
    return grad_scores, (parts.astype(BF16), single_state, lowered, grad_query, grad_gate)


def single_attend_end(pending, parts, weights, grads):
    _, single_state, lowered, grad_query, grad_gate = pending
    rows, width = lowered.shape
    grad_both = jnp.sum(parts.astype(F32), axis=0)
    grad_qkvg = jnp.concatenate(
        [grad_query.reshape(rows, width), grad_both, grad_gate], axis=-1
    ).astype(BF16)
    grads[(ATTEND, QKVG)] = outer_sum(lowered, grad_qkvg)
    grad_lowered = matmul(grad_qkvg, weights[(ATTEND, QKVG)].T)
    gain, shift = norm_pair(weights, ATTEND)
    grad_single, grads[(ATTEND, NORM_GAIN)], grads[(ATTEND, NORM_BIAS)] = norm_backward(
        single_state, gain, shift, grad_lowered
    )
    return grad_single


def after(values, *others):
    held = lax.optimization_barrier((values,) + others)
    return held


def in_turn():
    last = []

    def send(values, axes):
        if last:
            values = after(values, last.pop())[0]
        moved = swap(values, axes)
        last.append(moved)
        return moved

    return send


def pair_path(pair, info, alive, orders, weights, cotangent, middle, between, meet, send, group, parts):
    rows, length, width = pair.shape
    hidden = weights[(OUTGOING, PROJ_OUT)].shape[0]
    devices = length // rows
    cores = devices // parts
    order, order_back = orders
    read_first = functools.partial(read_tokens, order)
    read_last = functools.partial(read_turned, order)
    part = hidden // devices
    steps = rows // 16
    state_shape = (rows, width, length)
    block = rows // steps
    half = rows // 2
    flip_shape = (devices, rows, rows, width)
    product_shape = (devices, 2, part, rows, length)
    product_half = (devices, 2, part, half, length)
    tri_shape = (devices, part, rows, length)
    tri_half = (devices, part, half, length)
    channel_block = math.gcd(part, 4)

    def products(name, kernel, arrays, out_shape):
        axes = {4: 1, 5: 2}
        out = (out_shape, BF16, axes[len(out_shape)])
        return run_rows(
            kernel, name, part // channel_block,
            [(Both(pieces), axes[pieces[0].ndim]) for pieces in arrays],
            [out] * (rows // out_shape[-2]), [], 7,
        )

    def swap_all(pieces):
        return [send(values, group) for values in pieces]

    def by_hidden(pieces):
        return [values.reshape((hidden,) + values.shape[2:]) for values in pieces]

    def by_device(pieces):
        return [values.reshape((devices, part) + values.shape[1:]) for values in pieces]

    def cols(prefix):
        return weights[(prefix, COLS)]

    tri_cols = cols

    def turned(name):
        return weights[(name, T)]

    tri_scratch = ((hidden, block, length), F32)
    product_scratch = ((2 * hidden, block, length), F32)
    head_scratch = ((8, block, length), F32)
    wide = ((width, length), F32)
    flip_scratch = ((length, block, width), F32)
    table = ((TA_HEADS, length, length), F32)
    attend_saves = [((rows, TA_HEADS, length), F32, 0), (state_shape, BF16, 0)]

    product = run_rows(
        functools.partial(tri_pre_first_kernel, devices, read_first), "outgoing_in", steps,
        [
            (info, "smem"), (alive, None), (pair, 0), (tri_cols(OUTGOING), None),
            (turned((OUTGOING, PROJ_GATE)), None),
        ],
        [(product_shape, BF16, 3)], [product_scratch], 13,
    )
    between(0, None)
    product_one = swap_all(product)
    between(9, None)
    tri_one = products(
        "outgoing_product", functools.partial(tri_product_kernel, False), [product_one], tri_half
    )
    tri_one = by_hidden(swap_all(tri_one))
    tri_one = [tri_one[0], *meet(0, tri_one[1])]
    state_one, product = run_halves(
        functools.partial(tri_join_kernel, devices, read_first), "outgoing_out_incoming_in", steps,
        [
            ([info[:half], info[half:]], "smem"), (alive, None), (pair, 0), (tri_one, 1), (tri_cols(OUTGOING), None),
            (turned((OUTGOING, PROJ_OUT)), None), (turned((OUTGOING, GATE_OUT)), None),
            (tri_cols(INCOMING), None), (turned((INCOMING, PROJ_GATE)), None),
        ],
        [(state_shape, F32, 0), (product_half, BF16, 3)], [tri_scratch, product_scratch], 22,
    )
    product_two = list(meet(1, *swap_all(product)))
    tri_two = products(
        "incoming_product", functools.partial(tri_product_kernel, True), [product_two], tri_shape
    )
    tri_two = by_hidden(swap_all(tri_two))
    between(1, None)
    (tri_two,) = meet(2, *tri_two)
    cotangent = cotangent.reshape(rows, parts, cores, parts, -1, width).transpose(3, 2, 1, 4, 0, 5)
    cotangent = send(cotangent.reshape(flip_shape), group)
    state_two, bias = run_rows(
        tri_last_kernel, "incoming_out_starting_bias", steps,
        [
            (state_one, 0), (tri_two, 1), (tri_cols(INCOMING), None),
            (turned((INCOMING, PROJ_OUT)), None), (turned((INCOMING, GATE_OUT)), None),
            (cols(STARTING), None), (weights[(STARTING, BIAS_T)], None),
        ],
        [(state_shape, F32, 0), ((TA_HEADS, rows, length), BF16, 1)], [tri_scratch, head_scratch],
    )
    bias_one = lax.all_gather(bias, group, axis=0, tiled=False)
    flipped, totals_one, mixed_one = run_rows(
        starting_kernel, "starting_attention", steps,
        [
            (alive, None), (state_two, 0), (bias_one, None), (cols(STARTING), None),
            (turned((STARTING, QKVG)), None), (turned((STARTING, OUTPUT)), None),
        ],
        [(flip_shape, BF16, 2)] + attend_saves, [table, flip_scratch], 21,
    )
    state_three = Both([send(flipped, group)])
    cotangent = send(cotangent.reshape((parts, cores) + flip_shape[1:]), "z").reshape(flip_shape)
    (bias,) = run_rows(
        flipped_bias_kernel, "ending_bias", steps,
        [(state_three, 1), (cols(ENDING), None), (weights[(ENDING, BIAS_T)], None)],
        [((TA_HEADS, rows, length), BF16, 1)], [head_scratch],
    )
    bias_two = lax.all_gather(bias, group, axis=0, tiled=False)
    state_four, totals_two, mixed_two = run_rows(
        ending_kernel, "ending_attention", steps,
        [
            (alive, None), (state_three, 1), (bias_two, None), (cols(ENDING), None),
            (turned((ENDING, QKVG)), None), (turned((ENDING, OUTPUT)), None),
        ],
        [(state_shape, F32, 0)] + attend_saves, [table],
    )
    pair_cols, attend_cols = cols(PAIR), cols(ATTEND)
    state_four, cotangent = after(state_four, cotangent)
    state_five, pair_out, single_bias = run_rows(
        functools.partial(transition_kernel, order_back), "pair_transition", steps,
        [
            (state_four, 0), (pair_cols, None), (turned((PAIR, UP)), None), (turned((PAIR, DOWN)), None),
            (attend_cols, None), (turned((ATTEND, PAIR_PROJ)), None),
        ],
        [(state_shape, F32, 0), ((length, rows, width), BF16, 1), ((SA_HEADS, rows, length), BF16, 1)],
        [flip_scratch, ((SA_HEADS, block, length), F32)],
    )
    def turn(values):
        heads = values.shape[0]
        sent = values.reshape(heads, rows, devices, rows).transpose(2, 0, 3, 1)
        return send(sent, group).transpose(1, 2, 0, 3).reshape(heads, rows, length)

    single_grad_scores = turn(middle(turn(single_bias).astype(F32)))
    pair_out = send(pair_out.reshape((parts, -1) + pair_out.shape[1:]), "z")
    between(2, None)
    grads = {}
    grad_four, grads[(PAIR, UP)], grads[(PAIR, DOWN)], grads[(ATTEND, PAIR_PROJ)], vecs = run_rows(
        functools.partial(transition_back_kernel, read_last), "pair_transition_back", steps,
        [
            (state_four, 0), (state_five, 0), (cotangent, 1), (single_grad_scores, 1),
            (pair_cols, None), (turned((PAIR, UP)), None), (weights[(PAIR, UP)], None),
            (weights[(PAIR, DOWN)], None), (attend_cols, None), (weights[(ATTEND, PAIR_PROJ)], None),
        ],
        [
            (state_shape, F32, 0), (weights[(PAIR, UP)].shape, F32, None),
            (weights[(PAIR, DOWN)].shape, F32, None), (weights[(ATTEND, PAIR_PROJ)].shape, F32, None),
            ((8, width), F32, None),
        ],
        [wide, wide, wide, wide, ((SA_HEADS, block, length), F32)], 30,
    )
    grads[(PAIR, VECTORS)] = vecs

    def attention_back(prefix, read, read_grad, source, source_axis, grad, grad_axis, bias, totals, mixed):
        lowered_grad, bias_grad, grads[(prefix, QKVG)], grads[(prefix, OUTPUT)] = run_rows(
            functools.partial(attention_back_kernel, read, read_grad),
            "attention_back", steps,
            [
                (alive, None), (source, source_axis), (grad, grad_axis), (bias, None), (totals, 0),
                (mixed, 0), (cols(prefix), None), (turned((prefix, QKVG)), None),
                (weights[(prefix, QKVG)], None), (weights[(prefix, OUTPUT)], None),
            ],
            [
                (state_shape, BF16, 0), ((devices, TA_HEADS, rows, length), BF16, None),
                (weights[(prefix, QKVG)].shape, F32, None), (weights[(prefix, OUTPUT)].shape, F32, None),
            ],
            [table, table], 34,
        )
        return lowered_grad, send(bias_grad, group)

    lowered_grad, bias_grad = attention_back(
        ENDING, read_flipped, read_plain, state_three, 1, grad_four, 0, bias_two, totals_two, mixed_two
    )
    between(3, grads)
    flipped, bias_w_grad, vecs = run_rows(
        ending_end_kernel, "ending_attention_end", steps,
        [
            (state_three, 1), (grad_four, 0), (lowered_grad, 0), (bias_grad, 2), (cols(ENDING), None),
            (weights[(ENDING, BIAS_W)], None),
        ],
        [(flip_shape, BF16, 2), ((width, 8), F32, None), ((8, width), F32, None)],
        [wide, wide, head_scratch, flip_scratch],
    )
    grads[(ENDING, BIAS_PROJ)], grads[(ENDING, VECTORS)] = bias_w_grad, vecs
    flipped, held = after(flipped, grads[(ATTEND, PAIR_PROJ)])
    grads[(ATTEND, PAIR_PROJ)] = held
    grad_three = send(flipped, group)
    between(4, grads)
    grad_three = Both(meet(3, grad_three))
    pair_out = send(pair_out.reshape(flip_shape), group)
    pair_out = pair_out.reshape(parts, cores, rows, parts, -1, width).transpose(2, 3, 1, 0, 4, 5)
    pair_out = pair_out.reshape(rows, length, width)
    lowered_grad, bias_grad = attention_back(
        STARTING, read_plain, read_flipped, state_two, 0, grad_three, 1, bias_one, totals_one, mixed_one
    )
    between(7, grads)
    square = weights[(INCOMING, GATE_OUT)].shape
    (
        grad_two, grad_tri, gate_back, bias_w_grad, grads[(INCOMING, PROJ_OUT)], grads[(INCOMING, GATE_OUT)], vecs,
    ) = run_halves(
        starting_end_kernel, "starting_end_incoming_out_back", steps,
        [
            (state_two, 0), (grad_three, 1), (lowered_grad, 0), (bias_grad, 2), (cols(STARTING), None),
            (weights[(STARTING, BIAS_W)], None), (state_one, 0), (tri_two, 1), (tri_cols(INCOMING), None),
            (turned((INCOMING, PROJ_OUT)), None), (turned((INCOMING, GATE_OUT)), None),
            (weights[(INCOMING, PROJ_OUT)], None), (weights[(INCOMING, GATE_OUT)], None),
        ],
        [
            (state_shape, F32, 0), ((hidden, half, length), BF16, 1), (state_shape, BF16, 0),
            ((width, 8), F32, None), (square, F32, None), (square, F32, None), ((8, width), F32, None),
        ],
        [wide, wide, wide, wide, head_scratch, tri_scratch], 26,
    )
    grads[(STARTING, BIAS_PROJ)], grads[(STARTING, VECTORS)] = bias_w_grad, vecs
    grad_tri = swap_all(by_device(grad_tri))
    product_grad = products(
        "incoming_product_back", functools.partial(tri_product_back_kernel, True),
        [grad_tri, product_two], product_half,
    )
    product_grad = swap_all(product_grad)
    product_grad = [*meet(4, product_grad[0]), product_grad[1]]
    (
        grad_one, grad_tri, gate_back, grads[(INCOMING, PROJ_GATE)], grads[(OUTGOING, PROJ_OUT)],
        grads[(OUTGOING, GATE_OUT)], vecs,
    ) = run_halves(
        functools.partial(tri_join_back_kernel, read_first), "incoming_in_outgoing_out_back", steps,
        [
            ([info[:half], info[half:]], "smem"), (alive, None), (state_one, 0), (product_grad, 3), (gate_back, 0), (grad_two, 0),
            (tri_cols(INCOMING), None), (turned((INCOMING, PROJ_GATE)), None),
            (weights[(INCOMING, PROJ_GATE)], None), (pair, 0), (tri_one, 1), (tri_cols(OUTGOING), None),
            (turned((OUTGOING, PROJ_OUT)), None), (turned((OUTGOING, GATE_OUT)), None),
            (weights[(OUTGOING, PROJ_OUT)], None), (weights[(OUTGOING, GATE_OUT)], None),
        ],
        [
            (state_shape, F32, 0), ((hidden, half, length), BF16, 1), (state_shape, BF16, 0),
            (weights[(INCOMING, PROJ_GATE)].shape, F32, None), (square, F32, None), (square, F32, None),
            ((8, width), F32, None),
        ],
        [wide, wide, wide, wide, product_scratch, tri_scratch], 37,
    )
    grads[(INCOMING, VECTORS)] = vecs
    between(5, grads)
    grad_tri = swap_all(by_device(grad_tri))
    grad_tri = [grad_tri[0], *meet(5, grad_tri[1])]
    between(8, grads)
    product_grad = products(
        "outgoing_product_back", functools.partial(tri_product_back_kernel, False),
        [grad_tri, product_one], product_shape,
    )
    (product_grad,) = swap_all(product_grad)
    between(6, grads)
    pair_grad, grads[(OUTGOING, PROJ_GATE)], vecs = run_rows(
        functools.partial(tri_first_back_kernel, read_first, order_back), "outgoing_in_back", steps,
        [
            (info, "smem"), (alive, None), (pair, 0), (product_grad, 3), (gate_back, 0), (grad_one, 0),
            (tri_cols(OUTGOING), None), (turned((OUTGOING, PROJ_GATE)), None),
            (weights[(OUTGOING, PROJ_GATE)], None),
        ],
        [
            ((rows, length, width), BF16, 0), (weights[(OUTGOING, PROJ_GATE)].shape, F32, None),
            ((8, width), F32, None),
        ],
        [wide, wide, product_scratch], 20,
    )
    grads[(OUTGOING, VECTORS)] = vecs
    return pair_out, pair_grad, grads


HELD = {
    (PAIR, VECTORS): ((PAIR, NORM_GAIN), (PAIR, NORM_BIAS), (ATTEND, PAIR_GAIN), (ATTEND, PAIR_BIAS)),
    (ENDING, VECTORS): ((ENDING, NORM_GAIN), (ENDING, NORM_BIAS)),
    (STARTING, VECTORS): (
        (STARTING, NORM_GAIN), (STARTING, NORM_BIAS), (INCOMING, OUT_GAIN), (INCOMING, OUT_BIAS)
    ),
    (INCOMING, VECTORS): (
        (INCOMING, NORM_GAIN), (INCOMING, NORM_BIAS), (OUTGOING, OUT_GAIN), (OUTGOING, OUT_BIAS)
    ),
    (OUTGOING, VECTORS): ((OUTGOING, NORM_GAIN), (OUTGOING, NORM_BIAS)),
}


def vector_part(grads, name, prefix):
    pairs = [(row, held) for row, held in enumerate(HELD[name]) if prefix in (None, held[0])]
    return (pairs, grads[name])


def fast_shards(parts, cores, pair, single, lengths, params, moment_one, moment_two, pair_cotangent, single_cotangent):
    entries = layout(C, H, S, TA_HEADS, SA_HEADS)
    table, total = table_of(entries)
    count = total // STRIDE
    shard_size = params.shape[0]
    attend = table[(ATTEND, NORM_GAIN)][0]
    pair_lanes = -(-attend * STRIDE // count)
    single_lane = attend * STRIDE // count
    devices = parts * cores
    line, group = ("z", "core"), ("crop", "core")
    row_index = lax.axis_index(line)
    odd = ((row_index * shard_size) % STRIDE) // (STRIDE // 2)
    place = jnp.stack([odd, odd]).astype(jnp.int32)
    shard_rows = jnp.pad(params, (0, RUN * STRIDE * STRIDE - shard_size)).reshape(-1, STRIDE)
    (runs,) = whole_call(
        runs_kernel, "parameter_runs", [(place, "smem"), (shard_rows, None)],
        [((STRIDE, RUN, STRIDE), BF16)], [((STRIDE, RUN, STRIDE), F32)],
    )
    rows, length, width = pair.shape[1:]
    send = in_turn()
    pair_in = send(pair[0].reshape(parts, -1, length, width), "crop")
    first_runs = lax.all_gather(runs[:pair_lanes], line)
    pair_in, _, lengths = after(pair_in, runs, lengths)
    live = lax.all_gather(jnp.broadcast_to(lengths.astype(F32), (8, STRIDE)), "crop")
    pair_in = send(pair_in, "z").reshape(rows, length, width)
    weights = unpack_pair(table, total, first_runs)
    last_runs = after(runs[single_lane:], weights[(OUTGOING, COLS)])[0]
    last_runs = lax.all_gather(last_runs, line)
    weights.update(unpack_single(table, total, single_lane, last_runs))
    for index, name in enumerate(SINGLE_VECTORS):
        weights[name] = weights[(SINGLE, VECTORS)][index]
    size = rows // parts
    blocks = np.arange(length // size).reshape(parts, cores, parts)
    order = blocks.transpose(2, 1, 0).reshape(-1)
    orders = (order.tolist(), np.argsort(order).tolist())
    tokens = (order[:, None] * size + np.arange(size)).reshape(-1)
    live = live[lax.axis_index("z"), 0, 0]
    width = single.shape[2]
    mask = (tokens.astype(np.float32) < live).astype(F32)
    info = lax.dynamic_slice_in_dim(mask, lax.axis_index(group) * rows, rows).astype(jnp.int32)
    alive = jnp.broadcast_to(mask, (8, length))
    penalty = (mask - 1.0) * MASKED
    held = {}
    single_grads = {}

    def middle(bias):
        update, saved = single_attend(held["state"], held["projected"], bias, penalty, weights)
        single_mid = held["state"] + update
        update, saved_last = transition_forward(single_mid, weights, SINGLE)
        held["out"] = single_mid + update
        grad = held["back"] + transition_backward(saved_last, held["back"], weights, SINGLE, single_grads)
        held["grad"] = grad
        grad_scores, held["pending"] = single_attend_back(saved, grad, weights, single_grads)
        return grad_scores

    def meet(number, *values):
        if number == 0:
            others = [last_runs]
        elif number == 1:
            others = [weights[(SINGLE, UP)]]
        elif number == 2:
            others = [held["projected"][1]]
        elif number == 3:
            others = [reduced[3]]
        elif number == 4:
            others = [reduced[2]]
        else:
            others = [reduced[1]]
        return after(*values, *others)[: len(values)]

    def reduce_runs(sent):
        return jnp.sum(send(sent, line).astype(F32), axis=0).astype(BF16)

    reduced = {}
    lines_held = list(enumerate(SINGLE_VECTORS))
    late_lanes = -(-table[(INCOMING, NORM_GAIN)][0] * STRIDE // count)

    def lines():
        values = jnp.concatenate([single_grads[name].reshape(1, S) for name in SINGLE_VECTORS], axis=0)
        return jnp.pad(values, ((0, 8 - len(SINGLE_VECTORS)), (0, 0)))

    def between(number, grads):
        if number == 0:
            both = jnp.concatenate([single[0], single_cotangent[0]], axis=1)
            both = after(both, weights[(OUTGOING, COLS)])[0]
            held["both"] = send(both.reshape(parts, -1, 2 * width), "crop")
            return
        if number == 9:
            both = send(held["both"], "z").reshape(rows, 2 * width).astype(F32)
            held["state"], held["back"] = both[:, :width], both[:, width:]
            return
        if number == 8:
            reduced[1] = reduce_runs(reduced[1])
            return
        if number == 1:
            lowered, qkvg, both = single_project(held["state"], weights, devices)
            held["projected"] = lowered, qkvg, send(both, group)
            return
        if number == 2:
            pending = held["pending"]
            moved = send(pending[0], group)
            grad = held["grad"] + single_attend_end(pending, moved, weights, single_grads)
            held["both"] = jnp.concatenate([held["out"], grad], axis=1).reshape(parts, -1, 2 * width)
            return
        if number == 3:
            held["both"] = send(held["both"], "z")
            return
        if number == 7:
            both = send(held["both"], "crop").reshape(rows, 2 * width)
            held[SINGLE] = both[:, :width].astype(BF16), both[:, width:]
            return
        if number == 6:
            part = send(reduced[2].reshape((parts, -1) + reduced[2].shape[1:]), "crop")
            reduced[2] = jnp.sum(part.astype(F32), axis=0).astype(BF16)
            return
        if number == 4:
            sent = pack(
                "single_gradient", table, total, devices, (pair_lanes, STRIDE), attend,
                [(name, single_grads[name]) for name in SINGLE_MATRICES]
                + [((ATTEND, PAIR_PROJ), grads[(ATTEND, PAIR_PROJ)])]
                + [vector_part(grads, (PAIR, VECTORS), ATTEND), (lines_held, lines())],
            )
            reduced[3] = sent
            reduced[2] = lax.psum_scatter(sent, line, scatter_dimension=0, tiled=False)
            return
        taken = -(-(pair_lanes * count - (attend + 2 * S // STRIDE) * STRIDE) // (4 * S))
        first = table[(INCOMING, NORM_GAIN)][0]
        sent = pack(
            "pair_gradient", table, total, devices, (late_lanes, pair_lanes), first,
            [(name, grads[name]) for name in PAIR_MATRICES if table[name][0] >= first]
            + [(name, grads[name]) for name in ((STARTING, BIAS_PROJ), (ENDING, BIAS_PROJ))]
            + [vector_part(grads, name, None) for name in ((ENDING, VECTORS), (STARTING, VECTORS))]
            + [vector_part(grads, (INCOMING, VECTORS), INCOMING)]
            + [vector_part(grads, (PAIR, VECTORS), PAIR)]
            + [(lines_held[:2], lines()), ((ATTEND, QKVG), single_grads[(ATTEND, QKVG)][: -(-taken // 8) * 8])],
        )
        reduced[1] = sent

    pair_out, pair_grad, grads = pair_path(
        pair_in, info, alive, orders, weights, pair_cotangent[0], middle, between, meet, send, group, parts
    )
    first = table[(INCOMING, NORM_GAIN)][0]
    taken = -(-(late_lanes * count - (first + 2) * STRIDE) // (4 * H))
    sent = pack(
        "outgoing_gradient", table, total, devices, (0, late_lanes), 0,
        [(name, grads[name]) for name in PAIR_MATRICES if table[name][0] < first]
        + [vector_part(grads, (OUTGOING, VECTORS), None)]
        + [vector_part(grads, (INCOMING, VECTORS), None)]
        + [((INCOMING, PROJ_GATE), grads[(INCOMING, PROJ_GATE)][: -(-taken // 8) * 8])],
    )
    reduced[0] = reduce_runs(sent)
    pair_grad = send(pair_grad.reshape(parts, -1, length, pair_grad.shape[2]), "z")
    pair_grad = send(pair_grad, "crop").reshape(rows, length, -1).astype(F32)
    single_out, single_grad = held[SINGLE]
    summed = lax.all_gather(jnp.concatenate([reduced[0], reduced[1]], axis=0), "crop")
    others = lax.all_gather(reduced[2], "crop")
    shard, squares = whole_call(
        functools.partial(shard_kernel, shard_size), "gradient_share",
        [(place, "smem"), (summed, None), (others, None)],
        [((RUN * STRIDE, STRIDE), F32), ((8, STRIDE), F32)], [((STRIDE, RUN, STRIDE), F32)],
    )
    shard = shard.reshape(-1)[:shard_size]
    clip_norm = jnp.sqrt(jnp.sum(lax.all_gather(squares, line)))
    clipped = shard * (CLIP / jnp.maximum(clip_norm, CLIP))
    new_first = BETA_ONE * moment_one + (1.0 - BETA_ONE) * clipped
    new_second = BETA_TWO * moment_two + (1.0 - BETA_TWO) * clipped * clipped
    rates, decays = rate_tables(entries)
    rate_shard = lax.dynamic_slice_in_dim(jnp.asarray(rates), row_index * shard_size, shard_size)
    decay_shard = lax.dynamic_slice_in_dim(jnp.asarray(decays), row_index * shard_size, shard_size)
    first_hat = new_first / (1.0 - BETA_ONE**STEP)
    second_hat = new_second / (1.0 - BETA_TWO**STEP)
    new_params = params - rate_shard * (
        first_hat / (jnp.sqrt(second_hat) + ADAM_EPS) + decay_shard * params
    )
    return (
        pair_out[None],
        single_out[None],
        pair_grad[None],
        single_grad[None],
        new_params,
        new_first,
        new_second,
        clip_norm,
    )


def solution(mesh):
    crops, devices = mesh.devices.shape
    table, total = table_of(layout(C, H, S, TA_HEADS, SA_HEADS))
    count = total // STRIDE
    lanes = STRIDE + -table[(ATTEND, NORM_GAIN)][0] * STRIDE // count
    fast = devices == 2 * crops and LENGTH % (devices * 16) == 0 and count // devices + 2 <= RUN * STRIDE and lanes % crops == 0
    row = "row"
    if fast:
        mesh = jax.sharding.Mesh(mesh.devices.reshape(crops, crops, 2), ("crop", "z", "core"))
        row = ("z", "core")
    split = [P("crop", row, None, None), P("crop", row, None), P("crop"), P(row)]
    pair, single, lengths, share = split
    return jax.shard_map(
        functools.partial(fast_shards, crops, 2) if fast else shards,
        mesh=mesh,
        in_specs=(pair, single, lengths, share, share, share, pair, single),
        out_specs=(pair, single, pair, single, share, share, share, P()),
        check_vma=False,
    )
```

```python
import functools
import math

import jax
import jax.numpy as jnp
import numpy as np
from jax import lax
from jax.experimental import pallas as pl
from jax.experimental.pallas import tpu as pltpu
from jax.sharding import PartitionSpec as P

C = 128
H = 128
S = 384
TA_HEADS = 4
SA_HEADS = 16
STEP = 10
STRIDE = 128
LENGTH = 256

OUTGOING, INCOMING, STARTING, ENDING, PAIR, ATTEND, SINGLE = range(7)
(
    NORM_GAIN,
    NORM_BIAS,
    PROJ_GATE,
    OUT_GAIN,
    OUT_BIAS,
    PROJ_OUT,
    GATE_OUT,
    QKVG,
    BIAS_PROJ,
    OUTPUT,
    UP,
    DOWN,
    PAIR_GAIN,
    PAIR_BIAS,
    PAIR_PROJ,
    COLS,
    BIAS_W,
    BIAS_T,
    VECTORS,
    T,
) = range(7, 27)


EPSILON = 1e-05
MASKED = 1000000000.0
BETA_ONE = 0.9
BETA_TWO = 0.95
ADAM_EPS = 1e-08
CLIP = 1.0


def layout(pair_width, hidden_width, single_width, tri_heads, att_heads):
    entries = []
    for prefix in (OUTGOING, INCOMING):
        entries += [
            ((prefix, NORM_GAIN), (pair_width,)),
            ((prefix, NORM_BIAS), (pair_width,)),
            ((prefix, PROJ_GATE), (pair_width, 4 * hidden_width)),
            ((prefix, OUT_GAIN), (hidden_width,)),
            ((prefix, OUT_BIAS), (hidden_width,)),
            ((prefix, PROJ_OUT), (hidden_width, pair_width)),
            ((prefix, GATE_OUT), (pair_width, pair_width)),
        ]
    for prefix in (STARTING, ENDING):
        entries += [
            ((prefix, NORM_GAIN), (pair_width,)),
            ((prefix, NORM_BIAS), (pair_width,)),
            ((prefix, QKVG), (pair_width, 4 * pair_width)),
            ((prefix, BIAS_PROJ), (pair_width, tri_heads)),
            ((prefix, OUTPUT), (pair_width, pair_width)),
        ]
    entries += [
        ((PAIR, NORM_GAIN), (pair_width,)),
        ((PAIR, NORM_BIAS), (pair_width,)),
        ((PAIR, UP), (pair_width, 8 * pair_width)),
        ((PAIR, DOWN), (4 * pair_width, pair_width)),
        ((ATTEND, NORM_GAIN), (single_width,)),
        ((ATTEND, NORM_BIAS), (single_width,)),
        ((ATTEND, QKVG), (single_width, 4 * single_width)),
        ((ATTEND, PAIR_GAIN), (pair_width,)),
        ((ATTEND, PAIR_BIAS), (pair_width,)),
        ((ATTEND, PAIR_PROJ), (pair_width, att_heads)),
        ((ATTEND, OUTPUT), (single_width, single_width)),
        ((SINGLE, NORM_GAIN), (single_width,)),
        ((SINGLE, NORM_BIAS), (single_width,)),
        ((SINGLE, UP), (single_width, 8 * single_width)),
        ((SINGLE, DOWN), (4 * single_width, single_width)),
    ]
    return entries


def logical_order(flat):
    return flat.reshape(-1, STRIDE).T.reshape(-1)


def stored_order(vector):
    return vector.reshape(STRIDE, -1).T.reshape(-1)


def rate_tables(entries):
    rates = []
    decays = []
    for name, shape in entries:
        count = math.prod(shape)
        if len(shape) == 1:
            rates.append(np.full(count, 0.5, np.float32))
            decays.append(np.zeros(count, np.float32))
        else:
            rates.append(np.full(count, 2.0 / math.sqrt(shape[0]), np.float32))
            decays.append(np.full(count, 0.01, np.float32))
    rates = np.concatenate(rates)
    decays = np.concatenate(decays)
    return (rates.reshape(STRIDE, -1).T.reshape(-1), decays.reshape(STRIDE, -1).T.reshape(-1))


def unpack(flat, entries):
    pieces = {}
    offset = 0
    for name, shape in entries:
        count = math.prod(shape)
        pieces[name] = flat[offset : offset + count].reshape(shape)
        offset += count
    return pieces


def layer_norm(values, gain, shift):
    centred = values - jnp.mean(values, axis=-1, keepdims=True)
    spread = jnp.mean(centred * centred, axis=-1, keepdims=True)
    return centred * lax.rsqrt(spread + EPSILON) * gain + shift


def norm_backward(values, gain, shift, grad):
    _, pullback = jax.vjp(layer_norm, values, gain, shift)
    return pullback(grad)


def norm_pair(weights, prefix):
    return (
        weights[(prefix, NORM_GAIN)].astype(jnp.float32),
        weights[(prefix, NORM_BIAS)].astype(jnp.float32),
    )


def gated_pair(project, pair_mask):
    half = project.shape[-1] // 2
    return project[..., :half] * jax.nn.sigmoid(project[..., half:]) * pair_mask[..., None]


def gated_output(values, gate):
    return values * jax.nn.sigmoid(gate)


def swiglu(hidden):
    half = hidden.shape[-1] // 2
    return jax.nn.silu(hidden[..., :half]) * hidden[..., half:]


def matmul(left, right):
    return jnp.dot(left, right, preferred_element_type=jnp.float32)


def outer_sum(left, right):
    return jnp.einsum(
        "nc,nd->cd",
        left.reshape(-1, left.shape[-1]),
        right.reshape(-1, right.shape[-1]),
        preferred_element_type=jnp.float32,
    )


def flip(values):
    moved = lax.all_to_all(values, "row", split_axis=1, concat_axis=0, tiled=True)
    return jnp.swapaxes(moved, 0, 1)


def channel_forward(first, second, incoming):
    whole_first, whole_second = (
        lax.all_to_all(first, "row", split_axis=2, concat_axis=0, tiled=True),
        lax.all_to_all(second, "row", split_axis=2, concat_axis=0, tiled=True),
    )
    if incoming:
        local_tri = jnp.einsum(
            "kih,kjh->ijh", whole_first, whole_second, preferred_element_type=jnp.float32
        )
        local_tri = local_tri.astype(jnp.bfloat16).astype(jnp.float32)
    else:
        local_tri = jnp.einsum(
            "ikh,jkh->ijh", whole_first, whole_second, preferred_element_type=jnp.float32
        )
    tri = lax.all_to_all(
        local_tri.astype(jnp.bfloat16), "row", split_axis=0, concat_axis=2, tiled=True
    ).astype(local_tri.dtype)
    return (tri, whole_first, whole_second)


def channel_backward(grad_tri, whole_first, whole_second, incoming):
    whole_grad = lax.all_to_all(grad_tri, "row", split_axis=2, concat_axis=0, tiled=True)
    if incoming:
        grad_a = jnp.einsum(
            "ijh,kjh->kih", whole_grad, whole_second, preferred_element_type=jnp.float32
        )
        grad_b = jnp.einsum(
            "ijh,kih->kjh", whole_grad, whole_first, preferred_element_type=jnp.float32
        )
    else:
        grad_a = jnp.einsum(
            "ijh,jkh->ikh", whole_grad, whole_second, preferred_element_type=jnp.float32
        )
        grad_b = jnp.einsum(
            "ijh,ikh->jkh", whole_grad, whole_first, preferred_element_type=jnp.float32
        )
    return (
        lax.all_to_all(
            grad_a.astype(jnp.bfloat16), "row", split_axis=0, concat_axis=2, tiled=True
        ).astype(grad_a.dtype),
        lax.all_to_all(
            grad_b.astype(jnp.bfloat16), "row", split_axis=0, concat_axis=2, tiled=True
        ).astype(grad_b.dtype),
    )


def triangle_forward(state, pair_mask, weights, prefix, incoming):
    gain, shift = norm_pair(weights, prefix)
    lowered = layer_norm(state, gain, shift).astype(jnp.bfloat16)
    project = matmul(lowered, weights[(prefix, PROJ_GATE)])
    product = gated_pair(project, pair_mask).astype(jnp.bfloat16)
    half = product.shape[-1] // 2
    tri, own, other = channel_forward(product[..., :half], product[..., half:], incoming)
    out_gain = weights[(prefix, OUT_GAIN)].astype(jnp.float32)
    out_shift = weights[(prefix, OUT_BIAS)].astype(jnp.float32)
    out_low = layer_norm(tri, out_gain, out_shift).astype(jnp.bfloat16)
    output = matmul(out_low, weights[(prefix, PROJ_OUT)])
    gate_out = matmul(lowered, weights[(prefix, GATE_OUT)])
    update = gated_output(output, gate_out)
    return (update, (state, lowered, lowered, project, own, other, tri, out_low, output, gate_out))


def triangle_backward(saved, grad_update, pair_mask, weights, prefix, incoming, grads):
    state, lowered, framed, project, own, other, tri, out_low, output, gate_out = saved
    _, pullback = jax.vjp(gated_output, output, gate_out)
    grad_output, grad_gate = pullback(grad_update)
    grad_output = grad_output.astype(jnp.bfloat16)
    grad_gate = grad_gate.astype(jnp.bfloat16)
    grads[(prefix, PROJ_OUT)] = outer_sum(out_low, grad_output)
    grads[(prefix, GATE_OUT)] = outer_sum(lowered, grad_gate)
    grad_normed = matmul(grad_output, weights[(prefix, PROJ_OUT)].T)
    out_gain = weights[(prefix, OUT_GAIN)].astype(jnp.float32)
    out_shift = weights[(prefix, OUT_BIAS)].astype(jnp.float32)
    grad_tri, grads[(prefix, OUT_GAIN)], grads[(prefix, OUT_BIAS)] = norm_backward(
        tri, out_gain, out_shift, grad_normed
    )
    grad_tri = grad_tri.astype(jnp.bfloat16)
    grad_first, grad_second = channel_backward(grad_tri, own, other, incoming)
    _, pullback = jax.vjp(lambda values: gated_pair(values, pair_mask), project)
    (grad_project,) = pullback(jnp.concatenate([grad_first, grad_second], axis=-1))
    grad_project = grad_project.astype(jnp.bfloat16)
    grads[(prefix, PROJ_GATE)] = outer_sum(framed, grad_project)
    grad_framed = matmul(grad_project, weights[(prefix, PROJ_GATE)].T)
    if incoming:
        grad_framed = grad_framed.astype(jnp.bfloat16).astype(jnp.float32)
    grad_lowered = grad_framed + matmul(grad_gate, weights[(prefix, GATE_OUT)].T)
    gain, shift = norm_pair(weights, prefix)
    grad_state, grads[(prefix, NORM_GAIN)], grads[(prefix, NORM_BIAS)] = norm_backward(
        state, gain, shift, grad_lowered
    )
    return grad_state


def row_scores(query, key, bias, penalty, scale):
    scores = jnp.einsum("jhd,khd->hjk", query, key, preferred_element_type=jnp.float32) * scale
    return scores + bias.astype(jnp.float32) + penalty[None, None, :]


def attention_forward(state, penalty, weights, prefix, ending):
    gain, shift = norm_pair(weights, prefix)
    lowered = layer_norm(state, gain, shift).astype(jnp.bfloat16)
    framed = flip(lowered) if ending else lowered
    rows, length, width = framed.shape
    size = width // TA_HEADS
    scale = size ** (-0.5)
    qkvg = matmul(framed, weights[(prefix, QKVG)])
    queries = qkvg[..., :width].astype(jnp.bfloat16).reshape(rows, length, TA_HEADS, size)
    keys = qkvg[..., width : 2 * width].astype(jnp.bfloat16).reshape(rows, length, TA_HEADS, size)
    values = (
        qkvg[..., 2 * width : 3 * width].astype(jnp.bfloat16).reshape(rows, length, TA_HEADS, size)
    )
    gate = qkvg[..., 3 * width :]
    local_bias = (
        matmul(framed, weights[(prefix, BIAS_PROJ)]).astype(jnp.bfloat16).transpose(2, 0, 1)
    )
    bias = lax.all_gather(local_bias, "row", axis=1, tiled=True)

    def forward_row(items):
        query, key, value = items
        scores = row_scores(query, key, bias, penalty, scale)
        top = jnp.max(scores, axis=-1, keepdims=True)
        shifted = jnp.exp(scores - top)
        total = jnp.sum(shifted, axis=-1, keepdims=True)
        probs = (shifted / total).astype(jnp.bfloat16)
        mixed = jnp.einsum("hjk,khd->jhd", probs, value, preferred_element_type=jnp.float32)
        return (mixed, top[..., 0] + jnp.log(total[..., 0]))

    mixed, log_totals = lax.map(forward_row, (queries, keys, values))
    mixed = mixed.reshape(rows, length, width)
    gated_low = gated_output(mixed, gate).astype(jnp.bfloat16)
    returned = flip(gated_low) if ending else gated_low
    update = matmul(returned, weights[(prefix, OUTPUT)])
    return (update, (state, framed, queries, keys, values, gate, bias, mixed, log_totals, returned))


def attention_backward(saved, grad_update, penalty, weights, prefix, ending, grads):
    state, framed, queries, keys, values, gate, bias, mixed, log_totals, returned = saved
    rows, length, width = framed.shape
    size = width // TA_HEADS
    scale = size ** (-0.5)
    grad_low = grad_update.astype(jnp.bfloat16)
    grads[(prefix, OUTPUT)] = outer_sum(returned, grad_low)
    grad_gated = matmul(grad_low, weights[(prefix, OUTPUT)].T)
    if ending:
        grad_gated = flip(grad_gated.astype(jnp.bfloat16)).astype(jnp.float32)
    _, pullback = jax.vjp(gated_output, mixed, gate)
    grad_mixed, grad_gate = pullback(grad_gated)
    grad_mixed = grad_mixed.astype(jnp.bfloat16).reshape(rows, length, TA_HEADS, size)

    def back_row(carry, items):
        query, key, value, log_total, grad_row = items
        scores = row_scores(query, key, bias, penalty, scale)
        probs = jnp.exp(scores - log_total[..., None])
        grad_probs = jnp.einsum("jhd,khd->hjk", grad_row, value, preferred_element_type=jnp.float32)
        delta = jnp.sum(probs * grad_probs, axis=-1, keepdims=True)
        grad_scores = (probs * (grad_probs - delta)).astype(jnp.bfloat16)
        grad_query = (
            jnp.einsum("hjk,khd->jhd", grad_scores, key, preferred_element_type=jnp.float32) * scale
        )
        grad_key = (
            jnp.einsum("hjk,jhd->khd", grad_scores, query, preferred_element_type=jnp.float32)
            * scale
        )
        grad_value = jnp.einsum(
            "hjk,jhd->khd", probs.astype(jnp.bfloat16), grad_row, preferred_element_type=jnp.float32
        )
        return (carry + grad_scores.astype(jnp.float32), (grad_query, grad_key, grad_value))

    empty = jnp.zeros(bias.shape, jnp.float32)
    grad_bias, (grad_query, grad_key, grad_value) = lax.scan(
        back_row, empty, (queries, keys, values, log_totals, grad_mixed)
    )
    grad_bias = lax.psum_scatter(grad_bias, "row", scatter_dimension=1, tiled=True)
    grad_bias = grad_bias.transpose(1, 2, 0).astype(jnp.bfloat16)
    grad_qkvg = jnp.concatenate(
        [
            grad_query.reshape(rows, length, width),
            grad_key.reshape(rows, length, width),
            grad_value.reshape(rows, length, width),
            grad_gate,
        ],
        axis=-1,
    ).astype(jnp.bfloat16)
    grads[(prefix, QKVG)] = outer_sum(framed, grad_qkvg)
    grads[(prefix, BIAS_PROJ)] = outer_sum(framed, grad_bias)
    grad_framed = matmul(grad_qkvg, weights[(prefix, QKVG)].T) + matmul(
        grad_bias, weights[(prefix, BIAS_PROJ)].T
    )
    if ending:
        grad_framed = flip(grad_framed.astype(jnp.bfloat16)).astype(jnp.float32)
    gain, shift = norm_pair(weights, prefix)
    grad_state, grads[(prefix, NORM_GAIN)], grads[(prefix, NORM_BIAS)] = norm_backward(
        state, gain, shift, grad_framed
    )
    return grad_state


def transition_forward(state, weights, prefix):
    gain, shift = norm_pair(weights, prefix)
    lowered = layer_norm(state, gain, shift).astype(jnp.bfloat16)
    hidden = matmul(lowered, weights[(prefix, UP)])
    mixed_low = swiglu(hidden).astype(jnp.bfloat16)
    update = matmul(mixed_low, weights[(prefix, DOWN)])
    return (update, (state, lowered, hidden, mixed_low))


def transition_backward(saved, grad_update, weights, prefix, grads):
    state, lowered, hidden, mixed_low = saved
    grad_low = grad_update.astype(jnp.bfloat16)
    grads[(prefix, DOWN)] = outer_sum(mixed_low, grad_low)
    grad_mixed = matmul(grad_low, weights[(prefix, DOWN)].T)
    _, pullback = jax.vjp(swiglu, hidden)
    (grad_hidden,) = pullback(grad_mixed)
    grad_hidden = grad_hidden.astype(jnp.bfloat16)
    grads[(prefix, UP)] = outer_sum(lowered, grad_hidden)
    grad_lowered = matmul(grad_hidden, weights[(prefix, UP)].T)
    gain, shift = norm_pair(weights, prefix)
    grad_state, grads[(prefix, NORM_GAIN)], grads[(prefix, NORM_BIAS)] = norm_backward(
        state, gain, shift, grad_lowered
    )
    return grad_state


def single_forward(single_state, pair_state, penalty, weights):
    gain, shift = norm_pair(weights, ATTEND)
    lowered = layer_norm(single_state, gain, shift).astype(jnp.bfloat16)
    rows, width = lowered.shape
    size = width // SA_HEADS
    qkvg = matmul(lowered, weights[(ATTEND, QKVG)])
    query = qkvg[:, :width].astype(jnp.bfloat16).reshape(rows, SA_HEADS, size)
    key = qkvg[:, width : 2 * width].astype(jnp.bfloat16)
    value = qkvg[:, 2 * width : 3 * width].astype(jnp.bfloat16)
    gate = qkvg[:, 3 * width :]
    keys_all, values_all = (
        lax.all_gather(key, "row", axis=0, tiled=True),
        lax.all_gather(value, "row", axis=0, tiled=True),
    )
    keys_all = keys_all.reshape(-1, SA_HEADS, size)
    values_all = values_all.reshape(-1, SA_HEADS, size)
    pair_gain = weights[(ATTEND, PAIR_GAIN)].astype(jnp.float32)
    pair_shift = weights[(ATTEND, PAIR_BIAS)].astype(jnp.float32)
    pair_low = layer_norm(pair_state, pair_gain, pair_shift).astype(jnp.bfloat16)
    bias = matmul(pair_low, weights[(ATTEND, PAIR_PROJ)]).transpose(2, 0, 1)
    scores = jnp.einsum(
        "ihd,jhd->hij", query, keys_all, preferred_element_type=jnp.float32
    ) * size ** (-0.5)
    scores = scores + bias + penalty[None, None, :]
    probs = jax.nn.softmax(scores, axis=-1)
    probs_low = probs.astype(jnp.bfloat16)
    mixed = jnp.einsum(
        "hij,jhd->ihd", probs_low, values_all, preferred_element_type=jnp.float32
    ).reshape(rows, width)
    gated_low = gated_output(mixed, gate).astype(jnp.bfloat16)
    update = matmul(gated_low, weights[(ATTEND, OUTPUT)])
    return (
        update,
        (
            single_state,
            pair_state,
            lowered,
            query,
            keys_all,
            values_all,
            gate,
            pair_low,
            probs,
            probs_low,
            mixed,
            gated_low,
        ),
    )


def single_backward(saved, grad_update, weights, grads):
    (
        single_state,
        pair_state,
        lowered,
        query,
        keys_all,
        values_all,
        gate,
        pair_low,
        probs,
        probs_low,
        mixed,
        gated_low,
    ) = saved
    rows, width = lowered.shape
    size = width // SA_HEADS
    scale = size ** (-0.5)
    grad_low = grad_update.astype(jnp.bfloat16)
    grads[(ATTEND, OUTPUT)] = outer_sum(gated_low, grad_low)
    grad_gated = matmul(grad_low, weights[(ATTEND, OUTPUT)].T)
    _, pullback = jax.vjp(gated_output, mixed, gate)
    grad_mixed, grad_gate = pullback(grad_gated)
    grad_mixed = grad_mixed.astype(jnp.bfloat16).reshape(rows, SA_HEADS, size)
    grad_probs = jnp.einsum(
        "ihd,jhd->hij", grad_mixed, values_all, preferred_element_type=jnp.float32
    )
    delta = jnp.sum(probs * grad_probs, axis=-1, keepdims=True)
    grad_scores = (probs * (grad_probs - delta)).astype(jnp.bfloat16)
    grad_query = (
        jnp.einsum("hij,jhd->ihd", grad_scores, keys_all, preferred_element_type=jnp.float32)
        * scale
    )
    key_part = (
        jnp.einsum("hij,ihd->jhd", grad_scores, query, preferred_element_type=jnp.float32) * scale
    )
    value_part = jnp.einsum(
        "hij,ihd->jhd", probs_low, grad_mixed, preferred_element_type=jnp.float32
    )
    grad_key, grad_value = (
        lax.psum_scatter(key_part.reshape(-1, width), "row", scatter_dimension=0, tiled=True),
        lax.psum_scatter(value_part.reshape(-1, width), "row", scatter_dimension=0, tiled=True),
    )
    grad_qkvg = jnp.concatenate(
        [grad_query.reshape(rows, width), grad_key, grad_value, grad_gate], axis=-1
    ).astype(jnp.bfloat16)
    grads[(ATTEND, QKVG)] = outer_sum(lowered, grad_qkvg)
    grad_lowered = matmul(grad_qkvg, weights[(ATTEND, QKVG)].T)
    gain, shift = norm_pair(weights, ATTEND)
    grad_single, grads[(ATTEND, NORM_GAIN)], grads[(ATTEND, NORM_BIAS)] = norm_backward(
        single_state, gain, shift, grad_lowered
    )
    grad_bias = grad_scores.transpose(1, 2, 0)
    grads[(ATTEND, PAIR_PROJ)] = outer_sum(pair_low, grad_bias)
    grad_pair_low = matmul(grad_bias, weights[(ATTEND, PAIR_PROJ)].T)
    pair_gain = weights[(ATTEND, PAIR_GAIN)].astype(jnp.float32)
    pair_shift = weights[(ATTEND, PAIR_BIAS)].astype(jnp.float32)
    grad_pair, grads[(ATTEND, PAIR_GAIN)], grads[(ATTEND, PAIR_BIAS)] = norm_backward(
        pair_state, pair_gain, pair_shift, grad_pair_low
    )
    return (grad_single, grad_pair)


def shards(pair, single, lengths, params, moment_one, moment_two, pair_cotangent, single_cotangent):
    entries = layout(C, H, S, TA_HEADS, SA_HEADS)
    full = lax.all_gather(params.astype(jnp.bfloat16), "row", axis=0, tiled=True)
    weights = unpack(logical_order(full), entries)
    rows = pair.shape[1]
    length = pair.shape[2]
    first_row = lax.axis_index("row") * rows
    mask = (jnp.arange(length, dtype=jnp.int32) < lengths[0]).astype(jnp.float32)
    mask_rows = lax.dynamic_slice_in_dim(mask, first_row, rows)
    pair_mask = mask_rows[:, None] * mask[None, :]
    penalty = (mask - 1.0) * MASKED
    state = pair[0].astype(jnp.float32)
    saved = {}
    for prefix, incoming in ((OUTGOING, False), (INCOMING, True)):
        update, saved[prefix] = triangle_forward(state, pair_mask, weights, prefix, incoming)
        state = state + update
    for prefix, ending in ((STARTING, False), (ENDING, True)):
        update, saved[prefix] = attention_forward(state, penalty, weights, prefix, ending)
        state = state + update
    update, saved[PAIR] = transition_forward(state, weights, PAIR)
    pair_final = state + update
    single_state = single[0].astype(jnp.float32)
    update, saved[ATTEND] = single_forward(single_state, pair_final, penalty, weights)
    single_mid = single_state + update
    update, saved[SINGLE] = transition_forward(single_mid, weights, SINGLE)
    single_final = single_mid + update
    grads = {}
    grad_single = single_cotangent[0].astype(jnp.float32)
    grad_single = grad_single + transition_backward(
        saved[SINGLE], grad_single, weights, SINGLE, grads
    )
    from_single, from_pair = single_backward(saved[ATTEND], grad_single, weights, grads)
    grad_single = grad_single + from_single
    grad_pair = pair_cotangent[0].astype(jnp.float32) + from_pair
    grad_pair = grad_pair + transition_backward(saved[PAIR], grad_pair, weights, PAIR, grads)
    for prefix, ending in ((ENDING, True), (STARTING, False)):
        grad_pair = grad_pair + attention_backward(
            saved[prefix], grad_pair, penalty, weights, prefix, ending, grads
        )
    for prefix, incoming in ((INCOMING, True), (OUTGOING, False)):
        grad_pair = grad_pair + triangle_backward(
            saved[prefix], grad_pair, pair_mask, weights, prefix, incoming, grads
        )
    flat = stored_order(jnp.concatenate([grads[name].reshape(-1) for name, shape in entries]))
    shard_size = params.shape[0]
    row_index = lax.axis_index("row")
    total = lax.psum(flat, ("crop", "row"))
    shard = lax.dynamic_slice_in_dim(total, row_index * shard_size, shard_size)
    norm_squared = jnp.sum(total * total)
    clip_norm = jnp.sqrt(norm_squared)
    clipped = shard * (CLIP / jnp.maximum(clip_norm, CLIP))
    new_first = BETA_ONE * moment_one + (1.0 - BETA_ONE) * clipped
    new_second = BETA_TWO * moment_two + (1.0 - BETA_TWO) * clipped * clipped
    rates, decays = rate_tables(entries)
    rate_shard = lax.dynamic_slice_in_dim(jnp.asarray(rates), row_index * shard_size, shard_size)
    decay_shard = lax.dynamic_slice_in_dim(jnp.asarray(decays), row_index * shard_size, shard_size)
    first_hat = new_first / (1.0 - BETA_ONE**STEP)
    second_hat = new_second / (1.0 - BETA_TWO**STEP)
    new_params = params - rate_shard * (
        first_hat / (jnp.sqrt(second_hat) + ADAM_EPS) + decay_shard * params
    )
    return (
        pair_final.astype(jnp.bfloat16)[None],
        single_final.astype(jnp.bfloat16)[None],
        grad_pair[None],
        grad_single[None],
        new_params,
        new_first,
        new_second,
        clip_norm,
    )


F32 = jnp.float32
BF16 = jnp.bfloat16
LOG2E = 1.4426950408889634
VMEM_LIMIT = 56 * 1024 * 1024


def mm(left, right):
    return lax.dot_general(left, right, (((1,), (0,)), ((), ())), preferred_element_type=F32)


def mm_nt(left, right):
    return lax.dot_general(left, right, (((1,), (1,)), ((), ())), preferred_element_type=F32)


def mm_tn(left, right):
    return lax.dot_general(left, right, (((0,), (0,)), ((), ())), preferred_element_type=F32)


def standardize(values):
    centred = values - jnp.mean(values, axis=0, keepdims=True)
    spread = jnp.mean(centred * centred, axis=0, keepdims=True)
    inverse = lax.rsqrt(spread + EPSILON)
    return centred * inverse, inverse


def standardize_back(unit, inverse, grad_unit):
    first = jnp.mean(grad_unit, axis=0, keepdims=True)
    second = jnp.mean(grad_unit * unit, axis=0, keepdims=True)
    return inverse * (grad_unit - first - unit * second)


def sigmoid(values):
    return 0.5 * jnp.tanh(0.5 * values) + 0.5


def column(ref, index):
    return ref[:, index : index + 1]


def live_pair(info, alive, row):
    return jnp.concatenate(
        [jnp.where(info[row + place] > 0, alive[0:1], 0.0) for place in range(GROUP)], axis=1
    )


GROUP = 4
LAG = 4


def each_group(count, body):
    def step(index, carry):
        body(index * GROUP)
        return carry

    lax.fori_loop(0, count // GROUP, step, 0)


def each_channel(count, body):
    def step(index, carry):
        body(index)
        return carry

    lax.fori_loop(0, count, step, 0)


def join(read, ref, row):
    return jnp.concatenate([read(ref, row + place) for place in range(GROUP)], axis=1)


def pieces_of(values):
    length = values.shape[1] // GROUP
    return [values[:, place * length : (place + 1) * length] for place in range(GROUP)]


def put_rows(ref, row, values):
    for place, part in enumerate(pieces_of(values)):
        ref[row + place] = part.astype(ref.dtype)


def put_inner(scratch, row, values):
    for place, part in enumerate(pieces_of(values)):
        scratch[:, row + place, :] = part


def read_inner(scratch, row):
    return scratch[:, row, :]


def put_turned(scratch, row, values):
    for place, part in enumerate(pieces_of(values)):
        scratch[:, row + place, :] = part.T


def add_lanes(ref, values):
    ref[...] += sum(pieces_of(values))


def spec_full(shape):
    return pl.BlockSpec(shape, lambda step: (0,) * len(shape))


def cost(microseconds):
    return pl.CostEstimate(
        flops=int(microseconds * 1e9), bytes_accessed=int(microseconds * 3e6), transcendentals=0
    )


class Both(list):
    pass


def all_rows(ins, outs):
    extents = [shape[axis] for shape, dtype, axis in outs if axis is not None]
    for array, axis in ins:
        if isinstance(axis, int):
            extents += [member.shape[axis] for member in (array if isinstance(array, list) else [array])]
    return max(extents)


def run_rows(kernel, name, steps, ins, outs, scratch, time=15, half=None, before=None):
    grid = steps if half is None else steps // 2
    offset = grid * (half or 0)
    flat = []
    groups = []
    for array, axis in ins:
        members = array if isinstance(array, Both) else [array]
        flat += [(member, axis) for member in members]
        groups.append((len(members), isinstance(array, Both)))
    full = all_rows(flat, outs)

    def spec(shape, axis):
        if axis is None:
            return spec_full(shape)
        size = full // steps
        first = offset if shape[axis] == full else 0
        sizes = tuple(size if place == axis else extent for place, extent in enumerate(shape))
        return pl.BlockSpec(
            sizes,
            lambda step: tuple(step + first if place == axis else 0 for place in range(len(shape))),
        )

    in_specs = [
        pl.BlockSpec(memory_space=pltpu.SMEM) if axis == "smem" else spec(array.shape, axis)
        for array, axis in flat
    ]
    out_specs = [spec(shape, axis) for shape, dtype, axis in outs]
    arrays = [array for array, axis in flat]
    aliases = {}
    kept = []
    for place, (shape, dtype, axis) in enumerate(outs):
        if before is not None and (axis is None or shape[axis] == full):
            aliases[len(arrays)] = place
            kept.append(place)
            arrays.append(before[place])
            in_specs.append(spec_full(shape) if axis is None else pl.BlockSpec(memory_space=pl.ANY))

    def run(*refs):
        taken = iter(refs)
        given = []
        for number, together in groups:
            members = [next(taken) for _ in range(number)]
            given.append(members if together else members[0])
        held = {place: next(taken) for place in kept}
        results = [next(taken) for _ in outs]

        @pl.when(pl.program_id(0) == 0)
        def _():
            for place, (shape, dtype, axis) in enumerate(outs):
                if axis is None:
                    results[place][...] = (
                        held[place][...] if place in held else jnp.zeros(shape, dtype)
                    )

        kernel(*given, *results, *taken)

    return pl.pallas_call(
        run,
        grid=(grid,),
        in_specs=in_specs,
        out_specs=out_specs,
        out_shape=[jax.ShapeDtypeStruct(shape, dtype) for shape, dtype, axis in outs],
        scratch_shapes=[pltpu.VMEM(shape, dtype) for shape, dtype in scratch],
        input_output_aliases=aliases,
        compiler_params=pltpu.CompilerParams(vmem_limit_bytes=VMEM_LIMIT),
        cost_estimate=cost(time if half is None else time / 2),
        name=name,
    )(*arrays)


def run_halves(kernel, name, steps, ins, outs, scratch, time=15):
    results = []
    for half in range(2):
        chosen = [
            (array[half] if type(array) is list else array, axis) for array, axis in ins
        ]
        before = results[0] if half else None
        results.append(run_rows(kernel, name, steps, chosen, outs, scratch, time, half, before))
    full = all_rows(ins, outs)
    return [
        [results[0][place], results[1][place]]
        if axis is not None and shape[axis] != full
        else results[1][place]
        for place, (shape, dtype, axis) in enumerate(outs)
    ]


def zero_first(*refs):
    @pl.when(pl.program_id(0) == 0)
    def _():
        for ref in refs:
            ref[...] = jnp.zeros(ref.shape, ref.dtype)


def lane_sums(ref):
    return jnp.sum(ref[...].T, axis=0, keepdims=True)


def on_last(body):
    @pl.when(pl.program_id(0) == pl.num_programs(0) - 1)
    def _():
        body()


def read_plain(ref, row):
    return ref[row].astype(F32)


def reorder(values, order):
    size = values.shape[0] // len(order)
    return jnp.concatenate([values[place * size : (place + 1) * size] for place in order], axis=0)


def read_tokens(order, ref, row):
    return reorder(ref[row].astype(F32), order).T


def read_flipped(refs, row):
    parts = jnp.concatenate([ref[:, row] for ref in refs], axis=1)
    return parts.reshape(-1, parts.shape[-1]).astype(F32).T


def read_turned(order, ref, row):
    parts = ref[:, row]
    return reorder(parts.reshape(-1, parts.shape[-1]).astype(F32), order).T


def tri_pre_row(info, alive, row, state, cols, first, proj_t):
    unit, inverse = standardize(state)
    lowered = (unit * column(cols, first) + column(cols, first + 1)).astype(BF16)
    project = mm(proj_t[...], lowered)
    half = project.shape[0] // 2
    return project[:half] * sigmoid(project[half:]) * live_pair(info, alive, row)


def store_product(out, scratch, devices):
    hidden = scratch.shape[0] // 2
    part = hidden // devices

    def one(device, carry):
        out[device, 0] = scratch[pl.ds(device * part, part)].astype(BF16)
        out[device, 1] = scratch[pl.ds(hidden + device * part, part)].astype(BF16)
        return carry

    lax.fori_loop(0, devices, one, 0)


def copy_blocks(target, source, count):
    def one(index, carry):
        target[index] = source[index].astype(target.dtype)
        return carry

    lax.fori_loop(0, count, one, 0)


def store_flipped(out, scratch):
    devices, part = out.shape[0], out.shape[1]

    def one(device, carry):
        out[device] = scratch[pl.ds(device * part, part)].astype(out.dtype)
        return carry

    lax.fori_loop(0, devices, one, 0)


def tri_post_row(state, tri, cols, proj_t, gate_t):
    unit, inverse = standardize(state)
    lowered = (unit * column(cols, 0) + column(cols, 1)).astype(BF16)
    tri_unit, tri_inverse = standardize(tri)
    out_low = (tri_unit * column(cols, 2) + column(cols, 3)).astype(BF16)
    output = mm(proj_t[...], out_low)
    gate = sigmoid(mm(gate_t[...], lowered))
    return unit, inverse, lowered, tri_unit, tri_inverse, out_low, output, gate


def row_base(rows):
    return pl.program_id(0) * rows


def tri_pre_first_kernel(devices, read, info, alive, pair, cols, proj_t, out, scratch):
    rows = pair.shape[0]

    def body(row):
        product = tri_pre_row(
            info, alive, row_base(rows) + row, join(read, pair, row), cols, 0, proj_t
        )
        put_inner(scratch, row, product)

    each_group(rows, body)
    store_product(out, scratch, devices)


def whole_rows(refs, *place):
    parts = jnp.concatenate([ref[(slice(None),) + place] for ref in refs], axis=1)
    return parts.reshape(-1, parts.shape[-1])


def split_rows(values, outs, *place):
    part = outs[0].shape[-2]
    parts = values.astype(BF16).reshape(outs[0].shape[0], -1, values.shape[-1])
    for half, out in enumerate(outs):
        out[(slice(None),) + place] = parts[:, half * part : (half + 1) * part]


def tri_product_kernel(incoming, operands, *outs):
    def body(channel):
        first = whole_rows(operands, 0, channel)
        second = whole_rows(operands, 1, channel)
        tri = mm_tn(first, second) if incoming else mm_nt(first, second)
        split_rows(tri, outs, channel)

    each_channel(operands[0].shape[2], body)


def tri_join_kernel(
    devices, read, info, alive, source, tri_in, cols, proj_t, gate_t, next_cols, next_proj_t,
    state_out, out, tri_scratch, scratch,
):
    rows = state_out.shape[0]
    copy_blocks(tri_scratch, tri_in, tri_in.shape[0])

    def body(row):
        state = join(read, source, row)
        pieces = tri_post_row(state, join(read_inner, tri_scratch, row), cols, proj_t, gate_t)
        state = state + pieces[6] * pieces[7]
        put_rows(state_out, row, state)
        product = tri_pre_row(
            info, alive, row_base(rows) + row, state, next_cols, 0, next_proj_t
        )
        put_inner(scratch, row, product)

    each_group(rows, body)
    store_product(out, scratch, devices)


def tri_last_kernel(
    source, tri_in, cols, proj_t, gate_t, next_cols, bias_t, state_out, bias_out, tri_scratch, scratch
):
    rows = state_out.shape[0]
    copy_blocks(tri_scratch, tri_in, tri_in.shape[0])

    def body(row):
        state = join(read_plain, source, row)
        pieces = tri_post_row(state, join(read_inner, tri_scratch, row), cols, proj_t, gate_t)
        state = state + pieces[6] * pieces[7]
        put_rows(state_out, row, state)
        unit, inverse = standardize(state)
        lowered = (unit * column(next_cols, 0) + column(next_cols, 1)).astype(BF16)
        put_inner(scratch, row, mm(bias_t[...], lowered))

    each_group(rows, body)
    bias_out[...] = scratch[: bias_out.shape[0]].astype(BF16)


def flipped_bias_kernel(source, cols, bias_t, bias_out, scratch):
    rows = source[0].shape[1]

    def body(row):
        unit, inverse = standardize(join(read_flipped, source, row))
        lowered = (unit * column(cols, 0) + column(cols, 1)).astype(BF16)
        put_inner(scratch, row, mm(bias_t[...], lowered))

    each_group(rows, body)
    bias_out[...] = scratch[: bias_out.shape[0]].astype(BF16)


def fill_bias(alive, bias_in, table):
    @pl.when(pl.program_id(0) == 0)
    def _():
        length = table.shape[1]
        penalty = (alive[0:1] - 1.0) * (MASKED * LOG2E)
        for head in range(table.shape[0]):
            values = bias_in[:, head].reshape(length, length).astype(F32)
            table[head] = (values * LOG2E + penalty).T


def attention_row(state, cols, proj_t):
    unit, inverse = standardize(state)
    lowered = (unit * column(cols, 0) + column(cols, 1)).astype(BF16)
    project = mm(proj_t[...], lowered)
    width = project.shape[0] // 4
    size = width // TA_HEADS
    query = (project[:width] * (size**-0.5 * LOG2E)).astype(BF16)
    key = project[width : 2 * width].astype(BF16)
    value = project[2 * width : 3 * width].astype(BF16)
    gate = sigmoid(project[3 * width :])
    return unit, inverse, lowered, query, key, value, gate


def in_stages(blocks, first, second, third):
    early, late, done = {}, {}, {}
    count = len(blocks)
    for step in range(count + 2 * LAG):
        if step < count:
            early[step] = first(*blocks[step])
        if 0 <= step - LAG < count:
            late[step - LAG] = second(*blocks[step - LAG], early.pop(step - LAG))
        if 0 <= step - 2 * LAG < count:
            place = step - 2 * LAG
            done[blocks[place]] = third(*blocks[place], late.pop(place))
    return done


def head_rows(values, place, head):
    size, length = values.shape[0] // TA_HEADS, values.shape[1] // GROUP
    return values[head * size : (head + 1) * size, place * length : (place + 1) * length]


def gather_heads(done):
    return jnp.concatenate(
        [
            jnp.concatenate([done[place, head] for head in range(TA_HEADS)], axis=0)
            for place in range(GROUP)
        ],
        axis=1,
    )


ROW_BLOCKS = [(place, head) for place in range(GROUP) for head in range(TA_HEADS)]
HEAD_BLOCKS = [(place, head) for head in range(TA_HEADS) for place in range(GROUP)]


def attend_rows(state, row, cols, proj_t, output_t, table, totals, mixed_out):
    unit, inverse, lowered, query, key, value, gate = attention_row(state, cols, proj_t)

    def score(place, head):
        return mm_tn(head_rows(key, place, head), head_rows(query, place, head)) + table[head]

    def shift(place, head, scores):
        top = jnp.max(scores, axis=0, keepdims=True)
        return top, jnp.exp2(scores - top).astype(BF16)

    def mix(place, head, items):
        top, shifted = items
        values = head_rows(value, place, head)
        size = values.shape[0]
        values = jnp.concatenate([values, jnp.ones((16, values.shape[1]), BF16)], axis=0)
        result = mm(values, shifted)
        total = result[size : size + 1]
        return result[:size] / total, top + jnp.log2(total)

    done = in_stages(ROW_BLOCKS, score, shift, mix)
    mixed = gather_heads({block: items[0] for block, items in done.items()})
    put_rows(totals, row, gather_heads({block: items[1] for block, items in done.items()}))
    put_rows(mixed_out, row, mixed)
    return state + mm(output_t[...], (mixed * gate).astype(BF16))


def starting_kernel(
    alive, source, bias_in, cols, proj_t, output_t, out, totals, mixed, table, scratch
):
    fill_bias(alive, bias_in, table)
    rows = source.shape[0]

    def body(row):
        state = attend_rows(
            join(read_plain, source, row), row, cols, proj_t, output_t, table, totals, mixed
        )
        put_turned(scratch, row, state)

    each_group(rows, body)
    store_flipped(out, scratch)


def ending_kernel(alive, source, bias_in, cols, proj_t, output_t, out, totals, mixed, table):
    fill_bias(alive, bias_in, table)
    rows = source[0].shape[1]

    def body(row):
        state = attend_rows(
            join(read_flipped, source, row), row, cols, proj_t, output_t, table, totals, mixed
        )
        put_rows(out, row, state)

    each_group(rows, body)


def transition_kernel(
    order, source, cols, up_t, down_t, next_cols, bias_t, state_out, pair_out, bias_out, scratch, bias_scratch
):
    rows = source.shape[0]

    def body(row):
        state = join(read_plain, source, row)
        unit, inverse = standardize(state)
        lowered = (unit * column(cols, 0) + column(cols, 1)).astype(BF16)
        hidden = mm(up_t[...], lowered)
        half = hidden.shape[0] // 2
        first = hidden[:half]
        mixed = (first * sigmoid(first) * hidden[half:]).astype(BF16)
        state = state + mm(down_t[...], mixed)
        put_rows(state_out, row, state)
        put_turned(scratch, row, state)
        unit, inverse = standardize(state)
        lowered = (unit * column(next_cols, 0) + column(next_cols, 1)).astype(BF16)
        put_inner(bias_scratch, row, mm(bias_t[...], lowered))

    each_group(rows, body)
    size = pair_out.shape[0] // len(order)
    for place, held in enumerate(order):
        pair_out[place * size : (place + 1) * size] = scratch[held * size : (held + 1) * size].astype(BF16)
    bias_to_lanes(bias_out, bias_scratch)


def transition_back_kernel(
    read, mid, final, cotangent, bias_grad, cols, up_t, up, down, next_cols, bias_w,
    grad_out, up_grad, down_grad, bias_w_grad, vecs, norm_gain, norm_bias, pair_gain, pair_bias, bias_scratch,
):
    zero_first(norm_gain, norm_bias, pair_gain, pair_bias)
    rows = mid.shape[0]
    lanes_to_bias(bias_scratch, bias_grad)

    def body(row):
        grad = join(read, cotangent, row)
        unit, inverse = standardize(join(read_plain, final, row))
        gain = column(next_cols, 0)
        lowered = (unit * gain + column(next_cols, 1)).astype(BF16)
        grad_bias = join(read_inner, bias_scratch, row).astype(BF16)
        bias_w_grad[...] += mm_nt(lowered, grad_bias)
        grad_lowered = mm(bias_w[...], grad_bias)
        add_lanes(pair_gain, grad_lowered * unit)
        add_lanes(pair_bias, grad_lowered)
        grad = grad + standardize_back(unit, inverse, grad_lowered * gain)
        unit, inverse = standardize(join(read_plain, mid, row))
        gain = column(cols, 0)
        lowered = (unit * gain + column(cols, 1)).astype(BF16)
        hidden = mm(up_t[...], lowered)
        half = hidden.shape[0] // 2
        first, second = hidden[:half], hidden[half:]
        slope = sigmoid(first)
        silu = first * slope
        grad_low = grad.astype(BF16)
        grad_mixed = mm(down[...], grad_low)
        down_grad[...] += mm_nt((silu * second).astype(BF16), grad_low)
        grad_hidden = jnp.concatenate(
            [
                (grad_mixed * second * (slope + silu * (1.0 - slope))).astype(BF16),
                (grad_mixed * silu).astype(BF16),
            ],
            axis=0,
        )
        up_grad[...] += mm_nt(lowered, grad_hidden)
        grad_lowered = mm(up[...], grad_hidden)
        add_lanes(norm_gain, grad_lowered * unit)
        add_lanes(norm_bias, grad_lowered)
        put_rows(grad_out, row, grad + standardize_back(unit, inverse, grad_lowered * gain))

    each_group(rows, body)

    def finish():
        vecs[0:1] += lane_sums(norm_gain)
        vecs[1:2] += lane_sums(norm_bias)
        vecs[2:3] += lane_sums(pair_gain)
        vecs[3:4] += lane_sums(pair_bias)

    on_last(finish)


def attention_back_kernel(
    read, read_grad, alive, source, grad_in, bias_in, totals, mixed_in, cols, proj_t, proj, output,
    grad_out, bias_out, proj_grad, output_grad, table, grad_table,
):
    fill_bias(alive, bias_in, table)
    zero_first(grad_table)
    rows = grad_out.shape[0]

    def body(row):
        unit, inverse, lowered, query, key, value, gate = attention_row(
            join(read, source, row), cols, proj_t
        )
        mixed = join(read_plain, mixed_in, row)
        total = join(read_plain, totals, row)
        grad_low = join(read_grad, grad_in, row).astype(BF16)
        gated = mixed * gate
        output_grad[...] += mm_nt(gated.astype(BF16), grad_low)
        grad_gated = mm(output[...], grad_low)
        grad_gate = grad_gated * gated * (1.0 - gate)
        grad_mixed = (grad_gated * gate).astype(BF16)
        product = grad_mixed.astype(F32) * mixed
        size = query.shape[0] // TA_HEADS

        def score(place, head):
            scores = mm_tn(head_rows(key, place, head), head_rows(query, place, head))
            grads = mm_tn(head_rows(value, place, head), head_rows(grad_mixed, place, head))
            return scores + table[head], grads

        def slope(place, head, items):
            scores, grads = items
            probs = jnp.exp2(scores - head_rows(total, place, head))
            delta = jnp.sum(head_rows(product, place, head), axis=0, keepdims=True)
            grad_scores = probs * (grads - delta)
            grad_table[head] += grad_scores
            return probs.astype(BF16), grad_scores.astype(BF16)

        def back(place, head, items):
            probs, grad_scores = items
            return (
                mm(head_rows(key, place, head), grad_scores) * size**-0.5,
                mm_nt(head_rows(query, place, head), grad_scores) * (1.0 / LOG2E),
                mm_nt(head_rows(grad_mixed, place, head), probs),
            )

        done = in_stages(HEAD_BLOCKS, score, slope, back)
        grad_project = jnp.concatenate(
            [
                gather_heads({block: items[part] for block, items in done.items()})
                for part in range(3)
            ]
            + [grad_gate],
            axis=0,
        ).astype(BF16)
        proj_grad[...] += mm_nt(lowered, grad_project)
        put_rows(grad_out, row, mm(proj[...], grad_project))

    each_group(rows, body)

    def finish():
        for head in range(TA_HEADS):
            bias_out[:, head] = (
                grad_table[head].T.astype(BF16).reshape(bias_out.shape[0], bias_out.shape[2], -1)
            )

    on_last(finish)


def attention_end_row(
    state, grad, grad_lowered, grad_bias, cols, bias_w, bias_w_grad, norm_gain, norm_bias
):
    unit, inverse = standardize(state)
    gain = column(cols, 0)
    lowered = (unit * gain + column(cols, 1)).astype(BF16)
    bias_w_grad[...] += mm_nt(lowered, grad_bias)
    grad_lowered = grad_lowered + mm(bias_w[...], grad_bias)
    add_lanes(norm_gain, grad_lowered * unit)
    add_lanes(norm_bias, grad_lowered)
    return grad + standardize_back(unit, inverse, grad_lowered * gain)


def fill_bias_grad(scratch, bias_grad):
    heads = bias_grad.shape[1]
    total = bias_grad[0].astype(F32)
    for device in range(1, bias_grad.shape[0]):
        total = total + bias_grad[device].astype(F32)
    scratch[:heads] = total
    scratch[heads:] = jnp.zeros((scratch.shape[0] - heads,) + scratch.shape[1:], F32)


def ending_end_kernel(
    source, grad_in, grad_lowered, bias_grad, cols, bias_w,
    grad_out, bias_w_grad, vecs, norm_gain, norm_bias, bias_scratch, scratch,
):
    zero_first(norm_gain, norm_bias)
    fill_bias_grad(bias_scratch, bias_grad)
    rows = grad_in.shape[0]

    def body(row):
        grad = attention_end_row(
            join(read_flipped, source, row), join(read_plain, grad_in, row),
            join(read_plain, grad_lowered, row), join(read_inner, bias_scratch, row).astype(BF16), cols, bias_w, bias_w_grad, norm_gain, norm_bias,
        )
        put_turned(scratch, row, grad)

    each_group(rows, body)
    store_flipped(grad_out, scratch)

    def finish():
        vecs[0:1] += lane_sums(norm_gain)
        vecs[1:2] += lane_sums(norm_bias)

    on_last(finish)


def tri_post_back_row(
    state, tri, grad, cols, proj_t, gate_t, proj, gate_w, proj_grad, gate_grad, out_gain, out_bias
):
    unit, inverse, lowered, tri_unit, tri_inverse, out_low, output, gate = tri_post_row(
        state, tri, cols, proj_t, gate_t
    )
    grad_output = grad * gate
    grad_gate = (grad_output * output * (1.0 - gate)).astype(BF16)
    grad_output = grad_output.astype(BF16)
    proj_grad[...] += mm_nt(out_low, grad_output)
    gate_grad[...] += mm_nt(lowered, grad_gate)
    grad_normed = mm(proj[...], grad_output)
    add_lanes(out_gain, grad_normed * tri_unit)
    add_lanes(out_bias, grad_normed)
    grad_tri = standardize_back(tri_unit, tri_inverse, grad_normed * column(cols, 2))
    return grad_tri, mm(gate_w[...], grad_gate)


def starting_end_kernel(
    source, grad_in, grad_lowered, bias_grad, cols, bias_w,
    below, tri_in, tri_cols, proj_t, gate_t, proj, gate_w,
    grad_out, tri_out, gate_back, bias_w_grad, proj_grad, gate_grad, vecs,
    norm_gain, norm_bias, out_gain, out_bias, bias_scratch, tri_scratch,
):
    zero_first(norm_gain, norm_bias, out_gain, out_bias)
    fill_bias_grad(bias_scratch, bias_grad)
    copy_blocks(tri_scratch, tri_in, tri_in.shape[0])
    rows = source.shape[0]

    def body(row):
        grad = attention_end_row(
            join(read_plain, source, row), join(read_flipped, grad_in, row),
            join(read_plain, grad_lowered, row), join(read_inner, bias_scratch, row).astype(BF16), cols, bias_w, bias_w_grad, norm_gain, norm_bias,
        )
        put_rows(grad_out, row, grad)
        grad_tri, back = tri_post_back_row(
            join(read_plain, below, row), join(read_inner, tri_scratch, row), grad, tri_cols, proj_t, gate_t, proj, gate_w,
            proj_grad, gate_grad, out_gain, out_bias,
        )
        put_rows(gate_back, row, back)
        put_inner(tri_scratch, row, grad_tri)

    each_group(rows, body)
    copy_blocks(tri_out, tri_scratch, tri_out.shape[0])

    def finish():
        vecs[0:1] += lane_sums(norm_gain)
        vecs[1:2] += lane_sums(norm_bias)
        vecs[2:3] += lane_sums(out_gain)
        vecs[3:4] += lane_sums(out_bias)

    on_last(finish)


def tri_product_back_kernel(incoming, grad, operands, *outs):
    def body(channel):
        first = whole_rows(operands, 0, channel)
        second = whole_rows(operands, 1, channel)
        tri = whole_rows(grad, channel)
        if incoming:
            grad_first = mm_nt(second, tri)
            grad_second = mm(first, tri)
        else:
            grad_first = mm(tri, second)
            grad_second = mm_tn(tri, first)
        split_rows(grad_first, outs, 0, channel)
        split_rows(grad_second, outs, 1, channel)

    each_channel(operands[0].shape[2], body)


def tri_pre_back_row(
    info, alive, row, state, product_grad, gate_back, grad, cols, proj_t, proj, proj_grad, norm_gain, norm_bias
):
    unit, inverse = standardize(state)
    gain = column(cols, 0)
    lowered = (unit * gain + column(cols, 1)).astype(BF16)
    project = mm(proj_t[...], lowered)
    half = project.shape[0] // 2
    gate = sigmoid(project[half:])
    grad_first = product_grad * gate * live_pair(info, alive, row)
    grad_second = grad_first * project[:half] * (1.0 - gate)
    grad_project = jnp.concatenate([grad_first.astype(BF16), grad_second.astype(BF16)], axis=0)
    proj_grad[...] += mm_nt(lowered, grad_project)
    grad_lowered = mm(proj[...], grad_project) + gate_back
    add_lanes(norm_gain, grad_lowered * unit)
    add_lanes(norm_bias, grad_lowered)
    return grad + standardize_back(unit, inverse, grad_lowered * gain)


def fill_product_grad(scratch, product_grad):
    devices, part = product_grad.shape[0], product_grad.shape[2]

    def one(device, carry):
        scratch[pl.ds(device * part, part)] = product_grad[device, 0].astype(F32)
        scratch[pl.ds((devices + device) * part, part)] = product_grad[device, 1].astype(F32)
        return carry

    lax.fori_loop(0, devices, one, 0)


def tri_join_back_kernel(
    read, info, alive, source, product_grad, gate_in, grad_in, cols, proj_t, proj,
    below, tri_in, tri_cols, out_t, gate_t, out_w, gate_w,
    grad_out, tri_out, gate_back, proj_grad, out_grad, gate_grad, vecs,
    norm_gain, norm_bias, out_gain, out_bias, scratch, tri_scratch,
):
    zero_first(norm_gain, norm_bias, out_gain, out_bias)
    fill_product_grad(scratch, product_grad)
    copy_blocks(tri_scratch, tri_in, tri_in.shape[0])
    rows = source.shape[0]

    def body(row):
        grad = tri_pre_back_row(
            info, alive, row_base(rows) + row, join(read_plain, source, row),
            join(read_inner, scratch, row), join(read_plain, gate_in, row),
            join(read_plain, grad_in, row), cols, proj_t, proj, proj_grad, norm_gain, norm_bias,
        )
        put_rows(grad_out, row, grad)
        grad_tri, back = tri_post_back_row(
            join(read, below, row), join(read_inner, tri_scratch, row), grad, tri_cols, out_t, gate_t, out_w, gate_w,
            out_grad, gate_grad, out_gain, out_bias,
        )
        put_rows(gate_back, row, back)
        put_inner(tri_scratch, row, grad_tri)

    each_group(rows, body)
    copy_blocks(tri_out, tri_scratch, tri_out.shape[0])

    def finish():
        vecs[0:1] += lane_sums(norm_gain)
        vecs[1:2] += lane_sums(norm_bias)
        vecs[2:3] += lane_sums(out_gain)
        vecs[3:4] += lane_sums(out_bias)

    on_last(finish)


def tri_first_back_kernel(
    read, order, info, alive, source, product_grad, gate_in, grad_in, cols, proj_t, proj,
    grad_out, proj_grad, vecs, norm_gain, norm_bias, scratch,
):
    zero_first(norm_gain, norm_bias)
    fill_product_grad(scratch, product_grad)
    rows = source.shape[0]

    def body(row):
        grad = tri_pre_back_row(
            info, alive, row_base(rows) + row, join(read, source, row),
            join(read_inner, scratch, row), join(read_plain, gate_in, row),
            join(read_plain, grad_in, row), cols, proj_t, proj, proj_grad, norm_gain, norm_bias,
        )
        for place, part in enumerate(pieces_of(grad)):
            grad_out[row + place] = reorder(part.T, order).astype(grad_out.dtype)

    each_group(rows, body)

    def finish():
        vecs[0:1] += lane_sums(norm_gain)
        vecs[1:2] += lane_sums(norm_bias)

    on_last(finish)


RUN = 24


def table_of(entries):
    table = {}
    offset = 0
    for name, shape in entries:
        table[name] = (offset // STRIDE, shape)
        offset += math.prod(shape)
    return table, offset


def runs_kernel(info, shard, out, scratch):
    def one(block, carry):
        scratch[:, block, :] = shard[pl.ds(block * STRIDE, STRIDE), :].T
        return carry

    lax.fori_loop(0, RUN, one, 0)
    half = STRIDE // 2
    turn = info[0] * half

    def move(lane, carry):
        out[lane] = scratch[lax.rem(lane + turn, STRIDE)].astype(BF16)
        return carry

    lax.fori_loop(0, STRIDE, move, 0)


def run_place(shards, total, lane, shard):
    count = total // STRIDE
    whole = total // shards
    step, odd = whole // STRIDE, (whole % STRIDE) // (STRIDE // 2)
    extra = lax.div(shard * odd + jnp.where(lane < STRIDE // 2, 1, 0), 2)
    start = lane * count + shard * step + extra
    return lax.div(start, STRIDE), lax.rem(start, STRIDE)


def rows_from_runs(runs, rows, first_lane, total):
    shards, lanes = runs.shape[0], runs.shape[1]
    base = first_lane * (total // STRIDE) // STRIDE

    def one(index, carry):
        lane, shard = lax.div(index, shards), lax.rem(index, shards)
        row, shift = run_place(shards, total, first_lane + lane, shard)
        row = row - base
        turned = pltpu.roll(runs[shard, lane].astype(F32), shift, 1)
        place = lax.broadcasted_iota(jnp.int32, (RUN + 1, STRIDE), 1)
        last, before = carry
        joint = jnp.where(row - before == RUN, last[2:3], last[1:2])
        below = jnp.concatenate([joint, turned], axis=0)
        above = jnp.concatenate([turned, turned[RUN - 1 :]], axis=0)
        values = jnp.where(place < shift, below, above)
        rows[pl.ds(row, RUN + 1), :] = values
        return values[RUN - 2 :], row

    lax.fori_loop(0, shards * lanes, one, (jnp.zeros((3, STRIDE), F32), -RUN), unroll=4)


def runs_from_rows(rows, out, first_lane, base, total):
    shards, lanes = out.shape[0], out.shape[1]

    def one(index, carry):
        lane, shard = lax.div(index, shards), lax.rem(index, shards)
        row, shift = run_place(shards, total, first_lane + lane, shard)
        turned = pltpu.roll(rows[pl.ds(row - base, RUN + 1), :], (STRIDE - shift) % STRIDE, 1)
        place = lax.broadcasted_iota(jnp.int32, (RUN, STRIDE), 1)
        out[shard, lane] = jnp.where(
            place < STRIDE - shift, turned[:RUN], turned[1:]
        ).astype(BF16)
        return carry

    lax.fori_loop(0, shards * lanes, one, 0, unroll=4)


def row_height(base, first_lane, last_lane, total):
    end = (last_lane * (total // STRIDE)) // STRIDE + RUN + 2
    return -(-(end - base) // 8) * 8


def take_matrix(rows, first, shape):
    blocks = shape[1] // STRIDE
    return [
        rows[pl.ds(first + block, shape[0], stride=blocks), :]
        if blocks > 1
        else rows[first : first + shape[0], :]
        for block in range(blocks)
    ]


def put_matrix(rows, first, matrix):
    height, width = matrix.shape
    blocks = width // STRIDE
    for block in range(blocks):
        part = matrix[:, block * STRIDE : (block + 1) * STRIDE]
        if blocks > 1:
            rows[pl.ds(first + block, height, stride=blocks), :] = part
        else:
            rows[first : first + height, :] = part


def spread(index, heads, rows):
    lane = lax.broadcasted_iota(jnp.int32, (STRIDE, STRIDE), 0)
    channel = lax.broadcasted_iota(jnp.int32, (STRIDE, STRIDE), 1)
    return (channel == index * (STRIDE // heads) + lane // heads).astype(BF16)


def take_narrow(rows, first, heads, high):
    total = jnp.zeros((high, STRIDE), F32)
    head = lax.broadcasted_iota(jnp.int32, (high, STRIDE), 0)
    lane = lax.broadcasted_iota(jnp.int32, (high, STRIDE), 1)
    for index in range(heads):
        line = rows[first + index : first + index + 1, :]
        picked = jnp.where(lane % heads == head, line, 0.0).astype(BF16)
        total = total + mm(picked, spread(index, heads, rows))
    return total


def put_narrow(rows, first, heads, matrix):
    turned = matrix.T.astype(BF16)
    high = turned.shape[0]
    head = lax.broadcasted_iota(jnp.int32, (high, STRIDE), 0)
    lane = lax.broadcasted_iota(jnp.int32, (high, STRIDE), 1)
    for index in range(heads):
        wide = mm_nt(turned, spread(index, heads, rows))
        rows[first + index : first + index + 1, :] = jnp.sum(
            jnp.where(lane % heads == head, wide, 0.0), axis=0, keepdims=True
        )


PAIR_MATRICES = (
    (OUTGOING, PROJ_GATE), (OUTGOING, PROJ_OUT), (OUTGOING, GATE_OUT),
    (INCOMING, PROJ_GATE), (INCOMING, PROJ_OUT), (INCOMING, GATE_OUT),
    (STARTING, QKVG), (STARTING, OUTPUT), (ENDING, QKVG), (ENDING, OUTPUT), (PAIR, UP), (PAIR, DOWN),
)
PAIR_COLUMNS = (
    (OUTGOING, ((OUTGOING, NORM_GAIN), (OUTGOING, NORM_BIAS), (OUTGOING, OUT_GAIN), (OUTGOING, OUT_BIAS))),
    (INCOMING, ((INCOMING, NORM_GAIN), (INCOMING, NORM_BIAS), (INCOMING, OUT_GAIN), (INCOMING, OUT_BIAS))),
    (STARTING, ((STARTING, NORM_GAIN), (STARTING, NORM_BIAS))),
    (ENDING, ((ENDING, NORM_GAIN), (ENDING, NORM_BIAS))),
    (PAIR, ((PAIR, NORM_GAIN), (PAIR, NORM_BIAS))),
)
SINGLE_MATRICES = ((ATTEND, QKVG), (ATTEND, OUTPUT), (SINGLE, UP), (SINGLE, DOWN))
SINGLE_VECTORS = ((ATTEND, NORM_GAIN), (ATTEND, NORM_BIAS), (SINGLE, NORM_GAIN), (SINGLE, NORM_BIAS))


def put_columns(rows, out, table, base, names):
    out[...] = jnp.zeros(out.shape, F32)
    lines = [rows[table[name][0] - base : table[name][0] - base + 1, :] for name in names]
    lines.append(jnp.zeros((8 - len(lines), STRIDE), F32))
    out[...] = jnp.concatenate(lines, axis=0).T


def unpack_pair_kernel(table, total, runs, *refs):
    rows = refs[-1]
    outs = list(refs[:-1])
    rows_from_runs(runs, rows, 0, total)
    for name in PAIR_MATRICES:
        first, shape = table[name]
        plain, turned = outs.pop(0), outs.pop(0)
        for block, part in enumerate(take_matrix(rows, first, shape)):
            place = slice(block * STRIDE, (block + 1) * STRIDE)
            plain[:, place] = part.astype(BF16)
            turned[place, :] = part.T.astype(BF16)
    for prefix in (STARTING, ENDING):
        plain, turned = outs.pop(0), outs.pop(0)
        first, shape = table[(prefix, BIAS_PROJ)]
        matrix = take_narrow(rows, first, shape[1], 8)
        turned[...] = matrix.astype(BF16)
        plain[...] = matrix.T.astype(BF16)
    for prefix, names in PAIR_COLUMNS:
        put_columns(rows, outs.pop(0), table, 0, names)


def unpack_single_kernel(table, total, first_lane, runs, *refs):
    rows = refs[-1]
    outs = list(refs[:-1])
    rows_from_runs(runs, rows, first_lane, total)
    base = first_lane * (total // STRIDE) // STRIDE
    for name in SINGLE_MATRICES:
        first, shape = table[name]
        out = outs.pop(0)
        for block, part in enumerate(take_matrix(rows, first - base, shape)):
            out[:, block * STRIDE : (block + 1) * STRIDE] = part.astype(BF16)
    first, shape = table[(ATTEND, PAIR_PROJ)]
    matrix = take_narrow(rows, first - base, shape[1], shape[1])
    plain, turned = outs.pop(0), outs.pop(0)
    turned[...] = matrix.astype(BF16)
    plain[...] = matrix.T.astype(BF16)
    put_columns(rows, outs.pop(0), table, base, ((ATTEND, PAIR_GAIN), (ATTEND, PAIR_BIAS)))
    lines = outs.pop(0)
    lines[...] = jnp.zeros(lines.shape, F32)
    for index, name in enumerate(SINGLE_VECTORS):
        first, shape = table[name]
        for block in range(shape[0] // STRIDE):
            lines[index : index + 1, block * STRIDE : (block + 1) * STRIDE] = rows[
                first - base + block : first - base + block + 1, :
            ]


def pack_kernel(table, total, first_lane, base, names, *refs):
    ins, out, rows = refs[: len(names)], refs[-2], refs[-1]
    for name, ref in zip(names, ins):
        if isinstance(name, tuple):
            first, shape = table[name]
            if shape[1] % STRIDE:
                put_narrow(rows, first - base, shape[1], ref[...])
            else:
                put_matrix(rows, first - base, ref)
        else:
            for index, vector in name:
                first, shape = table[vector]
                for block in range(shape[0] // STRIDE):
                    rows[first + block - base : first + block - base + 1, :] = ref[
                        index : index + 1, block * STRIDE : (block + 1) * STRIDE
                    ]
    runs_from_rows(rows, out, first_lane, base, total)


def shard_kernel(whole, info, summed, others, out, squares, runs):
    half = STRIDE // 2
    crops, first, part = summed.shape[0], summed.shape[1], others.shape[1]

    def add(lane, carry):
        runs[lane] = sum(summed[crop, lane].astype(F32) for crop in range(crops))
        return carry

    lax.fori_loop(0, first, add, 0)
    for crop in range(crops):

        def move(lane, carry, crop=crop):
            runs[first + crop * part + lane] = others[crop, lane].astype(F32)
            return carry

        lax.fori_loop(0, part, move, 0)
    squares[...] = jnp.zeros(squares.shape, F32)

    def one(block, carry):
        first = runs[pl.ds(info[0] * half, half), block, :]
        second = runs[pl.ds(half - info[0] * half, half), block, :]
        values = jnp.concatenate([first, second], axis=0).T
        row = block * STRIDE + lax.broadcasted_iota(jnp.int32, values.shape, 0)
        lane = lax.broadcasted_iota(jnp.int32, values.shape, 1)
        values = jnp.where(row * STRIDE + lane < whole, values, 0.0)
        out[pl.ds(block * STRIDE, STRIDE), :] = values
        squares[...] += jnp.sum((values * values).reshape(-1, 8, STRIDE), axis=0)
        return carry

    lax.fori_loop(0, RUN, one, 0)


def whole_call(kernel, name, ins, outs, scratch, time=8):
    def spec(axis):
        return pl.BlockSpec(memory_space=pltpu.SMEM if axis == "smem" else pltpu.VMEM)

    return pl.pallas_call(
        kernel,
        in_specs=[spec(axis) for array, axis in ins],
        out_specs=[pl.BlockSpec(memory_space=pltpu.VMEM) for shape, dtype in outs],
        out_shape=[jax.ShapeDtypeStruct(shape, dtype) for shape, dtype in outs],
        scratch_shapes=[pltpu.VMEM(shape, dtype) for shape, dtype in scratch],
        compiler_params=pltpu.CompilerParams(vmem_limit_bytes=VMEM_LIMIT),
        cost_estimate=cost(time),
        name=name,
    )(*[array for array, axis in ins])


def unpack_pair(table, total, runs):
    outs = []
    names = []
    for name in PAIR_MATRICES:
        shape = table[name][1]
        outs += [(shape, BF16), (shape[::-1], BF16)]
        names += [name, (name, T)]
    for prefix in (STARTING, ENDING):
        outs += [((STRIDE, 8), BF16), ((8, STRIDE), BF16)]
        names += [(prefix, BIAS_W), (prefix, BIAS_T)]
    for prefix, parts in PAIR_COLUMNS:
        outs.append(((STRIDE, 8), F32))
        names.append((prefix, COLS))
    height = row_height(0, 0, runs.shape[1], total)
    values = whole_call(
        functools.partial(unpack_pair_kernel, table, total), "pair_weights", [(runs, None)], outs,
        [((height, STRIDE), F32)],
    )
    return dict(zip(names, values))


def unpack_single(table, total, first_lane, runs):
    outs = [(table[name][1], BF16) for name in SINGLE_MATRICES]
    names = list(SINGLE_MATRICES)
    shape = table[(ATTEND, PAIR_PROJ)][1]
    outs += [(shape, BF16), (shape[::-1], BF16), ((STRIDE, 8), F32), ((8, S), F32)]
    names += [(ATTEND, PAIR_PROJ), ((ATTEND, PAIR_PROJ), T), (ATTEND, COLS), (SINGLE, VECTORS)]
    base = first_lane * (total // STRIDE) // STRIDE
    height = row_height(base, first_lane, first_lane + runs.shape[1], total)
    values = whole_call(
        functools.partial(unpack_single_kernel, table, total, first_lane), "single_weights",
        [(runs, None)], outs, [((height, STRIDE), F32)],
    )
    return dict(zip(names, values))


def pack(name, table, total, shards, lanes, base, parts):
    height = row_height(base, *lanes, total)
    for held, array in parts:
        if isinstance(held, tuple):
            end = table[held][0] - base + array.shape[0] * max(1, array.shape[1] // STRIDE)
            height = max(height, -(-end // 8) * 8)
    return whole_call(
        functools.partial(pack_kernel, table, total, lanes[0], base, [held for held, array in parts]),
        name, [(array, None) for held, array in parts],
        [((shards, lanes[1] - lanes[0], RUN, STRIDE), BF16)], [((height, STRIDE), F32)],
    )[0]


def bias_to_lanes(out, scratch):
    heads, devices = scratch.shape[0], out.shape[0]
    part = scratch.shape[2] // devices
    per = STRIDE // part
    lane = lax.broadcasted_iota(jnp.int32, (scratch.shape[1], STRIDE), 1)
    for device in range(devices):
        block, place = device // per, device % per
        for first in range(0, heads, per):
            total = None
            for index in range(per):
                values = scratch[first + index, :, block * STRIDE : (block + 1) * STRIDE]
                values = pltpu.roll(values, (index - place) * part % STRIDE, 1)
                total = values if index == 0 else jnp.where(lane < index * part, total, values)
            out[device, :, first * part : first * part + STRIDE] = total.astype(out.dtype)


def lanes_to_bias(scratch, sent):
    heads, devices = scratch.shape[0], sent.shape[0]
    part = scratch.shape[2] // devices
    per = STRIDE // part
    lane = lax.broadcasted_iota(jnp.int32, (scratch.shape[1], STRIDE), 1)
    for head in range(heads):
        first, index = head // per * per, head % per
        for block in range(devices // per):
            total = None
            for place in range(per):
                values = sent[block * per + place, :, first * part : first * part + STRIDE].astype(F32)
                values = pltpu.roll(values, (place - index) * part % STRIDE, 1)
                total = values if place == 0 else jnp.where(lane < place * part, total, values)
            scratch[head, :, block * STRIDE : (block + 1) * STRIDE] = total


def standardize_lanes(values):
    centred = values - jnp.mean(values, axis=1, keepdims=True)
    inverse = lax.rsqrt(jnp.mean(centred * centred, axis=1, keepdims=True) + EPSILON)
    return centred * inverse, inverse


def single_kernel(
    state_in, back_in, project, kv, bias, alive, vectors, output_w, up, down,
    final_out, grad_out, score_grad, kv_grad, query_grad, gate_grad, output_grad, up_grad, down_grad, vecs,
):
    state = state_in[...]
    rows, width = state.shape
    size = width // SA_HEADS
    per = STRIDE // rows
    groups = SA_HEADS // per
    scale = size**-0.5
    tokens = kv.shape[0] * rows
    both = kv[...].reshape(tokens, 2 * width)
    keys, values = both[:, :width], both[:, width:]
    penalty = ((alive[...] - 1.0) * (MASKED * LOG2E)).T[:, 0:1]

    channel = lax.broadcasted_iota(jnp.int32, (width, STRIDE), 0)
    lane = lax.broadcasted_iota(jnp.int32, (width, STRIDE), 1)
    own = [lax.div(channel, size) == group * per + lax.div(lane, rows) for group in range(groups)]
    channel_b = lax.broadcasted_iota(jnp.int32, (STRIDE, width), 1)
    row_b = lax.broadcasted_iota(jnp.int32, (STRIDE, width), 0)
    own_b = [lax.div(channel_b, size) == group * per + lax.div(row_b, rows) for group in range(groups)]

    def spread_rows(matrix):
        turned = jnp.concatenate([matrix] * per, axis=0).T
        return [jnp.where(mask, turned, 0.0).astype(BF16) for mask in own]

    def collect(blocks):
        total = sum(jnp.where(mask, block, 0.0) for mask, block in zip(own_b, blocks))
        return sum(total[index * rows : (index + 1) * rows] for index in range(per))

    queries = spread_rows(project[:, :width] * (scale * LOG2E))
    gate = sigmoid(project[:, 3 * width :])
    scores = [
        mm(keys, queries[group])
        + bias[:, :, group * STRIDE : (group + 1) * STRIDE].reshape(tokens, STRIDE).astype(F32) * LOG2E
        + penalty
        for group in range(groups)
    ]
    shifted = [jnp.exp2(block - jnp.max(block, axis=0, keepdims=True)) for block in scores]
    probs = [block / jnp.sum(block, axis=0, keepdims=True) for block in shifted]
    probs_low = [block.astype(BF16) for block in probs]
    mixed = collect([mm_tn(block, values) for block in probs_low])
    gated = mixed * gate
    gated_low = gated.astype(BF16)
    state = state + mm(gated_low, output_w[...])

    unit, inverse = standardize_lanes(state)
    gain = vectors[2:3]
    lowered = (unit * gain + vectors[3:4]).astype(BF16)
    hidden = mm(lowered, up[...])
    half = hidden.shape[1] // 2
    first, second = hidden[:, :half], hidden[:, half:]
    slope = sigmoid(first)
    silu = first * slope
    swish = (silu * second).astype(BF16)
    final_out[...] = state + mm(swish, down[...])

    grad = back_in[...]
    grad_low = grad.astype(BF16)
    grad_mixed = mm_nt(grad_low, down[...])
    down_grad[...] = mm_tn(swish, grad_low)
    grad_hidden = jnp.concatenate(
        [
            (grad_mixed * second * (slope + silu * (1.0 - slope))).astype(BF16),
            (grad_mixed * silu).astype(BF16),
        ],
        axis=1,
    )
    grad_lowered = mm_nt(grad_hidden, up[...])
    vecs[...] = jnp.zeros(vecs.shape, F32)
    vecs[0:1] = jnp.sum(grad_lowered * unit, axis=0, keepdims=True)
    vecs[1:2] = jnp.sum(grad_lowered, axis=0, keepdims=True)
    grad_unit = grad_lowered * gain
    grad = grad + inverse * (
        grad_unit
        - jnp.mean(grad_unit, axis=1, keepdims=True)
        - unit * jnp.mean(grad_unit * unit, axis=1, keepdims=True)
    )
    grad_out[...] = grad

    grad_low = grad.astype(BF16)
    grad_gated = mm_nt(grad_low, output_w[...])
    gate_grad[...] = grad_gated * gated * (1.0 - gate)
    grads = spread_rows(grad_gated * gate)
    grad_probs = [mm(values, block) for block in grads]
    grad_scores = []
    for block, grad_block in zip(probs, grad_probs):
        delta = jnp.sum(block * grad_block, axis=0, keepdims=True)
        grad_scores.append((block * (grad_block - delta)).astype(BF16))
    for group, block in enumerate(grad_scores):
        score_grad[:, :, group * STRIDE : (group + 1) * STRIDE] = block.reshape(kv.shape[0], rows, STRIDE)
    query_grad[...] = collect([mm_tn(block, keys) for block in grad_scores]) * scale
    key_part = sum(mm_nt(block, query) for block, query in zip(grad_scores, queries)) * (1.0 / LOG2E)
    value_part = sum(mm_nt(block, grad_block) for block, grad_block in zip(probs_low, grads))
    kv_grad[:, :, :width] = key_part.astype(BF16).reshape(kv.shape[0], rows, width)
    kv_grad[:, :, width:] = value_part.astype(BF16).reshape(kv.shape[0], rows, width)
    output_grad[...] = mm_tn(gated_low, grad_low)
    up_grad[...] = mm_tn(lowered, grad_hidden)


def single_middle(state, back, projected, bias, alive, weights):
    lowered, project, kv = projected
    rows, width = state.shape
    devices = kv.shape[0]
    names = ((ATTEND, OUTPUT), (SINGLE, UP), (SINGLE, DOWN))
    matrices = [weights[name] for name in names]
    square = (rows, width)
    outs = [
        (square, F32), (square, F32), ((devices, rows, SA_HEADS * rows), BF16),
        ((devices, rows, 2 * width), BF16), (square, F32), (square, F32),
    ] + [(matrix.shape, F32) for matrix in matrices] + [((8, width), F32)]
    ins = [state, back, project, kv, bias, alive, weights[(SINGLE, VECTORS)]] + matrices
    final, grad, score_grad, kv_grad, query_grad, gate_grad, *found, vecs = whole_call(
        single_kernel, "single_path", [(array, None) for array in ins], outs, [], 15
    )
    grads = dict(zip(names, found))
    grads[(SINGLE, NORM_GAIN)], grads[(SINGLE, NORM_BIAS)] = vecs[0], vecs[1]
    return final, grad, score_grad, grads, (kv_grad, state, lowered, query_grad, gate_grad)


def swap(values, group):
    return lax.all_to_all(values, group, split_axis=0, concat_axis=0, tiled=True)


def single_project(single_state, weights, devices):
    gain, shift = norm_pair(weights, ATTEND)
    lowered = layer_norm(single_state, gain, shift).astype(BF16)
    width = lowered.shape[1]
    qkvg = matmul(lowered, weights[(ATTEND, QKVG)])
    both = qkvg[:, width : 3 * width].astype(BF16)
    both = jnp.broadcast_to(both[None], (devices,) + both.shape)
    return lowered, qkvg, both


def single_attend_end(pending, parts, weights, grads):
    _, single_state, lowered, grad_query, grad_gate = pending
    rows, width = lowered.shape
    grad_both = jnp.sum(parts.astype(F32), axis=0)
    grad_qkvg = jnp.concatenate(
        [grad_query.reshape(rows, width), grad_both, grad_gate], axis=-1
    ).astype(BF16)
    grads[(ATTEND, QKVG)] = outer_sum(lowered, grad_qkvg)
    grad_lowered = matmul(grad_qkvg, weights[(ATTEND, QKVG)].T)
    gain, shift = norm_pair(weights, ATTEND)
    grad_single, grads[(ATTEND, NORM_GAIN)], grads[(ATTEND, NORM_BIAS)] = norm_backward(
        single_state, gain, shift, grad_lowered
    )
    return grad_single


def after(values, *others):
    held = lax.optimization_barrier((values,) + others)
    return held


def in_turn():
    last = []

    def send(values, axes):
        if last:
            values = after(values, last.pop())[0]
        moved = swap(values, axes)
        last.append(moved)
        return moved

    return send


def pair_path(pair, info, alive, orders, weights, cotangent, middle, between, meet, send, group, parts):
    rows, length, width = pair.shape
    hidden = weights[(OUTGOING, PROJ_OUT)].shape[0]
    devices = length // rows
    cores = devices // parts
    order, order_back = orders
    read_first = functools.partial(read_tokens, order)
    read_last = functools.partial(read_turned, order)
    part = hidden // devices
    steps = rows // 16
    state_shape = (rows, width, length)
    block = rows // steps
    half = rows // 2
    flip_shape = (devices, rows, rows, width)
    product_shape = (devices, 2, part, rows, length)
    product_half = (devices, 2, part, half, length)
    tri_shape = (devices, part, rows, length)
    tri_half = (devices, part, half, length)
    channel_block = math.gcd(part, 4)

    def products(name, kernel, arrays, out_shape):
        axes = {4: 1, 5: 2}
        out = (out_shape, BF16, axes[len(out_shape)])
        return run_rows(
            kernel, name, part // channel_block,
            [(Both(pieces), axes[pieces[0].ndim]) for pieces in arrays],
            [out] * (rows // out_shape[-2]), [], 7,
        )

    def swap_all(pieces):
        return [send(values, group) for values in pieces]

    def by_hidden(pieces):
        return [values.reshape((hidden,) + values.shape[2:]) for values in pieces]

    def by_device(pieces):
        return [values.reshape((devices, part) + values.shape[1:]) for values in pieces]

    def cols(prefix):
        return weights[(prefix, COLS)]

    tri_cols = cols

    def turned(name):
        return weights[(name, T)]

    tri_scratch = ((hidden, block, length), F32)
    product_scratch = ((2 * hidden, block, length), F32)
    head_scratch = ((8, block, length), F32)
    wide = ((width, length), F32)
    flip_scratch = ((length, block, width), F32)
    table = ((TA_HEADS, length, length), F32)
    attend_saves = [((rows, TA_HEADS, length), F32, 0), (state_shape, BF16, 0)]

    product = run_rows(
        functools.partial(tri_pre_first_kernel, devices, read_first), "outgoing_in", steps,
        [
            (info, "smem"), (alive, None), (pair, 0), (tri_cols(OUTGOING), None),
            (turned((OUTGOING, PROJ_GATE)), None),
        ],
        [(product_shape, BF16, 3)], [product_scratch], 13,
    )
    between(0, product[0])
    product_one = swap_all(product)
    between(9, None)
    tri_one = products(
        "outgoing_product", functools.partial(tri_product_kernel, False), [product_one], tri_half
    )
    tri_one = by_hidden(swap_all(tri_one))
    tri_one = [tri_one[0], *meet(0, tri_one[1])]
    state_one, product = run_halves(
        functools.partial(tri_join_kernel, devices, read_first), "outgoing_out_incoming_in", steps,
        [
            ([info[:half], info[half:]], "smem"), (alive, None), (pair, 0), (tri_one, 1), (tri_cols(OUTGOING), None),
            (turned((OUTGOING, PROJ_OUT)), None), (turned((OUTGOING, GATE_OUT)), None),
            (tri_cols(INCOMING), None), (turned((INCOMING, PROJ_GATE)), None),
        ],
        [(state_shape, F32, 0), (product_half, BF16, 3)], [tri_scratch, product_scratch], 22,
    )
    product_two = list(meet(1, *swap_all(product)))
    tri_two = products(
        "incoming_product", functools.partial(tri_product_kernel, True), [product_two], tri_shape
    )
    tri_two = by_hidden(swap_all(tri_two))
    between(1, None)
    (tri_two,) = meet(2, *tri_two)
    cotangent = cotangent.reshape(rows, parts, cores, parts, -1, width).transpose(3, 2, 1, 4, 0, 5)
    cotangent = send(cotangent.reshape(flip_shape), group)
    state_two, bias = run_rows(
        tri_last_kernel, "incoming_out_starting_bias", steps,
        [
            (state_one, 0), (tri_two, 1), (tri_cols(INCOMING), None),
            (turned((INCOMING, PROJ_OUT)), None), (turned((INCOMING, GATE_OUT)), None),
            (cols(STARTING), None), (weights[(STARTING, BIAS_T)], None),
        ],
        [(state_shape, F32, 0), ((TA_HEADS, rows, length), BF16, 1)], [tri_scratch, head_scratch],
    )
    bias_one = lax.all_gather(bias, group, axis=0, tiled=False)
    flipped, totals_one, mixed_one = run_rows(
        starting_kernel, "starting_attention", steps,
        [
            (alive, None), (state_two, 0), (bias_one, None), (cols(STARTING), None),
            (turned((STARTING, QKVG)), None), (turned((STARTING, OUTPUT)), None),
        ],
        [(flip_shape, BF16, 2)] + attend_saves, [table, flip_scratch], 21,
    )
    state_three = Both([send(flipped, group)])
    cotangent = send(cotangent.reshape((parts, cores) + flip_shape[1:]), "z").reshape(flip_shape)
    (bias,) = run_rows(
        flipped_bias_kernel, "ending_bias", steps,
        [(state_three, 1), (cols(ENDING), None), (weights[(ENDING, BIAS_T)], None)],
        [((TA_HEADS, rows, length), BF16, 1)], [head_scratch],
    )
    bias_two = lax.all_gather(bias, group, axis=0, tiled=False)
    state_four, totals_two, mixed_two = run_rows(
        ending_kernel, "ending_attention", steps,
        [
            (alive, None), (state_three, 1), (bias_two, None), (cols(ENDING), None),
            (turned((ENDING, QKVG)), None), (turned((ENDING, OUTPUT)), None),
        ],
        [(state_shape, F32, 0)] + attend_saves, [table],
    )
    pair_cols, attend_cols = cols(PAIR), cols(ATTEND)
    state_four, cotangent = after(state_four, cotangent)
    state_five, pair_out, single_bias = run_rows(
        functools.partial(transition_kernel, order_back), "pair_transition", steps,
        [
            (state_four, 0), (pair_cols, None), (turned((PAIR, UP)), None), (turned((PAIR, DOWN)), None),
            (attend_cols, None), (turned((ATTEND, PAIR_PROJ)), None),
        ],
        [(state_shape, F32, 0), ((length, rows, width), BF16, 1), ((devices, rows, SA_HEADS * rows), BF16, 1)],
        [flip_scratch, ((SA_HEADS, block, length), F32)],
    )
    single_grad_scores = send(middle(send(single_bias, group)), group)
    pair_out = send(pair_out.reshape((parts, -1) + pair_out.shape[1:]), "z")
    between(2, None)
    grads = {}
    grad_four, grads[(PAIR, UP)], grads[(PAIR, DOWN)], grads[(ATTEND, PAIR_PROJ)], vecs = run_rows(
        functools.partial(transition_back_kernel, read_last), "pair_transition_back", steps,
        [
            (state_four, 0), (state_five, 0), (cotangent, 1), (single_grad_scores, 1),
            (pair_cols, None), (turned((PAIR, UP)), None), (weights[(PAIR, UP)], None),
            (weights[(PAIR, DOWN)], None), (attend_cols, None), (weights[(ATTEND, PAIR_PROJ)], None),
        ],
        [
            (state_shape, F32, 0), (weights[(PAIR, UP)].shape, F32, None),
            (weights[(PAIR, DOWN)].shape, F32, None), (weights[(ATTEND, PAIR_PROJ)].shape, F32, None),
            ((8, width), F32, None),
        ],
        [wide, wide, wide, wide, ((SA_HEADS, block, length), F32)], 30,
    )
    grads[(PAIR, VECTORS)] = vecs

    def attention_back(prefix, read, read_grad, source, source_axis, grad, grad_axis, bias, totals, mixed):
        lowered_grad, bias_grad, grads[(prefix, QKVG)], grads[(prefix, OUTPUT)] = run_rows(
            functools.partial(attention_back_kernel, read, read_grad),
            "attention_back", steps,
            [
                (alive, None), (source, source_axis), (grad, grad_axis), (bias, None), (totals, 0),
                (mixed, 0), (cols(prefix), None), (turned((prefix, QKVG)), None),
                (weights[(prefix, QKVG)], None), (weights[(prefix, OUTPUT)], None),
            ],
            [
                (state_shape, BF16, 0), ((devices, TA_HEADS, rows, length), BF16, None),
                (weights[(prefix, QKVG)].shape, F32, None), (weights[(prefix, OUTPUT)].shape, F32, None),
            ],
            [table, table], 34,
        )
        return lowered_grad, send(bias_grad, group)

    lowered_grad, bias_grad = attention_back(
        ENDING, read_flipped, read_plain, state_three, 1, grad_four, 0, bias_two, totals_two, mixed_two
    )
    between(3, grads)
    flipped, bias_w_grad, vecs = run_rows(
        ending_end_kernel, "ending_attention_end", steps,
        [
            (state_three, 1), (grad_four, 0), (lowered_grad, 0), (bias_grad, 2), (cols(ENDING), None),
            (weights[(ENDING, BIAS_W)], None),
        ],
        [(flip_shape, BF16, 2), ((width, 8), F32, None), ((8, width), F32, None)],
        [wide, wide, head_scratch, flip_scratch],
    )
    grads[(ENDING, BIAS_PROJ)], grads[(ENDING, VECTORS)] = bias_w_grad, vecs
    flipped, held = after(flipped, grads[(ATTEND, PAIR_PROJ)])
    grads[(ATTEND, PAIR_PROJ)] = held
    grad_three = send(flipped, group)
    between(4, grads)
    grad_three = Both(meet(3, grad_three))
    pair_out = send(pair_out.reshape(flip_shape), group)
    pair_out = pair_out.reshape(parts, cores, rows, parts, -1, width).transpose(2, 3, 1, 0, 4, 5)
    pair_out = pair_out.reshape(rows, length, width)
    lowered_grad, bias_grad = attention_back(
        STARTING, read_plain, read_flipped, state_two, 0, grad_three, 1, bias_one, totals_one, mixed_one
    )
    between(7, grads)
    square = weights[(INCOMING, GATE_OUT)].shape
    (
        grad_two, grad_tri, gate_back, bias_w_grad, grads[(INCOMING, PROJ_OUT)], grads[(INCOMING, GATE_OUT)], vecs,
    ) = run_halves(
        starting_end_kernel, "starting_end_incoming_out_back", steps,
        [
            (state_two, 0), (grad_three, 1), (lowered_grad, 0), (bias_grad, 2), (cols(STARTING), None),
            (weights[(STARTING, BIAS_W)], None), (state_one, 0), (tri_two, 1), (tri_cols(INCOMING), None),
            (turned((INCOMING, PROJ_OUT)), None), (turned((INCOMING, GATE_OUT)), None),
            (weights[(INCOMING, PROJ_OUT)], None), (weights[(INCOMING, GATE_OUT)], None),
        ],
        [
            (state_shape, F32, 0), ((hidden, half, length), BF16, 1), (state_shape, BF16, 0),
            ((width, 8), F32, None), (square, F32, None), (square, F32, None), ((8, width), F32, None),
        ],
        [wide, wide, wide, wide, head_scratch, tri_scratch], 26,
    )
    grads[(STARTING, BIAS_PROJ)], grads[(STARTING, VECTORS)] = bias_w_grad, vecs
    grad_tri = swap_all(by_device(grad_tri))
    product_grad = products(
        "incoming_product_back", functools.partial(tri_product_back_kernel, True),
        [grad_tri, product_two], product_half,
    )
    product_grad = swap_all(product_grad)
    product_grad = [*meet(4, product_grad[0]), product_grad[1]]
    (
        grad_one, grad_tri, gate_back, grads[(INCOMING, PROJ_GATE)], grads[(OUTGOING, PROJ_OUT)],
        grads[(OUTGOING, GATE_OUT)], vecs,
    ) = run_halves(
        functools.partial(tri_join_back_kernel, read_first), "incoming_in_outgoing_out_back", steps,
        [
            ([info[:half], info[half:]], "smem"), (alive, None), (state_one, 0), (product_grad, 3), (gate_back, 0), (grad_two, 0),
            (tri_cols(INCOMING), None), (turned((INCOMING, PROJ_GATE)), None),
            (weights[(INCOMING, PROJ_GATE)], None), (pair, 0), (tri_one, 1), (tri_cols(OUTGOING), None),
            (turned((OUTGOING, PROJ_OUT)), None), (turned((OUTGOING, GATE_OUT)), None),
            (weights[(OUTGOING, PROJ_OUT)], None), (weights[(OUTGOING, GATE_OUT)], None),
        ],
        [
            (state_shape, F32, 0), ((hidden, half, length), BF16, 1), (state_shape, BF16, 0),
            (weights[(INCOMING, PROJ_GATE)].shape, F32, None), (square, F32, None), (square, F32, None),
            ((8, width), F32, None),
        ],
        [wide, wide, wide, wide, product_scratch, tri_scratch], 37,
    )
    grads[(INCOMING, VECTORS)] = vecs
    between(5, grads)
    grad_tri = swap_all(by_device(grad_tri))
    grad_tri = [grad_tri[0], *meet(5, grad_tri[1])]
    product_grad = products(
        "outgoing_product_back", functools.partial(tri_product_back_kernel, False),
        [grad_tri, product_one], product_shape,
    )
    (product_grad,) = swap_all(product_grad)
    between(6, grads)
    pair_grad, grads[(OUTGOING, PROJ_GATE)], vecs = run_rows(
        functools.partial(tri_first_back_kernel, read_first, order_back), "outgoing_in_back", steps,
        [
            (info, "smem"), (alive, None), (pair, 0), (product_grad, 3), (gate_back, 0), (grad_one, 0),
            (tri_cols(OUTGOING), None), (turned((OUTGOING, PROJ_GATE)), None),
            (weights[(OUTGOING, PROJ_GATE)], None),
        ],
        [
            ((rows, length, width), BF16, 0), (weights[(OUTGOING, PROJ_GATE)].shape, F32, None),
            ((8, width), F32, None),
        ],
        [wide, wide, product_scratch], 20,
    )
    grads[(OUTGOING, VECTORS)] = vecs
    return pair_out, pair_grad, grads


HELD = {
    (PAIR, VECTORS): ((PAIR, NORM_GAIN), (PAIR, NORM_BIAS), (ATTEND, PAIR_GAIN), (ATTEND, PAIR_BIAS)),
    (ENDING, VECTORS): ((ENDING, NORM_GAIN), (ENDING, NORM_BIAS)),
    (STARTING, VECTORS): (
        (STARTING, NORM_GAIN), (STARTING, NORM_BIAS), (INCOMING, OUT_GAIN), (INCOMING, OUT_BIAS)
    ),
    (INCOMING, VECTORS): (
        (INCOMING, NORM_GAIN), (INCOMING, NORM_BIAS), (OUTGOING, OUT_GAIN), (OUTGOING, OUT_BIAS)
    ),
    (OUTGOING, VECTORS): ((OUTGOING, NORM_GAIN), (OUTGOING, NORM_BIAS)),
}


def vector_part(grads, table, name, first, last):
    pairs = [
        (row, held) for row, held in enumerate(HELD[name]) if first <= table[held][0] < last
    ]
    return (pairs, grads[name])


def fast_shards(parts, cores, pair, single, lengths, params, moment_one, moment_two, pair_cotangent, single_cotangent):
    entries = layout(C, H, S, TA_HEADS, SA_HEADS)
    table, total = table_of(entries)
    count = total // STRIDE
    shard_size = params.shape[0]
    attend = table[(ATTEND, NORM_GAIN)][0]
    pair_lanes = -(-attend * STRIDE // count)
    single_lane = attend * STRIDE // count
    devices = parts * cores
    line, group = ("z", "core"), ("crop", "core")
    row_index = lax.axis_index(line)
    odd = ((row_index * shard_size) % STRIDE) // (STRIDE // 2)
    place = jnp.stack([odd, odd]).astype(jnp.int32)
    shard_rows = jnp.pad(params, (0, RUN * STRIDE * STRIDE - shard_size)).reshape(-1, STRIDE)
    (runs,) = whole_call(
        runs_kernel, "parameter_runs", [(place, "smem"), (shard_rows, None)],
        [((STRIDE, RUN, STRIDE), BF16)], [((STRIDE, RUN, STRIDE), F32)],
    )
    rows, length, width = pair.shape[1:]
    send = in_turn()
    pair_in = send(pair[0].reshape(parts, -1, length, width), "crop")
    first_runs = lax.all_gather(runs[:pair_lanes], line)
    pair_in, _, lengths = after(pair_in, runs, lengths)
    live = lax.all_gather(jnp.broadcast_to(lengths.astype(F32), (8, STRIDE)), "crop")
    pair_in = send(pair_in, "z").reshape(rows, length, width)
    weights = unpack_pair(table, total, first_runs)
    size = rows // parts
    blocks = np.arange(length // size).reshape(parts, cores, parts)
    order = blocks.transpose(2, 1, 0).reshape(-1)
    orders = (order.tolist(), np.argsort(order).tolist())
    tokens = (order[:, None] * size + np.arange(size)).reshape(-1)
    live = live[lax.axis_index("z"), 0, 0]
    width = single.shape[2]
    mask = (tokens.astype(np.float32) < live).astype(F32)
    info = lax.dynamic_slice_in_dim(mask, lax.axis_index(group) * rows, rows).astype(jnp.int32)
    alive = jnp.broadcast_to(mask, (8, length))
    held = {}
    single_grads = {}

    def middle(bias):
        found = single_middle(held["state"], held["back"], held["projected"], bias, alive, weights)
        held["out"], held["grad"], grad_scores, grads, held["pending"] = found
        single_grads.update(grads)
        return grad_scores

    def meet(number, *values):
        if number == 0:
            others = [held["runs"]]
        elif number == 1:
            others = [weights[(SINGLE, UP)]]
        elif number == 2:
            others = [held["projected"][1]]
        elif number == 3:
            others = [reduced[3]]
        elif number == 4:
            values, reduced[2] = after(*values, reduced[2])
            return [values]
        else:
            others = [reduced[1]]
        return after(*values, *others)[: len(values)]

    def reduce_runs(sent):
        return jnp.sum(send(sent, line).astype(F32), axis=0).astype(BF16)

    reduced = {}
    lines_held = list(enumerate(SINGLE_VECTORS))
    late_lanes = -(-table[(OUTGOING, OUT_GAIN)][0] * STRIDE // count)
    late_end = table[(OUTGOING, GATE_OUT)][0]
    early = table[(OUTGOING, PROJ_OUT)][0]

    def lines():
        values = jnp.concatenate([single_grads[name].reshape(1, S) for name in SINGLE_VECTORS], axis=0)
        return jnp.pad(values, ((0, 8 - len(SINGLE_VECTORS)), (0, 0)))

    def between(number, grads):
        if number == 0:
            last_runs = after(runs[single_lane:], pair_in, weights[(OUTGOING, COLS)], live)[0]
            held["runs"] = lax.all_gather(last_runs, line)
            weights.update(unpack_single(table, total, single_lane, held["runs"]))
            for index, name in enumerate(SINGLE_VECTORS):
                weights[name] = weights[(SINGLE, VECTORS)][index]
            both = jnp.concatenate([single[0], single_cotangent[0]], axis=1)
            held["both"] = send(both.reshape(parts, -1, 2 * width), "crop")
            return
        if number == 9:
            both = send(held["both"], "z").reshape(rows, 2 * width).astype(F32)
            held["state"], held["back"] = both[:, :width], both[:, width:]
            return
        if number == 1:
            lowered, qkvg, both = single_project(held["state"], weights, devices)
            held["projected"] = lowered, qkvg, send(both, group)
            return
        if number == 2:
            pending = held["pending"]
            moved = send(pending[0], group)
            grad = held["grad"] + single_attend_end(pending, moved, weights, single_grads)
            held["both"] = jnp.concatenate([held["out"], grad], axis=1).reshape(parts, -1, 2 * width)
            return
        if number == 3:
            held["both"] = send(held["both"], "z")
            return
        if number == 7:
            both = send(held["both"], "crop").reshape(rows, 2 * width)
            held[SINGLE] = both[:, :width].astype(BF16), both[:, width:]
            return
        if number == 6:
            reduced[1] = reduce_runs(reduced[1])
            return
        if number == 4:
            sent = pack(
                "single_gradient", table, total, devices, (pair_lanes, STRIDE), attend,
                [(name, single_grads[name]) for name in SINGLE_MATRICES]
                + [((ATTEND, PAIR_PROJ), grads[(ATTEND, PAIR_PROJ)])]
                + [vector_part(grads, table, (PAIR, VECTORS), attend, total), (lines_held, lines())],
            )
            reduced[3] = sent
            sent = sent.reshape((devices * parts, -1) + sent.shape[2:])
            reduced[2] = lax.psum_scatter(sent, line + ("crop",), scatter_dimension=0, tiled=False)
            return
        taken = -(-(pair_lanes * count - (attend + 2 * S // STRIDE) * STRIDE) // (4 * S))
        sent = pack(
            "pair_gradient", table, total, devices, (late_lanes, pair_lanes), early,
            [(name, grads[name]) for name in PAIR_MATRICES if table[name][0] >= early]
            + [(name, grads[name]) for name in ((STARTING, BIAS_PROJ), (ENDING, BIAS_PROJ))]
            + [vector_part(grads, table, name, early, attend) for name in HELD if name in grads]
            + [(lines_held[:2], lines()), ((ATTEND, QKVG), single_grads[(ATTEND, QKVG)][: -(-taken // 8) * 8])],
        )
        reduced[1] = sent

    pair_out, pair_grad, grads = pair_path(
        pair_in, info, alive, orders, weights, pair_cotangent[0], middle, between, meet, send, group, parts
    )
    sent = pack(
        "outgoing_gradient", table, total, devices, (0, late_lanes), 0,
        [(name, grads[name]) for name in PAIR_MATRICES if table[name][0] < late_end]
        + [vector_part(grads, table, name, 0, late_end) for name in ((OUTGOING, VECTORS), (INCOMING, VECTORS))],
    )
    reduced[0] = reduce_runs(sent)
    pair_grad = send(pair_grad.reshape(parts, -1, length, pair_grad.shape[2]), "z")
    pair_grad = send(pair_grad, "crop").reshape(rows, length, -1).astype(F32)
    single_out, single_grad = held[SINGLE]
    summed = lax.all_gather(jnp.concatenate([reduced[0], reduced[1]], axis=0), "crop")
    others = lax.all_gather(reduced[2], "crop")
    shard, squares = whole_call(
        functools.partial(shard_kernel, shard_size), "gradient_share",
        [(place, "smem"), (summed, None), (others, None)],
        [((RUN * STRIDE, STRIDE), F32), ((8, STRIDE), F32)], [((STRIDE, RUN, STRIDE), F32)],
    )
    shard = shard.reshape(-1)[:shard_size]
    clip_norm = jnp.sqrt(jnp.sum(lax.all_gather(squares, line)))
    clipped = shard * (CLIP / jnp.maximum(clip_norm, CLIP))
    new_first = BETA_ONE * moment_one + (1.0 - BETA_ONE) * clipped
    new_second = BETA_TWO * moment_two + (1.0 - BETA_TWO) * clipped * clipped
    rates, decays = rate_tables(entries)
    rate_shard = lax.dynamic_slice_in_dim(jnp.asarray(rates), row_index * shard_size, shard_size)
    decay_shard = lax.dynamic_slice_in_dim(jnp.asarray(decays), row_index * shard_size, shard_size)
    first_hat = new_first / (1.0 - BETA_ONE**STEP)
    second_hat = new_second / (1.0 - BETA_TWO**STEP)
    new_params = params - rate_shard * (
        first_hat / (jnp.sqrt(second_hat) + ADAM_EPS) + decay_shard * params
    )
    return (
        pair_out[None],
        single_out[None],
        pair_grad[None],
        single_grad[None],
        new_params,
        new_first,
        new_second,
        clip_norm,
    )


def solution(mesh):
    crops, devices = mesh.devices.shape
    table, total = table_of(layout(C, H, S, TA_HEADS, SA_HEADS))
    count = total // STRIDE
    lanes = STRIDE + -table[(ATTEND, NORM_GAIN)][0] * STRIDE // count
    fast = devices == 2 * crops and LENGTH % (devices * 16) == 0 and count // devices + 2 <= RUN * STRIDE and lanes % crops == 0
    row = "row"
    if fast:
        mesh = jax.sharding.Mesh(mesh.devices.reshape(crops, crops, 2), ("crop", "z", "core"))
        row = ("z", "core")
    split = [P("crop", row, None, None), P("crop", row, None), P("crop"), P(row)]
    pair, single, lengths, share = split
    return jax.shard_map(
        functools.partial(fast_shards, crops, 2) if fast else shards,
        mesh=mesh,
        in_specs=(pair, single, lengths, share, share, share, pair, single),
        out_specs=(pair, single, pair, single, share, share, share, P()),
        check_vma=False,
    )
```

```python
import functools
import math

import jax
import jax.numpy as jnp
import numpy as np
from jax import lax
from jax.experimental import pallas as pl
from jax.experimental.pallas import tpu as pltpu
from jax.sharding import PartitionSpec as P

C = 128
H = 128
S = 384
TA_HEADS = 4
SA_HEADS = 16
STEP = 10
STRIDE = 128
LENGTH = 256

OUTGOING, INCOMING, STARTING, ENDING, PAIR, ATTEND, SINGLE = range(7)
(
    NORM_GAIN,
    NORM_BIAS,
    PROJ_GATE,
    OUT_GAIN,
    OUT_BIAS,
    PROJ_OUT,
    GATE_OUT,
    QKVG,
    BIAS_PROJ,
    OUTPUT,
    UP,
    DOWN,
    PAIR_GAIN,
    PAIR_BIAS,
    PAIR_PROJ,
    COLS,
    BIAS_W,
    BIAS_T,
    VECTORS,
    T,
) = range(7, 27)


EPSILON = 1e-05
MASKED = 1000000000.0
BETA_ONE = 0.9
BETA_TWO = 0.95
ADAM_EPS = 1e-08
CLIP = 1.0


def layout(pair_width, hidden_width, single_width, tri_heads, att_heads):
    entries = []
    for prefix in (OUTGOING, INCOMING):
        entries += [
            ((prefix, NORM_GAIN), (pair_width,)),
            ((prefix, NORM_BIAS), (pair_width,)),
            ((prefix, PROJ_GATE), (pair_width, 4 * hidden_width)),
            ((prefix, OUT_GAIN), (hidden_width,)),
            ((prefix, OUT_BIAS), (hidden_width,)),
            ((prefix, PROJ_OUT), (hidden_width, pair_width)),
            ((prefix, GATE_OUT), (pair_width, pair_width)),
        ]
    for prefix in (STARTING, ENDING):
        entries += [
            ((prefix, NORM_GAIN), (pair_width,)),
            ((prefix, NORM_BIAS), (pair_width,)),
            ((prefix, QKVG), (pair_width, 4 * pair_width)),
            ((prefix, BIAS_PROJ), (pair_width, tri_heads)),
            ((prefix, OUTPUT), (pair_width, pair_width)),
        ]
    entries += [
        ((PAIR, NORM_GAIN), (pair_width,)),
        ((PAIR, NORM_BIAS), (pair_width,)),
        ((PAIR, UP), (pair_width, 8 * pair_width)),
        ((PAIR, DOWN), (4 * pair_width, pair_width)),
        ((ATTEND, NORM_GAIN), (single_width,)),
        ((ATTEND, NORM_BIAS), (single_width,)),
        ((ATTEND, QKVG), (single_width, 4 * single_width)),
        ((ATTEND, PAIR_GAIN), (pair_width,)),
        ((ATTEND, PAIR_BIAS), (pair_width,)),
        ((ATTEND, PAIR_PROJ), (pair_width, att_heads)),
        ((ATTEND, OUTPUT), (single_width, single_width)),
        ((SINGLE, NORM_GAIN), (single_width,)),
        ((SINGLE, NORM_BIAS), (single_width,)),
        ((SINGLE, UP), (single_width, 8 * single_width)),
        ((SINGLE, DOWN), (4 * single_width, single_width)),
    ]
    return entries


def logical_order(flat):
    return flat.reshape(-1, STRIDE).T.reshape(-1)


def stored_order(vector):
    return vector.reshape(STRIDE, -1).T.reshape(-1)


def rate_tables(entries):
    rates = []
    decays = []
    for name, shape in entries:
        count = math.prod(shape)
        if len(shape) == 1:
            rates.append(np.full(count, 0.5, np.float32))
            decays.append(np.zeros(count, np.float32))
        else:
            rates.append(np.full(count, 2.0 / math.sqrt(shape[0]), np.float32))
            decays.append(np.full(count, 0.01, np.float32))
    rates = np.concatenate(rates)
    decays = np.concatenate(decays)
    return (rates.reshape(STRIDE, -1).T.reshape(-1), decays.reshape(STRIDE, -1).T.reshape(-1))


def unpack(flat, entries):
    pieces = {}
    offset = 0
    for name, shape in entries:
        count = math.prod(shape)
        pieces[name] = flat[offset : offset + count].reshape(shape)
        offset += count
    return pieces


def layer_norm(values, gain, shift):
    centred = values - jnp.mean(values, axis=-1, keepdims=True)
    spread = jnp.mean(centred * centred, axis=-1, keepdims=True)
    return centred * lax.rsqrt(spread + EPSILON) * gain + shift


def norm_backward(values, gain, shift, grad):
    _, pullback = jax.vjp(layer_norm, values, gain, shift)
    return pullback(grad)


def norm_pair(weights, prefix):
    return (
        weights[(prefix, NORM_GAIN)].astype(jnp.float32),
        weights[(prefix, NORM_BIAS)].astype(jnp.float32),
    )


def gated_pair(project, pair_mask):
    half = project.shape[-1] // 2
    return project[..., :half] * jax.nn.sigmoid(project[..., half:]) * pair_mask[..., None]


def gated_output(values, gate):
    return values * jax.nn.sigmoid(gate)


def swiglu(hidden):
    half = hidden.shape[-1] // 2
    return jax.nn.silu(hidden[..., :half]) * hidden[..., half:]


def matmul(left, right):
    return jnp.dot(left, right, preferred_element_type=jnp.float32)


def outer_sum(left, right):
    return jnp.einsum(
        "nc,nd->cd",
        left.reshape(-1, left.shape[-1]),
        right.reshape(-1, right.shape[-1]),
        preferred_element_type=jnp.float32,
    )


def flip(values):
    moved = lax.all_to_all(values, "row", split_axis=1, concat_axis=0, tiled=True)
    return jnp.swapaxes(moved, 0, 1)


def channel_forward(first, second, incoming):
    whole_first, whole_second = (
        lax.all_to_all(first, "row", split_axis=2, concat_axis=0, tiled=True),
        lax.all_to_all(second, "row", split_axis=2, concat_axis=0, tiled=True),
    )
    if incoming:
        local_tri = jnp.einsum(
            "kih,kjh->ijh", whole_first, whole_second, preferred_element_type=jnp.float32
        )
        local_tri = local_tri.astype(jnp.bfloat16).astype(jnp.float32)
    else:
        local_tri = jnp.einsum(
            "ikh,jkh->ijh", whole_first, whole_second, preferred_element_type=jnp.float32
        )
    tri = lax.all_to_all(
        local_tri.astype(jnp.bfloat16), "row", split_axis=0, concat_axis=2, tiled=True
    ).astype(local_tri.dtype)
    return (tri, whole_first, whole_second)


def channel_backward(grad_tri, whole_first, whole_second, incoming):
    whole_grad = lax.all_to_all(grad_tri, "row", split_axis=2, concat_axis=0, tiled=True)
    if incoming:
        grad_a = jnp.einsum(
            "ijh,kjh->kih", whole_grad, whole_second, preferred_element_type=jnp.float32
        )
        grad_b = jnp.einsum(
            "ijh,kih->kjh", whole_grad, whole_first, preferred_element_type=jnp.float32
        )
    else:
        grad_a = jnp.einsum(
            "ijh,jkh->ikh", whole_grad, whole_second, preferred_element_type=jnp.float32
        )
        grad_b = jnp.einsum(
            "ijh,ikh->jkh", whole_grad, whole_first, preferred_element_type=jnp.float32
        )
    return (
        lax.all_to_all(
            grad_a.astype(jnp.bfloat16), "row", split_axis=0, concat_axis=2, tiled=True
        ).astype(grad_a.dtype),
        lax.all_to_all(
            grad_b.astype(jnp.bfloat16), "row", split_axis=0, concat_axis=2, tiled=True
        ).astype(grad_b.dtype),
    )


def triangle_forward(state, pair_mask, weights, prefix, incoming):
    gain, shift = norm_pair(weights, prefix)
    lowered = layer_norm(state, gain, shift).astype(jnp.bfloat16)
    project = matmul(lowered, weights[(prefix, PROJ_GATE)])
    product = gated_pair(project, pair_mask).astype(jnp.bfloat16)
    half = product.shape[-1] // 2
    tri, own, other = channel_forward(product[..., :half], product[..., half:], incoming)
    out_gain = weights[(prefix, OUT_GAIN)].astype(jnp.float32)
    out_shift = weights[(prefix, OUT_BIAS)].astype(jnp.float32)
    out_low = layer_norm(tri, out_gain, out_shift).astype(jnp.bfloat16)
    output = matmul(out_low, weights[(prefix, PROJ_OUT)])
    gate_out = matmul(lowered, weights[(prefix, GATE_OUT)])
    update = gated_output(output, gate_out)
    return (update, (state, lowered, lowered, project, own, other, tri, out_low, output, gate_out))


def triangle_backward(saved, grad_update, pair_mask, weights, prefix, incoming, grads):
    state, lowered, framed, project, own, other, tri, out_low, output, gate_out = saved
    _, pullback = jax.vjp(gated_output, output, gate_out)
    grad_output, grad_gate = pullback(grad_update)
    grad_output = grad_output.astype(jnp.bfloat16)
    grad_gate = grad_gate.astype(jnp.bfloat16)
    grads[(prefix, PROJ_OUT)] = outer_sum(out_low, grad_output)
    grads[(prefix, GATE_OUT)] = outer_sum(lowered, grad_gate)
    grad_normed = matmul(grad_output, weights[(prefix, PROJ_OUT)].T)
    out_gain = weights[(prefix, OUT_GAIN)].astype(jnp.float32)
    out_shift = weights[(prefix, OUT_BIAS)].astype(jnp.float32)
    grad_tri, grads[(prefix, OUT_GAIN)], grads[(prefix, OUT_BIAS)] = norm_backward(
        tri, out_gain, out_shift, grad_normed
    )
    grad_tri = grad_tri.astype(jnp.bfloat16)
    grad_first, grad_second = channel_backward(grad_tri, own, other, incoming)
    _, pullback = jax.vjp(lambda values: gated_pair(values, pair_mask), project)
    (grad_project,) = pullback(jnp.concatenate([grad_first, grad_second], axis=-1))
    grad_project = grad_project.astype(jnp.bfloat16)
    grads[(prefix, PROJ_GATE)] = outer_sum(framed, grad_project)
    grad_framed = matmul(grad_project, weights[(prefix, PROJ_GATE)].T)
    if incoming:
        grad_framed = grad_framed.astype(jnp.bfloat16).astype(jnp.float32)
    grad_lowered = grad_framed + matmul(grad_gate, weights[(prefix, GATE_OUT)].T)
    gain, shift = norm_pair(weights, prefix)
    grad_state, grads[(prefix, NORM_GAIN)], grads[(prefix, NORM_BIAS)] = norm_backward(
        state, gain, shift, grad_lowered
    )
    return grad_state


def row_scores(query, key, bias, penalty, scale):
    scores = jnp.einsum("jhd,khd->hjk", query, key, preferred_element_type=jnp.float32) * scale
    return scores + bias.astype(jnp.float32) + penalty[None, None, :]


def attention_forward(state, penalty, weights, prefix, ending):
    gain, shift = norm_pair(weights, prefix)
    lowered = layer_norm(state, gain, shift).astype(jnp.bfloat16)
    framed = flip(lowered) if ending else lowered
    rows, length, width = framed.shape
    size = width // TA_HEADS
    scale = size ** (-0.5)
    qkvg = matmul(framed, weights[(prefix, QKVG)])
    queries = qkvg[..., :width].astype(jnp.bfloat16).reshape(rows, length, TA_HEADS, size)
    keys = qkvg[..., width : 2 * width].astype(jnp.bfloat16).reshape(rows, length, TA_HEADS, size)
    values = (
        qkvg[..., 2 * width : 3 * width].astype(jnp.bfloat16).reshape(rows, length, TA_HEADS, size)
    )
    gate = qkvg[..., 3 * width :]
    local_bias = (
        matmul(framed, weights[(prefix, BIAS_PROJ)]).astype(jnp.bfloat16).transpose(2, 0, 1)
    )
    bias = lax.all_gather(local_bias, "row", axis=1, tiled=True)

    def forward_row(items):
        query, key, value = items
        scores = row_scores(query, key, bias, penalty, scale)
        top = jnp.max(scores, axis=-1, keepdims=True)
        shifted = jnp.exp(scores - top)
        total = jnp.sum(shifted, axis=-1, keepdims=True)
        probs = (shifted / total).astype(jnp.bfloat16)
        mixed = jnp.einsum("hjk,khd->jhd", probs, value, preferred_element_type=jnp.float32)
        return (mixed, top[..., 0] + jnp.log(total[..., 0]))

    mixed, log_totals = lax.map(forward_row, (queries, keys, values))
    mixed = mixed.reshape(rows, length, width)
    gated_low = gated_output(mixed, gate).astype(jnp.bfloat16)
    returned = flip(gated_low) if ending else gated_low
    update = matmul(returned, weights[(prefix, OUTPUT)])
    return (update, (state, framed, queries, keys, values, gate, bias, mixed, log_totals, returned))


def attention_backward(saved, grad_update, penalty, weights, prefix, ending, grads):
    state, framed, queries, keys, values, gate, bias, mixed, log_totals, returned = saved
    rows, length, width = framed.shape
    size = width // TA_HEADS
    scale = size ** (-0.5)
    grad_low = grad_update.astype(jnp.bfloat16)
    grads[(prefix, OUTPUT)] = outer_sum(returned, grad_low)
    grad_gated = matmul(grad_low, weights[(prefix, OUTPUT)].T)
    if ending:
        grad_gated = flip(grad_gated.astype(jnp.bfloat16)).astype(jnp.float32)
    _, pullback = jax.vjp(gated_output, mixed, gate)
    grad_mixed, grad_gate = pullback(grad_gated)
    grad_mixed = grad_mixed.astype(jnp.bfloat16).reshape(rows, length, TA_HEADS, size)

    def back_row(carry, items):
        query, key, value, log_total, grad_row = items
        scores = row_scores(query, key, bias, penalty, scale)
        probs = jnp.exp(scores - log_total[..., None])
        grad_probs = jnp.einsum("jhd,khd->hjk", grad_row, value, preferred_element_type=jnp.float32)
        delta = jnp.sum(probs * grad_probs, axis=-1, keepdims=True)
        grad_scores = (probs * (grad_probs - delta)).astype(jnp.bfloat16)
        grad_query = (
            jnp.einsum("hjk,khd->jhd", grad_scores, key, preferred_element_type=jnp.float32) * scale
        )
        grad_key = (
            jnp.einsum("hjk,jhd->khd", grad_scores, query, preferred_element_type=jnp.float32)
            * scale
        )
        grad_value = jnp.einsum(
            "hjk,jhd->khd", probs.astype(jnp.bfloat16), grad_row, preferred_element_type=jnp.float32
        )
        return (carry + grad_scores.astype(jnp.float32), (grad_query, grad_key, grad_value))

    empty = jnp.zeros(bias.shape, jnp.float32)
    grad_bias, (grad_query, grad_key, grad_value) = lax.scan(
        back_row, empty, (queries, keys, values, log_totals, grad_mixed)
    )
    grad_bias = lax.psum_scatter(grad_bias, "row", scatter_dimension=1, tiled=True)
    grad_bias = grad_bias.transpose(1, 2, 0).astype(jnp.bfloat16)
    grad_qkvg = jnp.concatenate(
        [
            grad_query.reshape(rows, length, width),
            grad_key.reshape(rows, length, width),
            grad_value.reshape(rows, length, width),
            grad_gate,
        ],
        axis=-1,
    ).astype(jnp.bfloat16)
    grads[(prefix, QKVG)] = outer_sum(framed, grad_qkvg)
    grads[(prefix, BIAS_PROJ)] = outer_sum(framed, grad_bias)
    grad_framed = matmul(grad_qkvg, weights[(prefix, QKVG)].T) + matmul(
        grad_bias, weights[(prefix, BIAS_PROJ)].T
    )
    if ending:
        grad_framed = flip(grad_framed.astype(jnp.bfloat16)).astype(jnp.float32)
    gain, shift = norm_pair(weights, prefix)
    grad_state, grads[(prefix, NORM_GAIN)], grads[(prefix, NORM_BIAS)] = norm_backward(
        state, gain, shift, grad_framed
    )
    return grad_state


def transition_forward(state, weights, prefix):
    gain, shift = norm_pair(weights, prefix)
    lowered = layer_norm(state, gain, shift).astype(jnp.bfloat16)
    hidden = matmul(lowered, weights[(prefix, UP)])
    mixed_low = swiglu(hidden).astype(jnp.bfloat16)
    update = matmul(mixed_low, weights[(prefix, DOWN)])
    return (update, (state, lowered, hidden, mixed_low))


def transition_backward(saved, grad_update, weights, prefix, grads):
    state, lowered, hidden, mixed_low = saved
    grad_low = grad_update.astype(jnp.bfloat16)
    grads[(prefix, DOWN)] = outer_sum(mixed_low, grad_low)
    grad_mixed = matmul(grad_low, weights[(prefix, DOWN)].T)
    _, pullback = jax.vjp(swiglu, hidden)
    (grad_hidden,) = pullback(grad_mixed)
    grad_hidden = grad_hidden.astype(jnp.bfloat16)
    grads[(prefix, UP)] = outer_sum(lowered, grad_hidden)
    grad_lowered = matmul(grad_hidden, weights[(prefix, UP)].T)
    gain, shift = norm_pair(weights, prefix)
    grad_state, grads[(prefix, NORM_GAIN)], grads[(prefix, NORM_BIAS)] = norm_backward(
        state, gain, shift, grad_lowered
    )
    return grad_state


def single_forward(single_state, pair_state, penalty, weights):
    gain, shift = norm_pair(weights, ATTEND)
    lowered = layer_norm(single_state, gain, shift).astype(jnp.bfloat16)
    rows, width = lowered.shape
    size = width // SA_HEADS
    qkvg = matmul(lowered, weights[(ATTEND, QKVG)])
    query = qkvg[:, :width].astype(jnp.bfloat16).reshape(rows, SA_HEADS, size)
    key = qkvg[:, width : 2 * width].astype(jnp.bfloat16)
    value = qkvg[:, 2 * width : 3 * width].astype(jnp.bfloat16)
    gate = qkvg[:, 3 * width :]
    keys_all, values_all = (
        lax.all_gather(key, "row", axis=0, tiled=True),
        lax.all_gather(value, "row", axis=0, tiled=True),
    )
    keys_all = keys_all.reshape(-1, SA_HEADS, size)
    values_all = values_all.reshape(-1, SA_HEADS, size)
    pair_gain = weights[(ATTEND, PAIR_GAIN)].astype(jnp.float32)
    pair_shift = weights[(ATTEND, PAIR_BIAS)].astype(jnp.float32)
    pair_low = layer_norm(pair_state, pair_gain, pair_shift).astype(jnp.bfloat16)
    bias = matmul(pair_low, weights[(ATTEND, PAIR_PROJ)]).transpose(2, 0, 1)
    scores = jnp.einsum(
        "ihd,jhd->hij", query, keys_all, preferred_element_type=jnp.float32
    ) * size ** (-0.5)
    scores = scores + bias + penalty[None, None, :]
    probs = jax.nn.softmax(scores, axis=-1)
    probs_low = probs.astype(jnp.bfloat16)
    mixed = jnp.einsum(
        "hij,jhd->ihd", probs_low, values_all, preferred_element_type=jnp.float32
    ).reshape(rows, width)
    gated_low = gated_output(mixed, gate).astype(jnp.bfloat16)
    update = matmul(gated_low, weights[(ATTEND, OUTPUT)])
    return (
        update,
        (
            single_state,
            pair_state,
            lowered,
            query,
            keys_all,
            values_all,
            gate,
            pair_low,
            probs,
            probs_low,
            mixed,
            gated_low,
        ),
    )


def single_backward(saved, grad_update, weights, grads):
    (
        single_state,
        pair_state,
        lowered,
        query,
        keys_all,
        values_all,
        gate,
        pair_low,
        probs,
        probs_low,
        mixed,
        gated_low,
    ) = saved
    rows, width = lowered.shape
    size = width // SA_HEADS
    scale = size ** (-0.5)
    grad_low = grad_update.astype(jnp.bfloat16)
    grads[(ATTEND, OUTPUT)] = outer_sum(gated_low, grad_low)
    grad_gated = matmul(grad_low, weights[(ATTEND, OUTPUT)].T)
    _, pullback = jax.vjp(gated_output, mixed, gate)
    grad_mixed, grad_gate = pullback(grad_gated)
    grad_mixed = grad_mixed.astype(jnp.bfloat16).reshape(rows, SA_HEADS, size)
    grad_probs = jnp.einsum(
        "ihd,jhd->hij", grad_mixed, values_all, preferred_element_type=jnp.float32
    )
    delta = jnp.sum(probs * grad_probs, axis=-1, keepdims=True)
    grad_scores = (probs * (grad_probs - delta)).astype(jnp.bfloat16)
    grad_query = (
        jnp.einsum("hij,jhd->ihd", grad_scores, keys_all, preferred_element_type=jnp.float32)
        * scale
    )
    key_part = (
        jnp.einsum("hij,ihd->jhd", grad_scores, query, preferred_element_type=jnp.float32) * scale
    )
    value_part = jnp.einsum(
        "hij,ihd->jhd", probs_low, grad_mixed, preferred_element_type=jnp.float32
    )
    grad_key, grad_value = (
        lax.psum_scatter(key_part.reshape(-1, width), "row", scatter_dimension=0, tiled=True),
        lax.psum_scatter(value_part.reshape(-1, width), "row", scatter_dimension=0, tiled=True),
    )
    grad_qkvg = jnp.concatenate(
        [grad_query.reshape(rows, width), grad_key, grad_value, grad_gate], axis=-1
    ).astype(jnp.bfloat16)
    grads[(ATTEND, QKVG)] = outer_sum(lowered, grad_qkvg)
    grad_lowered = matmul(grad_qkvg, weights[(ATTEND, QKVG)].T)
    gain, shift = norm_pair(weights, ATTEND)
    grad_single, grads[(ATTEND, NORM_GAIN)], grads[(ATTEND, NORM_BIAS)] = norm_backward(
        single_state, gain, shift, grad_lowered
    )
    grad_bias = grad_scores.transpose(1, 2, 0)
    grads[(ATTEND, PAIR_PROJ)] = outer_sum(pair_low, grad_bias)
    grad_pair_low = matmul(grad_bias, weights[(ATTEND, PAIR_PROJ)].T)
    pair_gain = weights[(ATTEND, PAIR_GAIN)].astype(jnp.float32)
    pair_shift = weights[(ATTEND, PAIR_BIAS)].astype(jnp.float32)
    grad_pair, grads[(ATTEND, PAIR_GAIN)], grads[(ATTEND, PAIR_BIAS)] = norm_backward(
        pair_state, pair_gain, pair_shift, grad_pair_low
    )
    return (grad_single, grad_pair)


def shards(pair, single, lengths, params, moment_one, moment_two, pair_cotangent, single_cotangent):
    entries = layout(C, H, S, TA_HEADS, SA_HEADS)
    full = lax.all_gather(params.astype(jnp.bfloat16), "row", axis=0, tiled=True)
    weights = unpack(logical_order(full), entries)
    rows = pair.shape[1]
    length = pair.shape[2]
    first_row = lax.axis_index("row") * rows
    mask = (jnp.arange(length, dtype=jnp.int32) < lengths[0]).astype(jnp.float32)
    mask_rows = lax.dynamic_slice_in_dim(mask, first_row, rows)
    pair_mask = mask_rows[:, None] * mask[None, :]
    penalty = (mask - 1.0) * MASKED
    state = pair[0].astype(jnp.float32)
    saved = {}
    for prefix, incoming in ((OUTGOING, False), (INCOMING, True)):
        update, saved[prefix] = triangle_forward(state, pair_mask, weights, prefix, incoming)
        state = state + update
    for prefix, ending in ((STARTING, False), (ENDING, True)):
        update, saved[prefix] = attention_forward(state, penalty, weights, prefix, ending)
        state = state + update
    update, saved[PAIR] = transition_forward(state, weights, PAIR)
    pair_final = state + update
    single_state = single[0].astype(jnp.float32)
    update, saved[ATTEND] = single_forward(single_state, pair_final, penalty, weights)
    single_mid = single_state + update
    update, saved[SINGLE] = transition_forward(single_mid, weights, SINGLE)
    single_final = single_mid + update
    grads = {}
    grad_single = single_cotangent[0].astype(jnp.float32)
    grad_single = grad_single + transition_backward(
        saved[SINGLE], grad_single, weights, SINGLE, grads
    )
    from_single, from_pair = single_backward(saved[ATTEND], grad_single, weights, grads)
    grad_single = grad_single + from_single
    grad_pair = pair_cotangent[0].astype(jnp.float32) + from_pair
    grad_pair = grad_pair + transition_backward(saved[PAIR], grad_pair, weights, PAIR, grads)
    for prefix, ending in ((ENDING, True), (STARTING, False)):
        grad_pair = grad_pair + attention_backward(
            saved[prefix], grad_pair, penalty, weights, prefix, ending, grads
        )
    for prefix, incoming in ((INCOMING, True), (OUTGOING, False)):
        grad_pair = grad_pair + triangle_backward(
            saved[prefix], grad_pair, pair_mask, weights, prefix, incoming, grads
        )
    flat = stored_order(jnp.concatenate([grads[name].reshape(-1) for name, shape in entries]))
    shard_size = params.shape[0]
    row_index = lax.axis_index("row")
    total = lax.psum(flat, ("crop", "row"))
    shard = lax.dynamic_slice_in_dim(total, row_index * shard_size, shard_size)
    norm_squared = jnp.sum(total * total)
    clip_norm = jnp.sqrt(norm_squared)
    clipped = shard * (CLIP / jnp.maximum(clip_norm, CLIP))
    new_first = BETA_ONE * moment_one + (1.0 - BETA_ONE) * clipped
    new_second = BETA_TWO * moment_two + (1.0 - BETA_TWO) * clipped * clipped
    rates, decays = rate_tables(entries)
    rate_shard = lax.dynamic_slice_in_dim(jnp.asarray(rates), row_index * shard_size, shard_size)
    decay_shard = lax.dynamic_slice_in_dim(jnp.asarray(decays), row_index * shard_size, shard_size)
    first_hat = new_first / (1.0 - BETA_ONE**STEP)
    second_hat = new_second / (1.0 - BETA_TWO**STEP)
    new_params = params - rate_shard * (
        first_hat / (jnp.sqrt(second_hat) + ADAM_EPS) + decay_shard * params
    )
    return (
        pair_final.astype(jnp.bfloat16)[None],
        single_final.astype(jnp.bfloat16)[None],
        grad_pair[None],
        grad_single[None],
        new_params,
        new_first,
        new_second,
        clip_norm,
    )


F32 = jnp.float32
BF16 = jnp.bfloat16
LOG2E = 1.4426950408889634
VMEM_LIMIT = 56 * 1024 * 1024


def mm(left, right):
    return lax.dot_general(left, right, (((1,), (0,)), ((), ())), preferred_element_type=F32)


def mm_nt(left, right):
    return lax.dot_general(left, right, (((1,), (1,)), ((), ())), preferred_element_type=F32)


def mm_tn(left, right):
    return lax.dot_general(left, right, (((0,), (0,)), ((), ())), preferred_element_type=F32)


def standardize(values):
    centred = values - jnp.mean(values, axis=0, keepdims=True)
    spread = jnp.mean(centred * centred, axis=0, keepdims=True)
    inverse = lax.rsqrt(spread + EPSILON)
    return centred * inverse, inverse


def standardize_back(unit, inverse, grad_unit):
    first = jnp.mean(grad_unit, axis=0, keepdims=True)
    second = jnp.mean(grad_unit * unit, axis=0, keepdims=True)
    return inverse * (grad_unit - first - unit * second)


def sigmoid(values):
    return 0.5 * jnp.tanh(0.5 * values) + 0.5


def column(ref, index):
    return ref[:, index : index + 1]


def live_pair(info, alive, row):
    return jnp.concatenate(
        [jnp.where(info[row + place] > 0, alive[0:1], 0.0) for place in range(GROUP)], axis=1
    )


GROUP = 4
LAG = 4


def each_group(count, body):
    def step(index, carry):
        body(index * GROUP)
        return carry

    lax.fori_loop(0, count // GROUP, step, 0)


def each_channel(count, body):
    def step(index, carry):
        body(index)
        return carry

    lax.fori_loop(0, count, step, 0)


def join(read, ref, row):
    return jnp.concatenate([read(ref, row + place) for place in range(GROUP)], axis=1)


def pieces_of(values):
    length = values.shape[1] // GROUP
    return [values[:, place * length : (place + 1) * length] for place in range(GROUP)]


def put_rows(ref, row, values):
    for place, part in enumerate(pieces_of(values)):
        ref[row + place] = part.astype(ref.dtype)


def put_inner(scratch, row, values):
    for place, part in enumerate(pieces_of(values)):
        scratch[:, row + place, :] = part


def read_inner(scratch, row):
    return scratch[:, row, :]


def put_turned(scratch, row, values):
    for place, part in enumerate(pieces_of(values)):
        scratch[:, row + place, :] = part.T


def add_lanes(ref, values):
    ref[...] += sum(pieces_of(values))


def spec_full(shape):
    return pl.BlockSpec(shape, lambda step: (0,) * len(shape))


def cost(microseconds):
    return pl.CostEstimate(
        flops=int(microseconds * 1e9), bytes_accessed=int(microseconds * 3e6), transcendentals=0
    )


class Both(list):
    pass


def all_rows(ins, outs):
    extents = [shape[axis] for shape, dtype, axis in outs if axis is not None]
    for array, axis in ins:
        if isinstance(axis, int):
            extents += [member.shape[axis] for member in (array if isinstance(array, list) else [array])]
    return max(extents)


def run_rows(kernel, name, steps, ins, outs, scratch, time=15, half=None, before=None):
    grid = steps if half is None else steps // 2
    offset = grid * (half or 0)
    flat = []
    groups = []
    for array, axis in ins:
        members = array if isinstance(array, Both) else [array]
        flat += [(member, axis) for member in members]
        groups.append((len(members), isinstance(array, Both)))
    full = all_rows(flat, outs)

    def spec(shape, axis):
        if axis is None:
            return spec_full(shape)
        size = full // steps
        first = offset if shape[axis] == full else 0
        sizes = tuple(size if place == axis else extent for place, extent in enumerate(shape))
        return pl.BlockSpec(
            sizes,
            lambda step: tuple(step + first if place == axis else 0 for place in range(len(shape))),
        )

    in_specs = [
        pl.BlockSpec(memory_space=pltpu.SMEM) if axis == "smem" else spec(array.shape, axis)
        for array, axis in flat
    ]
    out_specs = [spec(shape, axis) for shape, dtype, axis in outs]
    arrays = [array for array, axis in flat]
    aliases = {}
    kept = []
    for place, (shape, dtype, axis) in enumerate(outs):
        if before is not None and (axis is None or shape[axis] == full):
            aliases[len(arrays)] = place
            kept.append(place)
            arrays.append(before[place])
            in_specs.append(spec_full(shape) if axis is None else pl.BlockSpec(memory_space=pl.ANY))

    def run(*refs):
        taken = iter(refs)
        given = []
        for number, together in groups:
            members = [next(taken) for _ in range(number)]
            given.append(members if together else members[0])
        held = {place: next(taken) for place in kept}
        results = [next(taken) for _ in outs]

        @pl.when(pl.program_id(0) == 0)
        def _():
            for place, (shape, dtype, axis) in enumerate(outs):
                if axis is None:
                    results[place][...] = (
                        held[place][...] if place in held else jnp.zeros(shape, dtype)
                    )

        kernel(*given, *results, *taken)

    return pl.pallas_call(
        run,
        grid=(grid,),
        in_specs=in_specs,
        out_specs=out_specs,
        out_shape=[jax.ShapeDtypeStruct(shape, dtype) for shape, dtype, axis in outs],
        scratch_shapes=[pltpu.VMEM(shape, dtype) for shape, dtype in scratch],
        input_output_aliases=aliases,
        compiler_params=pltpu.CompilerParams(vmem_limit_bytes=VMEM_LIMIT),
        cost_estimate=cost(time if half is None else time / 2),
        name=name,
    )(*arrays)


def run_halves(kernel, name, steps, ins, outs, scratch, time=15):
    results = []
    for half in range(2):
        chosen = [
            (array[half] if type(array) is list else array, axis) for array, axis in ins
        ]
        before = results[0] if half else None
        results.append(run_rows(kernel, name, steps, chosen, outs, scratch, time, half, before))
    full = all_rows(ins, outs)
    return [
        [results[0][place], results[1][place]]
        if axis is not None and shape[axis] != full
        else results[1][place]
        for place, (shape, dtype, axis) in enumerate(outs)
    ]


def zero_first(*refs):
    @pl.when(pl.program_id(0) == 0)
    def _():
        for ref in refs:
            ref[...] = jnp.zeros(ref.shape, ref.dtype)


def lane_sums(ref):
    return jnp.sum(ref[...].T, axis=0, keepdims=True)


def on_last(body):
    @pl.when(pl.program_id(0) == pl.num_programs(0) - 1)
    def _():
        body()


def read_plain(ref, row):
    return ref[row].astype(F32)


def reorder(values, order):
    size = values.shape[0] // len(order)
    return jnp.concatenate([values[place * size : (place + 1) * size] for place in order], axis=0)


def read_tokens(order, ref, row):
    return reorder(ref[row].astype(F32), order).T


def read_flipped(refs, row):
    parts = jnp.concatenate([ref[:, row] for ref in refs], axis=1)
    return parts.reshape(-1, parts.shape[-1]).astype(F32).T


def read_turned(order, ref, row):
    parts = ref[:, row]
    return reorder(parts.reshape(-1, parts.shape[-1]).astype(F32), order).T


def tri_pre_row(info, alive, row, state, cols, first, proj_t):
    unit, inverse = standardize(state)
    lowered = (unit * column(cols, first) + column(cols, first + 1)).astype(BF16)
    project = mm(proj_t[...], lowered)
    half = project.shape[0] // 2
    return project[:half] * sigmoid(project[half:]) * live_pair(info, alive, row)


def store_product(out, scratch, devices):
    hidden = scratch.shape[0] // 2
    part = hidden // devices

    def one(device, carry):
        out[device, 0] = scratch[pl.ds(device * part, part)].astype(BF16)
        out[device, 1] = scratch[pl.ds(hidden + device * part, part)].astype(BF16)
        return carry

    lax.fori_loop(0, devices, one, 0)


def copy_blocks(target, source, count):
    def one(index, carry):
        target[index] = source[index].astype(target.dtype)
        return carry

    lax.fori_loop(0, count, one, 0)


def store_flipped(out, scratch):
    devices, part = out.shape[0], out.shape[1]

    def one(device, carry):
        out[device] = scratch[pl.ds(device * part, part)].astype(out.dtype)
        return carry

    lax.fori_loop(0, devices, one, 0)


def tri_post_row(state, tri, cols, proj_t, gate_t):
    unit, inverse = standardize(state)
    lowered = (unit * column(cols, 0) + column(cols, 1)).astype(BF16)
    tri_unit, tri_inverse = standardize(tri)
    out_low = (tri_unit * column(cols, 2) + column(cols, 3)).astype(BF16)
    output = mm(proj_t[...], out_low)
    gate = sigmoid(mm(gate_t[...], lowered))
    return unit, inverse, lowered, tri_unit, tri_inverse, out_low, output, gate


def row_base(rows):
    return pl.program_id(0) * rows


def tri_pre_first_kernel(devices, read, info, alive, pair, cols, proj_t, out, scratch):
    rows = pair.shape[0]

    def body(row):
        product = tri_pre_row(
            info, alive, row_base(rows) + row, join(read, pair, row), cols, 0, proj_t
        )
        put_inner(scratch, row, product)

    each_group(rows, body)
    store_product(out, scratch, devices)


def whole_rows(refs, *place):
    parts = jnp.concatenate([ref[(slice(None),) + place] for ref in refs], axis=1)
    return parts.reshape(-1, parts.shape[-1])


def split_rows(values, outs, *place):
    part = outs[0].shape[-2]
    parts = values.astype(BF16).reshape(outs[0].shape[0], -1, values.shape[-1])
    for half, out in enumerate(outs):
        out[(slice(None),) + place] = parts[:, half * part : (half + 1) * part]


def tri_product_kernel(incoming, operands, *outs):
    def body(channel):
        first = whole_rows(operands, 0, channel)
        second = whole_rows(operands, 1, channel)
        tri = mm_tn(first, second) if incoming else mm_nt(first, second)
        split_rows(tri, outs, channel)

    each_channel(operands[0].shape[2], body)


def tri_join_kernel(
    devices, read, info, alive, source, tri_in, cols, proj_t, gate_t, next_cols, next_proj_t,
    state_out, out, tri_scratch, scratch,
):
    rows = state_out.shape[0]
    copy_blocks(tri_scratch, tri_in, tri_in.shape[0])

    def body(row):
        state = join(read, source, row)
        pieces = tri_post_row(state, join(read_inner, tri_scratch, row), cols, proj_t, gate_t)
        state = state + pieces[6] * pieces[7]
        put_rows(state_out, row, state)
        product = tri_pre_row(
            info, alive, row_base(rows) + row, state, next_cols, 0, next_proj_t
        )
        put_inner(scratch, row, product)

    each_group(rows, body)
    store_product(out, scratch, devices)


def tri_last_kernel(
    source, tri_in, cols, proj_t, gate_t, next_cols, bias_t, state_out, bias_out, tri_scratch, scratch
):
    rows = state_out.shape[0]
    copy_blocks(tri_scratch, tri_in, tri_in.shape[0])

    def body(row):
        state = join(read_plain, source, row)
        pieces = tri_post_row(state, join(read_inner, tri_scratch, row), cols, proj_t, gate_t)
        state = state + pieces[6] * pieces[7]
        put_rows(state_out, row, state)
        unit, inverse = standardize(state)
        lowered = (unit * column(next_cols, 0) + column(next_cols, 1)).astype(BF16)
        put_inner(scratch, row, mm(bias_t[...], lowered))

    each_group(rows, body)
    bias_out[...] = scratch[: bias_out.shape[0]].astype(BF16)


def flipped_bias_kernel(source, cols, bias_t, bias_out, scratch):
    rows = source[0].shape[1]

    def body(row):
        unit, inverse = standardize(join(read_flipped, source, row))
        lowered = (unit * column(cols, 0) + column(cols, 1)).astype(BF16)
        put_inner(scratch, row, mm(bias_t[...], lowered))

    each_group(rows, body)
    bias_out[...] = scratch[: bias_out.shape[0]].astype(BF16)


def fill_bias(alive, bias_in, table):
    @pl.when(pl.program_id(0) == 0)
    def _():
        length = table.shape[1]
        penalty = (alive[0:1] - 1.0) * (MASKED * LOG2E)
        for head in range(table.shape[0]):
            values = bias_in[:, head].reshape(length, length).astype(F32)
            table[head] = (values * LOG2E + penalty).T


def attention_row(state, cols, proj_t):
    unit, inverse = standardize(state)
    lowered = (unit * column(cols, 0) + column(cols, 1)).astype(BF16)
    project = mm(proj_t[...], lowered)
    width = project.shape[0] // 4
    size = width // TA_HEADS
    query = (project[:width] * (size**-0.5 * LOG2E)).astype(BF16)
    key = project[width : 2 * width].astype(BF16)
    value = project[2 * width : 3 * width].astype(BF16)
    gate = sigmoid(project[3 * width :])
    return unit, inverse, lowered, query, key, value, gate


def in_stages(blocks, first, second, third):
    early, late, done = {}, {}, {}
    count = len(blocks)
    for step in range(count + 2 * LAG):
        if step < count:
            early[step] = first(*blocks[step])
        if 0 <= step - LAG < count:
            late[step - LAG] = second(*blocks[step - LAG], early.pop(step - LAG))
        if 0 <= step - 2 * LAG < count:
            place = step - 2 * LAG
            done[blocks[place]] = third(*blocks[place], late.pop(place))
    return done


def head_rows(values, place, head):
    size, length = values.shape[0] // TA_HEADS, values.shape[1] // GROUP
    return values[head * size : (head + 1) * size, place * length : (place + 1) * length]


def gather_heads(done):
    return jnp.concatenate(
        [
            jnp.concatenate([done[place, head] for head in range(TA_HEADS)], axis=0)
            for place in range(GROUP)
        ],
        axis=1,
    )


ROW_BLOCKS = [(place, head) for place in range(GROUP) for head in range(TA_HEADS)]
HEAD_BLOCKS = [(place, head) for head in range(TA_HEADS) for place in range(GROUP)]


def attend_rows(state, row, cols, proj_t, output_t, table, totals, mixed_out):
    unit, inverse, lowered, query, key, value, gate = attention_row(state, cols, proj_t)

    def score(place, head):
        return mm_tn(head_rows(key, place, head), head_rows(query, place, head)) + table[head]

    def shift(place, head, scores):
        top = jnp.max(scores, axis=0, keepdims=True)
        return top, jnp.exp2(scores - top).astype(BF16)

    def mix(place, head, items):
        top, shifted = items
        values = head_rows(value, place, head)
        size = values.shape[0]
        values = jnp.concatenate([values, jnp.ones((16, values.shape[1]), BF16)], axis=0)
        result = mm(values, shifted)
        total = result[size : size + 1]
        return result[:size] / total, top + jnp.log2(total)

    done = in_stages(ROW_BLOCKS, score, shift, mix)
    mixed = gather_heads({block: items[0] for block, items in done.items()})
    put_rows(totals, row, gather_heads({block: items[1] for block, items in done.items()}))
    put_rows(mixed_out, row, mixed)
    return state + mm(output_t[...], (mixed * gate).astype(BF16))


def starting_kernel(
    alive, source, bias_in, cols, proj_t, output_t, out, totals, mixed, table, scratch
):
    fill_bias(alive, bias_in, table)
    rows = source.shape[0]

    def body(row):
        state = attend_rows(
            join(read_plain, source, row), row, cols, proj_t, output_t, table, totals, mixed
        )
        put_turned(scratch, row, state)

    each_group(rows, body)
    store_flipped(out, scratch)


def ending_kernel(alive, source, bias_in, cols, proj_t, output_t, out, totals, mixed, table):
    fill_bias(alive, bias_in, table)
    rows = source[0].shape[1]

    def body(row):
        state = attend_rows(
            join(read_flipped, source, row), row, cols, proj_t, output_t, table, totals, mixed
        )
        put_rows(out, row, state)

    each_group(rows, body)


def transition_kernel(
    order, source, cols, up_t, down_t, next_cols, bias_t, state_out, pair_out, bias_out, scratch, bias_scratch
):
    rows = source.shape[0]

    def body(row):
        state = join(read_plain, source, row)
        unit, inverse = standardize(state)
        lowered = (unit * column(cols, 0) + column(cols, 1)).astype(BF16)
        hidden = mm(up_t[...], lowered)
        half = hidden.shape[0] // 2
        first = hidden[:half]
        mixed = (first * sigmoid(first) * hidden[half:]).astype(BF16)
        state = state + mm(down_t[...], mixed)
        put_rows(state_out, row, state)
        put_turned(scratch, row, state)
        unit, inverse = standardize(state)
        lowered = (unit * column(next_cols, 0) + column(next_cols, 1)).astype(BF16)
        put_inner(bias_scratch, row, mm(bias_t[...], lowered))

    each_group(rows, body)
    size = pair_out.shape[0] // len(order)
    for place, held in enumerate(order):
        pair_out[place * size : (place + 1) * size] = scratch[held * size : (held + 1) * size].astype(BF16)
    bias_to_lanes(bias_out, bias_scratch)


def transition_back_kernel(
    read, mid, final, cotangent, bias_grad, cols, up_t, up, down, next_cols, bias_w,
    grad_out, up_grad, down_grad, bias_w_grad, vecs, norm_gain, norm_bias, pair_gain, pair_bias, bias_scratch,
):
    zero_first(norm_gain, norm_bias, pair_gain, pair_bias)
    rows = mid.shape[0]
    lanes_to_bias(bias_scratch, bias_grad)

    def body(row):
        grad = join(read, cotangent, row)
        unit, inverse = standardize(join(read_plain, final, row))
        gain = column(next_cols, 0)
        lowered = (unit * gain + column(next_cols, 1)).astype(BF16)
        grad_bias = join(read_inner, bias_scratch, row).astype(BF16)
        bias_w_grad[...] += mm_nt(lowered, grad_bias)
        grad_lowered = mm(bias_w[...], grad_bias)
        add_lanes(pair_gain, grad_lowered * unit)
        add_lanes(pair_bias, grad_lowered)
        grad = grad + standardize_back(unit, inverse, grad_lowered * gain)
        unit, inverse = standardize(join(read_plain, mid, row))
        gain = column(cols, 0)
        lowered = (unit * gain + column(cols, 1)).astype(BF16)
        hidden = mm(up_t[...], lowered)
        half = hidden.shape[0] // 2
        first, second = hidden[:half], hidden[half:]
        slope = sigmoid(first)
        silu = first * slope
        grad_low = grad.astype(BF16)
        grad_mixed = mm(down[...], grad_low)
        down_grad[...] += mm_nt((silu * second).astype(BF16), grad_low)
        grad_hidden = jnp.concatenate(
            [
                (grad_mixed * second * (slope + silu * (1.0 - slope))).astype(BF16),
                (grad_mixed * silu).astype(BF16),
            ],
            axis=0,
        )
        up_grad[...] += mm_nt(lowered, grad_hidden)
        grad_lowered = mm(up[...], grad_hidden)
        add_lanes(norm_gain, grad_lowered * unit)
        add_lanes(norm_bias, grad_lowered)
        put_rows(grad_out, row, grad + standardize_back(unit, inverse, grad_lowered * gain))

    each_group(rows, body)

    def finish():
        vecs[0:1] += lane_sums(norm_gain)
        vecs[1:2] += lane_sums(norm_bias)
        vecs[2:3] += lane_sums(pair_gain)
        vecs[3:4] += lane_sums(pair_bias)

    on_last(finish)


def attention_back_kernel(
    read, read_grad, alive, source, grad_in, bias_in, totals, mixed_in, cols, proj_t, proj, output,
    grad_out, bias_out, proj_grad, output_grad, table, grad_table,
):
    fill_bias(alive, bias_in, table)
    zero_first(grad_table)
    rows = grad_out.shape[0]

    def body(row):
        unit, inverse, lowered, query, key, value, gate = attention_row(
            join(read, source, row), cols, proj_t
        )
        mixed = join(read_plain, mixed_in, row)
        total = join(read_plain, totals, row)
        grad_low = join(read_grad, grad_in, row).astype(BF16)
        gated = mixed * gate
        output_grad[...] += mm_nt(gated.astype(BF16), grad_low)
        grad_gated = mm(output[...], grad_low)
        grad_gate = grad_gated * gated * (1.0 - gate)
        grad_mixed = (grad_gated * gate).astype(BF16)
        product = grad_mixed.astype(F32) * mixed
        size = query.shape[0] // TA_HEADS

        def score(place, head):
            scores = mm_tn(head_rows(key, place, head), head_rows(query, place, head))
            grads = mm_tn(head_rows(value, place, head), head_rows(grad_mixed, place, head))
            return scores + table[head], grads

        def slope(place, head, items):
            scores, grads = items
            probs = jnp.exp2(scores - head_rows(total, place, head))
            delta = jnp.sum(head_rows(product, place, head), axis=0, keepdims=True)
            grad_scores = probs * (grads - delta)
            grad_table[head] += grad_scores
            return probs.astype(BF16), grad_scores.astype(BF16)

        def back(place, head, items):
            probs, grad_scores = items
            return (
                mm(head_rows(key, place, head), grad_scores) * size**-0.5,
                mm_nt(head_rows(query, place, head), grad_scores) * (1.0 / LOG2E),
                mm_nt(head_rows(grad_mixed, place, head), probs),
            )

        done = in_stages(HEAD_BLOCKS, score, slope, back)
        grad_project = jnp.concatenate(
            [
                gather_heads({block: items[part] for block, items in done.items()})
                for part in range(3)
            ]
            + [grad_gate],
            axis=0,
        ).astype(BF16)
        proj_grad[...] += mm_nt(lowered, grad_project)
        put_rows(grad_out, row, mm(proj[...], grad_project))

    each_group(rows, body)

    def finish():
        for head in range(TA_HEADS):
            bias_out[:, head] = (
                grad_table[head].T.astype(BF16).reshape(bias_out.shape[0], bias_out.shape[2], -1)
            )

    on_last(finish)


def attention_end_row(
    state, grad, grad_lowered, grad_bias, cols, bias_w, bias_w_grad, norm_gain, norm_bias
):
    unit, inverse = standardize(state)
    gain = column(cols, 0)
    lowered = (unit * gain + column(cols, 1)).astype(BF16)
    bias_w_grad[...] += mm_nt(lowered, grad_bias)
    grad_lowered = grad_lowered + mm(bias_w[...], grad_bias)
    add_lanes(norm_gain, grad_lowered * unit)
    add_lanes(norm_bias, grad_lowered)
    return grad + standardize_back(unit, inverse, grad_lowered * gain)


def fill_bias_grad(scratch, bias_grad):
    heads = bias_grad.shape[1]
    total = bias_grad[0].astype(F32)
    for device in range(1, bias_grad.shape[0]):
        total = total + bias_grad[device].astype(F32)
    scratch[:heads] = total
    scratch[heads:] = jnp.zeros((scratch.shape[0] - heads,) + scratch.shape[1:], F32)


def ending_end_kernel(
    source, grad_in, grad_lowered, bias_grad, cols, bias_w,
    grad_out, bias_w_grad, vecs, norm_gain, norm_bias, bias_scratch, scratch,
):
    zero_first(norm_gain, norm_bias)
    fill_bias_grad(bias_scratch, bias_grad)
    rows = grad_in.shape[0]

    def body(row):
        grad = attention_end_row(
            join(read_flipped, source, row), join(read_plain, grad_in, row),
            join(read_plain, grad_lowered, row), join(read_inner, bias_scratch, row).astype(BF16), cols, bias_w, bias_w_grad, norm_gain, norm_bias,
        )
        put_turned(scratch, row, grad)

    each_group(rows, body)
    store_flipped(grad_out, scratch)

    def finish():
        vecs[0:1] += lane_sums(norm_gain)
        vecs[1:2] += lane_sums(norm_bias)

    on_last(finish)


def tri_post_back_row(
    state, tri, grad, cols, proj_t, gate_t, proj, gate_w, proj_grad, gate_grad, out_gain, out_bias
):
    unit, inverse, lowered, tri_unit, tri_inverse, out_low, output, gate = tri_post_row(
        state, tri, cols, proj_t, gate_t
    )
    grad_output = grad * gate
    grad_gate = (grad_output * output * (1.0 - gate)).astype(BF16)
    grad_output = grad_output.astype(BF16)
    proj_grad[...] += mm_nt(out_low, grad_output)
    gate_grad[...] += mm_nt(lowered, grad_gate)
    grad_normed = mm(proj[...], grad_output)
    add_lanes(out_gain, grad_normed * tri_unit)
    add_lanes(out_bias, grad_normed)
    grad_tri = standardize_back(tri_unit, tri_inverse, grad_normed * column(cols, 2))
    return grad_tri, mm(gate_w[...], grad_gate)


def starting_end_kernel(
    source, grad_in, grad_lowered, bias_grad, cols, bias_w,
    below, tri_in, tri_cols, proj_t, gate_t, proj, gate_w,
    grad_out, tri_out, gate_back, bias_w_grad, proj_grad, gate_grad, vecs,
    norm_gain, norm_bias, out_gain, out_bias, bias_scratch, tri_scratch,
):
    zero_first(norm_gain, norm_bias, out_gain, out_bias)
    fill_bias_grad(bias_scratch, bias_grad)
    copy_blocks(tri_scratch, tri_in, tri_in.shape[0])
    rows = source.shape[0]

    def body(row):
        grad = attention_end_row(
            join(read_plain, source, row), join(read_flipped, grad_in, row),
            join(read_plain, grad_lowered, row), join(read_inner, bias_scratch, row).astype(BF16), cols, bias_w, bias_w_grad, norm_gain, norm_bias,
        )
        put_rows(grad_out, row, grad)
        grad_tri, back = tri_post_back_row(
            join(read_plain, below, row), join(read_inner, tri_scratch, row), grad, tri_cols, proj_t, gate_t, proj, gate_w,
            proj_grad, gate_grad, out_gain, out_bias,
        )
        put_rows(gate_back, row, back)
        put_inner(tri_scratch, row, grad_tri)

    each_group(rows, body)
    copy_blocks(tri_out, tri_scratch, tri_out.shape[0])

    def finish():
        vecs[0:1] += lane_sums(norm_gain)
        vecs[1:2] += lane_sums(norm_bias)
        vecs[2:3] += lane_sums(out_gain)
        vecs[3:4] += lane_sums(out_bias)

    on_last(finish)


def tri_product_back_kernel(incoming, grad, operands, *outs):
    def body(channel):
        first = whole_rows(operands, 0, channel)
        second = whole_rows(operands, 1, channel)
        tri = whole_rows(grad, channel)
        if incoming:
            grad_first = mm_nt(second, tri)
            grad_second = mm(first, tri)
        else:
            grad_first = mm(tri, second)
            grad_second = mm_tn(tri, first)
        split_rows(grad_first, outs, 0, channel)
        split_rows(grad_second, outs, 1, channel)

    each_channel(operands[0].shape[2], body)


def tri_pre_back_row(
    info, alive, row, state, product_grad, gate_back, grad, cols, proj_t, proj, proj_grad, norm_gain, norm_bias
):
    unit, inverse = standardize(state)
    gain = column(cols, 0)
    lowered = (unit * gain + column(cols, 1)).astype(BF16)
    project = mm(proj_t[...], lowered)
    half = project.shape[0] // 2
    gate = sigmoid(project[half:])
    grad_first = product_grad * gate * live_pair(info, alive, row)
    grad_second = grad_first * project[:half] * (1.0 - gate)
    grad_project = jnp.concatenate([grad_first.astype(BF16), grad_second.astype(BF16)], axis=0)
    proj_grad[...] += mm_nt(lowered, grad_project)
    grad_lowered = mm(proj[...], grad_project) + gate_back
    add_lanes(norm_gain, grad_lowered * unit)
    add_lanes(norm_bias, grad_lowered)
    return grad + standardize_back(unit, inverse, grad_lowered * gain)


def fill_product_grad(scratch, product_grad):
    devices, part = product_grad.shape[0], product_grad.shape[2]

    def one(device, carry):
        scratch[pl.ds(device * part, part)] = product_grad[device, 0].astype(F32)
        scratch[pl.ds((devices + device) * part, part)] = product_grad[device, 1].astype(F32)
        return carry

    lax.fori_loop(0, devices, one, 0)


def tri_join_back_kernel(
    read, info, alive, source, product_grad, gate_in, grad_in, cols, proj_t, proj,
    below, tri_in, tri_cols, out_t, gate_t, out_w, gate_w,
    grad_out, tri_out, gate_back, proj_grad, out_grad, gate_grad, vecs,
    norm_gain, norm_bias, out_gain, out_bias, scratch, tri_scratch,
):
    zero_first(norm_gain, norm_bias, out_gain, out_bias)
    fill_product_grad(scratch, product_grad)
    copy_blocks(tri_scratch, tri_in, tri_in.shape[0])
    rows = source.shape[0]

    def body(row):
        grad = tri_pre_back_row(
            info, alive, row_base(rows) + row, join(read_plain, source, row),
            join(read_inner, scratch, row), join(read_plain, gate_in, row),
            join(read_plain, grad_in, row), cols, proj_t, proj, proj_grad, norm_gain, norm_bias,
        )
        put_rows(grad_out, row, grad)
        grad_tri, back = tri_post_back_row(
            join(read, below, row), join(read_inner, tri_scratch, row), grad, tri_cols, out_t, gate_t, out_w, gate_w,
            out_grad, gate_grad, out_gain, out_bias,
        )
        put_rows(gate_back, row, back)
        put_inner(tri_scratch, row, grad_tri)

    each_group(rows, body)
    copy_blocks(tri_out, tri_scratch, tri_out.shape[0])

    def finish():
        vecs[0:1] += lane_sums(norm_gain)
        vecs[1:2] += lane_sums(norm_bias)
        vecs[2:3] += lane_sums(out_gain)
        vecs[3:4] += lane_sums(out_bias)

    on_last(finish)


def tri_first_back_kernel(
    read, order, info, alive, source, product_grad, gate_in, grad_in, cols, proj_t, proj,
    grad_out, proj_grad, vecs, norm_gain, norm_bias, scratch,
):
    zero_first(norm_gain, norm_bias)
    fill_product_grad(scratch, product_grad)
    rows = source.shape[0]

    def body(row):
        grad = tri_pre_back_row(
            info, alive, row_base(rows) + row, join(read, source, row),
            join(read_inner, scratch, row), join(read_plain, gate_in, row),
            join(read_plain, grad_in, row), cols, proj_t, proj, proj_grad, norm_gain, norm_bias,
        )
        for place, part in enumerate(pieces_of(grad)):
            grad_out[row + place] = reorder(part.T, order).astype(grad_out.dtype)

    each_group(rows, body)

    def finish():
        vecs[0:1] += lane_sums(norm_gain)
        vecs[1:2] += lane_sums(norm_bias)

    on_last(finish)


RUN = 24


def table_of(entries):
    table = {}
    offset = 0
    for name, shape in entries:
        table[name] = (offset // STRIDE, shape)
        offset += math.prod(shape)
    return table, offset


def runs_kernel(info, shard, out, scratch):
    def one(block, carry):
        scratch[:, block, :] = shard[pl.ds(block * STRIDE, STRIDE), :].T
        return carry

    lax.fori_loop(0, RUN, one, 0)
    half = STRIDE // 2
    turn = info[0] * half

    def move(lane, carry):
        out[lane] = scratch[lax.rem(lane + turn, STRIDE)].astype(BF16)
        return carry

    lax.fori_loop(0, STRIDE, move, 0)


def run_place(shards, total, lane, shard):
    count = total // STRIDE
    whole = total // shards
    step, odd = whole // STRIDE, (whole % STRIDE) // (STRIDE // 2)
    extra = lax.div(shard * odd + jnp.where(lane < STRIDE // 2, 1, 0), 2)
    start = lane * count + shard * step + extra
    return lax.div(start, STRIDE), lax.rem(start, STRIDE)


def rows_from_runs(runs, rows, first_lane, total):
    shards, lanes = runs.shape[0], runs.shape[1]
    base = first_lane * (total // STRIDE) // STRIDE

    def one(index, carry):
        lane, shard = lax.div(index, shards), lax.rem(index, shards)
        row, shift = run_place(shards, total, first_lane + lane, shard)
        row = row - base
        turned = pltpu.roll(runs[shard, lane].astype(F32), shift, 1)
        place = lax.broadcasted_iota(jnp.int32, (RUN + 1, STRIDE), 1)
        last, before = carry
        joint = jnp.where(row - before == RUN, last[2:3], last[1:2])
        below = jnp.concatenate([joint, turned], axis=0)
        above = jnp.concatenate([turned, turned[RUN - 1 :]], axis=0)
        values = jnp.where(place < shift, below, above)
        rows[pl.ds(row, RUN + 1), :] = values
        return values[RUN - 2 :], row

    lax.fori_loop(0, shards * lanes, one, (jnp.zeros((3, STRIDE), F32), -RUN), unroll=4)


def runs_from_rows(rows, out, first_lane, base, total):
    shards, lanes = out.shape[0], out.shape[1]

    def one(index, carry):
        lane, shard = lax.div(index, shards), lax.rem(index, shards)
        row, shift = run_place(shards, total, first_lane + lane, shard)
        turned = pltpu.roll(rows[pl.ds(row - base, RUN + 1), :], (STRIDE - shift) % STRIDE, 1)
        place = lax.broadcasted_iota(jnp.int32, (RUN, STRIDE), 1)
        out[shard, lane] = jnp.where(
            place < STRIDE - shift, turned[:RUN], turned[1:]
        ).astype(BF16)
        return carry

    lax.fori_loop(0, shards * lanes, one, 0, unroll=4)


def row_height(base, first_lane, last_lane, total):
    end = (last_lane * (total // STRIDE)) // STRIDE + RUN + 2
    return -(-(end - base) // 8) * 8


def take_matrix(rows, first, shape):
    blocks = shape[1] // STRIDE
    return [
        rows[pl.ds(first + block, shape[0], stride=blocks), :]
        if blocks > 1
        else rows[first : first + shape[0], :]
        for block in range(blocks)
    ]


def put_matrix(rows, first, matrix):
    height, width = matrix.shape
    blocks = width // STRIDE
    for block in range(blocks):
        part = matrix[:, block * STRIDE : (block + 1) * STRIDE]
        if blocks > 1:
            rows[pl.ds(first + block, height, stride=blocks), :] = part
        else:
            rows[first : first + height, :] = part


def spread(index, heads, rows):
    lane = lax.broadcasted_iota(jnp.int32, (STRIDE, STRIDE), 0)
    channel = lax.broadcasted_iota(jnp.int32, (STRIDE, STRIDE), 1)
    return (channel == index * (STRIDE // heads) + lane // heads).astype(BF16)


def take_narrow(rows, first, heads, high):
    total = jnp.zeros((high, STRIDE), F32)
    head = lax.broadcasted_iota(jnp.int32, (high, STRIDE), 0)
    lane = lax.broadcasted_iota(jnp.int32, (high, STRIDE), 1)
    for index in range(heads):
        line = rows[first + index : first + index + 1, :]
        picked = jnp.where(lane % heads == head, line, 0.0).astype(BF16)
        total = total + mm(picked, spread(index, heads, rows))
    return total


def put_narrow(rows, first, heads, matrix):
    turned = matrix.T.astype(BF16)
    high = turned.shape[0]
    head = lax.broadcasted_iota(jnp.int32, (high, STRIDE), 0)
    lane = lax.broadcasted_iota(jnp.int32, (high, STRIDE), 1)
    for index in range(heads):
        wide = mm_nt(turned, spread(index, heads, rows))
        rows[first + index : first + index + 1, :] = jnp.sum(
            jnp.where(lane % heads == head, wide, 0.0), axis=0, keepdims=True
        )


PAIR_MATRICES = (
    (OUTGOING, PROJ_GATE), (OUTGOING, PROJ_OUT), (OUTGOING, GATE_OUT),
    (INCOMING, PROJ_GATE), (INCOMING, PROJ_OUT), (INCOMING, GATE_OUT),
    (STARTING, QKVG), (STARTING, OUTPUT), (ENDING, QKVG), (ENDING, OUTPUT), (PAIR, UP), (PAIR, DOWN),
)
PAIR_COLUMNS = (
    (OUTGOING, ((OUTGOING, NORM_GAIN), (OUTGOING, NORM_BIAS), (OUTGOING, OUT_GAIN), (OUTGOING, OUT_BIAS))),
    (INCOMING, ((INCOMING, NORM_GAIN), (INCOMING, NORM_BIAS), (INCOMING, OUT_GAIN), (INCOMING, OUT_BIAS))),
    (STARTING, ((STARTING, NORM_GAIN), (STARTING, NORM_BIAS))),
    (ENDING, ((ENDING, NORM_GAIN), (ENDING, NORM_BIAS))),
    (PAIR, ((PAIR, NORM_GAIN), (PAIR, NORM_BIAS))),
)
SINGLE_MATRICES = ((ATTEND, QKVG), (ATTEND, OUTPUT), (SINGLE, UP), (SINGLE, DOWN))
SINGLE_VECTORS = ((ATTEND, NORM_GAIN), (ATTEND, NORM_BIAS), (SINGLE, NORM_GAIN), (SINGLE, NORM_BIAS))


def put_columns(rows, out, table, base, names):
    out[...] = jnp.zeros(out.shape, F32)
    lines = [rows[table[name][0] - base : table[name][0] - base + 1, :] for name in names]
    lines.append(jnp.zeros((8 - len(lines), STRIDE), F32))
    out[...] = jnp.concatenate(lines, axis=0).T


def unpack_pair_kernel(table, total, runs, *refs):
    rows = refs[-1]
    outs = list(refs[:-1])
    rows_from_runs(runs, rows, 0, total)
    for name in PAIR_MATRICES:
        first, shape = table[name]
        plain, turned = outs.pop(0), outs.pop(0)
        for block, part in enumerate(take_matrix(rows, first, shape)):
            place = slice(block * STRIDE, (block + 1) * STRIDE)
            plain[:, place] = part.astype(BF16)
            turned[place, :] = part.T.astype(BF16)
    for prefix in (STARTING, ENDING):
        plain, turned = outs.pop(0), outs.pop(0)
        first, shape = table[(prefix, BIAS_PROJ)]
        matrix = take_narrow(rows, first, shape[1], 8)
        turned[...] = matrix.astype(BF16)
        plain[...] = matrix.T.astype(BF16)
    for prefix, names in PAIR_COLUMNS:
        put_columns(rows, outs.pop(0), table, 0, names)


def unpack_single_kernel(table, total, first_lane, runs, *refs):
    rows = refs[-1]
    outs = list(refs[:-1])
    rows_from_runs(runs, rows, first_lane, total)
    base = first_lane * (total // STRIDE) // STRIDE
    for name in SINGLE_MATRICES:
        first, shape = table[name]
        out = outs.pop(0)
        for block, part in enumerate(take_matrix(rows, first - base, shape)):
            out[:, block * STRIDE : (block + 1) * STRIDE] = part.astype(BF16)
    first, shape = table[(ATTEND, PAIR_PROJ)]
    matrix = take_narrow(rows, first - base, shape[1], shape[1])
    plain, turned = outs.pop(0), outs.pop(0)
    turned[...] = matrix.astype(BF16)
    plain[...] = matrix.T.astype(BF16)
    put_columns(rows, outs.pop(0), table, base, ((ATTEND, PAIR_GAIN), (ATTEND, PAIR_BIAS)))
    lines = outs.pop(0)
    lines[...] = jnp.zeros(lines.shape, F32)
    for index, name in enumerate(SINGLE_VECTORS):
        first, shape = table[name]
        for block in range(shape[0] // STRIDE):
            lines[index : index + 1, block * STRIDE : (block + 1) * STRIDE] = rows[
                first - base + block : first - base + block + 1, :
            ]


def pack_kernel(table, total, first_lane, base, names, *refs):
    ins, out, rows = refs[: len(names)], refs[-2], refs[-1]
    for name, ref in zip(names, ins):
        if isinstance(name, tuple):
            first, shape = table[name]
            if shape[1] % STRIDE:
                put_narrow(rows, first - base, shape[1], ref[...])
            else:
                put_matrix(rows, first - base, ref)
        else:
            for index, vector in name:
                first, shape = table[vector]
                for block in range(shape[0] // STRIDE):
                    rows[first + block - base : first + block - base + 1, :] = ref[
                        index : index + 1, block * STRIDE : (block + 1) * STRIDE
                    ]
    runs_from_rows(rows, out, first_lane, base, total)


def shard_kernel(whole, info, summed, others, out, squares, runs):
    half = STRIDE // 2
    crops, first, part = summed.shape[0], summed.shape[1], others.shape[1]

    def add(lane, carry):
        runs[lane] = sum(summed[crop, lane].astype(F32) for crop in range(crops))
        return carry

    lax.fori_loop(0, first, add, 0)
    for crop in range(crops):

        def move(lane, carry, crop=crop):
            runs[first + crop * part + lane] = others[crop, lane].astype(F32)
            return carry

        lax.fori_loop(0, part, move, 0)
    squares[...] = jnp.zeros(squares.shape, F32)

    def one(block, carry):
        first = runs[pl.ds(info[0] * half, half), block, :]
        second = runs[pl.ds(half - info[0] * half, half), block, :]
        values = jnp.concatenate([first, second], axis=0).T
        row = block * STRIDE + lax.broadcasted_iota(jnp.int32, values.shape, 0)
        lane = lax.broadcasted_iota(jnp.int32, values.shape, 1)
        values = jnp.where(row * STRIDE + lane < whole, values, 0.0)
        out[pl.ds(block * STRIDE, STRIDE), :] = values
        squares[...] += jnp.sum((values * values).reshape(-1, 8, STRIDE), axis=0)
        return carry

    lax.fori_loop(0, RUN, one, 0)


def whole_call(kernel, name, ins, outs, scratch, time=8):
    def spec(axis):
        return pl.BlockSpec(memory_space=pltpu.SMEM if axis == "smem" else pltpu.VMEM)

    return pl.pallas_call(
        kernel,
        in_specs=[spec(axis) for array, axis in ins],
        out_specs=[pl.BlockSpec(memory_space=pltpu.VMEM) for shape, dtype in outs],
        out_shape=[jax.ShapeDtypeStruct(shape, dtype) for shape, dtype in outs],
        scratch_shapes=[pltpu.VMEM(shape, dtype) for shape, dtype in scratch],
        compiler_params=pltpu.CompilerParams(vmem_limit_bytes=VMEM_LIMIT),
        cost_estimate=cost(time),
        name=name,
    )(*[array for array, axis in ins])


def unpack_pair(table, total, runs):
    outs = []
    names = []
    for name in PAIR_MATRICES:
        shape = table[name][1]
        outs += [(shape, BF16), (shape[::-1], BF16)]
        names += [name, (name, T)]
    for prefix in (STARTING, ENDING):
        outs += [((STRIDE, 8), BF16), ((8, STRIDE), BF16)]
        names += [(prefix, BIAS_W), (prefix, BIAS_T)]
    for prefix, parts in PAIR_COLUMNS:
        outs.append(((STRIDE, 8), F32))
        names.append((prefix, COLS))
    height = row_height(0, 0, runs.shape[1], total)
    values = whole_call(
        functools.partial(unpack_pair_kernel, table, total), "pair_weights", [(runs, None)], outs,
        [((height, STRIDE), F32)], 20,
    )
    return dict(zip(names, values))


def unpack_single(table, total, first_lane, runs):
    outs = [(table[name][1], BF16) for name in SINGLE_MATRICES]
    names = list(SINGLE_MATRICES)
    shape = table[(ATTEND, PAIR_PROJ)][1]
    outs += [(shape, BF16), (shape[::-1], BF16), ((STRIDE, 8), F32), ((8, S), F32)]
    names += [(ATTEND, PAIR_PROJ), ((ATTEND, PAIR_PROJ), T), (ATTEND, COLS), (SINGLE, VECTORS)]
    base = first_lane * (total // STRIDE) // STRIDE
    height = row_height(base, first_lane, first_lane + runs.shape[1], total)
    values = whole_call(
        functools.partial(unpack_single_kernel, table, total, first_lane), "single_weights",
        [(runs, None)], outs, [((height, STRIDE), F32)],
    )
    return dict(zip(names, values))


def pack(name, table, total, shards, lanes, base, parts):
    height = row_height(base, *lanes, total)
    for held, array in parts:
        if isinstance(held, tuple):
            end = table[held][0] - base + array.shape[0] * max(1, array.shape[1] // STRIDE)
            height = max(height, -(-end // 8) * 8)
    return whole_call(
        functools.partial(pack_kernel, table, total, lanes[0], base, [held for held, array in parts]),
        name, [(array, None) for held, array in parts],
        [((shards, lanes[1] - lanes[0], RUN, STRIDE), BF16)], [((height, STRIDE), F32)],
    )[0]


def bias_to_lanes(out, scratch):
    heads, devices = scratch.shape[0], out.shape[0]
    part = scratch.shape[2] // devices
    per = STRIDE // part
    lane = lax.broadcasted_iota(jnp.int32, (scratch.shape[1], STRIDE), 1)
    for device in range(devices):
        block, place = device // per, device % per
        for first in range(0, heads, per):
            total = None
            for index in range(per):
                values = scratch[first + index, :, block * STRIDE : (block + 1) * STRIDE]
                values = pltpu.roll(values, (index - place) * part % STRIDE, 1)
                total = values if index == 0 else jnp.where(lane < index * part, total, values)
            out[device, :, first * part : first * part + STRIDE] = total.astype(out.dtype)


def lanes_to_bias(scratch, sent):
    heads, devices = scratch.shape[0], sent.shape[0]
    part = scratch.shape[2] // devices
    per = STRIDE // part
    lane = lax.broadcasted_iota(jnp.int32, (scratch.shape[1], STRIDE), 1)
    for head in range(heads):
        first, index = head // per * per, head % per
        for block in range(devices // per):
            total = None
            for place in range(per):
                values = sent[block * per + place, :, first * part : first * part + STRIDE].astype(F32)
                values = pltpu.roll(values, (place - index) * part % STRIDE, 1)
                total = values if place == 0 else jnp.where(lane < place * part, total, values)
            scratch[head, :, block * STRIDE : (block + 1) * STRIDE] = total


def standardize_lanes(values):
    centred = values - jnp.mean(values, axis=1, keepdims=True)
    inverse = lax.rsqrt(jnp.mean(centred * centred, axis=1, keepdims=True) + EPSILON)
    return centred * inverse, inverse


def single_kernel(
    state_in, back_in, project, kv, bias, alive, vectors, output_w, up, down,
    final_out, grad_out, sent, query_grad, gate_grad, output_grad, up_grad, down_grad, vecs,
):
    state = state_in[...]
    rows, width = state.shape
    size = width // SA_HEADS
    per = STRIDE // rows
    groups = SA_HEADS // per
    scale = size**-0.5
    tokens = kv.shape[0] * rows
    both = kv[...].reshape(tokens, 2 * width)
    keys, values = both[:, :width], both[:, width:]
    penalty = ((alive[...] - 1.0) * (MASKED * LOG2E)).T[:, 0:1]

    channel = lax.broadcasted_iota(jnp.int32, (width, STRIDE), 0)
    lane = lax.broadcasted_iota(jnp.int32, (width, STRIDE), 1)
    own = [lax.div(channel, size) == group * per + lax.div(lane, rows) for group in range(groups)]
    channel_b = lax.broadcasted_iota(jnp.int32, (STRIDE, width), 1)
    row_b = lax.broadcasted_iota(jnp.int32, (STRIDE, width), 0)
    own_b = [lax.div(channel_b, size) == group * per + lax.div(row_b, rows) for group in range(groups)]

    def spread_rows(matrix):
        turned = jnp.concatenate([matrix] * per, axis=0).T
        return [jnp.where(mask, turned, 0.0).astype(BF16) for mask in own]

    def collect(blocks):
        total = sum(jnp.where(mask, block, 0.0) for mask, block in zip(own_b, blocks))
        return sum(total[index * rows : (index + 1) * rows] for index in range(per))

    queries = spread_rows(project[:, :width] * (scale * LOG2E))
    gate = sigmoid(project[:, 3 * width :])
    scores = [
        mm(keys, queries[group])
        + bias[:, :, group * STRIDE : (group + 1) * STRIDE].reshape(tokens, STRIDE).astype(F32) * LOG2E
        + penalty
        for group in range(groups)
    ]
    shifted = [jnp.exp2(block - jnp.max(block, axis=0, keepdims=True)) for block in scores]
    probs = [block / jnp.sum(block, axis=0, keepdims=True) for block in shifted]
    probs_low = [block.astype(BF16) for block in probs]
    mixed = collect([mm_tn(block, values) for block in probs_low])
    gated = mixed * gate
    gated_low = gated.astype(BF16)
    state = state + mm(gated_low, output_w[...])

    unit, inverse = standardize_lanes(state)
    gain = vectors[2:3]
    lowered = (unit * gain + vectors[3:4]).astype(BF16)
    hidden = mm(lowered, up[...])
    half = hidden.shape[1] // 2
    first, second = hidden[:, :half], hidden[:, half:]
    slope = sigmoid(first)
    silu = first * slope
    swish = (silu * second).astype(BF16)
    final_out[...] = state + mm(swish, down[...])

    grad = back_in[...]
    grad_low = grad.astype(BF16)
    grad_mixed = mm_nt(grad_low, down[...])
    down_grad[...] = mm_tn(swish, grad_low)
    grad_hidden = jnp.concatenate(
        [
            (grad_mixed * second * (slope + silu * (1.0 - slope))).astype(BF16),
            (grad_mixed * silu).astype(BF16),
        ],
        axis=1,
    )
    grad_lowered = mm_nt(grad_hidden, up[...])
    vecs[...] = jnp.zeros(vecs.shape, F32)
    vecs[0:1] = jnp.sum(grad_lowered * unit, axis=0, keepdims=True)
    vecs[1:2] = jnp.sum(grad_lowered, axis=0, keepdims=True)
    grad_unit = grad_lowered * gain
    grad = grad + inverse * (
        grad_unit
        - jnp.mean(grad_unit, axis=1, keepdims=True)
        - unit * jnp.mean(grad_unit * unit, axis=1, keepdims=True)
    )
    grad_out[...] = grad

    grad_low = grad.astype(BF16)
    grad_gated = mm_nt(grad_low, output_w[...])
    gate_grad[...] = grad_gated * gated * (1.0 - gate)
    grads = spread_rows(grad_gated * gate)
    grad_probs = [mm(values, block) for block in grads]
    grad_scores = []
    for block, grad_block in zip(probs, grad_probs):
        delta = jnp.sum(block * grad_block, axis=0, keepdims=True)
        grad_scores.append((block * (grad_block - delta)).astype(BF16))
    for group, block in enumerate(grad_scores):
        sent[:, :, group * STRIDE : (group + 1) * STRIDE] = block.reshape(kv.shape[0], rows, STRIDE)
    query_grad[...] = collect([mm_tn(block, keys) for block in grad_scores]) * scale
    key_part = sum(mm_nt(block, query) for block, query in zip(grad_scores, queries)) * (1.0 / LOG2E)
    value_part = sum(mm_nt(block, grad_block) for block, grad_block in zip(probs_low, grads))
    first = groups * STRIDE
    sent[:, :, first : first + width] = key_part.astype(BF16).reshape(kv.shape[0], rows, width)
    sent[:, :, first + width :] = value_part.astype(BF16).reshape(kv.shape[0], rows, width)
    output_grad[...] = mm_tn(gated_low, grad_low)
    up_grad[...] = mm_tn(lowered, grad_hidden)


def single_middle(state, back, projected, bias, alive, weights):
    lowered, project, kv = projected
    rows, width = state.shape
    devices = kv.shape[0]
    names = ((ATTEND, OUTPUT), (SINGLE, UP), (SINGLE, DOWN))
    matrices = [weights[name] for name in names]
    square = (rows, width)
    outs = [
        (square, F32), (square, F32), ((devices, rows, SA_HEADS * rows + 2 * width), BF16),
        (square, F32), (square, F32),
    ] + [(matrix.shape, F32) for matrix in matrices] + [((8, width), F32)]
    ins = [state, back, project, kv, bias, alive, weights[(SINGLE, VECTORS)]] + matrices
    final, grad, sent, query_grad, gate_grad, *found, vecs = whole_call(
        single_kernel, "single_path", [(array, None) for array in ins], outs, [], 15
    )
    grads = dict(zip(names, found))
    grads[(SINGLE, NORM_GAIN)], grads[(SINGLE, NORM_BIAS)] = vecs[0], vecs[1]
    return final, grad, sent, grads, (state, lowered, query_grad, gate_grad)


def swap(values, group):
    return lax.all_to_all(values, group, split_axis=0, concat_axis=0, tiled=True)


def single_project(single_state, weights, devices):
    gain, shift = norm_pair(weights, ATTEND)
    lowered = layer_norm(single_state, gain, shift).astype(BF16)
    width = lowered.shape[1]
    qkvg = matmul(lowered, weights[(ATTEND, QKVG)])
    both = qkvg[:, width : 3 * width].astype(BF16)
    both = jnp.broadcast_to(both[None], (devices,) + both.shape)
    return lowered, qkvg, both


def single_attend_end(pending, parts, weights, grads):
    single_state, lowered, grad_query, grad_gate = pending
    rows, width = lowered.shape
    grad_both = jnp.sum(parts.astype(F32), axis=0)
    grad_qkvg = jnp.concatenate(
        [grad_query.reshape(rows, width), grad_both, grad_gate], axis=-1
    ).astype(BF16)
    grads[(ATTEND, QKVG)] = outer_sum(lowered, grad_qkvg)
    grad_lowered = matmul(grad_qkvg, weights[(ATTEND, QKVG)].T)
    gain, shift = norm_pair(weights, ATTEND)
    grad_single, grads[(ATTEND, NORM_GAIN)], grads[(ATTEND, NORM_BIAS)] = norm_backward(
        single_state, gain, shift, grad_lowered
    )
    return grad_single


def after(values, *others):
    held = lax.optimization_barrier((values,) + others)
    return held


def in_turn():
    last = []

    def send(values, axes):
        if last:
            values = after(values, last.pop())[0]
        moved = swap(values, axes)
        last.append(moved)
        return moved

    return send


def pair_path(pair, info, alive, orders, weights, cotangent, middle, between, meet, send, group, parts):
    rows, length, width = pair.shape
    hidden = weights[(OUTGOING, PROJ_OUT)].shape[0]
    devices = length // rows
    cores = devices // parts
    order, order_back = orders
    read_first = functools.partial(read_tokens, order)
    read_last = functools.partial(read_turned, order)
    part = hidden // devices
    steps = rows // 16
    state_shape = (rows, width, length)
    block = rows // steps
    half = rows // 2
    flip_shape = (devices, rows, rows, width)
    product_shape = (devices, 2, part, rows, length)
    product_half = (devices, 2, part, half, length)
    tri_shape = (devices, part, rows, length)
    tri_half = (devices, part, half, length)
    channel_block = math.gcd(part, 4)

    def products(name, kernel, arrays, out_shape):
        axes = {4: 1, 5: 2}
        out = (out_shape, BF16, axes[len(out_shape)])
        return run_rows(
            kernel, name, part // channel_block,
            [(Both(pieces), axes[pieces[0].ndim]) for pieces in arrays],
            [out] * (rows // out_shape[-2]), [], 7,
        )

    def swap_all(pieces):
        return [send(values, group) for values in pieces]

    def by_hidden(pieces):
        return [values.reshape((hidden,) + values.shape[2:]) for values in pieces]

    def by_device(pieces):
        return [values.reshape((devices, part) + values.shape[1:]) for values in pieces]

    def cols(prefix):
        return weights[(prefix, COLS)]

    tri_cols = cols

    def turned(name):
        return weights[(name, T)]

    tri_scratch = ((hidden, block, length), F32)
    product_scratch = ((2 * hidden, block, length), F32)
    head_scratch = ((8, block, length), F32)
    wide = ((width, length), F32)
    flip_scratch = ((length, block, width), F32)
    table = ((TA_HEADS, length, length), F32)
    attend_saves = [((rows, TA_HEADS, length), F32, 0), (state_shape, BF16, 0)]

    product = run_rows(
        functools.partial(tri_pre_first_kernel, devices, read_first), "outgoing_in", steps,
        [
            (info, "smem"), (alive, None), (pair, 0), (tri_cols(OUTGOING), None),
            (turned((OUTGOING, PROJ_GATE)), None),
        ],
        [(product_shape, BF16, 3)], [product_scratch], 13,
    )
    between(0, product[0])
    product_one = swap_all(product)
    tri_one = products(
        "outgoing_product", functools.partial(tri_product_kernel, False), [product_one], tri_half
    )
    tri_one = by_hidden(swap_all(tri_one))
    tri_one = [tri_one[0], *meet(0, tri_one[1])]
    state_one, product = run_halves(
        functools.partial(tri_join_kernel, devices, read_first), "outgoing_out_incoming_in", steps,
        [
            ([info[:half], info[half:]], "smem"), (alive, None), (pair, 0), (tri_one, 1), (tri_cols(OUTGOING), None),
            (turned((OUTGOING, PROJ_OUT)), None), (turned((OUTGOING, GATE_OUT)), None),
            (tri_cols(INCOMING), None), (turned((INCOMING, PROJ_GATE)), None),
        ],
        [(state_shape, F32, 0), (product_half, BF16, 3)], [tri_scratch, product_scratch], 22,
    )
    product_two = list(meet(1, *swap_all(product)))
    tri_two = products(
        "incoming_product", functools.partial(tri_product_kernel, True), [product_two], tri_shape
    )
    tri_two = by_hidden(swap_all(tri_two))
    between(1, None)
    (tri_two,) = meet(2, *tri_two)
    cotangent = cotangent.reshape(rows, parts, cores, parts, -1, width).transpose(3, 2, 1, 4, 0, 5)
    cotangent = send(cotangent.reshape(flip_shape), group)
    state_two, bias = run_rows(
        tri_last_kernel, "incoming_out_starting_bias", steps,
        [
            (state_one, 0), (tri_two, 1), (tri_cols(INCOMING), None),
            (turned((INCOMING, PROJ_OUT)), None), (turned((INCOMING, GATE_OUT)), None),
            (cols(STARTING), None), (weights[(STARTING, BIAS_T)], None),
        ],
        [(state_shape, F32, 0), ((TA_HEADS, rows, length), BF16, 1)], [tri_scratch, head_scratch],
    )
    bias_one = lax.all_gather(bias, group, axis=0, tiled=False)
    flipped, totals_one, mixed_one = run_rows(
        starting_kernel, "starting_attention", steps,
        [
            (alive, None), (state_two, 0), (bias_one, None), (cols(STARTING), None),
            (turned((STARTING, QKVG)), None), (turned((STARTING, OUTPUT)), None),
        ],
        [(flip_shape, BF16, 2)] + attend_saves, [table, flip_scratch], 21,
    )
    state_three = Both([send(flipped, group)])
    cotangent = send(cotangent.reshape((parts, cores) + flip_shape[1:]), "z").reshape(flip_shape)
    (bias,) = run_rows(
        flipped_bias_kernel, "ending_bias", steps,
        [(state_three, 1), (cols(ENDING), None), (weights[(ENDING, BIAS_T)], None)],
        [((TA_HEADS, rows, length), BF16, 1)], [head_scratch],
    )
    bias_two = lax.all_gather(bias, group, axis=0, tiled=False)
    state_four, totals_two, mixed_two = run_rows(
        ending_kernel, "ending_attention", steps,
        [
            (alive, None), (state_three, 1), (bias_two, None), (cols(ENDING), None),
            (turned((ENDING, QKVG)), None), (turned((ENDING, OUTPUT)), None),
        ],
        [(state_shape, F32, 0)] + attend_saves, [table],
    )
    pair_cols, attend_cols = cols(PAIR), cols(ATTEND)
    state_five, pair_out, single_bias = run_rows(
        functools.partial(transition_kernel, order_back), "pair_transition", steps,
        [
            (state_four, 0), (pair_cols, None), (turned((PAIR, UP)), None), (turned((PAIR, DOWN)), None),
            (attend_cols, None), (turned((ATTEND, PAIR_PROJ)), None),
        ],
        [(state_shape, F32, 0), ((length, rows, width), BF16, 1), ((devices, rows, SA_HEADS * rows), BF16, 1)],
        [flip_scratch, ((SA_HEADS, block, length), F32)],
    )
    single_sent = send(middle(send(single_bias, group)), group)
    between(2, single_sent)
    pair_out = send(pair_out.reshape((parts, -1) + pair_out.shape[1:]), "z")
    grads = {}
    grad_four, grads[(PAIR, UP)], grads[(PAIR, DOWN)], grads[(ATTEND, PAIR_PROJ)], vecs = run_rows(
        functools.partial(transition_back_kernel, read_last), "pair_transition_back", steps,
        [
            (state_four, 0), (state_five, 0), (cotangent, 1), (single_sent, 1),
            (pair_cols, None), (turned((PAIR, UP)), None), (weights[(PAIR, UP)], None),
            (weights[(PAIR, DOWN)], None), (attend_cols, None), (weights[(ATTEND, PAIR_PROJ)], None),
        ],
        [
            (state_shape, F32, 0), (weights[(PAIR, UP)].shape, F32, None),
            (weights[(PAIR, DOWN)].shape, F32, None), (weights[(ATTEND, PAIR_PROJ)].shape, F32, None),
            ((8, width), F32, None),
        ],
        [wide, wide, wide, wide, ((SA_HEADS, block, length), F32)], 30,
    )
    grads[(PAIR, VECTORS)] = vecs

    def attention_back(prefix, read, read_grad, source, source_axis, grad, grad_axis, bias, totals, mixed):
        lowered_grad, bias_grad, grads[(prefix, QKVG)], grads[(prefix, OUTPUT)] = run_rows(
            functools.partial(attention_back_kernel, read, read_grad),
            "attention_back", steps,
            [
                (alive, None), (source, source_axis), (grad, grad_axis), (bias, None), (totals, 0),
                (mixed, 0), (cols(prefix), None), (turned((prefix, QKVG)), None),
                (weights[(prefix, QKVG)], None), (weights[(prefix, OUTPUT)], None),
            ],
            [
                (state_shape, BF16, 0), ((devices, TA_HEADS, rows, length), BF16, None),
                (weights[(prefix, QKVG)].shape, F32, None), (weights[(prefix, OUTPUT)].shape, F32, None),
            ],
            [table, table], 34,
        )
        return lowered_grad, send(bias_grad, group)

    lowered_grad, bias_grad = attention_back(
        ENDING, read_flipped, read_plain, state_three, 1, grad_four, 0, bias_two, totals_two, mixed_two
    )
    flipped, bias_w_grad, vecs = run_rows(
        ending_end_kernel, "ending_attention_end", steps,
        [
            (state_three, 1), (grad_four, 0), (lowered_grad, 0), (bias_grad, 2), (cols(ENDING), None),
            (weights[(ENDING, BIAS_W)], None),
        ],
        [(flip_shape, BF16, 2), ((width, 8), F32, None), ((8, width), F32, None)],
        [wide, wide, head_scratch, flip_scratch],
    )
    grads[(ENDING, BIAS_PROJ)], grads[(ENDING, VECTORS)] = bias_w_grad, vecs
    flipped, held = after(flipped, grads[(ATTEND, PAIR_PROJ)])
    grads[(ATTEND, PAIR_PROJ)] = held
    grad_three = send(flipped, group)
    between(4, grads)
    grad_three = Both(meet(3, grad_three))
    pair_out = send(pair_out.reshape(flip_shape), group)
    pair_out = pair_out.reshape(parts, cores, rows, parts, -1, width).transpose(2, 3, 1, 0, 4, 5)
    pair_out = pair_out.reshape(rows, length, width)
    lowered_grad, bias_grad = attention_back(
        STARTING, read_plain, read_flipped, state_two, 0, grad_three, 1, bias_one, totals_one, mixed_one
    )
    square = weights[(INCOMING, GATE_OUT)].shape
    (
        grad_two, grad_tri, gate_back, bias_w_grad, grads[(INCOMING, PROJ_OUT)], grads[(INCOMING, GATE_OUT)], vecs,
    ) = run_halves(
        starting_end_kernel, "starting_end_incoming_out_back", steps,
        [
            (state_two, 0), (grad_three, 1), (lowered_grad, 0), (bias_grad, 2), (cols(STARTING), None),
            (weights[(STARTING, BIAS_W)], None), (state_one, 0), (tri_two, 1), (tri_cols(INCOMING), None),
            (turned((INCOMING, PROJ_OUT)), None), (turned((INCOMING, GATE_OUT)), None),
            (weights[(INCOMING, PROJ_OUT)], None), (weights[(INCOMING, GATE_OUT)], None),
        ],
        [
            (state_shape, F32, 0), ((hidden, half, length), BF16, 1), (state_shape, BF16, 0),
            ((width, 8), F32, None), (square, F32, None), (square, F32, None), ((8, width), F32, None),
        ],
        [wide, wide, wide, wide, head_scratch, tri_scratch], 26,
    )
    grads[(STARTING, BIAS_PROJ)], grads[(STARTING, VECTORS)] = bias_w_grad, vecs
    grad_tri = swap_all(by_device(grad_tri))
    product_grad = products(
        "incoming_product_back", functools.partial(tri_product_back_kernel, True),
        [grad_tri, product_two], product_half,
    )
    product_grad = swap_all(product_grad)
    product_grad = [*meet(4, product_grad[0]), product_grad[1]]
    (
        grad_one, grad_tri, gate_back, grads[(INCOMING, PROJ_GATE)], grads[(OUTGOING, PROJ_OUT)],
        grads[(OUTGOING, GATE_OUT)], vecs,
    ) = run_halves(
        functools.partial(tri_join_back_kernel, read_first), "incoming_in_outgoing_out_back", steps,
        [
            ([info[:half], info[half:]], "smem"), (alive, None), (state_one, 0), (product_grad, 3), (gate_back, 0), (grad_two, 0),
            (tri_cols(INCOMING), None), (turned((INCOMING, PROJ_GATE)), None),
            (weights[(INCOMING, PROJ_GATE)], None), (pair, 0), (tri_one, 1), (tri_cols(OUTGOING), None),
            (turned((OUTGOING, PROJ_OUT)), None), (turned((OUTGOING, GATE_OUT)), None),
            (weights[(OUTGOING, PROJ_OUT)], None), (weights[(OUTGOING, GATE_OUT)], None),
        ],
        [
            (state_shape, F32, 0), ((hidden, half, length), BF16, 1), (state_shape, BF16, 0),
            (weights[(INCOMING, PROJ_GATE)].shape, F32, None), (square, F32, None), (square, F32, None),
            ((8, width), F32, None),
        ],
        [wide, wide, wide, wide, product_scratch, tri_scratch], 37,
    )
    grads[(INCOMING, VECTORS)] = vecs
    between(5, grads)
    grad_tri = swap_all(by_device(grad_tri))
    grad_tri = [grad_tri[0], *meet(5, grad_tri[1])]
    product_grad = products(
        "outgoing_product_back", functools.partial(tri_product_back_kernel, False),
        [grad_tri, product_one], product_shape,
    )
    (product_grad,) = swap_all(product_grad)
    between(6, grads)
    pair_grad, grads[(OUTGOING, PROJ_GATE)], vecs = run_rows(
        functools.partial(tri_first_back_kernel, read_first, order_back), "outgoing_in_back", steps,
        [
            (info, "smem"), (alive, None), (pair, 0), (product_grad, 3), (gate_back, 0), (grad_one, 0),
            (tri_cols(OUTGOING), None), (turned((OUTGOING, PROJ_GATE)), None),
            (weights[(OUTGOING, PROJ_GATE)], None),
        ],
        [
            ((rows, length, width), BF16, 0), (weights[(OUTGOING, PROJ_GATE)].shape, F32, None),
            ((8, width), F32, None),
        ],
        [wide, wide, product_scratch], 20,
    )
    grads[(OUTGOING, VECTORS)] = vecs
    return pair_out, pair_grad, grads


HELD = {
    (PAIR, VECTORS): ((PAIR, NORM_GAIN), (PAIR, NORM_BIAS), (ATTEND, PAIR_GAIN), (ATTEND, PAIR_BIAS)),
    (ENDING, VECTORS): ((ENDING, NORM_GAIN), (ENDING, NORM_BIAS)),
    (STARTING, VECTORS): (
        (STARTING, NORM_GAIN), (STARTING, NORM_BIAS), (INCOMING, OUT_GAIN), (INCOMING, OUT_BIAS)
    ),
    (INCOMING, VECTORS): (
        (INCOMING, NORM_GAIN), (INCOMING, NORM_BIAS), (OUTGOING, OUT_GAIN), (OUTGOING, OUT_BIAS)
    ),
    (OUTGOING, VECTORS): ((OUTGOING, NORM_GAIN), (OUTGOING, NORM_BIAS)),
}


def vector_part(grads, table, name, first, last):
    pairs = [
        (row, held) for row, held in enumerate(HELD[name]) if first <= table[held][0] < last
    ]
    return (pairs, grads[name])


def fast_shards(parts, cores, pair, single, lengths, params, moment_one, moment_two, pair_cotangent, single_cotangent):
    entries = layout(C, H, S, TA_HEADS, SA_HEADS)
    table, total = table_of(entries)
    count = total // STRIDE
    shard_size = params.shape[0]
    attend = table[(ATTEND, NORM_GAIN)][0]
    pair_lanes = -(-attend * STRIDE // count)
    single_lane = attend * STRIDE // count
    devices = parts * cores
    line, group = ("z", "core"), ("crop", "core")
    row_index = lax.axis_index(line)
    odd = ((row_index * shard_size) % STRIDE) // (STRIDE // 2)
    place = jnp.stack([odd, odd]).astype(jnp.int32)
    shard_rows = jnp.pad(params, (0, RUN * STRIDE * STRIDE - shard_size)).reshape(-1, STRIDE)
    (runs,) = whole_call(
        runs_kernel, "parameter_runs", [(place, "smem"), (shard_rows, None)],
        [((STRIDE, RUN, STRIDE), BF16)], [((STRIDE, RUN, STRIDE), F32)],
    )
    rows, length, width = pair.shape[1:]
    send = in_turn()
    pair_in = send(pair[0].reshape(parts, -1, length, width), "crop")
    first_runs = lax.all_gather(runs[:pair_lanes], line)
    pair_in, _, lengths = after(pair_in, runs, lengths)
    live = lax.all_gather(jnp.broadcast_to(lengths.astype(F32), (8, STRIDE)), "crop")
    pair_in = send(pair_in, "z").reshape(rows, length, width)
    weights = unpack_pair(table, total, first_runs)
    size = rows // parts
    blocks = np.arange(length // size).reshape(parts, cores, parts)
    order = blocks.transpose(2, 1, 0).reshape(-1)
    orders = (order.tolist(), np.argsort(order).tolist())
    tokens = (order[:, None] * size + np.arange(size)).reshape(-1)
    live = live[lax.axis_index("z"), 0, 0]
    width = single.shape[2]
    mask = (tokens.astype(np.float32) < live).astype(F32)
    info = lax.dynamic_slice_in_dim(mask, lax.axis_index(group) * rows, rows).astype(jnp.int32)
    alive = jnp.broadcast_to(mask, (8, length))
    held = {}
    single_grads = {}

    def middle(bias):
        found = single_middle(held["state"], held["back"], held["projected"], bias, alive, weights)
        held["out"], held["grad"], grad_scores, grads, held["pending"] = found
        single_grads.update(grads)
        return grad_scores

    def meet(number, *values):
        if number == 0:
            others = [held["runs"]]
        elif number == 1:
            others = [weights[(SINGLE, UP)], held["state"]]
        elif number == 2:
            others = [held["projected"][1]]
        elif number == 3:
            others = [reduced[3]]
        elif number == 4:
            values, reduced[2] = after(*values, reduced[2])
            return [values]
        else:
            values, held["both"], reduced[1] = after(*values, held["both"], reduced[1])
            return [values]
        return after(*values, *others)[: len(values)]

    def reduce_runs(sent):
        return jnp.sum(send(sent, line).astype(F32), axis=0).astype(BF16)

    reduced = {}
    lines_held = list(enumerate(SINGLE_VECTORS))
    late_lanes = -(-table[(OUTGOING, OUT_GAIN)][0] * STRIDE // count)
    late_end = table[(OUTGOING, GATE_OUT)][0]
    early = table[(OUTGOING, PROJ_OUT)][0]

    def lines():
        values = jnp.concatenate([single_grads[name].reshape(1, S) for name in SINGLE_VECTORS], axis=0)
        return jnp.pad(values, ((0, 8 - len(SINGLE_VECTORS)), (0, 0)))

    def between(number, grads):
        if number == 0:
            last_runs = after(runs[single_lane:], pair_in, weights[(OUTGOING, COLS)], live)[0]
            held["runs"] = lax.all_gather(last_runs, line)
            weights.update(unpack_single(table, total, single_lane, held["runs"]))
            for index, name in enumerate(SINGLE_VECTORS):
                weights[name] = weights[(SINGLE, VECTORS)][index]
            both = jnp.concatenate([single[0], single_cotangent[0]], axis=1)
            both = lax.all_gather(both, ("crop",) + line)
            both = both.reshape(parts, parts, cores, parts, -1, 2 * width)
            here = lax.axis_index("z"), lax.axis_index("core"), lax.axis_index("crop")
            both = both[here[0], :, here[1], here[2]].reshape(rows, 2 * width).astype(F32)
            held["state"], held["back"] = both[:, :width], both[:, width:]
            return
        if number == 1:
            lowered, qkvg, both = single_project(held["state"], weights, devices)
            held["projected"] = lowered, qkvg, send(both, group)
            return
        if number == 2:
            parts_held = grads[:, :, SA_HEADS * rows :]
            grad = held["grad"] + single_attend_end(held["pending"], parts_held, weights, single_grads)
            both = jnp.concatenate([held["out"], grad], axis=1).astype(BF16)
            held["both"] = lax.all_gather(both, ("crop",) + line)
            return
        if number == 6:
            reduced[1] = reduce_runs(reduced[1])
            return
        if number == 4:
            sent = pack(
                "single_gradient", table, total, devices, (pair_lanes, STRIDE), attend,
                [(name, single_grads[name]) for name in SINGLE_MATRICES]
                + [((ATTEND, PAIR_PROJ), grads[(ATTEND, PAIR_PROJ)])]
                + [vector_part(grads, table, (PAIR, VECTORS), attend, total), (lines_held, lines())],
            )
            reduced[3] = sent
            sent = sent.reshape((devices * parts, -1) + sent.shape[2:])
            reduced[2] = lax.psum_scatter(sent, line + ("crop",), scatter_dimension=0, tiled=False)
            return
        taken = -(-(pair_lanes * count - (attend + 2 * S // STRIDE) * STRIDE) // (4 * S))
        sent = pack(
            "pair_gradient", table, total, devices, (late_lanes, pair_lanes), early,
            [(name, grads[name]) for name in PAIR_MATRICES if table[name][0] >= early]
            + [(name, grads[name]) for name in ((STARTING, BIAS_PROJ), (ENDING, BIAS_PROJ))]
            + [vector_part(grads, table, name, early, attend) for name in HELD if name in grads]
            + [(lines_held[:2], lines()), ((ATTEND, QKVG), single_grads[(ATTEND, QKVG)][: -(-taken // 8) * 8])],
        )
        reduced[1] = sent

    pair_out, pair_grad, grads = pair_path(
        pair_in, info, alive, orders, weights, pair_cotangent[0], middle, between, meet, send, group, parts
    )
    sent = pack(
        "outgoing_gradient", table, total, devices, (0, late_lanes), 0,
        [(name, grads[name]) for name in PAIR_MATRICES if table[name][0] < late_end]
        + [vector_part(grads, table, name, 0, late_end) for name in ((OUTGOING, VECTORS), (INCOMING, VECTORS))],
    )
    reduced[0] = reduce_runs(sent)
    pair_grad = send(pair_grad.reshape(parts, -1, length, pair_grad.shape[2]), "z")
    pair_grad, held["z"] = send(pair_grad, "crop").reshape(rows, length, -1).astype(F32), pair_grad
    both = held["both"].reshape(parts, parts, cores, parts, -1, 2 * width)
    both = both[:, lax.axis_index("crop"), lax.axis_index("core"), lax.axis_index("z")]
    both = both.reshape(rows, 2 * width)
    single_out, single_grad = both[:, :width], both[:, width:].astype(F32)
    summed = lax.all_gather(jnp.concatenate([reduced[0], reduced[1]], axis=0), "crop")
    others = lax.all_gather(reduced[2], "crop")
    shard, squares = whole_call(
        functools.partial(shard_kernel, shard_size), "gradient_share",
        [(place, "smem"), (summed, None), (others, None)],
        [((RUN * STRIDE, STRIDE), F32), ((8, STRIDE), F32)], [((STRIDE, RUN, STRIDE), F32)],
    )
    shard = shard.reshape(-1)[:shard_size]
    squares = after(squares, held["z"])[0]
    clip_norm = jnp.sqrt(jnp.sum(lax.all_gather(squares, line)))
    clipped = shard * (CLIP / jnp.maximum(clip_norm, CLIP))
    new_first = BETA_ONE * moment_one + (1.0 - BETA_ONE) * clipped
    new_second = BETA_TWO * moment_two + (1.0 - BETA_TWO) * clipped * clipped
    rates, decays = rate_tables(entries)
    rate_shard = lax.dynamic_slice_in_dim(jnp.asarray(rates), row_index * shard_size, shard_size)
    decay_shard = lax.dynamic_slice_in_dim(jnp.asarray(decays), row_index * shard_size, shard_size)
    first_hat = new_first / (1.0 - BETA_ONE**STEP)
    second_hat = new_second / (1.0 - BETA_TWO**STEP)
    new_params = params - rate_shard * (
        first_hat / (jnp.sqrt(second_hat) + ADAM_EPS) + decay_shard * params
    )
    return (
        pair_out[None],
        single_out[None],
        pair_grad[None],
        single_grad[None],
        new_params,
        new_first,
        new_second,
        clip_norm,
    )


def solution(mesh):
    crops, devices = mesh.devices.shape
    table, total = table_of(layout(C, H, S, TA_HEADS, SA_HEADS))
    count = total // STRIDE
    lanes = STRIDE + -table[(ATTEND, NORM_GAIN)][0] * STRIDE // count
    fast = devices == 2 * crops and LENGTH % (devices * 16) == 0 and count // devices + 2 <= RUN * STRIDE and lanes % crops == 0
    row = "row"
    if fast:
        mesh = jax.sharding.Mesh(mesh.devices.reshape(crops, crops, 2), ("crop", "z", "core"))
        row = ("z", "core")
    split = [P("crop", row, None, None), P("crop", row, None), P("crop"), P(row)]
    pair, single, lengths, share = split
    return jax.shard_map(
        functools.partial(fast_shards, crops, 2) if fast else shards,
        mesh=mesh,
        in_specs=(pair, single, lengths, share, share, share, pair, single),
        out_specs=(pair, single, pair, single, share, share, share, P()),
        check_vma=False,
    )
```

```python
import functools
import math

import jax
import jax.numpy as jnp
import numpy as np
from jax import lax
from jax.experimental import pallas as pl
from jax.experimental.pallas import tpu as pltpu
from jax.sharding import PartitionSpec as P

C = 128
H = 128
S = 384
TA_HEADS = 4
SA_HEADS = 16
STEP = 10
STRIDE = 128
LENGTH = 256

OUTGOING, INCOMING, STARTING, ENDING, PAIR, ATTEND, SINGLE = range(7)
(
    NORM_GAIN,
    NORM_BIAS,
    PROJ_GATE,
    OUT_GAIN,
    OUT_BIAS,
    PROJ_OUT,
    GATE_OUT,
    QKVG,
    BIAS_PROJ,
    OUTPUT,
    UP,
    DOWN,
    PAIR_GAIN,
    PAIR_BIAS,
    PAIR_PROJ,
    COLS,
    BIAS_W,
    BIAS_T,
    VECTORS,
    T,
) = range(7, 27)


EPSILON = 1e-05
MASKED = 1000000000.0
BETA_ONE = 0.9
BETA_TWO = 0.95
ADAM_EPS = 1e-08
CLIP = 1.0


def layout(pair_width, hidden_width, single_width, tri_heads, att_heads):
    entries = []
    for prefix in (OUTGOING, INCOMING):
        entries += [
            ((prefix, NORM_GAIN), (pair_width,)),
            ((prefix, NORM_BIAS), (pair_width,)),
            ((prefix, PROJ_GATE), (pair_width, 4 * hidden_width)),
            ((prefix, OUT_GAIN), (hidden_width,)),
            ((prefix, OUT_BIAS), (hidden_width,)),
            ((prefix, PROJ_OUT), (hidden_width, pair_width)),
            ((prefix, GATE_OUT), (pair_width, pair_width)),
        ]
    for prefix in (STARTING, ENDING):
        entries += [
            ((prefix, NORM_GAIN), (pair_width,)),
            ((prefix, NORM_BIAS), (pair_width,)),
            ((prefix, QKVG), (pair_width, 4 * pair_width)),
            ((prefix, BIAS_PROJ), (pair_width, tri_heads)),
            ((prefix, OUTPUT), (pair_width, pair_width)),
        ]
    entries += [
        ((PAIR, NORM_GAIN), (pair_width,)),
        ((PAIR, NORM_BIAS), (pair_width,)),
        ((PAIR, UP), (pair_width, 8 * pair_width)),
        ((PAIR, DOWN), (4 * pair_width, pair_width)),
        ((ATTEND, NORM_GAIN), (single_width,)),
        ((ATTEND, NORM_BIAS), (single_width,)),
        ((ATTEND, QKVG), (single_width, 4 * single_width)),
        ((ATTEND, PAIR_GAIN), (pair_width,)),
        ((ATTEND, PAIR_BIAS), (pair_width,)),
        ((ATTEND, PAIR_PROJ), (pair_width, att_heads)),
        ((ATTEND, OUTPUT), (single_width, single_width)),
        ((SINGLE, NORM_GAIN), (single_width,)),
        ((SINGLE, NORM_BIAS), (single_width,)),
        ((SINGLE, UP), (single_width, 8 * single_width)),
        ((SINGLE, DOWN), (4 * single_width, single_width)),
    ]
    return entries


def logical_order(flat):
    return flat.reshape(-1, STRIDE).T.reshape(-1)


def stored_order(vector):
    return vector.reshape(STRIDE, -1).T.reshape(-1)


def rate_tables(entries):
    rates = []
    decays = []
    for name, shape in entries:
        count = math.prod(shape)
        if len(shape) == 1:
            rates.append(np.full(count, 0.5, np.float32))
            decays.append(np.zeros(count, np.float32))
        else:
            rates.append(np.full(count, 2.0 / math.sqrt(shape[0]), np.float32))
            decays.append(np.full(count, 0.01, np.float32))
    rates = np.concatenate(rates)
    decays = np.concatenate(decays)
    return (rates.reshape(STRIDE, -1).T.reshape(-1), decays.reshape(STRIDE, -1).T.reshape(-1))


def unpack(flat, entries):
    pieces = {}
    offset = 0
    for name, shape in entries:
        count = math.prod(shape)
        pieces[name] = flat[offset : offset + count].reshape(shape)
        offset += count
    return pieces


def layer_norm(values, gain, shift):
    centred = values - jnp.mean(values, axis=-1, keepdims=True)
    spread = jnp.mean(centred * centred, axis=-1, keepdims=True)
    return centred * lax.rsqrt(spread + EPSILON) * gain + shift


def norm_backward(values, gain, shift, grad):
    _, pullback = jax.vjp(layer_norm, values, gain, shift)
    return pullback(grad)


def norm_pair(weights, prefix):
    return (
        weights[(prefix, NORM_GAIN)].astype(jnp.float32),
        weights[(prefix, NORM_BIAS)].astype(jnp.float32),
    )


def gated_pair(project, pair_mask):
    half = project.shape[-1] // 2
    return project[..., :half] * jax.nn.sigmoid(project[..., half:]) * pair_mask[..., None]


def gated_output(values, gate):
    return values * jax.nn.sigmoid(gate)


def swiglu(hidden):
    half = hidden.shape[-1] // 2
    return jax.nn.silu(hidden[..., :half]) * hidden[..., half:]


def matmul(left, right):
    return jnp.dot(left, right, preferred_element_type=jnp.float32)


def outer_sum(left, right):
    return jnp.einsum(
        "nc,nd->cd",
        left.reshape(-1, left.shape[-1]),
        right.reshape(-1, right.shape[-1]),
        preferred_element_type=jnp.float32,
    )


def flip(values):
    moved = lax.all_to_all(values, "row", split_axis=1, concat_axis=0, tiled=True)
    return jnp.swapaxes(moved, 0, 1)


def channel_forward(first, second, incoming):
    whole_first, whole_second = (
        lax.all_to_all(first, "row", split_axis=2, concat_axis=0, tiled=True),
        lax.all_to_all(second, "row", split_axis=2, concat_axis=0, tiled=True),
    )
    if incoming:
        local_tri = jnp.einsum(
            "kih,kjh->ijh", whole_first, whole_second, preferred_element_type=jnp.float32
        )
        local_tri = local_tri.astype(jnp.bfloat16).astype(jnp.float32)
    else:
        local_tri = jnp.einsum(
            "ikh,jkh->ijh", whole_first, whole_second, preferred_element_type=jnp.float32
        )
    tri = lax.all_to_all(
        local_tri.astype(jnp.bfloat16), "row", split_axis=0, concat_axis=2, tiled=True
    ).astype(local_tri.dtype)
    return (tri, whole_first, whole_second)


def channel_backward(grad_tri, whole_first, whole_second, incoming):
    whole_grad = lax.all_to_all(grad_tri, "row", split_axis=2, concat_axis=0, tiled=True)
    if incoming:
        grad_a = jnp.einsum(
            "ijh,kjh->kih", whole_grad, whole_second, preferred_element_type=jnp.float32
        )
        grad_b = jnp.einsum(
            "ijh,kih->kjh", whole_grad, whole_first, preferred_element_type=jnp.float32
        )
    else:
        grad_a = jnp.einsum(
            "ijh,jkh->ikh", whole_grad, whole_second, preferred_element_type=jnp.float32
        )
        grad_b = jnp.einsum(
            "ijh,ikh->jkh", whole_grad, whole_first, preferred_element_type=jnp.float32
        )
    return (
        lax.all_to_all(
            grad_a.astype(jnp.bfloat16), "row", split_axis=0, concat_axis=2, tiled=True
        ).astype(grad_a.dtype),
        lax.all_to_all(
            grad_b.astype(jnp.bfloat16), "row", split_axis=0, concat_axis=2, tiled=True
        ).astype(grad_b.dtype),
    )


def triangle_forward(state, pair_mask, weights, prefix, incoming):
    gain, shift = norm_pair(weights, prefix)
    lowered = layer_norm(state, gain, shift).astype(jnp.bfloat16)
    project = matmul(lowered, weights[(prefix, PROJ_GATE)])
    product = gated_pair(project, pair_mask).astype(jnp.bfloat16)
    half = product.shape[-1] // 2
    tri, own, other = channel_forward(product[..., :half], product[..., half:], incoming)
    out_gain = weights[(prefix, OUT_GAIN)].astype(jnp.float32)
    out_shift = weights[(prefix, OUT_BIAS)].astype(jnp.float32)
    out_low = layer_norm(tri, out_gain, out_shift).astype(jnp.bfloat16)
    output = matmul(out_low, weights[(prefix, PROJ_OUT)])
    gate_out = matmul(lowered, weights[(prefix, GATE_OUT)])
    update = gated_output(output, gate_out)
    return (update, (state, lowered, lowered, project, own, other, tri, out_low, output, gate_out))


def triangle_backward(saved, grad_update, pair_mask, weights, prefix, incoming, grads):
    state, lowered, framed, project, own, other, tri, out_low, output, gate_out = saved
    _, pullback = jax.vjp(gated_output, output, gate_out)
    grad_output, grad_gate = pullback(grad_update)
    grad_output = grad_output.astype(jnp.bfloat16)
    grad_gate = grad_gate.astype(jnp.bfloat16)
    grads[(prefix, PROJ_OUT)] = outer_sum(out_low, grad_output)
    grads[(prefix, GATE_OUT)] = outer_sum(lowered, grad_gate)
    grad_normed = matmul(grad_output, weights[(prefix, PROJ_OUT)].T)
    out_gain = weights[(prefix, OUT_GAIN)].astype(jnp.float32)
    out_shift = weights[(prefix, OUT_BIAS)].astype(jnp.float32)
    grad_tri, grads[(prefix, OUT_GAIN)], grads[(prefix, OUT_BIAS)] = norm_backward(
        tri, out_gain, out_shift, grad_normed
    )
    grad_tri = grad_tri.astype(jnp.bfloat16)
    grad_first, grad_second = channel_backward(grad_tri, own, other, incoming)
    _, pullback = jax.vjp(lambda values: gated_pair(values, pair_mask), project)
    (grad_project,) = pullback(jnp.concatenate([grad_first, grad_second], axis=-1))
    grad_project = grad_project.astype(jnp.bfloat16)
    grads[(prefix, PROJ_GATE)] = outer_sum(framed, grad_project)
    grad_framed = matmul(grad_project, weights[(prefix, PROJ_GATE)].T)
    if incoming:
        grad_framed = grad_framed.astype(jnp.bfloat16).astype(jnp.float32)
    grad_lowered = grad_framed + matmul(grad_gate, weights[(prefix, GATE_OUT)].T)
    gain, shift = norm_pair(weights, prefix)
    grad_state, grads[(prefix, NORM_GAIN)], grads[(prefix, NORM_BIAS)] = norm_backward(
        state, gain, shift, grad_lowered
    )
    return grad_state


def row_scores(query, key, bias, penalty, scale):
    scores = jnp.einsum("jhd,khd->hjk", query, key, preferred_element_type=jnp.float32) * scale
    return scores + bias.astype(jnp.float32) + penalty[None, None, :]


def attention_forward(state, penalty, weights, prefix, ending):
    gain, shift = norm_pair(weights, prefix)
    lowered = layer_norm(state, gain, shift).astype(jnp.bfloat16)
    framed = flip(lowered) if ending else lowered
    rows, length, width = framed.shape
    size = width // TA_HEADS
    scale = size ** (-0.5)
    qkvg = matmul(framed, weights[(prefix, QKVG)])
    queries = qkvg[..., :width].astype(jnp.bfloat16).reshape(rows, length, TA_HEADS, size)
    keys = qkvg[..., width : 2 * width].astype(jnp.bfloat16).reshape(rows, length, TA_HEADS, size)
    values = (
        qkvg[..., 2 * width : 3 * width].astype(jnp.bfloat16).reshape(rows, length, TA_HEADS, size)
    )
    gate = qkvg[..., 3 * width :]
    local_bias = (
        matmul(framed, weights[(prefix, BIAS_PROJ)]).astype(jnp.bfloat16).transpose(2, 0, 1)
    )
    bias = lax.all_gather(local_bias, "row", axis=1, tiled=True)

    def forward_row(items):
        query, key, value = items
        scores = row_scores(query, key, bias, penalty, scale)
        top = jnp.max(scores, axis=-1, keepdims=True)
        shifted = jnp.exp(scores - top)
        total = jnp.sum(shifted, axis=-1, keepdims=True)
        probs = (shifted / total).astype(jnp.bfloat16)
        mixed = jnp.einsum("hjk,khd->jhd", probs, value, preferred_element_type=jnp.float32)
        return (mixed, top[..., 0] + jnp.log(total[..., 0]))

    mixed, log_totals = lax.map(forward_row, (queries, keys, values))
    mixed = mixed.reshape(rows, length, width)
    gated_low = gated_output(mixed, gate).astype(jnp.bfloat16)
    returned = flip(gated_low) if ending else gated_low
    update = matmul(returned, weights[(prefix, OUTPUT)])
    return (update, (state, framed, queries, keys, values, gate, bias, mixed, log_totals, returned))


def attention_backward(saved, grad_update, penalty, weights, prefix, ending, grads):
    state, framed, queries, keys, values, gate, bias, mixed, log_totals, returned = saved
    rows, length, width = framed.shape
    size = width // TA_HEADS
    scale = size ** (-0.5)
    grad_low = grad_update.astype(jnp.bfloat16)
    grads[(prefix, OUTPUT)] = outer_sum(returned, grad_low)
    grad_gated = matmul(grad_low, weights[(prefix, OUTPUT)].T)
    if ending:
        grad_gated = flip(grad_gated.astype(jnp.bfloat16)).astype(jnp.float32)
    _, pullback = jax.vjp(gated_output, mixed, gate)
    grad_mixed, grad_gate = pullback(grad_gated)
    grad_mixed = grad_mixed.astype(jnp.bfloat16).reshape(rows, length, TA_HEADS, size)

    def back_row(carry, items):
        query, key, value, log_total, grad_row = items
        scores = row_scores(query, key, bias, penalty, scale)
        probs = jnp.exp(scores - log_total[..., None])
        grad_probs = jnp.einsum("jhd,khd->hjk", grad_row, value, preferred_element_type=jnp.float32)
        delta = jnp.sum(probs * grad_probs, axis=-1, keepdims=True)
        grad_scores = (probs * (grad_probs - delta)).astype(jnp.bfloat16)
        grad_query = (
            jnp.einsum("hjk,khd->jhd", grad_scores, key, preferred_element_type=jnp.float32) * scale
        )
        grad_key = (
            jnp.einsum("hjk,jhd->khd", grad_scores, query, preferred_element_type=jnp.float32)
            * scale
        )
        grad_value = jnp.einsum(
            "hjk,jhd->khd", probs.astype(jnp.bfloat16), grad_row, preferred_element_type=jnp.float32
        )
        return (carry + grad_scores.astype(jnp.float32), (grad_query, grad_key, grad_value))

    empty = jnp.zeros(bias.shape, jnp.float32)
    grad_bias, (grad_query, grad_key, grad_value) = lax.scan(
        back_row, empty, (queries, keys, values, log_totals, grad_mixed)
    )
    grad_bias = lax.psum_scatter(grad_bias, "row", scatter_dimension=1, tiled=True)
    grad_bias = grad_bias.transpose(1, 2, 0).astype(jnp.bfloat16)
    grad_qkvg = jnp.concatenate(
        [
            grad_query.reshape(rows, length, width),
            grad_key.reshape(rows, length, width),
            grad_value.reshape(rows, length, width),
            grad_gate,
        ],
        axis=-1,
    ).astype(jnp.bfloat16)
    grads[(prefix, QKVG)] = outer_sum(framed, grad_qkvg)
    grads[(prefix, BIAS_PROJ)] = outer_sum(framed, grad_bias)
    grad_framed = matmul(grad_qkvg, weights[(prefix, QKVG)].T) + matmul(
        grad_bias, weights[(prefix, BIAS_PROJ)].T
    )
    if ending:
        grad_framed = flip(grad_framed.astype(jnp.bfloat16)).astype(jnp.float32)
    gain, shift = norm_pair(weights, prefix)
    grad_state, grads[(prefix, NORM_GAIN)], grads[(prefix, NORM_BIAS)] = norm_backward(
        state, gain, shift, grad_framed
    )
    return grad_state


def transition_forward(state, weights, prefix):
    gain, shift = norm_pair(weights, prefix)
    lowered = layer_norm(state, gain, shift).astype(jnp.bfloat16)
    hidden = matmul(lowered, weights[(prefix, UP)])
    mixed_low = swiglu(hidden).astype(jnp.bfloat16)
    update = matmul(mixed_low, weights[(prefix, DOWN)])
    return (update, (state, lowered, hidden, mixed_low))


def transition_backward(saved, grad_update, weights, prefix, grads):
    state, lowered, hidden, mixed_low = saved
    grad_low = grad_update.astype(jnp.bfloat16)
    grads[(prefix, DOWN)] = outer_sum(mixed_low, grad_low)
    grad_mixed = matmul(grad_low, weights[(prefix, DOWN)].T)
    _, pullback = jax.vjp(swiglu, hidden)
    (grad_hidden,) = pullback(grad_mixed)
    grad_hidden = grad_hidden.astype(jnp.bfloat16)
    grads[(prefix, UP)] = outer_sum(lowered, grad_hidden)
    grad_lowered = matmul(grad_hidden, weights[(prefix, UP)].T)
    gain, shift = norm_pair(weights, prefix)
    grad_state, grads[(prefix, NORM_GAIN)], grads[(prefix, NORM_BIAS)] = norm_backward(
        state, gain, shift, grad_lowered
    )
    return grad_state


def single_forward(single_state, pair_state, penalty, weights):
    gain, shift = norm_pair(weights, ATTEND)
    lowered = layer_norm(single_state, gain, shift).astype(jnp.bfloat16)
    rows, width = lowered.shape
    size = width // SA_HEADS
    qkvg = matmul(lowered, weights[(ATTEND, QKVG)])
    query = qkvg[:, :width].astype(jnp.bfloat16).reshape(rows, SA_HEADS, size)
    key = qkvg[:, width : 2 * width].astype(jnp.bfloat16)
    value = qkvg[:, 2 * width : 3 * width].astype(jnp.bfloat16)
    gate = qkvg[:, 3 * width :]
    keys_all, values_all = (
        lax.all_gather(key, "row", axis=0, tiled=True),
        lax.all_gather(value, "row", axis=0, tiled=True),
    )
    keys_all = keys_all.reshape(-1, SA_HEADS, size)
    values_all = values_all.reshape(-1, SA_HEADS, size)
    pair_gain = weights[(ATTEND, PAIR_GAIN)].astype(jnp.float32)
    pair_shift = weights[(ATTEND, PAIR_BIAS)].astype(jnp.float32)
    pair_low = layer_norm(pair_state, pair_gain, pair_shift).astype(jnp.bfloat16)
    bias = matmul(pair_low, weights[(ATTEND, PAIR_PROJ)]).transpose(2, 0, 1)
    scores = jnp.einsum(
        "ihd,jhd->hij", query, keys_all, preferred_element_type=jnp.float32
    ) * size ** (-0.5)
    scores = scores + bias + penalty[None, None, :]
    probs = jax.nn.softmax(scores, axis=-1)
    probs_low = probs.astype(jnp.bfloat16)
    mixed = jnp.einsum(
        "hij,jhd->ihd", probs_low, values_all, preferred_element_type=jnp.float32
    ).reshape(rows, width)
    gated_low = gated_output(mixed, gate).astype(jnp.bfloat16)
    update = matmul(gated_low, weights[(ATTEND, OUTPUT)])
    return (
        update,
        (
            single_state,
            pair_state,
            lowered,
            query,
            keys_all,
            values_all,
            gate,
            pair_low,
            probs,
            probs_low,
            mixed,
            gated_low,
        ),
    )


def single_backward(saved, grad_update, weights, grads):
    (
        single_state,
        pair_state,
        lowered,
        query,
        keys_all,
        values_all,
        gate,
        pair_low,
        probs,
        probs_low,
        mixed,
        gated_low,
    ) = saved
    rows, width = lowered.shape
    size = width // SA_HEADS
    scale = size ** (-0.5)
    grad_low = grad_update.astype(jnp.bfloat16)
    grads[(ATTEND, OUTPUT)] = outer_sum(gated_low, grad_low)
    grad_gated = matmul(grad_low, weights[(ATTEND, OUTPUT)].T)
    _, pullback = jax.vjp(gated_output, mixed, gate)
    grad_mixed, grad_gate = pullback(grad_gated)
    grad_mixed = grad_mixed.astype(jnp.bfloat16).reshape(rows, SA_HEADS, size)
    grad_probs = jnp.einsum(
        "ihd,jhd->hij", grad_mixed, values_all, preferred_element_type=jnp.float32
    )
    delta = jnp.sum(probs * grad_probs, axis=-1, keepdims=True)
    grad_scores = (probs * (grad_probs - delta)).astype(jnp.bfloat16)
    grad_query = (
        jnp.einsum("hij,jhd->ihd", grad_scores, keys_all, preferred_element_type=jnp.float32)
        * scale
    )
    key_part = (
        jnp.einsum("hij,ihd->jhd", grad_scores, query, preferred_element_type=jnp.float32) * scale
    )
    value_part = jnp.einsum(
        "hij,ihd->jhd", probs_low, grad_mixed, preferred_element_type=jnp.float32
    )
    grad_key, grad_value = (
        lax.psum_scatter(key_part.reshape(-1, width), "row", scatter_dimension=0, tiled=True),
        lax.psum_scatter(value_part.reshape(-1, width), "row", scatter_dimension=0, tiled=True),
    )
    grad_qkvg = jnp.concatenate(
        [grad_query.reshape(rows, width), grad_key, grad_value, grad_gate], axis=-1
    ).astype(jnp.bfloat16)
    grads[(ATTEND, QKVG)] = outer_sum(lowered, grad_qkvg)
    grad_lowered = matmul(grad_qkvg, weights[(ATTEND, QKVG)].T)
    gain, shift = norm_pair(weights, ATTEND)
    grad_single, grads[(ATTEND, NORM_GAIN)], grads[(ATTEND, NORM_BIAS)] = norm_backward(
        single_state, gain, shift, grad_lowered
    )
    grad_bias = grad_scores.transpose(1, 2, 0)
    grads[(ATTEND, PAIR_PROJ)] = outer_sum(pair_low, grad_bias)
    grad_pair_low = matmul(grad_bias, weights[(ATTEND, PAIR_PROJ)].T)
    pair_gain = weights[(ATTEND, PAIR_GAIN)].astype(jnp.float32)
    pair_shift = weights[(ATTEND, PAIR_BIAS)].astype(jnp.float32)
    grad_pair, grads[(ATTEND, PAIR_GAIN)], grads[(ATTEND, PAIR_BIAS)] = norm_backward(
        pair_state, pair_gain, pair_shift, grad_pair_low
    )
    return (grad_single, grad_pair)


def shards(pair, single, lengths, params, moment_one, moment_two, pair_cotangent, single_cotangent):
    entries = layout(C, H, S, TA_HEADS, SA_HEADS)
    full = lax.all_gather(params.astype(jnp.bfloat16), "row", axis=0, tiled=True)
    weights = unpack(logical_order(full), entries)
    rows = pair.shape[1]
    length = pair.shape[2]
    first_row = lax.axis_index("row") * rows
    mask = (jnp.arange(length, dtype=jnp.int32) < lengths[0]).astype(jnp.float32)
    mask_rows = lax.dynamic_slice_in_dim(mask, first_row, rows)
    pair_mask = mask_rows[:, None] * mask[None, :]
    penalty = (mask - 1.0) * MASKED
    state = pair[0].astype(jnp.float32)
    saved = {}
    for prefix, incoming in ((OUTGOING, False), (INCOMING, True)):
        update, saved[prefix] = triangle_forward(state, pair_mask, weights, prefix, incoming)
        state = state + update
    for prefix, ending in ((STARTING, False), (ENDING, True)):
        update, saved[prefix] = attention_forward(state, penalty, weights, prefix, ending)
        state = state + update
    update, saved[PAIR] = transition_forward(state, weights, PAIR)
    pair_final = state + update
    single_state = single[0].astype(jnp.float32)
    update, saved[ATTEND] = single_forward(single_state, pair_final, penalty, weights)
    single_mid = single_state + update
    update, saved[SINGLE] = transition_forward(single_mid, weights, SINGLE)
    single_final = single_mid + update
    grads = {}
    grad_single = single_cotangent[0].astype(jnp.float32)
    grad_single = grad_single + transition_backward(
        saved[SINGLE], grad_single, weights, SINGLE, grads
    )
    from_single, from_pair = single_backward(saved[ATTEND], grad_single, weights, grads)
    grad_single = grad_single + from_single
    grad_pair = pair_cotangent[0].astype(jnp.float32) + from_pair
    grad_pair = grad_pair + transition_backward(saved[PAIR], grad_pair, weights, PAIR, grads)
    for prefix, ending in ((ENDING, True), (STARTING, False)):
        grad_pair = grad_pair + attention_backward(
            saved[prefix], grad_pair, penalty, weights, prefix, ending, grads
        )
    for prefix, incoming in ((INCOMING, True), (OUTGOING, False)):
        grad_pair = grad_pair + triangle_backward(
            saved[prefix], grad_pair, pair_mask, weights, prefix, incoming, grads
        )
    flat = stored_order(jnp.concatenate([grads[name].reshape(-1) for name, shape in entries]))
    shard_size = params.shape[0]
    row_index = lax.axis_index("row")
    total = lax.psum(flat, ("crop", "row"))
    shard = lax.dynamic_slice_in_dim(total, row_index * shard_size, shard_size)
    norm_squared = jnp.sum(total * total)
    clip_norm = jnp.sqrt(norm_squared)
    clipped = shard * (CLIP / jnp.maximum(clip_norm, CLIP))
    new_first = BETA_ONE * moment_one + (1.0 - BETA_ONE) * clipped
    new_second = BETA_TWO * moment_two + (1.0 - BETA_TWO) * clipped * clipped
    rates, decays = rate_tables(entries)
    rate_shard = lax.dynamic_slice_in_dim(jnp.asarray(rates), row_index * shard_size, shard_size)
    decay_shard = lax.dynamic_slice_in_dim(jnp.asarray(decays), row_index * shard_size, shard_size)
    first_hat = new_first / (1.0 - BETA_ONE**STEP)
    second_hat = new_second / (1.0 - BETA_TWO**STEP)
    new_params = params - rate_shard * (
        first_hat / (jnp.sqrt(second_hat) + ADAM_EPS) + decay_shard * params
    )
    return (
        pair_final.astype(jnp.bfloat16)[None],
        single_final.astype(jnp.bfloat16)[None],
        grad_pair[None],
        grad_single[None],
        new_params,
        new_first,
        new_second,
        clip_norm,
    )


F32 = jnp.float32
BF16 = jnp.bfloat16
LOG2E = 1.4426950408889634
VMEM_LIMIT = 56 * 1024 * 1024


def mm(left, right):
    return lax.dot_general(left, right, (((1,), (0,)), ((), ())), preferred_element_type=F32)


def mm_nt(left, right):
    return lax.dot_general(left, right, (((1,), (1,)), ((), ())), preferred_element_type=F32)


def mm_tn(left, right):
    return lax.dot_general(left, right, (((0,), (0,)), ((), ())), preferred_element_type=F32)


def standardize(values):
    centred = values - jnp.mean(values, axis=0, keepdims=True)
    spread = jnp.mean(centred * centred, axis=0, keepdims=True)
    inverse = lax.rsqrt(spread + EPSILON)
    return centred * inverse, inverse


def standardize_back(unit, inverse, grad_unit):
    first = jnp.mean(grad_unit, axis=0, keepdims=True)
    second = jnp.mean(grad_unit * unit, axis=0, keepdims=True)
    return inverse * (grad_unit - first - unit * second)


def sigmoid(values):
    return 0.5 * jnp.tanh(0.5 * values) + 0.5


def column(ref, index):
    return ref[:, index : index + 1]


def live_pair(info, alive, row):
    return jnp.concatenate(
        [jnp.where(info[row + place] > 0, alive[0:1], 0.0) for place in range(GROUP)], axis=1
    )


GROUP = 8
LAG = 4


def each_group(count, body):
    def step(index, carry):
        body(index * GROUP)
        return carry

    lax.fori_loop(0, count // GROUP, step, 0, unroll=2)


def each_channel(count, body):
    def step(index, carry):
        body(index)
        return carry

    lax.fori_loop(0, count, step, 0)


def join(read, ref, row):
    return jnp.concatenate([read(ref, row + place) for place in range(GROUP)], axis=1)


def pieces_of(values):
    length = values.shape[1] // GROUP
    return [values[:, place * length : (place + 1) * length] for place in range(GROUP)]


def put_rows(ref, row, values):
    for place, part in enumerate(pieces_of(values)):
        ref[row + place] = part.astype(ref.dtype)


def put_inner(scratch, row, values):
    for place, part in enumerate(pieces_of(values)):
        scratch[:, row + place, :] = part


def read_inner(scratch, row):
    return scratch[:, row, :]


def put_turned(scratch, row, values):
    for place, part in enumerate(pieces_of(values)):
        scratch[:, row + place, :] = part.T


def add_lanes(ref, values):
    ref[...] += sum(pieces_of(values))


def spec_full(shape):
    return pl.BlockSpec(shape, lambda step: (0,) * len(shape))


def cost(microseconds):
    return pl.CostEstimate(
        flops=int(microseconds * 1e9), bytes_accessed=int(microseconds * 3e6), transcendentals=0
    )


class Both(list):
    pass


def all_rows(ins, outs):
    extents = [shape[axis] for shape, dtype, axis in outs if axis is not None]
    for array, axis in ins:
        if isinstance(axis, int):
            extents += [member.shape[axis] for member in (array if isinstance(array, list) else [array])]
    return max(extents)


def run_rows(kernel, name, steps, ins, outs, scratch, time=15, half=None, before=None):
    grid = steps if half is None else steps // 2
    offset = grid * (half or 0)
    flat = []
    groups = []
    for array, axis in ins:
        members = array if isinstance(array, Both) else [array]
        flat += [(member, axis) for member in members]
        groups.append((len(members), isinstance(array, Both)))
    full = all_rows(flat, outs)

    def spec(shape, axis):
        if axis is None:
            return spec_full(shape)
        size = full // steps
        first = offset if shape[axis] == full else 0
        sizes = tuple(size if place == axis else extent for place, extent in enumerate(shape))
        return pl.BlockSpec(
            sizes,
            lambda step: tuple(step + first if place == axis else 0 for place in range(len(shape))),
        )

    in_specs = [
        pl.BlockSpec(memory_space=pltpu.SMEM) if axis == "smem" else spec(array.shape, axis)
        for array, axis in flat
    ]
    out_specs = [spec(shape, axis) for shape, dtype, axis in outs]
    arrays = [array for array, axis in flat]
    aliases = {}
    kept = []
    for place, (shape, dtype, axis) in enumerate(outs):
        if before is not None and (axis is None or shape[axis] == full):
            aliases[len(arrays)] = place
            kept.append(place)
            arrays.append(before[place])
            in_specs.append(spec_full(shape) if axis is None else pl.BlockSpec(memory_space=pl.ANY))

    def run(*refs):
        taken = iter(refs)
        given = []
        for number, together in groups:
            members = [next(taken) for _ in range(number)]
            given.append(members if together else members[0])
        held = {place: next(taken) for place in kept}
        results = [next(taken) for _ in outs]

        @pl.when(pl.program_id(0) == 0)
        def _():
            for place, (shape, dtype, axis) in enumerate(outs):
                if axis is None:
                    results[place][...] = (
                        held[place][...] if place in held else jnp.zeros(shape, dtype)
                    )

        kernel(*given, *results, *taken)

    return pl.pallas_call(
        run,
        grid=(grid,),
        in_specs=in_specs,
        out_specs=out_specs,
        out_shape=[jax.ShapeDtypeStruct(shape, dtype) for shape, dtype, axis in outs],
        scratch_shapes=[pltpu.VMEM(shape, dtype) for shape, dtype in scratch],
        input_output_aliases=aliases,
        compiler_params=pltpu.CompilerParams(vmem_limit_bytes=VMEM_LIMIT),
        cost_estimate=cost(time if half is None else time / 2),
        name=name,
    )(*arrays)


def run_halves(kernel, name, steps, ins, outs, scratch, time=15):
    results = []
    for half in range(2):
        chosen = [
            (array[half] if type(array) is list else array, axis) for array, axis in ins
        ]
        before = results[0] if half else None
        results.append(run_rows(kernel, name, steps, chosen, outs, scratch, time, half, before))
    full = all_rows(ins, outs)
    return [
        [results[0][place], results[1][place]]
        if axis is not None and shape[axis] != full
        else results[1][place]
        for place, (shape, dtype, axis) in enumerate(outs)
    ]


def zero_first(*refs):
    @pl.when(pl.program_id(0) == 0)
    def _():
        for ref in refs:
            ref[...] = jnp.zeros(ref.shape, ref.dtype)


def lane_sums(ref):
    return jnp.sum(ref[...].T, axis=0, keepdims=True)


def on_last(body):
    @pl.when(pl.program_id(0) == pl.num_programs(0) - 1)
    def _():
        body()


def read_plain(ref, row):
    return ref[row].astype(F32)


def reorder(values, order):
    size = values.shape[0] // len(order)
    return jnp.concatenate([values[place * size : (place + 1) * size] for place in order], axis=0)


def read_tokens(order, ref, row):
    return reorder(ref[row].astype(F32), order).T


def read_flipped(refs, row):
    parts = jnp.concatenate([ref[:, row] for ref in refs], axis=1)
    return parts.reshape(-1, parts.shape[-1]).astype(F32).T


def read_turned(order, ref, row):
    parts = ref[:, row]
    return reorder(parts.reshape(-1, parts.shape[-1]).astype(F32), order).T


def tri_pre_row(info, alive, row, state, cols, first, proj_t):
    unit, inverse = standardize(state)
    lowered = (unit * column(cols, first) + column(cols, first + 1)).astype(BF16)
    project = mm(proj_t[...], lowered)
    half = project.shape[0] // 2
    return project[:half] * sigmoid(project[half:]) * live_pair(info, alive, row)


def store_product(out, scratch, devices):
    hidden = scratch.shape[0] // 2
    part = hidden // devices

    def one(device, carry):
        out[device, 0] = scratch[pl.ds(device * part, part)].astype(BF16)
        out[device, 1] = scratch[pl.ds(hidden + device * part, part)].astype(BF16)
        return carry

    lax.fori_loop(0, devices, one, 0)


def copy_blocks(target, source, count):
    def one(index, carry):
        target[index] = source[index].astype(target.dtype)
        return carry

    lax.fori_loop(0, count, one, 0)


def store_flipped(out, scratch):
    devices, part = out.shape[0], out.shape[1]

    def one(device, carry):
        out[device] = scratch[pl.ds(device * part, part)].astype(out.dtype)
        return carry

    lax.fori_loop(0, devices, one, 0)


def tri_post_row(state, tri, cols, proj_t, gate_t):
    unit, inverse = standardize(state)
    lowered = (unit * column(cols, 0) + column(cols, 1)).astype(BF16)
    tri_unit, tri_inverse = standardize(tri)
    out_low = (tri_unit * column(cols, 2) + column(cols, 3)).astype(BF16)
    output = mm(proj_t[...], out_low)
    gate = sigmoid(mm(gate_t[...], lowered))
    return unit, inverse, lowered, tri_unit, tri_inverse, out_low, output, gate


def row_base(rows):
    return pl.program_id(0) * rows


def tri_pre_first_kernel(devices, read, info, alive, pair, cols, proj_t, out, scratch):
    rows = pair.shape[0]

    def body(row):
        product = tri_pre_row(
            info, alive, row_base(rows) + row, join(read, pair, row), cols, 0, proj_t
        )
        put_inner(scratch, row, product)

    each_group(rows, body)
    store_product(out, scratch, devices)


def whole_rows(refs, *place):
    parts = jnp.concatenate([ref[(slice(None),) + place] for ref in refs], axis=1)
    return parts.reshape(-1, parts.shape[-1])


def split_rows(values, outs, *place):
    part = outs[0].shape[-2]
    parts = values.astype(BF16).reshape(outs[0].shape[0], -1, values.shape[-1])
    for half, out in enumerate(outs):
        out[(slice(None),) + place] = parts[:, half * part : (half + 1) * part]


def tri_product_kernel(incoming, operands, *outs):
    def body(channel):
        first = whole_rows(operands, 0, channel)
        second = whole_rows(operands, 1, channel)
        tri = mm_tn(first, second) if incoming else mm_nt(first, second)
        split_rows(tri, outs, channel)

    each_channel(operands[0].shape[2], body)


def tri_join_kernel(
    devices, read, info, alive, source, tri_in, cols, proj_t, gate_t, next_cols, next_proj_t,
    state_out, out, tri_scratch, scratch,
):
    rows = state_out.shape[0]
    copy_blocks(tri_scratch, tri_in, tri_in.shape[0])

    def body(row):
        state = join(read, source, row)
        pieces = tri_post_row(state, join(read_inner, tri_scratch, row), cols, proj_t, gate_t)
        state = state + pieces[6] * pieces[7]
        put_rows(state_out, row, state)
        product = tri_pre_row(
            info, alive, row_base(rows) + row, state, next_cols, 0, next_proj_t
        )
        put_inner(scratch, row, product)

    each_group(rows, body)
    store_product(out, scratch, devices)


def tri_last_kernel(
    source, tri_in, cols, proj_t, gate_t, next_cols, bias_t, state_out, bias_out, tri_scratch, scratch
):
    rows = state_out.shape[0]
    copy_blocks(tri_scratch, tri_in, tri_in.shape[0])

    def body(row):
        state = join(read_plain, source, row)
        pieces = tri_post_row(state, join(read_inner, tri_scratch, row), cols, proj_t, gate_t)
        state = state + pieces[6] * pieces[7]
        put_rows(state_out, row, state)
        unit, inverse = standardize(state)
        lowered = (unit * column(next_cols, 0) + column(next_cols, 1)).astype(BF16)
        put_inner(scratch, row, mm(bias_t[...], lowered))

    each_group(rows, body)
    bias_out[...] = scratch[: bias_out.shape[0]].astype(BF16)


def fill_bias(alive, bias_in, table, turned):
    @pl.when(pl.program_id(0) == 0)
    def _():
        length = table.shape[1]
        penalty = (alive[...] - 1.0) * (MASKED * LOG2E)
        for head in range(table.shape[0]):
            values = bias_in[:, head].reshape(length, length).astype(F32) * LOG2E
            if turned:
                table[head] = values + penalty.T[:, 0:1]
            else:
                table[head] = (values + penalty[0:1]).T


def attention_row(state, cols, proj_t):
    unit, inverse = standardize(state)
    lowered = (unit * column(cols, 0) + column(cols, 1)).astype(BF16)
    project = mm(proj_t[...], lowered)
    width = project.shape[0] // 4
    size = width // TA_HEADS
    query = (project[:width] * (size**-0.5 * LOG2E)).astype(BF16)
    key = project[width : 2 * width].astype(BF16)
    value = project[2 * width : 3 * width].astype(BF16)
    gate = sigmoid(project[3 * width :])
    return unit, inverse, lowered, query, key, value, gate


def in_stages(blocks, first, second, third):
    early, late, done = {}, {}, {}
    count = len(blocks)
    for step in range(count + 2 * LAG):
        if step < count:
            early[step] = first(*blocks[step])
        if 0 <= step - LAG < count:
            late[step - LAG] = second(*blocks[step - LAG], early.pop(step - LAG))
        if 0 <= step - 2 * LAG < count:
            place = step - 2 * LAG
            done[blocks[place]] = third(*blocks[place], late.pop(place))
    return done


def head_rows(values, place, head):
    size, length = values.shape[0] // TA_HEADS, values.shape[1] // GROUP
    return values[head * size : (head + 1) * size, place * length : (place + 1) * length]


def gather_heads(done):
    return jnp.concatenate(
        [
            jnp.concatenate([done[place, head] for head in range(TA_HEADS)], axis=0)
            for place in range(GROUP)
        ],
        axis=1,
    )


ROW_BLOCKS = [(place, head) for place in range(GROUP) for head in range(TA_HEADS)]
HEAD_BLOCKS = [(place, head) for head in range(TA_HEADS) for place in range(GROUP)]


def attend_rows(state, row, cols, proj_t, output_t, table, totals, mixed_out):
    unit, inverse, lowered, query, key, value, gate = attention_row(state, cols, proj_t)

    def score(place, head):
        return mm_tn(head_rows(key, place, head), head_rows(query, place, head)) + table[head]

    def shift(place, head, scores):
        top = jnp.max(scores, axis=0, keepdims=True)
        return top, jnp.exp2(scores - top).astype(BF16)

    def mix(place, head, items):
        top, shifted = items
        values = head_rows(value, place, head)
        size = values.shape[0]
        values = jnp.concatenate([values, jnp.ones((16, values.shape[1]), BF16)], axis=0)
        result = mm(values, shifted)
        total = result[size : size + 1]
        return result[:size] / total, top + jnp.log2(total)

    done = in_stages(ROW_BLOCKS, score, shift, mix)
    mixed = gather_heads({block: items[0] for block, items in done.items()})
    put_rows(totals, row, gather_heads({block: items[1] for block, items in done.items()}))
    put_rows(mixed_out, row, mixed)
    return state + mm(output_t[...], (mixed * gate).astype(BF16))


def starting_kernel(
    alive, source, bias_in, cols, proj_t, output_t, next_cols, bias_t, out, totals, mixed, bias_out,
    table, scratch, bias_scratch,
):
    fill_bias(alive, bias_in, table, False)
    rows = source.shape[0]

    def body(row):
        state = attend_rows(
            join(read_plain, source, row), row, cols, proj_t, output_t, table, totals, mixed
        )
        put_turned(scratch, row, state)
        unit, inverse = standardize(state)
        lowered = (unit * column(next_cols, 0) + column(next_cols, 1)).astype(BF16)
        put_inner(bias_scratch, row, mm(bias_t[...], lowered))

    each_group(rows, body)
    store_flipped(out, scratch)
    bias_out[...] = bias_scratch[: bias_out.shape[0]].astype(BF16)


def ending_kernel(alive, source, bias_in, cols, proj_t, output_t, out, totals, mixed, table):
    fill_bias(alive, bias_in, table, True)
    rows = source[0].shape[1]

    def body(row):
        state = attend_rows(
            join(read_flipped, source, row), row, cols, proj_t, output_t, table, totals, mixed
        )
        put_rows(out, row, state)

    each_group(rows, body)


def transition_kernel(
    order, source, cols, up_t, down_t, next_cols, bias_t, state_out, pair_out, bias_out, scratch, bias_scratch
):
    rows = source.shape[0]

    def body(row):
        state = join(read_plain, source, row)
        unit, inverse = standardize(state)
        lowered = (unit * column(cols, 0) + column(cols, 1)).astype(BF16)
        hidden = mm(up_t[...], lowered)
        half = hidden.shape[0] // 2
        first = hidden[:half]
        mixed = (first * sigmoid(first) * hidden[half:]).astype(BF16)
        state = state + mm(down_t[...], mixed)
        put_rows(state_out, row, state)
        put_turned(scratch, row, state)
        unit, inverse = standardize(state)
        lowered = (unit * column(next_cols, 0) + column(next_cols, 1)).astype(BF16)
        put_inner(bias_scratch, row, mm(bias_t[...], lowered))

    each_group(rows, body)
    size = pair_out.shape[0] // len(order)
    for place, held in enumerate(order):
        pair_out[place * size : (place + 1) * size] = scratch[held * size : (held + 1) * size].astype(BF16)
    bias_to_lanes(bias_out, bias_scratch)


def transition_back_kernel(
    read, mid, final, cotangent, bias_grad, cols, up_t, up, down, next_cols, bias_w,
    grad_out, up_grad, down_grad, bias_w_grad, vecs, norm_gain, norm_bias, pair_gain, pair_bias, bias_scratch,
):
    zero_first(norm_gain, norm_bias, pair_gain, pair_bias)
    rows = mid.shape[0]
    lanes_to_bias(bias_scratch, bias_grad)

    def body(row):
        grad = join(read, cotangent, row)
        unit, inverse = standardize(join(read_plain, final, row))
        gain = column(next_cols, 0)
        lowered = (unit * gain + column(next_cols, 1)).astype(BF16)
        grad_bias = join(read_inner, bias_scratch, row).astype(BF16)
        bias_w_grad[...] += mm_nt(lowered, grad_bias)
        grad_lowered = mm(bias_w[...], grad_bias)
        add_lanes(pair_gain, grad_lowered * unit)
        add_lanes(pair_bias, grad_lowered)
        grad = grad + standardize_back(unit, inverse, grad_lowered * gain)
        unit, inverse = standardize(join(read_plain, mid, row))
        gain = column(cols, 0)
        lowered = (unit * gain + column(cols, 1)).astype(BF16)
        hidden = mm(up_t[...], lowered)
        half = hidden.shape[0] // 2
        first, second = hidden[:half], hidden[half:]
        slope = sigmoid(first)
        silu = first * slope
        grad_low = grad.astype(BF16)
        grad_mixed = mm(down[...], grad_low)
        down_grad[...] += mm_nt((silu * second).astype(BF16), grad_low)
        grad_hidden = jnp.concatenate(
            [
                (grad_mixed * second * (slope + silu * (1.0 - slope))).astype(BF16),
                (grad_mixed * silu).astype(BF16),
            ],
            axis=0,
        )
        up_grad[...] += mm_nt(lowered, grad_hidden)
        grad_lowered = mm(up[...], grad_hidden)
        add_lanes(norm_gain, grad_lowered * unit)
        add_lanes(norm_bias, grad_lowered)
        put_rows(grad_out, row, grad + standardize_back(unit, inverse, grad_lowered * gain))

    each_group(rows, body)

    def finish():
        vecs[0:1] += lane_sums(norm_gain)
        vecs[1:2] += lane_sums(norm_bias)
        vecs[2:3] += lane_sums(pair_gain)
        vecs[3:4] += lane_sums(pair_bias)

    on_last(finish)


def attention_back_kernel(
    turned, read, read_grad, alive, source, grad_in, bias_in, totals, mixed_in, cols, proj_t, proj, output,
    grad_out, bias_out, proj_grad, output_grad, table, grad_table,
):
    fill_bias(alive, bias_in, table, turned)
    zero_first(grad_table)
    rows = grad_out.shape[0]

    def body(row):
        unit, inverse, lowered, query, key, value, gate = attention_row(
            join(read, source, row), cols, proj_t
        )
        mixed = join(read_plain, mixed_in, row)
        total = join(read_plain, totals, row)
        grad_low = join(read_grad, grad_in, row).astype(BF16)
        gated = mixed * gate
        output_grad[...] += mm_nt(gated.astype(BF16), grad_low)
        grad_gated = mm(output[...], grad_low)
        grad_gate = grad_gated * gated * (1.0 - gate)
        grad_mixed = (grad_gated * gate).astype(BF16)
        product = grad_mixed.astype(F32) * mixed
        size = query.shape[0] // TA_HEADS

        def score(place, head):
            scores = mm_tn(head_rows(key, place, head), head_rows(query, place, head))
            grads = mm_tn(head_rows(value, place, head), head_rows(grad_mixed, place, head))
            return scores + table[head], grads

        def slope(place, head, items):
            scores, grads = items
            probs = jnp.exp2(scores - head_rows(total, place, head))
            delta = jnp.sum(head_rows(product, place, head), axis=0, keepdims=True)
            grad_scores = probs * (grads - delta)
            grad_table[head] += grad_scores
            return probs.astype(BF16), grad_scores.astype(BF16)

        def back(place, head, items):
            probs, grad_scores = items
            return (
                mm(head_rows(key, place, head), grad_scores) * size**-0.5,
                mm_nt(head_rows(query, place, head), grad_scores) * (1.0 / LOG2E),
                mm_nt(head_rows(grad_mixed, place, head), probs),
            )

        done = in_stages(HEAD_BLOCKS, score, slope, back)
        grad_project = jnp.concatenate(
            [
                gather_heads({block: items[part] for block, items in done.items()})
                for part in range(3)
            ]
            + [grad_gate],
            axis=0,
        ).astype(BF16)
        proj_grad[...] += mm_nt(lowered, grad_project)
        put_rows(grad_out, row, mm(proj[...], grad_project))

    each_group(rows, body)

    def finish():
        for head in range(TA_HEADS):
            bias_out[:, head] = (
                grad_table[head].T.astype(BF16).reshape(bias_out.shape[0], bias_out.shape[2], -1)
            )

    on_last(finish)


def attention_end_row(
    state, grad, grad_lowered, grad_bias, cols, bias_w, bias_w_grad, norm_gain, norm_bias
):
    unit, inverse = standardize(state)
    gain = column(cols, 0)
    lowered = (unit * gain + column(cols, 1)).astype(BF16)
    bias_w_grad[...] += mm_nt(lowered, grad_bias)
    grad_lowered = grad_lowered + mm(bias_w[...], grad_bias)
    add_lanes(norm_gain, grad_lowered * unit)
    add_lanes(norm_bias, grad_lowered)
    return grad + standardize_back(unit, inverse, grad_lowered * gain)


def fill_bias_grad(scratch, bias_grad):
    heads = bias_grad.shape[1]
    total = bias_grad[0].astype(F32)
    for device in range(1, bias_grad.shape[0]):
        total = total + bias_grad[device].astype(F32)
    scratch[:heads] = total
    scratch[heads:] = jnp.zeros((scratch.shape[0] - heads,) + scratch.shape[1:], F32)


def ending_end_kernel(
    source, grad_in, grad_lowered, bias_grad, cols, bias_w,
    grad_out, bias_w_grad, vecs, norm_gain, norm_bias, bias_scratch, scratch,
):
    zero_first(norm_gain, norm_bias)
    fill_bias_grad(bias_scratch, bias_grad)
    rows = grad_in.shape[0]

    def body(row):
        grad = attention_end_row(
            join(read_flipped, source, row), join(read_plain, grad_in, row),
            join(read_plain, grad_lowered, row), join(read_inner, bias_scratch, row).astype(BF16), cols, bias_w, bias_w_grad, norm_gain, norm_bias,
        )
        put_turned(scratch, row, grad)

    each_group(rows, body)
    store_flipped(grad_out, scratch)

    def finish():
        vecs[0:1] += lane_sums(norm_gain)
        vecs[1:2] += lane_sums(norm_bias)

    on_last(finish)


def tri_post_back_row(
    state, tri, grad, cols, proj_t, gate_t, proj, gate_w, proj_grad, gate_grad, out_gain, out_bias
):
    unit, inverse, lowered, tri_unit, tri_inverse, out_low, output, gate = tri_post_row(
        state, tri, cols, proj_t, gate_t
    )
    grad_output = grad * gate
    grad_gate = (grad_output * output * (1.0 - gate)).astype(BF16)
    grad_output = grad_output.astype(BF16)
    proj_grad[...] += mm_nt(out_low, grad_output)
    gate_grad[...] += mm_nt(lowered, grad_gate)
    grad_normed = mm(proj[...], grad_output)
    add_lanes(out_gain, grad_normed * tri_unit)
    add_lanes(out_bias, grad_normed)
    grad_tri = standardize_back(tri_unit, tri_inverse, grad_normed * column(cols, 2))
    return grad_tri, mm(gate_w[...], grad_gate)


def starting_end_kernel(
    source, grad_in, grad_lowered, bias_grad, cols, bias_w,
    below, tri_in, tri_cols, proj_t, gate_t, proj, gate_w,
    grad_out, tri_out, gate_back, bias_w_grad, proj_grad, gate_grad, vecs,
    norm_gain, norm_bias, out_gain, out_bias, bias_scratch, tri_scratch,
):
    zero_first(norm_gain, norm_bias, out_gain, out_bias)
    fill_bias_grad(bias_scratch, bias_grad)
    copy_blocks(tri_scratch, tri_in, tri_in.shape[0])
    rows = source.shape[0]

    def body(row):
        grad = attention_end_row(
            join(read_plain, source, row), join(read_flipped, grad_in, row),
            join(read_plain, grad_lowered, row), join(read_inner, bias_scratch, row).astype(BF16), cols, bias_w, bias_w_grad, norm_gain, norm_bias,
        )
        put_rows(grad_out, row, grad)
        grad_tri, back = tri_post_back_row(
            join(read_plain, below, row), join(read_inner, tri_scratch, row), grad, tri_cols, proj_t, gate_t, proj, gate_w,
            proj_grad, gate_grad, out_gain, out_bias,
        )
        put_rows(gate_back, row, back)
        put_inner(tri_scratch, row, grad_tri)

    each_group(rows, body)
    copy_blocks(tri_out, tri_scratch, tri_out.shape[0])

    def finish():
        vecs[0:1] += lane_sums(norm_gain)
        vecs[1:2] += lane_sums(norm_bias)
        vecs[2:3] += lane_sums(out_gain)
        vecs[3:4] += lane_sums(out_bias)

    on_last(finish)


def tri_product_back_kernel(incoming, grad, operands, *outs):
    def body(channel):
        first = whole_rows(operands, 0, channel)
        second = whole_rows(operands, 1, channel)
        tri = whole_rows(grad, channel)
        if incoming:
            grad_first = mm_nt(second, tri)
            grad_second = mm(first, tri)
        else:
            grad_first = mm(tri, second)
            grad_second = mm_tn(tri, first)
        split_rows(grad_first, outs, 0, channel)
        split_rows(grad_second, outs, 1, channel)

    each_channel(operands[0].shape[2], body)


def tri_pre_back_row(
    info, alive, row, state, product_grad, gate_back, grad, cols, proj_t, proj, proj_grad, norm_gain, norm_bias
):
    unit, inverse = standardize(state)
    gain = column(cols, 0)
    lowered = (unit * gain + column(cols, 1)).astype(BF16)
    project = mm(proj_t[...], lowered)
    half = project.shape[0] // 2
    gate = sigmoid(project[half:])
    grad_first = product_grad * gate * live_pair(info, alive, row)
    grad_second = grad_first * project[:half] * (1.0 - gate)
    grad_project = jnp.concatenate([grad_first.astype(BF16), grad_second.astype(BF16)], axis=0)
    proj_grad[...] += mm_nt(lowered, grad_project)
    grad_lowered = mm(proj[...], grad_project) + gate_back
    add_lanes(norm_gain, grad_lowered * unit)
    add_lanes(norm_bias, grad_lowered)
    return grad + standardize_back(unit, inverse, grad_lowered * gain)


def fill_product_grad(scratch, product_grad):
    devices, part = product_grad.shape[0], product_grad.shape[2]

    def one(device, carry):
        scratch[pl.ds(device * part, part)] = product_grad[device, 0].astype(F32)
        scratch[pl.ds((devices + device) * part, part)] = product_grad[device, 1].astype(F32)
        return carry

    lax.fori_loop(0, devices, one, 0)


def tri_join_back_kernel(
    read, info, alive, source, product_grad, gate_in, grad_in, cols, proj_t, proj,
    below, tri_in, tri_cols, out_t, gate_t, out_w, gate_w,
    grad_out, tri_out, gate_back, proj_grad, out_grad, gate_grad, vecs,
    norm_gain, norm_bias, out_gain, out_bias, scratch, tri_scratch,
):
    zero_first(norm_gain, norm_bias, out_gain, out_bias)
    fill_product_grad(scratch, product_grad)
    copy_blocks(tri_scratch, tri_in, tri_in.shape[0])
    rows = source.shape[0]

    def body(row):
        grad = tri_pre_back_row(
            info, alive, row_base(rows) + row, join(read_plain, source, row),
            join(read_inner, scratch, row), join(read_plain, gate_in, row),
            join(read_plain, grad_in, row), cols, proj_t, proj, proj_grad, norm_gain, norm_bias,
        )
        put_rows(grad_out, row, grad)
        grad_tri, back = tri_post_back_row(
            join(read, below, row), join(read_inner, tri_scratch, row), grad, tri_cols, out_t, gate_t, out_w, gate_w,
            out_grad, gate_grad, out_gain, out_bias,
        )
        put_rows(gate_back, row, back)
        put_inner(tri_scratch, row, grad_tri)

    each_group(rows, body)
    copy_blocks(tri_out, tri_scratch, tri_out.shape[0])

    def finish():
        vecs[0:1] += lane_sums(norm_gain)
        vecs[1:2] += lane_sums(norm_bias)
        vecs[2:3] += lane_sums(out_gain)
        vecs[3:4] += lane_sums(out_bias)

    on_last(finish)


def tri_first_back_kernel(
    read, order, info, alive, source, product_grad, gate_in, grad_in, cols, proj_t, proj,
    grad_out, proj_grad, vecs, norm_gain, norm_bias, scratch,
):
    zero_first(norm_gain, norm_bias)
    fill_product_grad(scratch, product_grad)
    rows = source.shape[0]

    def body(row):
        grad = tri_pre_back_row(
            info, alive, row_base(rows) + row, join(read, source, row),
            join(read_inner, scratch, row), join(read_plain, gate_in, row),
            join(read_plain, grad_in, row), cols, proj_t, proj, proj_grad, norm_gain, norm_bias,
        )
        for place, part in enumerate(pieces_of(grad)):
            grad_out[row + place] = reorder(part.T, order).astype(grad_out.dtype)

    each_group(rows, body)

    def finish():
        vecs[0:1] += lane_sums(norm_gain)
        vecs[1:2] += lane_sums(norm_bias)

    on_last(finish)


RUN = 24


def table_of(entries):
    table = {}
    offset = 0
    for name, shape in entries:
        table[name] = (offset // STRIDE, shape)
        offset += math.prod(shape)
    return table, offset


def runs_kernel(info, shard, out, scratch):
    def one(block, carry):
        scratch[:, block, :] = shard[pl.ds(block * STRIDE, STRIDE), :].T
        return carry

    lax.fori_loop(0, RUN, one, 0)
    half = STRIDE // 2
    turn = info[0] * half

    def move(lane, carry):
        out[lane] = scratch[lax.rem(lane + turn, STRIDE)].astype(BF16)
        return carry

    lax.fori_loop(0, STRIDE, move, 0)


def run_place(shards, total, lane, shard):
    count = total // STRIDE
    whole = total // shards
    step, odd = whole // STRIDE, (whole % STRIDE) // (STRIDE // 2)
    extra = lax.div(shard * odd + jnp.where(lane < STRIDE // 2, 1, 0), 2)
    start = lane * count + shard * step + extra
    return lax.div(start, STRIDE), lax.rem(start, STRIDE)


def rows_from_runs(runs, rows, first_lane, total):
    shards, lanes = runs.shape[0], runs.shape[1]
    base = first_lane * (total // STRIDE) // STRIDE

    def one(index, carry):
        lane, shard = lax.div(index, shards), lax.rem(index, shards)
        row, shift = run_place(shards, total, first_lane + lane, shard)
        row = row - base
        turned = pltpu.roll(runs[shard, lane].astype(F32), shift, 1)
        place = lax.broadcasted_iota(jnp.int32, (RUN + 1, STRIDE), 1)
        last, before = carry
        joint = jnp.where(row - before == RUN, last[2:3], last[1:2])
        below = jnp.concatenate([joint, turned], axis=0)
        above = jnp.concatenate([turned, turned[RUN - 1 :]], axis=0)
        values = jnp.where(place < shift, below, above)
        rows[pl.ds(row, RUN + 1), :] = values
        return values[RUN - 2 :], row

    lax.fori_loop(0, shards * lanes, one, (jnp.zeros((3, STRIDE), F32), -RUN), unroll=4)


def runs_from_rows(rows, out, first_lane, base, total):
    shards, lanes = out.shape[0], out.shape[1]

    def one(index, carry):
        lane, shard = lax.div(index, shards), lax.rem(index, shards)
        row, shift = run_place(shards, total, first_lane + lane, shard)
        turned = pltpu.roll(rows[pl.ds(row - base, RUN + 1), :], (STRIDE - shift) % STRIDE, 1)
        place = lax.broadcasted_iota(jnp.int32, (RUN, STRIDE), 1)
        out[shard, lane] = jnp.where(
            place < STRIDE - shift, turned[:RUN], turned[1:]
        ).astype(BF16)
        return carry

    lax.fori_loop(0, shards * lanes, one, 0, unroll=4)


def row_height(base, first_lane, last_lane, total):
    end = (last_lane * (total // STRIDE)) // STRIDE + RUN + 2
    return -(-(end - base) // 8) * 8


def take_matrix(rows, first, shape):
    blocks = shape[1] // STRIDE
    return [
        rows[pl.ds(first + block, shape[0], stride=blocks), :]
        if blocks > 1
        else rows[first : first + shape[0], :]
        for block in range(blocks)
    ]


def put_matrix(rows, first, matrix):
    height, width = matrix.shape
    blocks = width // STRIDE
    for block in range(blocks):
        part = matrix[:, block * STRIDE : (block + 1) * STRIDE]
        if blocks > 1:
            rows[pl.ds(first + block, height, stride=blocks), :] = part
        else:
            rows[first : first + height, :] = part


def spread(index, heads, rows):
    lane = lax.broadcasted_iota(jnp.int32, (STRIDE, STRIDE), 0)
    channel = lax.broadcasted_iota(jnp.int32, (STRIDE, STRIDE), 1)
    return (channel == index * (STRIDE // heads) + lane // heads).astype(BF16)


def take_narrow(rows, first, heads, high):
    total = jnp.zeros((high, STRIDE), F32)
    head = lax.broadcasted_iota(jnp.int32, (high, STRIDE), 0)
    lane = lax.broadcasted_iota(jnp.int32, (high, STRIDE), 1)
    for index in range(heads):
        line = rows[first + index : first + index + 1, :]
        picked = jnp.where(lane % heads == head, line, 0.0).astype(BF16)
        total = total + mm(picked, spread(index, heads, rows))
    return total


def put_narrow(rows, first, heads, matrix):
    turned = matrix.T.astype(BF16)
    high = turned.shape[0]
    head = lax.broadcasted_iota(jnp.int32, (high, STRIDE), 0)
    lane = lax.broadcasted_iota(jnp.int32, (high, STRIDE), 1)
    for index in range(heads):
        wide = mm_nt(turned, spread(index, heads, rows))
        rows[first + index : first + index + 1, :] = jnp.sum(
            jnp.where(lane % heads == head, wide, 0.0), axis=0, keepdims=True
        )


PAIR_MATRICES = (
    (OUTGOING, PROJ_GATE), (OUTGOING, PROJ_OUT), (OUTGOING, GATE_OUT),
    (INCOMING, PROJ_GATE), (INCOMING, PROJ_OUT), (INCOMING, GATE_OUT),
    (STARTING, QKVG), (STARTING, OUTPUT), (ENDING, QKVG), (ENDING, OUTPUT), (PAIR, UP), (PAIR, DOWN),
)
PAIR_COLUMNS = (
    (OUTGOING, ((OUTGOING, NORM_GAIN), (OUTGOING, NORM_BIAS), (OUTGOING, OUT_GAIN), (OUTGOING, OUT_BIAS))),
    (INCOMING, ((INCOMING, NORM_GAIN), (INCOMING, NORM_BIAS), (INCOMING, OUT_GAIN), (INCOMING, OUT_BIAS))),
    (STARTING, ((STARTING, NORM_GAIN), (STARTING, NORM_BIAS))),
    (ENDING, ((ENDING, NORM_GAIN), (ENDING, NORM_BIAS))),
    (PAIR, ((PAIR, NORM_GAIN), (PAIR, NORM_BIAS))),
)
SINGLE_MATRICES = ((ATTEND, QKVG), (ATTEND, OUTPUT), (SINGLE, UP), (SINGLE, DOWN))
SINGLE_VECTORS = ((ATTEND, NORM_GAIN), (ATTEND, NORM_BIAS), (SINGLE, NORM_GAIN), (SINGLE, NORM_BIAS))


def put_columns(rows, out, table, base, names):
    out[...] = jnp.zeros(out.shape, F32)
    lines = [rows[table[name][0] - base : table[name][0] - base + 1, :] for name in names]
    lines.append(jnp.zeros((8 - len(lines), STRIDE), F32))
    out[...] = jnp.concatenate(lines, axis=0).T


def unpack_pair_kernel(table, total, runs, *refs):
    rows = refs[-1]
    outs = list(refs[:-1])
    rows_from_runs(runs, rows, 0, total)
    for name in PAIR_MATRICES:
        first, shape = table[name]
        plain, turned = outs.pop(0), outs.pop(0)
        for block, part in enumerate(take_matrix(rows, first, shape)):
            place = slice(block * STRIDE, (block + 1) * STRIDE)
            plain[:, place] = part.astype(BF16)
            turned[place, :] = part.T.astype(BF16)
    for prefix in (STARTING, ENDING):
        plain, turned = outs.pop(0), outs.pop(0)
        first, shape = table[(prefix, BIAS_PROJ)]
        matrix = take_narrow(rows, first, shape[1], 8)
        turned[...] = matrix.astype(BF16)
        plain[...] = matrix.T.astype(BF16)
    for prefix, names in PAIR_COLUMNS:
        put_columns(rows, outs.pop(0), table, 0, names)


def unpack_single_kernel(table, total, first_lane, runs, *refs):
    rows = refs[-1]
    outs = list(refs[:-1])
    rows_from_runs(runs, rows, first_lane, total)
    base = first_lane * (total // STRIDE) // STRIDE
    for name in SINGLE_MATRICES:
        first, shape = table[name]
        out = outs.pop(0)
        for block, part in enumerate(take_matrix(rows, first - base, shape)):
            out[:, block * STRIDE : (block + 1) * STRIDE] = part.astype(BF16)
    first, shape = table[(ATTEND, PAIR_PROJ)]
    matrix = take_narrow(rows, first - base, shape[1], shape[1])
    plain, turned = outs.pop(0), outs.pop(0)
    turned[...] = matrix.astype(BF16)
    plain[...] = matrix.T.astype(BF16)
    put_columns(rows, outs.pop(0), table, base, ((ATTEND, PAIR_GAIN), (ATTEND, PAIR_BIAS)))
    lines = outs.pop(0)
    lines[...] = jnp.zeros(lines.shape, F32)
    for index, name in enumerate(SINGLE_VECTORS):
        first, shape = table[name]
        for block in range(shape[0] // STRIDE):
            lines[index : index + 1, block * STRIDE : (block + 1) * STRIDE] = rows[
                first - base + block : first - base + block + 1, :
            ]


def pack_kernel(table, total, first_lane, base, names, *refs):
    ins, out, rows = refs[: len(names)], refs[-2], refs[-1]
    for name, ref in zip(names, ins):
        if isinstance(name, tuple):
            first, shape = table[name]
            if shape[1] % STRIDE:
                put_narrow(rows, first - base, shape[1], ref[...])
            else:
                put_matrix(rows, first - base, ref)
        else:
            for index, vector in name:
                first, shape = table[vector]
                for block in range(shape[0] // STRIDE):
                    rows[first + block - base : first + block - base + 1, :] = ref[
                        index : index + 1, block * STRIDE : (block + 1) * STRIDE
                    ]
    runs_from_rows(rows, out, first_lane, base, total)


def shard_kernel(whole, info, summed, others, out, squares, runs):
    half = STRIDE // 2
    crops, first, part = summed.shape[0], summed.shape[1], others.shape[1]

    def add(lane, carry):
        runs[lane] = sum(summed[crop, lane].astype(F32) for crop in range(crops))
        return carry

    lax.fori_loop(0, first, add, 0)
    for crop in range(crops):

        def move(lane, carry, crop=crop):
            runs[first + crop * part + lane] = others[crop, lane].astype(F32)
            return carry

        lax.fori_loop(0, part, move, 0)
    squares[...] = jnp.zeros(squares.shape, F32)

    def one(block, carry):
        first = runs[pl.ds(info[0] * half, half), block, :]
        second = runs[pl.ds(half - info[0] * half, half), block, :]
        values = jnp.concatenate([first, second], axis=0).T
        row = block * STRIDE + lax.broadcasted_iota(jnp.int32, values.shape, 0)
        lane = lax.broadcasted_iota(jnp.int32, values.shape, 1)
        values = jnp.where(row * STRIDE + lane < whole, values, 0.0)
        out[pl.ds(block * STRIDE, STRIDE), :] = values
        squares[...] += jnp.sum((values * values).reshape(-1, 8, STRIDE), axis=0)
        return carry

    lax.fori_loop(0, RUN, one, 0)


def whole_call(kernel, name, ins, outs, scratch, time=8):
    def spec(axis):
        return pl.BlockSpec(memory_space=pltpu.SMEM if axis == "smem" else pltpu.VMEM)

    return pl.pallas_call(
        kernel,
        in_specs=[spec(axis) for array, axis in ins],
        out_specs=[pl.BlockSpec(memory_space=pltpu.VMEM) for shape, dtype in outs],
        out_shape=[jax.ShapeDtypeStruct(shape, dtype) for shape, dtype in outs],
        scratch_shapes=[pltpu.VMEM(shape, dtype) for shape, dtype in scratch],
        compiler_params=pltpu.CompilerParams(vmem_limit_bytes=VMEM_LIMIT),
        cost_estimate=cost(time),
        name=name,
    )(*[array for array, axis in ins])


def unpack_pair(table, total, runs):
    outs = []
    names = []
    for name in PAIR_MATRICES:
        shape = table[name][1]
        outs += [(shape, BF16), (shape[::-1], BF16)]
        names += [name, (name, T)]
    for prefix in (STARTING, ENDING):
        outs += [((STRIDE, 8), BF16), ((8, STRIDE), BF16)]
        names += [(prefix, BIAS_W), (prefix, BIAS_T)]
    for prefix, parts in PAIR_COLUMNS:
        outs.append(((STRIDE, 8), F32))
        names.append((prefix, COLS))
    height = row_height(0, 0, runs.shape[1], total)
    values = whole_call(
        functools.partial(unpack_pair_kernel, table, total), "pair_weights", [(runs, None)], outs,
        [((height, STRIDE), F32)], 20,
    )
    return dict(zip(names, values))


def unpack_single(table, total, first_lane, runs):
    outs = [(table[name][1], BF16) for name in SINGLE_MATRICES]
    names = list(SINGLE_MATRICES)
    shape = table[(ATTEND, PAIR_PROJ)][1]
    outs += [(shape, BF16), (shape[::-1], BF16), ((STRIDE, 8), F32), ((8, S), F32)]
    names += [(ATTEND, PAIR_PROJ), ((ATTEND, PAIR_PROJ), T), (ATTEND, COLS), (SINGLE, VECTORS)]
    base = first_lane * (total // STRIDE) // STRIDE
    height = row_height(base, first_lane, first_lane + runs.shape[1], total)
    values = whole_call(
        functools.partial(unpack_single_kernel, table, total, first_lane), "single_weights",
        [(runs, None)], outs, [((height, STRIDE), F32)],
    )
    return dict(zip(names, values))


def pack(name, table, total, shards, lanes, base, parts):
    height = row_height(base, *lanes, total)
    for held, array in parts:
        if isinstance(held, tuple):
            end = table[held][0] - base + array.shape[0] * max(1, array.shape[1] // STRIDE)
            height = max(height, -(-end // 8) * 8)
    return whole_call(
        functools.partial(pack_kernel, table, total, lanes[0], base, [held for held, array in parts]),
        name, [(array, None) for held, array in parts],
        [((shards, lanes[1] - lanes[0], RUN, STRIDE), BF16)], [((height, STRIDE), F32)],
    )[0]


def bias_to_lanes(out, scratch):
    heads, devices = scratch.shape[0], out.shape[0]
    part = scratch.shape[2] // devices
    per = STRIDE // part
    lane = lax.broadcasted_iota(jnp.int32, (scratch.shape[1], STRIDE), 1)
    for device in range(devices):
        block, place = device // per, device % per
        for first in range(0, heads, per):
            total = None
            for index in range(per):
                values = scratch[first + index, :, block * STRIDE : (block + 1) * STRIDE]
                values = pltpu.roll(values, (index - place) * part % STRIDE, 1)
                total = values if index == 0 else jnp.where(lane < index * part, total, values)
            out[device, :, first * part : first * part + STRIDE] = total.astype(out.dtype)


def lanes_to_bias(scratch, sent):
    heads, devices = scratch.shape[0], sent.shape[0]
    part = scratch.shape[2] // devices
    per = STRIDE // part
    lane = lax.broadcasted_iota(jnp.int32, (scratch.shape[1], STRIDE), 1)
    for head in range(heads):
        first, index = head // per * per, head % per
        for block in range(devices // per):
            total = None
            for place in range(per):
                values = sent[block * per + place, :, first * part : first * part + STRIDE].astype(F32)
                values = pltpu.roll(values, (place - index) * part % STRIDE, 1)
                total = values if place == 0 else jnp.where(lane < place * part, total, values)
            scratch[head, :, block * STRIDE : (block + 1) * STRIDE] = total


def standardize_lanes(values):
    centred = values - jnp.mean(values, axis=1, keepdims=True)
    inverse = lax.rsqrt(jnp.mean(centred * centred, axis=1, keepdims=True) + EPSILON)
    return centred * inverse, inverse


def single_kernel(
    state_in, back_in, project, kv, bias, alive, vectors, output_w, up, down,
    final_out, grad_out, sent, query_grad, gate_grad, output_grad, up_grad, down_grad, vecs,
):
    state = state_in[...]
    rows, width = state.shape
    size = width // SA_HEADS
    per = STRIDE // rows
    groups = SA_HEADS // per
    scale = size**-0.5
    tokens = kv.shape[0] * rows
    both = kv[...].reshape(tokens, 2 * width)
    keys, values = both[:, :width], both[:, width:]
    penalty = ((alive[...] - 1.0) * (MASKED * LOG2E)).T[:, 0:1]

    channel = lax.broadcasted_iota(jnp.int32, (width, STRIDE), 0)
    lane = lax.broadcasted_iota(jnp.int32, (width, STRIDE), 1)
    own = [lax.div(channel, size) == group * per + lax.div(lane, rows) for group in range(groups)]
    channel_b = lax.broadcasted_iota(jnp.int32, (STRIDE, width), 1)
    row_b = lax.broadcasted_iota(jnp.int32, (STRIDE, width), 0)
    own_b = [lax.div(channel_b, size) == group * per + lax.div(row_b, rows) for group in range(groups)]

    def spread_rows(matrix):
        turned = jnp.concatenate([matrix] * per, axis=0).T
        return [jnp.where(mask, turned, 0.0).astype(BF16) for mask in own]

    def collect(blocks):
        total = sum(jnp.where(mask, block, 0.0) for mask, block in zip(own_b, blocks))
        return sum(total[index * rows : (index + 1) * rows] for index in range(per))

    queries = spread_rows(project[:, :width] * (scale * LOG2E))
    gate = sigmoid(project[:, 3 * width :])
    scores = [
        mm(keys, queries[group])
        + bias[:, :, group * STRIDE : (group + 1) * STRIDE].reshape(tokens, STRIDE).astype(F32) * LOG2E
        + penalty
        for group in range(groups)
    ]
    shifted = [jnp.exp2(block - jnp.max(block, axis=0, keepdims=True)) for block in scores]
    probs = [block / jnp.sum(block, axis=0, keepdims=True) for block in shifted]
    probs_low = [block.astype(BF16) for block in probs]
    mixed = collect([mm_tn(block, values) for block in probs_low])
    gated = mixed * gate
    gated_low = gated.astype(BF16)
    state = state + mm(gated_low, output_w[...])

    unit, inverse = standardize_lanes(state)
    gain = vectors[2:3]
    lowered = (unit * gain + vectors[3:4]).astype(BF16)
    hidden = mm(lowered, up[...])
    half = hidden.shape[1] // 2
    first, second = hidden[:, :half], hidden[:, half:]
    slope = sigmoid(first)
    silu = first * slope
    swish = (silu * second).astype(BF16)
    final_out[...] = state + mm(swish, down[...])

    grad = back_in[...]
    grad_low = grad.astype(BF16)
    grad_mixed = mm_nt(grad_low, down[...])
    down_grad[...] = mm_tn(swish, grad_low)
    grad_hidden = jnp.concatenate(
        [
            (grad_mixed * second * (slope + silu * (1.0 - slope))).astype(BF16),
            (grad_mixed * silu).astype(BF16),
        ],
        axis=1,
    )
    grad_lowered = mm_nt(grad_hidden, up[...])
    vecs[...] = jnp.zeros(vecs.shape, F32)
    vecs[0:1] = jnp.sum(grad_lowered * unit, axis=0, keepdims=True)
    vecs[1:2] = jnp.sum(grad_lowered, axis=0, keepdims=True)
    grad_unit = grad_lowered * gain
    grad = grad + inverse * (
        grad_unit
        - jnp.mean(grad_unit, axis=1, keepdims=True)
        - unit * jnp.mean(grad_unit * unit, axis=1, keepdims=True)
    )
    grad_out[...] = grad

    grad_low = grad.astype(BF16)
    grad_gated = mm_nt(grad_low, output_w[...])
    gate_grad[...] = grad_gated * gated * (1.0 - gate)
    grads = spread_rows(grad_gated * gate)
    grad_probs = [mm(values, block) for block in grads]
    grad_scores = []
    for block, grad_block in zip(probs, grad_probs):
        delta = jnp.sum(block * grad_block, axis=0, keepdims=True)
        grad_scores.append((block * (grad_block - delta)).astype(BF16))
    for group, block in enumerate(grad_scores):
        sent[:, :, group * STRIDE : (group + 1) * STRIDE] = block.reshape(kv.shape[0], rows, STRIDE)
    query_grad[...] = collect([mm_tn(block, keys) for block in grad_scores]) * scale
    key_part = sum(mm_nt(block, query) for block, query in zip(grad_scores, queries)) * (1.0 / LOG2E)
    value_part = sum(mm_nt(block, grad_block) for block, grad_block in zip(probs_low, grads))
    first = groups * STRIDE
    sent[:, :, first : first + width] = key_part.astype(BF16).reshape(kv.shape[0], rows, width)
    sent[:, :, first + width :] = value_part.astype(BF16).reshape(kv.shape[0], rows, width)
    output_grad[...] = mm_tn(gated_low, grad_low)
    up_grad[...] = mm_tn(lowered, grad_hidden)


def single_middle(state, back, projected, bias, alive, weights):
    lowered, project, kv = projected
    rows, width = state.shape
    devices = kv.shape[0]
    names = ((ATTEND, OUTPUT), (SINGLE, UP), (SINGLE, DOWN))
    matrices = [weights[name] for name in names]
    square = (rows, width)
    outs = [
        (square, F32), (square, F32), ((devices, rows, SA_HEADS * rows + 2 * width), BF16),
        (square, F32), (square, F32),
    ] + [(matrix.shape, F32) for matrix in matrices] + [((8, width), F32)]
    ins = [state, back, project, kv, bias, alive, weights[(SINGLE, VECTORS)]] + matrices
    final, grad, sent, query_grad, gate_grad, *found, vecs = whole_call(
        single_kernel, "single_path", [(array, None) for array in ins], outs, [], 15
    )
    grads = dict(zip(names, found))
    grads[(SINGLE, NORM_GAIN)], grads[(SINGLE, NORM_BIAS)] = vecs[0], vecs[1]
    return final, grad, sent, grads, (state, lowered, query_grad, gate_grad)


def swap(values, group):
    return lax.all_to_all(values, group, split_axis=0, concat_axis=0, tiled=True)


def single_project(single_state, weights, devices):
    gain, shift = norm_pair(weights, ATTEND)
    lowered = layer_norm(single_state, gain, shift).astype(BF16)
    width = lowered.shape[1]
    qkvg = matmul(lowered, weights[(ATTEND, QKVG)])
    both = qkvg[:, width : 3 * width].astype(BF16)
    both = jnp.broadcast_to(both[None], (devices,) + both.shape)
    return lowered, qkvg, both


def single_attend_end(pending, parts, weights, grads):
    single_state, lowered, grad_query, grad_gate = pending
    rows, width = lowered.shape
    grad_both = jnp.sum(parts.astype(F32), axis=0)
    grad_qkvg = jnp.concatenate(
        [grad_query.reshape(rows, width), grad_both, grad_gate], axis=-1
    ).astype(BF16)
    grads[(ATTEND, QKVG)] = outer_sum(lowered, grad_qkvg)
    grad_lowered = matmul(grad_qkvg, weights[(ATTEND, QKVG)].T)
    gain, shift = norm_pair(weights, ATTEND)
    grad_single, grads[(ATTEND, NORM_GAIN)], grads[(ATTEND, NORM_BIAS)] = norm_backward(
        single_state, gain, shift, grad_lowered
    )
    return grad_single


def after(values, *others):
    held = lax.optimization_barrier((values,) + others)
    return held


def in_turn():
    last = []

    def send(values, axes):
        if last:
            values = after(values, last.pop())[0]
        moved = swap(values, axes)
        last.append(moved)
        return moved

    return send


def pair_path(pair, info, alive, orders, weights, cotangent, middle, between, meet, send, group, parts):
    rows, length, width = pair.shape
    hidden = weights[(OUTGOING, PROJ_OUT)].shape[0]
    devices = length // rows
    cores = devices // parts
    order, order_back = orders
    read_first = functools.partial(read_tokens, order)
    read_last = functools.partial(read_turned, order)
    part = hidden // devices
    steps = rows // 16
    state_shape = (rows, width, length)
    block = rows // steps
    half = rows // 2
    flip_shape = (devices, rows, rows, width)
    product_shape = (devices, 2, part, rows, length)
    product_half = (devices, 2, part, half, length)
    tri_shape = (devices, part, rows, length)
    tri_half = (devices, part, half, length)
    channel_block = math.gcd(part, 4)

    def products(name, kernel, arrays, out_shape):
        axes = {4: 1, 5: 2}
        out = (out_shape, BF16, axes[len(out_shape)])
        return run_rows(
            kernel, name, part // channel_block,
            [(Both(pieces), axes[pieces[0].ndim]) for pieces in arrays],
            [out] * (rows // out_shape[-2]), [], 7,
        )

    def swap_all(pieces):
        return [send(values, group) for values in pieces]

    def by_hidden(pieces):
        return [values.reshape((hidden,) + values.shape[2:]) for values in pieces]

    def by_device(pieces):
        return [values.reshape((devices, part) + values.shape[1:]) for values in pieces]

    def cols(prefix):
        return weights[(prefix, COLS)]

    tri_cols = cols

    def turned(name):
        return weights[(name, T)]

    tri_scratch = ((hidden, block, length), F32)
    product_scratch = ((2 * hidden, block, length), F32)
    head_scratch = ((8, block, length), F32)
    wide = ((width, length), F32)
    flip_scratch = ((length, block, width), F32)
    table = ((TA_HEADS, length, length), F32)
    attend_saves = [((rows, TA_HEADS, length), F32, 0), (state_shape, BF16, 0)]

    product = run_rows(
        functools.partial(tri_pre_first_kernel, devices, read_first), "outgoing_in", steps,
        [
            (info, "smem"), (alive, None), (pair, 0), (tri_cols(OUTGOING), None),
            (turned((OUTGOING, PROJ_GATE)), None),
        ],
        [(product_shape, BF16, 3)], [product_scratch], 13,
    )
    between(0, product[0])
    product_one = swap_all(product)
    tri_one = products(
        "outgoing_product", functools.partial(tri_product_kernel, False), [product_one], tri_half
    )
    tri_one = by_hidden(swap_all(tri_one))
    tri_one = [tri_one[0], *meet(0, tri_one[1])]
    state_one, product = run_halves(
        functools.partial(tri_join_kernel, devices, read_first), "outgoing_out_incoming_in", steps,
        [
            ([info[:half], info[half:]], "smem"), (alive, None), (pair, 0), (tri_one, 1), (tri_cols(OUTGOING), None),
            (turned((OUTGOING, PROJ_OUT)), None), (turned((OUTGOING, GATE_OUT)), None),
            (tri_cols(INCOMING), None), (turned((INCOMING, PROJ_GATE)), None),
        ],
        [(state_shape, F32, 0), (product_half, BF16, 3)], [tri_scratch, product_scratch], 22,
    )
    product_two = list(meet(1, *swap_all(product)))
    tri_two = products(
        "incoming_product", functools.partial(tri_product_kernel, True), [product_two], tri_shape
    )
    tri_two = by_hidden(swap_all(tri_two))
    between(1, None)
    (tri_two,) = meet(2, *tri_two)
    cotangent = cotangent.reshape(rows, parts, cores, parts, -1, width).transpose(3, 2, 1, 4, 0, 5)
    cotangent = send(cotangent.reshape(flip_shape), group)
    state_two, bias = run_rows(
        tri_last_kernel, "incoming_out_starting_bias", steps,
        [
            (state_one, 0), (tri_two, 1), (tri_cols(INCOMING), None),
            (turned((INCOMING, PROJ_OUT)), None), (turned((INCOMING, GATE_OUT)), None),
            (cols(STARTING), None), (weights[(STARTING, BIAS_T)], None),
        ],
        [(state_shape, F32, 0), ((TA_HEADS, rows, length), BF16, 1)], [tri_scratch, head_scratch],
    )
    (bias,) = meet(7, bias)
    bias_one = lax.all_gather(bias, group, axis=0, tiled=False)
    flipped, totals_one, mixed_one, bias = run_rows(
        starting_kernel, "starting_attention", steps,
        [
            (alive, None), (state_two, 0), (bias_one, None), (cols(STARTING), None),
            (turned((STARTING, QKVG)), None), (turned((STARTING, OUTPUT)), None), (cols(ENDING), None),
            (weights[(ENDING, BIAS_T)], None),
        ],
        [(flip_shape, BF16, 2)] + attend_saves + [((TA_HEADS, rows, length), BF16, 1)],
        [table, flip_scratch, head_scratch], 21,
    )
    state_three = Both([send(flipped, group)])
    bias_two = lax.all_gather(bias, group, axis=0, tiled=False)
    cotangent, bias_two = after(cotangent, bias_two)
    cotangent = send(cotangent.reshape((parts, cores) + flip_shape[1:]), "z").reshape(flip_shape)
    state_four, totals_two, mixed_two = run_rows(
        ending_kernel, "ending_attention", steps,
        [
            (alive, None), (state_three, 1), (bias_two, None), (cols(ENDING), None),
            (turned((ENDING, QKVG)), None), (turned((ENDING, OUTPUT)), None),
        ],
        [(state_shape, F32, 0)] + attend_saves, [table],
    )
    pair_cols, attend_cols = cols(PAIR), cols(ATTEND)
    state_five, pair_out, single_bias = run_rows(
        functools.partial(transition_kernel, order_back), "pair_transition", steps,
        [
            (state_four, 0), (pair_cols, None), (turned((PAIR, UP)), None), (turned((PAIR, DOWN)), None),
            (attend_cols, None), (turned((ATTEND, PAIR_PROJ)), None),
        ],
        [(state_shape, F32, 0), ((length, rows, width), BF16, 1), ((devices, rows, SA_HEADS * rows), BF16, 1)],
        [flip_scratch, ((SA_HEADS, block, length), F32)],
    )
    single_sent = send(middle(send(single_bias, group)), group)
    between(2, single_sent)
    pair_out = send(pair_out.reshape((parts, -1) + pair_out.shape[1:]), "z")
    grads = {}
    grad_four, grads[(PAIR, UP)], grads[(PAIR, DOWN)], grads[(ATTEND, PAIR_PROJ)], vecs = run_rows(
        functools.partial(transition_back_kernel, read_last), "pair_transition_back", steps,
        [
            (state_four, 0), (state_five, 0), (cotangent, 1), (single_sent, 1),
            (pair_cols, None), (turned((PAIR, UP)), None), (weights[(PAIR, UP)], None),
            (weights[(PAIR, DOWN)], None), (attend_cols, None), (weights[(ATTEND, PAIR_PROJ)], None),
        ],
        [
            (state_shape, F32, 0), (weights[(PAIR, UP)].shape, F32, None),
            (weights[(PAIR, DOWN)].shape, F32, None), (weights[(ATTEND, PAIR_PROJ)].shape, F32, None),
            ((8, width), F32, None),
        ],
        [wide, wide, wide, wide, ((SA_HEADS, block, length), F32)], 30,
    )
    grads[(PAIR, VECTORS)] = vecs

    def attention_back(prefix, read, read_grad, source, source_axis, grad, grad_axis, bias, totals, mixed):
        lowered_grad, bias_grad, grads[(prefix, QKVG)], grads[(prefix, OUTPUT)] = run_rows(
            functools.partial(attention_back_kernel, prefix == ENDING, read, read_grad),
            "attention_back", steps,
            [
                (alive, None), (source, source_axis), (grad, grad_axis), (bias, None), (totals, 0),
                (mixed, 0), (cols(prefix), None), (turned((prefix, QKVG)), None),
                (weights[(prefix, QKVG)], None), (weights[(prefix, OUTPUT)], None),
            ],
            [
                (state_shape, BF16, 0), ((devices, TA_HEADS, rows, length), BF16, None),
                (weights[(prefix, QKVG)].shape, F32, None), (weights[(prefix, OUTPUT)].shape, F32, None),
            ],
            [table, table], 34,
        )
        return lowered_grad, send(bias_grad, group)

    lowered_grad, bias_grad = attention_back(
        ENDING, read_flipped, read_plain, state_three, 1, grad_four, 0, bias_two, totals_two, mixed_two
    )
    (bias_grad,) = meet(8, bias_grad)
    flipped, bias_w_grad, vecs = run_rows(
        ending_end_kernel, "ending_attention_end", steps,
        [
            (state_three, 1), (grad_four, 0), (lowered_grad, 0), (bias_grad, 2), (cols(ENDING), None),
            (weights[(ENDING, BIAS_W)], None),
        ],
        [(flip_shape, BF16, 2), ((width, 8), F32, None), ((8, width), F32, None)],
        [wide, wide, head_scratch, flip_scratch],
    )
    grads[(ENDING, BIAS_PROJ)], grads[(ENDING, VECTORS)] = bias_w_grad, vecs
    flipped, held = after(flipped, grads[(ATTEND, PAIR_PROJ)])
    grads[(ATTEND, PAIR_PROJ)] = held
    grad_three = send(flipped, group)
    between(4, grads)
    grad_three = Both(meet(3, grad_three))
    pair_out = send(pair_out.reshape(flip_shape), group)
    pair_out = pair_out.reshape(parts, cores, rows, parts, -1, width).transpose(2, 3, 1, 0, 4, 5)
    pair_out = pair_out.reshape(rows, length, width)
    lowered_grad, bias_grad = attention_back(
        STARTING, read_plain, read_flipped, state_two, 0, grad_three, 1, bias_one, totals_one, mixed_one
    )
    square = weights[(INCOMING, GATE_OUT)].shape
    (
        grad_two, grad_tri, gate_back, bias_w_grad, grads[(INCOMING, PROJ_OUT)], grads[(INCOMING, GATE_OUT)], vecs,
    ) = run_halves(
        starting_end_kernel, "starting_end_incoming_out_back", steps,
        [
            (state_two, 0), (grad_three, 1), (lowered_grad, 0), (bias_grad, 2), (cols(STARTING), None),
            (weights[(STARTING, BIAS_W)], None), (state_one, 0), (tri_two, 1), (tri_cols(INCOMING), None),
            (turned((INCOMING, PROJ_OUT)), None), (turned((INCOMING, GATE_OUT)), None),
            (weights[(INCOMING, PROJ_OUT)], None), (weights[(INCOMING, GATE_OUT)], None),
        ],
        [
            (state_shape, F32, 0), ((hidden, half, length), BF16, 1), (state_shape, BF16, 0),
            ((width, 8), F32, None), (square, F32, None), (square, F32, None), ((8, width), F32, None),
        ],
        [wide, wide, wide, wide, head_scratch, tri_scratch], 26,
    )
    grads[(STARTING, BIAS_PROJ)], grads[(STARTING, VECTORS)] = bias_w_grad, vecs
    grad_tri = swap_all(by_device(grad_tri))
    product_grad = products(
        "incoming_product_back", functools.partial(tri_product_back_kernel, True),
        [grad_tri, product_two], product_half,
    )
    product_grad = swap_all(product_grad)
    product_grad = [*meet(4, product_grad[0]), product_grad[1]]
    (
        grad_one, grad_tri, gate_back, grads[(INCOMING, PROJ_GATE)], grads[(OUTGOING, PROJ_OUT)],
        grads[(OUTGOING, GATE_OUT)], vecs,
    ) = run_halves(
        functools.partial(tri_join_back_kernel, read_first), "incoming_in_outgoing_out_back", steps,
        [
            ([info[:half], info[half:]], "smem"), (alive, None), (state_one, 0), (product_grad, 3), (gate_back, 0), (grad_two, 0),
            (tri_cols(INCOMING), None), (turned((INCOMING, PROJ_GATE)), None),
            (weights[(INCOMING, PROJ_GATE)], None), (pair, 0), (tri_one, 1), (tri_cols(OUTGOING), None),
            (turned((OUTGOING, PROJ_OUT)), None), (turned((OUTGOING, GATE_OUT)), None),
            (weights[(OUTGOING, PROJ_OUT)], None), (weights[(OUTGOING, GATE_OUT)], None),
        ],
        [
            (state_shape, F32, 0), ((hidden, half, length), BF16, 1), (state_shape, BF16, 0),
            (weights[(INCOMING, PROJ_GATE)].shape, F32, None), (square, F32, None), (square, F32, None),
            ((8, width), F32, None),
        ],
        [wide, wide, wide, wide, product_scratch, tri_scratch], 37,
    )
    grads[(INCOMING, VECTORS)] = vecs
    between(5, grads)
    grad_tri = swap_all(by_device(grad_tri))
    grad_tri = [grad_tri[0], *meet(5, grad_tri[1])]
    product_grad = products(
        "outgoing_product_back", functools.partial(tri_product_back_kernel, False),
        [grad_tri, product_one], product_shape,
    )
    (product_grad,) = swap_all(product_grad)
    between(6, grads)
    pair_grad, grads[(OUTGOING, PROJ_GATE)], vecs = run_rows(
        functools.partial(tri_first_back_kernel, read_first, order_back), "outgoing_in_back", steps,
        [
            (info, "smem"), (alive, None), (pair, 0), (product_grad, 3), (gate_back, 0), (grad_one, 0),
            (tri_cols(OUTGOING), None), (turned((OUTGOING, PROJ_GATE)), None),
            (weights[(OUTGOING, PROJ_GATE)], None),
        ],
        [
            ((rows, length, width), BF16, 0), (weights[(OUTGOING, PROJ_GATE)].shape, F32, None),
            ((8, width), F32, None),
        ],
        [wide, wide, product_scratch], 20,
    )
    grads[(OUTGOING, VECTORS)] = vecs
    return pair_out, pair_grad, grads


HELD = {
    (PAIR, VECTORS): ((PAIR, NORM_GAIN), (PAIR, NORM_BIAS), (ATTEND, PAIR_GAIN), (ATTEND, PAIR_BIAS)),
    (ENDING, VECTORS): ((ENDING, NORM_GAIN), (ENDING, NORM_BIAS)),
    (STARTING, VECTORS): (
        (STARTING, NORM_GAIN), (STARTING, NORM_BIAS), (INCOMING, OUT_GAIN), (INCOMING, OUT_BIAS)
    ),
    (INCOMING, VECTORS): (
        (INCOMING, NORM_GAIN), (INCOMING, NORM_BIAS), (OUTGOING, OUT_GAIN), (OUTGOING, OUT_BIAS)
    ),
    (OUTGOING, VECTORS): ((OUTGOING, NORM_GAIN), (OUTGOING, NORM_BIAS)),
}


def vector_part(grads, table, name, first, last):
    pairs = [
        (row, held) for row, held in enumerate(HELD[name]) if first <= table[held][0] < last
    ]
    return (pairs, grads[name])


def fast_shards(parts, cores, pair, single, lengths, params, moment_one, moment_two, pair_cotangent, single_cotangent):
    entries = layout(C, H, S, TA_HEADS, SA_HEADS)
    table, total = table_of(entries)
    count = total // STRIDE
    shard_size = params.shape[0]
    attend = table[(ATTEND, NORM_GAIN)][0]
    pair_lanes = -(-attend * STRIDE // count)
    single_lane = attend * STRIDE // count
    devices = parts * cores
    line, group = ("z", "core"), ("crop", "core")
    row_index = lax.axis_index(line)
    odd = ((row_index * shard_size) % STRIDE) // (STRIDE // 2)
    place = jnp.stack([odd, odd]).astype(jnp.int32)
    shard_rows = jnp.pad(params, (0, RUN * STRIDE * STRIDE - shard_size)).reshape(-1, STRIDE)
    (runs,) = whole_call(
        runs_kernel, "parameter_runs", [(place, "smem"), (shard_rows, None)],
        [((STRIDE, RUN, STRIDE), BF16)], [((STRIDE, RUN, STRIDE), F32)],
    )
    rows, length, width = pair.shape[1:]
    send = in_turn()
    pair_in = send(pair[0].reshape(parts, -1, length, width), "crop")
    first_runs = lax.all_gather(runs[:pair_lanes], line)
    pair_in, _, lengths = after(pair_in, runs, lengths)
    live = lax.all_gather(jnp.broadcast_to(lengths.astype(F32), (8, STRIDE)), "crop")
    pair_in = send(pair_in, "z").reshape(rows, length, width)
    weights = unpack_pair(table, total, first_runs)
    size = rows // parts
    blocks = np.arange(length // size).reshape(parts, cores, parts)
    order = blocks.transpose(2, 1, 0).reshape(-1)
    orders = (order.tolist(), np.argsort(order).tolist())
    tokens = (order[:, None] * size + np.arange(size)).reshape(-1)
    live = live[lax.axis_index("z"), 0, 0]
    width = single.shape[2]
    mask = (tokens.astype(np.float32) < live).astype(F32)
    info = lax.dynamic_slice_in_dim(mask, lax.axis_index(group) * rows, rows).astype(jnp.int32)
    alive = jnp.broadcast_to(mask, (8, length))
    held = {}
    single_grads = {}

    def middle(bias):
        found = single_middle(held["state"], held["back"], held["projected"], bias, alive, weights)
        held["out"], held["grad"], grad_scores, grads, held["pending"] = found
        single_grads.update(grads)
        return grad_scores

    def meet(number, *values):
        if number == 0:
            others = [held["runs"]]
        elif number == 1:
            others = [weights[(SINGLE, UP)], held["state"]]
        elif number == 2:
            others = [held["projected"][1]]
        elif number == 3:
            others = [reduced[3]]
        elif number == 7:
            others = [held["projected"][2]]
        elif number == 8:
            others = [single_grads[(ATTEND, QKVG)]]
        elif number == 4:
            values, reduced[2] = after(*values, reduced[2])
            return [values]
        else:
            values, held["both"], reduced[1] = after(*values, held["both"], reduced[1])
            return [values]
        return after(*values, *others)[: len(values)]

    def reduce_runs(sent):
        return jnp.sum(send(sent, line).astype(F32), axis=0).astype(BF16)

    reduced = {}
    lines_held = list(enumerate(SINGLE_VECTORS))
    late_lanes = -(-table[(OUTGOING, OUT_GAIN)][0] * STRIDE // count)
    late_end = table[(OUTGOING, GATE_OUT)][0]
    early = table[(OUTGOING, PROJ_OUT)][0]

    def lines():
        values = jnp.concatenate([single_grads[name].reshape(1, S) for name in SINGLE_VECTORS], axis=0)
        return jnp.pad(values, ((0, 8 - len(SINGLE_VECTORS)), (0, 0)))

    def between(number, grads):
        if number == 0:
            last_runs = after(runs[single_lane:], pair_in, weights[(OUTGOING, COLS)], live)[0]
            held["runs"] = lax.all_gather(last_runs, line)
            weights.update(unpack_single(table, total, single_lane, held["runs"]))
            for index, name in enumerate(SINGLE_VECTORS):
                weights[name] = weights[(SINGLE, VECTORS)][index]
            both = jnp.concatenate([single[0], single_cotangent[0]], axis=1)
            both = lax.all_gather(both, ("crop",) + line)
            both = both.reshape(parts, parts, cores, parts, -1, 2 * width)
            here = lax.axis_index("z"), lax.axis_index("core"), lax.axis_index("crop")
            both = both[here[0], :, here[1], here[2]].reshape(rows, 2 * width).astype(F32)
            held["state"], held["back"] = both[:, :width], both[:, width:]
            return
        if number == 1:
            lowered, qkvg, both = single_project(held["state"], weights, devices)
            held["projected"] = lowered, qkvg, send(both, group)
            return
        if number == 2:
            parts_held = grads[:, :, SA_HEADS * rows :]
            grad = held["grad"] + single_attend_end(held["pending"], parts_held, weights, single_grads)
            both = jnp.concatenate([held["out"], grad], axis=1).astype(BF16)
            held["both"] = lax.all_gather(both, ("crop",) + line)
            return
        if number == 6:
            reduced[1] = reduce_runs(reduced[1])
            return
        if number == 4:
            sent = pack(
                "single_gradient", table, total, devices, (pair_lanes, STRIDE), attend,
                [(name, single_grads[name]) for name in SINGLE_MATRICES]
                + [((ATTEND, PAIR_PROJ), grads[(ATTEND, PAIR_PROJ)])]
                + [vector_part(grads, table, (PAIR, VECTORS), attend, total), (lines_held, lines())],
            )
            reduced[3] = sent
            sent = sent.reshape((devices * parts, -1) + sent.shape[2:])
            reduced[2] = lax.psum_scatter(sent, line + ("crop",), scatter_dimension=0, tiled=False)
            return
        taken = -(-(pair_lanes * count - (attend + 2 * S // STRIDE) * STRIDE) // (4 * S))
        sent = pack(
            "pair_gradient", table, total, devices, (late_lanes, pair_lanes), early,
            [(name, grads[name]) for name in PAIR_MATRICES if table[name][0] >= early]
            + [(name, grads[name]) for name in ((STARTING, BIAS_PROJ), (ENDING, BIAS_PROJ))]
            + [vector_part(grads, table, name, early, attend) for name in HELD if name in grads]
            + [(lines_held[:2], lines()), ((ATTEND, QKVG), single_grads[(ATTEND, QKVG)][: -(-taken // 8) * 8])],
        )
        reduced[1] = sent

    pair_out, pair_grad, grads = pair_path(
        pair_in, info, alive, orders, weights, pair_cotangent[0], middle, between, meet, send, group, parts
    )
    sent = pack(
        "outgoing_gradient", table, total, devices, (0, late_lanes), 0,
        [(name, grads[name]) for name in PAIR_MATRICES if table[name][0] < late_end]
        + [vector_part(grads, table, name, 0, late_end) for name in ((OUTGOING, VECTORS), (INCOMING, VECTORS))],
    )
    reduced[0] = reduce_runs(sent)
    pair_grad = send(pair_grad.reshape(parts, -1, length, pair_grad.shape[2]), "z")
    pair_grad, held["z"] = send(pair_grad, "crop").reshape(rows, length, -1).astype(F32), pair_grad
    both = held["both"].reshape(parts, parts, cores, parts, -1, 2 * width)
    both = both[:, lax.axis_index("crop"), lax.axis_index("core"), lax.axis_index("z")]
    both = both.reshape(rows, 2 * width)
    single_out, single_grad = both[:, :width], both[:, width:].astype(F32)
    summed = lax.all_gather(jnp.concatenate([reduced[0], reduced[1]], axis=0), "crop")
    others = lax.all_gather(reduced[2], "crop")
    shard, squares = whole_call(
        functools.partial(shard_kernel, shard_size), "gradient_share",
        [(place, "smem"), (summed, None), (others, None)],
        [((RUN * STRIDE, STRIDE), F32), ((8, STRIDE), F32)], [((STRIDE, RUN, STRIDE), F32)],
    )
    shard = shard.reshape(-1)[:shard_size]
    squares = after(squares, held["z"])[0]
    clip_norm = jnp.sqrt(jnp.sum(lax.all_gather(squares, line)))
    clipped = shard * (CLIP / jnp.maximum(clip_norm, CLIP))
    new_first = BETA_ONE * moment_one + (1.0 - BETA_ONE) * clipped
    new_second = BETA_TWO * moment_two + (1.0 - BETA_TWO) * clipped * clipped
    rates, decays = rate_tables(entries)
    rate_shard = lax.dynamic_slice_in_dim(jnp.asarray(rates), row_index * shard_size, shard_size)
    decay_shard = lax.dynamic_slice_in_dim(jnp.asarray(decays), row_index * shard_size, shard_size)
    first_hat = new_first / (1.0 - BETA_ONE**STEP)
    second_hat = new_second / (1.0 - BETA_TWO**STEP)
    new_params = params - rate_shard * (
        first_hat / (jnp.sqrt(second_hat) + ADAM_EPS) + decay_shard * params
    )
    return (
        pair_out[None],
        single_out[None],
        pair_grad[None],
        single_grad[None],
        new_params,
        new_first,
        new_second,
        clip_norm,
    )


def solution(mesh):
    crops, devices = mesh.devices.shape
    table, total = table_of(layout(C, H, S, TA_HEADS, SA_HEADS))
    count = total // STRIDE
    lanes = STRIDE + -table[(ATTEND, NORM_GAIN)][0] * STRIDE // count
    fast = devices == 2 * crops and LENGTH % (devices * 16) == 0 and count // devices + 2 <= RUN * STRIDE and lanes % crops == 0
    row = "row"
    if fast:
        mesh = jax.sharding.Mesh(mesh.devices.reshape(crops, crops, 2), ("crop", "z", "core"))
        row = ("z", "core")
    split = [P("crop", row, None, None), P("crop", row, None), P("crop"), P(row)]
    pair, single, lengths, share = split
    return jax.shard_map(
        functools.partial(fast_shards, crops, 2) if fast else shards,
        mesh=mesh,
        in_specs=(pair, single, lengths, share, share, share, pair, single),
        out_specs=(pair, single, pair, single, share, share, share, P()),
        check_vma=False,
    )
```

```python
import functools
import math

import jax
import jax.numpy as jnp
import numpy as np
from jax import lax
from jax.experimental import pallas as pl
from jax.experimental.pallas import tpu as pltpu
from jax.sharding import PartitionSpec as P

C = 128
H = 128
S = 384
TA_HEADS = 4
SA_HEADS = 16
STEP = 10
STRIDE = 128
LENGTH = 256

OUTGOING, INCOMING, STARTING, ENDING, PAIR, ATTEND, SINGLE = range(7)
(
    NORM_GAIN,
    NORM_BIAS,
    PROJ_GATE,
    OUT_GAIN,
    OUT_BIAS,
    PROJ_OUT,
    GATE_OUT,
    QKVG,
    BIAS_PROJ,
    OUTPUT,
    UP,
    DOWN,
    PAIR_GAIN,
    PAIR_BIAS,
    PAIR_PROJ,
    COLS,
    BIAS_W,
    BIAS_T,
    VECTORS,
    T,
) = range(7, 27)


EPSILON = 1e-05
MASKED = 1000000000.0
BETA_ONE = 0.9
BETA_TWO = 0.95
ADAM_EPS = 1e-08
CLIP = 1.0


def layout(pair_width, hidden_width, single_width, tri_heads, att_heads):
    entries = []
    for prefix in (OUTGOING, INCOMING):
        entries += [
            ((prefix, NORM_GAIN), (pair_width,)),
            ((prefix, NORM_BIAS), (pair_width,)),
            ((prefix, PROJ_GATE), (pair_width, 4 * hidden_width)),
            ((prefix, OUT_GAIN), (hidden_width,)),
            ((prefix, OUT_BIAS), (hidden_width,)),
            ((prefix, PROJ_OUT), (hidden_width, pair_width)),
            ((prefix, GATE_OUT), (pair_width, pair_width)),
        ]
    for prefix in (STARTING, ENDING):
        entries += [
            ((prefix, NORM_GAIN), (pair_width,)),
            ((prefix, NORM_BIAS), (pair_width,)),
            ((prefix, QKVG), (pair_width, 4 * pair_width)),
            ((prefix, BIAS_PROJ), (pair_width, tri_heads)),
            ((prefix, OUTPUT), (pair_width, pair_width)),
        ]
    entries += [
        ((PAIR, NORM_GAIN), (pair_width,)),
        ((PAIR, NORM_BIAS), (pair_width,)),
        ((PAIR, UP), (pair_width, 8 * pair_width)),
        ((PAIR, DOWN), (4 * pair_width, pair_width)),
        ((ATTEND, NORM_GAIN), (single_width,)),
        ((ATTEND, NORM_BIAS), (single_width,)),
        ((ATTEND, QKVG), (single_width, 4 * single_width)),
        ((ATTEND, PAIR_GAIN), (pair_width,)),
        ((ATTEND, PAIR_BIAS), (pair_width,)),
        ((ATTEND, PAIR_PROJ), (pair_width, att_heads)),
        ((ATTEND, OUTPUT), (single_width, single_width)),
        ((SINGLE, NORM_GAIN), (single_width,)),
        ((SINGLE, NORM_BIAS), (single_width,)),
        ((SINGLE, UP), (single_width, 8 * single_width)),
        ((SINGLE, DOWN), (4 * single_width, single_width)),
    ]
    return entries


def logical_order(flat):
    return flat.reshape(-1, STRIDE).T.reshape(-1)


def stored_order(vector):
    return vector.reshape(STRIDE, -1).T.reshape(-1)


def rate_tables(entries):
    rates = []
    decays = []
    for name, shape in entries:
        count = math.prod(shape)
        if len(shape) == 1:
            rates.append(np.full(count, 0.5, np.float32))
            decays.append(np.zeros(count, np.float32))
        else:
            rates.append(np.full(count, 2.0 / math.sqrt(shape[0]), np.float32))
            decays.append(np.full(count, 0.01, np.float32))
    rates = np.concatenate(rates)
    decays = np.concatenate(decays)
    return (rates.reshape(STRIDE, -1).T.reshape(-1), decays.reshape(STRIDE, -1).T.reshape(-1))


def unpack(flat, entries):
    pieces = {}
    offset = 0
    for name, shape in entries:
        count = math.prod(shape)
        pieces[name] = flat[offset : offset + count].reshape(shape)
        offset += count
    return pieces


def layer_norm(values, gain, shift):
    centred = values - jnp.mean(values, axis=-1, keepdims=True)
    spread = jnp.mean(centred * centred, axis=-1, keepdims=True)
    return centred * lax.rsqrt(spread + EPSILON) * gain + shift


def norm_backward(values, gain, shift, grad):
    _, pullback = jax.vjp(layer_norm, values, gain, shift)
    return pullback(grad)


def norm_pair(weights, prefix):
    return (
        weights[(prefix, NORM_GAIN)].astype(jnp.float32),
        weights[(prefix, NORM_BIAS)].astype(jnp.float32),
    )


def gated_pair(project, pair_mask):
    half = project.shape[-1] // 2
    return project[..., :half] * jax.nn.sigmoid(project[..., half:]) * pair_mask[..., None]


def gated_output(values, gate):
    return values * jax.nn.sigmoid(gate)


def swiglu(hidden):
    half = hidden.shape[-1] // 2
    return jax.nn.silu(hidden[..., :half]) * hidden[..., half:]


def matmul(left, right):
    return jnp.dot(left, right, preferred_element_type=jnp.float32)


def outer_sum(left, right):
    return jnp.einsum(
        "nc,nd->cd",
        left.reshape(-1, left.shape[-1]),
        right.reshape(-1, right.shape[-1]),
        preferred_element_type=jnp.float32,
    )


def flip(values):
    moved = lax.all_to_all(values, "row", split_axis=1, concat_axis=0, tiled=True)
    return jnp.swapaxes(moved, 0, 1)


def channel_forward(first, second, incoming):
    whole_first, whole_second = (
        lax.all_to_all(first, "row", split_axis=2, concat_axis=0, tiled=True),
        lax.all_to_all(second, "row", split_axis=2, concat_axis=0, tiled=True),
    )
    if incoming:
        local_tri = jnp.einsum(
            "kih,kjh->ijh", whole_first, whole_second, preferred_element_type=jnp.float32
        )
        local_tri = local_tri.astype(jnp.bfloat16).astype(jnp.float32)
    else:
        local_tri = jnp.einsum(
            "ikh,jkh->ijh", whole_first, whole_second, preferred_element_type=jnp.float32
        )
    tri = lax.all_to_all(
        local_tri.astype(jnp.bfloat16), "row", split_axis=0, concat_axis=2, tiled=True
    ).astype(local_tri.dtype)
    return (tri, whole_first, whole_second)


def channel_backward(grad_tri, whole_first, whole_second, incoming):
    whole_grad = lax.all_to_all(grad_tri, "row", split_axis=2, concat_axis=0, tiled=True)
    if incoming:
        grad_a = jnp.einsum(
            "ijh,kjh->kih", whole_grad, whole_second, preferred_element_type=jnp.float32
        )
        grad_b = jnp.einsum(
            "ijh,kih->kjh", whole_grad, whole_first, preferred_element_type=jnp.float32
        )
    else:
        grad_a = jnp.einsum(
            "ijh,jkh->ikh", whole_grad, whole_second, preferred_element_type=jnp.float32
        )
        grad_b = jnp.einsum(
            "ijh,ikh->jkh", whole_grad, whole_first, preferred_element_type=jnp.float32
        )
    return (
        lax.all_to_all(
            grad_a.astype(jnp.bfloat16), "row", split_axis=0, concat_axis=2, tiled=True
        ).astype(grad_a.dtype),
        lax.all_to_all(
            grad_b.astype(jnp.bfloat16), "row", split_axis=0, concat_axis=2, tiled=True
        ).astype(grad_b.dtype),
    )


def triangle_forward(state, pair_mask, weights, prefix, incoming):
    gain, shift = norm_pair(weights, prefix)
    lowered = layer_norm(state, gain, shift).astype(jnp.bfloat16)
    project = matmul(lowered, weights[(prefix, PROJ_GATE)])
    product = gated_pair(project, pair_mask).astype(jnp.bfloat16)
    half = product.shape[-1] // 2
    tri, own, other = channel_forward(product[..., :half], product[..., half:], incoming)
    out_gain = weights[(prefix, OUT_GAIN)].astype(jnp.float32)
    out_shift = weights[(prefix, OUT_BIAS)].astype(jnp.float32)
    out_low = layer_norm(tri, out_gain, out_shift).astype(jnp.bfloat16)
    output = matmul(out_low, weights[(prefix, PROJ_OUT)])
    gate_out = matmul(lowered, weights[(prefix, GATE_OUT)])
    update = gated_output(output, gate_out)
    return (update, (state, lowered, lowered, project, own, other, tri, out_low, output, gate_out))


def triangle_backward(saved, grad_update, pair_mask, weights, prefix, incoming, grads):
    state, lowered, framed, project, own, other, tri, out_low, output, gate_out = saved
    _, pullback = jax.vjp(gated_output, output, gate_out)
    grad_output, grad_gate = pullback(grad_update)
    grad_output = grad_output.astype(jnp.bfloat16)
    grad_gate = grad_gate.astype(jnp.bfloat16)
    grads[(prefix, PROJ_OUT)] = outer_sum(out_low, grad_output)
    grads[(prefix, GATE_OUT)] = outer_sum(lowered, grad_gate)
    grad_normed = matmul(grad_output, weights[(prefix, PROJ_OUT)].T)
    out_gain = weights[(prefix, OUT_GAIN)].astype(jnp.float32)
    out_shift = weights[(prefix, OUT_BIAS)].astype(jnp.float32)
    grad_tri, grads[(prefix, OUT_GAIN)], grads[(prefix, OUT_BIAS)] = norm_backward(
        tri, out_gain, out_shift, grad_normed
    )
    grad_tri = grad_tri.astype(jnp.bfloat16)
    grad_first, grad_second = channel_backward(grad_tri, own, other, incoming)
    _, pullback = jax.vjp(lambda values: gated_pair(values, pair_mask), project)
    (grad_project,) = pullback(jnp.concatenate([grad_first, grad_second], axis=-1))
    grad_project = grad_project.astype(jnp.bfloat16)
    grads[(prefix, PROJ_GATE)] = outer_sum(framed, grad_project)
    grad_framed = matmul(grad_project, weights[(prefix, PROJ_GATE)].T)
    if incoming:
        grad_framed = grad_framed.astype(jnp.bfloat16).astype(jnp.float32)
    grad_lowered = grad_framed + matmul(grad_gate, weights[(prefix, GATE_OUT)].T)
    gain, shift = norm_pair(weights, prefix)
    grad_state, grads[(prefix, NORM_GAIN)], grads[(prefix, NORM_BIAS)] = norm_backward(
        state, gain, shift, grad_lowered
    )
    return grad_state


def row_scores(query, key, bias, penalty, scale):
    scores = jnp.einsum("jhd,khd->hjk", query, key, preferred_element_type=jnp.float32) * scale
    return scores + bias.astype(jnp.float32) + penalty[None, None, :]


def attention_forward(state, penalty, weights, prefix, ending):
    gain, shift = norm_pair(weights, prefix)
    lowered = layer_norm(state, gain, shift).astype(jnp.bfloat16)
    framed = flip(lowered) if ending else lowered
    rows, length, width = framed.shape
    size = width // TA_HEADS
    scale = size ** (-0.5)
    qkvg = matmul(framed, weights[(prefix, QKVG)])
    queries = qkvg[..., :width].astype(jnp.bfloat16).reshape(rows, length, TA_HEADS, size)
    keys = qkvg[..., width : 2 * width].astype(jnp.bfloat16).reshape(rows, length, TA_HEADS, size)
    values = (
        qkvg[..., 2 * width : 3 * width].astype(jnp.bfloat16).reshape(rows, length, TA_HEADS, size)
    )
    gate = qkvg[..., 3 * width :]
    local_bias = (
        matmul(framed, weights[(prefix, BIAS_PROJ)]).astype(jnp.bfloat16).transpose(2, 0, 1)
    )
    bias = lax.all_gather(local_bias, "row", axis=1, tiled=True)

    def forward_row(items):
        query, key, value = items
        scores = row_scores(query, key, bias, penalty, scale)
        top = jnp.max(scores, axis=-1, keepdims=True)
        shifted = jnp.exp(scores - top)
        total = jnp.sum(shifted, axis=-1, keepdims=True)
        probs = (shifted / total).astype(jnp.bfloat16)
        mixed = jnp.einsum("hjk,khd->jhd", probs, value, preferred_element_type=jnp.float32)
        return (mixed, top[..., 0] + jnp.log(total[..., 0]))

    mixed, log_totals = lax.map(forward_row, (queries, keys, values))
    mixed = mixed.reshape(rows, length, width)
    gated_low = gated_output(mixed, gate).astype(jnp.bfloat16)
    returned = flip(gated_low) if ending else gated_low
    update = matmul(returned, weights[(prefix, OUTPUT)])
    return (update, (state, framed, queries, keys, values, gate, bias, mixed, log_totals, returned))


def attention_backward(saved, grad_update, penalty, weights, prefix, ending, grads):
    state, framed, queries, keys, values, gate, bias, mixed, log_totals, returned = saved
    rows, length, width = framed.shape
    size = width // TA_HEADS
    scale = size ** (-0.5)
    grad_low = grad_update.astype(jnp.bfloat16)
    grads[(prefix, OUTPUT)] = outer_sum(returned, grad_low)
    grad_gated = matmul(grad_low, weights[(prefix, OUTPUT)].T)
    if ending:
        grad_gated = flip(grad_gated.astype(jnp.bfloat16)).astype(jnp.float32)
    _, pullback = jax.vjp(gated_output, mixed, gate)
    grad_mixed, grad_gate = pullback(grad_gated)
    grad_mixed = grad_mixed.astype(jnp.bfloat16).reshape(rows, length, TA_HEADS, size)

    def back_row(carry, items):
        query, key, value, log_total, grad_row = items
        scores = row_scores(query, key, bias, penalty, scale)
        probs = jnp.exp(scores - log_total[..., None])
        grad_probs = jnp.einsum("jhd,khd->hjk", grad_row, value, preferred_element_type=jnp.float32)
        delta = jnp.sum(probs * grad_probs, axis=-1, keepdims=True)
        grad_scores = (probs * (grad_probs - delta)).astype(jnp.bfloat16)
        grad_query = (
            jnp.einsum("hjk,khd->jhd", grad_scores, key, preferred_element_type=jnp.float32) * scale
        )
        grad_key = (
            jnp.einsum("hjk,jhd->khd", grad_scores, query, preferred_element_type=jnp.float32)
            * scale
        )
        grad_value = jnp.einsum(
            "hjk,jhd->khd", probs.astype(jnp.bfloat16), grad_row, preferred_element_type=jnp.float32
        )
        return (carry + grad_scores.astype(jnp.float32), (grad_query, grad_key, grad_value))

    empty = jnp.zeros(bias.shape, jnp.float32)
    grad_bias, (grad_query, grad_key, grad_value) = lax.scan(
        back_row, empty, (queries, keys, values, log_totals, grad_mixed)
    )
    grad_bias = lax.psum_scatter(grad_bias, "row", scatter_dimension=1, tiled=True)
    grad_bias = grad_bias.transpose(1, 2, 0).astype(jnp.bfloat16)
    grad_qkvg = jnp.concatenate(
        [
            grad_query.reshape(rows, length, width),
            grad_key.reshape(rows, length, width),
            grad_value.reshape(rows, length, width),
            grad_gate,
        ],
        axis=-1,
    ).astype(jnp.bfloat16)
    grads[(prefix, QKVG)] = outer_sum(framed, grad_qkvg)
    grads[(prefix, BIAS_PROJ)] = outer_sum(framed, grad_bias)
    grad_framed = matmul(grad_qkvg, weights[(prefix, QKVG)].T) + matmul(
        grad_bias, weights[(prefix, BIAS_PROJ)].T
    )
    if ending:
        grad_framed = flip(grad_framed.astype(jnp.bfloat16)).astype(jnp.float32)
    gain, shift = norm_pair(weights, prefix)
    grad_state, grads[(prefix, NORM_GAIN)], grads[(prefix, NORM_BIAS)] = norm_backward(
        state, gain, shift, grad_framed
    )
    return grad_state


def transition_forward(state, weights, prefix):
    gain, shift = norm_pair(weights, prefix)
    lowered = layer_norm(state, gain, shift).astype(jnp.bfloat16)
    hidden = matmul(lowered, weights[(prefix, UP)])
    mixed_low = swiglu(hidden).astype(jnp.bfloat16)
    update = matmul(mixed_low, weights[(prefix, DOWN)])
    return (update, (state, lowered, hidden, mixed_low))


def transition_backward(saved, grad_update, weights, prefix, grads):
    state, lowered, hidden, mixed_low = saved
    grad_low = grad_update.astype(jnp.bfloat16)
    grads[(prefix, DOWN)] = outer_sum(mixed_low, grad_low)
    grad_mixed = matmul(grad_low, weights[(prefix, DOWN)].T)
    _, pullback = jax.vjp(swiglu, hidden)
    (grad_hidden,) = pullback(grad_mixed)
    grad_hidden = grad_hidden.astype(jnp.bfloat16)
    grads[(prefix, UP)] = outer_sum(lowered, grad_hidden)
    grad_lowered = matmul(grad_hidden, weights[(prefix, UP)].T)
    gain, shift = norm_pair(weights, prefix)
    grad_state, grads[(prefix, NORM_GAIN)], grads[(prefix, NORM_BIAS)] = norm_backward(
        state, gain, shift, grad_lowered
    )
    return grad_state


def single_forward(single_state, pair_state, penalty, weights):
    gain, shift = norm_pair(weights, ATTEND)
    lowered = layer_norm(single_state, gain, shift).astype(jnp.bfloat16)
    rows, width = lowered.shape
    size = width // SA_HEADS
    qkvg = matmul(lowered, weights[(ATTEND, QKVG)])
    query = qkvg[:, :width].astype(jnp.bfloat16).reshape(rows, SA_HEADS, size)
    key = qkvg[:, width : 2 * width].astype(jnp.bfloat16)
    value = qkvg[:, 2 * width : 3 * width].astype(jnp.bfloat16)
    gate = qkvg[:, 3 * width :]
    keys_all, values_all = (
        lax.all_gather(key, "row", axis=0, tiled=True),
        lax.all_gather(value, "row", axis=0, tiled=True),
    )
    keys_all = keys_all.reshape(-1, SA_HEADS, size)
    values_all = values_all.reshape(-1, SA_HEADS, size)
    pair_gain = weights[(ATTEND, PAIR_GAIN)].astype(jnp.float32)
    pair_shift = weights[(ATTEND, PAIR_BIAS)].astype(jnp.float32)
    pair_low = layer_norm(pair_state, pair_gain, pair_shift).astype(jnp.bfloat16)
    bias = matmul(pair_low, weights[(ATTEND, PAIR_PROJ)]).transpose(2, 0, 1)
    scores = jnp.einsum(
        "ihd,jhd->hij", query, keys_all, preferred_element_type=jnp.float32
    ) * size ** (-0.5)
    scores = scores + bias + penalty[None, None, :]
    probs = jax.nn.softmax(scores, axis=-1)
    probs_low = probs.astype(jnp.bfloat16)
    mixed = jnp.einsum(
        "hij,jhd->ihd", probs_low, values_all, preferred_element_type=jnp.float32
    ).reshape(rows, width)
    gated_low = gated_output(mixed, gate).astype(jnp.bfloat16)
    update = matmul(gated_low, weights[(ATTEND, OUTPUT)])
    return (
        update,
        (
            single_state,
            pair_state,
            lowered,
            query,
            keys_all,
            values_all,
            gate,
            pair_low,
            probs,
            probs_low,
            mixed,
            gated_low,
        ),
    )


def single_backward(saved, grad_update, weights, grads):
    (
        single_state,
        pair_state,
        lowered,
        query,
        keys_all,
        values_all,
        gate,
        pair_low,
        probs,
        probs_low,
        mixed,
        gated_low,
    ) = saved
    rows, width = lowered.shape
    size = width // SA_HEADS
    scale = size ** (-0.5)
    grad_low = grad_update.astype(jnp.bfloat16)
    grads[(ATTEND, OUTPUT)] = outer_sum(gated_low, grad_low)
    grad_gated = matmul(grad_low, weights[(ATTEND, OUTPUT)].T)
    _, pullback = jax.vjp(gated_output, mixed, gate)
    grad_mixed, grad_gate = pullback(grad_gated)
    grad_mixed = grad_mixed.astype(jnp.bfloat16).reshape(rows, SA_HEADS, size)
    grad_probs = jnp.einsum(
        "ihd,jhd->hij", grad_mixed, values_all, preferred_element_type=jnp.float32
    )
    delta = jnp.sum(probs * grad_probs, axis=-1, keepdims=True)
    grad_scores = (probs * (grad_probs - delta)).astype(jnp.bfloat16)
    grad_query = (
        jnp.einsum("hij,jhd->ihd", grad_scores, keys_all, preferred_element_type=jnp.float32)
        * scale
    )
    key_part = (
        jnp.einsum("hij,ihd->jhd", grad_scores, query, preferred_element_type=jnp.float32) * scale
    )
    value_part = jnp.einsum(
        "hij,ihd->jhd", probs_low, grad_mixed, preferred_element_type=jnp.float32
    )
    grad_key, grad_value = (
        lax.psum_scatter(key_part.reshape(-1, width), "row", scatter_dimension=0, tiled=True),
        lax.psum_scatter(value_part.reshape(-1, width), "row", scatter_dimension=0, tiled=True),
    )
    grad_qkvg = jnp.concatenate(
        [grad_query.reshape(rows, width), grad_key, grad_value, grad_gate], axis=-1
    ).astype(jnp.bfloat16)
    grads[(ATTEND, QKVG)] = outer_sum(lowered, grad_qkvg)
    grad_lowered = matmul(grad_qkvg, weights[(ATTEND, QKVG)].T)
    gain, shift = norm_pair(weights, ATTEND)
    grad_single, grads[(ATTEND, NORM_GAIN)], grads[(ATTEND, NORM_BIAS)] = norm_backward(
        single_state, gain, shift, grad_lowered
    )
    grad_bias = grad_scores.transpose(1, 2, 0)
    grads[(ATTEND, PAIR_PROJ)] = outer_sum(pair_low, grad_bias)
    grad_pair_low = matmul(grad_bias, weights[(ATTEND, PAIR_PROJ)].T)
    pair_gain = weights[(ATTEND, PAIR_GAIN)].astype(jnp.float32)
    pair_shift = weights[(ATTEND, PAIR_BIAS)].astype(jnp.float32)
    grad_pair, grads[(ATTEND, PAIR_GAIN)], grads[(ATTEND, PAIR_BIAS)] = norm_backward(
        pair_state, pair_gain, pair_shift, grad_pair_low
    )
    return (grad_single, grad_pair)


def shards(pair, single, lengths, params, moment_one, moment_two, pair_cotangent, single_cotangent):
    entries = layout(C, H, S, TA_HEADS, SA_HEADS)
    full = lax.all_gather(params.astype(jnp.bfloat16), "row", axis=0, tiled=True)
    weights = unpack(logical_order(full), entries)
    rows = pair.shape[1]
    length = pair.shape[2]
    first_row = lax.axis_index("row") * rows
    mask = (jnp.arange(length, dtype=jnp.int32) < lengths[0]).astype(jnp.float32)
    mask_rows = lax.dynamic_slice_in_dim(mask, first_row, rows)
    pair_mask = mask_rows[:, None] * mask[None, :]
    penalty = (mask - 1.0) * MASKED
    state = pair[0].astype(jnp.float32)
    saved = {}
    for prefix, incoming in ((OUTGOING, False), (INCOMING, True)):
        update, saved[prefix] = triangle_forward(state, pair_mask, weights, prefix, incoming)
        state = state + update
    for prefix, ending in ((STARTING, False), (ENDING, True)):
        update, saved[prefix] = attention_forward(state, penalty, weights, prefix, ending)
        state = state + update
    update, saved[PAIR] = transition_forward(state, weights, PAIR)
    pair_final = state + update
    single_state = single[0].astype(jnp.float32)
    update, saved[ATTEND] = single_forward(single_state, pair_final, penalty, weights)
    single_mid = single_state + update
    update, saved[SINGLE] = transition_forward(single_mid, weights, SINGLE)
    single_final = single_mid + update
    grads = {}
    grad_single = single_cotangent[0].astype(jnp.float32)
    grad_single = grad_single + transition_backward(
        saved[SINGLE], grad_single, weights, SINGLE, grads
    )
    from_single, from_pair = single_backward(saved[ATTEND], grad_single, weights, grads)
    grad_single = grad_single + from_single
    grad_pair = pair_cotangent[0].astype(jnp.float32) + from_pair
    grad_pair = grad_pair + transition_backward(saved[PAIR], grad_pair, weights, PAIR, grads)
    for prefix, ending in ((ENDING, True), (STARTING, False)):
        grad_pair = grad_pair + attention_backward(
            saved[prefix], grad_pair, penalty, weights, prefix, ending, grads
        )
    for prefix, incoming in ((INCOMING, True), (OUTGOING, False)):
        grad_pair = grad_pair + triangle_backward(
            saved[prefix], grad_pair, pair_mask, weights, prefix, incoming, grads
        )
    flat = stored_order(jnp.concatenate([grads[name].reshape(-1) for name, shape in entries]))
    shard_size = params.shape[0]
    row_index = lax.axis_index("row")
    total = lax.psum(flat, ("crop", "row"))
    shard = lax.dynamic_slice_in_dim(total, row_index * shard_size, shard_size)
    norm_squared = jnp.sum(total * total)
    clip_norm = jnp.sqrt(norm_squared)
    clipped = shard * (CLIP / jnp.maximum(clip_norm, CLIP))
    new_first = BETA_ONE * moment_one + (1.0 - BETA_ONE) * clipped
    new_second = BETA_TWO * moment_two + (1.0 - BETA_TWO) * clipped * clipped
    rates, decays = rate_tables(entries)
    rate_shard = lax.dynamic_slice_in_dim(jnp.asarray(rates), row_index * shard_size, shard_size)
    decay_shard = lax.dynamic_slice_in_dim(jnp.asarray(decays), row_index * shard_size, shard_size)
    first_hat = new_first / (1.0 - BETA_ONE**STEP)
    second_hat = new_second / (1.0 - BETA_TWO**STEP)
    new_params = params - rate_shard * (
        first_hat / (jnp.sqrt(second_hat) + ADAM_EPS) + decay_shard * params
    )
    return (
        pair_final.astype(jnp.bfloat16)[None],
        single_final.astype(jnp.bfloat16)[None],
        grad_pair[None],
        grad_single[None],
        new_params,
        new_first,
        new_second,
        clip_norm,
    )


F32 = jnp.float32
BF16 = jnp.bfloat16
LOG2E = 1.4426950408889634
VMEM_LIMIT = 56 * 1024 * 1024


def mm(left, right):
    return lax.dot_general(left, right, (((1,), (0,)), ((), ())), preferred_element_type=F32)


def mm_nt(left, right):
    return lax.dot_general(left, right, (((1,), (1,)), ((), ())), preferred_element_type=F32)


def mm_tn(left, right):
    return lax.dot_general(left, right, (((0,), (0,)), ((), ())), preferred_element_type=F32)


def standardize(values):
    centred = values - jnp.mean(values, axis=0, keepdims=True)
    spread = jnp.mean(centred * centred, axis=0, keepdims=True)
    inverse = lax.rsqrt(spread + EPSILON)
    return centred * inverse, inverse


def standardize_back(unit, inverse, grad_unit):
    first = jnp.mean(grad_unit, axis=0, keepdims=True)
    second = jnp.mean(grad_unit * unit, axis=0, keepdims=True)
    return inverse * (grad_unit - first - unit * second)


def sigmoid(values):
    return 0.5 * jnp.tanh(0.5 * values) + 0.5


def column(ref, index):
    return ref[:, index : index + 1]


def live_pair(info, alive, row):
    return jnp.concatenate(
        [jnp.where(info[row + place] > 0, alive[0:1], 0.0) for place in range(GROUP)], axis=1
    )


GROUP = 8
LAG = 4


def each_group(count, body):
    def step(index, carry):
        body(index * GROUP)
        return carry

    lax.fori_loop(0, count // GROUP, step, 0, unroll=2)


def each_channel(count, body):
    def step(index, carry):
        body(index)
        return carry

    lax.fori_loop(0, count, step, 0)


def join(read, ref, row):
    return jnp.concatenate([read(ref, row + place) for place in range(GROUP)], axis=1)


def pieces_of(values):
    length = values.shape[1] // GROUP
    return [values[:, place * length : (place + 1) * length] for place in range(GROUP)]


def put_rows(ref, row, values):
    for place, part in enumerate(pieces_of(values)):
        ref[row + place] = part.astype(ref.dtype)


def put_inner(scratch, row, values):
    for place, part in enumerate(pieces_of(values)):
        scratch[:, row + place, :] = part


def read_inner(scratch, row):
    return scratch[:, row, :]


def put_turned(scratch, row, values):
    for place, part in enumerate(pieces_of(values)):
        scratch[:, row + place, :] = part.T


def add_lanes(ref, values):
    ref[...] += sum(pieces_of(values))


def spec_full(shape):
    return pl.BlockSpec(shape, lambda step: (0,) * len(shape))


def cost(microseconds):
    return pl.CostEstimate(
        flops=int(microseconds * 1e9), bytes_accessed=int(microseconds * 3e6), transcendentals=0
    )


class Both(list):
    pass


def all_rows(ins, outs):
    extents = [shape[axis] for shape, dtype, axis in outs if axis is not None]
    for array, axis in ins:
        if isinstance(axis, int):
            extents += [member.shape[axis] for member in (array if isinstance(array, list) else [array])]
    return max(extents)


def run_rows(kernel, name, steps, ins, outs, scratch, time=15, half=None, before=None):
    grid = steps if half is None else steps // 2
    offset = grid * (half or 0)
    flat = []
    groups = []
    for array, axis in ins:
        members = array if isinstance(array, Both) else [array]
        flat += [(member, axis) for member in members]
        groups.append((len(members), isinstance(array, Both)))
    full = all_rows(flat, outs)

    def spec(shape, axis):
        if axis is None:
            return spec_full(shape)
        size = full // steps
        first = offset if shape[axis] == full else 0
        sizes = tuple(size if place == axis else extent for place, extent in enumerate(shape))
        return pl.BlockSpec(
            sizes,
            lambda step: tuple(step + first if place == axis else 0 for place in range(len(shape))),
        )

    in_specs = [
        pl.BlockSpec(memory_space=pltpu.SMEM) if axis == "smem" else spec(array.shape, axis)
        for array, axis in flat
    ]
    out_specs = [spec(shape, axis) for shape, dtype, axis in outs]
    arrays = [array for array, axis in flat]
    aliases = {}
    kept = []
    for place, (shape, dtype, axis) in enumerate(outs):
        if before is not None and (axis is None or shape[axis] == full):
            aliases[len(arrays)] = place
            kept.append(place)
            arrays.append(before[place])
            in_specs.append(spec_full(shape) if axis is None else pl.BlockSpec(memory_space=pl.ANY))

    def run(*refs):
        taken = iter(refs)
        given = []
        for number, together in groups:
            members = [next(taken) for _ in range(number)]
            given.append(members if together else members[0])
        held = {place: next(taken) for place in kept}
        results = [next(taken) for _ in outs]

        @pl.when(pl.program_id(0) == 0)
        def _():
            for place, (shape, dtype, axis) in enumerate(outs):
                if axis is None:
                    results[place][...] = (
                        held[place][...] if place in held else jnp.zeros(shape, dtype)
                    )

        kernel(*given, *results, *taken)

    return pl.pallas_call(
        run,
        grid=(grid,),
        in_specs=in_specs,
        out_specs=out_specs,
        out_shape=[jax.ShapeDtypeStruct(shape, dtype) for shape, dtype, axis in outs],
        scratch_shapes=[pltpu.VMEM(shape, dtype) for shape, dtype in scratch],
        input_output_aliases=aliases,
        compiler_params=pltpu.CompilerParams(vmem_limit_bytes=VMEM_LIMIT),
        cost_estimate=cost(time if half is None else time / 2),
        name=name,
    )(*arrays)


def run_halves(kernel, name, steps, ins, outs, scratch, time=15):
    results = []
    for half in range(2):
        chosen = [
            (array[half] if type(array) is list else array, axis) for array, axis in ins
        ]
        before = results[0] if half else None
        results.append(run_rows(kernel, name, steps, chosen, outs, scratch, time, half, before))
    full = all_rows(ins, outs)
    return [
        [results[0][place], results[1][place]]
        if axis is not None and shape[axis] != full
        else results[1][place]
        for place, (shape, dtype, axis) in enumerate(outs)
    ]


def zero_first(*refs):
    @pl.when(pl.program_id(0) == 0)
    def _():
        for ref in refs:
            ref[...] = jnp.zeros(ref.shape, ref.dtype)


def lane_sums(ref):
    return jnp.sum(ref[...].T, axis=0, keepdims=True)


def on_last(body):
    @pl.when(pl.program_id(0) == pl.num_programs(0) - 1)
    def _():
        body()


def read_plain(ref, row):
    return ref[row].astype(F32)


def reorder(values, order):
    size = values.shape[0] // len(order)
    return jnp.concatenate([values[place * size : (place + 1) * size] for place in order], axis=0)


def read_tokens(order, ref, row):
    return reorder(ref[row].astype(F32), order).T


def read_flipped(refs, row):
    parts = jnp.concatenate([ref[:, row] for ref in refs], axis=1)
    return parts.reshape(-1, parts.shape[-1]).astype(F32).T


def read_turned(order, ref, row):
    parts = ref[:, row]
    return reorder(parts.reshape(-1, parts.shape[-1]).astype(F32), order).T


def tri_pre_row(info, alive, row, state, cols, first, proj_t):
    unit, inverse = standardize(state)
    lowered = (unit * column(cols, first) + column(cols, first + 1)).astype(BF16)
    project = mm(proj_t[...], lowered)
    half = project.shape[0] // 2
    return project[:half] * sigmoid(project[half:]) * live_pair(info, alive, row)


def store_product(out, scratch, devices):
    hidden = scratch.shape[0] // 2
    part = hidden // devices

    def one(device, carry):
        out[device, 0] = scratch[pl.ds(device * part, part)].astype(BF16)
        out[device, 1] = scratch[pl.ds(hidden + device * part, part)].astype(BF16)
        return carry

    lax.fori_loop(0, devices, one, 0)


def copy_blocks(target, source, count):
    def one(index, carry):
        target[index] = source[index].astype(target.dtype)
        return carry

    lax.fori_loop(0, count, one, 0)


def store_flipped(out, scratch):
    devices, part = out.shape[0], out.shape[1]

    def one(device, carry):
        out[device] = scratch[pl.ds(device * part, part)].astype(out.dtype)
        return carry

    lax.fori_loop(0, devices, one, 0)


def tri_post_row(state, tri, cols, proj_t, gate_t):
    unit, inverse = standardize(state)
    lowered = (unit * column(cols, 0) + column(cols, 1)).astype(BF16)
    tri_unit, tri_inverse = standardize(tri)
    out_low = (tri_unit * column(cols, 2) + column(cols, 3)).astype(BF16)
    output = mm(proj_t[...], out_low)
    gate = sigmoid(mm(gate_t[...], lowered))
    return unit, inverse, lowered, tri_unit, tri_inverse, out_low, output, gate


def row_base(rows):
    return pl.program_id(0) * rows


def tri_pre_first_kernel(devices, read, info, alive, pair, cols, proj_t, out, scratch):
    rows = pair.shape[0]

    def body(row):
        product = tri_pre_row(
            info, alive, row_base(rows) + row, join(read, pair, row), cols, 0, proj_t
        )
        put_inner(scratch, row, product)

    each_group(rows, body)
    store_product(out, scratch, devices)


def whole_rows(refs, *place):
    parts = jnp.concatenate([ref[(slice(None),) + place] for ref in refs], axis=1)
    return parts.reshape(-1, parts.shape[-1])


def split_rows(values, outs, *place):
    part = outs[0].shape[-2]
    parts = values.astype(BF16).reshape(outs[0].shape[0], -1, values.shape[-1])
    for half, out in enumerate(outs):
        out[(slice(None),) + place] = parts[:, half * part : (half + 1) * part]


def tri_product_kernel(incoming, operands, *outs):
    def body(channel):
        first = whole_rows(operands, 0, channel)
        second = whole_rows(operands, 1, channel)
        tri = mm_tn(first, second) if incoming else mm_nt(first, second)
        split_rows(tri, outs, channel)

    each_channel(operands[0].shape[2], body)


def tri_join_kernel(
    devices, read, info, alive, source, tri_in, cols, proj_t, gate_t, next_cols, next_proj_t,
    state_out, out, tri_scratch, scratch,
):
    rows = state_out.shape[0]
    copy_blocks(tri_scratch, tri_in, tri_in.shape[0])

    def body(row):
        state = join(read, source, row)
        pieces = tri_post_row(state, join(read_inner, tri_scratch, row), cols, proj_t, gate_t)
        state = state + pieces[6] * pieces[7]
        put_rows(state_out, row, state)
        product = tri_pre_row(
            info, alive, row_base(rows) + row, state, next_cols, 0, next_proj_t
        )
        put_inner(scratch, row, product)

    each_group(rows, body)
    store_product(out, scratch, devices)


def tri_last_kernel(
    source, tri_in, cols, proj_t, gate_t, next_cols, bias_t, state_out, bias_out, tri_scratch, scratch
):
    rows = state_out.shape[0]
    copy_blocks(tri_scratch, tri_in, tri_in.shape[0])

    def body(row):
        state = join(read_plain, source, row)
        pieces = tri_post_row(state, join(read_inner, tri_scratch, row), cols, proj_t, gate_t)
        state = state + pieces[6] * pieces[7]
        put_rows(state_out, row, state)
        unit, inverse = standardize(state)
        lowered = (unit * column(next_cols, 0) + column(next_cols, 1)).astype(BF16)
        put_inner(scratch, row, mm(bias_t[...], lowered))

    each_group(rows, body)
    bias_out[...] = scratch[: bias_out.shape[0]].astype(BF16)


def fill_bias(alive, bias_in, table, turned):
    @pl.when(pl.program_id(0) == 0)
    def _():
        length = table.shape[1]
        penalty = (alive[...] - 1.0) * (MASKED * LOG2E)
        for head in range(table.shape[0]):
            values = bias_in[:, head].reshape(length, length).astype(F32) * LOG2E
            if turned:
                table[head] = values + penalty.T[:, 0:1]
            else:
                table[head] = (values + penalty[0:1]).T


def attention_row(state, cols, proj_t):
    unit, inverse = standardize(state)
    lowered = (unit * column(cols, 0) + column(cols, 1)).astype(BF16)
    project = mm(proj_t[...], lowered)
    width = project.shape[0] // 4
    size = width // TA_HEADS
    query = (project[:width] * (size**-0.5 * LOG2E)).astype(BF16)
    key = project[width : 2 * width].astype(BF16)
    value = project[2 * width : 3 * width].astype(BF16)
    gate = sigmoid(project[3 * width :])
    return unit, inverse, lowered, query, key, value, gate


def in_stages(blocks, first, second, third):
    early, late, done = {}, {}, {}
    count = len(blocks)
    for step in range(count + 2 * LAG):
        if step < count:
            early[step] = first(*blocks[step])
        if 0 <= step - LAG < count:
            late[step - LAG] = second(*blocks[step - LAG], early.pop(step - LAG))
        if 0 <= step - 2 * LAG < count:
            place = step - 2 * LAG
            done[blocks[place]] = third(*blocks[place], late.pop(place))
    return done


def head_rows(values, place, head):
    size, length = values.shape[0] // TA_HEADS, values.shape[1] // GROUP
    return values[head * size : (head + 1) * size, place * length : (place + 1) * length]


def gather_heads(done):
    return jnp.concatenate(
        [
            jnp.concatenate([done[place, head] for head in range(TA_HEADS)], axis=0)
            for place in range(GROUP)
        ],
        axis=1,
    )


ROW_BLOCKS = [(place, head) for place in range(GROUP) for head in range(TA_HEADS)]
HEAD_BLOCKS = [(place, head) for head in range(TA_HEADS) for place in range(GROUP)]


def attend_rows(state, row, cols, proj_t, output_t, table, totals, mixed_out):
    unit, inverse, lowered, query, key, value, gate = attention_row(state, cols, proj_t)

    def score(place, head):
        return mm_tn(head_rows(key, place, head), head_rows(query, place, head)) + table[head]

    def shift(place, head, scores):
        top = jnp.max(scores, axis=0, keepdims=True)
        return top, jnp.exp2(scores - top).astype(BF16)

    def mix(place, head, items):
        top, shifted = items
        values = head_rows(value, place, head)
        size = values.shape[0]
        values = jnp.concatenate([values, jnp.ones((16, values.shape[1]), BF16)], axis=0)
        result = mm(values, shifted)
        total = result[size : size + 1]
        return result[:size] / total, top + jnp.log2(total)

    done = in_stages(ROW_BLOCKS, score, shift, mix)
    mixed = gather_heads({block: items[0] for block, items in done.items()})
    put_rows(totals, row, gather_heads({block: items[1] for block, items in done.items()}))
    put_rows(mixed_out, row, mixed)
    return state + mm(output_t[...], (mixed * gate).astype(BF16))


def starting_kernel(
    alive, source, bias_in, cols, proj_t, output_t, next_cols, bias_t, out, totals, mixed, bias_out,
    table, scratch, bias_scratch,
):
    fill_bias(alive, bias_in, table, False)
    rows = source.shape[0]

    def body(row):
        state = attend_rows(
            join(read_plain, source, row), row, cols, proj_t, output_t, table, totals, mixed
        )
        put_turned(scratch, row, state)
        unit, inverse = standardize(state)
        lowered = (unit * column(next_cols, 0) + column(next_cols, 1)).astype(BF16)
        put_inner(bias_scratch, row, mm(bias_t[...], lowered))

    each_group(rows, body)
    store_flipped(out, scratch)
    bias_out[...] = bias_scratch[: bias_out.shape[0]].astype(BF16)


def ending_kernel(alive, source, bias_in, cols, proj_t, output_t, out, totals, mixed, table):
    fill_bias(alive, bias_in, table, True)
    rows = source[0].shape[1]

    def body(row):
        state = attend_rows(
            join(read_flipped, source, row), row, cols, proj_t, output_t, table, totals, mixed
        )
        put_rows(out, row, state)

    each_group(rows, body)


def transition_kernel(
    order, source, cols, up_t, down_t, next_cols, bias_t, state_out, pair_out, bias_out, scratch, bias_scratch
):
    rows = source.shape[0]

    def body(row):
        state = join(read_plain, source, row)
        unit, inverse = standardize(state)
        lowered = (unit * column(cols, 0) + column(cols, 1)).astype(BF16)
        hidden = mm(up_t[...], lowered)
        half = hidden.shape[0] // 2
        first = hidden[:half]
        mixed = (first * sigmoid(first) * hidden[half:]).astype(BF16)
        state = state + mm(down_t[...], mixed)
        put_rows(state_out, row, state)
        put_turned(scratch, row, state)
        unit, inverse = standardize(state)
        lowered = (unit * column(next_cols, 0) + column(next_cols, 1)).astype(BF16)
        put_inner(bias_scratch, row, mm(bias_t[...], lowered))

    each_group(rows, body)
    size = pair_out.shape[0] // len(order)
    for place, held in enumerate(order):
        pair_out[place * size : (place + 1) * size] = scratch[held * size : (held + 1) * size].astype(BF16)
    bias_to_lanes(bias_out, bias_scratch)


def transition_back_kernel(
    read, mid, final, cotangent, bias_grad, cols, up_t, up, down, next_cols, bias_w,
    grad_out, up_grad, down_grad, bias_w_grad, vecs, norm_gain, norm_bias, pair_gain, pair_bias, bias_scratch,
):
    zero_first(norm_gain, norm_bias, pair_gain, pair_bias)
    rows = mid.shape[0]
    lanes_to_bias(bias_scratch, bias_grad)

    def body(row):
        grad = join(read, cotangent, row)
        unit, inverse = standardize(join(read_plain, final, row))
        gain = column(next_cols, 0)
        lowered = (unit * gain + column(next_cols, 1)).astype(BF16)
        grad_bias = join(read_inner, bias_scratch, row).astype(BF16)
        bias_w_grad[...] += mm_nt(lowered, grad_bias)
        grad_lowered = mm(bias_w[...], grad_bias)
        add_lanes(pair_gain, grad_lowered * unit)
        add_lanes(pair_bias, grad_lowered)
        grad = grad + standardize_back(unit, inverse, grad_lowered * gain)
        unit, inverse = standardize(join(read_plain, mid, row))
        gain = column(cols, 0)
        lowered = (unit * gain + column(cols, 1)).astype(BF16)
        hidden = mm(up_t[...], lowered)
        half = hidden.shape[0] // 2
        first, second = hidden[:half], hidden[half:]
        slope = sigmoid(first)
        silu = first * slope
        grad_low = grad.astype(BF16)
        grad_mixed = mm(down[...], grad_low)
        down_grad[...] += mm_nt((silu * second).astype(BF16), grad_low)
        grad_hidden = jnp.concatenate(
            [
                (grad_mixed * second * (slope + silu * (1.0 - slope))).astype(BF16),
                (grad_mixed * silu).astype(BF16),
            ],
            axis=0,
        )
        up_grad[...] += mm_nt(lowered, grad_hidden)
        grad_lowered = mm(up[...], grad_hidden)
        add_lanes(norm_gain, grad_lowered * unit)
        add_lanes(norm_bias, grad_lowered)
        put_rows(grad_out, row, grad + standardize_back(unit, inverse, grad_lowered * gain))

    each_group(rows, body)

    def finish():
        vecs[0:1] += lane_sums(norm_gain)
        vecs[1:2] += lane_sums(norm_bias)
        vecs[2:3] += lane_sums(pair_gain)
        vecs[3:4] += lane_sums(pair_bias)

    on_last(finish)


def attention_back_kernel(
    turned, read, read_grad, alive, source, grad_in, bias_in, totals, mixed_in, cols, proj_t, proj, output,
    grad_out, bias_out, proj_grad, output_grad, table, grad_table,
):
    fill_bias(alive, bias_in, table, turned)
    zero_first(grad_table)
    rows = grad_out.shape[0]

    def body(row):
        unit, inverse, lowered, query, key, value, gate = attention_row(
            join(read, source, row), cols, proj_t
        )
        mixed = join(read_plain, mixed_in, row)
        total = join(read_plain, totals, row)
        grad_low = join(read_grad, grad_in, row).astype(BF16)
        gated = mixed * gate
        output_grad[...] += mm_nt(gated.astype(BF16), grad_low)
        grad_gated = mm(output[...], grad_low)
        grad_gate = grad_gated * gated * (1.0 - gate)
        grad_mixed = (grad_gated * gate).astype(BF16)
        product = grad_mixed.astype(F32) * mixed
        size = query.shape[0] // TA_HEADS

        def score(place, head):
            scores = mm_tn(head_rows(key, place, head), head_rows(query, place, head))
            grads = mm_tn(head_rows(value, place, head), head_rows(grad_mixed, place, head))
            return scores + table[head], grads

        def slope(place, head, items):
            scores, grads = items
            probs = jnp.exp2(scores - head_rows(total, place, head))
            delta = jnp.sum(head_rows(product, place, head), axis=0, keepdims=True)
            grad_scores = probs * (grads - delta)
            grad_table[head] += grad_scores
            return probs.astype(BF16), grad_scores.astype(BF16)

        def back(place, head, items):
            probs, grad_scores = items
            return (
                mm(head_rows(key, place, head), grad_scores) * size**-0.5,
                mm_nt(head_rows(query, place, head), grad_scores) * (1.0 / LOG2E),
                mm_nt(head_rows(grad_mixed, place, head), probs),
            )

        done = in_stages(HEAD_BLOCKS, score, slope, back)
        grad_project = jnp.concatenate(
            [
                gather_heads({block: items[part] for block, items in done.items()})
                for part in range(3)
            ]
            + [grad_gate],
            axis=0,
        ).astype(BF16)
        proj_grad[...] += mm_nt(lowered, grad_project)
        put_rows(grad_out, row, mm(proj[...], grad_project))

    each_group(rows, body)

    def finish():
        for head in range(TA_HEADS):
            bias_out[:, head] = (
                grad_table[head].T.astype(BF16).reshape(bias_out.shape[0], bias_out.shape[2], -1)
            )

    on_last(finish)


def attention_end_row(
    state, grad, grad_lowered, grad_bias, cols, bias_w, bias_w_grad, norm_gain, norm_bias
):
    unit, inverse = standardize(state)
    gain = column(cols, 0)
    lowered = (unit * gain + column(cols, 1)).astype(BF16)
    bias_w_grad[...] += mm_nt(lowered, grad_bias)
    grad_lowered = grad_lowered + mm(bias_w[...], grad_bias)
    add_lanes(norm_gain, grad_lowered * unit)
    add_lanes(norm_bias, grad_lowered)
    return grad + standardize_back(unit, inverse, grad_lowered * gain)


def fill_bias_grad(scratch, bias_grad):
    heads = bias_grad.shape[1]
    total = bias_grad[0].astype(F32)
    for device in range(1, bias_grad.shape[0]):
        total = total + bias_grad[device].astype(F32)
    scratch[:heads] = total
    scratch[heads:] = jnp.zeros((scratch.shape[0] - heads,) + scratch.shape[1:], F32)


def ending_end_kernel(
    source, grad_in, grad_lowered, bias_grad, cols, bias_w,
    grad_out, bias_w_grad, vecs, norm_gain, norm_bias, bias_scratch, scratch,
):
    zero_first(norm_gain, norm_bias)
    fill_bias_grad(bias_scratch, bias_grad)
    rows = grad_in.shape[0]

    def body(row):
        grad = attention_end_row(
            join(read_flipped, source, row), join(read_plain, grad_in, row),
            join(read_plain, grad_lowered, row), join(read_inner, bias_scratch, row).astype(BF16), cols, bias_w, bias_w_grad, norm_gain, norm_bias,
        )
        put_turned(scratch, row, grad)

    each_group(rows, body)
    store_flipped(grad_out, scratch)

    def finish():
        vecs[0:1] += lane_sums(norm_gain)
        vecs[1:2] += lane_sums(norm_bias)

    on_last(finish)


def tri_post_back_row(
    state, tri, grad, cols, proj_t, gate_t, proj, gate_w, proj_grad, gate_grad, out_gain, out_bias
):
    unit, inverse, lowered, tri_unit, tri_inverse, out_low, output, gate = tri_post_row(
        state, tri, cols, proj_t, gate_t
    )
    grad_output = grad * gate
    grad_gate = (grad_output * output * (1.0 - gate)).astype(BF16)
    grad_output = grad_output.astype(BF16)
    proj_grad[...] += mm_nt(out_low, grad_output)
    gate_grad[...] += mm_nt(lowered, grad_gate)
    grad_normed = mm(proj[...], grad_output)
    add_lanes(out_gain, grad_normed * tri_unit)
    add_lanes(out_bias, grad_normed)
    grad_tri = standardize_back(tri_unit, tri_inverse, grad_normed * column(cols, 2))
    return grad_tri, mm(gate_w[...], grad_gate)


def starting_end_kernel(
    source, grad_in, grad_lowered, bias_grad, cols, bias_w,
    below, tri_in, tri_cols, proj_t, gate_t, proj, gate_w,
    grad_out, tri_out, gate_back, bias_w_grad, proj_grad, gate_grad, vecs,
    norm_gain, norm_bias, out_gain, out_bias, bias_scratch, tri_scratch,
):
    zero_first(norm_gain, norm_bias, out_gain, out_bias)
    fill_bias_grad(bias_scratch, bias_grad)
    copy_blocks(tri_scratch, tri_in, tri_in.shape[0])
    rows = source.shape[0]

    def body(row):
        grad = attention_end_row(
            join(read_plain, source, row), join(read_flipped, grad_in, row),
            join(read_plain, grad_lowered, row), join(read_inner, bias_scratch, row).astype(BF16), cols, bias_w, bias_w_grad, norm_gain, norm_bias,
        )
        put_rows(grad_out, row, grad)
        grad_tri, back = tri_post_back_row(
            join(read_plain, below, row), join(read_inner, tri_scratch, row), grad, tri_cols, proj_t, gate_t, proj, gate_w,
            proj_grad, gate_grad, out_gain, out_bias,
        )
        put_rows(gate_back, row, back)
        put_inner(tri_scratch, row, grad_tri)

    each_group(rows, body)
    copy_blocks(tri_out, tri_scratch, tri_out.shape[0])

    def finish():
        vecs[0:1] += lane_sums(norm_gain)
        vecs[1:2] += lane_sums(norm_bias)
        vecs[2:3] += lane_sums(out_gain)
        vecs[3:4] += lane_sums(out_bias)

    on_last(finish)


def tri_product_back_kernel(incoming, grad, operands, *outs):
    def body(channel):
        first = whole_rows(operands, 0, channel)
        second = whole_rows(operands, 1, channel)
        tri = whole_rows(grad, channel)
        if incoming:
            grad_first = mm_nt(second, tri)
            grad_second = mm(first, tri)
        else:
            grad_first = mm(tri, second)
            grad_second = mm_tn(tri, first)
        split_rows(grad_first, outs, 0, channel)
        split_rows(grad_second, outs, 1, channel)

    each_channel(operands[0].shape[2], body)


def tri_pre_back_row(
    info, alive, row, state, product_grad, gate_back, grad, cols, proj_t, proj, proj_grad, norm_gain, norm_bias
):
    unit, inverse = standardize(state)
    gain = column(cols, 0)
    lowered = (unit * gain + column(cols, 1)).astype(BF16)
    project = mm(proj_t[...], lowered)
    half = project.shape[0] // 2
    gate = sigmoid(project[half:])
    grad_first = product_grad * gate * live_pair(info, alive, row)
    grad_second = grad_first * project[:half] * (1.0 - gate)
    grad_project = jnp.concatenate([grad_first.astype(BF16), grad_second.astype(BF16)], axis=0)
    proj_grad[...] += mm_nt(lowered, grad_project)
    grad_lowered = mm(proj[...], grad_project) + gate_back
    add_lanes(norm_gain, grad_lowered * unit)
    add_lanes(norm_bias, grad_lowered)
    return grad + standardize_back(unit, inverse, grad_lowered * gain)


def fill_product_grad(scratch, product_grad):
    devices, part = product_grad.shape[0], product_grad.shape[2]

    def one(device, carry):
        scratch[pl.ds(device * part, part)] = product_grad[device, 0].astype(F32)
        scratch[pl.ds((devices + device) * part, part)] = product_grad[device, 1].astype(F32)
        return carry

    lax.fori_loop(0, devices, one, 0)


def tri_join_back_kernel(
    read, info, alive, source, product_grad, gate_in, grad_in, cols, proj_t, proj,
    below, tri_in, tri_cols, out_t, gate_t, out_w, gate_w,
    grad_out, tri_out, gate_back, proj_grad, out_grad, gate_grad, vecs,
    norm_gain, norm_bias, out_gain, out_bias, scratch, tri_scratch,
):
    zero_first(norm_gain, norm_bias, out_gain, out_bias)
    fill_product_grad(scratch, product_grad)
    copy_blocks(tri_scratch, tri_in, tri_in.shape[0])
    rows = source.shape[0]

    def body(row):
        grad = tri_pre_back_row(
            info, alive, row_base(rows) + row, join(read_plain, source, row),
            join(read_inner, scratch, row), join(read_plain, gate_in, row),
            join(read_plain, grad_in, row), cols, proj_t, proj, proj_grad, norm_gain, norm_bias,
        )
        put_rows(grad_out, row, grad)
        grad_tri, back = tri_post_back_row(
            join(read, below, row), join(read_inner, tri_scratch, row), grad, tri_cols, out_t, gate_t, out_w, gate_w,
            out_grad, gate_grad, out_gain, out_bias,
        )
        put_rows(gate_back, row, back)
        put_inner(tri_scratch, row, grad_tri)

    each_group(rows, body)
    copy_blocks(tri_out, tri_scratch, tri_out.shape[0])

    def finish():
        vecs[0:1] += lane_sums(norm_gain)
        vecs[1:2] += lane_sums(norm_bias)
        vecs[2:3] += lane_sums(out_gain)
        vecs[3:4] += lane_sums(out_bias)

    on_last(finish)


def tri_first_back_kernel(
    read, order, info, alive, source, product_grad, gate_in, grad_in, cols, proj_t, proj,
    grad_out, proj_grad, vecs, norm_gain, norm_bias, scratch,
):
    zero_first(norm_gain, norm_bias)
    fill_product_grad(scratch, product_grad)
    rows = source.shape[0]

    def body(row):
        grad = tri_pre_back_row(
            info, alive, row_base(rows) + row, join(read, source, row),
            join(read_inner, scratch, row), join(read_plain, gate_in, row),
            join(read_plain, grad_in, row), cols, proj_t, proj, proj_grad, norm_gain, norm_bias,
        )
        for place, part in enumerate(pieces_of(grad)):
            grad_out[row + place] = reorder(part.T, order).astype(grad_out.dtype)

    each_group(rows, body)

    def finish():
        vecs[0:1] += lane_sums(norm_gain)
        vecs[1:2] += lane_sums(norm_bias)

    on_last(finish)


RUN = 24


def table_of(entries):
    table = {}
    offset = 0
    for name, shape in entries:
        table[name] = (offset // STRIDE, shape)
        offset += math.prod(shape)
    return table, offset


def runs_kernel(info, shard, out, scratch):
    def one(block, carry):
        scratch[:, block, :] = shard[pl.ds(block * STRIDE, STRIDE), :].T
        return carry

    lax.fori_loop(0, RUN, one, 0)
    half = STRIDE // 2
    turn = info[0] * half

    def move(lane, carry):
        out[lane] = scratch[lax.rem(lane + turn, STRIDE)].astype(BF16)
        return carry

    lax.fori_loop(0, STRIDE, move, 0)


def run_place(shards, total, lane, shard):
    count = total // STRIDE
    whole = total // shards
    step, odd = whole // STRIDE, (whole % STRIDE) // (STRIDE // 2)
    extra = lax.div(shard * odd + jnp.where(lane < STRIDE // 2, 1, 0), 2)
    start = lane * count + shard * step + extra
    return lax.div(start, STRIDE), lax.rem(start, STRIDE)


def rows_from_runs(runs, rows, first_lane, total):
    shards, lanes = runs.shape[0], runs.shape[1]
    base = first_lane * (total // STRIDE) // STRIDE

    def one(index, carry):
        lane, shard = lax.div(index, shards), lax.rem(index, shards)
        row, shift = run_place(shards, total, first_lane + lane, shard)
        row = row - base
        turned = pltpu.roll(runs[shard, lane].astype(F32), shift, 1)
        place = lax.broadcasted_iota(jnp.int32, (RUN + 1, STRIDE), 1)
        last, before = carry
        joint = jnp.where(row - before == RUN, last[2:3], last[1:2])
        below = jnp.concatenate([joint, turned], axis=0)
        above = jnp.concatenate([turned, turned[RUN - 1 :]], axis=0)
        values = jnp.where(place < shift, below, above)
        rows[pl.ds(row, RUN + 1), :] = values
        return values[RUN - 2 :], row

    lax.fori_loop(0, shards * lanes, one, (jnp.zeros((3, STRIDE), F32), -RUN), unroll=4)


def runs_from_rows(rows, out, first_lane, base, total):
    shards, lanes = out.shape[0], out.shape[1]

    def one(index, carry):
        lane, shard = lax.div(index, shards), lax.rem(index, shards)
        row, shift = run_place(shards, total, first_lane + lane, shard)
        turned = pltpu.roll(rows[pl.ds(row - base, RUN + 1), :], (STRIDE - shift) % STRIDE, 1)
        place = lax.broadcasted_iota(jnp.int32, (RUN, STRIDE), 1)
        out[shard, lane] = jnp.where(
            place < STRIDE - shift, turned[:RUN], turned[1:]
        ).astype(BF16)
        return carry

    lax.fori_loop(0, shards * lanes, one, 0, unroll=4)


def row_height(base, first_lane, last_lane, total):
    end = (last_lane * (total // STRIDE)) // STRIDE + RUN + 2
    return -(-(end - base) // 8) * 8


def take_matrix(rows, first, shape):
    blocks = shape[1] // STRIDE
    return [
        rows[pl.ds(first + block, shape[0], stride=blocks), :]
        if blocks > 1
        else rows[first : first + shape[0], :]
        for block in range(blocks)
    ]


def put_matrix(rows, first, matrix):
    height, width = matrix.shape
    blocks = width // STRIDE
    for block in range(blocks):
        part = matrix[:, block * STRIDE : (block + 1) * STRIDE]
        if blocks > 1:
            rows[pl.ds(first + block, height, stride=blocks), :] = part
        else:
            rows[first : first + height, :] = part


def spread(index, heads, rows):
    lane = lax.broadcasted_iota(jnp.int32, (STRIDE, STRIDE), 0)
    channel = lax.broadcasted_iota(jnp.int32, (STRIDE, STRIDE), 1)
    return (channel == index * (STRIDE // heads) + lane // heads).astype(BF16)


def take_narrow(rows, first, heads, high):
    total = jnp.zeros((high, STRIDE), F32)
    head = lax.broadcasted_iota(jnp.int32, (high, STRIDE), 0)
    lane = lax.broadcasted_iota(jnp.int32, (high, STRIDE), 1)
    for index in range(heads):
        line = rows[first + index : first + index + 1, :]
        picked = jnp.where(lane % heads == head, line, 0.0).astype(BF16)
        total = total + mm(picked, spread(index, heads, rows))
    return total


def put_narrow(rows, first, heads, matrix):
    turned = matrix.T.astype(BF16)
    high = turned.shape[0]
    head = lax.broadcasted_iota(jnp.int32, (high, STRIDE), 0)
    lane = lax.broadcasted_iota(jnp.int32, (high, STRIDE), 1)
    for index in range(heads):
        wide = mm_nt(turned, spread(index, heads, rows))
        rows[first + index : first + index + 1, :] = jnp.sum(
            jnp.where(lane % heads == head, wide, 0.0), axis=0, keepdims=True
        )


PAIR_MATRICES = (
    (OUTGOING, PROJ_GATE), (OUTGOING, PROJ_OUT), (OUTGOING, GATE_OUT),
    (INCOMING, PROJ_GATE), (INCOMING, PROJ_OUT), (INCOMING, GATE_OUT),
    (STARTING, QKVG), (STARTING, OUTPUT), (ENDING, QKVG), (ENDING, OUTPUT), (PAIR, UP), (PAIR, DOWN),
)
PAIR_COLUMNS = (
    (OUTGOING, ((OUTGOING, NORM_GAIN), (OUTGOING, NORM_BIAS), (OUTGOING, OUT_GAIN), (OUTGOING, OUT_BIAS))),
    (INCOMING, ((INCOMING, NORM_GAIN), (INCOMING, NORM_BIAS), (INCOMING, OUT_GAIN), (INCOMING, OUT_BIAS))),
    (STARTING, ((STARTING, NORM_GAIN), (STARTING, NORM_BIAS))),
    (ENDING, ((ENDING, NORM_GAIN), (ENDING, NORM_BIAS))),
    (PAIR, ((PAIR, NORM_GAIN), (PAIR, NORM_BIAS))),
)
SINGLE_MATRICES = ((ATTEND, QKVG), (ATTEND, OUTPUT), (SINGLE, UP), (SINGLE, DOWN))
SINGLE_VECTORS = ((ATTEND, NORM_GAIN), (ATTEND, NORM_BIAS), (SINGLE, NORM_GAIN), (SINGLE, NORM_BIAS))


def put_columns(rows, out, table, base, names):
    out[...] = jnp.zeros(out.shape, F32)
    lines = [rows[table[name][0] - base : table[name][0] - base + 1, :] for name in names]
    lines.append(jnp.zeros((8 - len(lines), STRIDE), F32))
    out[...] = jnp.concatenate(lines, axis=0).T


def unpack_pair_kernel(table, total, runs, *refs):
    rows = refs[-1]
    outs = list(refs[:-1])
    rows_from_runs(runs, rows, 0, total)
    for name in PAIR_MATRICES:
        first, shape = table[name]
        plain, turned = outs.pop(0), outs.pop(0)
        for block, part in enumerate(take_matrix(rows, first, shape)):
            place = slice(block * STRIDE, (block + 1) * STRIDE)
            plain[:, place] = part.astype(BF16)
            turned[place, :] = part.T.astype(BF16)
    for prefix in (STARTING, ENDING):
        plain, turned = outs.pop(0), outs.pop(0)
        first, shape = table[(prefix, BIAS_PROJ)]
        matrix = take_narrow(rows, first, shape[1], 8)
        turned[...] = matrix.astype(BF16)
        plain[...] = matrix.T.astype(BF16)
    for prefix, names in PAIR_COLUMNS:
        put_columns(rows, outs.pop(0), table, 0, names)


def unpack_single_kernel(table, total, first_lane, runs, *refs):
    rows = refs[-1]
    outs = list(refs[:-1])
    rows_from_runs(runs, rows, first_lane, total)
    base = first_lane * (total // STRIDE) // STRIDE
    for name in SINGLE_MATRICES:
        first, shape = table[name]
        out = outs.pop(0)
        for block, part in enumerate(take_matrix(rows, first - base, shape)):
            out[:, block * STRIDE : (block + 1) * STRIDE] = part.astype(BF16)
    first, shape = table[(ATTEND, PAIR_PROJ)]
    matrix = take_narrow(rows, first - base, shape[1], shape[1])
    plain, turned = outs.pop(0), outs.pop(0)
    turned[...] = matrix.astype(BF16)
    plain[...] = matrix.T.astype(BF16)
    put_columns(rows, outs.pop(0), table, base, ((ATTEND, PAIR_GAIN), (ATTEND, PAIR_BIAS)))
    lines = outs.pop(0)
    lines[...] = jnp.zeros(lines.shape, F32)
    for index, name in enumerate(SINGLE_VECTORS):
        first, shape = table[name]
        for block in range(shape[0] // STRIDE):
            lines[index : index + 1, block * STRIDE : (block + 1) * STRIDE] = rows[
                first - base + block : first - base + block + 1, :
            ]


def pack_kernel(table, total, first_lane, base, names, *refs):
    ins, out, rows = refs[: len(names)], refs[-2], refs[-1]
    for name, ref in zip(names, ins):
        if isinstance(name, tuple):
            first, shape = table[name]
            if shape[1] % STRIDE:
                put_narrow(rows, first - base, shape[1], ref[...])
            else:
                put_matrix(rows, first - base, ref)
        else:
            for index, vector in name:
                first, shape = table[vector]
                for block in range(shape[0] // STRIDE):
                    rows[first + block - base : first + block - base + 1, :] = ref[
                        index : index + 1, block * STRIDE : (block + 1) * STRIDE
                    ]
    runs_from_rows(rows, out, first_lane, base, total)


def shard_kernel(whole, info, summed, others, out, squares, runs):
    half = STRIDE // 2
    crops, first, part = summed.shape[0], summed.shape[1], others.shape[1]

    def add(lane, carry):
        runs[lane] = sum(summed[crop, lane].astype(F32) for crop in range(crops))
        return carry

    lax.fori_loop(0, first, add, 0)
    for crop in range(crops):

        def move(lane, carry, crop=crop):
            runs[first + crop * part + lane] = others[crop, lane].astype(F32)
            return carry

        lax.fori_loop(0, part, move, 0)
    squares[...] = jnp.zeros(squares.shape, F32)

    def one(block, carry):
        first = runs[pl.ds(info[0] * half, half), block, :]
        second = runs[pl.ds(half - info[0] * half, half), block, :]
        values = jnp.concatenate([first, second], axis=0).T
        row = block * STRIDE + lax.broadcasted_iota(jnp.int32, values.shape, 0)
        lane = lax.broadcasted_iota(jnp.int32, values.shape, 1)
        values = jnp.where(row * STRIDE + lane < whole, values, 0.0)
        out[pl.ds(block * STRIDE, STRIDE), :] = values
        squares[...] += jnp.sum((values * values).reshape(-1, 8, STRIDE), axis=0)
        return carry

    lax.fori_loop(0, RUN, one, 0)


def whole_call(kernel, name, ins, outs, scratch, time=8):
    def spec(axis):
        return pl.BlockSpec(memory_space=pltpu.SMEM if axis == "smem" else pltpu.VMEM)

    return pl.pallas_call(
        kernel,
        in_specs=[spec(axis) for array, axis in ins],
        out_specs=[pl.BlockSpec(memory_space=pltpu.VMEM) for shape, dtype in outs],
        out_shape=[jax.ShapeDtypeStruct(shape, dtype) for shape, dtype in outs],
        scratch_shapes=[pltpu.VMEM(shape, dtype) for shape, dtype in scratch],
        compiler_params=pltpu.CompilerParams(vmem_limit_bytes=VMEM_LIMIT),
        cost_estimate=cost(time),
        name=name,
    )(*[array for array, axis in ins])


def unpack_pair(table, total, runs):
    outs = []
    names = []
    for name in PAIR_MATRICES:
        shape = table[name][1]
        outs += [(shape, BF16), (shape[::-1], BF16)]
        names += [name, (name, T)]
    for prefix in (STARTING, ENDING):
        outs += [((STRIDE, 8), BF16), ((8, STRIDE), BF16)]
        names += [(prefix, BIAS_W), (prefix, BIAS_T)]
    for prefix, parts in PAIR_COLUMNS:
        outs.append(((STRIDE, 8), F32))
        names.append((prefix, COLS))
    height = row_height(0, 0, runs.shape[1], total)
    values = whole_call(
        functools.partial(unpack_pair_kernel, table, total), "pair_weights", [(runs, None)], outs,
        [((height, STRIDE), F32)], 20,
    )
    return dict(zip(names, values))


def unpack_single(table, total, first_lane, runs):
    outs = [(table[name][1], BF16) for name in SINGLE_MATRICES]
    names = list(SINGLE_MATRICES)
    shape = table[(ATTEND, PAIR_PROJ)][1]
    outs += [(shape, BF16), (shape[::-1], BF16), ((STRIDE, 8), F32), ((8, S), F32)]
    names += [(ATTEND, PAIR_PROJ), ((ATTEND, PAIR_PROJ), T), (ATTEND, COLS), (SINGLE, VECTORS)]
    base = first_lane * (total // STRIDE) // STRIDE
    height = row_height(base, first_lane, first_lane + runs.shape[1], total)
    values = whole_call(
        functools.partial(unpack_single_kernel, table, total, first_lane), "single_weights",
        [(runs, None)], outs, [((height, STRIDE), F32)],
    )
    return dict(zip(names, values))


def pack(name, table, total, shards, lanes, base, parts):
    height = row_height(base, *lanes, total)
    for held, array in parts:
        if isinstance(held, tuple):
            end = table[held][0] - base + array.shape[0] * max(1, array.shape[1] // STRIDE)
            height = max(height, -(-end // 8) * 8)
    return whole_call(
        functools.partial(pack_kernel, table, total, lanes[0], base, [held for held, array in parts]),
        name, [(array, None) for held, array in parts],
        [((shards, lanes[1] - lanes[0], RUN, STRIDE), BF16)], [((height, STRIDE), F32)],
    )[0]


def bias_to_lanes(out, scratch):
    heads, devices = scratch.shape[0], out.shape[0]
    part = scratch.shape[2] // devices
    per = STRIDE // part
    lane = lax.broadcasted_iota(jnp.int32, (scratch.shape[1], STRIDE), 1)
    for device in range(devices):
        block, place = device // per, device % per
        for first in range(0, heads, per):
            total = None
            for index in range(per):
                values = scratch[first + index, :, block * STRIDE : (block + 1) * STRIDE]
                values = pltpu.roll(values, (index - place) * part % STRIDE, 1)
                total = values if index == 0 else jnp.where(lane < index * part, total, values)
            out[device, :, first * part : first * part + STRIDE] = total.astype(out.dtype)


def lanes_to_bias(scratch, sent):
    heads, devices = scratch.shape[0], sent.shape[0]
    part = scratch.shape[2] // devices
    per = STRIDE // part
    lane = lax.broadcasted_iota(jnp.int32, (scratch.shape[1], STRIDE), 1)
    for head in range(heads):
        first, index = head // per * per, head % per
        for block in range(devices // per):
            total = None
            for place in range(per):
                values = sent[block * per + place, :, first * part : first * part + STRIDE].astype(F32)
                values = pltpu.roll(values, (place - index) * part % STRIDE, 1)
                total = values if place == 0 else jnp.where(lane < place * part, total, values)
            scratch[head, :, block * STRIDE : (block + 1) * STRIDE] = total


def standardize_lanes(values):
    centred = values - jnp.mean(values, axis=1, keepdims=True)
    inverse = lax.rsqrt(jnp.mean(centred * centred, axis=1, keepdims=True) + EPSILON)
    return centred * inverse, inverse


def single_kernel(
    state_in, back_in, project, kv, bias, alive, vectors, output_w, up, down,
    final_out, grad_out, sent, query_grad, gate_grad, output_grad, up_grad, down_grad, vecs,
):
    state = state_in[...]
    rows, width = state.shape
    size = width // SA_HEADS
    per = STRIDE // rows
    groups = SA_HEADS // per
    scale = size**-0.5
    tokens = kv.shape[0] * rows
    both = kv[...].reshape(tokens, 2 * width)
    keys, values = both[:, :width], both[:, width:]
    penalty = ((alive[...] - 1.0) * (MASKED * LOG2E)).T[:, 0:1]

    channel = lax.broadcasted_iota(jnp.int32, (width, STRIDE), 0)
    lane = lax.broadcasted_iota(jnp.int32, (width, STRIDE), 1)
    own = [lax.div(channel, size) == group * per + lax.div(lane, rows) for group in range(groups)]
    channel_b = lax.broadcasted_iota(jnp.int32, (STRIDE, width), 1)
    row_b = lax.broadcasted_iota(jnp.int32, (STRIDE, width), 0)
    own_b = [lax.div(channel_b, size) == group * per + lax.div(row_b, rows) for group in range(groups)]

    def spread_rows(matrix):
        turned = jnp.concatenate([matrix] * per, axis=0).T
        return [jnp.where(mask, turned, 0.0).astype(BF16) for mask in own]

    def collect(blocks):
        total = sum(jnp.where(mask, block, 0.0) for mask, block in zip(own_b, blocks))
        return sum(total[index * rows : (index + 1) * rows] for index in range(per))

    queries = spread_rows(project[:, :width] * (scale * LOG2E))
    gate = sigmoid(project[:, 3 * width :])
    scores = [
        mm(keys, queries[group])
        + bias[:, :, group * STRIDE : (group + 1) * STRIDE].reshape(tokens, STRIDE).astype(F32) * LOG2E
        + penalty
        for group in range(groups)
    ]
    shifted = [jnp.exp2(block - jnp.max(block, axis=0, keepdims=True)) for block in scores]
    probs = [block / jnp.sum(block, axis=0, keepdims=True) for block in shifted]
    probs_low = [block.astype(BF16) for block in probs]
    mixed = collect([mm_tn(block, values) for block in probs_low])
    gated = mixed * gate
    gated_low = gated.astype(BF16)
    state = state + mm(gated_low, output_w[...])

    unit, inverse = standardize_lanes(state)
    gain = vectors[2:3]
    lowered = (unit * gain + vectors[3:4]).astype(BF16)
    hidden = mm(lowered, up[...])
    half = hidden.shape[1] // 2
    first, second = hidden[:, :half], hidden[:, half:]
    slope = sigmoid(first)
    silu = first * slope
    swish = (silu * second).astype(BF16)
    final_out[...] = state + mm(swish, down[...])

    grad = back_in[...]
    grad_low = grad.astype(BF16)
    grad_mixed = mm_nt(grad_low, down[...])
    down_grad[...] = mm_tn(swish, grad_low)
    grad_hidden = jnp.concatenate(
        [
            (grad_mixed * second * (slope + silu * (1.0 - slope))).astype(BF16),
            (grad_mixed * silu).astype(BF16),
        ],
        axis=1,
    )
    grad_lowered = mm_nt(grad_hidden, up[...])
    vecs[...] = jnp.zeros(vecs.shape, F32)
    vecs[0:1] = jnp.sum(grad_lowered * unit, axis=0, keepdims=True)
    vecs[1:2] = jnp.sum(grad_lowered, axis=0, keepdims=True)
    grad_unit = grad_lowered * gain
    grad = grad + inverse * (
        grad_unit
        - jnp.mean(grad_unit, axis=1, keepdims=True)
        - unit * jnp.mean(grad_unit * unit, axis=1, keepdims=True)
    )
    grad_out[...] = grad

    grad_low = grad.astype(BF16)
    grad_gated = mm_nt(grad_low, output_w[...])
    gate_grad[...] = grad_gated * gated * (1.0 - gate)
    grads = spread_rows(grad_gated * gate)
    grad_probs = [mm(values, block) for block in grads]
    grad_scores = []
    for block, grad_block in zip(probs, grad_probs):
        delta = jnp.sum(block * grad_block, axis=0, keepdims=True)
        grad_scores.append((block * (grad_block - delta)).astype(BF16))
    for group, block in enumerate(grad_scores):
        sent[:, :, group * STRIDE : (group + 1) * STRIDE] = block.reshape(kv.shape[0], rows, STRIDE)
    query_grad[...] = collect([mm_tn(block, keys) for block in grad_scores]) * scale
    key_part = sum(mm_nt(block, query) for block, query in zip(grad_scores, queries)) * (1.0 / LOG2E)
    value_part = sum(mm_nt(block, grad_block) for block, grad_block in zip(probs_low, grads))
    first = groups * STRIDE
    sent[:, :, first : first + width] = key_part.astype(BF16).reshape(kv.shape[0], rows, width)
    sent[:, :, first + width :] = value_part.astype(BF16).reshape(kv.shape[0], rows, width)
    output_grad[...] = mm_tn(gated_low, grad_low)
    up_grad[...] = mm_tn(lowered, grad_hidden)


def single_middle(state, back, projected, bias, alive, weights):
    lowered, project, kv = projected
    rows, width = state.shape
    devices = kv.shape[0]
    names = ((ATTEND, OUTPUT), (SINGLE, UP), (SINGLE, DOWN))
    matrices = [weights[name] for name in names]
    square = (rows, width)
    outs = [
        (square, F32), (square, F32), ((devices, rows, SA_HEADS * rows + 2 * width), BF16),
        (square, F32), (square, F32),
    ] + [(matrix.shape, F32) for matrix in matrices] + [((8, width), F32)]
    ins = [state, back, project, kv, bias, alive, weights[(SINGLE, VECTORS)]] + matrices
    final, grad, sent, query_grad, gate_grad, *found, vecs = whole_call(
        single_kernel, "single_path", [(array, None) for array in ins], outs, [], 1
    )
    grads = dict(zip(names, found))
    grads[(SINGLE, NORM_GAIN)], grads[(SINGLE, NORM_BIAS)] = vecs[0], vecs[1]
    return final, grad, sent, grads, (state, lowered, query_grad, gate_grad)


def swap(values, group):
    return lax.all_to_all(values, group, split_axis=0, concat_axis=0, tiled=True)


def single_project(single_state, weights, devices):
    gain, shift = norm_pair(weights, ATTEND)
    lowered = layer_norm(single_state, gain, shift).astype(BF16)
    width = lowered.shape[1]
    qkvg = matmul(lowered, weights[(ATTEND, QKVG)])
    both = qkvg[:, width : 3 * width].astype(BF16)
    both = jnp.broadcast_to(both[None], (devices,) + both.shape)
    return lowered, qkvg, both


def single_attend_end(pending, parts, weights, grads):
    single_state, lowered, grad_query, grad_gate = pending
    rows, width = lowered.shape
    grad_both = jnp.sum(parts.astype(F32), axis=0)
    grad_qkvg = jnp.concatenate(
        [grad_query.reshape(rows, width), grad_both, grad_gate], axis=-1
    ).astype(BF16)
    grads[(ATTEND, QKVG)] = outer_sum(lowered, grad_qkvg)
    grad_lowered = matmul(grad_qkvg, weights[(ATTEND, QKVG)].T)
    gain, shift = norm_pair(weights, ATTEND)
    grad_single, grads[(ATTEND, NORM_GAIN)], grads[(ATTEND, NORM_BIAS)] = norm_backward(
        single_state, gain, shift, grad_lowered
    )
    return grad_single


def after(values, *others):
    held = lax.optimization_barrier((values,) + others)
    return held


def in_turn():
    last = []

    def send(values, axes):
        if last:
            values = after(values, last.pop())[0]
        moved = swap(values, axes)
        last.append(moved)
        return moved

    return send


def along_line(values, axis):
    count = values.shape[0]
    here = lax.axis_index(axis)
    moved = jnp.zeros_like(values)
    for step in range(count):
        part = lax.dynamic_slice_in_dim(values, lax.rem(here + step, count), 1)
        if step:
            part = lax.ppermute(part, axis, [(place, (place + step) % count) for place in range(count)])
        moved = lax.dynamic_update_slice_in_dim(moved, part, lax.rem(here + count - step, count), 0)
    return moved


def pair_path(pair, info, alive, orders, weights, cotangent, middle, between, meet, send, group, parts):
    rows, length, width = pair.shape
    hidden = weights[(OUTGOING, PROJ_OUT)].shape[0]
    devices = length // rows
    cores = devices // parts
    order, order_back = orders
    read_first = functools.partial(read_tokens, order)
    read_last = functools.partial(read_turned, order)
    part = hidden // devices
    steps = rows // 16
    state_shape = (rows, width, length)
    block = rows // steps
    half = rows // 2
    flip_shape = (devices, rows, rows, width)
    product_shape = (devices, 2, part, rows, length)
    product_half = (devices, 2, part, half, length)
    tri_shape = (devices, part, rows, length)
    tri_half = (devices, part, half, length)
    channel_block = math.gcd(part, 4)

    def products(name, kernel, arrays, out_shape):
        axes = {4: 1, 5: 2}
        out = (out_shape, BF16, axes[len(out_shape)])
        return run_rows(
            kernel, name, part // channel_block,
            [(Both(pieces), axes[pieces[0].ndim]) for pieces in arrays],
            [out] * (rows // out_shape[-2]), [], 7,
        )

    def swap_all(pieces):
        return [send(values, group) for values in pieces]

    def by_hidden(pieces):
        return [values.reshape((hidden,) + values.shape[2:]) for values in pieces]

    def by_device(pieces):
        return [values.reshape((devices, part) + values.shape[1:]) for values in pieces]

    def cols(prefix):
        return weights[(prefix, COLS)]

    tri_cols = cols

    def turned(name):
        return weights[(name, T)]

    tri_scratch = ((hidden, block, length), F32)
    product_scratch = ((2 * hidden, block, length), F32)
    head_scratch = ((8, block, length), F32)
    wide = ((width, length), F32)
    flip_scratch = ((length, block, width), F32)
    table = ((TA_HEADS, length, length), F32)
    attend_saves = [((rows, TA_HEADS, length), F32, 0), (state_shape, BF16, 0)]

    product = run_rows(
        functools.partial(tri_pre_first_kernel, devices, read_first), "outgoing_in", steps,
        [
            (info, "smem"), (alive, None), (pair, 0), (tri_cols(OUTGOING), None),
            (turned((OUTGOING, PROJ_GATE)), None),
        ],
        [(product_shape, BF16, 3)], [product_scratch], 13,
    )
    between(0, product[0])
    product_one = swap_all(product)
    tri_one = products(
        "outgoing_product", functools.partial(tri_product_kernel, False), [product_one], tri_half
    )
    tri_one = by_hidden(swap_all(tri_one))
    tri_one = [tri_one[0], *meet(0, tri_one[1])]
    state_one, product = run_halves(
        functools.partial(tri_join_kernel, devices, read_first), "outgoing_out_incoming_in", steps,
        [
            ([info[:half], info[half:]], "smem"), (alive, None), (pair, 0), (tri_one, 1), (tri_cols(OUTGOING), None),
            (turned((OUTGOING, PROJ_OUT)), None), (turned((OUTGOING, GATE_OUT)), None),
            (tri_cols(INCOMING), None), (turned((INCOMING, PROJ_GATE)), None),
        ],
        [(state_shape, F32, 0), (product_half, BF16, 3)], [tri_scratch, product_scratch], 22,
    )
    product_two = list(meet(1, *swap_all(product)))
    tri_two = products(
        "incoming_product", functools.partial(tri_product_kernel, True), [product_two], tri_shape
    )
    tri_two = by_hidden(swap_all(tri_two))
    between(1, None)
    (tri_two,) = meet(2, *tri_two)
    cotangent = cotangent.reshape(rows, parts, cores, parts, -1, width).transpose(3, 2, 1, 4, 0, 5)
    cotangent = send(cotangent.reshape(flip_shape), group)
    state_two, bias = run_rows(
        tri_last_kernel, "incoming_out_starting_bias", steps,
        [
            (state_one, 0), (tri_two, 1), (tri_cols(INCOMING), None),
            (turned((INCOMING, PROJ_OUT)), None), (turned((INCOMING, GATE_OUT)), None),
            (cols(STARTING), None), (weights[(STARTING, BIAS_T)], None),
        ],
        [(state_shape, F32, 0), ((TA_HEADS, rows, length), BF16, 1)], [tri_scratch, head_scratch],
    )
    bias_one = lax.all_gather(bias, group, axis=0, tiled=False)
    flipped, totals_one, mixed_one, bias = run_rows(
        starting_kernel, "starting_attention", steps,
        [
            (alive, None), (state_two, 0), (bias_one, None), (cols(STARTING), None),
            (turned((STARTING, QKVG)), None), (turned((STARTING, OUTPUT)), None), (cols(ENDING), None),
            (weights[(ENDING, BIAS_T)], None),
        ],
        [(flip_shape, BF16, 2)] + attend_saves + [((TA_HEADS, rows, length), BF16, 1)],
        [table, flip_scratch, head_scratch], 21,
    )
    state_three = Both([send(flipped, group)])
    bias_two = lax.all_gather(bias, group, axis=0, tiled=False)
    cotangent = along_line(cotangent.reshape((parts, cores) + flip_shape[1:]), "z").reshape(flip_shape)
    state_four, totals_two, mixed_two = run_rows(
        ending_kernel, "ending_attention", steps,
        [
            (alive, None), (state_three, 1), (bias_two, None), (cols(ENDING), None),
            (turned((ENDING, QKVG)), None), (turned((ENDING, OUTPUT)), None),
        ],
        [(state_shape, F32, 0)] + attend_saves, [table], 1,
    )
    pair_cols, attend_cols = cols(PAIR), cols(ATTEND)
    state_five, pair_out, single_bias = run_rows(
        functools.partial(transition_kernel, order_back), "pair_transition", steps,
        [
            (state_four, 0), (pair_cols, None), (turned((PAIR, UP)), None), (turned((PAIR, DOWN)), None),
            (attend_cols, None), (turned((ATTEND, PAIR_PROJ)), None),
        ],
        [(state_shape, F32, 0), ((length, rows, width), BF16, 1), ((devices, rows, SA_HEADS * rows), BF16, 1)],
        [flip_scratch, ((SA_HEADS, block, length), F32)], 1,
    )
    single_sent = send(middle(send(single_bias, group)), group)
    between(2, single_sent)
    pair_out = send(pair_out.reshape((parts, -1) + pair_out.shape[1:]), "z")
    grads = {}
    grad_four, grads[(PAIR, UP)], grads[(PAIR, DOWN)], grads[(ATTEND, PAIR_PROJ)], vecs = run_rows(
        functools.partial(transition_back_kernel, read_last), "pair_transition_back", steps,
        [
            (state_four, 0), (state_five, 0), (cotangent, 1), (single_sent, 1),
            (pair_cols, None), (turned((PAIR, UP)), None), (weights[(PAIR, UP)], None),
            (weights[(PAIR, DOWN)], None), (attend_cols, None), (weights[(ATTEND, PAIR_PROJ)], None),
        ],
        [
            (state_shape, F32, 0), (weights[(PAIR, UP)].shape, F32, None),
            (weights[(PAIR, DOWN)].shape, F32, None), (weights[(ATTEND, PAIR_PROJ)].shape, F32, None),
            ((8, width), F32, None),
        ],
        [wide, wide, wide, wide, ((SA_HEADS, block, length), F32)], 30,
    )
    grads[(PAIR, VECTORS)] = vecs

    def attention_back(prefix, read, read_grad, source, source_axis, grad, grad_axis, bias, totals, mixed):
        lowered_grad, bias_grad, grads[(prefix, QKVG)], grads[(prefix, OUTPUT)] = run_rows(
            functools.partial(attention_back_kernel, prefix == ENDING, read, read_grad),
            "attention_back", steps,
            [
                (alive, None), (source, source_axis), (grad, grad_axis), (bias, None), (totals, 0),
                (mixed, 0), (cols(prefix), None), (turned((prefix, QKVG)), None),
                (weights[(prefix, QKVG)], None), (weights[(prefix, OUTPUT)], None),
            ],
            [
                (state_shape, BF16, 0), ((devices, TA_HEADS, rows, length), BF16, None),
                (weights[(prefix, QKVG)].shape, F32, None), (weights[(prefix, OUTPUT)].shape, F32, None),
            ],
            [table, table], 34,
        )
        return lowered_grad, send(bias_grad, group)

    lowered_grad, bias_grad = attention_back(
        ENDING, read_flipped, read_plain, state_three, 1, grad_four, 0, bias_two, totals_two, mixed_two
    )
    (bias_grad,) = meet(8, bias_grad)
    flipped, bias_w_grad, vecs = run_rows(
        ending_end_kernel, "ending_attention_end", steps,
        [
            (state_three, 1), (grad_four, 0), (lowered_grad, 0), (bias_grad, 2), (cols(ENDING), None),
            (weights[(ENDING, BIAS_W)], None),
        ],
        [(flip_shape, BF16, 2), ((width, 8), F32, None), ((8, width), F32, None)],
        [wide, wide, head_scratch, flip_scratch],
    )
    grads[(ENDING, BIAS_PROJ)], grads[(ENDING, VECTORS)] = bias_w_grad, vecs
    flipped, held = after(flipped, grads[(ATTEND, PAIR_PROJ)])
    grads[(ATTEND, PAIR_PROJ)] = held
    grad_three = send(flipped, group)
    between(4, grads)
    grad_three = Both(meet(3, grad_three))
    pair_out = send(pair_out.reshape(flip_shape), group)
    pair_out = pair_out.reshape(parts, cores, rows, parts, -1, width).transpose(2, 3, 1, 0, 4, 5)
    pair_out = pair_out.reshape(rows, length, width)
    lowered_grad, bias_grad = attention_back(
        STARTING, read_plain, read_flipped, state_two, 0, grad_three, 1, bias_one, totals_one, mixed_one
    )
    square = weights[(INCOMING, GATE_OUT)].shape
    (
        grad_two, grad_tri, gate_back, bias_w_grad, grads[(INCOMING, PROJ_OUT)], grads[(INCOMING, GATE_OUT)], vecs,
    ) = run_halves(
        starting_end_kernel, "starting_end_incoming_out_back", steps,
        [
            (state_two, 0), (grad_three, 1), (lowered_grad, 0), (bias_grad, 2), (cols(STARTING), None),
            (weights[(STARTING, BIAS_W)], None), (state_one, 0), (tri_two, 1), (tri_cols(INCOMING), None),
            (turned((INCOMING, PROJ_OUT)), None), (turned((INCOMING, GATE_OUT)), None),
            (weights[(INCOMING, PROJ_OUT)], None), (weights[(INCOMING, GATE_OUT)], None),
        ],
        [
            (state_shape, F32, 0), ((hidden, half, length), BF16, 1), (state_shape, BF16, 0),
            ((width, 8), F32, None), (square, F32, None), (square, F32, None), ((8, width), F32, None),
        ],
        [wide, wide, wide, wide, head_scratch, tri_scratch], 26,
    )
    grads[(STARTING, BIAS_PROJ)], grads[(STARTING, VECTORS)] = bias_w_grad, vecs
    grad_tri = swap_all(by_device(grad_tri))
    product_grad = products(
        "incoming_product_back", functools.partial(tri_product_back_kernel, True),
        [grad_tri, product_two], product_half,
    )
    product_grad = swap_all(product_grad)
    product_grad = [*meet(4, product_grad[0]), product_grad[1]]
    (
        grad_one, grad_tri, gate_back, grads[(INCOMING, PROJ_GATE)], grads[(OUTGOING, PROJ_OUT)],
        grads[(OUTGOING, GATE_OUT)], vecs,
    ) = run_halves(
        functools.partial(tri_join_back_kernel, read_first), "incoming_in_outgoing_out_back", steps,
        [
            ([info[:half], info[half:]], "smem"), (alive, None), (state_one, 0), (product_grad, 3), (gate_back, 0), (grad_two, 0),
            (tri_cols(INCOMING), None), (turned((INCOMING, PROJ_GATE)), None),
            (weights[(INCOMING, PROJ_GATE)], None), (pair, 0), (tri_one, 1), (tri_cols(OUTGOING), None),
            (turned((OUTGOING, PROJ_OUT)), None), (turned((OUTGOING, GATE_OUT)), None),
            (weights[(OUTGOING, PROJ_OUT)], None), (weights[(OUTGOING, GATE_OUT)], None),
        ],
        [
            (state_shape, F32, 0), ((hidden, half, length), BF16, 1), (state_shape, BF16, 0),
            (weights[(INCOMING, PROJ_GATE)].shape, F32, None), (square, F32, None), (square, F32, None),
            ((8, width), F32, None),
        ],
        [wide, wide, wide, wide, product_scratch, tri_scratch], 37,
    )
    grads[(INCOMING, VECTORS)] = vecs
    between(5, grads)
    grad_tri = swap_all(by_device(grad_tri))
    grad_tri = [grad_tri[0], *meet(5, grad_tri[1])]
    product_grad = products(
        "outgoing_product_back", functools.partial(tri_product_back_kernel, False),
        [grad_tri, product_one], product_shape,
    )
    (product_grad,) = swap_all(product_grad)
    between(6, grads)
    pair_grad, grads[(OUTGOING, PROJ_GATE)], vecs = run_rows(
        functools.partial(tri_first_back_kernel, read_first, order_back), "outgoing_in_back", steps,
        [
            (info, "smem"), (alive, None), (pair, 0), (product_grad, 3), (gate_back, 0), (grad_one, 0),
            (tri_cols(OUTGOING), None), (turned((OUTGOING, PROJ_GATE)), None),
            (weights[(OUTGOING, PROJ_GATE)], None),
        ],
        [
            ((rows, length, width), BF16, 0), (weights[(OUTGOING, PROJ_GATE)].shape, F32, None),
            ((8, width), F32, None),
        ],
        [wide, wide, product_scratch], 20,
    )
    grads[(OUTGOING, VECTORS)] = vecs
    return pair_out, pair_grad, grads


HELD = {
    (PAIR, VECTORS): ((PAIR, NORM_GAIN), (PAIR, NORM_BIAS), (ATTEND, PAIR_GAIN), (ATTEND, PAIR_BIAS)),
    (ENDING, VECTORS): ((ENDING, NORM_GAIN), (ENDING, NORM_BIAS)),
    (STARTING, VECTORS): (
        (STARTING, NORM_GAIN), (STARTING, NORM_BIAS), (INCOMING, OUT_GAIN), (INCOMING, OUT_BIAS)
    ),
    (INCOMING, VECTORS): (
        (INCOMING, NORM_GAIN), (INCOMING, NORM_BIAS), (OUTGOING, OUT_GAIN), (OUTGOING, OUT_BIAS)
    ),
    (OUTGOING, VECTORS): ((OUTGOING, NORM_GAIN), (OUTGOING, NORM_BIAS)),
}


def vector_part(grads, table, name, first, last):
    pairs = [
        (row, held) for row, held in enumerate(HELD[name]) if first <= table[held][0] < last
    ]
    return (pairs, grads[name])


def fast_shards(parts, cores, pair, single, lengths, params, moment_one, moment_two, pair_cotangent, single_cotangent):
    entries = layout(C, H, S, TA_HEADS, SA_HEADS)
    table, total = table_of(entries)
    count = total // STRIDE
    shard_size = params.shape[0]
    attend = table[(ATTEND, NORM_GAIN)][0]
    pair_lanes = -(-attend * STRIDE // count)
    single_lane = attend * STRIDE // count
    devices = parts * cores
    line, group = ("z", "core"), ("crop", "core")
    row_index = lax.axis_index(line)
    odd = ((row_index * shard_size) % STRIDE) // (STRIDE // 2)
    place = jnp.stack([odd, odd]).astype(jnp.int32)
    shard_rows = jnp.pad(params, (0, RUN * STRIDE * STRIDE - shard_size)).reshape(-1, STRIDE)
    (runs,) = whole_call(
        runs_kernel, "parameter_runs", [(place, "smem"), (shard_rows, None)],
        [((STRIDE, RUN, STRIDE), BF16)], [((STRIDE, RUN, STRIDE), F32)],
    )
    rows, length, width = pair.shape[1:]
    send = in_turn()
    pair_in = send(pair[0].reshape(parts, -1, length, width), "crop")
    first_runs = lax.all_gather(runs[:pair_lanes], line)
    pair_in, _, lengths = after(pair_in, runs, lengths)
    live = lax.all_gather(jnp.broadcast_to(lengths.astype(F32), (8, STRIDE)), "crop")
    pair_in = send(pair_in, "z").reshape(rows, length, width)
    weights = unpack_pair(table, total, first_runs)
    size = rows // parts
    blocks = np.arange(length // size).reshape(parts, cores, parts)
    order = blocks.transpose(2, 1, 0).reshape(-1)
    orders = (order.tolist(), np.argsort(order).tolist())
    tokens = (order[:, None] * size + np.arange(size)).reshape(-1)
    live = live[lax.axis_index("z"), 0, 0]
    width = single.shape[2]
    mask = (tokens.astype(np.float32) < live).astype(F32)
    info = lax.dynamic_slice_in_dim(mask, lax.axis_index(group) * rows, rows).astype(jnp.int32)
    alive = jnp.broadcast_to(mask, (8, length))
    held = {}
    single_grads = {}

    def middle(bias):
        found = single_middle(held["state"], held["back"], held["projected"], bias, alive, weights)
        held["out"], held["grad"], grad_scores, grads, held["pending"] = found
        single_grads.update(grads)
        return grad_scores

    def meet(number, *values):
        if number == 0:
            others = [held["runs"]]
        elif number == 1:
            others = [weights[(SINGLE, UP)], held["state"]]
        elif number == 2:
            others = [held["projected"][1]]
        elif number == 3:
            others = [reduced[3]]
        elif number == 8:
            others = [single_grads[(ATTEND, QKVG)]]
        elif number == 4:
            values, reduced[2] = after(*values, reduced[2])
            return [values]
        else:
            values, held["both"], reduced[1] = after(*values, held["both"], reduced[1])
            return [values]
        return after(*values, *others)[: len(values)]

    def reduce_runs(sent):
        return jnp.sum(send(sent, line).astype(F32), axis=0).astype(BF16)

    reduced = {}
    lines_held = list(enumerate(SINGLE_VECTORS))
    late_lanes = -(-table[(OUTGOING, OUT_GAIN)][0] * STRIDE // count)
    late_end = table[(OUTGOING, GATE_OUT)][0]
    early = table[(OUTGOING, PROJ_OUT)][0]

    def lines():
        values = jnp.concatenate([single_grads[name].reshape(1, S) for name in SINGLE_VECTORS], axis=0)
        return jnp.pad(values, ((0, 8 - len(SINGLE_VECTORS)), (0, 0)))

    def between(number, grads):
        if number == 0:
            last_runs = after(runs[single_lane:], pair_in, weights[(OUTGOING, COLS)], live)[0]
            held["runs"] = lax.all_gather(last_runs, line)
            weights.update(unpack_single(table, total, single_lane, held["runs"]))
            for index, name in enumerate(SINGLE_VECTORS):
                weights[name] = weights[(SINGLE, VECTORS)][index]
            both = jnp.concatenate([single[0], single_cotangent[0]], axis=1)
            both = lax.all_gather(both, ("crop",) + line)
            both = both.reshape(parts, parts, cores, parts, -1, 2 * width)
            here = lax.axis_index("z"), lax.axis_index("core"), lax.axis_index("crop")
            both = both[here[0], :, here[1], here[2]].reshape(rows, 2 * width).astype(F32)
            held["state"], held["back"] = both[:, :width], both[:, width:]
            return
        if number == 1:
            lowered, qkvg, both = single_project(held["state"], weights, devices)
            held["projected"] = lowered, qkvg, send(both, group)
            return
        if number == 2:
            parts_held = grads[:, :, SA_HEADS * rows :]
            grad = held["grad"] + single_attend_end(held["pending"], parts_held, weights, single_grads)
            both = jnp.concatenate([held["out"], grad], axis=1).astype(BF16)
            held["both"] = lax.all_gather(both, ("crop",) + line)
            return
        if number == 6:
            reduced[1] = reduce_runs(reduced[1])
            return
        if number == 4:
            sent = pack(
                "single_gradient", table, total, devices, (pair_lanes, STRIDE), attend,
                [(name, single_grads[name]) for name in SINGLE_MATRICES]
                + [((ATTEND, PAIR_PROJ), grads[(ATTEND, PAIR_PROJ)])]
                + [vector_part(grads, table, (PAIR, VECTORS), attend, total), (lines_held, lines())],
            )
            reduced[3] = sent
            sent = sent.reshape((devices * parts, -1) + sent.shape[2:])
            reduced[2] = lax.psum_scatter(sent, line + ("crop",), scatter_dimension=0, tiled=False)
            return
        taken = -(-(pair_lanes * count - (attend + 2 * S // STRIDE) * STRIDE) // (4 * S))
        sent = pack(
            "pair_gradient", table, total, devices, (late_lanes, pair_lanes), early,
            [(name, grads[name]) for name in PAIR_MATRICES if table[name][0] >= early]
            + [(name, grads[name]) for name in ((STARTING, BIAS_PROJ), (ENDING, BIAS_PROJ))]
            + [vector_part(grads, table, name, early, attend) for name in HELD if name in grads]
            + [(lines_held[:2], lines()), ((ATTEND, QKVG), single_grads[(ATTEND, QKVG)][: -(-taken // 8) * 8])],
        )
        reduced[1] = sent

    pair_out, pair_grad, grads = pair_path(
        pair_in, info, alive, orders, weights, pair_cotangent[0], middle, between, meet, send, group, parts
    )
    sent = pack(
        "outgoing_gradient", table, total, devices, (0, late_lanes), 0,
        [(name, grads[name]) for name in PAIR_MATRICES if table[name][0] < late_end]
        + [vector_part(grads, table, name, 0, late_end) for name in ((OUTGOING, VECTORS), (INCOMING, VECTORS))],
    )
    reduced[0] = reduce_runs(sent)
    pair_grad = send(pair_grad.reshape(parts, -1, length, pair_grad.shape[2]), "z")
    pair_grad, held["z"] = send(pair_grad, "crop").reshape(rows, length, -1).astype(F32), pair_grad
    both = held["both"].reshape(parts, parts, cores, parts, -1, 2 * width)
    both = both[:, lax.axis_index("crop"), lax.axis_index("core"), lax.axis_index("z")]
    both = both.reshape(rows, 2 * width)
    single_out, single_grad = both[:, :width], both[:, width:].astype(F32)
    summed = lax.all_gather(jnp.concatenate([reduced[0], reduced[1]], axis=0), "crop")
    others = lax.all_gather(reduced[2], "crop")
    shard, squares = whole_call(
        functools.partial(shard_kernel, shard_size), "gradient_share",
        [(place, "smem"), (summed, None), (others, None)],
        [((RUN * STRIDE, STRIDE), F32), ((8, STRIDE), F32)], [((STRIDE, RUN, STRIDE), F32)],
    )
    shard = shard.reshape(-1)[:shard_size]
    squares = after(squares, held["z"])[0]
    clip_norm = jnp.sqrt(jnp.sum(lax.all_gather(squares, line)))
    clipped = shard * (CLIP / jnp.maximum(clip_norm, CLIP))
    new_first = BETA_ONE * moment_one + (1.0 - BETA_ONE) * clipped
    new_second = BETA_TWO * moment_two + (1.0 - BETA_TWO) * clipped * clipped
    rates, decays = rate_tables(entries)
    rate_shard = lax.dynamic_slice_in_dim(jnp.asarray(rates), row_index * shard_size, shard_size)
    decay_shard = lax.dynamic_slice_in_dim(jnp.asarray(decays), row_index * shard_size, shard_size)
    first_hat = new_first / (1.0 - BETA_ONE**STEP)
    second_hat = new_second / (1.0 - BETA_TWO**STEP)
    new_params = params - rate_shard * (
        first_hat / (jnp.sqrt(second_hat) + ADAM_EPS) + decay_shard * params
    )
    return (
        pair_out[None],
        single_out[None],
        pair_grad[None],
        single_grad[None],
        new_params,
        new_first,
        new_second,
        clip_norm,
    )


def solution(mesh):
    crops, devices = mesh.devices.shape
    table, total = table_of(layout(C, H, S, TA_HEADS, SA_HEADS))
    count = total // STRIDE
    lanes = STRIDE + -table[(ATTEND, NORM_GAIN)][0] * STRIDE // count
    fast = devices == 2 * crops and LENGTH % (devices * 16) == 0 and count // devices + 2 <= RUN * STRIDE and lanes % crops == 0
    row = "row"
    if fast:
        mesh = jax.sharding.Mesh(mesh.devices.reshape(crops, crops, 2), ("crop", "z", "core"))
        row = ("z", "core")
    split = [P("crop", row, None, None), P("crop", row, None), P("crop"), P(row)]
    pair, single, lengths, share = split
    return jax.shard_map(
        functools.partial(fast_shards, crops, 2) if fast else shards,
        mesh=mesh,
        in_specs=(pair, single, lengths, share, share, share, pair, single),
        out_specs=(pair, single, pair, single, share, share, share, P()),
        check_vma=False,
    )
```

```python
import functools
import math

import jax
import jax.numpy as jnp
import numpy as np
from jax import lax
from jax.experimental import pallas as pl
from jax.experimental.pallas import tpu as pltpu
from jax.sharding import PartitionSpec as P

C = 128
H = 128
S = 384
TA_HEADS = 4
SA_HEADS = 16
STEP = 10
STRIDE = 128
LENGTH = 256

OUTGOING, INCOMING, STARTING, ENDING, PAIR, ATTEND, SINGLE = range(7)
(
    NORM_GAIN,
    NORM_BIAS,
    PROJ_GATE,
    OUT_GAIN,
    OUT_BIAS,
    PROJ_OUT,
    GATE_OUT,
    QKVG,
    BIAS_PROJ,
    OUTPUT,
    UP,
    DOWN,
    PAIR_GAIN,
    PAIR_BIAS,
    PAIR_PROJ,
    COLS,
    BIAS_W,
    BIAS_T,
    VECTORS,
    T,
) = range(7, 27)


EPSILON = 1e-05
MASKED = 1000000000.0
BETA_ONE = 0.9
BETA_TWO = 0.95
ADAM_EPS = 1e-08
CLIP = 1.0


def layout(pair_width, hidden_width, single_width, tri_heads, att_heads):
    entries = []
    for prefix in (OUTGOING, INCOMING):
        entries += [
            ((prefix, NORM_GAIN), (pair_width,)),
            ((prefix, NORM_BIAS), (pair_width,)),
            ((prefix, PROJ_GATE), (pair_width, 4 * hidden_width)),
            ((prefix, OUT_GAIN), (hidden_width,)),
            ((prefix, OUT_BIAS), (hidden_width,)),
            ((prefix, PROJ_OUT), (hidden_width, pair_width)),
            ((prefix, GATE_OUT), (pair_width, pair_width)),
        ]
    for prefix in (STARTING, ENDING):
        entries += [
            ((prefix, NORM_GAIN), (pair_width,)),
            ((prefix, NORM_BIAS), (pair_width,)),
            ((prefix, QKVG), (pair_width, 4 * pair_width)),
            ((prefix, BIAS_PROJ), (pair_width, tri_heads)),
            ((prefix, OUTPUT), (pair_width, pair_width)),
        ]
    entries += [
        ((PAIR, NORM_GAIN), (pair_width,)),
        ((PAIR, NORM_BIAS), (pair_width,)),
        ((PAIR, UP), (pair_width, 8 * pair_width)),
        ((PAIR, DOWN), (4 * pair_width, pair_width)),
        ((ATTEND, NORM_GAIN), (single_width,)),
        ((ATTEND, NORM_BIAS), (single_width,)),
        ((ATTEND, QKVG), (single_width, 4 * single_width)),
        ((ATTEND, PAIR_GAIN), (pair_width,)),
        ((ATTEND, PAIR_BIAS), (pair_width,)),
        ((ATTEND, PAIR_PROJ), (pair_width, att_heads)),
        ((ATTEND, OUTPUT), (single_width, single_width)),
        ((SINGLE, NORM_GAIN), (single_width,)),
        ((SINGLE, NORM_BIAS), (single_width,)),
        ((SINGLE, UP), (single_width, 8 * single_width)),
        ((SINGLE, DOWN), (4 * single_width, single_width)),
    ]
    return entries


def logical_order(flat):
    return flat.reshape(-1, STRIDE).T.reshape(-1)


def stored_order(vector):
    return vector.reshape(STRIDE, -1).T.reshape(-1)


def rate_tables(entries):
    rates = []
    decays = []
    for name, shape in entries:
        count = math.prod(shape)
        if len(shape) == 1:
            rates.append(np.full(count, 0.5, np.float32))
            decays.append(np.zeros(count, np.float32))
        else:
            rates.append(np.full(count, 2.0 / math.sqrt(shape[0]), np.float32))
            decays.append(np.full(count, 0.01, np.float32))
    rates = np.concatenate(rates)
    decays = np.concatenate(decays)
    return (rates.reshape(STRIDE, -1).T.reshape(-1), decays.reshape(STRIDE, -1).T.reshape(-1))


def unpack(flat, entries):
    pieces = {}
    offset = 0
    for name, shape in entries:
        count = math.prod(shape)
        pieces[name] = flat[offset : offset + count].reshape(shape)
        offset += count
    return pieces


def layer_norm(values, gain, shift):
    centred = values - jnp.mean(values, axis=-1, keepdims=True)
    spread = jnp.mean(centred * centred, axis=-1, keepdims=True)
    return centred * lax.rsqrt(spread + EPSILON) * gain + shift


def norm_backward(values, gain, shift, grad):
    _, pullback = jax.vjp(layer_norm, values, gain, shift)
    return pullback(grad)


def norm_pair(weights, prefix):
    return (
        weights[(prefix, NORM_GAIN)].astype(jnp.float32),
        weights[(prefix, NORM_BIAS)].astype(jnp.float32),
    )


def gated_pair(project, pair_mask):
    half = project.shape[-1] // 2
    return project[..., :half] * jax.nn.sigmoid(project[..., half:]) * pair_mask[..., None]


def gated_output(values, gate):
    return values * jax.nn.sigmoid(gate)


def swiglu(hidden):
    half = hidden.shape[-1] // 2
    return jax.nn.silu(hidden[..., :half]) * hidden[..., half:]


def matmul(left, right):
    return jnp.dot(left, right, preferred_element_type=jnp.float32)


def outer_sum(left, right):
    return jnp.einsum(
        "nc,nd->cd",
        left.reshape(-1, left.shape[-1]),
        right.reshape(-1, right.shape[-1]),
        preferred_element_type=jnp.float32,
    )


def flip(values):
    moved = lax.all_to_all(values, "row", split_axis=1, concat_axis=0, tiled=True)
    return jnp.swapaxes(moved, 0, 1)


def channel_forward(first, second, incoming):
    whole_first, whole_second = (
        lax.all_to_all(first, "row", split_axis=2, concat_axis=0, tiled=True),
        lax.all_to_all(second, "row", split_axis=2, concat_axis=0, tiled=True),
    )
    if incoming:
        local_tri = jnp.einsum(
            "kih,kjh->ijh", whole_first, whole_second, preferred_element_type=jnp.float32
        )
        local_tri = local_tri.astype(jnp.bfloat16).astype(jnp.float32)
    else:
        local_tri = jnp.einsum(
            "ikh,jkh->ijh", whole_first, whole_second, preferred_element_type=jnp.float32
        )
    tri = lax.all_to_all(
        local_tri.astype(jnp.bfloat16), "row", split_axis=0, concat_axis=2, tiled=True
    ).astype(local_tri.dtype)
    return (tri, whole_first, whole_second)


def channel_backward(grad_tri, whole_first, whole_second, incoming):
    whole_grad = lax.all_to_all(grad_tri, "row", split_axis=2, concat_axis=0, tiled=True)
    if incoming:
        grad_a = jnp.einsum(
            "ijh,kjh->kih", whole_grad, whole_second, preferred_element_type=jnp.float32
        )
        grad_b = jnp.einsum(
            "ijh,kih->kjh", whole_grad, whole_first, preferred_element_type=jnp.float32
        )
    else:
        grad_a = jnp.einsum(
            "ijh,jkh->ikh", whole_grad, whole_second, preferred_element_type=jnp.float32
        )
        grad_b = jnp.einsum(
            "ijh,ikh->jkh", whole_grad, whole_first, preferred_element_type=jnp.float32
        )
    return (
        lax.all_to_all(
            grad_a.astype(jnp.bfloat16), "row", split_axis=0, concat_axis=2, tiled=True
        ).astype(grad_a.dtype),
        lax.all_to_all(
            grad_b.astype(jnp.bfloat16), "row", split_axis=0, concat_axis=2, tiled=True
        ).astype(grad_b.dtype),
    )


def triangle_forward(state, pair_mask, weights, prefix, incoming):
    gain, shift = norm_pair(weights, prefix)
    lowered = layer_norm(state, gain, shift).astype(jnp.bfloat16)
    project = matmul(lowered, weights[(prefix, PROJ_GATE)])
    product = gated_pair(project, pair_mask).astype(jnp.bfloat16)
    half = product.shape[-1] // 2
    tri, own, other = channel_forward(product[..., :half], product[..., half:], incoming)
    out_gain = weights[(prefix, OUT_GAIN)].astype(jnp.float32)
    out_shift = weights[(prefix, OUT_BIAS)].astype(jnp.float32)
    out_low = layer_norm(tri, out_gain, out_shift).astype(jnp.bfloat16)
    output = matmul(out_low, weights[(prefix, PROJ_OUT)])
    gate_out = matmul(lowered, weights[(prefix, GATE_OUT)])
    update = gated_output(output, gate_out)
    return (update, (state, lowered, lowered, project, own, other, tri, out_low, output, gate_out))


def triangle_backward(saved, grad_update, pair_mask, weights, prefix, incoming, grads):
    state, lowered, framed, project, own, other, tri, out_low, output, gate_out = saved
    _, pullback = jax.vjp(gated_output, output, gate_out)
    grad_output, grad_gate = pullback(grad_update)
    grad_output = grad_output.astype(jnp.bfloat16)
    grad_gate = grad_gate.astype(jnp.bfloat16)
    grads[(prefix, PROJ_OUT)] = outer_sum(out_low, grad_output)
    grads[(prefix, GATE_OUT)] = outer_sum(lowered, grad_gate)
    grad_normed = matmul(grad_output, weights[(prefix, PROJ_OUT)].T)
    out_gain = weights[(prefix, OUT_GAIN)].astype(jnp.float32)
    out_shift = weights[(prefix, OUT_BIAS)].astype(jnp.float32)
    grad_tri, grads[(prefix, OUT_GAIN)], grads[(prefix, OUT_BIAS)] = norm_backward(
        tri, out_gain, out_shift, grad_normed
    )
    grad_tri = grad_tri.astype(jnp.bfloat16)
    grad_first, grad_second = channel_backward(grad_tri, own, other, incoming)
    _, pullback = jax.vjp(lambda values: gated_pair(values, pair_mask), project)
    (grad_project,) = pullback(jnp.concatenate([grad_first, grad_second], axis=-1))
    grad_project = grad_project.astype(jnp.bfloat16)
    grads[(prefix, PROJ_GATE)] = outer_sum(framed, grad_project)
    grad_framed = matmul(grad_project, weights[(prefix, PROJ_GATE)].T)
    if incoming:
        grad_framed = grad_framed.astype(jnp.bfloat16).astype(jnp.float32)
    grad_lowered = grad_framed + matmul(grad_gate, weights[(prefix, GATE_OUT)].T)
    gain, shift = norm_pair(weights, prefix)
    grad_state, grads[(prefix, NORM_GAIN)], grads[(prefix, NORM_BIAS)] = norm_backward(
        state, gain, shift, grad_lowered
    )
    return grad_state


def row_scores(query, key, bias, penalty, scale):
    scores = jnp.einsum("jhd,khd->hjk", query, key, preferred_element_type=jnp.float32) * scale
    return scores + bias.astype(jnp.float32) + penalty[None, None, :]


def attention_forward(state, penalty, weights, prefix, ending):
    gain, shift = norm_pair(weights, prefix)
    lowered = layer_norm(state, gain, shift).astype(jnp.bfloat16)
    framed = flip(lowered) if ending else lowered
    rows, length, width = framed.shape
    size = width // TA_HEADS
    scale = size ** (-0.5)
    qkvg = matmul(framed, weights[(prefix, QKVG)])
    queries = qkvg[..., :width].astype(jnp.bfloat16).reshape(rows, length, TA_HEADS, size)
    keys = qkvg[..., width : 2 * width].astype(jnp.bfloat16).reshape(rows, length, TA_HEADS, size)
    values = (
        qkvg[..., 2 * width : 3 * width].astype(jnp.bfloat16).reshape(rows, length, TA_HEADS, size)
    )
    gate = qkvg[..., 3 * width :]
    local_bias = (
        matmul(framed, weights[(prefix, BIAS_PROJ)]).astype(jnp.bfloat16).transpose(2, 0, 1)
    )
    bias = lax.all_gather(local_bias, "row", axis=1, tiled=True)

    def forward_row(items):
        query, key, value = items
        scores = row_scores(query, key, bias, penalty, scale)
        top = jnp.max(scores, axis=-1, keepdims=True)
        shifted = jnp.exp(scores - top)
        total = jnp.sum(shifted, axis=-1, keepdims=True)
        probs = (shifted / total).astype(jnp.bfloat16)
        mixed = jnp.einsum("hjk,khd->jhd", probs, value, preferred_element_type=jnp.float32)
        return (mixed, top[..., 0] + jnp.log(total[..., 0]))

    mixed, log_totals = lax.map(forward_row, (queries, keys, values))
    mixed = mixed.reshape(rows, length, width)
    gated_low = gated_output(mixed, gate).astype(jnp.bfloat16)
    returned = flip(gated_low) if ending else gated_low
    update = matmul(returned, weights[(prefix, OUTPUT)])
    return (update, (state, framed, queries, keys, values, gate, bias, mixed, log_totals, returned))


def attention_backward(saved, grad_update, penalty, weights, prefix, ending, grads):
    state, framed, queries, keys, values, gate, bias, mixed, log_totals, returned = saved
    rows, length, width = framed.shape
    size = width // TA_HEADS
    scale = size ** (-0.5)
    grad_low = grad_update.astype(jnp.bfloat16)
    grads[(prefix, OUTPUT)] = outer_sum(returned, grad_low)
    grad_gated = matmul(grad_low, weights[(prefix, OUTPUT)].T)
    if ending:
        grad_gated = flip(grad_gated.astype(jnp.bfloat16)).astype(jnp.float32)
    _, pullback = jax.vjp(gated_output, mixed, gate)
    grad_mixed, grad_gate = pullback(grad_gated)
    grad_mixed = grad_mixed.astype(jnp.bfloat16).reshape(rows, length, TA_HEADS, size)

    def back_row(carry, items):
        query, key, value, log_total, grad_row = items
        scores = row_scores(query, key, bias, penalty, scale)
        probs = jnp.exp(scores - log_total[..., None])
        grad_probs = jnp.einsum("jhd,khd->hjk", grad_row, value, preferred_element_type=jnp.float32)
        delta = jnp.sum(probs * grad_probs, axis=-1, keepdims=True)
        grad_scores = (probs * (grad_probs - delta)).astype(jnp.bfloat16)
        grad_query = (
            jnp.einsum("hjk,khd->jhd", grad_scores, key, preferred_element_type=jnp.float32) * scale
        )
        grad_key = (
            jnp.einsum("hjk,jhd->khd", grad_scores, query, preferred_element_type=jnp.float32)
            * scale
        )
        grad_value = jnp.einsum(
            "hjk,jhd->khd", probs.astype(jnp.bfloat16), grad_row, preferred_element_type=jnp.float32
        )
        return (carry + grad_scores.astype(jnp.float32), (grad_query, grad_key, grad_value))

    empty = jnp.zeros(bias.shape, jnp.float32)
    grad_bias, (grad_query, grad_key, grad_value) = lax.scan(
        back_row, empty, (queries, keys, values, log_totals, grad_mixed)
    )
    grad_bias = lax.psum_scatter(grad_bias, "row", scatter_dimension=1, tiled=True)
    grad_bias = grad_bias.transpose(1, 2, 0).astype(jnp.bfloat16)
    grad_qkvg = jnp.concatenate(
        [
            grad_query.reshape(rows, length, width),
            grad_key.reshape(rows, length, width),
            grad_value.reshape(rows, length, width),
            grad_gate,
        ],
        axis=-1,
    ).astype(jnp.bfloat16)
    grads[(prefix, QKVG)] = outer_sum(framed, grad_qkvg)
    grads[(prefix, BIAS_PROJ)] = outer_sum(framed, grad_bias)
    grad_framed = matmul(grad_qkvg, weights[(prefix, QKVG)].T) + matmul(
        grad_bias, weights[(prefix, BIAS_PROJ)].T
    )
    if ending:
        grad_framed = flip(grad_framed.astype(jnp.bfloat16)).astype(jnp.float32)
    gain, shift = norm_pair(weights, prefix)
    grad_state, grads[(prefix, NORM_GAIN)], grads[(prefix, NORM_BIAS)] = norm_backward(
        state, gain, shift, grad_framed
    )
    return grad_state


def transition_forward(state, weights, prefix):
    gain, shift = norm_pair(weights, prefix)
    lowered = layer_norm(state, gain, shift).astype(jnp.bfloat16)
    hidden = matmul(lowered, weights[(prefix, UP)])
    mixed_low = swiglu(hidden).astype(jnp.bfloat16)
    update = matmul(mixed_low, weights[(prefix, DOWN)])
    return (update, (state, lowered, hidden, mixed_low))


def transition_backward(saved, grad_update, weights, prefix, grads):
    state, lowered, hidden, mixed_low = saved
    grad_low = grad_update.astype(jnp.bfloat16)
    grads[(prefix, DOWN)] = outer_sum(mixed_low, grad_low)
    grad_mixed = matmul(grad_low, weights[(prefix, DOWN)].T)
    _, pullback = jax.vjp(swiglu, hidden)
    (grad_hidden,) = pullback(grad_mixed)
    grad_hidden = grad_hidden.astype(jnp.bfloat16)
    grads[(prefix, UP)] = outer_sum(lowered, grad_hidden)
    grad_lowered = matmul(grad_hidden, weights[(prefix, UP)].T)
    gain, shift = norm_pair(weights, prefix)
    grad_state, grads[(prefix, NORM_GAIN)], grads[(prefix, NORM_BIAS)] = norm_backward(
        state, gain, shift, grad_lowered
    )
    return grad_state


def single_forward(single_state, pair_state, penalty, weights):
    gain, shift = norm_pair(weights, ATTEND)
    lowered = layer_norm(single_state, gain, shift).astype(jnp.bfloat16)
    rows, width = lowered.shape
    size = width // SA_HEADS
    qkvg = matmul(lowered, weights[(ATTEND, QKVG)])
    query = qkvg[:, :width].astype(jnp.bfloat16).reshape(rows, SA_HEADS, size)
    key = qkvg[:, width : 2 * width].astype(jnp.bfloat16)
    value = qkvg[:, 2 * width : 3 * width].astype(jnp.bfloat16)
    gate = qkvg[:, 3 * width :]
    keys_all, values_all = (
        lax.all_gather(key, "row", axis=0, tiled=True),
        lax.all_gather(value, "row", axis=0, tiled=True),
    )
    keys_all = keys_all.reshape(-1, SA_HEADS, size)
    values_all = values_all.reshape(-1, SA_HEADS, size)
    pair_gain = weights[(ATTEND, PAIR_GAIN)].astype(jnp.float32)
    pair_shift = weights[(ATTEND, PAIR_BIAS)].astype(jnp.float32)
    pair_low = layer_norm(pair_state, pair_gain, pair_shift).astype(jnp.bfloat16)
    bias = matmul(pair_low, weights[(ATTEND, PAIR_PROJ)]).transpose(2, 0, 1)
    scores = jnp.einsum(
        "ihd,jhd->hij", query, keys_all, preferred_element_type=jnp.float32
    ) * size ** (-0.5)
    scores = scores + bias + penalty[None, None, :]
    probs = jax.nn.softmax(scores, axis=-1)
    probs_low = probs.astype(jnp.bfloat16)
    mixed = jnp.einsum(
        "hij,jhd->ihd", probs_low, values_all, preferred_element_type=jnp.float32
    ).reshape(rows, width)
    gated_low = gated_output(mixed, gate).astype(jnp.bfloat16)
    update = matmul(gated_low, weights[(ATTEND, OUTPUT)])
    return (
        update,
        (
            single_state,
            pair_state,
            lowered,
            query,
            keys_all,
            values_all,
            gate,
            pair_low,
            probs,
            probs_low,
            mixed,
            gated_low,
        ),
    )


def single_backward(saved, grad_update, weights, grads):
    (
        single_state,
        pair_state,
        lowered,
        query,
        keys_all,
        values_all,
        gate,
        pair_low,
        probs,
        probs_low,
        mixed,
        gated_low,
    ) = saved
    rows, width = lowered.shape
    size = width // SA_HEADS
    scale = size ** (-0.5)
    grad_low = grad_update.astype(jnp.bfloat16)
    grads[(ATTEND, OUTPUT)] = outer_sum(gated_low, grad_low)
    grad_gated = matmul(grad_low, weights[(ATTEND, OUTPUT)].T)
    _, pullback = jax.vjp(gated_output, mixed, gate)
    grad_mixed, grad_gate = pullback(grad_gated)
    grad_mixed = grad_mixed.astype(jnp.bfloat16).reshape(rows, SA_HEADS, size)
    grad_probs = jnp.einsum(
        "ihd,jhd->hij", grad_mixed, values_all, preferred_element_type=jnp.float32
    )
    delta = jnp.sum(probs * grad_probs, axis=-1, keepdims=True)
    grad_scores = (probs * (grad_probs - delta)).astype(jnp.bfloat16)
    grad_query = (
        jnp.einsum("hij,jhd->ihd", grad_scores, keys_all, preferred_element_type=jnp.float32)
        * scale
    )
    key_part = (
        jnp.einsum("hij,ihd->jhd", grad_scores, query, preferred_element_type=jnp.float32) * scale
    )
    value_part = jnp.einsum(
        "hij,ihd->jhd", probs_low, grad_mixed, preferred_element_type=jnp.float32
    )
    grad_key, grad_value = (
        lax.psum_scatter(key_part.reshape(-1, width), "row", scatter_dimension=0, tiled=True),
        lax.psum_scatter(value_part.reshape(-1, width), "row", scatter_dimension=0, tiled=True),
    )
    grad_qkvg = jnp.concatenate(
        [grad_query.reshape(rows, width), grad_key, grad_value, grad_gate], axis=-1
    ).astype(jnp.bfloat16)
    grads[(ATTEND, QKVG)] = outer_sum(lowered, grad_qkvg)
    grad_lowered = matmul(grad_qkvg, weights[(ATTEND, QKVG)].T)
    gain, shift = norm_pair(weights, ATTEND)
    grad_single, grads[(ATTEND, NORM_GAIN)], grads[(ATTEND, NORM_BIAS)] = norm_backward(
        single_state, gain, shift, grad_lowered
    )
    grad_bias = grad_scores.transpose(1, 2, 0)
    grads[(ATTEND, PAIR_PROJ)] = outer_sum(pair_low, grad_bias)
    grad_pair_low = matmul(grad_bias, weights[(ATTEND, PAIR_PROJ)].T)
    pair_gain = weights[(ATTEND, PAIR_GAIN)].astype(jnp.float32)
    pair_shift = weights[(ATTEND, PAIR_BIAS)].astype(jnp.float32)
    grad_pair, grads[(ATTEND, PAIR_GAIN)], grads[(ATTEND, PAIR_BIAS)] = norm_backward(
        pair_state, pair_gain, pair_shift, grad_pair_low
    )
    return (grad_single, grad_pair)


def shards(pair, single, lengths, params, moment_one, moment_two, pair_cotangent, single_cotangent):
    entries = layout(C, H, S, TA_HEADS, SA_HEADS)
    full = lax.all_gather(params.astype(jnp.bfloat16), "row", axis=0, tiled=True)
    weights = unpack(logical_order(full), entries)
    rows = pair.shape[1]
    length = pair.shape[2]
    first_row = lax.axis_index("row") * rows
    mask = (jnp.arange(length, dtype=jnp.int32) < lengths[0]).astype(jnp.float32)
    mask_rows = lax.dynamic_slice_in_dim(mask, first_row, rows)
    pair_mask = mask_rows[:, None] * mask[None, :]
    penalty = (mask - 1.0) * MASKED
    state = pair[0].astype(jnp.float32)
    saved = {}
    for prefix, incoming in ((OUTGOING, False), (INCOMING, True)):
        update, saved[prefix] = triangle_forward(state, pair_mask, weights, prefix, incoming)
        state = state + update
    for prefix, ending in ((STARTING, False), (ENDING, True)):
        update, saved[prefix] = attention_forward(state, penalty, weights, prefix, ending)
        state = state + update
    update, saved[PAIR] = transition_forward(state, weights, PAIR)
    pair_final = state + update
    single_state = single[0].astype(jnp.float32)
    update, saved[ATTEND] = single_forward(single_state, pair_final, penalty, weights)
    single_mid = single_state + update
    update, saved[SINGLE] = transition_forward(single_mid, weights, SINGLE)
    single_final = single_mid + update
    grads = {}
    grad_single = single_cotangent[0].astype(jnp.float32)
    grad_single = grad_single + transition_backward(
        saved[SINGLE], grad_single, weights, SINGLE, grads
    )
    from_single, from_pair = single_backward(saved[ATTEND], grad_single, weights, grads)
    grad_single = grad_single + from_single
    grad_pair = pair_cotangent[0].astype(jnp.float32) + from_pair
    grad_pair = grad_pair + transition_backward(saved[PAIR], grad_pair, weights, PAIR, grads)
    for prefix, ending in ((ENDING, True), (STARTING, False)):
        grad_pair = grad_pair + attention_backward(
            saved[prefix], grad_pair, penalty, weights, prefix, ending, grads
        )
    for prefix, incoming in ((INCOMING, True), (OUTGOING, False)):
        grad_pair = grad_pair + triangle_backward(
            saved[prefix], grad_pair, pair_mask, weights, prefix, incoming, grads
        )
    flat = stored_order(jnp.concatenate([grads[name].reshape(-1) for name, shape in entries]))
    shard_size = params.shape[0]
    row_index = lax.axis_index("row")
    total = lax.psum(flat, ("crop", "row"))
    shard = lax.dynamic_slice_in_dim(total, row_index * shard_size, shard_size)
    norm_squared = jnp.sum(total * total)
    clip_norm = jnp.sqrt(norm_squared)
    clipped = shard * (CLIP / jnp.maximum(clip_norm, CLIP))
    new_first = BETA_ONE * moment_one + (1.0 - BETA_ONE) * clipped
    new_second = BETA_TWO * moment_two + (1.0 - BETA_TWO) * clipped * clipped
    rates, decays = rate_tables(entries)
    rate_shard = lax.dynamic_slice_in_dim(jnp.asarray(rates), row_index * shard_size, shard_size)
    decay_shard = lax.dynamic_slice_in_dim(jnp.asarray(decays), row_index * shard_size, shard_size)
    first_hat = new_first / (1.0 - BETA_ONE**STEP)
    second_hat = new_second / (1.0 - BETA_TWO**STEP)
    new_params = params - rate_shard * (
        first_hat / (jnp.sqrt(second_hat) + ADAM_EPS) + decay_shard * params
    )
    return (
        pair_final.astype(jnp.bfloat16)[None],
        single_final.astype(jnp.bfloat16)[None],
        grad_pair[None],
        grad_single[None],
        new_params,
        new_first,
        new_second,
        clip_norm,
    )


F32 = jnp.float32
BF16 = jnp.bfloat16
LOG2E = 1.4426950408889634
VMEM_LIMIT = 56 * 1024 * 1024


def mm(left, right):
    return lax.dot_general(left, right, (((1,), (0,)), ((), ())), preferred_element_type=F32)


def mm_nt(left, right):
    return lax.dot_general(left, right, (((1,), (1,)), ((), ())), preferred_element_type=F32)


def mm_tn(left, right):
    return lax.dot_general(left, right, (((0,), (0,)), ((), ())), preferred_element_type=F32)


def standardize(values):
    centred = values - jnp.mean(values, axis=0, keepdims=True)
    spread = jnp.mean(centred * centred, axis=0, keepdims=True)
    inverse = lax.rsqrt(spread + EPSILON)
    return centred * inverse, inverse


def standardize_back(unit, inverse, grad_unit):
    first = jnp.mean(grad_unit, axis=0, keepdims=True)
    second = jnp.mean(grad_unit * unit, axis=0, keepdims=True)
    return inverse * (grad_unit - first - unit * second)


def sigmoid(values):
    return 0.5 * jnp.tanh(0.5 * values) + 0.5


def column(ref, index):
    return ref[:, index : index + 1]


def live_pair(info, alive, row):
    return jnp.concatenate(
        [jnp.where(info[row + place] > 0, alive[0:1], 0.0) for place in range(GROUP)], axis=1
    )


GROUP = 8
LAG = 4


def each_group(count, body):
    def step(index, carry):
        body(index * GROUP)
        return carry

    lax.fori_loop(0, count // GROUP, step, 0, unroll=2)


def each_channel(count, body):
    def step(index, carry):
        body(index)
        return carry

    lax.fori_loop(0, count, step, 0)


def join(read, ref, row):
    return jnp.concatenate([read(ref, row + place) for place in range(GROUP)], axis=1)


def pieces_of(values):
    length = values.shape[1] // GROUP
    return [values[:, place * length : (place + 1) * length] for place in range(GROUP)]


def put_rows(ref, row, values):
    for place, part in enumerate(pieces_of(values)):
        ref[row + place] = part.astype(ref.dtype)


def put_inner(scratch, row, values):
    for place, part in enumerate(pieces_of(values)):
        scratch[:, row + place, :] = part


def read_inner(scratch, row):
    return scratch[:, row, :]


def put_turned(scratch, row, values):
    for place, part in enumerate(pieces_of(values)):
        scratch[:, row + place, :] = part.T


def add_lanes(ref, values):
    ref[...] += sum(pieces_of(values))


def spec_full(shape):
    return pl.BlockSpec(shape, lambda step: (0,) * len(shape))


def cost(microseconds):
    return pl.CostEstimate(
        flops=int(microseconds * 1e9), bytes_accessed=int(microseconds * 3e6), transcendentals=0
    )


class Both(list):
    pass


def all_rows(ins, outs):
    extents = [shape[axis] for shape, dtype, axis in outs if axis is not None]
    for array, axis in ins:
        if isinstance(axis, int):
            extents += [member.shape[axis] for member in (array if isinstance(array, list) else [array])]
    return max(extents)


def run_rows(kernel, name, steps, ins, outs, scratch, time=15, half=None, before=None):
    grid = steps if half is None else steps // 2
    offset = grid * (half or 0)
    flat = []
    groups = []
    for array, axis in ins:
        members = array if isinstance(array, Both) else [array]
        flat += [(member, axis) for member in members]
        groups.append((len(members), isinstance(array, Both)))
    full = all_rows(flat, outs)

    def spec(shape, axis):
        if axis is None:
            return spec_full(shape)
        size = full // steps
        first = offset if shape[axis] == full else 0
        sizes = tuple(size if place == axis else extent for place, extent in enumerate(shape))
        return pl.BlockSpec(
            sizes,
            lambda step: tuple(step + first if place == axis else 0 for place in range(len(shape))),
        )

    in_specs = [
        pl.BlockSpec(memory_space=pltpu.SMEM) if axis == "smem" else spec(array.shape, axis)
        for array, axis in flat
    ]
    out_specs = [spec(shape, axis) for shape, dtype, axis in outs]
    arrays = [array for array, axis in flat]
    aliases = {}
    kept = []
    for place, (shape, dtype, axis) in enumerate(outs):
        if before is not None and (axis is None or shape[axis] == full):
            aliases[len(arrays)] = place
            kept.append(place)
            arrays.append(before[place])
            in_specs.append(spec_full(shape) if axis is None else pl.BlockSpec(memory_space=pl.ANY))

    def run(*refs):
        taken = iter(refs)
        given = []
        for number, together in groups:
            members = [next(taken) for _ in range(number)]
            given.append(members if together else members[0])
        held = {place: next(taken) for place in kept}
        results = [next(taken) for _ in outs]

        @pl.when(pl.program_id(0) == 0)
        def _():
            for place, (shape, dtype, axis) in enumerate(outs):
                if axis is None:
                    results[place][...] = (
                        held[place][...] if place in held else jnp.zeros(shape, dtype)
                    )

        kernel(*given, *results, *taken)

    return pl.pallas_call(
        run,
        grid=(grid,),
        in_specs=in_specs,
        out_specs=out_specs,
        out_shape=[jax.ShapeDtypeStruct(shape, dtype) for shape, dtype, axis in outs],
        scratch_shapes=[pltpu.VMEM(shape, dtype) for shape, dtype in scratch],
        input_output_aliases=aliases,
        compiler_params=pltpu.CompilerParams(vmem_limit_bytes=VMEM_LIMIT),
        cost_estimate=cost(time if half is None else time / 2),
        name=name,
    )(*arrays)


def run_halves(kernel, name, steps, ins, outs, scratch, time=15):
    results = []
    for half in range(2):
        chosen = [
            (array[half] if type(array) is list else array, axis) for array, axis in ins
        ]
        before = results[0] if half else None
        results.append(run_rows(kernel, name, steps, chosen, outs, scratch, time, half, before))
    full = all_rows(ins, outs)
    return [
        [results[0][place], results[1][place]]
        if axis is not None and shape[axis] != full
        else results[1][place]
        for place, (shape, dtype, axis) in enumerate(outs)
    ]


def zero_first(*refs):
    @pl.when(pl.program_id(0) == 0)
    def _():
        for ref in refs:
            ref[...] = jnp.zeros(ref.shape, ref.dtype)


def lane_sums(ref):
    return jnp.sum(ref[...].T, axis=0, keepdims=True)


def on_last(body):
    @pl.when(pl.program_id(0) == pl.num_programs(0) - 1)
    def _():
        body()


def read_plain(ref, row):
    return ref[row].astype(F32)


def reorder(values, order):
    size = values.shape[0] // len(order)
    return jnp.concatenate([values[place * size : (place + 1) * size] for place in order], axis=0)


def read_tokens(order, ref, row):
    return reorder(ref[row].astype(F32), order).T


def read_flipped(refs, row):
    parts = jnp.concatenate([ref[:, row] for ref in refs], axis=1)
    return parts.reshape(-1, parts.shape[-1]).astype(F32).T


def read_turned(order, ref, row):
    parts = ref[:, row]
    return reorder(parts.reshape(-1, parts.shape[-1]).astype(F32), order).T


def tri_pre_row(info, alive, row, state, cols, first, proj_t):
    unit, inverse = standardize(state)
    lowered = (unit * column(cols, first) + column(cols, first + 1)).astype(BF16)
    project = mm(proj_t[...], lowered)
    half = project.shape[0] // 2
    return project[:half] * sigmoid(project[half:]) * live_pair(info, alive, row)


def store_product(out, scratch, devices):
    hidden = scratch.shape[0] // 2
    part = hidden // devices

    def one(device, carry):
        out[device, 0] = scratch[pl.ds(device * part, part)].astype(BF16)
        out[device, 1] = scratch[pl.ds(hidden + device * part, part)].astype(BF16)
        return carry

    lax.fori_loop(0, devices, one, 0)


def copy_blocks(target, source, count):
    def one(index, carry):
        target[index] = source[index].astype(target.dtype)
        return carry

    lax.fori_loop(0, count, one, 0)


def store_flipped(out, scratch):
    devices, part = out.shape[0], out.shape[1]

    def one(device, carry):
        out[device] = scratch[pl.ds(device * part, part)].astype(out.dtype)
        return carry

    lax.fori_loop(0, devices, one, 0)


def tri_post_row(state, tri, cols, proj_t, gate_t):
    unit, inverse = standardize(state)
    lowered = (unit * column(cols, 0) + column(cols, 1)).astype(BF16)
    tri_unit, tri_inverse = standardize(tri)
    out_low = (tri_unit * column(cols, 2) + column(cols, 3)).astype(BF16)
    output = mm(proj_t[...], out_low)
    gate = sigmoid(mm(gate_t[...], lowered))
    return unit, inverse, lowered, tri_unit, tri_inverse, out_low, output, gate


def row_base(rows):
    return pl.program_id(0) * rows


def tri_pre_first_kernel(devices, read, info, alive, pair, cols, proj_t, out, scratch):
    rows = pair.shape[0]

    def body(row):
        product = tri_pre_row(
            info, alive, row_base(rows) + row, join(read, pair, row), cols, 0, proj_t
        )
        put_inner(scratch, row, product)

    each_group(rows, body)
    store_product(out, scratch, devices)


def whole_rows(refs, *place):
    parts = jnp.concatenate([ref[(slice(None),) + place] for ref in refs], axis=1)
    return parts.reshape(-1, parts.shape[-1])


def split_rows(values, outs, *place):
    part = outs[0].shape[-2]
    parts = values.astype(BF16).reshape(outs[0].shape[0], -1, values.shape[-1])
    for half, out in enumerate(outs):
        out[(slice(None),) + place] = parts[:, half * part : (half + 1) * part]


def tri_product_kernel(incoming, operands, *outs):
    def body(channel):
        first = whole_rows(operands, 0, channel)
        second = whole_rows(operands, 1, channel)
        tri = mm_tn(first, second) if incoming else mm_nt(first, second)
        split_rows(tri, outs, channel)

    each_channel(operands[0].shape[2], body)


def tri_join_kernel(
    devices, read, info, alive, source, tri_in, cols, proj_t, gate_t, next_cols, next_proj_t,
    state_out, out, tri_scratch, scratch,
):
    rows = state_out.shape[0]
    copy_blocks(tri_scratch, tri_in, tri_in.shape[0])

    def body(row):
        state = join(read, source, row)
        pieces = tri_post_row(state, join(read_inner, tri_scratch, row), cols, proj_t, gate_t)
        state = state + pieces[6] * pieces[7]
        put_rows(state_out, row, state)
        product = tri_pre_row(
            info, alive, row_base(rows) + row, state, next_cols, 0, next_proj_t
        )
        put_inner(scratch, row, product)

    each_group(rows, body)
    store_product(out, scratch, devices)


def tri_last_kernel(
    source, tri_in, cols, proj_t, gate_t, next_cols, bias_t, state_out, bias_out, tri_scratch, scratch
):
    rows = state_out.shape[0]
    copy_blocks(tri_scratch, tri_in, tri_in.shape[0])

    def body(row):
        state = join(read_plain, source, row)
        pieces = tri_post_row(state, join(read_inner, tri_scratch, row), cols, proj_t, gate_t)
        state = state + pieces[6] * pieces[7]
        put_rows(state_out, row, state)
        unit, inverse = standardize(state)
        lowered = (unit * column(next_cols, 0) + column(next_cols, 1)).astype(BF16)
        put_inner(scratch, row, mm(bias_t[...], lowered))

    each_group(rows, body)
    bias_out[...] = scratch[: bias_out.shape[0]].astype(BF16)


def fill_bias(alive, bias_in, table, turned):
    @pl.when(pl.program_id(0) == 0)
    def _():
        length = table.shape[1]
        penalty = (alive[...] - 1.0) * (MASKED * LOG2E)
        for head in range(table.shape[0]):
            values = bias_in[:, head].reshape(length, length).astype(F32) * LOG2E
            if turned:
                table[head] = values + penalty.T[:, 0:1]
            else:
                table[head] = (values + penalty[0:1]).T


def attention_row(state, cols, proj_t):
    unit, inverse = standardize(state)
    lowered = (unit * column(cols, 0) + column(cols, 1)).astype(BF16)
    project = mm(proj_t[...], lowered)
    width = project.shape[0] // 4
    size = width // TA_HEADS
    query = (project[:width] * (size**-0.5 * LOG2E)).astype(BF16)
    key = project[width : 2 * width].astype(BF16)
    value = project[2 * width : 3 * width].astype(BF16)
    gate = sigmoid(project[3 * width :])
    return unit, inverse, lowered, query, key, value, gate


def in_stages(blocks, first, second, third):
    early, late, done = {}, {}, {}
    count = len(blocks)
    for step in range(count + 2 * LAG):
        if step < count:
            early[step] = first(*blocks[step])
        if 0 <= step - LAG < count:
            late[step - LAG] = second(*blocks[step - LAG], early.pop(step - LAG))
        if 0 <= step - 2 * LAG < count:
            place = step - 2 * LAG
            done[blocks[place]] = third(*blocks[place], late.pop(place))
    return done


def head_rows(values, place, head):
    size, length = values.shape[0] // TA_HEADS, values.shape[1] // GROUP
    return values[head * size : (head + 1) * size, place * length : (place + 1) * length]


def gather_heads(done):
    return jnp.concatenate(
        [
            jnp.concatenate([done[place, head] for head in range(TA_HEADS)], axis=0)
            for place in range(GROUP)
        ],
        axis=1,
    )


ROW_BLOCKS = [(place, head) for place in range(GROUP) for head in range(TA_HEADS)]
HEAD_BLOCKS = [(place, head) for head in range(TA_HEADS) for place in range(GROUP)]


def attend_rows(state, row, cols, proj_t, output_t, table, totals, mixed_out):
    unit, inverse, lowered, query, key, value, gate = attention_row(state, cols, proj_t)

    def score(place, head):
        return mm_tn(head_rows(key, place, head), head_rows(query, place, head)) + table[head]

    def shift(place, head, scores):
        top = jnp.max(scores, axis=0, keepdims=True)
        return top, jnp.exp2(scores - top).astype(BF16)

    def mix(place, head, items):
        top, shifted = items
        values = head_rows(value, place, head)
        size = values.shape[0]
        values = jnp.concatenate([values, jnp.ones((16, values.shape[1]), BF16)], axis=0)
        result = mm(values, shifted)
        total = result[size : size + 1]
        return result[:size] / total, top + jnp.log2(total)

    done = in_stages(ROW_BLOCKS, score, shift, mix)
    mixed = gather_heads({block: items[0] for block, items in done.items()})
    put_rows(totals, row, gather_heads({block: items[1] for block, items in done.items()}))
    put_rows(mixed_out, row, mixed)
    return state + mm(output_t[...], (mixed * gate).astype(BF16))


def starting_kernel(
    alive, source, bias_in, cols, proj_t, output_t, next_cols, bias_t, out, totals, mixed, bias_out,
    table, scratch, bias_scratch,
):
    fill_bias(alive, bias_in, table, False)
    rows = source.shape[0]

    def body(row):
        state = attend_rows(
            join(read_plain, source, row), row, cols, proj_t, output_t, table, totals, mixed
        )
        put_turned(scratch, row, state)
        unit, inverse = standardize(state)
        lowered = (unit * column(next_cols, 0) + column(next_cols, 1)).astype(BF16)
        put_inner(bias_scratch, row, mm(bias_t[...], lowered))

    each_group(rows, body)
    store_flipped(out, scratch)
    bias_out[...] = bias_scratch[: bias_out.shape[0]].astype(BF16)


def ending_kernel(alive, source, bias_in, cols, proj_t, output_t, out, totals, mixed, table):
    fill_bias(alive, bias_in, table, True)
    rows = source[0].shape[1]

    def body(row):
        state = attend_rows(
            join(read_flipped, source, row), row, cols, proj_t, output_t, table, totals, mixed
        )
        put_rows(out, row, state)

    each_group(rows, body)


def transition_kernel(
    order, source, cols, up_t, down_t, next_cols, bias_t, state_out, pair_out, bias_out, scratch, bias_scratch
):
    rows = source.shape[0]

    def body(row):
        state = join(read_plain, source, row)
        unit, inverse = standardize(state)
        lowered = (unit * column(cols, 0) + column(cols, 1)).astype(BF16)
        hidden = mm(up_t[...], lowered)
        half = hidden.shape[0] // 2
        first = hidden[:half]
        mixed = (first * sigmoid(first) * hidden[half:]).astype(BF16)
        state = state + mm(down_t[...], mixed)
        put_rows(state_out, row, state)
        put_turned(scratch, row, state)
        unit, inverse = standardize(state)
        lowered = (unit * column(next_cols, 0) + column(next_cols, 1)).astype(BF16)
        put_inner(bias_scratch, row, mm(bias_t[...], lowered))

    each_group(rows, body)
    size = pair_out.shape[0] // len(order)
    for place, held in enumerate(order):
        pair_out[place * size : (place + 1) * size] = scratch[held * size : (held + 1) * size].astype(BF16)
    bias_to_lanes(bias_out, bias_scratch)


def transition_back_kernel(
    read, mid, final, cotangent, bias_grad, cols, up_t, up, down, next_cols, bias_w,
    grad_out, up_grad, down_grad, bias_w_grad, vecs, norm_gain, norm_bias, pair_gain, pair_bias, bias_scratch,
):
    zero_first(norm_gain, norm_bias, pair_gain, pair_bias)
    rows = mid.shape[0]
    lanes_to_bias(bias_scratch, bias_grad)

    def body(row):
        grad = join(read, cotangent, row)
        unit, inverse = standardize(join(read_plain, final, row))
        gain = column(next_cols, 0)
        lowered = (unit * gain + column(next_cols, 1)).astype(BF16)
        grad_bias = join(read_inner, bias_scratch, row).astype(BF16)
        bias_w_grad[...] += mm_nt(lowered, grad_bias)
        grad_lowered = mm(bias_w[...], grad_bias)
        add_lanes(pair_gain, grad_lowered * unit)
        add_lanes(pair_bias, grad_lowered)
        grad = grad + standardize_back(unit, inverse, grad_lowered * gain)
        unit, inverse = standardize(join(read_plain, mid, row))
        gain = column(cols, 0)
        lowered = (unit * gain + column(cols, 1)).astype(BF16)
        hidden = mm(up_t[...], lowered)
        half = hidden.shape[0] // 2
        first, second = hidden[:half], hidden[half:]
        slope = sigmoid(first)
        silu = first * slope
        grad_low = grad.astype(BF16)
        grad_mixed = mm(down[...], grad_low)
        down_grad[...] += mm_nt((silu * second).astype(BF16), grad_low)
        grad_hidden = jnp.concatenate(
            [
                (grad_mixed * second * (slope + silu * (1.0 - slope))).astype(BF16),
                (grad_mixed * silu).astype(BF16),
            ],
            axis=0,
        )
        up_grad[...] += mm_nt(lowered, grad_hidden)
        grad_lowered = mm(up[...], grad_hidden)
        add_lanes(norm_gain, grad_lowered * unit)
        add_lanes(norm_bias, grad_lowered)
        put_rows(grad_out, row, grad + standardize_back(unit, inverse, grad_lowered * gain))

    each_group(rows, body)

    def finish():
        vecs[0:1] += lane_sums(norm_gain)
        vecs[1:2] += lane_sums(norm_bias)
        vecs[2:3] += lane_sums(pair_gain)
        vecs[3:4] += lane_sums(pair_bias)

    on_last(finish)


def attention_back_kernel(
    turned, read, read_grad, alive, source, grad_in, bias_in, totals, mixed_in, cols, proj_t, proj, output,
    grad_out, bias_out, proj_grad, output_grad, table, grad_table,
):
    fill_bias(alive, bias_in, table, turned)
    zero_first(grad_table)
    rows = grad_out.shape[0]

    def body(row):
        unit, inverse, lowered, query, key, value, gate = attention_row(
            join(read, source, row), cols, proj_t
        )
        mixed = join(read_plain, mixed_in, row)
        total = join(read_plain, totals, row)
        grad_low = join(read_grad, grad_in, row).astype(BF16)
        gated = mixed * gate
        output_grad[...] += mm_nt(gated.astype(BF16), grad_low)
        grad_gated = mm(output[...], grad_low)
        grad_gate = grad_gated * gated * (1.0 - gate)
        grad_mixed = (grad_gated * gate).astype(BF16)
        product = grad_mixed.astype(F32) * mixed
        size = query.shape[0] // TA_HEADS

        def score(place, head):
            scores = mm_tn(head_rows(key, place, head), head_rows(query, place, head))
            grads = mm_tn(head_rows(value, place, head), head_rows(grad_mixed, place, head))
            return scores + table[head], grads

        def slope(place, head, items):
            scores, grads = items
            probs = jnp.exp2(scores - head_rows(total, place, head))
            delta = jnp.sum(head_rows(product, place, head), axis=0, keepdims=True)
            grad_scores = probs * (grads - delta)
            grad_table[head] += grad_scores
            return probs.astype(BF16), grad_scores.astype(BF16)

        def back(place, head, items):
            probs, grad_scores = items
            return (
                mm(head_rows(key, place, head), grad_scores) * size**-0.5,
                mm_nt(head_rows(query, place, head), grad_scores) * (1.0 / LOG2E),
                mm_nt(head_rows(grad_mixed, place, head), probs),
            )

        done = in_stages(HEAD_BLOCKS, score, slope, back)
        grad_project = jnp.concatenate(
            [
                gather_heads({block: items[part] for block, items in done.items()})
                for part in range(3)
            ]
            + [grad_gate],
            axis=0,
        ).astype(BF16)
        proj_grad[...] += mm_nt(lowered, grad_project)
        put_rows(grad_out, row, mm(proj[...], grad_project))

    each_group(rows, body)

    def finish():
        for head in range(TA_HEADS):
            bias_out[:, head] = (
                grad_table[head].T.astype(BF16).reshape(bias_out.shape[0], bias_out.shape[2], -1)
            )

    on_last(finish)


def attention_end_row(
    state, grad, grad_lowered, grad_bias, cols, bias_w, bias_w_grad, norm_gain, norm_bias
):
    unit, inverse = standardize(state)
    gain = column(cols, 0)
    lowered = (unit * gain + column(cols, 1)).astype(BF16)
    bias_w_grad[...] += mm_nt(lowered, grad_bias)
    grad_lowered = grad_lowered + mm(bias_w[...], grad_bias)
    add_lanes(norm_gain, grad_lowered * unit)
    add_lanes(norm_bias, grad_lowered)
    return grad + standardize_back(unit, inverse, grad_lowered * gain)


def fill_bias_grad(scratch, bias_grad):
    heads = bias_grad.shape[1]
    total = bias_grad[0].astype(F32)
    for device in range(1, bias_grad.shape[0]):
        total = total + bias_grad[device].astype(F32)
    scratch[:heads] = total
    scratch[heads:] = jnp.zeros((scratch.shape[0] - heads,) + scratch.shape[1:], F32)


def ending_end_kernel(
    source, grad_in, grad_lowered, bias_grad, cols, bias_w,
    grad_out, bias_w_grad, vecs, norm_gain, norm_bias, bias_scratch, scratch,
):
    zero_first(norm_gain, norm_bias)
    fill_bias_grad(bias_scratch, bias_grad)
    rows = grad_in.shape[0]

    def body(row):
        grad = attention_end_row(
            join(read_flipped, source, row), join(read_plain, grad_in, row),
            join(read_plain, grad_lowered, row), join(read_inner, bias_scratch, row).astype(BF16), cols, bias_w, bias_w_grad, norm_gain, norm_bias,
        )
        put_turned(scratch, row, grad)

    each_group(rows, body)
    store_flipped(grad_out, scratch)

    def finish():
        vecs[0:1] += lane_sums(norm_gain)
        vecs[1:2] += lane_sums(norm_bias)

    on_last(finish)


def tri_post_back_row(
    state, tri, grad, cols, proj_t, gate_t, proj, gate_w, proj_grad, gate_grad, out_gain, out_bias
):
    unit, inverse, lowered, tri_unit, tri_inverse, out_low, output, gate = tri_post_row(
        state, tri, cols, proj_t, gate_t
    )
    grad_output = grad * gate
    grad_gate = (grad_output * output * (1.0 - gate)).astype(BF16)
    grad_output = grad_output.astype(BF16)
    proj_grad[...] += mm_nt(out_low, grad_output)
    gate_grad[...] += mm_nt(lowered, grad_gate)
    grad_normed = mm(proj[...], grad_output)
    add_lanes(out_gain, grad_normed * tri_unit)
    add_lanes(out_bias, grad_normed)
    grad_tri = standardize_back(tri_unit, tri_inverse, grad_normed * column(cols, 2))
    return grad_tri, mm(gate_w[...], grad_gate)


def starting_end_kernel(
    source, grad_in, grad_lowered, bias_grad, cols, bias_w,
    below, tri_in, tri_cols, proj_t, gate_t, proj, gate_w,
    grad_out, tri_out, gate_back, bias_w_grad, proj_grad, gate_grad, vecs,
    norm_gain, norm_bias, out_gain, out_bias, bias_scratch, tri_scratch,
):
    zero_first(norm_gain, norm_bias, out_gain, out_bias)
    fill_bias_grad(bias_scratch, bias_grad)
    copy_blocks(tri_scratch, tri_in, tri_in.shape[0])
    rows = source.shape[0]

    def body(row):
        grad = attention_end_row(
            join(read_plain, source, row), join(read_flipped, grad_in, row),
            join(read_plain, grad_lowered, row), join(read_inner, bias_scratch, row).astype(BF16), cols, bias_w, bias_w_grad, norm_gain, norm_bias,
        )
        put_rows(grad_out, row, grad)
        grad_tri, back = tri_post_back_row(
            join(read_plain, below, row), join(read_inner, tri_scratch, row), grad, tri_cols, proj_t, gate_t, proj, gate_w,
            proj_grad, gate_grad, out_gain, out_bias,
        )
        put_rows(gate_back, row, back)
        put_inner(tri_scratch, row, grad_tri)

    each_group(rows, body)
    copy_blocks(tri_out, tri_scratch, tri_out.shape[0])

    def finish():
        vecs[0:1] += lane_sums(norm_gain)
        vecs[1:2] += lane_sums(norm_bias)
        vecs[2:3] += lane_sums(out_gain)
        vecs[3:4] += lane_sums(out_bias)

    on_last(finish)


def tri_product_back_kernel(incoming, grad, operands, *outs):
    def body(channel):
        first = whole_rows(operands, 0, channel)
        second = whole_rows(operands, 1, channel)
        tri = whole_rows(grad, channel)
        if incoming:
            grad_first = mm_nt(second, tri)
            grad_second = mm(first, tri)
        else:
            grad_first = mm(tri, second)
            grad_second = mm_tn(tri, first)
        split_rows(grad_first, outs, 0, channel)
        split_rows(grad_second, outs, 1, channel)

    each_channel(operands[0].shape[2], body)


def tri_pre_back_row(
    info, alive, row, state, product_grad, gate_back, grad, cols, proj_t, proj, proj_grad, norm_gain, norm_bias
):
    unit, inverse = standardize(state)
    gain = column(cols, 0)
    lowered = (unit * gain + column(cols, 1)).astype(BF16)
    project = mm(proj_t[...], lowered)
    half = project.shape[0] // 2
    gate = sigmoid(project[half:])
    grad_first = product_grad * gate * live_pair(info, alive, row)
    grad_second = grad_first * project[:half] * (1.0 - gate)
    grad_project = jnp.concatenate([grad_first.astype(BF16), grad_second.astype(BF16)], axis=0)
    proj_grad[...] += mm_nt(lowered, grad_project)
    grad_lowered = mm(proj[...], grad_project) + gate_back
    add_lanes(norm_gain, grad_lowered * unit)
    add_lanes(norm_bias, grad_lowered)
    return grad + standardize_back(unit, inverse, grad_lowered * gain)


def fill_product_grad(scratch, product_grad):
    devices, part = product_grad.shape[0], product_grad.shape[2]

    def one(device, carry):
        scratch[pl.ds(device * part, part)] = product_grad[device, 0].astype(F32)
        scratch[pl.ds((devices + device) * part, part)] = product_grad[device, 1].astype(F32)
        return carry

    lax.fori_loop(0, devices, one, 0)


def tri_join_back_kernel(
    read, info, alive, source, product_grad, gate_in, grad_in, cols, proj_t, proj,
    below, tri_in, tri_cols, out_t, gate_t, out_w, gate_w,
    grad_out, tri_out, gate_back, proj_grad, out_grad, gate_grad, vecs,
    norm_gain, norm_bias, out_gain, out_bias, scratch, tri_scratch,
):
    zero_first(norm_gain, norm_bias, out_gain, out_bias)
    fill_product_grad(scratch, product_grad)
    copy_blocks(tri_scratch, tri_in, tri_in.shape[0])
    rows = source.shape[0]

    def body(row):
        grad = tri_pre_back_row(
            info, alive, row_base(rows) + row, join(read_plain, source, row),
            join(read_inner, scratch, row), join(read_plain, gate_in, row),
            join(read_plain, grad_in, row), cols, proj_t, proj, proj_grad, norm_gain, norm_bias,
        )
        put_rows(grad_out, row, grad)
        grad_tri, back = tri_post_back_row(
            join(read, below, row), join(read_inner, tri_scratch, row), grad, tri_cols, out_t, gate_t, out_w, gate_w,
            out_grad, gate_grad, out_gain, out_bias,
        )
        put_rows(gate_back, row, back)
        put_inner(tri_scratch, row, grad_tri)

    each_group(rows, body)
    copy_blocks(tri_out, tri_scratch, tri_out.shape[0])

    def finish():
        vecs[0:1] += lane_sums(norm_gain)
        vecs[1:2] += lane_sums(norm_bias)
        vecs[2:3] += lane_sums(out_gain)
        vecs[3:4] += lane_sums(out_bias)

    on_last(finish)


def tri_first_back_kernel(
    read, order, info, alive, source, product_grad, gate_in, grad_in, cols, proj_t, proj,
    grad_out, proj_grad, vecs, norm_gain, norm_bias, scratch,
):
    zero_first(norm_gain, norm_bias)
    fill_product_grad(scratch, product_grad)
    rows = source.shape[0]

    def body(row):
        grad = tri_pre_back_row(
            info, alive, row_base(rows) + row, join(read, source, row),
            join(read_inner, scratch, row), join(read_plain, gate_in, row),
            join(read_plain, grad_in, row), cols, proj_t, proj, proj_grad, norm_gain, norm_bias,
        )
        for place, part in enumerate(pieces_of(grad)):
            grad_out[row + place] = reorder(part.T, order).astype(grad_out.dtype)

    each_group(rows, body)

    def finish():
        vecs[0:1] += lane_sums(norm_gain)
        vecs[1:2] += lane_sums(norm_bias)

    on_last(finish)


RUN = 24


def table_of(entries):
    table = {}
    offset = 0
    for name, shape in entries:
        table[name] = (offset // STRIDE, shape)
        offset += math.prod(shape)
    return table, offset


def runs_kernel(info, shard, out, scratch):
    def one(block, carry):
        scratch[:, block, :] = shard[pl.ds(block * STRIDE, STRIDE), :].T
        return carry

    lax.fori_loop(0, RUN, one, 0)
    half = STRIDE // 2
    turn = info[0] * half

    def move(lane, carry):
        out[lane] = scratch[lax.rem(lane + turn, STRIDE)].astype(BF16)
        return carry

    lax.fori_loop(0, STRIDE, move, 0)


def run_place(shards, total, lane, shard):
    count = total // STRIDE
    whole = total // shards
    step, odd = whole // STRIDE, (whole % STRIDE) // (STRIDE // 2)
    extra = lax.div(shard * odd + jnp.where(lane < STRIDE // 2, 1, 0), 2)
    start = lane * count + shard * step + extra
    return lax.div(start, STRIDE), lax.rem(start, STRIDE)


def rows_from_runs(runs, rows, first_lane, total):
    shards, lanes = runs.shape[0], runs.shape[1]
    base = first_lane * (total // STRIDE) // STRIDE

    def one(index, carry):
        lane, shard = lax.div(index, shards), lax.rem(index, shards)
        row, shift = run_place(shards, total, first_lane + lane, shard)
        row = row - base
        turned = pltpu.roll(runs[shard, lane].astype(F32), shift, 1)
        place = lax.broadcasted_iota(jnp.int32, (RUN + 1, STRIDE), 1)
        last, before = carry
        joint = jnp.where(row - before == RUN, last[2:3], last[1:2])
        below = jnp.concatenate([joint, turned], axis=0)
        above = jnp.concatenate([turned, turned[RUN - 1 :]], axis=0)
        values = jnp.where(place < shift, below, above)
        rows[pl.ds(row, RUN + 1), :] = values
        return values[RUN - 2 :], row

    lax.fori_loop(0, shards * lanes, one, (jnp.zeros((3, STRIDE), F32), -RUN), unroll=4)


def runs_from_rows(rows, out, first_lane, base, total):
    shards, lanes = out.shape[0], out.shape[1]

    def one(index, carry):
        lane, shard = lax.div(index, shards), lax.rem(index, shards)
        row, shift = run_place(shards, total, first_lane + lane, shard)
        turned = pltpu.roll(rows[pl.ds(row - base, RUN + 1), :], (STRIDE - shift) % STRIDE, 1)
        place = lax.broadcasted_iota(jnp.int32, (RUN, STRIDE), 1)
        out[shard, lane] = jnp.where(
            place < STRIDE - shift, turned[:RUN], turned[1:]
        ).astype(BF16)
        return carry

    lax.fori_loop(0, shards * lanes, one, 0, unroll=16 if shards * lanes % 16 == 0 else 8)


def row_height(base, first_lane, last_lane, total):
    end = (last_lane * (total // STRIDE)) // STRIDE + RUN + 2
    return -(-(end - base) // 8) * 8


def take_matrix(rows, first, shape):
    blocks = shape[1] // STRIDE
    return [
        rows[pl.ds(first + block, shape[0], stride=blocks), :]
        if blocks > 1
        else rows[first : first + shape[0], :]
        for block in range(blocks)
    ]


def put_matrix(rows, first, matrix):
    height, width = matrix.shape
    blocks = width // STRIDE
    for block in range(blocks):
        part = matrix[:, block * STRIDE : (block + 1) * STRIDE]
        if blocks > 1:
            rows[pl.ds(first + block, height, stride=blocks), :] = part
        else:
            rows[first : first + height, :] = part


def spread(index, heads, rows):
    lane = lax.broadcasted_iota(jnp.int32, (STRIDE, STRIDE), 0)
    channel = lax.broadcasted_iota(jnp.int32, (STRIDE, STRIDE), 1)
    return (channel == index * (STRIDE // heads) + lane // heads).astype(BF16)


def take_narrow(rows, first, heads, high):
    total = jnp.zeros((high, STRIDE), F32)
    head = lax.broadcasted_iota(jnp.int32, (high, STRIDE), 0)
    lane = lax.broadcasted_iota(jnp.int32, (high, STRIDE), 1)
    for index in range(heads):
        line = rows[first + index : first + index + 1, :]
        picked = jnp.where(lane % heads == head, line, 0.0).astype(BF16)
        total = total + mm(picked, spread(index, heads, rows))
    return total


def put_narrow(rows, first, heads, matrix):
    turned = matrix.T.astype(BF16)
    high = turned.shape[0]
    head = lax.broadcasted_iota(jnp.int32, (high, STRIDE), 0)
    lane = lax.broadcasted_iota(jnp.int32, (high, STRIDE), 1)
    for index in range(heads):
        wide = mm_nt(turned, spread(index, heads, rows))
        rows[first + index : first + index + 1, :] = jnp.sum(
            jnp.where(lane % heads == head, wide, 0.0), axis=0, keepdims=True
        )


PAIR_MATRICES = (
    (OUTGOING, PROJ_GATE), (OUTGOING, PROJ_OUT), (OUTGOING, GATE_OUT),
    (INCOMING, PROJ_GATE), (INCOMING, PROJ_OUT), (INCOMING, GATE_OUT),
    (STARTING, QKVG), (STARTING, OUTPUT), (ENDING, QKVG), (ENDING, OUTPUT), (PAIR, UP), (PAIR, DOWN),
)
PAIR_COLUMNS = (
    (OUTGOING, ((OUTGOING, NORM_GAIN), (OUTGOING, NORM_BIAS), (OUTGOING, OUT_GAIN), (OUTGOING, OUT_BIAS))),
    (INCOMING, ((INCOMING, NORM_GAIN), (INCOMING, NORM_BIAS), (INCOMING, OUT_GAIN), (INCOMING, OUT_BIAS))),
    (STARTING, ((STARTING, NORM_GAIN), (STARTING, NORM_BIAS))),
    (ENDING, ((ENDING, NORM_GAIN), (ENDING, NORM_BIAS))),
    (PAIR, ((PAIR, NORM_GAIN), (PAIR, NORM_BIAS))),
)
SINGLE_MATRICES = ((ATTEND, QKVG), (ATTEND, OUTPUT), (SINGLE, UP), (SINGLE, DOWN))
SINGLE_VECTORS = ((ATTEND, NORM_GAIN), (ATTEND, NORM_BIAS), (SINGLE, NORM_GAIN), (SINGLE, NORM_BIAS))


def put_columns(rows, out, table, base, names):
    out[...] = jnp.zeros(out.shape, F32)
    lines = [rows[table[name][0] - base : table[name][0] - base + 1, :] for name in names]
    lines.append(jnp.zeros((8 - len(lines), STRIDE), F32))
    out[...] = jnp.concatenate(lines, axis=0).T


def unpack_pair_kernel(table, total, runs, *refs):
    rows = refs[-1]
    outs = list(refs[:-1])
    rows_from_runs(runs, rows, 0, total)
    for name in PAIR_MATRICES:
        first, shape = table[name]
        plain, turned = outs.pop(0), outs.pop(0)
        for block, part in enumerate(take_matrix(rows, first, shape)):
            place = slice(block * STRIDE, (block + 1) * STRIDE)
            plain[:, place] = part.astype(BF16)
            turned[place, :] = part.T.astype(BF16)
    for prefix in (STARTING, ENDING):
        plain, turned = outs.pop(0), outs.pop(0)
        first, shape = table[(prefix, BIAS_PROJ)]
        matrix = take_narrow(rows, first, shape[1], 8)
        turned[...] = matrix.astype(BF16)
        plain[...] = matrix.T.astype(BF16)
    for prefix, names in PAIR_COLUMNS:
        put_columns(rows, outs.pop(0), table, 0, names)


def unpack_single_kernel(table, total, first_lane, runs, *refs):
    rows = refs[-1]
    outs = list(refs[:-1])
    rows_from_runs(runs, rows, first_lane, total)
    base = first_lane * (total // STRIDE) // STRIDE
    for name in SINGLE_MATRICES:
        first, shape = table[name]
        out = outs.pop(0)
        for block, part in enumerate(take_matrix(rows, first - base, shape)):
            out[:, block * STRIDE : (block + 1) * STRIDE] = part.astype(BF16)
    first, shape = table[(ATTEND, PAIR_PROJ)]
    matrix = take_narrow(rows, first - base, shape[1], shape[1])
    plain, turned = outs.pop(0), outs.pop(0)
    turned[...] = matrix.astype(BF16)
    plain[...] = matrix.T.astype(BF16)
    put_columns(rows, outs.pop(0), table, base, ((ATTEND, PAIR_GAIN), (ATTEND, PAIR_BIAS)))
    lines = outs.pop(0)
    lines[...] = jnp.zeros(lines.shape, F32)
    for index, name in enumerate(SINGLE_VECTORS):
        first, shape = table[name]
        for block in range(shape[0] // STRIDE):
            lines[index : index + 1, block * STRIDE : (block + 1) * STRIDE] = rows[
                first - base + block : first - base + block + 1, :
            ]


def pack_kernel(table, total, first_lane, base, names, *refs):
    ins, out, rows = refs[: len(names)], refs[-2], refs[-1]
    for name, ref in zip(names, ins):
        if isinstance(name, tuple):
            first, shape = table[name]
            if shape[1] % STRIDE:
                put_narrow(rows, first - base, shape[1], ref[...])
            else:
                put_matrix(rows, first - base, ref)
        else:
            for index, vector in name:
                first, shape = table[vector]
                for block in range(shape[0] // STRIDE):
                    rows[first + block - base : first + block - base + 1, :] = ref[
                        index : index + 1, block * STRIDE : (block + 1) * STRIDE
                    ]
    runs_from_rows(rows, out, first_lane, base, total)


def shard_kernel(whole, info, summed, others, out, squares, runs):
    half = STRIDE // 2
    crops, first, part = summed.shape[0], summed.shape[1], others.shape[1]

    def add(lane, carry):
        runs[lane] = sum(summed[crop, lane].astype(F32) for crop in range(crops))
        return carry

    lax.fori_loop(0, first, add, 0)
    for crop in range(crops):

        def move(lane, carry, crop=crop):
            runs[first + crop * part + lane] = others[crop, lane].astype(F32)
            return carry

        lax.fori_loop(0, part, move, 0)
    squares[...] = jnp.zeros(squares.shape, F32)

    def one(block, carry):
        first = runs[pl.ds(info[0] * half, half), block, :]
        second = runs[pl.ds(half - info[0] * half, half), block, :]
        values = jnp.concatenate([first, second], axis=0).T
        row = block * STRIDE + lax.broadcasted_iota(jnp.int32, values.shape, 0)
        lane = lax.broadcasted_iota(jnp.int32, values.shape, 1)
        values = jnp.where(row * STRIDE + lane < whole, values, 0.0)
        out[pl.ds(block * STRIDE, STRIDE), :] = values
        squares[...] += jnp.sum((values * values).reshape(-1, 8, STRIDE), axis=0)
        return carry

    lax.fori_loop(0, RUN, one, 0)


def whole_call(kernel, name, ins, outs, scratch, time=8):
    def spec(axis):
        return pl.BlockSpec(memory_space=pltpu.SMEM if axis == "smem" else pltpu.VMEM)

    return pl.pallas_call(
        kernel,
        in_specs=[spec(axis) for array, axis in ins],
        out_specs=[pl.BlockSpec(memory_space=pltpu.VMEM) for shape, dtype in outs],
        out_shape=[jax.ShapeDtypeStruct(shape, dtype) for shape, dtype in outs],
        scratch_shapes=[pltpu.VMEM(shape, dtype) for shape, dtype in scratch],
        compiler_params=pltpu.CompilerParams(vmem_limit_bytes=VMEM_LIMIT),
        cost_estimate=cost(time),
        name=name,
    )(*[array for array, axis in ins])


def unpack_pair(table, total, runs):
    outs = []
    names = []
    for name in PAIR_MATRICES:
        shape = table[name][1]
        outs += [(shape, BF16), (shape[::-1], BF16)]
        names += [name, (name, T)]
    for prefix in (STARTING, ENDING):
        outs += [((STRIDE, 8), BF16), ((8, STRIDE), BF16)]
        names += [(prefix, BIAS_W), (prefix, BIAS_T)]
    for prefix, parts in PAIR_COLUMNS:
        outs.append(((STRIDE, 8), F32))
        names.append((prefix, COLS))
    height = row_height(0, 0, runs.shape[1], total)
    values = whole_call(
        functools.partial(unpack_pair_kernel, table, total), "pair_weights", [(runs, None)], outs,
        [((height, STRIDE), F32)], 20,
    )
    return dict(zip(names, values))


def unpack_single(table, total, first_lane, runs):
    outs = [(table[name][1], BF16) for name in SINGLE_MATRICES]
    names = list(SINGLE_MATRICES)
    shape = table[(ATTEND, PAIR_PROJ)][1]
    outs += [(shape, BF16), (shape[::-1], BF16), ((STRIDE, 8), F32), ((8, S), F32)]
    names += [(ATTEND, PAIR_PROJ), ((ATTEND, PAIR_PROJ), T), (ATTEND, COLS), (SINGLE, VECTORS)]
    base = first_lane * (total // STRIDE) // STRIDE
    height = row_height(base, first_lane, first_lane + runs.shape[1], total)
    values = whole_call(
        functools.partial(unpack_single_kernel, table, total, first_lane), "single_weights",
        [(runs, None)], outs, [((height, STRIDE), F32)],
    )
    return dict(zip(names, values))


def pack(name, table, total, shards, lanes, base, parts):
    height = row_height(base, *lanes, total)
    for held, array in parts:
        if isinstance(held, tuple):
            end = table[held][0] - base + array.shape[0] * max(1, array.shape[1] // STRIDE)
            height = max(height, -(-end // 8) * 8)
    return whole_call(
        functools.partial(pack_kernel, table, total, lanes[0], base, [held for held, array in parts]),
        name, [(array, None) for held, array in parts],
        [((shards, lanes[1] - lanes[0], RUN, STRIDE), BF16)], [((height, STRIDE), F32)],
    )[0]


def bias_to_lanes(out, scratch):
    heads, devices = scratch.shape[0], out.shape[0]
    part = scratch.shape[2] // devices
    per = STRIDE // part
    lane = lax.broadcasted_iota(jnp.int32, (scratch.shape[1], STRIDE), 1)
    for device in range(devices):
        block, place = device // per, device % per
        for first in range(0, heads, per):
            total = None
            for index in range(per):
                values = scratch[first + index, :, block * STRIDE : (block + 1) * STRIDE]
                values = pltpu.roll(values, (index - place) * part % STRIDE, 1)
                total = values if index == 0 else jnp.where(lane < index * part, total, values)
            out[device, :, first * part : first * part + STRIDE] = total.astype(out.dtype)


def lanes_to_bias(scratch, sent):
    heads, devices = scratch.shape[0], sent.shape[0]
    part = scratch.shape[2] // devices
    per = STRIDE // part
    lane = lax.broadcasted_iota(jnp.int32, (scratch.shape[1], STRIDE), 1)
    for head in range(heads):
        first, index = head // per * per, head % per
        for block in range(devices // per):
            total = None
            for place in range(per):
                values = sent[block * per + place, :, first * part : first * part + STRIDE].astype(F32)
                values = pltpu.roll(values, (place - index) * part % STRIDE, 1)
                total = values if place == 0 else jnp.where(lane < place * part, total, values)
            scratch[head, :, block * STRIDE : (block + 1) * STRIDE] = total


def standardize_lanes(values):
    centred = values - jnp.mean(values, axis=1, keepdims=True)
    inverse = lax.rsqrt(jnp.mean(centred * centred, axis=1, keepdims=True) + EPSILON)
    return centred * inverse, inverse


def single_kernel(
    state_in, back_in, project, kv, bias, alive, vectors, output_w, up, down,
    final_out, grad_out, sent, query_grad, gate_grad, output_grad, up_grad, down_grad, vecs,
):
    state = state_in[...]
    rows, width = state.shape
    size = width // SA_HEADS
    per = STRIDE // rows
    groups = SA_HEADS // per
    scale = size**-0.5
    tokens = kv.shape[0] * rows
    both = kv[...].reshape(tokens, 2 * width)
    keys, values = both[:, :width], both[:, width:]
    penalty = ((alive[...] - 1.0) * (MASKED * LOG2E)).T[:, 0:1]

    channel = lax.broadcasted_iota(jnp.int32, (width, STRIDE), 0)
    lane = lax.broadcasted_iota(jnp.int32, (width, STRIDE), 1)
    own = [lax.div(channel, size) == group * per + lax.div(lane, rows) for group in range(groups)]
    channel_b = lax.broadcasted_iota(jnp.int32, (STRIDE, width), 1)
    row_b = lax.broadcasted_iota(jnp.int32, (STRIDE, width), 0)
    own_b = [lax.div(channel_b, size) == group * per + lax.div(row_b, rows) for group in range(groups)]

    def spread_rows(matrix):
        turned = jnp.concatenate([matrix] * per, axis=0).T
        return [jnp.where(mask, turned, 0.0).astype(BF16) for mask in own]

    def collect(blocks):
        total = sum(jnp.where(mask, block, 0.0) for mask, block in zip(own_b, blocks))
        return sum(total[index * rows : (index + 1) * rows] for index in range(per))

    queries = spread_rows(project[:, :width] * (scale * LOG2E))
    gate = sigmoid(project[:, 3 * width :])
    scores = [
        mm(keys, queries[group])
        + bias[:, :, group * STRIDE : (group + 1) * STRIDE].reshape(tokens, STRIDE).astype(F32) * LOG2E
        + penalty
        for group in range(groups)
    ]
    shifted = [jnp.exp2(block - jnp.max(block, axis=0, keepdims=True)) for block in scores]
    probs = [block / jnp.sum(block, axis=0, keepdims=True) for block in shifted]
    probs_low = [block.astype(BF16) for block in probs]
    mixed = collect([mm_tn(block, values) for block in probs_low])
    gated = mixed * gate
    gated_low = gated.astype(BF16)
    state = state + mm(gated_low, output_w[...])

    unit, inverse = standardize_lanes(state)
    gain = vectors[2:3]
    lowered = (unit * gain + vectors[3:4]).astype(BF16)
    hidden = mm(lowered, up[...])
    half = hidden.shape[1] // 2
    first, second = hidden[:, :half], hidden[:, half:]
    slope = sigmoid(first)
    silu = first * slope
    swish = (silu * second).astype(BF16)
    final_out[...] = state + mm(swish, down[...])

    grad = back_in[...]
    grad_low = grad.astype(BF16)
    grad_mixed = mm_nt(grad_low, down[...])
    down_grad[...] = mm_tn(swish, grad_low)
    grad_hidden = jnp.concatenate(
        [
            (grad_mixed * second * (slope + silu * (1.0 - slope))).astype(BF16),
            (grad_mixed * silu).astype(BF16),
        ],
        axis=1,
    )
    grad_lowered = mm_nt(grad_hidden, up[...])
    vecs[...] = jnp.zeros(vecs.shape, F32)
    vecs[0:1] = jnp.sum(grad_lowered * unit, axis=0, keepdims=True)
    vecs[1:2] = jnp.sum(grad_lowered, axis=0, keepdims=True)
    grad_unit = grad_lowered * gain
    grad = grad + inverse * (
        grad_unit
        - jnp.mean(grad_unit, axis=1, keepdims=True)
        - unit * jnp.mean(grad_unit * unit, axis=1, keepdims=True)
    )
    grad_out[...] = grad

    grad_low = grad.astype(BF16)
    grad_gated = mm_nt(grad_low, output_w[...])
    gate_grad[...] = grad_gated * gated * (1.0 - gate)
    grads = spread_rows(grad_gated * gate)
    grad_probs = [mm(values, block) for block in grads]
    grad_scores = []
    for block, grad_block in zip(probs, grad_probs):
        delta = jnp.sum(block * grad_block, axis=0, keepdims=True)
        grad_scores.append((block * (grad_block - delta)).astype(BF16))
    for group, block in enumerate(grad_scores):
        sent[:, :, group * STRIDE : (group + 1) * STRIDE] = block.reshape(kv.shape[0], rows, STRIDE)
    query_grad[...] = collect([mm_tn(block, keys) for block in grad_scores]) * scale
    key_part = sum(mm_nt(block, query) for block, query in zip(grad_scores, queries)) * (1.0 / LOG2E)
    value_part = sum(mm_nt(block, grad_block) for block, grad_block in zip(probs_low, grads))
    first = groups * STRIDE
    sent[:, :, first : first + width] = key_part.astype(BF16).reshape(kv.shape[0], rows, width)
    sent[:, :, first + width :] = value_part.astype(BF16).reshape(kv.shape[0], rows, width)
    output_grad[...] = mm_tn(gated_low, grad_low)
    up_grad[...] = mm_tn(lowered, grad_hidden)


def single_middle(state, back, projected, bias, alive, weights):
    lowered, project, kv = projected
    rows, width = state.shape
    devices = kv.shape[0]
    names = ((ATTEND, OUTPUT), (SINGLE, UP), (SINGLE, DOWN))
    matrices = [weights[name] for name in names]
    square = (rows, width)
    outs = [
        (square, F32), (square, F32), ((devices, rows, SA_HEADS * rows + 2 * width), BF16),
        (square, F32), (square, F32),
    ] + [(matrix.shape, F32) for matrix in matrices] + [((8, width), F32)]
    ins = [state, back, project, kv, bias, alive, weights[(SINGLE, VECTORS)]] + matrices
    final, grad, sent, query_grad, gate_grad, *found, vecs = whole_call(
        single_kernel, "single_path", [(array, None) for array in ins], outs, [], 1
    )
    grads = dict(zip(names, found))
    grads[(SINGLE, NORM_GAIN)], grads[(SINGLE, NORM_BIAS)] = vecs[0], vecs[1]
    return final, grad, sent, grads, (state, lowered, query_grad, gate_grad)


def swap(values, group):
    return lax.all_to_all(values, group, split_axis=0, concat_axis=0, tiled=True)


def single_project(single_state, weights, devices):
    gain, shift = norm_pair(weights, ATTEND)
    lowered = layer_norm(single_state, gain, shift).astype(BF16)
    width = lowered.shape[1]
    qkvg = matmul(lowered, weights[(ATTEND, QKVG)])
    both = qkvg[:, width : 3 * width].astype(BF16)
    both = jnp.broadcast_to(both[None], (devices,) + both.shape)
    return lowered, qkvg, both


def single_attend_end(pending, parts, weights, grads):
    single_state, lowered, grad_query, grad_gate = pending
    rows, width = lowered.shape
    grad_both = jnp.sum(parts.astype(F32), axis=0)
    grad_qkvg = jnp.concatenate(
        [grad_query.reshape(rows, width), grad_both, grad_gate], axis=-1
    ).astype(BF16)
    grads[(ATTEND, QKVG)] = outer_sum(lowered, grad_qkvg)
    grad_lowered = matmul(grad_qkvg, weights[(ATTEND, QKVG)].T)
    gain, shift = norm_pair(weights, ATTEND)
    grad_single, grads[(ATTEND, NORM_GAIN)], grads[(ATTEND, NORM_BIAS)] = norm_backward(
        single_state, gain, shift, grad_lowered
    )
    return grad_single


def after(values, *others):
    held = lax.optimization_barrier((values,) + others)
    return held


def in_turn():
    last = []

    def send(values, axes):
        if last:
            values = after(values, last.pop())[0]
        moved = swap(values, axes)
        last.append(moved)
        return moved

    return send


def along_line(values, axis):
    count = values.shape[0]
    here = lax.axis_index(axis)
    moved = jnp.zeros_like(values)
    for step in range(count):
        part = lax.dynamic_slice_in_dim(values, lax.rem(here + step, count), 1)
        if step:
            part = lax.ppermute(part, axis, [(place, (place + step) % count) for place in range(count)])
        moved = lax.dynamic_update_slice_in_dim(moved, part, lax.rem(here + count - step, count), 0)
    return moved


def pair_path(pair, info, alive, orders, weights, cotangent, middle, between, meet, send, group, parts):
    rows, length, width = pair.shape
    hidden = weights[(OUTGOING, PROJ_OUT)].shape[0]
    devices = length // rows
    cores = devices // parts
    order, order_back = orders
    read_first = functools.partial(read_tokens, order)
    read_last = functools.partial(read_turned, order)
    part = hidden // devices
    steps = rows // 16
    state_shape = (rows, width, length)
    block = rows // steps
    half = rows // 2
    flip_shape = (devices, rows, rows, width)
    product_shape = (devices, 2, part, rows, length)
    product_half = (devices, 2, part, half, length)
    tri_shape = (devices, part, rows, length)
    tri_half = (devices, part, half, length)
    channel_block = math.gcd(part, 4)

    def products(name, kernel, arrays, out_shape):
        axes = {4: 1, 5: 2}
        out = (out_shape, BF16, axes[len(out_shape)])
        return run_rows(
            kernel, name, part // channel_block,
            [(Both(pieces), axes[pieces[0].ndim]) for pieces in arrays],
            [out] * (rows // out_shape[-2]), [], 7,
        )

    def swap_all(pieces):
        return [send(values, group) for values in pieces]

    def by_hidden(pieces):
        return [values.reshape((hidden,) + values.shape[2:]) for values in pieces]

    def by_device(pieces):
        return [values.reshape((devices, part) + values.shape[1:]) for values in pieces]

    def cols(prefix):
        return weights[(prefix, COLS)]

    tri_cols = cols

    def turned(name):
        return weights[(name, T)]

    tri_scratch = ((hidden, block, length), F32)
    product_scratch = ((2 * hidden, block, length), F32)
    head_scratch = ((8, block, length), F32)
    wide = ((width, length), F32)
    flip_scratch = ((length, block, width), F32)
    table = ((TA_HEADS, length, length), F32)
    attend_saves = [((rows, TA_HEADS, length), F32, 0), (state_shape, BF16, 0)]

    product = run_rows(
        functools.partial(tri_pre_first_kernel, devices, read_first), "outgoing_in", steps,
        [
            (info, "smem"), (alive, None), (pair, 0), (tri_cols(OUTGOING), None),
            (turned((OUTGOING, PROJ_GATE)), None),
        ],
        [(product_shape, BF16, 3)], [product_scratch], 13,
    )
    between(0, product[0])
    product_one = swap_all(product)
    tri_one = products(
        "outgoing_product", functools.partial(tri_product_kernel, False), [product_one], tri_half
    )
    tri_one = by_hidden(swap_all(tri_one))
    tri_one = [tri_one[0], *meet(0, tri_one[1])]
    state_one, product = run_halves(
        functools.partial(tri_join_kernel, devices, read_first), "outgoing_out_incoming_in", steps,
        [
            ([info[:half], info[half:]], "smem"), (alive, None), (pair, 0), (tri_one, 1), (tri_cols(OUTGOING), None),
            (turned((OUTGOING, PROJ_OUT)), None), (turned((OUTGOING, GATE_OUT)), None),
            (tri_cols(INCOMING), None), (turned((INCOMING, PROJ_GATE)), None),
        ],
        [(state_shape, F32, 0), (product_half, BF16, 3)], [tri_scratch, product_scratch], 22,
    )
    product_two = list(meet(1, *swap_all(product)))
    tri_two = products(
        "incoming_product", functools.partial(tri_product_kernel, True), [product_two], tri_shape
    )
    tri_two = by_hidden(swap_all(tri_two))
    between(1, None)
    (tri_two,) = meet(2, *tri_two)
    cotangent = cotangent.reshape(rows, parts, cores, parts, -1, width).transpose(3, 2, 1, 4, 0, 5)
    cotangent = send(cotangent.reshape(flip_shape), group)
    state_two, bias = run_rows(
        tri_last_kernel, "incoming_out_starting_bias", steps,
        [
            (state_one, 0), (tri_two, 1), (tri_cols(INCOMING), None),
            (turned((INCOMING, PROJ_OUT)), None), (turned((INCOMING, GATE_OUT)), None),
            (cols(STARTING), None), (weights[(STARTING, BIAS_T)], None),
        ],
        [(state_shape, F32, 0), ((TA_HEADS, rows, length), BF16, 1)], [tri_scratch, head_scratch],
    )
    bias_one = lax.all_gather(bias, group, axis=0, tiled=False)
    flipped, totals_one, mixed_one, bias = run_rows(
        starting_kernel, "starting_attention", steps,
        [
            (alive, None), (state_two, 0), (bias_one, None), (cols(STARTING), None),
            (turned((STARTING, QKVG)), None), (turned((STARTING, OUTPUT)), None), (cols(ENDING), None),
            (weights[(ENDING, BIAS_T)], None),
        ],
        [(flip_shape, BF16, 2)] + attend_saves + [((TA_HEADS, rows, length), BF16, 1)],
        [table, flip_scratch, head_scratch], 21,
    )
    state_three = Both([send(flipped, group)])
    bias_two = lax.all_gather(bias, group, axis=0, tiled=False)
    cotangent = along_line(cotangent.reshape((parts, cores) + flip_shape[1:]), "z").reshape(flip_shape)
    state_four, totals_two, mixed_two = run_rows(
        ending_kernel, "ending_attention", steps,
        [
            (alive, None), (state_three, 1), (bias_two, None), (cols(ENDING), None),
            (turned((ENDING, QKVG)), None), (turned((ENDING, OUTPUT)), None),
        ],
        [(state_shape, F32, 0)] + attend_saves, [table], 1,
    )
    pair_cols, attend_cols = cols(PAIR), cols(ATTEND)
    state_five, pair_out, single_bias = run_rows(
        functools.partial(transition_kernel, order_back), "pair_transition", steps,
        [
            (state_four, 0), (pair_cols, None), (turned((PAIR, UP)), None), (turned((PAIR, DOWN)), None),
            (attend_cols, None), (turned((ATTEND, PAIR_PROJ)), None),
        ],
        [(state_shape, F32, 0), ((length, rows, width), BF16, 1), ((devices, rows, SA_HEADS * rows), BF16, 1)],
        [flip_scratch, ((SA_HEADS, block, length), F32)], 1,
    )
    single_sent = send(middle(send(single_bias, group)), group)
    between(2, single_sent)
    pair_out = send(pair_out.reshape((parts, -1) + pair_out.shape[1:]), "z")
    grads = {}
    grad_four, grads[(PAIR, UP)], grads[(PAIR, DOWN)], grads[(ATTEND, PAIR_PROJ)], vecs = run_rows(
        functools.partial(transition_back_kernel, read_last), "pair_transition_back", steps,
        [
            (state_four, 0), (state_five, 0), (cotangent, 1), (single_sent, 1),
            (pair_cols, None), (turned((PAIR, UP)), None), (weights[(PAIR, UP)], None),
            (weights[(PAIR, DOWN)], None), (attend_cols, None), (weights[(ATTEND, PAIR_PROJ)], None),
        ],
        [
            (state_shape, F32, 0), (weights[(PAIR, UP)].shape, F32, None),
            (weights[(PAIR, DOWN)].shape, F32, None), (weights[(ATTEND, PAIR_PROJ)].shape, F32, None),
            ((8, width), F32, None),
        ],
        [wide, wide, wide, wide, ((SA_HEADS, block, length), F32)], 30,
    )
    grads[(PAIR, VECTORS)] = vecs

    def attention_back(prefix, read, read_grad, source, source_axis, grad, grad_axis, bias, totals, mixed):
        lowered_grad, bias_grad, grads[(prefix, QKVG)], grads[(prefix, OUTPUT)] = run_rows(
            functools.partial(attention_back_kernel, prefix == ENDING, read, read_grad),
            "attention_back", steps,
            [
                (alive, None), (source, source_axis), (grad, grad_axis), (bias, None), (totals, 0),
                (mixed, 0), (cols(prefix), None), (turned((prefix, QKVG)), None),
                (weights[(prefix, QKVG)], None), (weights[(prefix, OUTPUT)], None),
            ],
            [
                (state_shape, BF16, 0), ((devices, TA_HEADS, rows, length), BF16, None),
                (weights[(prefix, QKVG)].shape, F32, None), (weights[(prefix, OUTPUT)].shape, F32, None),
            ],
            [table, table], 34,
        )
        return lowered_grad, send(bias_grad, group)

    lowered_grad, bias_grad = attention_back(
        ENDING, read_flipped, read_plain, state_three, 1, grad_four, 0, bias_two, totals_two, mixed_two
    )
    (bias_grad,) = meet(8, bias_grad)
    flipped, bias_w_grad, vecs = run_rows(
        ending_end_kernel, "ending_attention_end", steps,
        [
            (state_three, 1), (grad_four, 0), (lowered_grad, 0), (bias_grad, 2), (cols(ENDING), None),
            (weights[(ENDING, BIAS_W)], None),
        ],
        [(flip_shape, BF16, 2), ((width, 8), F32, None), ((8, width), F32, None)],
        [wide, wide, head_scratch, flip_scratch],
    )
    grads[(ENDING, BIAS_PROJ)], grads[(ENDING, VECTORS)] = bias_w_grad, vecs
    flipped, held = after(flipped, grads[(ATTEND, PAIR_PROJ)])
    grads[(ATTEND, PAIR_PROJ)] = held
    grad_three = send(flipped, group)
    between(4, grads)
    grad_three = Both(meet(3, grad_three))
    pair_out = send(pair_out.reshape(flip_shape), group)
    pair_out = pair_out.reshape(parts, cores, rows, parts, -1, width).transpose(2, 3, 1, 0, 4, 5)
    pair_out = pair_out.reshape(rows, length, width)
    lowered_grad, bias_grad = attention_back(
        STARTING, read_plain, read_flipped, state_two, 0, grad_three, 1, bias_one, totals_one, mixed_one
    )
    square = weights[(INCOMING, GATE_OUT)].shape
    (
        grad_two, grad_tri, gate_back, bias_w_grad, grads[(INCOMING, PROJ_OUT)], grads[(INCOMING, GATE_OUT)], vecs,
    ) = run_halves(
        starting_end_kernel, "starting_end_incoming_out_back", steps,
        [
            (state_two, 0), (grad_three, 1), (lowered_grad, 0), (bias_grad, 2), (cols(STARTING), None),
            (weights[(STARTING, BIAS_W)], None), (state_one, 0), (tri_two, 1), (tri_cols(INCOMING), None),
            (turned((INCOMING, PROJ_OUT)), None), (turned((INCOMING, GATE_OUT)), None),
            (weights[(INCOMING, PROJ_OUT)], None), (weights[(INCOMING, GATE_OUT)], None),
        ],
        [
            (state_shape, F32, 0), ((hidden, half, length), BF16, 1), (state_shape, BF16, 0),
            ((width, 8), F32, None), (square, F32, None), (square, F32, None), ((8, width), F32, None),
        ],
        [wide, wide, wide, wide, head_scratch, tri_scratch], 26,
    )
    grads[(STARTING, BIAS_PROJ)], grads[(STARTING, VECTORS)] = bias_w_grad, vecs
    grad_tri = swap_all(by_device(grad_tri))
    product_grad = products(
        "incoming_product_back", functools.partial(tri_product_back_kernel, True),
        [grad_tri, product_two], product_half,
    )
    product_grad = swap_all(product_grad)
    between(9, grads)
    product_grad = [*meet(4, product_grad[0]), product_grad[1]]
    (
        grad_one, grad_tri, gate_back, grads[(INCOMING, PROJ_GATE)], grads[(OUTGOING, PROJ_OUT)],
        grads[(OUTGOING, GATE_OUT)], vecs,
    ) = run_halves(
        functools.partial(tri_join_back_kernel, read_first), "incoming_in_outgoing_out_back", steps,
        [
            ([info[:half], info[half:]], "smem"), (alive, None), (state_one, 0), (product_grad, 3), (gate_back, 0), (grad_two, 0),
            (tri_cols(INCOMING), None), (turned((INCOMING, PROJ_GATE)), None),
            (weights[(INCOMING, PROJ_GATE)], None), (pair, 0), (tri_one, 1), (tri_cols(OUTGOING), None),
            (turned((OUTGOING, PROJ_OUT)), None), (turned((OUTGOING, GATE_OUT)), None),
            (weights[(OUTGOING, PROJ_OUT)], None), (weights[(OUTGOING, GATE_OUT)], None),
        ],
        [
            (state_shape, F32, 0), ((hidden, half, length), BF16, 1), (state_shape, BF16, 0),
            (weights[(INCOMING, PROJ_GATE)].shape, F32, None), (square, F32, None), (square, F32, None),
            ((8, width), F32, None),
        ],
        [wide, wide, wide, wide, product_scratch, tri_scratch], 37,
    )
    grads[(INCOMING, VECTORS)] = vecs
    between(5, grads)
    grad_tri = swap_all(by_device(grad_tri))
    grad_tri = [grad_tri[0], *meet(5, grad_tri[1])]
    product_grad = products(
        "outgoing_product_back", functools.partial(tri_product_back_kernel, False),
        [grad_tri, product_one], product_shape,
    )
    (product_grad,) = meet(6, *swap_all(product_grad))
    between(6, grads)
    pair_grad, grads[(OUTGOING, PROJ_GATE)], vecs = run_rows(
        functools.partial(tri_first_back_kernel, read_first, order_back), "outgoing_in_back", steps,
        [
            (info, "smem"), (alive, None), (pair, 0), (product_grad, 3), (gate_back, 0), (grad_one, 0),
            (tri_cols(OUTGOING), None), (turned((OUTGOING, PROJ_GATE)), None),
            (weights[(OUTGOING, PROJ_GATE)], None),
        ],
        [
            ((rows, length, width), BF16, 0), (weights[(OUTGOING, PROJ_GATE)].shape, F32, None),
            ((8, width), F32, None),
        ],
        [wide, wide, product_scratch], 20,
    )
    grads[(OUTGOING, VECTORS)] = vecs
    return pair_out, pair_grad, grads


HELD = {
    (PAIR, VECTORS): ((PAIR, NORM_GAIN), (PAIR, NORM_BIAS), (ATTEND, PAIR_GAIN), (ATTEND, PAIR_BIAS)),
    (ENDING, VECTORS): ((ENDING, NORM_GAIN), (ENDING, NORM_BIAS)),
    (STARTING, VECTORS): (
        (STARTING, NORM_GAIN), (STARTING, NORM_BIAS), (INCOMING, OUT_GAIN), (INCOMING, OUT_BIAS)
    ),
    (INCOMING, VECTORS): (
        (INCOMING, NORM_GAIN), (INCOMING, NORM_BIAS), (OUTGOING, OUT_GAIN), (OUTGOING, OUT_BIAS)
    ),
    (OUTGOING, VECTORS): ((OUTGOING, NORM_GAIN), (OUTGOING, NORM_BIAS)),
}


def vector_part(grads, table, name, first, last):
    pairs = [
        (row, held) for row, held in enumerate(HELD[name]) if first <= table[held][0] < last
    ]
    return (pairs, grads[name])


def fast_shards(parts, cores, pair, single, lengths, params, moment_one, moment_two, pair_cotangent, single_cotangent):
    entries = layout(C, H, S, TA_HEADS, SA_HEADS)
    table, total = table_of(entries)
    count = total // STRIDE
    shard_size = params.shape[0]
    attend = table[(ATTEND, NORM_GAIN)][0]
    pair_lanes = -(-attend * STRIDE // count)
    single_lane = attend * STRIDE // count
    devices = parts * cores
    line, group = ("z", "core"), ("crop", "core")
    row_index = lax.axis_index(line)
    odd = ((row_index * shard_size) % STRIDE) // (STRIDE // 2)
    place = jnp.stack([odd, odd]).astype(jnp.int32)
    shard_rows = jnp.pad(params, (0, RUN * STRIDE * STRIDE - shard_size)).reshape(-1, STRIDE)
    (runs,) = whole_call(
        runs_kernel, "parameter_runs", [(place, "smem"), (shard_rows, None)],
        [((STRIDE, RUN, STRIDE), BF16)], [((STRIDE, RUN, STRIDE), F32)],
    )
    rows, length, width = pair.shape[1:]
    send = in_turn()
    pair_in = send(pair[0].reshape(parts, -1, length, width), "crop")
    first_runs = lax.all_gather(runs[:pair_lanes], line)
    pair_in, _, lengths = after(pair_in, runs, lengths)
    live = lax.all_gather(jnp.broadcast_to(lengths.astype(F32), (8, STRIDE)), "crop")
    pair_in = send(pair_in, "z").reshape(rows, length, width)
    weights = unpack_pair(table, total, first_runs)
    size = rows // parts
    blocks = np.arange(length // size).reshape(parts, cores, parts)
    order = blocks.transpose(2, 1, 0).reshape(-1)
    orders = (order.tolist(), np.argsort(order).tolist())
    tokens = (order[:, None] * size + np.arange(size)).reshape(-1)
    live = live[lax.axis_index("z"), 0, 0]
    width = single.shape[2]
    mask = (tokens.astype(np.float32) < live).astype(F32)
    info = lax.dynamic_slice_in_dim(mask, lax.axis_index(group) * rows, rows).astype(jnp.int32)
    alive = jnp.broadcast_to(mask, (8, length))
    held = {}
    single_grads = {}

    def middle(bias):
        found = single_middle(held["state"], held["back"], held["projected"], bias, alive, weights)
        held["out"], held["grad"], grad_scores, grads, held["pending"] = found
        single_grads.update(grads)
        return grad_scores

    def meet(number, *values):
        if number == 0:
            others = [held["runs"]]
        elif number == 1:
            others = [weights[(SINGLE, UP)], held["state"]]
        elif number == 2:
            others = [held["projected"][1]]
        elif number == 3:
            others = [reduced[3]]
        elif number == 8:
            others = [single_grads[(ATTEND, QKVG)]]
        elif number == 6:
            values, reduced[5] = after(*values, reduced[5])
            return [values]
        elif number == 4:
            values, reduced[2], _ = after(*values, reduced[2], reduced[4])
            return [values]
        else:
            values, held["both"], reduced[1] = after(*values, held["both"], reduced[1])
            return [values]
        return after(*values, *others)[: len(values)]

    def reduce_runs(sent):
        return jnp.sum(send(sent, line).astype(F32), axis=0).astype(BF16)

    reduced = {}
    lines_held = list(enumerate(SINGLE_VECTORS))
    late_lanes = -(-table[(OUTGOING, OUT_GAIN)][0] * STRIDE // count)
    late_end = table[(OUTGOING, GATE_OUT)][0]
    early = table[(OUTGOING, PROJ_OUT)][0]
    attend_lanes = -(-table[(STARTING, NORM_GAIN)][0] * STRIDE // count)
    first_row = table[(STARTING, NORM_GAIN)][0]
    last_row = table[(STARTING, BIAS_PROJ)][0]

    def lines():
        values = jnp.concatenate([single_grads[name].reshape(1, S) for name in SINGLE_VECTORS], axis=0)
        return jnp.pad(values, ((0, 8 - len(SINGLE_VECTORS)), (0, 0)))

    def between(number, grads):
        if number == 0:
            last_runs = after(runs[single_lane:], pair_in, weights[(OUTGOING, COLS)], live)[0]
            held["runs"] = lax.all_gather(last_runs, line)
            weights.update(unpack_single(table, total, single_lane, held["runs"]))
            for index, name in enumerate(SINGLE_VECTORS):
                weights[name] = weights[(SINGLE, VECTORS)][index]
            both = jnp.concatenate([single[0], single_cotangent[0]], axis=1)
            both = lax.all_gather(both, ("crop",) + line)
            both = both.reshape(parts, parts, cores, parts, -1, 2 * width)
            here = lax.axis_index("z"), lax.axis_index("core"), lax.axis_index("crop")
            both = both[here[0], :, here[1], here[2]].reshape(rows, 2 * width).astype(F32)
            held["state"], held["back"] = both[:, :width], both[:, width:]
            return
        if number == 1:
            lowered, qkvg, both = single_project(held["state"], weights, devices)
            held["projected"] = lowered, qkvg, send(both, group)
            return
        if number == 2:
            parts_held = grads[:, :, SA_HEADS * rows :]
            grad = held["grad"] + single_attend_end(held["pending"], parts_held, weights, single_grads)
            both = jnp.concatenate([held["out"], grad], axis=1).astype(BF16)
            held["both"] = lax.all_gather(both, ("crop",) + line)
            return
        if number == 6:
            reduced[1] = reduce_runs(reduced[1])
            return
        if number == 4:
            sent = pack(
                "single_gradient", table, total, devices, (pair_lanes, STRIDE), attend,
                [(name, single_grads[name]) for name in SINGLE_MATRICES]
                + [((ATTEND, PAIR_PROJ), grads[(ATTEND, PAIR_PROJ)])]
                + [vector_part(grads, table, (PAIR, VECTORS), attend, total), (lines_held, lines())],
            )
            reduced[3] = sent
            sent = sent.reshape((devices * parts, -1) + sent.shape[2:])
            reduced[2] = lax.psum_scatter(sent, line + ("crop",), scatter_dimension=0, tiled=False)
            return
        vectors = [name for name in HELD if name in grads]
        if number == 9:
            taken = -(-(pair_lanes * count - (attend + 2 * S // STRIDE) * STRIDE) // (4 * S))
            sent = pack(
                "attention_gradient", table, total, devices, (attend_lanes, pair_lanes), first_row,
                [(name, grads[name]) for name in PAIR_MATRICES if table[name][0] >= first_row]
                + [(name, grads[name]) for name in ((STARTING, BIAS_PROJ), (ENDING, BIAS_PROJ))]
                + [vector_part(grads, table, name, first_row, attend) for name in vectors]
                + [(lines_held[:2], lines()), ((ATTEND, QKVG), single_grads[(ATTEND, QKVG)][: -(-taken // 8) * 8])],
            )
            reduced[4] = sent
            reduced[5] = lax.psum_scatter(sent, line, scatter_dimension=0, tiled=False)
            return
        sent = pack(
            "pair_gradient", table, total, devices, (late_lanes, attend_lanes), early,
            [(name, grads[name]) for name in PAIR_MATRICES if early <= table[name][0] < last_row]
            + [vector_part(grads, table, name, early, last_row) for name in vectors],
        )
        reduced[1] = sent

    pair_out, pair_grad, grads = pair_path(
        pair_in, info, alive, orders, weights, pair_cotangent[0], middle, between, meet, send, group, parts
    )
    sent = pack(
        "outgoing_gradient", table, total, devices, (0, late_lanes), 0,
        [(name, grads[name]) for name in PAIR_MATRICES if table[name][0] < late_end]
        + [vector_part(grads, table, name, 0, late_end) for name in ((OUTGOING, VECTORS), (INCOMING, VECTORS))],
    )
    reduced[0] = reduce_runs(sent)
    pair_grad = send(pair_grad.reshape(parts, -1, length, pair_grad.shape[2]), "z")
    pair_grad, held["z"] = send(pair_grad, "crop").reshape(rows, length, -1).astype(F32), pair_grad
    both = held["both"].reshape(parts, parts, cores, parts, -1, 2 * width)
    both = both[:, lax.axis_index("crop"), lax.axis_index("core"), lax.axis_index("z")]
    both = both.reshape(rows, 2 * width)
    single_out, single_grad = both[:, :width], both[:, width:].astype(F32)
    summed = lax.all_gather(jnp.concatenate([reduced[0], reduced[1], reduced[5]], axis=0), "crop")
    others = lax.all_gather(reduced[2], "crop")
    shard, squares = whole_call(
        functools.partial(shard_kernel, shard_size), "gradient_share",
        [(place, "smem"), (summed, None), (others, None)],
        [((RUN * STRIDE, STRIDE), F32), ((8, STRIDE), F32)], [((STRIDE, RUN, STRIDE), F32)],
    )
    shard = shard.reshape(-1)[:shard_size]
    squares = after(squares, held["z"])[0]
    clip_norm = jnp.sqrt(jnp.sum(lax.all_gather(squares, line)))
    clipped = shard * (CLIP / jnp.maximum(clip_norm, CLIP))
    new_first = BETA_ONE * moment_one + (1.0 - BETA_ONE) * clipped
    new_second = BETA_TWO * moment_two + (1.0 - BETA_TWO) * clipped * clipped
    rates, decays = rate_tables(entries)
    rate_shard = lax.dynamic_slice_in_dim(jnp.asarray(rates), row_index * shard_size, shard_size)
    decay_shard = lax.dynamic_slice_in_dim(jnp.asarray(decays), row_index * shard_size, shard_size)
    first_hat = new_first / (1.0 - BETA_ONE**STEP)
    second_hat = new_second / (1.0 - BETA_TWO**STEP)
    new_params = params - rate_shard * (
        first_hat / (jnp.sqrt(second_hat) + ADAM_EPS) + decay_shard * params
    )
    return (
        pair_out[None],
        single_out[None],
        pair_grad[None],
        single_grad[None],
        new_params,
        new_first,
        new_second,
        clip_norm,
    )


def solution(mesh):
    crops, devices = mesh.devices.shape
    table, total = table_of(layout(C, H, S, TA_HEADS, SA_HEADS))
    count = total // STRIDE
    lanes = STRIDE + -table[(ATTEND, NORM_GAIN)][0] * STRIDE // count
    fast = devices == 2 * crops and LENGTH % (devices * 16) == 0 and count // devices + 2 <= RUN * STRIDE and lanes % crops == 0
    row = "row"
    if fast:
        mesh = jax.sharding.Mesh(mesh.devices.reshape(crops, crops, 2), ("crop", "z", "core"))
        row = ("z", "core")
    split = [P("crop", row, None, None), P("crop", row, None), P("crop"), P(row)]
    pair, single, lengths, share = split
    return jax.shard_map(
        functools.partial(fast_shards, crops, 2) if fast else shards,
        mesh=mesh,
        in_specs=(pair, single, lengths, share, share, share, pair, single),
        out_specs=(pair, single, pair, single, share, share, share, P()),
        check_vma=False,
    )
```

```python
import functools
import math

import jax
import jax.numpy as jnp
import numpy as np
from jax import lax
from jax.experimental import pallas as pl
from jax.experimental.pallas import tpu as pltpu
from jax.sharding import PartitionSpec as P

C = 128
H = 128
S = 384
TA_HEADS = 4
SA_HEADS = 16
STEP = 10
STRIDE = 128
LENGTH = 256

OUTGOING, INCOMING, STARTING, ENDING, PAIR, ATTEND, SINGLE = range(7)
(
    NORM_GAIN,
    NORM_BIAS,
    PROJ_GATE,
    OUT_GAIN,
    OUT_BIAS,
    PROJ_OUT,
    GATE_OUT,
    QKVG,
    BIAS_PROJ,
    OUTPUT,
    UP,
    DOWN,
    PAIR_GAIN,
    PAIR_BIAS,
    PAIR_PROJ,
    COLS,
    BIAS_W,
    BIAS_T,
    VECTORS,
    T,
) = range(7, 27)


EPSILON = 1e-05
MASKED = 1000000000.0
BETA_ONE = 0.9
BETA_TWO = 0.95
ADAM_EPS = 1e-08
CLIP = 1.0


def layout(pair_width, hidden_width, single_width, tri_heads, att_heads):
    entries = []
    for prefix in (OUTGOING, INCOMING):
        entries += [
            ((prefix, NORM_GAIN), (pair_width,)),
            ((prefix, NORM_BIAS), (pair_width,)),
            ((prefix, PROJ_GATE), (pair_width, 4 * hidden_width)),
            ((prefix, OUT_GAIN), (hidden_width,)),
            ((prefix, OUT_BIAS), (hidden_width,)),
            ((prefix, PROJ_OUT), (hidden_width, pair_width)),
            ((prefix, GATE_OUT), (pair_width, pair_width)),
        ]
    for prefix in (STARTING, ENDING):
        entries += [
            ((prefix, NORM_GAIN), (pair_width,)),
            ((prefix, NORM_BIAS), (pair_width,)),
            ((prefix, QKVG), (pair_width, 4 * pair_width)),
            ((prefix, BIAS_PROJ), (pair_width, tri_heads)),
            ((prefix, OUTPUT), (pair_width, pair_width)),
        ]
    entries += [
        ((PAIR, NORM_GAIN), (pair_width,)),
        ((PAIR, NORM_BIAS), (pair_width,)),
        ((PAIR, UP), (pair_width, 8 * pair_width)),
        ((PAIR, DOWN), (4 * pair_width, pair_width)),
        ((ATTEND, NORM_GAIN), (single_width,)),
        ((ATTEND, NORM_BIAS), (single_width,)),
        ((ATTEND, QKVG), (single_width, 4 * single_width)),
        ((ATTEND, PAIR_GAIN), (pair_width,)),
        ((ATTEND, PAIR_BIAS), (pair_width,)),
        ((ATTEND, PAIR_PROJ), (pair_width, att_heads)),
        ((ATTEND, OUTPUT), (single_width, single_width)),
        ((SINGLE, NORM_GAIN), (single_width,)),
        ((SINGLE, NORM_BIAS), (single_width,)),
        ((SINGLE, UP), (single_width, 8 * single_width)),
        ((SINGLE, DOWN), (4 * single_width, single_width)),
    ]
    return entries


def logical_order(flat):
    return flat.reshape(-1, STRIDE).T.reshape(-1)


def stored_order(vector):
    return vector.reshape(STRIDE, -1).T.reshape(-1)


def rate_tables(entries):
    rates = []
    decays = []
    for name, shape in entries:
        count = math.prod(shape)
        if len(shape) == 1:
            rates.append(np.full(count, 0.5, np.float32))
            decays.append(np.zeros(count, np.float32))
        else:
            rates.append(np.full(count, 2.0 / math.sqrt(shape[0]), np.float32))
            decays.append(np.full(count, 0.01, np.float32))
    rates = np.concatenate(rates)
    decays = np.concatenate(decays)
    return (rates.reshape(STRIDE, -1).T.reshape(-1), decays.reshape(STRIDE, -1).T.reshape(-1))


def unpack(flat, entries):
    pieces = {}
    offset = 0
    for name, shape in entries:
        count = math.prod(shape)
        pieces[name] = flat[offset : offset + count].reshape(shape)
        offset += count
    return pieces


def layer_norm(values, gain, shift):
    centred = values - jnp.mean(values, axis=-1, keepdims=True)
    spread = jnp.mean(centred * centred, axis=-1, keepdims=True)
    return centred * lax.rsqrt(spread + EPSILON) * gain + shift


def norm_backward(values, gain, shift, grad):
    _, pullback = jax.vjp(layer_norm, values, gain, shift)
    return pullback(grad)


def norm_pair(weights, prefix):
    return (
        weights[(prefix, NORM_GAIN)].astype(jnp.float32),
        weights[(prefix, NORM_BIAS)].astype(jnp.float32),
    )


def gated_pair(project, pair_mask):
    half = project.shape[-1] // 2
    return project[..., :half] * jax.nn.sigmoid(project[..., half:]) * pair_mask[..., None]


def gated_output(values, gate):
    return values * jax.nn.sigmoid(gate)


def swiglu(hidden):
    half = hidden.shape[-1] // 2
    return jax.nn.silu(hidden[..., :half]) * hidden[..., half:]


def matmul(left, right):
    return jnp.dot(left, right, preferred_element_type=jnp.float32)


def outer_sum(left, right):
    return jnp.einsum(
        "nc,nd->cd",
        left.reshape(-1, left.shape[-1]),
        right.reshape(-1, right.shape[-1]),
        preferred_element_type=jnp.float32,
    )


def flip(values):
    moved = lax.all_to_all(values, "row", split_axis=1, concat_axis=0, tiled=True)
    return jnp.swapaxes(moved, 0, 1)


def channel_forward(first, second, incoming):
    whole_first, whole_second = (
        lax.all_to_all(first, "row", split_axis=2, concat_axis=0, tiled=True),
        lax.all_to_all(second, "row", split_axis=2, concat_axis=0, tiled=True),
    )
    if incoming:
        local_tri = jnp.einsum(
            "kih,kjh->ijh", whole_first, whole_second, preferred_element_type=jnp.float32
        )
        local_tri = local_tri.astype(jnp.bfloat16).astype(jnp.float32)
    else:
        local_tri = jnp.einsum(
            "ikh,jkh->ijh", whole_first, whole_second, preferred_element_type=jnp.float32
        )
    tri = lax.all_to_all(
        local_tri.astype(jnp.bfloat16), "row", split_axis=0, concat_axis=2, tiled=True
    ).astype(local_tri.dtype)
    return (tri, whole_first, whole_second)


def channel_backward(grad_tri, whole_first, whole_second, incoming):
    whole_grad = lax.all_to_all(grad_tri, "row", split_axis=2, concat_axis=0, tiled=True)
    if incoming:
        grad_a = jnp.einsum(
            "ijh,kjh->kih", whole_grad, whole_second, preferred_element_type=jnp.float32
        )
        grad_b = jnp.einsum(
            "ijh,kih->kjh", whole_grad, whole_first, preferred_element_type=jnp.float32
        )
    else:
        grad_a = jnp.einsum(
            "ijh,jkh->ikh", whole_grad, whole_second, preferred_element_type=jnp.float32
        )
        grad_b = jnp.einsum(
            "ijh,ikh->jkh", whole_grad, whole_first, preferred_element_type=jnp.float32
        )
    return (
        lax.all_to_all(
            grad_a.astype(jnp.bfloat16), "row", split_axis=0, concat_axis=2, tiled=True
        ).astype(grad_a.dtype),
        lax.all_to_all(
            grad_b.astype(jnp.bfloat16), "row", split_axis=0, concat_axis=2, tiled=True
        ).astype(grad_b.dtype),
    )


def triangle_forward(state, pair_mask, weights, prefix, incoming):
    gain, shift = norm_pair(weights, prefix)
    lowered = layer_norm(state, gain, shift).astype(jnp.bfloat16)
    project = matmul(lowered, weights[(prefix, PROJ_GATE)])
    product = gated_pair(project, pair_mask).astype(jnp.bfloat16)
    half = product.shape[-1] // 2
    tri, own, other = channel_forward(product[..., :half], product[..., half:], incoming)
    out_gain = weights[(prefix, OUT_GAIN)].astype(jnp.float32)
    out_shift = weights[(prefix, OUT_BIAS)].astype(jnp.float32)
    out_low = layer_norm(tri, out_gain, out_shift).astype(jnp.bfloat16)
    output = matmul(out_low, weights[(prefix, PROJ_OUT)])
    gate_out = matmul(lowered, weights[(prefix, GATE_OUT)])
    update = gated_output(output, gate_out)
    return (update, (state, lowered, lowered, project, own, other, tri, out_low, output, gate_out))


def triangle_backward(saved, grad_update, pair_mask, weights, prefix, incoming, grads):
    state, lowered, framed, project, own, other, tri, out_low, output, gate_out = saved
    _, pullback = jax.vjp(gated_output, output, gate_out)
    grad_output, grad_gate = pullback(grad_update)
    grad_output = grad_output.astype(jnp.bfloat16)
    grad_gate = grad_gate.astype(jnp.bfloat16)
    grads[(prefix, PROJ_OUT)] = outer_sum(out_low, grad_output)
    grads[(prefix, GATE_OUT)] = outer_sum(lowered, grad_gate)
    grad_normed = matmul(grad_output, weights[(prefix, PROJ_OUT)].T)
    out_gain = weights[(prefix, OUT_GAIN)].astype(jnp.float32)
    out_shift = weights[(prefix, OUT_BIAS)].astype(jnp.float32)
    grad_tri, grads[(prefix, OUT_GAIN)], grads[(prefix, OUT_BIAS)] = norm_backward(
        tri, out_gain, out_shift, grad_normed
    )
    grad_tri = grad_tri.astype(jnp.bfloat16)
    grad_first, grad_second = channel_backward(grad_tri, own, other, incoming)
    _, pullback = jax.vjp(lambda values: gated_pair(values, pair_mask), project)
    (grad_project,) = pullback(jnp.concatenate([grad_first, grad_second], axis=-1))
    grad_project = grad_project.astype(jnp.bfloat16)
    grads[(prefix, PROJ_GATE)] = outer_sum(framed, grad_project)
    grad_framed = matmul(grad_project, weights[(prefix, PROJ_GATE)].T)
    if incoming:
        grad_framed = grad_framed.astype(jnp.bfloat16).astype(jnp.float32)
    grad_lowered = grad_framed + matmul(grad_gate, weights[(prefix, GATE_OUT)].T)
    gain, shift = norm_pair(weights, prefix)
    grad_state, grads[(prefix, NORM_GAIN)], grads[(prefix, NORM_BIAS)] = norm_backward(
        state, gain, shift, grad_lowered
    )
    return grad_state


def row_scores(query, key, bias, penalty, scale):
    scores = jnp.einsum("jhd,khd->hjk", query, key, preferred_element_type=jnp.float32) * scale
    return scores + bias.astype(jnp.float32) + penalty[None, None, :]


def attention_forward(state, penalty, weights, prefix, ending):
    gain, shift = norm_pair(weights, prefix)
    lowered = layer_norm(state, gain, shift).astype(jnp.bfloat16)
    framed = flip(lowered) if ending else lowered
    rows, length, width = framed.shape
    size = width // TA_HEADS
    scale = size ** (-0.5)
    qkvg = matmul(framed, weights[(prefix, QKVG)])
    queries = qkvg[..., :width].astype(jnp.bfloat16).reshape(rows, length, TA_HEADS, size)
    keys = qkvg[..., width : 2 * width].astype(jnp.bfloat16).reshape(rows, length, TA_HEADS, size)
    values = (
        qkvg[..., 2 * width : 3 * width].astype(jnp.bfloat16).reshape(rows, length, TA_HEADS, size)
    )
    gate = qkvg[..., 3 * width :]
    local_bias = (
        matmul(framed, weights[(prefix, BIAS_PROJ)]).astype(jnp.bfloat16).transpose(2, 0, 1)
    )
    bias = lax.all_gather(local_bias, "row", axis=1, tiled=True)

    def forward_row(items):
        query, key, value = items
        scores = row_scores(query, key, bias, penalty, scale)
        top = jnp.max(scores, axis=-1, keepdims=True)
        shifted = jnp.exp(scores - top)
        total = jnp.sum(shifted, axis=-1, keepdims=True)
        probs = (shifted / total).astype(jnp.bfloat16)
        mixed = jnp.einsum("hjk,khd->jhd", probs, value, preferred_element_type=jnp.float32)
        return (mixed, top[..., 0] + jnp.log(total[..., 0]))

    mixed, log_totals = lax.map(forward_row, (queries, keys, values))
    mixed = mixed.reshape(rows, length, width)
    gated_low = gated_output(mixed, gate).astype(jnp.bfloat16)
    returned = flip(gated_low) if ending else gated_low
    update = matmul(returned, weights[(prefix, OUTPUT)])
    return (update, (state, framed, queries, keys, values, gate, bias, mixed, log_totals, returned))


def attention_backward(saved, grad_update, penalty, weights, prefix, ending, grads):
    state, framed, queries, keys, values, gate, bias, mixed, log_totals, returned = saved
    rows, length, width = framed.shape
    size = width // TA_HEADS
    scale = size ** (-0.5)
    grad_low = grad_update.astype(jnp.bfloat16)
    grads[(prefix, OUTPUT)] = outer_sum(returned, grad_low)
    grad_gated = matmul(grad_low, weights[(prefix, OUTPUT)].T)
    if ending:
        grad_gated = flip(grad_gated.astype(jnp.bfloat16)).astype(jnp.float32)
    _, pullback = jax.vjp(gated_output, mixed, gate)
    grad_mixed, grad_gate = pullback(grad_gated)
    grad_mixed = grad_mixed.astype(jnp.bfloat16).reshape(rows, length, TA_HEADS, size)

    def back_row(carry, items):
        query, key, value, log_total, grad_row = items
        scores = row_scores(query, key, bias, penalty, scale)
        probs = jnp.exp(scores - log_total[..., None])
        grad_probs = jnp.einsum("jhd,khd->hjk", grad_row, value, preferred_element_type=jnp.float32)
        delta = jnp.sum(probs * grad_probs, axis=-1, keepdims=True)
        grad_scores = (probs * (grad_probs - delta)).astype(jnp.bfloat16)
        grad_query = (
            jnp.einsum("hjk,khd->jhd", grad_scores, key, preferred_element_type=jnp.float32) * scale
        )
        grad_key = (
            jnp.einsum("hjk,jhd->khd", grad_scores, query, preferred_element_type=jnp.float32)
            * scale
        )
        grad_value = jnp.einsum(
            "hjk,jhd->khd", probs.astype(jnp.bfloat16), grad_row, preferred_element_type=jnp.float32
        )
        return (carry + grad_scores.astype(jnp.float32), (grad_query, grad_key, grad_value))

    empty = jnp.zeros(bias.shape, jnp.float32)
    grad_bias, (grad_query, grad_key, grad_value) = lax.scan(
        back_row, empty, (queries, keys, values, log_totals, grad_mixed)
    )
    grad_bias = lax.psum_scatter(grad_bias, "row", scatter_dimension=1, tiled=True)
    grad_bias = grad_bias.transpose(1, 2, 0).astype(jnp.bfloat16)
    grad_qkvg = jnp.concatenate(
        [
            grad_query.reshape(rows, length, width),
            grad_key.reshape(rows, length, width),
            grad_value.reshape(rows, length, width),
            grad_gate,
        ],
        axis=-1,
    ).astype(jnp.bfloat16)
    grads[(prefix, QKVG)] = outer_sum(framed, grad_qkvg)
    grads[(prefix, BIAS_PROJ)] = outer_sum(framed, grad_bias)
    grad_framed = matmul(grad_qkvg, weights[(prefix, QKVG)].T) + matmul(
        grad_bias, weights[(prefix, BIAS_PROJ)].T
    )
    if ending:
        grad_framed = flip(grad_framed.astype(jnp.bfloat16)).astype(jnp.float32)
    gain, shift = norm_pair(weights, prefix)
    grad_state, grads[(prefix, NORM_GAIN)], grads[(prefix, NORM_BIAS)] = norm_backward(
        state, gain, shift, grad_framed
    )
    return grad_state


def transition_forward(state, weights, prefix):
    gain, shift = norm_pair(weights, prefix)
    lowered = layer_norm(state, gain, shift).astype(jnp.bfloat16)
    hidden = matmul(lowered, weights[(prefix, UP)])
    mixed_low = swiglu(hidden).astype(jnp.bfloat16)
    update = matmul(mixed_low, weights[(prefix, DOWN)])
    return (update, (state, lowered, hidden, mixed_low))


def transition_backward(saved, grad_update, weights, prefix, grads):
    state, lowered, hidden, mixed_low = saved
    grad_low = grad_update.astype(jnp.bfloat16)
    grads[(prefix, DOWN)] = outer_sum(mixed_low, grad_low)
    grad_mixed = matmul(grad_low, weights[(prefix, DOWN)].T)
    _, pullback = jax.vjp(swiglu, hidden)
    (grad_hidden,) = pullback(grad_mixed)
    grad_hidden = grad_hidden.astype(jnp.bfloat16)
    grads[(prefix, UP)] = outer_sum(lowered, grad_hidden)
    grad_lowered = matmul(grad_hidden, weights[(prefix, UP)].T)
    gain, shift = norm_pair(weights, prefix)
    grad_state, grads[(prefix, NORM_GAIN)], grads[(prefix, NORM_BIAS)] = norm_backward(
        state, gain, shift, grad_lowered
    )
    return grad_state


def single_forward(single_state, pair_state, penalty, weights):
    gain, shift = norm_pair(weights, ATTEND)
    lowered = layer_norm(single_state, gain, shift).astype(jnp.bfloat16)
    rows, width = lowered.shape
    size = width // SA_HEADS
    qkvg = matmul(lowered, weights[(ATTEND, QKVG)])
    query = qkvg[:, :width].astype(jnp.bfloat16).reshape(rows, SA_HEADS, size)
    key = qkvg[:, width : 2 * width].astype(jnp.bfloat16)
    value = qkvg[:, 2 * width : 3 * width].astype(jnp.bfloat16)
    gate = qkvg[:, 3 * width :]
    keys_all, values_all = (
        lax.all_gather(key, "row", axis=0, tiled=True),
        lax.all_gather(value, "row", axis=0, tiled=True),
    )
    keys_all = keys_all.reshape(-1, SA_HEADS, size)
    values_all = values_all.reshape(-1, SA_HEADS, size)
    pair_gain = weights[(ATTEND, PAIR_GAIN)].astype(jnp.float32)
    pair_shift = weights[(ATTEND, PAIR_BIAS)].astype(jnp.float32)
    pair_low = layer_norm(pair_state, pair_gain, pair_shift).astype(jnp.bfloat16)
    bias = matmul(pair_low, weights[(ATTEND, PAIR_PROJ)]).transpose(2, 0, 1)
    scores = jnp.einsum(
        "ihd,jhd->hij", query, keys_all, preferred_element_type=jnp.float32
    ) * size ** (-0.5)
    scores = scores + bias + penalty[None, None, :]
    probs = jax.nn.softmax(scores, axis=-1)
    probs_low = probs.astype(jnp.bfloat16)
    mixed = jnp.einsum(
        "hij,jhd->ihd", probs_low, values_all, preferred_element_type=jnp.float32
    ).reshape(rows, width)
    gated_low = gated_output(mixed, gate).astype(jnp.bfloat16)
    update = matmul(gated_low, weights[(ATTEND, OUTPUT)])
    return (
        update,
        (
            single_state,
            pair_state,
            lowered,
            query,
            keys_all,
            values_all,
            gate,
            pair_low,
            probs,
            probs_low,
            mixed,
            gated_low,
        ),
    )


def single_backward(saved, grad_update, weights, grads):
    (
        single_state,
        pair_state,
        lowered,
        query,
        keys_all,
        values_all,
        gate,
        pair_low,
        probs,
        probs_low,
        mixed,
        gated_low,
    ) = saved
    rows, width = lowered.shape
    size = width // SA_HEADS
    scale = size ** (-0.5)
    grad_low = grad_update.astype(jnp.bfloat16)
    grads[(ATTEND, OUTPUT)] = outer_sum(gated_low, grad_low)
    grad_gated = matmul(grad_low, weights[(ATTEND, OUTPUT)].T)
    _, pullback = jax.vjp(gated_output, mixed, gate)
    grad_mixed, grad_gate = pullback(grad_gated)
    grad_mixed = grad_mixed.astype(jnp.bfloat16).reshape(rows, SA_HEADS, size)
    grad_probs = jnp.einsum(
        "ihd,jhd->hij", grad_mixed, values_all, preferred_element_type=jnp.float32
    )
    delta = jnp.sum(probs * grad_probs, axis=-1, keepdims=True)
    grad_scores = (probs * (grad_probs - delta)).astype(jnp.bfloat16)
    grad_query = (
        jnp.einsum("hij,jhd->ihd", grad_scores, keys_all, preferred_element_type=jnp.float32)
        * scale
    )
    key_part = (
        jnp.einsum("hij,ihd->jhd", grad_scores, query, preferred_element_type=jnp.float32) * scale
    )
    value_part = jnp.einsum(
        "hij,ihd->jhd", probs_low, grad_mixed, preferred_element_type=jnp.float32
    )
    grad_key, grad_value = (
        lax.psum_scatter(key_part.reshape(-1, width), "row", scatter_dimension=0, tiled=True),
        lax.psum_scatter(value_part.reshape(-1, width), "row", scatter_dimension=0, tiled=True),
    )
    grad_qkvg = jnp.concatenate(
        [grad_query.reshape(rows, width), grad_key, grad_value, grad_gate], axis=-1
    ).astype(jnp.bfloat16)
    grads[(ATTEND, QKVG)] = outer_sum(lowered, grad_qkvg)
    grad_lowered = matmul(grad_qkvg, weights[(ATTEND, QKVG)].T)
    gain, shift = norm_pair(weights, ATTEND)
    grad_single, grads[(ATTEND, NORM_GAIN)], grads[(ATTEND, NORM_BIAS)] = norm_backward(
        single_state, gain, shift, grad_lowered
    )
    grad_bias = grad_scores.transpose(1, 2, 0)
    grads[(ATTEND, PAIR_PROJ)] = outer_sum(pair_low, grad_bias)
    grad_pair_low = matmul(grad_bias, weights[(ATTEND, PAIR_PROJ)].T)
    pair_gain = weights[(ATTEND, PAIR_GAIN)].astype(jnp.float32)
    pair_shift = weights[(ATTEND, PAIR_BIAS)].astype(jnp.float32)
    grad_pair, grads[(ATTEND, PAIR_GAIN)], grads[(ATTEND, PAIR_BIAS)] = norm_backward(
        pair_state, pair_gain, pair_shift, grad_pair_low
    )
    return (grad_single, grad_pair)


def shards(pair, single, lengths, params, moment_one, moment_two, pair_cotangent, single_cotangent):
    entries = layout(C, H, S, TA_HEADS, SA_HEADS)
    full = lax.all_gather(params.astype(jnp.bfloat16), "row", axis=0, tiled=True)
    weights = unpack(logical_order(full), entries)
    rows = pair.shape[1]
    length = pair.shape[2]
    first_row = lax.axis_index("row") * rows
    mask = (jnp.arange(length, dtype=jnp.int32) < lengths[0]).astype(jnp.float32)
    mask_rows = lax.dynamic_slice_in_dim(mask, first_row, rows)
    pair_mask = mask_rows[:, None] * mask[None, :]
    penalty = (mask - 1.0) * MASKED
    state = pair[0].astype(jnp.float32)
    saved = {}
    for prefix, incoming in ((OUTGOING, False), (INCOMING, True)):
        update, saved[prefix] = triangle_forward(state, pair_mask, weights, prefix, incoming)
        state = state + update
    for prefix, ending in ((STARTING, False), (ENDING, True)):
        update, saved[prefix] = attention_forward(state, penalty, weights, prefix, ending)
        state = state + update
    update, saved[PAIR] = transition_forward(state, weights, PAIR)
    pair_final = state + update
    single_state = single[0].astype(jnp.float32)
    update, saved[ATTEND] = single_forward(single_state, pair_final, penalty, weights)
    single_mid = single_state + update
    update, saved[SINGLE] = transition_forward(single_mid, weights, SINGLE)
    single_final = single_mid + update
    grads = {}
    grad_single = single_cotangent[0].astype(jnp.float32)
    grad_single = grad_single + transition_backward(
        saved[SINGLE], grad_single, weights, SINGLE, grads
    )
    from_single, from_pair = single_backward(saved[ATTEND], grad_single, weights, grads)
    grad_single = grad_single + from_single
    grad_pair = pair_cotangent[0].astype(jnp.float32) + from_pair
    grad_pair = grad_pair + transition_backward(saved[PAIR], grad_pair, weights, PAIR, grads)
    for prefix, ending in ((ENDING, True), (STARTING, False)):
        grad_pair = grad_pair + attention_backward(
            saved[prefix], grad_pair, penalty, weights, prefix, ending, grads
        )
    for prefix, incoming in ((INCOMING, True), (OUTGOING, False)):
        grad_pair = grad_pair + triangle_backward(
            saved[prefix], grad_pair, pair_mask, weights, prefix, incoming, grads
        )
    flat = stored_order(jnp.concatenate([grads[name].reshape(-1) for name, shape in entries]))
    shard_size = params.shape[0]
    row_index = lax.axis_index("row")
    total = lax.psum(flat, ("crop", "row"))
    shard = lax.dynamic_slice_in_dim(total, row_index * shard_size, shard_size)
    norm_squared = jnp.sum(total * total)
    clip_norm = jnp.sqrt(norm_squared)
    clipped = shard * (CLIP / jnp.maximum(clip_norm, CLIP))
    new_first = BETA_ONE * moment_one + (1.0 - BETA_ONE) * clipped
    new_second = BETA_TWO * moment_two + (1.0 - BETA_TWO) * clipped * clipped
    rates, decays = rate_tables(entries)
    rate_shard = lax.dynamic_slice_in_dim(jnp.asarray(rates), row_index * shard_size, shard_size)
    decay_shard = lax.dynamic_slice_in_dim(jnp.asarray(decays), row_index * shard_size, shard_size)
    first_hat = new_first / (1.0 - BETA_ONE**STEP)
    second_hat = new_second / (1.0 - BETA_TWO**STEP)
    new_params = params - rate_shard * (
        first_hat / (jnp.sqrt(second_hat) + ADAM_EPS) + decay_shard * params
    )
    return (
        pair_final.astype(jnp.bfloat16)[None],
        single_final.astype(jnp.bfloat16)[None],
        grad_pair[None],
        grad_single[None],
        new_params,
        new_first,
        new_second,
        clip_norm,
    )


F32 = jnp.float32
BF16 = jnp.bfloat16
LOG2E = 1.4426950408889634
VMEM_LIMIT = 56 * 1024 * 1024


def mm(left, right):
    return lax.dot_general(left, right, (((1,), (0,)), ((), ())), preferred_element_type=F32)


def mm_nt(left, right):
    return lax.dot_general(left, right, (((1,), (1,)), ((), ())), preferred_element_type=F32)


def mm_tn(left, right):
    return lax.dot_general(left, right, (((0,), (0,)), ((), ())), preferred_element_type=F32)


def standardize(values):
    centred = values - jnp.mean(values, axis=0, keepdims=True)
    spread = jnp.mean(centred * centred, axis=0, keepdims=True)
    inverse = lax.rsqrt(spread + EPSILON)
    return centred * inverse, inverse


def standardize_back(unit, inverse, grad_unit):
    first = jnp.mean(grad_unit, axis=0, keepdims=True)
    second = jnp.mean(grad_unit * unit, axis=0, keepdims=True)
    return inverse * (grad_unit - first - unit * second)


def sigmoid(values):
    return 0.5 * jnp.tanh(0.5 * values) + 0.5


def column(ref, index):
    return ref[:, index : index + 1]


def live_pair(info, alive, row):
    return jnp.concatenate(
        [jnp.where(info[row + place] > 0, alive[0:1], 0.0) for place in range(GROUP)], axis=1
    )


GROUP = 8
LAG = 4


def each_group(count, body):
    def step(index, carry):
        body(index * GROUP)
        return carry

    lax.fori_loop(0, count // GROUP, step, 0, unroll=2)


def each_channel(count, body):
    def step(index, carry):
        body(index)
        return carry

    lax.fori_loop(0, count, step, 0)


def join(read, ref, row):
    return jnp.concatenate([read(ref, row + place) for place in range(GROUP)], axis=1)


def pieces_of(values):
    length = values.shape[1] // GROUP
    return [values[:, place * length : (place + 1) * length] for place in range(GROUP)]


def put_rows(ref, row, values):
    for place, part in enumerate(pieces_of(values)):
        ref[row + place] = part.astype(ref.dtype)


def put_inner(scratch, row, values):
    for place, part in enumerate(pieces_of(values)):
        scratch[:, row + place, :] = part


def read_inner(scratch, row):
    return scratch[:, row, :]


def put_turned(scratch, row, values):
    for place, part in enumerate(pieces_of(values)):
        scratch[:, row + place, :] = part.T


def add_lanes(ref, values):
    ref[...] += sum(pieces_of(values))


def spec_full(shape):
    return pl.BlockSpec(shape, lambda step: (0,) * len(shape))


def cost(microseconds):
    return pl.CostEstimate(
        flops=int(microseconds * 1e9), bytes_accessed=int(microseconds * 3e6), transcendentals=0
    )


class Both(list):
    pass


def all_rows(ins, outs):
    extents = [shape[axis] for shape, dtype, axis in outs if axis is not None]
    for array, axis in ins:
        if isinstance(axis, int):
            extents += [member.shape[axis] for member in (array if isinstance(array, list) else [array])]
    return max(extents)


def run_rows(kernel, name, steps, ins, outs, scratch, time=15, half=None, before=None):
    grid = steps if half is None else steps // 2
    offset = grid * (half or 0)
    flat = []
    groups = []
    for array, axis in ins:
        members = array if isinstance(array, Both) else [array]
        flat += [(member, axis) for member in members]
        groups.append((len(members), isinstance(array, Both)))
    full = all_rows(flat, outs)

    def spec(shape, axis):
        if axis is None:
            return spec_full(shape)
        size = full // steps
        first = offset if shape[axis] == full else 0
        sizes = tuple(size if place == axis else extent for place, extent in enumerate(shape))
        return pl.BlockSpec(
            sizes,
            lambda step: tuple(step + first if place == axis else 0 for place in range(len(shape))),
        )

    in_specs = [
        pl.BlockSpec(memory_space=pltpu.SMEM) if axis == "smem" else spec(array.shape, axis)
        for array, axis in flat
    ]
    out_specs = [spec(shape, axis) for shape, dtype, axis in outs]
    arrays = [array for array, axis in flat]
    aliases = {}
    kept = []
    for place, (shape, dtype, axis) in enumerate(outs):
        if before is not None and (axis is None or shape[axis] == full):
            aliases[len(arrays)] = place
            kept.append(place)
            arrays.append(before[place])
            in_specs.append(spec_full(shape) if axis is None else pl.BlockSpec(memory_space=pl.ANY))

    def run(*refs):
        taken = iter(refs)
        given = []
        for number, together in groups:
            members = [next(taken) for _ in range(number)]
            given.append(members if together else members[0])
        held = {place: next(taken) for place in kept}
        results = [next(taken) for _ in outs]

        @pl.when(pl.program_id(0) == 0)
        def _():
            for place, (shape, dtype, axis) in enumerate(outs):
                if axis is None:
                    results[place][...] = (
                        held[place][...] if place in held else jnp.zeros(shape, dtype)
                    )

        kernel(*given, *results, *taken)

    return pl.pallas_call(
        run,
        grid=(grid,),
        in_specs=in_specs,
        out_specs=out_specs,
        out_shape=[jax.ShapeDtypeStruct(shape, dtype) for shape, dtype, axis in outs],
        scratch_shapes=[pltpu.VMEM(shape, dtype) for shape, dtype in scratch],
        input_output_aliases=aliases,
        compiler_params=pltpu.CompilerParams(vmem_limit_bytes=VMEM_LIMIT),
        cost_estimate=cost(time if half is None else time / 2),
        name=name,
    )(*arrays)


def run_halves(kernel, name, steps, ins, outs, scratch, time=15):
    results = []
    for half in range(2):
        chosen = [
            (array[half] if type(array) is list else array, axis) for array, axis in ins
        ]
        before = results[0] if half else None
        results.append(run_rows(kernel, name, steps, chosen, outs, scratch, time, half, before))
    full = all_rows(ins, outs)
    return [
        [results[0][place], results[1][place]]
        if axis is not None and shape[axis] != full
        else results[1][place]
        for place, (shape, dtype, axis) in enumerate(outs)
    ]


def zero_first(*refs):
    @pl.when(pl.program_id(0) == 0)
    def _():
        for ref in refs:
            ref[...] = jnp.zeros(ref.shape, ref.dtype)


def lane_sums(ref):
    return jnp.sum(ref[...].T, axis=0, keepdims=True)


def on_last(body):
    @pl.when(pl.program_id(0) == pl.num_programs(0) - 1)
    def _():
        body()


def read_plain(ref, row):
    return ref[row].astype(F32)


def reorder(values, order):
    size = values.shape[0] // len(order)
    return jnp.concatenate([values[place * size : (place + 1) * size] for place in order], axis=0)


def read_tokens(order, ref, row):
    return reorder(ref[row].astype(F32), order).T


def read_flipped(refs, row):
    parts = jnp.concatenate([ref[:, row] for ref in refs], axis=1)
    return parts.reshape(-1, parts.shape[-1]).astype(F32).T


def read_turned(order, ref, row):
    parts = ref[:, row]
    return reorder(parts.reshape(-1, parts.shape[-1]).astype(F32), order).T


def tri_pre_row(info, alive, row, state, cols, first, proj_t):
    unit, inverse = standardize(state)
    lowered = (unit * column(cols, first) + column(cols, first + 1)).astype(BF16)
    project = mm(proj_t[...], lowered)
    half = project.shape[0] // 2
    return project[:half] * sigmoid(project[half:]) * live_pair(info, alive, row)


def store_product(out, scratch, devices):
    hidden = scratch.shape[0] // 2
    part = hidden // devices

    def one(device, carry):
        out[device, 0] = scratch[pl.ds(device * part, part)].astype(BF16)
        out[device, 1] = scratch[pl.ds(hidden + device * part, part)].astype(BF16)
        return carry

    lax.fori_loop(0, devices, one, 0)


def copy_blocks(target, source, count):
    def one(index, carry):
        target[index] = source[index].astype(target.dtype)
        return carry

    lax.fori_loop(0, count, one, 0)


def store_flipped(out, scratch):
    devices, part = out.shape[0], out.shape[1]

    def one(device, carry):
        out[device] = scratch[pl.ds(device * part, part)].astype(out.dtype)
        return carry

    lax.fori_loop(0, devices, one, 0)


def tri_post_row(state, tri, cols, proj_t, gate_t):
    unit, inverse = standardize(state)
    lowered = (unit * column(cols, 0) + column(cols, 1)).astype(BF16)
    tri_unit, tri_inverse = standardize(tri)
    out_low = (tri_unit * column(cols, 2) + column(cols, 3)).astype(BF16)
    output = mm(proj_t[...], out_low)
    gate = sigmoid(mm(gate_t[...], lowered))
    return unit, inverse, lowered, tri_unit, tri_inverse, out_low, output, gate


def row_base(rows):
    return pl.program_id(0) * rows


def tri_pre_first_kernel(devices, read, info, alive, pair, cols, proj_t, out, scratch):
    rows = pair.shape[0]

    def body(row):
        product = tri_pre_row(
            info, alive, row_base(rows) + row, join(read, pair, row), cols, 0, proj_t
        )
        put_inner(scratch, row, product)

    each_group(rows, body)
    store_product(out, scratch, devices)


def whole_rows(refs, *place):
    parts = jnp.concatenate([ref[(slice(None),) + place] for ref in refs], axis=1)
    return parts.reshape(-1, parts.shape[-1])


def split_rows(values, outs, *place):
    part = outs[0].shape[-2]
    parts = values.astype(BF16).reshape(outs[0].shape[0], -1, values.shape[-1])
    for half, out in enumerate(outs):
        out[(slice(None),) + place] = parts[:, half * part : (half + 1) * part]


def tri_product_kernel(incoming, operands, *outs):
    def body(channel):
        first = whole_rows(operands, 0, channel)
        second = whole_rows(operands, 1, channel)
        tri = mm_tn(first, second) if incoming else mm_nt(first, second)
        split_rows(tri, outs, channel)

    each_channel(operands[0].shape[2], body)


def tri_join_kernel(
    devices, read, info, alive, source, tri_in, cols, proj_t, gate_t, next_cols, next_proj_t,
    state_out, out, tri_scratch, scratch,
):
    rows = state_out.shape[0]
    copy_blocks(tri_scratch, tri_in, tri_in.shape[0])

    def body(row):
        state = join(read, source, row)
        pieces = tri_post_row(state, join(read_inner, tri_scratch, row), cols, proj_t, gate_t)
        state = state + pieces[6] * pieces[7]
        put_rows(state_out, row, state)
        product = tri_pre_row(
            info, alive, row_base(rows) + row, state, next_cols, 0, next_proj_t
        )
        put_inner(scratch, row, product)

    each_group(rows, body)
    store_product(out, scratch, devices)


def tri_last_kernel(
    source, tri_in, cols, proj_t, gate_t, next_cols, bias_t, state_out, bias_out, tri_scratch, scratch
):
    rows = state_out.shape[0]
    copy_blocks(tri_scratch, tri_in, tri_in.shape[0])

    def body(row):
        state = join(read_plain, source, row)
        pieces = tri_post_row(state, join(read_inner, tri_scratch, row), cols, proj_t, gate_t)
        state = state + pieces[6] * pieces[7]
        put_rows(state_out, row, state)
        unit, inverse = standardize(state)
        lowered = (unit * column(next_cols, 0) + column(next_cols, 1)).astype(BF16)
        put_inner(scratch, row, mm(bias_t[...], lowered))

    each_group(rows, body)
    bias_out[...] = scratch[: bias_out.shape[0]].astype(BF16)


def fill_bias(alive, bias_in, table, turned):
    @pl.when(pl.program_id(0) == 0)
    def _():
        length = table.shape[1]
        penalty = (alive[...] - 1.0) * (MASKED * LOG2E)
        for head in range(table.shape[0]):
            values = bias_in[:, head].reshape(length, length).astype(F32) * LOG2E
            if turned:
                table[head] = values + penalty.T[:, 0:1]
            else:
                table[head] = (values + penalty[0:1]).T


def attention_row(state, cols, proj_t):
    unit, inverse = standardize(state)
    lowered = (unit * column(cols, 0) + column(cols, 1)).astype(BF16)
    project = mm(proj_t[...], lowered)
    width = project.shape[0] // 4
    size = width // TA_HEADS
    query = (project[:width] * (size**-0.5 * LOG2E)).astype(BF16)
    key = project[width : 2 * width].astype(BF16)
    value = project[2 * width : 3 * width].astype(BF16)
    gate = sigmoid(project[3 * width :])
    return unit, inverse, lowered, query, key, value, gate


def in_stages(blocks, first, second, third):
    early, late, done = {}, {}, {}
    count = len(blocks)
    for step in range(count + 2 * LAG):
        if step < count:
            early[step] = first(*blocks[step])
        if 0 <= step - LAG < count:
            late[step - LAG] = second(*blocks[step - LAG], early.pop(step - LAG))
        if 0 <= step - 2 * LAG < count:
            place = step - 2 * LAG
            done[blocks[place]] = third(*blocks[place], late.pop(place))
    return done


def head_rows(values, place, head):
    size, length = values.shape[0] // TA_HEADS, values.shape[1] // GROUP
    return values[head * size : (head + 1) * size, place * length : (place + 1) * length]


def gather_heads(done):
    return jnp.concatenate(
        [
            jnp.concatenate([done[place, head] for head in range(TA_HEADS)], axis=0)
            for place in range(GROUP)
        ],
        axis=1,
    )


ROW_BLOCKS = [(place, head) for place in range(GROUP) for head in range(TA_HEADS)]
HEAD_BLOCKS = [(place, head) for head in range(TA_HEADS) for place in range(GROUP)]


def attend_rows(state, row, cols, proj_t, output_t, table, totals, mixed_out):
    unit, inverse, lowered, query, key, value, gate = attention_row(state, cols, proj_t)

    def score(place, head):
        return mm_tn(head_rows(key, place, head), head_rows(query, place, head)) + table[head]

    def shift(place, head, scores):
        top = jnp.max(scores, axis=0, keepdims=True)
        return top, jnp.exp2(scores - top).astype(BF16)

    def mix(place, head, items):
        top, shifted = items
        values = head_rows(value, place, head)
        size = values.shape[0]
        values = jnp.concatenate([values, jnp.ones((16, values.shape[1]), BF16)], axis=0)
        result = mm(values, shifted)
        total = result[size : size + 1]
        return result[:size] / total, top + jnp.log2(total)

    done = in_stages(ROW_BLOCKS, score, shift, mix)
    mixed = gather_heads({block: items[0] for block, items in done.items()})
    put_rows(totals, row, gather_heads({block: items[1] for block, items in done.items()}))
    put_rows(mixed_out, row, mixed)
    return state + mm(output_t[...], (mixed * gate).astype(BF16))


def starting_kernel(
    alive, source, bias_in, cols, proj_t, output_t, next_cols, bias_t, out, totals, mixed, bias_out,
    table, scratch, bias_scratch,
):
    fill_bias(alive, bias_in, table, False)
    rows = source.shape[0]

    def body(row):
        state = attend_rows(
            join(read_plain, source, row), row, cols, proj_t, output_t, table, totals, mixed
        )
        put_turned(scratch, row, state)
        unit, inverse = standardize(state)
        lowered = (unit * column(next_cols, 0) + column(next_cols, 1)).astype(BF16)
        put_inner(bias_scratch, row, mm(bias_t[...], lowered))

    each_group(rows, body)
    store_flipped(out, scratch)
    bias_out[...] = bias_scratch[: bias_out.shape[0]].astype(BF16)


def ending_kernel(alive, source, bias_in, cols, proj_t, output_t, out, totals, mixed, table):
    fill_bias(alive, bias_in, table, True)
    rows = source[0].shape[1]

    def body(row):
        state = attend_rows(
            join(read_flipped, source, row), row, cols, proj_t, output_t, table, totals, mixed
        )
        put_rows(out, row, state)

    each_group(rows, body)


def transition_kernel(
    order, source, cols, up_t, down_t, next_cols, bias_t, state_out, pair_out, bias_out, scratch, bias_scratch
):
    rows = source.shape[0]

    def body(row):
        state = join(read_plain, source, row)
        unit, inverse = standardize(state)
        lowered = (unit * column(cols, 0) + column(cols, 1)).astype(BF16)
        hidden = mm(up_t[...], lowered)
        half = hidden.shape[0] // 2
        first = hidden[:half]
        mixed = (first * sigmoid(first) * hidden[half:]).astype(BF16)
        state = state + mm(down_t[...], mixed)
        put_rows(state_out, row, state)
        put_turned(scratch, row, state)
        unit, inverse = standardize(state)
        lowered = (unit * column(next_cols, 0) + column(next_cols, 1)).astype(BF16)
        put_inner(bias_scratch, row, mm(bias_t[...], lowered))

    each_group(rows, body)
    size = pair_out.shape[0] // len(order)
    for place, held in enumerate(order):
        pair_out[place * size : (place + 1) * size] = scratch[held * size : (held + 1) * size].astype(BF16)
    bias_to_lanes(bias_out, bias_scratch)


def transition_back_kernel(
    read, mid, final, cotangent, bias_grad, cols, up_t, up, down, next_cols, bias_w,
    grad_out, up_grad, down_grad, bias_w_grad, vecs, norm_gain, norm_bias, pair_gain, pair_bias, bias_scratch,
):
    zero_first(norm_gain, norm_bias, pair_gain, pair_bias)
    rows = mid.shape[0]
    lanes_to_bias(bias_scratch, bias_grad)

    def body(row):
        grad = join(read, cotangent, row)
        unit, inverse = standardize(join(read_plain, final, row))
        gain = column(next_cols, 0)
        lowered = (unit * gain + column(next_cols, 1)).astype(BF16)
        grad_bias = join(read_inner, bias_scratch, row).astype(BF16)
        bias_w_grad[...] += mm_nt(lowered, grad_bias)
        grad_lowered = mm(bias_w[...], grad_bias)
        add_lanes(pair_gain, grad_lowered * unit)
        add_lanes(pair_bias, grad_lowered)
        grad = grad + standardize_back(unit, inverse, grad_lowered * gain)
        unit, inverse = standardize(join(read_plain, mid, row))
        gain = column(cols, 0)
        lowered = (unit * gain + column(cols, 1)).astype(BF16)
        hidden = mm(up_t[...], lowered)
        half = hidden.shape[0] // 2
        first, second = hidden[:half], hidden[half:]
        slope = sigmoid(first)
        silu = first * slope
        grad_low = grad.astype(BF16)
        grad_mixed = mm(down[...], grad_low)
        down_grad[...] += mm_nt((silu * second).astype(BF16), grad_low)
        grad_hidden = jnp.concatenate(
            [
                (grad_mixed * second * (slope + silu * (1.0 - slope))).astype(BF16),
                (grad_mixed * silu).astype(BF16),
            ],
            axis=0,
        )
        up_grad[...] += mm_nt(lowered, grad_hidden)
        grad_lowered = mm(up[...], grad_hidden)
        add_lanes(norm_gain, grad_lowered * unit)
        add_lanes(norm_bias, grad_lowered)
        put_rows(grad_out, row, grad + standardize_back(unit, inverse, grad_lowered * gain))

    each_group(rows, body)

    def finish():
        vecs[0:1] += lane_sums(norm_gain)
        vecs[1:2] += lane_sums(norm_bias)
        vecs[2:3] += lane_sums(pair_gain)
        vecs[3:4] += lane_sums(pair_bias)

    on_last(finish)


def attention_back_kernel(
    turned, read, read_grad, alive, source, grad_in, bias_in, totals, mixed_in, cols, proj_t, proj, output,
    grad_out, bias_out, proj_grad, output_grad, table, grad_table,
):
    fill_bias(alive, bias_in, table, turned)
    zero_first(grad_table)
    rows = grad_out.shape[0]

    def body(row):
        unit, inverse, lowered, query, key, value, gate = attention_row(
            join(read, source, row), cols, proj_t
        )
        mixed = join(read_plain, mixed_in, row)
        total = join(read_plain, totals, row)
        grad_low = join(read_grad, grad_in, row).astype(BF16)
        gated = mixed * gate
        output_grad[...] += mm_nt(gated.astype(BF16), grad_low)
        grad_gated = mm(output[...], grad_low)
        grad_gate = grad_gated * gated * (1.0 - gate)
        grad_mixed = (grad_gated * gate).astype(BF16)
        product = grad_mixed.astype(F32) * mixed
        size = query.shape[0] // TA_HEADS

        def score(place, head):
            scores = mm_tn(head_rows(key, place, head), head_rows(query, place, head))
            grads = mm_tn(head_rows(value, place, head), head_rows(grad_mixed, place, head))
            return scores + table[head], grads

        def slope(place, head, items):
            scores, grads = items
            probs = jnp.exp2(scores - head_rows(total, place, head))
            delta = jnp.sum(head_rows(product, place, head), axis=0, keepdims=True)
            grad_scores = probs * (grads - delta)
            grad_table[head] += grad_scores
            return probs.astype(BF16), grad_scores.astype(BF16)

        def back(place, head, items):
            probs, grad_scores = items
            return (
                mm(head_rows(key, place, head), grad_scores) * size**-0.5,
                mm_nt(head_rows(query, place, head), grad_scores) * (1.0 / LOG2E),
                mm_nt(head_rows(grad_mixed, place, head), probs),
            )

        done = in_stages(HEAD_BLOCKS, score, slope, back)
        grad_project = jnp.concatenate(
            [
                gather_heads({block: items[part] for block, items in done.items()})
                for part in range(3)
            ]
            + [grad_gate],
            axis=0,
        ).astype(BF16)
        proj_grad[...] += mm_nt(lowered, grad_project)
        put_rows(grad_out, row, mm(proj[...], grad_project))

    each_group(rows, body)

    def finish():
        for head in range(TA_HEADS):
            bias_out[:, head] = (
                grad_table[head].T.astype(BF16).reshape(bias_out.shape[0], bias_out.shape[2], -1)
            )

    on_last(finish)


def attention_end_row(
    state, grad, grad_lowered, grad_bias, cols, bias_w, bias_w_grad, norm_gain, norm_bias
):
    unit, inverse = standardize(state)
    gain = column(cols, 0)
    lowered = (unit * gain + column(cols, 1)).astype(BF16)
    bias_w_grad[...] += mm_nt(lowered, grad_bias)
    grad_lowered = grad_lowered + mm(bias_w[...], grad_bias)
    add_lanes(norm_gain, grad_lowered * unit)
    add_lanes(norm_bias, grad_lowered)
    return grad + standardize_back(unit, inverse, grad_lowered * gain)


def fill_bias_grad(scratch, bias_grad):
    heads = bias_grad.shape[1]
    total = bias_grad[0].astype(F32)
    for device in range(1, bias_grad.shape[0]):
        total = total + bias_grad[device].astype(F32)
    scratch[:heads] = total
    scratch[heads:] = jnp.zeros((scratch.shape[0] - heads,) + scratch.shape[1:], F32)


def ending_end_kernel(
    source, grad_in, grad_lowered, bias_grad, cols, bias_w,
    grad_out, bias_w_grad, vecs, norm_gain, norm_bias, bias_scratch, scratch,
):
    zero_first(norm_gain, norm_bias)
    fill_bias_grad(bias_scratch, bias_grad)
    rows = grad_in.shape[0]

    def body(row):
        grad = attention_end_row(
            join(read_flipped, source, row), join(read_plain, grad_in, row),
            join(read_plain, grad_lowered, row), join(read_inner, bias_scratch, row).astype(BF16), cols, bias_w, bias_w_grad, norm_gain, norm_bias,
        )
        put_turned(scratch, row, grad)

    each_group(rows, body)
    store_flipped(grad_out, scratch)

    def finish():
        vecs[0:1] += lane_sums(norm_gain)
        vecs[1:2] += lane_sums(norm_bias)

    on_last(finish)


def tri_post_back_row(
    state, tri, grad, cols, proj_t, gate_t, proj, gate_w, proj_grad, gate_grad, out_gain, out_bias
):
    unit, inverse, lowered, tri_unit, tri_inverse, out_low, output, gate = tri_post_row(
        state, tri, cols, proj_t, gate_t
    )
    grad_output = grad * gate
    grad_gate = (grad_output * output * (1.0 - gate)).astype(BF16)
    grad_output = grad_output.astype(BF16)
    proj_grad[...] += mm_nt(out_low, grad_output)
    gate_grad[...] += mm_nt(lowered, grad_gate)
    grad_normed = mm(proj[...], grad_output)
    add_lanes(out_gain, grad_normed * tri_unit)
    add_lanes(out_bias, grad_normed)
    grad_tri = standardize_back(tri_unit, tri_inverse, grad_normed * column(cols, 2))
    return grad_tri, mm(gate_w[...], grad_gate)


def starting_end_kernel(
    source, grad_in, grad_lowered, bias_grad, cols, bias_w,
    below, tri_in, tri_cols, proj_t, gate_t, proj, gate_w,
    grad_out, tri_out, gate_back, bias_w_grad, proj_grad, gate_grad, vecs,
    norm_gain, norm_bias, out_gain, out_bias, bias_scratch, tri_scratch,
):
    zero_first(norm_gain, norm_bias, out_gain, out_bias)
    fill_bias_grad(bias_scratch, bias_grad)
    copy_blocks(tri_scratch, tri_in, tri_in.shape[0])
    rows = source.shape[0]

    def body(row):
        grad = attention_end_row(
            join(read_plain, source, row), join(read_flipped, grad_in, row),
            join(read_plain, grad_lowered, row), join(read_inner, bias_scratch, row).astype(BF16), cols, bias_w, bias_w_grad, norm_gain, norm_bias,
        )
        put_rows(grad_out, row, grad)
        grad_tri, back = tri_post_back_row(
            join(read_plain, below, row), join(read_inner, tri_scratch, row), grad, tri_cols, proj_t, gate_t, proj, gate_w,
            proj_grad, gate_grad, out_gain, out_bias,
        )
        put_rows(gate_back, row, back)
        put_inner(tri_scratch, row, grad_tri)

    each_group(rows, body)
    copy_blocks(tri_out, tri_scratch, tri_out.shape[0])

    def finish():
        vecs[0:1] += lane_sums(norm_gain)
        vecs[1:2] += lane_sums(norm_bias)
        vecs[2:3] += lane_sums(out_gain)
        vecs[3:4] += lane_sums(out_bias)

    on_last(finish)


def tri_product_back_kernel(incoming, grad, operands, *outs):
    def body(channel):
        first = whole_rows(operands, 0, channel)
        second = whole_rows(operands, 1, channel)
        tri = whole_rows(grad, channel)
        if incoming:
            grad_first = mm_nt(second, tri)
            grad_second = mm(first, tri)
        else:
            grad_first = mm(tri, second)
            grad_second = mm_tn(tri, first)
        split_rows(grad_first, outs, 0, channel)
        split_rows(grad_second, outs, 1, channel)

    each_channel(operands[0].shape[2], body)


def tri_pre_back_row(
    info, alive, row, state, product_grad, gate_back, grad, cols, proj_t, proj, proj_grad, norm_gain, norm_bias
):
    unit, inverse = standardize(state)
    gain = column(cols, 0)
    lowered = (unit * gain + column(cols, 1)).astype(BF16)
    project = mm(proj_t[...], lowered)
    half = project.shape[0] // 2
    gate = sigmoid(project[half:])
    grad_first = product_grad * gate * live_pair(info, alive, row)
    grad_second = grad_first * project[:half] * (1.0 - gate)
    grad_project = jnp.concatenate([grad_first.astype(BF16), grad_second.astype(BF16)], axis=0)
    proj_grad[...] += mm_nt(lowered, grad_project)
    grad_lowered = mm(proj[...], grad_project) + gate_back
    add_lanes(norm_gain, grad_lowered * unit)
    add_lanes(norm_bias, grad_lowered)
    return grad + standardize_back(unit, inverse, grad_lowered * gain)


def fill_product_grad(scratch, product_grad):
    devices, part = product_grad.shape[0], product_grad.shape[2]

    def one(device, carry):
        scratch[pl.ds(device * part, part)] = product_grad[device, 0].astype(F32)
        scratch[pl.ds((devices + device) * part, part)] = product_grad[device, 1].astype(F32)
        return carry

    lax.fori_loop(0, devices, one, 0)


def tri_join_back_kernel(
    read, info, alive, source, product_grad, gate_in, grad_in, cols, proj_t, proj,
    below, tri_in, tri_cols, out_t, gate_t, out_w, gate_w,
    grad_out, tri_out, gate_back, proj_grad, out_grad, gate_grad, vecs,
    norm_gain, norm_bias, out_gain, out_bias, scratch, tri_scratch,
):
    zero_first(norm_gain, norm_bias, out_gain, out_bias)
    fill_product_grad(scratch, product_grad)
    copy_blocks(tri_scratch, tri_in, tri_in.shape[0])
    rows = source.shape[0]

    def body(row):
        grad = tri_pre_back_row(
            info, alive, row_base(rows) + row, join(read_plain, source, row),
            join(read_inner, scratch, row), join(read_plain, gate_in, row),
            join(read_plain, grad_in, row), cols, proj_t, proj, proj_grad, norm_gain, norm_bias,
        )
        put_rows(grad_out, row, grad)
        grad_tri, back = tri_post_back_row(
            join(read, below, row), join(read_inner, tri_scratch, row), grad, tri_cols, out_t, gate_t, out_w, gate_w,
            out_grad, gate_grad, out_gain, out_bias,
        )
        put_rows(gate_back, row, back)
        put_inner(tri_scratch, row, grad_tri)

    each_group(rows, body)
    copy_blocks(tri_out, tri_scratch, tri_out.shape[0])

    def finish():
        vecs[0:1] += lane_sums(norm_gain)
        vecs[1:2] += lane_sums(norm_bias)
        vecs[2:3] += lane_sums(out_gain)
        vecs[3:4] += lane_sums(out_bias)

    on_last(finish)


def tri_first_back_kernel(
    read, order, info, alive, source, product_grad, gate_in, grad_in, cols, proj_t, proj,
    grad_out, proj_grad, vecs, norm_gain, norm_bias, scratch,
):
    zero_first(norm_gain, norm_bias)
    fill_product_grad(scratch, product_grad)
    rows = source.shape[0]

    def body(row):
        grad = tri_pre_back_row(
            info, alive, row_base(rows) + row, join(read, source, row),
            join(read_inner, scratch, row), join(read_plain, gate_in, row),
            join(read_plain, grad_in, row), cols, proj_t, proj, proj_grad, norm_gain, norm_bias,
        )
        for place, part in enumerate(pieces_of(grad)):
            grad_out[row + place] = reorder(part.T, order).astype(grad_out.dtype)

    each_group(rows, body)

    def finish():
        vecs[0:1] += lane_sums(norm_gain)
        vecs[1:2] += lane_sums(norm_bias)

    on_last(finish)


RUN = 24


def table_of(entries):
    table = {}
    offset = 0
    for name, shape in entries:
        table[name] = (offset // STRIDE, shape)
        offset += math.prod(shape)
    return table, offset


def runs_kernel(info, shard, out, scratch):
    def one(block, carry):
        scratch[:, block, :] = shard[pl.ds(block * STRIDE, STRIDE), :].T
        return carry

    lax.fori_loop(0, RUN, one, 0)
    half = STRIDE // 2
    turn = info[0] * half

    def move(lane, carry):
        out[lane] = scratch[lax.rem(lane + turn, STRIDE)].astype(BF16)
        return carry

    lax.fori_loop(0, STRIDE, move, 0)


def run_place(shards, total, lane, shard):
    count = total // STRIDE
    whole = total // shards
    step, odd = whole // STRIDE, (whole % STRIDE) // (STRIDE // 2)
    extra = lax.div(shard * odd + jnp.where(lane < STRIDE // 2, 1, 0), 2)
    start = lane * count + shard * step + extra
    return lax.div(start, STRIDE), lax.rem(start, STRIDE)


def rows_from_runs(runs, rows, first_lane, total):
    shards, lanes = runs.shape[0], runs.shape[1]
    base = first_lane * (total // STRIDE) // STRIDE

    def one(index, carry):
        lane, shard = lax.div(index, shards), lax.rem(index, shards)
        row, shift = run_place(shards, total, first_lane + lane, shard)
        row = row - base
        turned = pltpu.roll(runs[shard, lane].astype(F32), shift, 1)
        place = lax.broadcasted_iota(jnp.int32, (RUN + 1, STRIDE), 1)
        last, before = carry
        joint = jnp.where(row - before == RUN, last[2:3], last[1:2])
        below = jnp.concatenate([joint, turned], axis=0)
        above = jnp.concatenate([turned, turned[RUN - 1 :]], axis=0)
        values = jnp.where(place < shift, below, above)
        rows[pl.ds(row, RUN + 1), :] = values
        return values[RUN - 2 :], row

    lax.fori_loop(0, shards * lanes, one, (jnp.zeros((3, STRIDE), F32), -RUN), unroll=4)


def runs_from_rows(rows, out, first_lane, base, total):
    shards, lanes = out.shape[0], out.shape[1]

    def one(index, carry):
        lane, shard = lax.div(index, shards), lax.rem(index, shards)
        row, shift = run_place(shards, total, first_lane + lane, shard)
        turned = pltpu.roll(rows[pl.ds(row - base, RUN + 1), :], (STRIDE - shift) % STRIDE, 1)
        place = lax.broadcasted_iota(jnp.int32, (RUN, STRIDE), 1)
        out[shard, lane] = jnp.where(
            place < STRIDE - shift, turned[:RUN], turned[1:]
        ).astype(BF16)
        return carry

    lax.fori_loop(0, shards * lanes, one, 0, unroll=16 if shards * lanes % 16 == 0 else 8)


def row_height(base, first_lane, last_lane, total):
    end = (last_lane * (total // STRIDE)) // STRIDE + RUN + 2
    return -(-(end - base) // 8) * 8


def take_matrix(rows, first, shape):
    blocks = shape[1] // STRIDE
    return [
        rows[pl.ds(first + block, shape[0], stride=blocks), :]
        if blocks > 1
        else rows[first : first + shape[0], :]
        for block in range(blocks)
    ]


def put_matrix(rows, first, matrix):
    height, width = matrix.shape
    blocks = width // STRIDE
    for block in range(blocks):
        part = matrix[:, block * STRIDE : (block + 1) * STRIDE]
        if blocks > 1:
            rows[pl.ds(first + block, height, stride=blocks), :] = part
        else:
            rows[first : first + height, :] = part


def spread(index, heads, rows):
    lane = lax.broadcasted_iota(jnp.int32, (STRIDE, STRIDE), 0)
    channel = lax.broadcasted_iota(jnp.int32, (STRIDE, STRIDE), 1)
    return (channel == index * (STRIDE // heads) + lane // heads).astype(BF16)


def take_narrow(rows, first, heads, high):
    total = jnp.zeros((high, STRIDE), F32)
    head = lax.broadcasted_iota(jnp.int32, (high, STRIDE), 0)
    lane = lax.broadcasted_iota(jnp.int32, (high, STRIDE), 1)
    for index in range(heads):
        line = rows[first + index : first + index + 1, :]
        picked = jnp.where(lane % heads == head, line, 0.0).astype(BF16)
        total = total + mm(picked, spread(index, heads, rows))
    return total


def put_narrow(rows, first, heads, matrix):
    turned = matrix.T.astype(BF16)
    high = turned.shape[0]
    head = lax.broadcasted_iota(jnp.int32, (high, STRIDE), 0)
    lane = lax.broadcasted_iota(jnp.int32, (high, STRIDE), 1)
    for index in range(heads):
        wide = mm_nt(turned, spread(index, heads, rows))
        rows[first + index : first + index + 1, :] = jnp.sum(
            jnp.where(lane % heads == head, wide, 0.0), axis=0, keepdims=True
        )


PAIR_MATRICES = (
    (OUTGOING, PROJ_GATE), (OUTGOING, PROJ_OUT), (OUTGOING, GATE_OUT),
    (INCOMING, PROJ_GATE), (INCOMING, PROJ_OUT), (INCOMING, GATE_OUT),
    (STARTING, QKVG), (STARTING, OUTPUT), (ENDING, QKVG), (ENDING, OUTPUT), (PAIR, UP), (PAIR, DOWN),
)
PAIR_COLUMNS = (
    (OUTGOING, ((OUTGOING, NORM_GAIN), (OUTGOING, NORM_BIAS), (OUTGOING, OUT_GAIN), (OUTGOING, OUT_BIAS))),
    (INCOMING, ((INCOMING, NORM_GAIN), (INCOMING, NORM_BIAS), (INCOMING, OUT_GAIN), (INCOMING, OUT_BIAS))),
    (STARTING, ((STARTING, NORM_GAIN), (STARTING, NORM_BIAS))),
    (ENDING, ((ENDING, NORM_GAIN), (ENDING, NORM_BIAS))),
    (PAIR, ((PAIR, NORM_GAIN), (PAIR, NORM_BIAS))),
)
SINGLE_MATRICES = ((ATTEND, QKVG), (ATTEND, OUTPUT), (SINGLE, UP), (SINGLE, DOWN))
SINGLE_VECTORS = ((ATTEND, NORM_GAIN), (ATTEND, NORM_BIAS), (SINGLE, NORM_GAIN), (SINGLE, NORM_BIAS))


def put_columns(rows, out, table, base, names):
    out[...] = jnp.zeros(out.shape, F32)
    lines = [rows[table[name][0] - base : table[name][0] - base + 1, :] for name in names]
    lines.append(jnp.zeros((8 - len(lines), STRIDE), F32))
    out[...] = jnp.concatenate(lines, axis=0).T


def unpack_pair_kernel(table, total, runs, *refs):
    rows = refs[-1]
    outs = list(refs[:-1])
    rows_from_runs(runs, rows, 0, total)
    for name in PAIR_MATRICES:
        first, shape = table[name]
        plain, turned = outs.pop(0), outs.pop(0)
        for block, part in enumerate(take_matrix(rows, first, shape)):
            place = slice(block * STRIDE, (block + 1) * STRIDE)
            plain[:, place] = part.astype(BF16)
            turned[place, :] = part.T.astype(BF16)
    for prefix in (STARTING, ENDING):
        plain, turned = outs.pop(0), outs.pop(0)
        first, shape = table[(prefix, BIAS_PROJ)]
        matrix = take_narrow(rows, first, shape[1], 8)
        turned[...] = matrix.astype(BF16)
        plain[...] = matrix.T.astype(BF16)
    for prefix, names in PAIR_COLUMNS:
        put_columns(rows, outs.pop(0), table, 0, names)


def unpack_single_kernel(table, total, first_lane, runs, *refs):
    rows = refs[-1]
    outs = list(refs[:-1])
    rows_from_runs(runs, rows, first_lane, total)
    base = first_lane * (total // STRIDE) // STRIDE
    for name in SINGLE_MATRICES:
        first, shape = table[name]
        out = outs.pop(0)
        for block, part in enumerate(take_matrix(rows, first - base, shape)):
            out[:, block * STRIDE : (block + 1) * STRIDE] = part.astype(BF16)
    first, shape = table[(ATTEND, PAIR_PROJ)]
    matrix = take_narrow(rows, first - base, shape[1], shape[1])
    plain, turned = outs.pop(0), outs.pop(0)
    turned[...] = matrix.astype(BF16)
    plain[...] = matrix.T.astype(BF16)
    put_columns(rows, outs.pop(0), table, base, ((ATTEND, PAIR_GAIN), (ATTEND, PAIR_BIAS)))
    lines = outs.pop(0)
    lines[...] = jnp.zeros(lines.shape, F32)
    for index, name in enumerate(SINGLE_VECTORS):
        first, shape = table[name]
        for block in range(shape[0] // STRIDE):
            lines[index : index + 1, block * STRIDE : (block + 1) * STRIDE] = rows[
                first - base + block : first - base + block + 1, :
            ]


def pack_kernel(table, total, first_lane, base, names, *refs):
    ins, out, rows = refs[: len(names)], refs[-2], refs[-1]
    for name, ref in zip(names, ins):
        if isinstance(name, tuple):
            first, shape = table[name]
            if shape[1] % STRIDE:
                put_narrow(rows, first - base, shape[1], ref[...])
            else:
                put_matrix(rows, first - base, ref)
        else:
            for index, vector in name:
                first, shape = table[vector]
                for block in range(shape[0] // STRIDE):
                    rows[first + block - base : first + block - base + 1, :] = ref[
                        index : index + 1, block * STRIDE : (block + 1) * STRIDE
                    ]
    runs_from_rows(rows, out, first_lane, base, total)


def shard_kernel(whole, info, summed, others, out, squares, runs):
    half = STRIDE // 2
    crops, first, part = summed.shape[0], summed.shape[1], others.shape[1]

    def add(lane, carry):
        runs[lane] = sum(summed[crop, lane].astype(F32) for crop in range(crops))
        return carry

    lax.fori_loop(0, first, add, 0)
    for crop in range(crops):

        def move(lane, carry, crop=crop):
            runs[first + crop * part + lane] = others[crop, lane].astype(F32)
            return carry

        lax.fori_loop(0, part, move, 0)
    squares[...] = jnp.zeros(squares.shape, F32)

    def one(block, carry):
        first = runs[pl.ds(info[0] * half, half), block, :]
        second = runs[pl.ds(half - info[0] * half, half), block, :]
        values = jnp.concatenate([first, second], axis=0).T
        row = block * STRIDE + lax.broadcasted_iota(jnp.int32, values.shape, 0)
        lane = lax.broadcasted_iota(jnp.int32, values.shape, 1)
        values = jnp.where(row * STRIDE + lane < whole, values, 0.0)
        out[pl.ds(block * STRIDE, STRIDE), :] = values
        squares[...] += jnp.sum((values * values).reshape(-1, 8, STRIDE), axis=0)
        return carry

    lax.fori_loop(0, RUN, one, 0)


def whole_call(kernel, name, ins, outs, scratch, time=8):
    def spec(axis):
        return pl.BlockSpec(memory_space=pltpu.SMEM if axis == "smem" else pltpu.VMEM)

    return pl.pallas_call(
        kernel,
        in_specs=[spec(axis) for array, axis in ins],
        out_specs=[pl.BlockSpec(memory_space=pltpu.VMEM) for shape, dtype in outs],
        out_shape=[jax.ShapeDtypeStruct(shape, dtype) for shape, dtype in outs],
        scratch_shapes=[pltpu.VMEM(shape, dtype) for shape, dtype in scratch],
        compiler_params=pltpu.CompilerParams(vmem_limit_bytes=VMEM_LIMIT),
        cost_estimate=cost(time),
        name=name,
    )(*[array for array, axis in ins])


def unpack_pair(table, total, runs):
    outs = []
    names = []
    for name in PAIR_MATRICES:
        shape = table[name][1]
        outs += [(shape, BF16), (shape[::-1], BF16)]
        names += [name, (name, T)]
    for prefix in (STARTING, ENDING):
        outs += [((STRIDE, 8), BF16), ((8, STRIDE), BF16)]
        names += [(prefix, BIAS_W), (prefix, BIAS_T)]
    for prefix, parts in PAIR_COLUMNS:
        outs.append(((STRIDE, 8), F32))
        names.append((prefix, COLS))
    height = row_height(0, 0, runs.shape[1], total)
    values = whole_call(
        functools.partial(unpack_pair_kernel, table, total), "pair_weights", [(runs, None)], outs,
        [((height, STRIDE), F32)], 20,
    )
    return dict(zip(names, values))


def unpack_single(table, total, first_lane, runs):
    outs = [(table[name][1], BF16) for name in SINGLE_MATRICES]
    names = list(SINGLE_MATRICES)
    shape = table[(ATTEND, PAIR_PROJ)][1]
    outs += [(shape, BF16), (shape[::-1], BF16), ((STRIDE, 8), F32), ((8, S), F32)]
    names += [(ATTEND, PAIR_PROJ), ((ATTEND, PAIR_PROJ), T), (ATTEND, COLS), (SINGLE, VECTORS)]
    base = first_lane * (total // STRIDE) // STRIDE
    height = row_height(base, first_lane, first_lane + runs.shape[1], total)
    values = whole_call(
        functools.partial(unpack_single_kernel, table, total, first_lane), "single_weights",
        [(runs, None)], outs, [((height, STRIDE), F32)],
    )
    return dict(zip(names, values))


def pack(name, table, total, shards, lanes, base, parts):
    height = row_height(base, *lanes, total)
    for held, array in parts:
        if isinstance(held, tuple):
            end = table[held][0] - base + array.shape[0] * max(1, array.shape[1] // STRIDE)
            height = max(height, -(-end // 8) * 8)
    return whole_call(
        functools.partial(pack_kernel, table, total, lanes[0], base, [held for held, array in parts]),
        name, [(array, None) for held, array in parts],
        [((shards, lanes[1] - lanes[0], RUN, STRIDE), BF16)], [((height, STRIDE), F32)],
    )[0]


def bias_to_lanes(out, scratch):
    heads, devices = scratch.shape[0], out.shape[0]
    part = scratch.shape[2] // devices
    per = STRIDE // part
    lane = lax.broadcasted_iota(jnp.int32, (scratch.shape[1], STRIDE), 1)
    for device in range(devices):
        block, place = device // per, device % per
        for first in range(0, heads, per):
            total = None
            for index in range(per):
                values = scratch[first + index, :, block * STRIDE : (block + 1) * STRIDE]
                values = pltpu.roll(values, (index - place) * part % STRIDE, 1)
                total = values if index == 0 else jnp.where(lane < index * part, total, values)
            out[device, :, first * part : first * part + STRIDE] = total.astype(out.dtype)


def lanes_to_bias(scratch, sent):
    heads, devices = scratch.shape[0], sent.shape[0]
    part = scratch.shape[2] // devices
    per = STRIDE // part
    lane = lax.broadcasted_iota(jnp.int32, (scratch.shape[1], STRIDE), 1)
    for head in range(heads):
        first, index = head // per * per, head % per
        for block in range(devices // per):
            total = None
            for place in range(per):
                values = sent[block * per + place, :, first * part : first * part + STRIDE].astype(F32)
                values = pltpu.roll(values, (place - index) * part % STRIDE, 1)
                total = values if place == 0 else jnp.where(lane < place * part, total, values)
            scratch[head, :, block * STRIDE : (block + 1) * STRIDE] = total


def standardize_lanes(values):
    centred = values - jnp.mean(values, axis=1, keepdims=True)
    inverse = lax.rsqrt(jnp.mean(centred * centred, axis=1, keepdims=True) + EPSILON)
    return centred * inverse, inverse


def single_kernel(
    state_in, back_in, project, kv, bias, alive, vectors, output_w, up, down,
    final_out, grad_out, sent, query_grad, gate_grad, output_grad, up_grad, down_grad, vecs,
):
    state = state_in[...]
    rows, width = state.shape
    size = width // SA_HEADS
    per = STRIDE // rows
    groups = SA_HEADS // per
    scale = size**-0.5
    tokens = kv.shape[0] * rows
    both = kv[...].reshape(tokens, 2 * width)
    keys, values = both[:, :width], both[:, width:]
    penalty = ((alive[...] - 1.0) * (MASKED * LOG2E)).T[:, 0:1]

    channel = lax.broadcasted_iota(jnp.int32, (width, STRIDE), 0)
    lane = lax.broadcasted_iota(jnp.int32, (width, STRIDE), 1)
    own = [lax.div(channel, size) == group * per + lax.div(lane, rows) for group in range(groups)]
    channel_b = lax.broadcasted_iota(jnp.int32, (STRIDE, width), 1)
    row_b = lax.broadcasted_iota(jnp.int32, (STRIDE, width), 0)
    own_b = [lax.div(channel_b, size) == group * per + lax.div(row_b, rows) for group in range(groups)]

    def spread_rows(matrix):
        turned = jnp.concatenate([matrix] * per, axis=0).T
        return [jnp.where(mask, turned, 0.0).astype(BF16) for mask in own]

    def collect(blocks):
        total = sum(jnp.where(mask, block, 0.0) for mask, block in zip(own_b, blocks))
        return sum(total[index * rows : (index + 1) * rows] for index in range(per))

    queries = spread_rows(project[:, :width] * (scale * LOG2E))
    gate = sigmoid(project[:, 3 * width :])
    scores = [
        mm(keys, queries[group])
        + bias[:, :, group * STRIDE : (group + 1) * STRIDE].reshape(tokens, STRIDE).astype(F32) * LOG2E
        + penalty
        for group in range(groups)
    ]
    shifted = [jnp.exp2(block - jnp.max(block, axis=0, keepdims=True)) for block in scores]
    probs = [block / jnp.sum(block, axis=0, keepdims=True) for block in shifted]
    probs_low = [block.astype(BF16) for block in probs]
    mixed = collect([mm_tn(block, values) for block in probs_low])
    gated = mixed * gate
    gated_low = gated.astype(BF16)
    state = state + mm(gated_low, output_w[...])

    unit, inverse = standardize_lanes(state)
    gain = vectors[2:3]
    lowered = (unit * gain + vectors[3:4]).astype(BF16)
    hidden = mm(lowered, up[...])
    half = hidden.shape[1] // 2
    first, second = hidden[:, :half], hidden[:, half:]
    slope = sigmoid(first)
    silu = first * slope
    swish = (silu * second).astype(BF16)
    final_out[...] = state + mm(swish, down[...])

    grad = back_in[...]
    grad_low = grad.astype(BF16)
    grad_mixed = mm_nt(grad_low, down[...])
    down_grad[...] = mm_tn(swish, grad_low)
    grad_hidden = jnp.concatenate(
        [
            (grad_mixed * second * (slope + silu * (1.0 - slope))).astype(BF16),
            (grad_mixed * silu).astype(BF16),
        ],
        axis=1,
    )
    grad_lowered = mm_nt(grad_hidden, up[...])
    vecs[...] = jnp.zeros(vecs.shape, F32)
    vecs[0:1] = jnp.sum(grad_lowered * unit, axis=0, keepdims=True)
    vecs[1:2] = jnp.sum(grad_lowered, axis=0, keepdims=True)
    grad_unit = grad_lowered * gain
    grad = grad + inverse * (
        grad_unit
        - jnp.mean(grad_unit, axis=1, keepdims=True)
        - unit * jnp.mean(grad_unit * unit, axis=1, keepdims=True)
    )
    grad_out[...] = grad

    grad_low = grad.astype(BF16)
    grad_gated = mm_nt(grad_low, output_w[...])
    gate_grad[...] = grad_gated * gated * (1.0 - gate)
    grads = spread_rows(grad_gated * gate)
    grad_probs = [mm(values, block) for block in grads]
    grad_scores = []
    for block, grad_block in zip(probs, grad_probs):
        delta = jnp.sum(block * grad_block, axis=0, keepdims=True)
        grad_scores.append((block * (grad_block - delta)).astype(BF16))
    for group, block in enumerate(grad_scores):
        sent[:, :, group * STRIDE : (group + 1) * STRIDE] = block.reshape(kv.shape[0], rows, STRIDE)
    query_grad[...] = collect([mm_tn(block, keys) for block in grad_scores]) * scale
    key_part = sum(mm_nt(block, query) for block, query in zip(grad_scores, queries)) * (1.0 / LOG2E)
    value_part = sum(mm_nt(block, grad_block) for block, grad_block in zip(probs_low, grads))
    first = groups * STRIDE
    sent[:, :, first : first + width] = key_part.astype(BF16).reshape(kv.shape[0], rows, width)
    sent[:, :, first + width :] = value_part.astype(BF16).reshape(kv.shape[0], rows, width)
    output_grad[...] = mm_tn(gated_low, grad_low)
    up_grad[...] = mm_tn(lowered, grad_hidden)


def single_middle(state, back, projected, bias, alive, weights):
    lowered, project, kv = projected
    rows, width = state.shape
    devices = kv.shape[0]
    names = ((ATTEND, OUTPUT), (SINGLE, UP), (SINGLE, DOWN))
    matrices = [weights[name] for name in names]
    square = (rows, width)
    outs = [
        (square, F32), (square, F32), ((devices, rows, SA_HEADS * rows + 2 * width), BF16),
        (square, F32), (square, F32),
    ] + [(matrix.shape, F32) for matrix in matrices] + [((8, width), F32)]
    ins = [state, back, project, kv, bias, alive, weights[(SINGLE, VECTORS)]] + matrices
    final, grad, sent, query_grad, gate_grad, *found, vecs = whole_call(
        single_kernel, "single_path", [(array, None) for array in ins], outs, [], 1
    )
    grads = dict(zip(names, found))
    grads[(SINGLE, NORM_GAIN)], grads[(SINGLE, NORM_BIAS)] = vecs[0], vecs[1]
    return final, grad, sent, grads, (state, lowered, query_grad, gate_grad)


def swap(values, group):
    return lax.all_to_all(values, group, split_axis=0, concat_axis=0, tiled=True)


def single_project(single_state, weights, devices):
    gain, shift = norm_pair(weights, ATTEND)
    lowered = layer_norm(single_state, gain, shift).astype(BF16)
    width = lowered.shape[1]
    qkvg = matmul(lowered, weights[(ATTEND, QKVG)])
    both = qkvg[:, width : 3 * width].astype(BF16)
    both = jnp.broadcast_to(both[None], (devices,) + both.shape)
    return lowered, qkvg, both


def single_attend_end(pending, parts, weights, grads):
    single_state, lowered, grad_query, grad_gate = pending
    rows, width = lowered.shape
    grad_both = jnp.sum(parts.astype(F32), axis=0)
    grad_qkvg = jnp.concatenate(
        [grad_query.reshape(rows, width), grad_both, grad_gate], axis=-1
    ).astype(BF16)
    grads[(ATTEND, QKVG)] = outer_sum(lowered, grad_qkvg)
    grad_lowered = matmul(grad_qkvg, weights[(ATTEND, QKVG)].T)
    gain, shift = norm_pair(weights, ATTEND)
    grad_single, grads[(ATTEND, NORM_GAIN)], grads[(ATTEND, NORM_BIAS)] = norm_backward(
        single_state, gain, shift, grad_lowered
    )
    return grad_single


def after(values, *others):
    held = lax.optimization_barrier((values,) + others)
    return held


def in_turn():
    last = []

    def send(values, axes):
        if last:
            values = after(values, last.pop())[0]
        moved = swap(values, axes)
        last.append(moved)
        return moved

    return send


def along_line(values, axis):
    count = values.shape[0]
    here = lax.axis_index(axis)
    moved = jnp.zeros_like(values)
    for step in range(count):
        part = lax.dynamic_slice_in_dim(values, lax.rem(here + step, count), 1)
        if step:
            part = lax.ppermute(part, axis, [(place, (place + step) % count) for place in range(count)])
        moved = lax.dynamic_update_slice_in_dim(moved, part, lax.rem(here + count - step, count), 0)
    return moved


def pair_path(pair, info, alive, orders, weights, cotangent, middle, between, meet, send, group, parts):
    rows, length, width = pair.shape
    hidden = weights[(OUTGOING, PROJ_OUT)].shape[0]
    devices = length // rows
    cores = devices // parts
    order, order_back = orders
    read_first = functools.partial(read_tokens, order)
    read_last = functools.partial(read_turned, order)
    part = hidden // devices
    steps = rows // 16
    state_shape = (rows, width, length)
    block = rows // steps
    half = rows // 2
    flip_shape = (devices, rows, rows, width)
    product_shape = (devices, 2, part, rows, length)
    product_half = (devices, 2, part, half, length)
    tri_shape = (devices, part, rows, length)
    tri_half = (devices, part, half, length)
    channel_block = math.gcd(part, 4)

    def products(name, kernel, arrays, out_shape):
        axes = {4: 1, 5: 2}
        out = (out_shape, BF16, axes[len(out_shape)])
        return run_rows(
            kernel, name, part // channel_block,
            [(Both(pieces), axes[pieces[0].ndim]) for pieces in arrays],
            [out] * (rows // out_shape[-2]), [], 7,
        )

    def swap_all(pieces):
        return [send(values, group) for values in pieces]

    def by_hidden(pieces):
        return [values.reshape((hidden,) + values.shape[2:]) for values in pieces]

    def by_device(pieces):
        return [values.reshape((devices, part) + values.shape[1:]) for values in pieces]

    def cols(prefix):
        return weights[(prefix, COLS)]

    tri_cols = cols

    def turned(name):
        return weights[(name, T)]

    tri_scratch = ((hidden, block, length), F32)
    product_scratch = ((2 * hidden, block, length), F32)
    head_scratch = ((8, block, length), F32)
    wide = ((width, length), F32)
    flip_scratch = ((length, block, width), F32)
    table = ((TA_HEADS, length, length), F32)
    attend_saves = [((rows, TA_HEADS, length), F32, 0), (state_shape, BF16, 0)]

    product = run_rows(
        functools.partial(tri_pre_first_kernel, devices, read_first), "outgoing_in", steps,
        [
            (info, "smem"), (alive, None), (pair, 0), (tri_cols(OUTGOING), None),
            (turned((OUTGOING, PROJ_GATE)), None),
        ],
        [(product_shape, BF16, 3)], [product_scratch], 13,
    )
    between(0, product[0])
    product_one = swap_all(product)
    tri_one = products(
        "outgoing_product", functools.partial(tri_product_kernel, False), [product_one], tri_half
    )
    tri_one = by_hidden(swap_all(tri_one))
    tri_one = [tri_one[0], *meet(0, tri_one[1])]
    state_one, product = run_halves(
        functools.partial(tri_join_kernel, devices, read_first), "outgoing_out_incoming_in", steps,
        [
            ([info[:half], info[half:]], "smem"), (alive, None), (pair, 0), (tri_one, 1), (tri_cols(OUTGOING), None),
            (turned((OUTGOING, PROJ_OUT)), None), (turned((OUTGOING, GATE_OUT)), None),
            (tri_cols(INCOMING), None), (turned((INCOMING, PROJ_GATE)), None),
        ],
        [(state_shape, F32, 0), (product_half, BF16, 3)], [tri_scratch, product_scratch], 22,
    )
    product_two = list(meet(1, *swap_all(product)))
    tri_two = products(
        "incoming_product", functools.partial(tri_product_kernel, True), [product_two], tri_shape
    )
    tri_two = by_hidden(swap_all(tri_two))
    between(1, None)
    (tri_two,) = meet(2, *tri_two)
    cotangent = cotangent.reshape(rows, parts, cores, parts, -1, width).transpose(3, 2, 1, 4, 0, 5)
    cotangent = send(cotangent.reshape(flip_shape), group)
    state_two, bias = run_rows(
        tri_last_kernel, "incoming_out_starting_bias", steps,
        [
            (state_one, 0), (tri_two, 1), (tri_cols(INCOMING), None),
            (turned((INCOMING, PROJ_OUT)), None), (turned((INCOMING, GATE_OUT)), None),
            (cols(STARTING), None), (weights[(STARTING, BIAS_T)], None),
        ],
        [(state_shape, F32, 0), ((TA_HEADS, rows, length), BF16, 1)], [tri_scratch, head_scratch],
    )
    bias_one = lax.all_gather(bias, group, axis=0, tiled=False)
    flipped, totals_one, mixed_one, bias = run_rows(
        starting_kernel, "starting_attention", steps,
        [
            (alive, None), (state_two, 0), (bias_one, None), (cols(STARTING), None),
            (turned((STARTING, QKVG)), None), (turned((STARTING, OUTPUT)), None), (cols(ENDING), None),
            (weights[(ENDING, BIAS_T)], None),
        ],
        [(flip_shape, BF16, 2)] + attend_saves + [((TA_HEADS, rows, length), BF16, 1)],
        [table, flip_scratch, head_scratch], 21,
    )
    state_three = Both([send(flipped, group)])
    bias_two = lax.all_gather(bias, group, axis=0, tiled=False)
    cotangent = along_line(cotangent.reshape((parts, cores) + flip_shape[1:]), "z").reshape(flip_shape)
    state_four, totals_two, mixed_two = run_rows(
        ending_kernel, "ending_attention", steps,
        [
            (alive, None), (state_three, 1), (bias_two, None), (cols(ENDING), None),
            (turned((ENDING, QKVG)), None), (turned((ENDING, OUTPUT)), None),
        ],
        [(state_shape, F32, 0)] + attend_saves, [table], 1,
    )
    pair_cols, attend_cols = cols(PAIR), cols(ATTEND)
    state_five, pair_out, single_bias = run_rows(
        functools.partial(transition_kernel, order_back), "pair_transition", steps,
        [
            (state_four, 0), (pair_cols, None), (turned((PAIR, UP)), None), (turned((PAIR, DOWN)), None),
            (attend_cols, None), (turned((ATTEND, PAIR_PROJ)), None),
        ],
        [(state_shape, F32, 0), ((length, rows, width), BF16, 1), ((devices, rows, SA_HEADS * rows), BF16, 1)],
        [flip_scratch, ((SA_HEADS, block, length), F32)], 1,
    )
    single_sent = send(middle(send(single_bias, group)), group)
    between(2, single_sent)
    pair_out = send(pair_out.reshape((parts, -1) + pair_out.shape[1:]), "z")
    grads = {}
    grad_four, grads[(PAIR, UP)], grads[(PAIR, DOWN)], grads[(ATTEND, PAIR_PROJ)], vecs = run_rows(
        functools.partial(transition_back_kernel, read_last), "pair_transition_back", steps,
        [
            (state_four, 0), (state_five, 0), (cotangent, 1), (single_sent, 1),
            (pair_cols, None), (turned((PAIR, UP)), None), (weights[(PAIR, UP)], None),
            (weights[(PAIR, DOWN)], None), (attend_cols, None), (weights[(ATTEND, PAIR_PROJ)], None),
        ],
        [
            (state_shape, F32, 0), (weights[(PAIR, UP)].shape, F32, None),
            (weights[(PAIR, DOWN)].shape, F32, None), (weights[(ATTEND, PAIR_PROJ)].shape, F32, None),
            ((8, width), F32, None),
        ],
        [wide, wide, wide, wide, ((SA_HEADS, block, length), F32)], 30,
    )
    grads[(PAIR, VECTORS)] = vecs

    def attention_back(prefix, read, read_grad, source, source_axis, grad, grad_axis, bias, totals, mixed):
        lowered_grad, bias_grad, grads[(prefix, QKVG)], grads[(prefix, OUTPUT)] = run_rows(
            functools.partial(attention_back_kernel, prefix == ENDING, read, read_grad),
            "attention_back", steps,
            [
                (alive, None), (source, source_axis), (grad, grad_axis), (bias, None), (totals, 0),
                (mixed, 0), (cols(prefix), None), (turned((prefix, QKVG)), None),
                (weights[(prefix, QKVG)], None), (weights[(prefix, OUTPUT)], None),
            ],
            [
                (state_shape, BF16, 0), ((devices, TA_HEADS, rows, length), BF16, None),
                (weights[(prefix, QKVG)].shape, F32, None), (weights[(prefix, OUTPUT)].shape, F32, None),
            ],
            [table, table], 34,
        )
        return lowered_grad, send(bias_grad, group)

    lowered_grad, bias_grad = attention_back(
        ENDING, read_flipped, read_plain, state_three, 1, grad_four, 0, bias_two, totals_two, mixed_two
    )
    (bias_grad,) = meet(8, bias_grad)
    flipped, bias_w_grad, vecs = run_rows(
        ending_end_kernel, "ending_attention_end", steps,
        [
            (state_three, 1), (grad_four, 0), (lowered_grad, 0), (bias_grad, 2), (cols(ENDING), None),
            (weights[(ENDING, BIAS_W)], None),
        ],
        [(flip_shape, BF16, 2), ((width, 8), F32, None), ((8, width), F32, None)],
        [wide, wide, head_scratch, flip_scratch],
    )
    grads[(ENDING, BIAS_PROJ)], grads[(ENDING, VECTORS)] = bias_w_grad, vecs
    flipped, held = after(flipped, grads[(ATTEND, PAIR_PROJ)])
    grads[(ATTEND, PAIR_PROJ)] = held
    grad_three = send(flipped, group)
    between(4, grads)
    grad_three = Both(meet(3, grad_three))
    pair_out = send(pair_out.reshape(flip_shape), group)
    pair_out = pair_out.reshape(parts, cores, rows, parts, -1, width).transpose(2, 3, 1, 0, 4, 5)
    pair_out = pair_out.reshape(rows, length, width)
    lowered_grad, bias_grad = attention_back(
        STARTING, read_plain, read_flipped, state_two, 0, grad_three, 1, bias_one, totals_one, mixed_one
    )
    square = weights[(INCOMING, GATE_OUT)].shape
    (
        grad_two, grad_tri, gate_back, bias_w_grad, grads[(INCOMING, PROJ_OUT)], grads[(INCOMING, GATE_OUT)], vecs,
    ) = run_halves(
        starting_end_kernel, "starting_end_incoming_out_back", steps,
        [
            (state_two, 0), (grad_three, 1), (lowered_grad, 0), (bias_grad, 2), (cols(STARTING), None),
            (weights[(STARTING, BIAS_W)], None), (state_one, 0), (tri_two, 1), (tri_cols(INCOMING), None),
            (turned((INCOMING, PROJ_OUT)), None), (turned((INCOMING, GATE_OUT)), None),
            (weights[(INCOMING, PROJ_OUT)], None), (weights[(INCOMING, GATE_OUT)], None),
        ],
        [
            (state_shape, F32, 0), ((hidden, half, length), BF16, 1), (state_shape, BF16, 0),
            ((width, 8), F32, None), (square, F32, None), (square, F32, None), ((8, width), F32, None),
        ],
        [wide, wide, wide, wide, head_scratch, tri_scratch], 26,
    )
    grads[(STARTING, BIAS_PROJ)], grads[(STARTING, VECTORS)] = bias_w_grad, vecs
    grad_tri = swap_all(by_device(grad_tri))
    product_grad = products(
        "incoming_product_back", functools.partial(tri_product_back_kernel, True),
        [grad_tri, product_two], product_half,
    )
    arrived = send(product_grad[0], group)
    between(9, grads)
    product_grad = [*meet(4, arrived), send(*meet(7, product_grad[1]), group)]
    (
        grad_one, grad_tri, gate_back, grads[(INCOMING, PROJ_GATE)], grads[(OUTGOING, PROJ_OUT)],
        grads[(OUTGOING, GATE_OUT)], vecs,
    ) = run_halves(
        functools.partial(tri_join_back_kernel, read_first), "incoming_in_outgoing_out_back", steps,
        [
            ([info[:half], info[half:]], "smem"), (alive, None), (state_one, 0), (product_grad, 3), (gate_back, 0), (grad_two, 0),
            (tri_cols(INCOMING), None), (turned((INCOMING, PROJ_GATE)), None),
            (weights[(INCOMING, PROJ_GATE)], None), (pair, 0), (tri_one, 1), (tri_cols(OUTGOING), None),
            (turned((OUTGOING, PROJ_OUT)), None), (turned((OUTGOING, GATE_OUT)), None),
            (weights[(OUTGOING, PROJ_OUT)], None), (weights[(OUTGOING, GATE_OUT)], None),
        ],
        [
            (state_shape, F32, 0), ((hidden, half, length), BF16, 1), (state_shape, BF16, 0),
            (weights[(INCOMING, PROJ_GATE)].shape, F32, None), (square, F32, None), (square, F32, None),
            ((8, width), F32, None),
        ],
        [wide, wide, wide, wide, product_scratch, tri_scratch], 37,
    )
    grads[(INCOMING, VECTORS)] = vecs
    between(5, grads)
    grad_tri = swap_all(by_device(grad_tri))
    grad_tri = [grad_tri[0], *meet(5, grad_tri[1])]
    product_grad = products(
        "outgoing_product_back", functools.partial(tri_product_back_kernel, False),
        [grad_tri, product_one], product_shape,
    )
    (product_grad,) = meet(6, *swap_all(product_grad))
    between(6, grads)
    pair_grad, grads[(OUTGOING, PROJ_GATE)], vecs = run_rows(
        functools.partial(tri_first_back_kernel, read_first, order_back), "outgoing_in_back", steps,
        [
            (info, "smem"), (alive, None), (pair, 0), (product_grad, 3), (gate_back, 0), (grad_one, 0),
            (tri_cols(OUTGOING), None), (turned((OUTGOING, PROJ_GATE)), None),
            (weights[(OUTGOING, PROJ_GATE)], None),
        ],
        [
            ((rows, length, width), BF16, 0), (weights[(OUTGOING, PROJ_GATE)].shape, F32, None),
            ((8, width), F32, None),
        ],
        [wide, wide, product_scratch], 20,
    )
    grads[(OUTGOING, VECTORS)] = vecs
    return pair_out, pair_grad, grads


HELD = {
    (PAIR, VECTORS): ((PAIR, NORM_GAIN), (PAIR, NORM_BIAS), (ATTEND, PAIR_GAIN), (ATTEND, PAIR_BIAS)),
    (ENDING, VECTORS): ((ENDING, NORM_GAIN), (ENDING, NORM_BIAS)),
    (STARTING, VECTORS): (
        (STARTING, NORM_GAIN), (STARTING, NORM_BIAS), (INCOMING, OUT_GAIN), (INCOMING, OUT_BIAS)
    ),
    (INCOMING, VECTORS): (
        (INCOMING, NORM_GAIN), (INCOMING, NORM_BIAS), (OUTGOING, OUT_GAIN), (OUTGOING, OUT_BIAS)
    ),
    (OUTGOING, VECTORS): ((OUTGOING, NORM_GAIN), (OUTGOING, NORM_BIAS)),
}


def vector_part(grads, table, name, first, last):
    pairs = [
        (row, held) for row, held in enumerate(HELD[name]) if first <= table[held][0] < last
    ]
    return (pairs, grads[name])


def fast_shards(parts, cores, pair, single, lengths, params, moment_one, moment_two, pair_cotangent, single_cotangent):
    entries = layout(C, H, S, TA_HEADS, SA_HEADS)
    table, total = table_of(entries)
    count = total // STRIDE
    shard_size = params.shape[0]
    attend = table[(ATTEND, NORM_GAIN)][0]
    pair_lanes = -(-attend * STRIDE // count)
    single_lane = attend * STRIDE // count
    devices = parts * cores
    line, group = ("z", "core"), ("crop", "core")
    row_index = lax.axis_index(line)
    odd = ((row_index * shard_size) % STRIDE) // (STRIDE // 2)
    place = jnp.stack([odd, odd]).astype(jnp.int32)
    shard_rows = jnp.pad(params, (0, RUN * STRIDE * STRIDE - shard_size)).reshape(-1, STRIDE)
    (runs,) = whole_call(
        runs_kernel, "parameter_runs", [(place, "smem"), (shard_rows, None)],
        [((STRIDE, RUN, STRIDE), BF16)], [((STRIDE, RUN, STRIDE), F32)],
    )
    rows, length, width = pair.shape[1:]
    send = in_turn()
    pair_in = send(pair[0].reshape(parts, -1, length, width), "crop")
    first_runs = lax.all_gather(runs[:pair_lanes], line)
    pair_in, _, lengths = after(pair_in, runs, lengths)
    live = lax.all_gather(jnp.broadcast_to(lengths.astype(F32), (8, STRIDE)), "crop")
    pair_in = send(pair_in, "z").reshape(rows, length, width)
    weights = unpack_pair(table, total, first_runs)
    size = rows // parts
    blocks = np.arange(length // size).reshape(parts, cores, parts)
    order = blocks.transpose(2, 1, 0).reshape(-1)
    orders = (order.tolist(), np.argsort(order).tolist())
    tokens = (order[:, None] * size + np.arange(size)).reshape(-1)
    live = live[lax.axis_index("z"), 0, 0]
    width = single.shape[2]
    mask = (tokens.astype(np.float32) < live).astype(F32)
    info = lax.dynamic_slice_in_dim(mask, lax.axis_index(group) * rows, rows).astype(jnp.int32)
    alive = jnp.broadcast_to(mask, (8, length))
    held = {}
    single_grads = {}

    def middle(bias):
        found = single_middle(held["state"], held["back"], held["projected"], bias, alive, weights)
        held["out"], held["grad"], grad_scores, grads, held["pending"] = found
        single_grads.update(grads)
        return grad_scores

    def meet(number, *values):
        if number == 0:
            others = [held["runs"]]
        elif number == 1:
            others = [weights[(SINGLE, UP)], held["state"]]
        elif number == 2:
            others = [held["projected"][1]]
        elif number == 3:
            others = [reduced[3]]
        elif number == 8:
            others = [single_grads[(ATTEND, QKVG)]]
        elif number == 6:
            values, reduced[5] = after(*values, reduced[5])
            return [values]
        elif number == 4:
            values, reduced[2] = after(*values, reduced[2])
            return [values]
        elif number == 7:
            others = [reduced[4]]
        else:
            values, held["both"], reduced[1] = after(*values, held["both"], reduced[1])
            return [values]
        return after(*values, *others)[: len(values)]

    def reduce_runs(sent):
        return jnp.sum(send(sent, line).astype(F32), axis=0).astype(BF16)

    reduced = {}
    lines_held = list(enumerate(SINGLE_VECTORS))
    late_lanes = -(-table[(OUTGOING, OUT_GAIN)][0] * STRIDE // count)
    late_end = table[(OUTGOING, GATE_OUT)][0]
    early = table[(OUTGOING, PROJ_OUT)][0]
    attend_lanes = -(-table[(STARTING, NORM_GAIN)][0] * STRIDE // count)
    first_row = table[(STARTING, NORM_GAIN)][0]
    last_row = table[(STARTING, BIAS_PROJ)][0]

    def lines():
        values = jnp.concatenate([single_grads[name].reshape(1, S) for name in SINGLE_VECTORS], axis=0)
        return jnp.pad(values, ((0, 8 - len(SINGLE_VECTORS)), (0, 0)))

    def between(number, grads):
        if number == 0:
            last_runs = after(runs[single_lane:], pair_in, weights[(OUTGOING, COLS)], live)[0]
            held["runs"] = lax.all_gather(last_runs, line)
            weights.update(unpack_single(table, total, single_lane, held["runs"]))
            for index, name in enumerate(SINGLE_VECTORS):
                weights[name] = weights[(SINGLE, VECTORS)][index]
            both = jnp.concatenate([single[0], single_cotangent[0]], axis=1)
            both = lax.all_gather(both, ("crop",) + line)
            both = both.reshape(parts, parts, cores, parts, -1, 2 * width)
            here = lax.axis_index("z"), lax.axis_index("core"), lax.axis_index("crop")
            both = both[here[0], :, here[1], here[2]].reshape(rows, 2 * width).astype(F32)
            held["state"], held["back"] = both[:, :width], both[:, width:]
            return
        if number == 1:
            lowered, qkvg, both = single_project(held["state"], weights, devices)
            held["projected"] = lowered, qkvg, send(both, group)
            return
        if number == 2:
            parts_held = grads[:, :, SA_HEADS * rows :]
            grad = held["grad"] + single_attend_end(held["pending"], parts_held, weights, single_grads)
            both = jnp.concatenate([held["out"], grad], axis=1).astype(BF16)
            held["both"] = lax.all_gather(both, ("crop",) + line)
            return
        if number == 6:
            reduced[1] = reduce_runs(reduced[1])
            return
        if number == 4:
            sent = pack(
                "single_gradient", table, total, devices, (pair_lanes, STRIDE), attend,
                [(name, single_grads[name]) for name in SINGLE_MATRICES]
                + [((ATTEND, PAIR_PROJ), grads[(ATTEND, PAIR_PROJ)])]
                + [vector_part(grads, table, (PAIR, VECTORS), attend, total), (lines_held, lines())],
            )
            reduced[3] = sent
            sent = sent.reshape((devices * parts, -1) + sent.shape[2:])
            reduced[2] = lax.psum_scatter(sent, line + ("crop",), scatter_dimension=0, tiled=False)
            return
        vectors = [name for name in HELD if name in grads]
        if number == 9:
            taken = -(-(pair_lanes * count - (attend + 2 * S // STRIDE) * STRIDE) // (4 * S))
            sent = pack(
                "attention_gradient", table, total, devices, (attend_lanes, pair_lanes), first_row,
                [(name, grads[name]) for name in PAIR_MATRICES if table[name][0] >= first_row]
                + [(name, grads[name]) for name in ((STARTING, BIAS_PROJ), (ENDING, BIAS_PROJ))]
                + [vector_part(grads, table, name, first_row, attend) for name in vectors]
                + [(lines_held[:2], lines()), ((ATTEND, QKVG), single_grads[(ATTEND, QKVG)][: -(-taken // 8) * 8])],
            )
            reduced[4] = sent
            reduced[5] = lax.psum_scatter(sent, line, scatter_dimension=0, tiled=False)
            return
        sent = pack(
            "pair_gradient", table, total, devices, (late_lanes, attend_lanes), early,
            [(name, grads[name]) for name in PAIR_MATRICES if early <= table[name][0] < last_row]
            + [vector_part(grads, table, name, early, last_row) for name in vectors],
        )
        reduced[1] = sent

    pair_out, pair_grad, grads = pair_path(
        pair_in, info, alive, orders, weights, pair_cotangent[0], middle, between, meet, send, group, parts
    )
    sent = pack(
        "outgoing_gradient", table, total, devices, (0, late_lanes), 0,
        [(name, grads[name]) for name in PAIR_MATRICES if table[name][0] < late_end]
        + [vector_part(grads, table, name, 0, late_end) for name in ((OUTGOING, VECTORS), (INCOMING, VECTORS))],
    )
    reduced[0] = reduce_runs(sent)
    pair_grad = send(pair_grad.reshape(parts, -1, length, pair_grad.shape[2]), "z")
    pair_grad, held["z"] = send(pair_grad, "crop").reshape(rows, length, -1).astype(F32), pair_grad
    both = held["both"].reshape(parts, parts, cores, parts, -1, 2 * width)
    both = both[:, lax.axis_index("crop"), lax.axis_index("core"), lax.axis_index("z")]
    both = both.reshape(rows, 2 * width)
    single_out, single_grad = both[:, :width], both[:, width:].astype(F32)
    summed = lax.all_gather(jnp.concatenate([reduced[0], reduced[1], reduced[5]], axis=0), "crop")
    others = lax.all_gather(reduced[2], "crop")
    shard, squares = whole_call(
        functools.partial(shard_kernel, shard_size), "gradient_share",
        [(place, "smem"), (summed, None), (others, None)],
        [((RUN * STRIDE, STRIDE), F32), ((8, STRIDE), F32)], [((STRIDE, RUN, STRIDE), F32)],
    )
    shard = shard.reshape(-1)[:shard_size]
    squares = after(squares, held["z"])[0]
    clip_norm = jnp.sqrt(jnp.sum(lax.all_gather(squares, line)))
    clipped = shard * (CLIP / jnp.maximum(clip_norm, CLIP))
    new_first = BETA_ONE * moment_one + (1.0 - BETA_ONE) * clipped
    new_second = BETA_TWO * moment_two + (1.0 - BETA_TWO) * clipped * clipped
    rates, decays = rate_tables(entries)
    rate_shard = lax.dynamic_slice_in_dim(jnp.asarray(rates), row_index * shard_size, shard_size)
    decay_shard = lax.dynamic_slice_in_dim(jnp.asarray(decays), row_index * shard_size, shard_size)
    first_hat = new_first / (1.0 - BETA_ONE**STEP)
    second_hat = new_second / (1.0 - BETA_TWO**STEP)
    new_params = params - rate_shard * (
        first_hat / (jnp.sqrt(second_hat) + ADAM_EPS) + decay_shard * params
    )
    return (
        pair_out[None],
        single_out[None],
        pair_grad[None],
        single_grad[None],
        new_params,
        new_first,
        new_second,
        clip_norm,
    )


def solution(mesh):
    crops, devices = mesh.devices.shape
    table, total = table_of(layout(C, H, S, TA_HEADS, SA_HEADS))
    count = total // STRIDE
    lanes = STRIDE + -table[(ATTEND, NORM_GAIN)][0] * STRIDE // count
    fast = devices == 2 * crops and LENGTH % (devices * 16) == 0 and count // devices + 2 <= RUN * STRIDE and lanes % crops == 0
    row = "row"
    if fast:
        mesh = jax.sharding.Mesh(mesh.devices.reshape(crops, crops, 2), ("crop", "z", "core"))
        row = ("z", "core")
    split = [P("crop", row, None, None), P("crop", row, None), P("crop"), P(row)]
    pair, single, lengths, share = split
    return jax.shard_map(
        functools.partial(fast_shards, crops, 2) if fast else shards,
        mesh=mesh,
        in_specs=(pair, single, lengths, share, share, share, pair, single),
        out_specs=(pair, single, pair, single, share, share, share, P()),
        check_vma=False,
    )
```
